32 devices in a mesh: section: 2 (over y), dp: 16 (over z, x, core).
Axes of the slice: x: 2, y: 2, z: 4, core: 2. Of those that a mesh axis runs over, the one named last changes fastest.
Arguments:
- tokens_in: bfloat16 [2, 1024, 768], P(None, 'dp'), may hold values from -6 to 6
- segment_ids: int32 [2, 1024], P(None, 'dp'), may hold values from 0 to 6, as said below
- out_grad: bfloat16 [2, 1024, 768], P(None, 'dp'), may hold values from -6 to 6
- qkv_weight: bfloat16 [2, 768, 2304], P('section', 'dp'), may hold values from -0.21875 to 0.21875
- attn_out_weight: bfloat16 [2, 768, 768], P('section', 'dp'), may hold values from -1.75 to 1.75
- mlp_in_weight: bfloat16 [2, 768, 2304], P('section', 'dp'), may hold values from -0.21875 to 0.21875
- mlp_out_weight: bfloat16 [2, 1152, 768], P('section', 'dp'), may hold values from -0.1875 to 0.1875
- attn_gain: bfloat16 [2, 768], P('section', 'dp'), may hold values from 0.25 to 1.75
- mlp_gain: bfloat16 [2, 768], P('section', 'dp'), may hold values from 0.25 to 1.75
Outputs:
- layer_outputs: bfloat16 [2, 2, 1024, 768], P('section', None, 'dp')
- input_grads: bfloat16 [2, 2, 1024, 768], P('section', None, 'dp')
- qkv_grad: float32 [2, 768, 2304], P('section', 'dp')
- attn_out_grad: float32 [2, 768, 768], P('section', 'dp')
- mlp_in_grad: float32 [2, 768, 2304], P('section', 'dp')
- mlp_out_grad: float32 [2, 1152, 768], P('section', 'dp')
- attn_gain_grad: float32 [2, 768], P('section', 'dp')
- mlp_gain_grad: float32 [2, 768], P('section', 'dp')
The draws below stay inside these ranges and needn't reach their ends.
Inputs may be any that keep to these rules, and one draw needn't show every extreme that they name: `segment_ids`: within each sequence of 1024 tokens the numbers start at 0, never fall and rise by exactly one at each document start: 3 starts lie among positions 1 to 62 and 3 among positions 962 to 1023 of the sequence, none elsewhere.
All inputs are finite; a program needn't handle non-finite values.
Results may differ from the reference program's by a relative error of at most 0.024.
Values may be sent and summed in bfloat16 or wider, within the bound.
No kernel may reach another device: no remote copies, remote signals or barrier semaphores. Data moves between devices by JAX's collectives and lax.ppermute only.
A program may use at most 192 MiB of HBM per device.

```python
import math
import jax
import jax.numpy as jnp
from jax import lax

HEAD_DIM = 64
FF = 1152
D = 768
TOK = 64
MB = 2
HALF_WIN = 64
CUTS = 3
SEQ_LEN = 1024
ROWS = 1024


def draw_segment_ids(key, part):
    key = jax.random.fold_in(key, 7)
    seq_count = MB * (ROWS // SEQ_LEN)
    seq_keys = jax.random.split(key, seq_count)

    def one_sequence(seq_key):
        first_key, last_key = jax.random.split(seq_key)
        first_cuts = 1 + jax.random.permutation(first_key, TOK - 2)[:CUTS]
        last_cuts = SEQ_LEN - TOK + 2 + jax.random.permutation(last_key, TOK - 2)[:CUTS]
        starts_mask = jnp.zeros((SEQ_LEN,), jnp.int32).at[first_cuts].set(1).at[last_cuts].set(1)
        return jnp.cumsum(starts_mask).astype(jnp.int32)
    return jax.vmap(one_sequence)(seq_keys).reshape(MB, ROWS).astype(jnp.int32)


def steps_of(own_key, extent, shards, least, largest):
    def one(dim, blocks):
        steps = jax.random.uniform(jax.random.fold_in(jax.random.fold_in(own_key, 6), dim), (blocks,), jnp.float32, least / len(shards), largest / len(shards))
        return jnp.repeat(jnp.exp(steps), extent[dim] // blocks).reshape((-1,) + (1,) * (len(extent) - dim - 1))

    factor_of = one(*shards[0])
    for cut in shards[1:]:
        factor_of = factor_of * one(*cut)
    return factor_of


def bell_draw(own_key, extent, deviation, limit, cuts=(), dtype=jnp.bfloat16):
    drawn = jax.random.normal(own_key, extent, jnp.float32) * deviation
    if len(cuts) > 0:
        drawn = steps_of(own_key, extent, cuts, -0.22, 0.18) * drawn
    return jnp.clip(drawn, min=-limit, max=limit).astype(dtype)


def setup_inputs(seed: int = 0) -> dict:
    key_list = jax.random.split(jax.random.key(seed), 10)
    tokens_in = bell_draw(key_list[0], (MB, ROWS, D), 1.0, 6.0, ((1, 16),))
    segment_ids = draw_segment_ids(jax.random.fold_in(key_list[9], 71), 0)
    out_grad = bell_draw(key_list[2], (MB, ROWS, D), 1.0, 6.0, ((1, 16),))
    qkv_weight = bell_draw(key_list[3], (2, D, 3 * D), D ** -0.5, 0.21875, ((0, 2), (1, 16)))
    attn_out_weight = bell_draw(key_list[4], (2, D, D), (D // 64) ** -0.5, 1.75, ((0, 2), (1, 16)))
    mlp_in_weight = bell_draw(key_list[5], (2, D, 2 * FF), D ** -0.5, 0.21875, ((0, 2), (1, 16)))
    mlp_out_weight = bell_draw(key_list[6], (2, FF, D), FF ** -0.5, 0.1875, ((0, 2), (1, 16)))
    attn_gain = jnp.clip(1.0 + 0.15 * jax.random.normal(key_list[7], (2, D), jnp.float32), 0.25, 1.75).astype(jnp.bfloat16)
    mlp_gain = jnp.clip(1.0 + 0.15 * jax.random.normal(key_list[8], (2, D), jnp.float32), 0.25, 1.75).astype(jnp.bfloat16)
    return {"tokens_in": tokens_in, "segment_ids": segment_ids, "out_grad": out_grad, "qkv_weight": qkv_weight, "attn_out_weight": attn_out_weight, "mlp_in_weight": mlp_in_weight, "mlp_out_weight": mlp_out_weight, "attn_gain": attn_gain, "mlp_gain": mlp_gain}


@jax.custom_vjp
def low(v):
    return lax.optimization_barrier(v.astype(jnp.bfloat16)).astype(jnp.float32)

@jax.custom_vjp
def low_back(v):
    return v

def low_keep(v):
    return (low(v), None)

def low_pass(kept, grad):
    return (grad,)

def back_keep(v):
    return (v, None)

def back_low(kept, grad):
    return (low(grad),)
low.defvjp(low_keep, low_pass)
low_back.defvjp(back_keep, back_low)
local_log_base = math.log(10000.0)
global_log_base = math.log(160000.0)
masked_score = -1e+30

def matmul(left, right):
    return jnp.dot(left, right, precision=lax.Precision.HIGHEST, preferred_element_type=jnp.float32)

def normalize(values, gain_row):
    center = values - lax.optimization_barrier(jnp.mean(values, -1, keepdims=True))
    spread = lax.optimization_barrier(jnp.mean(center * center, -1, keepdims=True))
    return center * lax.rsqrt(spread + 1e-05) * gain_row

def angles(positions, log_base, head_dim):
    half_dim = head_dim // 2
    fraction = (2 * jnp.arange(half_dim)).astype(jnp.float32) / head_dim
    inverse = jnp.exp(-fraction * log_base)
    angle_table = positions.astype(jnp.float32)[:, None] * inverse[None, :]
    angle_table = jnp.concatenate([angle_table, angle_table], -1)
    return (jnp.cos(angle_table)[:, None, :], jnp.sin(angle_table)[:, None, :])

def rotate(values, cosine, sine_table):
    half_dim = values.shape[-1] // 2
    turned = jnp.concatenate([-values[..., half_dim:], values[..., :half_dim]], -1)
    return values * cosine + turned * sine_table

def transformer_layer(activations, segments, params, window_reach, log_base):
    w_qkv, w_attn, w_in, w_out, gain_attn, gain_mlp = params
    seq_total, seq_len, model_width = activations.shape
    head_count = model_width // HEAD_DIM
    flat_acts = activations.reshape(-1, model_width)
    normed_a = low(normalize(flat_acts, gain_attn))
    projected = low_back(matmul(normed_a, w_qkv)).reshape(seq_total, seq_len, 3 * model_width)
    cosine, sine_table = angles(jnp.arange(seq_len), log_base, HEAD_DIM)
    head_shape = (seq_total, seq_len, head_count, HEAD_DIM)
    queries = low(rotate(projected[..., :model_width].reshape(head_shape), cosine, sine_table))
    keys_all = low(rotate(projected[..., model_width:2 * model_width].reshape(head_shape), cosine, sine_table))
    values_all = low(projected[..., 2 * model_width:]).reshape(head_shape)
    per_step = 1
    for option in range(1, seq_total + 1):
        if seq_total % option == 0 and option * seq_len <= 4096:
            per_step = option
    block_count = seq_total // per_step

    def attend(block_in):
        query_block, key_block, value_block, seg_block = block_in
        positions = jnp.arange(seq_len)
        in_reach = jnp.abs(positions[:, None] - positions[None, :]) <= window_reach
        visible = (seg_block[:, :, None] == seg_block[:, None, :]) & in_reach[None]
        raw_scores = jnp.einsum('bqhd,bkhd->bhqk', query_block, key_block, precision=lax.Precision.HIGHEST) * (1.0 / math.sqrt(HEAD_DIM))
        scores = low_back(jnp.where(visible[:, None], raw_scores, masked_score))
        attn_probs = jax.nn.softmax(scores, axis=-1)
        return jnp.einsum('bhqk,bkhd->bqhd', low(attn_probs), value_block, precision=lax.Precision.HIGHEST)
    blocks = tuple((array_in.reshape((block_count, per_step) + array_in.shape[1:]) for array_in in (queries, keys_all, values_all, segments)))
    attended = lax.map(jax.checkpoint(attend), blocks).reshape(-1, model_width)
    attended = low_back(low(attended))
    middle = flat_acts + low_back(matmul(attended, w_attn))
    normed_m = low(normalize(middle, gain_mlp))
    gate_up = low_back(matmul(normed_m, w_in))
    half_width = gate_up.shape[1] // 2
    mixed_act = low(jax.nn.gelu(gate_up[:, :half_width], approximate=False) * gate_up[:, half_width:])
    result = middle + low_back(matmul(mixed_act, w_out))
    return result.reshape(seq_total, seq_len, model_width)

def reference(tokens_in, segment_ids, out_grad, qkv_weight, attn_out_weight, mlp_in_weight, mlp_out_weight, attn_gain, mlp_gain):
    shaped = (-1, SEQ_LEN, tokens_in.shape[-1])
    activations = tokens_in.astype(jnp.float32).reshape(shaped)
    segments = segment_ids.reshape(-1, SEQ_LEN)
    cotangent = out_grad.astype(jnp.float32).reshape(shaped)
    params = tuple((weight_in.astype(jnp.float32) for weight_in in (qkv_weight, attn_out_weight, mlp_in_weight, mlp_out_weight, attn_gain, mlp_gain)))
    layer_offset = jnp.zeros_like(activations)

    def forward(first_acts, weights, shift_in):
        lower_layer = tuple((weight_in[0] for weight_in in weights))
        upper_layer = tuple((weight_in[1] for weight_in in weights))
        hidden = low(transformer_layer(first_acts, segments, lower_layer, HALF_WIN, local_log_base))
        final_acts = transformer_layer(low_back(hidden) + shift_in, segments, upper_layer, SEQ_LEN, global_log_base)
        return (final_acts, hidden)
    final_acts, pullback, hidden = jax.vjp(forward, activations, params, layer_offset, has_aux=True)
    d_acts, d_params, d_offset = pullback(cotangent)
    out_shape = (2,) + tokens_in.shape
    layer_outputs = jnp.stack([hidden, final_acts]).reshape(out_shape).astype(jnp.bfloat16)
    input_grads = jnp.stack([d_acts, d_offset]).reshape(out_shape).astype(jnp.bfloat16)
    return (layer_outputs, input_grads, d_params[0], d_params[1], d_params[2], d_params[3], d_params[4], d_params[5])
```

```python
import math

import jax
import jax.numpy as jnp
from jax import lax
from jax.sharding import PartitionSpec as P

HEAD_DIM = 64
GROUP = 16
HALF_WIN = 64
HEADS = 12

local_log_base = math.log(10000.0)
global_log_base = math.log(160000.0)
masked_score = -1e30
SCALE = 1.0 / math.sqrt(HEAD_DIM)
BF = jnp.bfloat16
F32 = jnp.float32


def dot(left, right):
    return jnp.dot(left, right, preferred_element_type=F32)


def dot_bt(left, right):
    return lax.dot_general(left, right, (((1,), (1,)), ((), ())), preferred_element_type=F32)


def dot_at(left, right):
    return lax.dot_general(left, right, (((0,), (0,)), ((), ())), preferred_element_type=F32)


def moments(values):
    center = values - jnp.mean(values, -1, keepdims=True)
    scale = lax.rsqrt(jnp.mean(center * center, -1, keepdims=True) + 1e-05)
    return center * scale, scale


def norm_back(grad_out, gain_row, xhat, scale):
    scaled = grad_out * gain_row
    mean_grad = jnp.mean(scaled, -1, keepdims=True)
    mean_dot = jnp.mean(scaled * xhat, -1, keepdims=True)
    return (scaled - mean_grad - xhat * mean_dot) * scale


def angles(positions, log_base):
    half_dim = HEAD_DIM // 2
    fraction = (2 * jnp.arange(half_dim)).astype(F32) / HEAD_DIM
    inverse = jnp.exp(-fraction * log_base)
    table = positions.astype(F32)[:, None] * inverse[None, :]
    table = jnp.concatenate([table, table], -1)
    cosine, sine = jnp.cos(table), jnp.sin(table)
    return jnp.tile(cosine, (2, 1))[:, None, :], jnp.tile(sine, (2, 1))[:, None, :]


def rotate(values, tables):
    cosine, sine = tables
    heads = values.reshape(values.shape[0], HEADS, HEAD_DIM)
    half = HEAD_DIM // 2
    turned = jnp.concatenate([-heads[..., half:], heads[..., :half]], -1)
    return (heads * cosine + turned * sine).reshape(values.shape)


def unrotate(grads, tables):
    cosine, sine = tables
    heads = grads.reshape(grads.shape[0], HEADS, HEAD_DIM)
    half = HEAD_DIM // 2
    scaled = heads * sine
    turned = jnp.concatenate([scaled[..., half:], -scaled[..., :half]], -1)
    return (heads * cosine + turned).reshape(grads.shape)


def project(layer_in, weights, tables):
    width = layer_in.shape[1]
    xhat, scale = moments(layer_in)
    normed = (xhat * weights["gain_attn"]).astype(BF)
    projected = dot(normed, weights["qkv"])
    queries = rotate(projected[:, :width], tables).astype(BF)
    keys = rotate(projected[:, width : 2 * width], tables).astype(BF)
    values = projected[:, 2 * width :].astype(BF)
    return normed, queries, keys, values


def finish_forward(layer_in, attended, weights):
    middle = layer_in + dot(attended, weights["attn"])
    xhat, scale = moments(middle)
    normed = (xhat * weights["gain_mlp"]).astype(BF)
    gate_up = dot(normed, weights["mlp_in"])
    half = gate_up.shape[1] // 2
    gate, up = gate_up[:, :half], gate_up[:, half:]
    mixed = (jax.nn.gelu(gate, approximate=False) * up).astype(BF)
    result = (middle + dot(mixed, weights["mlp_out"])).astype(BF)
    return result, (normed, gate_up, mixed, xhat, scale)


def start_backward(upstream, saved, weights):
    normed, gate_up, mixed, xhat, scale = saved
    d_mlp = upstream.astype(BF)
    d_mixed = dot_bt(d_mlp, weights["mlp_out"])
    half = gate_up.shape[1] // 2
    gate, up = gate_up[:, :half], gate_up[:, half:]
    cdf = 0.5 * (1.0 + lax.erf(gate * math.sqrt(0.5)))
    density = jnp.exp(-0.5 * gate * gate) * (1.0 / math.sqrt(2.0 * math.pi))
    d_gate = d_mixed * up * (cdf + gate * density)
    d_up = d_mixed * gate * cdf
    d_gate_up = jnp.concatenate([d_gate, d_up], 1).astype(BF)
    d_normed = dot_bt(d_gate_up, weights["mlp_in"])
    gain_grad = jnp.sum(d_normed * xhat, 0)
    d_middle = upstream + norm_back(d_normed, weights["gain_mlp"], xhat, scale)
    d_attn = d_middle.astype(BF)
    d_attended = dot_bt(d_attn, weights["attn"]).astype(BF)
    return d_middle, d_attended, (normed, d_gate_up, mixed, d_mlp, d_attn), gain_grad


def finish_backward(d_middle, d_projected, layer_in, weights):
    d_normed = dot_bt(d_projected, weights["qkv"])
    xhat, scale = moments(layer_in)
    gain_grad = jnp.sum(d_normed * xhat, 0)
    grad = d_middle + norm_back(d_normed, weights["gain_attn"], xhat, scale)
    return grad.astype(BF), gain_grad


def neighbours(count, step):
    return [
        (i, i + step)
        for i in range(count)
        if 0 <= i + step < count and i // GROUP == (i + step) // GROUP
    ]


def with_halo(rows, count):
    before = lax.ppermute(rows, "dp", neighbours(count, 1))
    after = lax.ppermute(rows, "dp", neighbours(count, -1))
    return jnp.concatenate([before, rows, after], 1)


def local_scores(queries, keys, visible):
    raw = jnp.einsum("bqhd,bkhd->bhqk", queries, keys, preferred_element_type=F32) * SCALE
    scores = jnp.where(visible[:, None], raw, masked_score)
    peak = jnp.max(scores, -1, keepdims=True)
    weights = jnp.exp(scores - peak)
    return weights / jnp.sum(weights, -1, keepdims=True)


def heads_of(rows):
    return rows.reshape(2, -1, HEADS, HEAD_DIM)


def local_forward(queries, keys_values, visible):
    width = queries.shape[1]
    keys, values = keys_values[..., :width], keys_values[..., width:]
    probs = local_scores(heads_of(queries), heads_of(keys), visible)
    attended = jnp.einsum(
        "bhqk,bkhd->bqhd", probs.astype(BF), heads_of(values), preferred_element_type=F32
    )
    return attended.reshape(queries.shape).astype(BF), probs


def local_backward(d_attended, probs, queries, keys_values, count):
    rows, width = queries.shape
    row_count = rows // 2
    keys, values = keys_values[..., :width], keys_values[..., width:]
    d_heads = heads_of(d_attended)
    d_probs = jnp.einsum(
        "bqhd,bkhd->bhqk", d_heads, heads_of(values), preferred_element_type=F32
    )
    delta = jnp.sum(probs * d_probs, -1, keepdims=True)
    d_scores = (probs * (d_probs - delta)).astype(BF)
    d_queries = (
        jnp.einsum("bhqk,bkhd->bqhd", d_scores, heads_of(keys), preferred_element_type=F32) * SCALE
    )
    d_keys = (
        jnp.einsum("bhqk,bqhd->bkhd", d_scores, heads_of(queries), preferred_element_type=F32)
        * SCALE
    )
    d_values = jnp.einsum(
        "bhqk,bqhd->bkhd", probs.astype(BF), d_heads, preferred_element_type=F32
    )
    d_kv = jnp.concatenate(
        [d_keys.reshape(2, -1, width), d_values.reshape(2, -1, width)], 2
    )
    to_before = d_kv[:, :row_count].astype(BF)
    to_after = d_kv[:, 2 * row_count :].astype(BF)
    from_after = lax.ppermute(to_before, "dp", neighbours(count, -1))
    from_before = lax.ppermute(to_after, "dp", neighbours(count, 1))
    d_kv = d_kv[:, row_count : 2 * row_count] + from_after.astype(F32) + from_before.astype(F32)
    d_kv = d_kv.reshape(rows, 2 * width)
    return d_queries.reshape(rows, width), d_kv[:, :width], d_kv[:, width:]


def split_heads(rows):
    row_count = rows.shape[0] // 2
    half = row_count // 2
    parts = rows.reshape(2, row_count, 4, 3, HEAD_DIM)
    own = parts[:, :, :, 0::2].transpose(0, 2, 3, 1, 4)
    shared = parts[:, :, :, 1].reshape(2, 2, half, 4, HEAD_DIM).transpose(0, 3, 1, 2, 4)
    return jnp.concatenate([own, shared], 3).reshape(GROUP, row_count + half, HEAD_DIM)


def join_heads(blocks):
    row_count = blocks.shape[1] * 2 // 3
    half = row_count // 2
    parts = blocks.reshape(2, 4, 2, row_count + half, HEAD_DIM)
    own = parts[:, :, :, :row_count].transpose(0, 3, 1, 2, 4)
    shared = parts[:, :, :, row_count:].transpose(0, 2, 3, 1, 4).reshape(2, row_count, 4, HEAD_DIM)
    rows = jnp.stack([own[:, :, :, 0], shared, own[:, :, :, 1]], 3)
    return rows.reshape(2 * row_count, HEADS * HEAD_DIM)


def fold(blocks):
    half = blocks.shape[1] // 2
    return jnp.concatenate([blocks[:, :half], blocks[:, half:]], 2)


def unfold(blocks):
    return jnp.concatenate([blocks[..., :HEAD_DIM], blocks[..., HEAD_DIM:]], 1)


def exchange(blocks, count):
    groups = [list(range(s, s + GROUP)) for s in range(0, count, GROUP)]
    return lax.all_to_all(blocks, "dp", 0, 0, axis_index_groups=groups)


def other_core(rows, count):
    return lax.ppermute(rows, "dp", [(i, i ^ 1) for i in range(count)])


def pack_three(first, second, third):
    return jnp.concatenate([jnp.concatenate([first, second], 2), fold(third)], 1)


def unpack_three(blocks):
    rows = blocks.shape[1] * 2 // 3
    pair = blocks[:, :rows]
    return pair[..., :HEAD_DIM], pair[..., HEAD_DIM:], unfold(blocks[:, rows:])


def own_rows(blocks):
    row_count = blocks.shape[1] * 2 // 3
    return blocks[:, :row_count].reshape(-1, HEAD_DIM)


def shared_rows(blocks):
    row_count = blocks.shape[1] * 2 // 3
    return blocks[:, row_count:].reshape(-1, HEAD_DIM)


def to_blocks(own, shared):
    return jnp.concatenate(
        [own.reshape(GROUP, -1, HEAD_DIM), shared.reshape(GROUP, -1, HEAD_DIM)], 1
    )


def soft_attend(queries, keys, values, query_seg, key_seg):
    raw = dot_bt(queries, keys) * SCALE
    scores = jnp.where(query_seg[:, None] == key_seg[None, :], raw, masked_score)
    peak = jnp.max(scores, -1, keepdims=True)
    weights = jnp.exp(scores - peak)
    probs = weights / jnp.sum(weights, -1, keepdims=True)
    return dot(probs.astype(BF), values), probs


def soft_back(d_out, probs, queries, keys, values):
    d_probs = dot_bt(d_out, values)
    delta = jnp.sum(probs * d_probs, -1, keepdims=True)
    d_scores = (probs * (d_probs - delta)).astype(BF)
    d_queries = dot(d_scores, keys) * SCALE
    d_keys = dot_at(d_scores, queries) * SCALE
    d_values = dot_at(probs.astype(BF), d_out)
    return d_queries, d_keys, d_values


def global_forward(queries, keys, values, own_seg, shared_seg, count):
    sent = pack_three(split_heads(queries), split_heads(keys), split_heads(values))
    got_q, got_k, got_v = unpack_three(exchange(sent, count))
    shared_kv = jnp.concatenate([shared_rows(got_k), shared_rows(got_v)], 1)
    both_kv = jnp.concatenate([shared_kv, other_core(shared_kv, count)], 0)
    own_in = (own_rows(got_q), own_rows(got_k), own_rows(got_v))
    shared_in = (shared_rows(got_q), both_kv[:, :HEAD_DIM], both_kv[:, HEAD_DIM:])
    own_out, own_probs = soft_attend(*own_in, own_seg, own_seg)
    shared_out, shared_probs = soft_attend(
        *shared_in, shared_seg[: shared_seg.shape[0] // 2], shared_seg
    )
    back = fold(to_blocks(own_out.astype(BF), shared_out.astype(BF)))
    attended = join_heads(unfold(exchange(back, count)))
    return attended, (own_in, own_probs, shared_in, shared_probs)


def global_backward(d_attended, saved, count):
    own_in, own_probs, shared_in, shared_probs = saved
    got = unfold(exchange(fold(split_heads(d_attended)), count))
    own_grads = soft_back(own_rows(got), own_probs, *own_in)
    shared_q, shared_k, shared_v = soft_back(shared_rows(got), shared_probs, *shared_in)
    d_kv = jnp.concatenate([shared_k, shared_v], 1)
    half = d_kv.shape[0] // 2
    d_kv = d_kv[:half] + other_core(d_kv[half:].astype(BF), count).astype(F32)
    shared_grads = (shared_q, d_kv[:, :HEAD_DIM], d_kv[:, HEAD_DIM:])
    blocks = [
        to_blocks(own.astype(BF), shared.astype(BF))
        for own, shared in zip(own_grads, shared_grads)
    ]
    back = unpack_three(exchange(pack_three(*blocks), count))
    return tuple(join_heads(part).astype(F32) for part in back)


def to_other_section(rows, step):
    return lax.ppermute(rows, "section", [(0, 1)] if step > 0 else [(1, 0)])


def on_device(
    tokens_in,
    segment_ids,
    out_grad,
    qkv_weight,
    attn_out_weight,
    mlp_in_weight,
    mlp_out_weight,
    attn_gain,
    mlp_gain,
):
    lower = lax.axis_index("section") == 0
    count = lax.axis_size("dp")
    replica = lax.axis_index("dp")
    group_pos = replica % GROUP
    micro_count, row_count, width = tokens_in.shape
    shard = qkv_weight.shape[1]
    wide = mlp_out_weight.shape[1] * width // shard
    gains = jnp.stack([attn_gain[0], mlp_gain[0]], 1)
    gains = jnp.pad(gains, ((0, 0), (0, 126)))
    first = lax.all_gather(
        jnp.concatenate([qkv_weight[0], gains], 1), "dp", axis=0, tiled=True
    )
    second = lax.all_gather(
        jnp.concatenate(
            [attn_out_weight[0], mlp_in_weight[0], mlp_out_weight[0].reshape(shard, wide)], 1
        ),
        "dp",
        axis=0,
        tiled=True,
    )
    weights = {
        "qkv": first[:, : 3 * width],
        "gain_attn": first[:, 3 * width].astype(F32)[None],
        "gain_mlp": first[:, 3 * width + 1].astype(F32)[None],
        "attn": second[:, :width],
        "mlp_in": second[:, width : second.shape[1] - wide],
        "mlp_out": second[:, second.shape[1] - wide :].reshape(-1, width),
    }

    groups = [list(range(s, s + GROUP)) for s in range(0, count, GROUP)]
    segments = lax.all_gather(segment_ids, "dp", axis=1, tiled=True, axis_index_groups=groups)
    positions = group_pos * row_count + jnp.arange(row_count)
    local_tables = angles(positions, local_log_base)
    global_tables = angles(positions, global_log_base)

    key_pos = positions[0] - row_count + jnp.arange(3 * row_count)
    around = jnp.pad(segments, ((0, 0), (row_count, row_count)), constant_values=-1)
    key_seg = lax.dynamic_slice_in_dim(around, group_pos * row_count, 3 * row_count, 1)
    visible = (segment_ids[:, :, None] == key_seg[:, None, :]) & (
        jnp.abs(positions[:, None] - key_pos[None, :]) <= HALF_WIN
    )[None]

    own_seg = lax.dynamic_index_in_dim(segments, group_pos // 8, 0, keepdims=False)
    halves = own_seg.reshape(GROUP, 2, row_count // 2)
    mine = lax.dynamic_index_in_dim(halves, group_pos % 2, 1, keepdims=False).reshape(-1)
    theirs = lax.dynamic_index_in_dim(halves, 1 - group_pos % 2, 1, keepdims=False).reshape(-1)
    shared_seg = jnp.concatenate([mine, theirs])

    in_0 = tokens_in.reshape(-1, width).astype(F32)
    normed_0, q_0, k_0, v_0 = project(in_0, weights, local_tables)
    kv_0 = with_halo(jnp.concatenate([k_0, v_0], 1).reshape(2, row_count, 2 * width), count)
    att_0, probs_0 = local_forward(q_0, kv_0, visible)
    out_0, saved_0 = finish_forward(in_0, att_0, weights)

    in_1 = to_other_section(out_0, 1).astype(F32)
    normed_1, q_1, k_1, v_1 = project(in_1, weights, global_tables)
    att_1, kept_1 = global_forward(q_1, k_1, v_1, own_seg, shared_seg, count)
    out_1, saved_1 = finish_forward(in_1, att_1, weights)

    up_1 = out_grad.reshape(-1, width).astype(F32)
    d_mid_1, d_att_1, ops_1, gain_mlp_1 = start_backward(up_1, saved_1, weights)
    d_q, d_k, d_v = global_backward(d_att_1, kept_1, count)
    d_proj_1 = jnp.concatenate(
        [unrotate(d_q, global_tables), unrotate(d_k, global_tables), d_v], 1
    ).astype(BF)
    grad_1, gain_attn_1 = finish_backward(d_mid_1, d_proj_1, in_1, weights)

    up_0 = to_other_section(grad_1, -1).astype(F32)
    d_mid_0, d_att_0, ops_0, gain_mlp_0 = start_backward(up_0, saved_0, weights)
    n2, d_gu, mixed, d_mlp, d_attn = (
        jnp.where(lower, a, b) for a, b in zip(ops_0, ops_1)
    )
    mlp_grads = jnp.concatenate(
        [
            dot_at(n2, d_gu).astype(BF),
            dot_at(mixed, d_mlp).astype(BF).reshape(width, -1),
        ],
        1,
    )
    mlp_share = lax.psum_scatter(mlp_grads, "dp", scatter_dimension=0, tiled=True)
    d_q, d_k, d_v = local_backward(d_att_0, probs_0, q_0, kv_0, count)
    d_proj_0 = jnp.concatenate(
        [unrotate(d_q, local_tables), unrotate(d_k, local_tables), d_v], 1
    ).astype(BF)
    grad_0, gain_attn_0 = finish_backward(d_mid_0, d_proj_0, in_0, weights)

    n1, d_proj, att = (
        jnp.where(lower, a, b)
        for a, b in ((normed_0, normed_1), (d_proj_0, d_proj_1), (att_0, att_1))
    )
    gain_grads = jnp.where(
        lower,
        jnp.stack([gain_attn_0, gain_mlp_0], 1),
        jnp.stack([gain_attn_1, gain_mlp_1], 1),
    )
    attn_grads = jnp.concatenate(
        [
            dot_at(n1, d_proj).astype(BF),
            dot_at(att, d_attn).astype(BF),
            jnp.pad(gain_grads, ((0, 0), (0, 126))).astype(BF),
        ],
        1,
    )
    attn_share = lax.psum_scatter(attn_grads, "dp", scatter_dimension=0, tiled=True)
    mlp_share, attn_share = mlp_share.astype(F32), attn_share.astype(F32)
    return (
        jnp.where(lower, out_0, out_1).reshape(1, micro_count, row_count, width),
        jnp.where(lower, grad_0, grad_1).reshape(1, micro_count, row_count, width),
        attn_share[None, :, : 3 * width],
        attn_share[None, :, 3 * width : 4 * width],
        mlp_share[None, :, : mlp_share.shape[1] - wide],
        mlp_share[:, mlp_share.shape[1] - wide :].reshape(1, -1, width),
        attn_share[None, :, 4 * width],
        attn_share[None, :, 4 * width + 1],
    )


def solution(mesh):
    in_specs = (
        P(None, "dp", None),
        P(None, "dp"),
        P(None, "dp", None),
        P("section", "dp", None),
        P("section", "dp", None),
        P("section", "dp", None),
        P("section", "dp", None),
        P("section", "dp"),
        P("section", "dp"),
    )
    out_specs = (
        P("section", None, "dp", None),
        P("section", None, "dp", None),
        P("section", "dp", None),
        P("section", "dp", None),
        P("section", "dp", None),
        P("section", "dp", None),
        P("section", "dp"),
        P("section", "dp"),
    )
    return jax.shard_map(
        on_device, mesh=mesh, in_specs=in_specs, out_specs=out_specs, check_vma=False
    )
```

```python
import math

import jax
import jax.numpy as jnp
from jax import lax
from jax.sharding import PartitionSpec as P

HEAD_DIM = 64
GROUP = 16
HALF_WIN = 64
HEADS = 12

local_log_base = math.log(10000.0)
global_log_base = math.log(160000.0)
masked_score = -1e30
SCALE = 1.0 / math.sqrt(HEAD_DIM)
BF = jnp.bfloat16
F32 = jnp.float32


def dot(left, right):
    return jnp.dot(left, right, preferred_element_type=F32)


def dot_bt(left, right):
    return lax.dot_general(left, right, (((1,), (1,)), ((), ())), preferred_element_type=F32)


def dot_at(left, right):
    return lax.dot_general(left, right, (((0,), (0,)), ((), ())), preferred_element_type=F32)


def moments(values):
    center = values - jnp.mean(values, -1, keepdims=True)
    scale = lax.rsqrt(jnp.mean(center * center, -1, keepdims=True) + 1e-05)
    return center * scale, scale


def norm_back(grad_out, gain_row, xhat, scale):
    scaled = grad_out * gain_row
    mean_grad = jnp.mean(scaled, -1, keepdims=True)
    mean_dot = jnp.mean(scaled * xhat, -1, keepdims=True)
    return (scaled - mean_grad - xhat * mean_dot) * scale


def angles(positions, log_base):
    half_dim = HEAD_DIM // 2
    fraction = (2 * jnp.arange(half_dim)).astype(F32) / HEAD_DIM
    inverse = jnp.exp(-fraction * log_base)
    table = positions.astype(F32)[:, None] * inverse[None, :]
    table = jnp.concatenate([table, table], -1)
    cosine, sine = jnp.cos(table), jnp.sin(table)
    return jnp.tile(cosine, (2, 1))[:, None, :], jnp.tile(sine, (2, 1))[:, None, :]


def rotate(values, tables):
    cosine, sine = tables
    heads = values.reshape(values.shape[0], HEADS, HEAD_DIM)
    half = HEAD_DIM // 2
    turned = jnp.concatenate([-heads[..., half:], heads[..., :half]], -1)
    return (heads * cosine + turned * sine).reshape(values.shape)


def unrotate(grads, tables):
    cosine, sine = tables
    heads = grads.reshape(grads.shape[0], HEADS, HEAD_DIM)
    half = HEAD_DIM // 2
    scaled = heads * sine
    turned = jnp.concatenate([scaled[..., half:], -scaled[..., :half]], -1)
    return (heads * cosine + turned).reshape(grads.shape)


def project(layer_in, weights, tables):
    width = layer_in.shape[1]
    xhat, scale = moments(layer_in)
    normed = (xhat * weights["gain_attn"]).astype(BF)
    projected = dot(normed, weights["qkv"])
    queries = rotate(projected[:, :width], tables).astype(BF)
    keys = rotate(projected[:, width : 2 * width], tables).astype(BF)
    values = projected[:, 2 * width :].astype(BF)
    return normed, queries, keys, values


def finish_forward(layer_in, attended, weights):
    middle = layer_in + dot(attended, weights["attn"])
    xhat, scale = moments(middle)
    normed = (xhat * weights["gain_mlp"]).astype(BF)
    gate_up = dot(normed, weights["mlp_in"])
    half = gate_up.shape[1] // 2
    gate, up = gate_up[:, :half], gate_up[:, half:]
    mixed = (jax.nn.gelu(gate, approximate=False) * up).astype(BF)
    result = (middle + dot(mixed, weights["mlp_out"])).astype(BF)
    return result, (normed, gate_up, mixed, xhat, scale)


def start_backward(upstream, saved, weights):
    normed, gate_up, mixed, xhat, scale = saved
    d_mlp = upstream.astype(BF)
    d_mixed = dot_bt(d_mlp, weights["mlp_out"])
    half = gate_up.shape[1] // 2
    gate, up = gate_up[:, :half], gate_up[:, half:]
    cdf = 0.5 * (1.0 + lax.erf(gate * math.sqrt(0.5)))
    density = jnp.exp(-0.5 * gate * gate) * (1.0 / math.sqrt(2.0 * math.pi))
    d_gate = d_mixed * up * (cdf + gate * density)
    d_up = d_mixed * gate * cdf
    d_gate_up = jnp.concatenate([d_gate, d_up], 1).astype(BF)
    d_normed = dot_bt(d_gate_up, weights["mlp_in"])
    gain_grad = jnp.sum(d_normed * xhat, 0)
    d_middle = upstream + norm_back(d_normed, weights["gain_mlp"], xhat, scale)
    d_attn = d_middle.astype(BF)
    d_attended = dot_bt(d_attn, weights["attn"]).astype(BF)
    return d_middle, d_attended, (normed, d_gate_up, mixed, d_mlp, d_attn), gain_grad


def finish_backward(d_middle, d_projected, layer_in, weights):
    d_normed = dot_bt(d_projected, weights["qkv"])
    xhat, scale = moments(layer_in)
    gain_grad = jnp.sum(d_normed * xhat, 0)
    grad = d_middle + norm_back(d_normed, weights["gain_attn"], xhat, scale)
    return grad.astype(BF), gain_grad


def neighbours(count, step):
    return [
        (i, i + step)
        for i in range(count)
        if 0 <= i + step < count and i // GROUP == (i + step) // GROUP
    ]


def with_halo(rows, count):
    before = lax.ppermute(rows, "dp", neighbours(count, 1))
    after = lax.ppermute(rows, "dp", neighbours(count, -1))
    return jnp.concatenate([before, rows, after], 1)


def local_scores(queries, keys, visible):
    raw = jnp.einsum("bqhd,bkhd->bhqk", queries, keys, preferred_element_type=F32) * SCALE
    scores = jnp.where(visible[:, None], raw, masked_score)
    peak = jnp.max(scores, -1, keepdims=True)
    weights = jnp.exp(scores - peak)
    return weights / jnp.sum(weights, -1, keepdims=True)


def heads_of(rows):
    return rows.reshape(2, -1, HEADS, HEAD_DIM)


def local_forward(queries, keys_values, visible):
    width = queries.shape[1]
    keys, values = keys_values[..., :width], keys_values[..., width:]
    probs = local_scores(heads_of(queries), heads_of(keys), visible)
    attended = jnp.einsum(
        "bhqk,bkhd->bqhd", probs.astype(BF), heads_of(values), preferred_element_type=F32
    )
    return attended.reshape(queries.shape).astype(BF), probs


def local_backward(d_attended, probs, queries, keys_values, count):
    rows, width = queries.shape
    row_count = rows // 2
    keys, values = keys_values[..., :width], keys_values[..., width:]
    d_heads = heads_of(d_attended)
    d_probs = jnp.einsum(
        "bqhd,bkhd->bhqk", d_heads, heads_of(values), preferred_element_type=F32
    )
    delta = jnp.sum(probs * d_probs, -1, keepdims=True)
    d_scores = (probs * (d_probs - delta)).astype(BF)
    d_queries = (
        jnp.einsum("bhqk,bkhd->bqhd", d_scores, heads_of(keys), preferred_element_type=F32) * SCALE
    )
    d_keys = (
        jnp.einsum("bhqk,bqhd->bkhd", d_scores, heads_of(queries), preferred_element_type=F32)
        * SCALE
    )
    d_values = jnp.einsum(
        "bhqk,bqhd->bkhd", probs.astype(BF), d_heads, preferred_element_type=F32
    )
    d_kv = jnp.concatenate(
        [d_keys.reshape(2, -1, width), d_values.reshape(2, -1, width)], 2
    )
    to_before = d_kv[:, :row_count].astype(BF)
    to_after = d_kv[:, 2 * row_count :].astype(BF)
    from_after = lax.ppermute(to_before, "dp", neighbours(count, -1))
    from_before = lax.ppermute(to_after, "dp", neighbours(count, 1))
    d_kv = d_kv[:, row_count : 2 * row_count] + from_after.astype(F32) + from_before.astype(F32)
    d_kv = d_kv.reshape(rows, 2 * width)
    return d_queries.reshape(rows, width), d_kv[:, :width], d_kv[:, width:]


def split_heads(rows):
    row_count = rows.shape[0] // 2
    half = row_count // 2
    parts = rows.reshape(2, row_count, 4, 3, HEAD_DIM)
    own = parts[:, :, :, 0::2].transpose(0, 2, 3, 1, 4)
    shared = parts[:, :, :, 1].reshape(2, 2, half, 4, HEAD_DIM).transpose(0, 3, 1, 2, 4)
    return jnp.concatenate([own, shared], 3).reshape(GROUP, row_count + half, HEAD_DIM)


def join_heads(blocks):
    row_count = blocks.shape[1] * 2 // 3
    half = row_count // 2
    parts = blocks.reshape(2, 4, 2, row_count + half, HEAD_DIM)
    own = parts[:, :, :, :row_count].transpose(0, 3, 1, 2, 4)
    shared = parts[:, :, :, row_count:].transpose(0, 2, 3, 1, 4).reshape(2, row_count, 4, HEAD_DIM)
    rows = jnp.stack([own[:, :, :, 0], shared, own[:, :, :, 1]], 3)
    return rows.reshape(2 * row_count, HEADS * HEAD_DIM)


def fold(blocks):
    half = blocks.shape[1] // 2
    return jnp.concatenate([blocks[:, :half], blocks[:, half:]], 2)


def unfold(blocks):
    return jnp.concatenate([blocks[..., :HEAD_DIM], blocks[..., HEAD_DIM:]], 1)


def exchange(blocks, count):
    groups = [list(range(s, s + GROUP)) for s in range(0, count, GROUP)]
    return lax.all_to_all(blocks, "dp", 0, 0, axis_index_groups=groups)


def other_core(rows, count):
    return lax.ppermute(rows, "dp", [(i, i ^ 1) for i in range(count)])


def pack_three(first, second, third):
    return jnp.concatenate([jnp.concatenate([first, second], 2), fold(third)], 1)


def unpack_three(blocks):
    rows = blocks.shape[1] * 2 // 3
    pair = blocks[:, :rows]
    return pair[..., :HEAD_DIM], pair[..., HEAD_DIM:], unfold(blocks[:, rows:])


def own_rows(blocks):
    row_count = blocks.shape[1] * 2 // 3
    return blocks[:, :row_count].reshape(-1, HEAD_DIM)


def shared_rows(blocks):
    row_count = blocks.shape[1] * 2 // 3
    return blocks[:, row_count:].reshape(-1, HEAD_DIM)


def to_blocks(own, shared):
    return jnp.concatenate(
        [own.reshape(GROUP, -1, HEAD_DIM), shared.reshape(GROUP, -1, HEAD_DIM)], 1
    )


def soft_attend(queries, keys, values, query_seg, key_seg):
    raw = dot_bt(queries, keys) * SCALE
    scores = jnp.where(query_seg[:, None] == key_seg[None, :], raw, masked_score)
    peak = jnp.max(scores, -1, keepdims=True)
    weights = jnp.exp(scores - peak)
    probs = weights / jnp.sum(weights, -1, keepdims=True)
    return dot(probs.astype(BF), values), probs


def soft_back(d_out, probs, queries, keys, values):
    d_probs = dot_bt(d_out, values)
    delta = jnp.sum(probs * d_probs, -1, keepdims=True)
    d_scores = (probs * (d_probs - delta)).astype(BF)
    d_queries = dot(d_scores, keys) * SCALE
    d_keys = dot_at(d_scores, queries) * SCALE
    d_values = dot_at(probs.astype(BF), d_out)
    return d_queries, d_keys, d_values


def global_forward(queries, keys, values, own_seg, shared_seg, count):
    sent = pack_three(split_heads(queries), split_heads(keys), split_heads(values))
    got_q, got_k, got_v = unpack_three(exchange(sent, count))
    shared_kv = jnp.concatenate([shared_rows(got_k), shared_rows(got_v)], 1)
    both_kv = jnp.concatenate([shared_kv, other_core(shared_kv, count)], 0)
    own_in = (own_rows(got_q), own_rows(got_k), own_rows(got_v))
    shared_in = (shared_rows(got_q), both_kv[:, :HEAD_DIM], both_kv[:, HEAD_DIM:])
    own_out, own_probs = soft_attend(*own_in, own_seg, own_seg)
    shared_out, shared_probs = soft_attend(
        *shared_in, shared_seg[: shared_seg.shape[0] // 2], shared_seg
    )
    back = fold(to_blocks(own_out.astype(BF), shared_out.astype(BF)))
    attended = join_heads(unfold(exchange(back, count)))
    return attended, (own_in, own_probs, shared_in, shared_probs)


def global_backward(d_attended, saved, count):
    own_in, own_probs, shared_in, shared_probs = saved
    got = unfold(exchange(fold(split_heads(d_attended)), count))
    own_grads = soft_back(own_rows(got), own_probs, *own_in)
    shared_q, shared_k, shared_v = soft_back(shared_rows(got), shared_probs, *shared_in)
    d_kv = jnp.concatenate([shared_k, shared_v], 1)
    half = d_kv.shape[0] // 2
    d_kv = d_kv[:half] + other_core(d_kv[half:].astype(BF), count).astype(F32)
    shared_grads = (shared_q, d_kv[:, :HEAD_DIM], d_kv[:, HEAD_DIM:])
    blocks = [
        to_blocks(own.astype(BF), shared.astype(BF))
        for own, shared in zip(own_grads, shared_grads)
    ]
    back = unpack_three(exchange(pack_three(*blocks), count))
    return tuple(join_heads(part).astype(F32) for part in back)


def to_other_section(rows, step):
    return lax.ppermute(rows, "section", [(0, 1)] if step > 0 else [(1, 0)])


def partner(rows, apart, count):
    return lax.ppermute(rows, "dp", [(i, i ^ apart) for i in range(count)])


def gather_group(piece, group_pos, count):
    pieces = {0: piece}
    for apart in (4, 8, 12):
        pieces[apart] = partner(piece, apart, count)
    for apart in (0, 4, 8, 12):
        pieces[apart + 2] = partner(pieces[apart], 2, count)
    for apart in range(0, GROUP, 2):
        pieces[apart + 1] = partner(pieces[apart], 1, count)
    whole = jnp.zeros((GROUP,) + piece.shape, piece.dtype)
    for apart, item in pieces.items():
        start = (group_pos ^ apart,) + (0,) * piece.ndim
        whole = lax.dynamic_update_slice(whole, item[None], start)
    return whole


def gather_rows(piece, group_pos, count):
    whole = gather_group(piece, group_pos, count)
    if count > GROUP:
        groups = [list(range(s, count, GROUP)) for s in range(GROUP)]
        whole = lax.all_gather(whole, "dp", axis=0, tiled=True, axis_index_groups=groups)
    return whole.reshape(-1, piece.shape[-1])


def plane_rows(rows, group_pos, count):
    parts = rows.reshape(count // GROUP, 4, 4, *rows.shape[1:])
    place = group_pos % 4
    taken = []
    for apart in range(4):
        block = lax.dynamic_index_in_dim(parts, place ^ apart, 2, keepdims=False)
        taken.append(partner(block, apart, count) if apart else block)
    return jnp.concatenate(taken, -1).swapaxes(0, 1)


def plane_tokens(rows, count):
    across = partner(rows, 2, count)
    beside = partner(rows, 1, count)
    return jnp.concatenate([rows, beside, across, partner(across, 1, count)], 0)


def plane_product(left, right):
    planes, groups, rows, tokens = left.shape
    product = dot(left.reshape(-1, tokens), right)
    return product.reshape(planes, groups, rows, -1)


def stacked_columns(blocks, width):
    return jnp.concatenate(
        [blocks[..., c : c + width] for c in range(0, blocks.shape[-1], width)], -2
    )


def sum_planes(blocks, count):
    groups = [
        [s + 4 * z + k for z in range(4)] for s in range(0, count, GROUP) for k in range(4)
    ]
    got = lax.all_to_all(blocks.astype(BF), "dp", 0, 0, axis_index_groups=groups)
    total = jnp.sum(got.astype(F32), 0)
    if count > GROUP:
        apart = [list(range(s, count, GROUP)) for s in range(GROUP)]
        total = lax.psum_scatter(total, "dp", scatter_dimension=0, axis_index_groups=apart)
        return total
    return total[0]


def on_device(
    tokens_in,
    segment_ids,
    out_grad,
    qkv_weight,
    attn_out_weight,
    mlp_in_weight,
    mlp_out_weight,
    attn_gain,
    mlp_gain,
):
    lower = lax.axis_index("section") == 0
    count = lax.axis_size("dp")
    replica = lax.axis_index("dp")
    group_pos = replica % GROUP
    micro_count, row_count, width = tokens_in.shape
    shard = qkv_weight.shape[1]
    wide = mlp_out_weight.shape[1] * width // shard
    own_ids = segment_ids.reshape(-1)
    id_columns = -(-own_ids.size // shard)
    ids = jnp.pad(own_ids.astype(BF), (0, id_columns * shard - own_ids.size))
    extra = jnp.concatenate(
        [attn_gain[0][:, None], mlp_gain[0][:, None], ids.reshape(shard, id_columns)], 1
    )
    extra = jnp.pad(extra, ((0, 0), (0, 128 - extra.shape[1])))
    second = lax.all_gather(
        jnp.concatenate(
            [attn_out_weight[0], mlp_in_weight[0], mlp_out_weight[0].reshape(shard, wide)], 1
        ),
        "dp",
        axis=0,
        tiled=True,
    )
    first = gather_rows(jnp.concatenate([qkv_weight[0], extra], 1), group_pos, count)
    weights = {
        "qkv": first[:, : 3 * width],
        "gain_attn": first[:, 3 * width].astype(F32)[None],
        "gain_mlp": first[:, 3 * width + 1].astype(F32)[None],
        "attn": second[:, :width],
        "mlp_in": second[:, width : second.shape[1] - wide],
        "mlp_out": second[:, second.shape[1] - wide :].reshape(-1, width),
    }
    all_ids = first[:, 3 * width + 2 : 3 * width + 2 + id_columns].reshape(count, -1)
    all_ids = lax.dynamic_slice_in_dim(all_ids, replica - group_pos, GROUP, 0)
    all_ids = all_ids[:, : own_ids.size].reshape(GROUP, micro_count, row_count)
    segments = all_ids.swapaxes(0, 1).reshape(micro_count, GROUP * row_count).astype(jnp.int32)

    positions = group_pos * row_count + jnp.arange(row_count)
    local_tables = angles(positions, local_log_base)
    global_tables = angles(positions, global_log_base)

    key_pos = positions[0] - row_count + jnp.arange(3 * row_count)
    around = jnp.pad(segments, ((0, 0), (row_count, row_count)), constant_values=-1)
    key_seg = lax.dynamic_slice_in_dim(around, group_pos * row_count, 3 * row_count, 1)
    visible = (segment_ids[:, :, None] == key_seg[:, None, :]) & (
        jnp.abs(positions[:, None] - key_pos[None, :]) <= HALF_WIN
    )[None]

    own_seg = lax.dynamic_index_in_dim(segments, group_pos // 8, 0, keepdims=False)
    halves = own_seg.reshape(GROUP, 2, row_count // 2)
    mine = lax.dynamic_index_in_dim(halves, group_pos % 2, 1, keepdims=False).reshape(-1)
    theirs = lax.dynamic_index_in_dim(halves, 1 - group_pos % 2, 1, keepdims=False).reshape(-1)
    shared_seg = jnp.concatenate([mine, theirs])

    in_0 = tokens_in.reshape(-1, width).astype(F32)
    normed_0, q_0, k_0, v_0 = project(in_0, weights, local_tables)
    kv_0 = with_halo(jnp.concatenate([k_0, v_0], 1).reshape(2, row_count, 2 * width), count)
    att_0, probs_0 = local_forward(q_0, kv_0, visible)
    out_0, saved_0 = finish_forward(in_0, att_0, weights)

    in_1 = to_other_section(out_0, 1).astype(F32)
    normed_1, q_1, k_1, v_1 = project(in_1, weights, global_tables)
    att_1, kept_1 = global_forward(q_1, k_1, v_1, own_seg, shared_seg, count)
    out_1, saved_1 = finish_forward(in_1, att_1, weights)

    n1, att, n2, mixed = (
        jnp.where(lower, a, b).T.reshape(count, -1, micro_count * row_count)
        for a, b in (
            (normed_0, normed_1),
            (att_0, att_1),
            (saved_0[0], saved_1[0]),
            (saved_0[2], saved_1[2]),
        )
    )
    left = plane_rows(jnp.concatenate([n1, att, n2, mixed], 1), group_pos, count)

    up_1 = out_grad.reshape(-1, width).astype(F32)
    d_mid_1, d_att_1, ops_1, gain_mlp_1 = start_backward(up_1, saved_1, weights)
    d_q, d_k, d_v = global_backward(d_att_1, kept_1, count)
    d_proj_1 = jnp.concatenate(
        [unrotate(d_q, global_tables), unrotate(d_k, global_tables), d_v], 1
    ).astype(BF)
    grad_1, gain_attn_1 = finish_backward(d_mid_1, d_proj_1, in_1, weights)

    up_0 = to_other_section(grad_1, -1).astype(F32)
    d_mid_0, d_att_0, ops_0, gain_mlp_0 = start_backward(up_0, saved_0, weights)
    _, d_gu, _, d_mlp, d_attn = (jnp.where(lower, a, b) for a, b in zip(ops_0, ops_1))
    right = plane_tokens(jnp.concatenate([d_gu, d_mlp, d_attn], 1), count)
    inner = d_gu.shape[1]
    early = jnp.concatenate(
        [
            stacked_columns(
                plane_product(left[:, :, 2 * shard : 3 * shard], right[:, :inner]), width
            ),
            plane_product(left[:, :, 3 * shard :], right[:, inner : inner + width]),
            plane_product(left[:, :, shard : 2 * shard], right[:, inner + width :]),
        ],
        2,
    )
    early = sum_planes(early, count)
    d_q, d_k, d_v = local_backward(d_att_0, probs_0, q_0, kv_0, count)
    d_proj_0 = jnp.concatenate(
        [unrotate(d_q, local_tables), unrotate(d_k, local_tables), d_v], 1
    ).astype(BF)
    d_proj = jnp.where(lower, d_proj_0, d_proj_1)
    late = stacked_columns(
        plane_product(left[:, :, :shard], plane_tokens(d_proj, count)), width
    )
    grad_0, gain_attn_0 = finish_backward(d_mid_0, d_proj_0, in_0, weights)

    gains = jnp.where(
        lower, jnp.stack([gain_attn_0, gain_mlp_0]), jnp.stack([gain_attn_1, gain_mlp_1])
    )
    gains = gains + partner(gains, 1, count)
    gains = gains + partner(gains, 2, count)
    gains = gains.reshape(2, count // GROUP, 4, 4, shard)
    gains = lax.dynamic_index_in_dim(gains, group_pos % 4, 3, keepdims=False)
    gains = jnp.pad(
        gains.transpose(2, 1, 0, 3), ((0, 0), (0, 0), (0, 14), (0, width - shard))
    )
    late = sum_planes(jnp.concatenate([late, gains], 2), count)

    def columns(rows, parts):
        return jnp.concatenate([rows[p * shard : (p + 1) * shard] for p in range(parts)], 1)[None]

    parts = inner // width
    return (
        jnp.where(lower, out_0, out_1).reshape(1, micro_count, row_count, width),
        jnp.where(lower, grad_0, grad_1).reshape(1, micro_count, row_count, width),
        columns(late, 3),
        early[early.shape[0] - shard :][None],
        columns(early, parts),
        early[parts * shard : early.shape[0] - shard][None],
        late[3 * shard, :shard][None],
        late[3 * shard + 1, :shard][None],
    )


def solution(mesh):
    in_specs = (
        P(None, "dp", None),
        P(None, "dp"),
        P(None, "dp", None),
        P("section", "dp", None),
        P("section", "dp", None),
        P("section", "dp", None),
        P("section", "dp", None),
        P("section", "dp"),
        P("section", "dp"),
    )
    out_specs = (
        P("section", None, "dp", None),
        P("section", None, "dp", None),
        P("section", "dp", None),
        P("section", "dp", None),
        P("section", "dp", None),
        P("section", "dp", None),
        P("section", "dp"),
        P("section", "dp"),
    )
    return jax.shard_map(
        on_device, mesh=mesh, in_specs=in_specs, out_specs=out_specs, check_vma=False
    )
```

```python
import math

import jax
import jax.numpy as jnp
from jax import lax
from jax.experimental import pallas as pl
from jax.experimental.pallas import tpu as pltpu
from jax.sharding import PartitionSpec as P

HEAD_DIM = 64
GROUP = 16
HALF_WIN = 64
LANES = 128
TILE = 256

local_log_base = math.log(10000.0)
global_log_base = math.log(160000.0)
masked_score = -1e30
SCALE = 1.0 / math.sqrt(HEAD_DIM)
BF = jnp.bfloat16
F32 = jnp.float32


def dot(left, right):
    return jnp.dot(left, right, preferred_element_type=F32)


def dot_bt(left, right):
    return lax.dot_general(left, right, (((1,), (1,)), ((), ())), preferred_element_type=F32)


def dot_at(left, right):
    return lax.dot_general(left, right, (((0,), (0,)), ((), ())), preferred_element_type=F32)


def moments(values):
    center = values - jnp.mean(values, -1, keepdims=True)
    scale = lax.rsqrt(jnp.mean(center * center, -1, keepdims=True) + 1e-05)
    return center * scale, scale


def norm_back(grad_out, gain_row, xhat, scale):
    scaled = grad_out * gain_row
    mean_grad = jnp.mean(scaled, -1, keepdims=True)
    mean_dot = jnp.mean(scaled * xhat, -1, keepdims=True)
    return (scaled - mean_grad - xhat * mean_dot) * scale


def angles(positions, log_base):
    half_dim = HEAD_DIM // 2
    fraction = (2 * jnp.arange(half_dim)).astype(F32) / HEAD_DIM
    inverse = jnp.exp(-fraction * log_base)
    table = positions.astype(F32)[:, None] * inverse[None, :]
    cosine, sine = jnp.cos(table), jnp.sin(table)
    none = jnp.zeros_like(sine)
    cosine = jnp.concatenate([cosine, cosine], 1)
    to_first = jnp.concatenate([-sine, none], 1)
    to_second = jnp.concatenate([none, sine], 1)
    return jnp.tile(jnp.stack([cosine, to_first, to_second]), (1, 2, 2))


def on_core(body, outs, args, scratch=()):
    return pl.pallas_call(
        body,
        out_shape=[jax.ShapeDtypeStruct(shape, dtype) for shape, dtype in outs],
        in_specs=[pl.BlockSpec(memory_space=pltpu.VMEM)] * len(args),
        out_specs=[pl.BlockSpec(memory_space=pltpu.VMEM)] * len(outs),
        scratch_shapes=scratch,
        compiler_params=pltpu.CompilerParams(vmem_limit_bytes=48 * 2**20),
    )(*args)


def low_lanes():
    return lax.broadcasted_iota(jnp.int32, (1, LANES), 1) < HEAD_DIM


def swap(chunk):
    return pltpu.roll(chunk, HEAD_DIM, 1)


def chunks_of(rows):
    return [rows[:, c : c + LANES] for c in range(0, rows.shape[1], LANES)]


def rotate(chunk, tables):
    cosine, to_first, to_second = tables
    quarter = HEAD_DIM // 2
    return (
        chunk * cosine
        + pltpu.roll(chunk, LANES - quarter, 1) * to_first
        + pltpu.roll(chunk, quarter, 1) * to_second
    )


def unrotate(chunk, tables):
    cosine, to_first, to_second = tables
    quarter = HEAD_DIM // 2
    return (
        chunk * cosine
        - pltpu.roll(chunk, LANES - quarter, 1) * to_first
        - pltpu.roll(chunk, quarter, 1) * to_second
    )


def low_and_high(chunks):
    swapped = [swap(chunk) for chunk in chunks]
    low = [(swapped if h % 2 else chunks)[h // 2] for h in range(2 * len(chunks))]
    high = [(chunks if h % 2 else swapped)[h // 2] for h in range(2 * len(chunks))]
    return low, high


def targets():
    for d in range(GROUP):
        micro, chip, half = d // 8, d % 8 // 2, d % 2
        yield d, micro, 3 * chip + 2 * half, 3 * chip + 1, half


def pack_folded(chunks, ref, base):
    low, high = low_and_high(chunks)
    first = low_lanes()
    rows = chunks[0].shape[0] // 2
    half, fold = rows // 2, rows * 3 // 4
    for d, micro, own, shared, side in targets():
        start = micro * rows
        part = start + side * half
        upper = jnp.concatenate(
            [high[own][start + fold : start + rows], high[shared][part : part + half]], 0
        )
        ref[d, base : base + fold] = jnp.where(
            first, low[own][start : start + fold], upper
        ).astype(BF)


def pack_pairs(lefts, rights, ref):
    low, high = low_and_high(lefts)[0], low_and_high(rights)[1]
    first = low_lanes()
    rows = lefts[0].shape[0] // 2
    half = rows // 2
    for d, micro, own, shared, side in targets():
        start = micro * rows
        part = start + side * half
        ref[d, 0:rows] = jnp.where(
            first, low[own][start : start + rows], high[own][start : start + rows]
        ).astype(BF)
        ref[d, rows : rows + half] = jnp.where(
            first, low[shared][part : part + half], high[shared][part : part + half]
        ).astype(BF)


def unpack_folded(ref, base, rows):
    first = low_lanes()
    fold = rows * 3 // 4
    low, high = {}, {}
    shared_parts = {}
    for d, micro, own, shared, side in targets():
        block = ref[d, base : base + fold].astype(F32)
        mine = jnp.concatenate([block, swap(block[: rows - fold])], 0)
        if own % 2:
            high[micro, own] = swap(mine)
        else:
            low[micro, own] = mine
        shared_parts[micro, shared, side] = block[rows - fold :]
        if side:
            both = jnp.concatenate([shared_parts[micro, shared, 0], block[rows - fold :]], 0)
            if shared % 2:
                high[micro, shared] = both
            else:
                low[micro, shared] = swap(both)
    heads = GROUP // 4 * 3
    return [
        jnp.concatenate(
            [jnp.where(first, low[m, h], high[m, h + 1]) for m in range(2)], 0
        )
        for h in range(0, heads, 2)
    ]


def unpack_pairs(ref, rows):
    first = low_lanes()
    half = rows // 2
    pairs = {}
    parts = {}
    for d, micro, own, shared, side in targets():
        pairs[micro, own] = ref[d, 0:rows].astype(F32)
        parts[side] = ref[d, rows : rows + half].astype(F32)
        if side:
            pairs[micro, shared] = jnp.concatenate([parts[0], parts[1]], 0)
    heads = GROUP // 4 * 3
    lefts, rights = [], []
    for h in range(0, heads, 2):
        even, odd = [pairs[m, h] for m in range(2)], [pairs[m, h + 1] for m in range(2)]
        lefts.append(
            jnp.concatenate([jnp.where(first, a, swap(b)) for a, b in zip(even, odd)], 0)
        )
        rights.append(
            jnp.concatenate([jnp.where(first, swap(a), b) for a, b in zip(even, odd)], 0)
        )
    return lefts, rights


def mlp_forward(layer_in, attended, gain, wide_ref, out_ref):
    width = layer_in.shape[1]
    inner = wide_ref.shape[1] - width - out_ref.shape[0] * width // wide_ref.shape[0]
    middle = layer_in + dot(attended, wide_ref[:, :width])
    xhat, _ = moments(middle)
    normed = (xhat * gain).astype(BF)
    gate_up = dot(normed, wide_ref[:, width : width + inner])
    gate, up = gate_up[:, : inner // 2], gate_up[:, inner // 2 :]
    cdf = 0.5 * (1.0 + lax.erf(gate * math.sqrt(0.5)))
    mixed = (gate * cdf * up).astype(BF)
    result = (middle + dot(mixed, out_ref[...])).astype(BF)
    return middle, normed, gate, up, mixed, result


def mlp_backward(upstream, middle, gate, up, gain, wide_ref, out_ref):
    width = middle.shape[1]
    inner = 2 * gate.shape[1]
    d_mixed = dot_bt(upstream, out_ref[...])
    cdf = 0.5 * (1.0 + lax.erf(gate * math.sqrt(0.5)))
    density = jnp.exp(-0.5 * gate * gate) * (1.0 / math.sqrt(2.0 * math.pi))
    d_gate = d_mixed * up * (cdf + gate * density)
    d_up = d_mixed * gate * cdf
    d_gate_up = jnp.concatenate([d_gate.astype(BF), d_up.astype(BF)], 1)
    d_normed = dot_bt(d_gate_up, wide_ref[:, width : width + inner])
    xhat, scale = moments(middle)
    gain_grad = jnp.sum(d_normed * xhat, 0, keepdims=True)
    d_middle = upstream.astype(F32) + norm_back(d_normed, gain, xhat, scale)
    d_attn = d_middle.astype(BF)
    d_attended = dot_bt(d_attn, wide_ref[:, :width])
    return d_gate_up, gain_grad, d_middle, d_attn, d_attended


def project(x_ref, gain_ref, first_ref, table_ref, normed_ref):
    width = x_ref.shape[1]
    xhat, _ = moments(x_ref[...].astype(F32))
    normed = (xhat * gain_ref[...]).astype(BF)
    normed_ref[...] = normed
    tables = [table_ref[i] for i in range(3)]
    queries = chunks_of(dot(normed, first_ref[:, :width]))
    keys = chunks_of(dot(normed, first_ref[:, width : 2 * width]))
    values = dot(normed, first_ref[:, 2 * width : 3 * width])
    return [rotate(c, tables) for c in queries], [rotate(c, tables) for c in keys], values


def input_backward(d_middle, d_projected, x_ref, gain_ref, first_ref, grad_ref, gain_out_ref):
    d_normed = dot_bt(d_projected, first_ref[:, : d_projected.shape[1]])
    xhat, scale = moments(x_ref[...].astype(F32))
    gain_out_ref[...] = jnp.sum(d_normed * xhat, 0, keepdims=True)
    grad_ref[...] = (d_middle + norm_back(d_normed, gain_ref[...], xhat, scale)).astype(BF)


def local_project_body(x_ref, gain_ref, first_ref, table_ref, normed_ref, q_ref, kv_ref):
    queries, keys, values = project(x_ref, gain_ref, first_ref, table_ref, normed_ref)
    width = values.shape[1]
    for j, (q, k) in enumerate(zip(queries, keys)):
        q_ref[:, LANES * j : LANES * (j + 1)] = q.astype(BF)
        kv_ref[:, LANES * j : LANES * (j + 1)] = k.astype(BF)
    kv_ref[:, width:] = values.astype(BF)


def two_heads(chunk):
    first = low_lanes()
    wide = chunk.astype(F32)
    return jnp.concatenate([jnp.where(first, wide, 0.0), jnp.where(first, 0.0, wide)], 0)


def pick_heads(rows):
    half = rows.shape[0] // 2
    return jnp.where(low_lanes(), rows[:half], rows[half:])


def local_parts(q_ref, before_ref, own_ref, after_ref):
    rows = q_ref.shape[0] // 2
    width = q_ref.shape[1]
    for micro in range(2):
        for j in range(width // LANES):
            here = slice(micro * rows, (micro + 1) * rows)
            lanes = slice(LANES * j, LANES * (j + 1))
            more = slice(width + LANES * j, width + LANES * (j + 1))
            keys, values = (
                jnp.concatenate([ref[here, part] for ref in (before_ref, own_ref, after_ref)], 0)
                for part in (lanes, more)
            )
            queries = (two_heads(q_ref[here, lanes]) * SCALE).astype(BF)
            yield micro * (width // LANES) + j, micro, here, lanes, more, queries, keys, values


def local_forward_body(q_ref, before_ref, own_ref, after_ref, bias_ref, att_ref, total_ref):
    parts = local_parts(q_ref, before_ref, own_ref, after_ref)
    for index, micro, here, lanes, _, queries, keys, values in parts:
        scores = dot_bt(keys, queries) + bias_ref[micro]
        peak = jnp.max(scores, 0, keepdims=True)
        weights = jnp.exp(scores - peak)
        total = jnp.sum(weights, 0, keepdims=True)
        total_ref[index] = peak + jnp.log(total)
        probs = (weights * (1.0 / total)).astype(BF)
        att_ref[here, lanes] = pick_heads(dot_at(probs, values)).astype(BF)


def local_backward_body(
    q_ref, before_ref, own_ref, after_ref, bias_ref, total_ref, d_ref, table_ref,
    dq_ref, d_own_ref, d_before_ref, d_after_ref,
):
    tables = [table_ref[i] for i in range(3)]
    parts = local_parts(q_ref, before_ref, own_ref, after_ref)
    rows = q_ref.shape[0] // 2
    for index, micro, here, lanes, more, queries, keys, values in parts:
        d_out = two_heads(d_ref[here, lanes]).astype(BF)
        probs = jnp.exp(dot_bt(keys, queries) + bias_ref[micro] - total_ref[index])
        d_probs = dot_bt(values, d_out)
        product = probs * d_probs
        delta = jnp.sum(product, 0, keepdims=True)
        d_scores = (product - probs * delta).astype(BF)
        d_queries = pick_heads(dot_at(d_scores, keys)) * SCALE
        local_tables = [table[here] for table in tables]
        dq_ref[here, lanes] = unrotate(d_queries, local_tables).astype(BF)
        for part, grads in ((lanes, dot(d_scores, queries)), (more, dot(probs.astype(BF), d_out))):
            d_before_ref[here, part] = grads[:rows].astype(BF)
            d_own_ref[here, part] = grads[rows : 2 * rows]
            d_after_ref[here, part] = grads[2 * rows :].astype(BF)


def local_join_body(dq_ref, own_ref, low_ref, high_ref, table_ref, out_ref):
    tables = [table_ref[i] for i in range(3)]
    width = dq_ref.shape[1]
    out_ref[:, :width] = dq_ref[...]
    total = own_ref[...] + low_ref[...].astype(F32) + high_ref[...].astype(F32)
    for j, chunk in enumerate(chunks_of(total[:, :width])):
        start = width + LANES * j
        out_ref[:, start : start + LANES] = unrotate(chunk, tables).astype(BF)
    out_ref[:, 2 * width :] = total[:, width:].astype(BF)


def local_middle_body(
    x_ref, att_ref, gain_ref, wide_ref, w_out_ref, out_ref, normed_ref, mixed_ref, middle_ref, gate_up_ref
):
    middle, normed, gate, up, mixed, result = mlp_forward(
        x_ref[...].astype(F32), att_ref[...], gain_ref[...], wide_ref, w_out_ref
    )
    out_ref[...] = result
    normed_ref[...] = normed
    mixed_ref[...] = mixed
    middle_ref[...] = middle
    half = gate.shape[1]
    gate_up_ref[:, :half] = gate
    gate_up_ref[:, half:] = up


def local_back_middle_body(
    up_ref, middle_ref, gate_up_ref, gain_ref, wide_ref, w_out_ref,
    d_gate_up_ref, gain_out_ref, d_middle_ref, d_attn_ref, d_att_ref,
):
    half = gate_up_ref.shape[1] // 2
    d_gate_up, gain_grad, d_middle, d_attn, d_attended = mlp_backward(
        up_ref[...], middle_ref[...], gate_up_ref[:, :half], gate_up_ref[:, half:],
        gain_ref[...], wide_ref, w_out_ref,
    )
    d_gate_up_ref[...] = d_gate_up
    gain_out_ref[...] = gain_grad
    d_middle_ref[...] = d_middle
    d_attn_ref[...] = d_attn
    d_att_ref[...] = d_attended.astype(BF)


def input_backward_body(
    d_middle_ref, d_proj_ref, x_ref, gain_ref, first_ref, grad_ref, gain_out_ref
):
    input_backward(
        d_middle_ref[...], d_proj_ref[...], x_ref, gain_ref, first_ref, grad_ref, gain_out_ref
    )


def global_project_body(x_ref, gain_ref, first_ref, table_ref, normed_ref, sent_ref):
    queries, keys, values = project(x_ref, gain_ref, first_ref, table_ref, normed_ref)
    pack_pairs(queries, keys, sent_ref)
    pack_folded(chunks_of(values), sent_ref, sent_ref.shape[1] * 2 // 3)


def flat(blocks):
    return blocks.reshape(-1, LANES)


def own_unfolded(ref, base, rows):
    fold = rows * 3 // 4
    block = ref[:, base : base + fold].astype(F32)
    rest = swap(flat(block[:, : rows - fold])).reshape(GROUP, rows - fold, LANES)
    return flat(jnp.concatenate([block, rest], 1))


def shared_unfolded(ref, start, rows):
    return swap(flat(ref[:, start : start + rows // 2].astype(F32)))


def fill_heads(got_ref, other_ref, own_seg_ref, shared_seg_ref, q_scr, k_scr, v_scr):
    rows = got_ref.shape[1] * 4 // 9
    half = rows // 2
    first = low_lanes()
    lane = lax.broadcasted_iota(jnp.int32, (1, LANES), 1) - HEAD_DIM
    own = flat(got_ref[:, 0:rows].astype(F32))
    shared = flat(got_ref[:, rows : rows + half].astype(F32))
    other = flat(other_ref[:, 0:half].astype(F32))
    count = own.shape[0]
    own_hit = lane == own_seg_ref[...]
    shared_hit = lane == shared_seg_ref[...]
    both = jnp.concatenate([shared, other], 0)
    for start, pairs, hit in (
        (0, own, own_hit),
        (count, shared, shared_hit[: count // 2]),
    ):
        marked = jnp.where(hit, 1.0, 0.0)
        q_scr[start : start + pairs.shape[0]] = jnp.where(first, pairs * SCALE, marked).astype(BF)
    for unit, pairs, hit in ((0, own, own_hit), (1, both, shared_hit)):
        marked = jnp.where(hit, 0.0, masked_score)
        k_scr[unit] = jnp.where(first, swap(pairs), marked).astype(BF)
    base = rows + half
    v_scr[0] = jnp.where(first, own_unfolded(got_ref, base, rows), 0.0).astype(BF)
    start = base + rows - rows * 3 // 4
    shared_v = jnp.concatenate(
        [shared_unfolded(got_ref, start, rows), shared_unfolded(other_ref, half, rows)], 0
    )
    v_scr[1] = jnp.where(first, shared_v, 0.0).astype(BF)


def fold_out(own, shared, rows, ref, base):
    fold = rows * 3 // 4
    blocks = own.reshape(GROUP, rows, LANES)
    swapped = swap(own).reshape(GROUP, rows, LANES)
    upper = jnp.concatenate(
        [swapped[:, fold:], swap(shared).reshape(GROUP, rows // 2, LANES)], 1
    )
    ref[:, base : base + fold] = jnp.where(low_lanes(), blocks[:, :fold], upper).astype(BF)


def global_forward_body(
    got_ref, other_ref, own_seg_ref, shared_seg_ref, out_ref, total_ref,
    q_scr, k_scr, v_scr, vt_scr, o_scr,
):
    fill_heads(got_ref, other_ref, own_seg_ref, shared_seg_ref, q_scr, k_scr, v_scr)
    for unit in range(2):
        vt_scr[unit] = v_scr[unit].astype(F32).T.astype(BF)
    count = k_scr.shape[1]

    def step(tile, carry):
        unit = tile // (count // TILE)
        rows = pl.ds(pl.multiple_of(tile * TILE, TILE), TILE)
        scores = dot_bt(k_scr[unit], q_scr[rows])
        peak = jnp.max(scores, 0, keepdims=True)
        weights = jnp.exp(scores - peak)
        total = jnp.sum(weights, 0, keepdims=True)
        total_ref[tile] = peak + jnp.log(total)
        out = dot(vt_scr[unit], weights.astype(BF)) * (1.0 / total)
        o_scr[rows] = out.T
        return carry

    lax.fori_loop(0, q_scr.shape[0] // TILE, step, 0)
    rows = got_ref.shape[1] * 4 // 9
    fold_out(o_scr[:count], o_scr[count:], rows, out_ref, 0)


def global_backward_body(
    got_ref, other_ref, own_seg_ref, shared_seg_ref, total_ref, d_ref, sent_ref, to_other_ref,
    q_scr, k_scr, v_scr, kt_scr, d_scr, dq_scr, dk_scr, dv_scr,
):
    fill_heads(got_ref, other_ref, own_seg_ref, shared_seg_ref, q_scr, k_scr, v_scr)
    first = low_lanes()
    rows = got_ref.shape[1] * 4 // 9
    half = rows // 2
    for unit in range(2):
        keys = jnp.where(first, k_scr[unit].astype(F32), 0.0)
        kt_scr[unit] = keys.T.astype(BF)
    count = k_scr.shape[1]
    d_scr[:count] = jnp.where(first, own_unfolded(d_ref, 0, rows), 0.0).astype(BF)
    d_scr[count:] = jnp.where(
        first, shared_unfolded(d_ref, rows - rows * 3 // 4, rows), 0.0
    ).astype(BF)
    dk_scr[...] = jnp.zeros_like(dk_scr)
    dv_scr[...] = jnp.zeros_like(dv_scr)

    def step(tile, carry):
        unit = tile // (count // TILE)
        here = pl.ds(pl.multiple_of(tile * TILE, TILE), TILE)
        queries, d_out = q_scr[here], d_scr[here]
        probs = jnp.exp(dot_bt(k_scr[unit], queries) - total_ref[tile])
        d_probs = dot_bt(v_scr[unit], d_out)
        product = probs * d_probs
        delta = jnp.sum(product, 0, keepdims=True)
        d_scores = (product - probs * delta).astype(BF)
        dv_scr[unit] += dot(probs.astype(BF), d_out)
        dk_scr[unit] += dot(d_scores, queries)
        dq_scr[here] = dot(kt_scr[unit], d_scores).T * SCALE
        return carry

    lax.fori_loop(0, q_scr.shape[0] // TILE, step, 0)
    mine = count // 2
    own = jnp.where(first, dq_scr[:count], swap(dk_scr[0]))
    sent_ref[:, 0:rows] = own.reshape(GROUP, rows, LANES).astype(BF)
    shared_k, shared_v = dk_scr[1], dv_scr[1]
    shared = jnp.where(first, dq_scr[count:], swap(shared_k[:mine]))
    sent_ref[:, rows : rows + half] = shared.reshape(GROUP, half, LANES).astype(BF)
    fold_out(dv_scr[0], shared_v[:mine], rows, sent_ref, rows + half)
    for place, grads in enumerate((shared_k, shared_v)):
        other = jnp.where(first, 0.0, swap(grads[mine:])).reshape(GROUP, half, LANES)
        to_other_ref[:, place * half : (place + 1) * half] = other.astype(BF)


def global_middle_body(
    got_ref, x_ref, up_ref, gain_ref, wide_ref, w_out_ref,
    out_ref, att_ref, normed_ref, mixed_ref, d_gate_up_ref, gain_out_ref, d_middle_ref, d_attn_ref, sent_ref,
):
    rows = x_ref.shape[0] // 2
    attended = jnp.concatenate([c.astype(BF) for c in unpack_folded(got_ref, 0, rows)], 1)
    att_ref[...] = attended
    gain = gain_ref[...]
    middle, normed, gate, up, mixed, result = mlp_forward(
        x_ref[...].astype(F32), attended, gain, wide_ref, w_out_ref
    )
    out_ref[...] = result
    normed_ref[...] = normed
    mixed_ref[...] = mixed
    d_gate_up, gain_grad, d_middle, d_attn, d_attended = mlp_backward(
        up_ref[...], middle, gate, up, gain, wide_ref, w_out_ref
    )
    d_gate_up_ref[...] = d_gate_up
    gain_out_ref[...] = gain_grad
    d_middle_ref[...] = d_middle
    d_attn_ref[...] = d_attn
    pack_folded(chunks_of(d_attended), sent_ref, 0)


def global_finish_body(
    got_ref, d_middle_ref, x_ref, gain_ref, first_ref, table_ref, d_proj_ref, grad_ref, gain_out_ref
):
    tables = [table_ref[i] for i in range(3)]
    rows = x_ref.shape[0] // 2
    width = x_ref.shape[1]
    d_queries, d_keys = unpack_pairs(got_ref, rows)
    d_values = unpack_folded(got_ref, rows * 3 // 2, rows)
    parts = [unrotate(c, tables).astype(BF) for c in d_queries + d_keys]
    d_projected = jnp.concatenate(parts + [c.astype(BF) for c in d_values], 1)
    d_proj_ref[...] = d_projected
    input_backward(
        d_middle_ref[...], d_projected, x_ref, gain_ref, first_ref, grad_ref, gain_out_ref
    )


def neighbours(count, step):
    return [
        (i, i + step)
        for i in range(count)
        if 0 <= i + step < count and i // GROUP == (i + step) // GROUP
    ]


def exchange(blocks, count):
    groups = [list(range(s, s + GROUP)) for s in range(0, count, GROUP)]
    return lax.all_to_all(blocks, "dp", 0, 0, axis_index_groups=groups)


def to_other_section(rows, step):
    return lax.ppermute(rows, "section", [(0, 1)] if step > 0 else [(1, 0)])


def partner(rows, apart, count):
    return lax.ppermute(rows, "dp", [(i, i ^ apart) for i in range(count)])


def gather_group(piece, group_pos, count):
    pieces = {0: piece}
    for apart in (4, 8, 12):
        pieces[apart] = partner(piece, apart, count)
    for apart in (0, 4, 8, 12):
        pieces[apart + 2] = partner(pieces[apart], 2, count)
    for apart in range(0, GROUP, 2):
        pieces[apart + 1] = partner(pieces[apart], 1, count)
    whole = jnp.zeros((GROUP,) + piece.shape, piece.dtype)
    for apart, item in pieces.items():
        start = (group_pos ^ apart,) + (0,) * piece.ndim
        whole = lax.dynamic_update_slice(whole, item[None], start)
    return whole


def gather_rows(piece, group_pos, count):
    whole = gather_group(piece, group_pos, count)
    if count > GROUP:
        groups = [list(range(s, count, GROUP)) for s in range(GROUP)]
        whole = lax.all_gather(whole, "dp", axis=0, tiled=True, axis_index_groups=groups)
    return whole.reshape(-1, piece.shape[-1])


def plane_rows(rows, group_pos, count):
    parts = rows.reshape(count // GROUP, 4, 4, *rows.shape[1:])
    place = group_pos % 4
    taken = []
    for apart in range(4):
        block = lax.dynamic_index_in_dim(parts, place ^ apart, 2, keepdims=False)
        taken.append(partner(block, apart, count) if apart else block)
    return jnp.concatenate(taken, -1).swapaxes(0, 1)


def plane_tokens(rows, count):
    across = partner(rows, 2, count)
    beside = partner(rows, 1, count)
    return jnp.concatenate([rows, beside, across, partner(across, 1, count)], 0)


def plane_product(left, right):
    planes, groups, rows, tokens = left.shape
    product = dot(left.reshape(-1, tokens), right)
    return product.reshape(planes, groups, rows, -1)


def stacked_columns(blocks, width):
    return jnp.concatenate(
        [blocks[..., c : c + width] for c in range(0, blocks.shape[-1], width)], -2
    )


def sum_planes(blocks, count):
    groups = [
        [s + 4 * z + k for z in range(4)] for s in range(0, count, GROUP) for k in range(4)
    ]
    got = lax.all_to_all(blocks.astype(BF), "dp", 0, 0, axis_index_groups=groups)
    total = jnp.sum(got.astype(F32), 0)
    if count > GROUP:
        apart = [list(range(s, count, GROUP)) for s in range(GROUP)]
        total = lax.psum_scatter(total, "dp", scatter_dimension=0, axis_index_groups=apart)
        return total
    return total[0]


def on_device(
    tokens_in,
    segment_ids,
    out_grad,
    qkv_weight,
    attn_out_weight,
    mlp_in_weight,
    mlp_out_weight,
    attn_gain,
    mlp_gain,
):
    lower = lax.axis_index("section") == 0
    count = lax.axis_size("dp")
    replica = lax.axis_index("dp")
    group_pos = replica % GROUP
    micro_count, row_count, width = tokens_in.shape
    shard = qkv_weight.shape[1]
    wide = mlp_out_weight.shape[1] * width // shard
    own_ids = segment_ids.reshape(-1)
    id_columns = -(-own_ids.size // shard)
    ids = jnp.pad(own_ids.astype(BF), (0, id_columns * shard - own_ids.size))
    extra = jnp.concatenate(
        [attn_gain[0][:, None], mlp_gain[0][:, None], ids.reshape(shard, id_columns)], 1
    )
    extra = jnp.pad(extra, ((0, 0), (0, 128 - extra.shape[1])))
    second = lax.all_gather(
        jnp.concatenate(
            [attn_out_weight[0], mlp_in_weight[0], mlp_out_weight[0].reshape(shard, wide)], 1
        ),
        "dp",
        axis=0,
        tiled=True,
    )
    first = gather_rows(jnp.concatenate([qkv_weight[0], extra], 1), group_pos, count)
    gain_attn = first[:, 3 * width].astype(F32)[None]
    gain_mlp = first[:, 3 * width + 1].astype(F32)[None]
    w_out = second[:, second.shape[1] - wide :].reshape(-1, width)
    all_ids = first[:, 3 * width + 2 : 3 * width + 2 + id_columns].reshape(count, -1)
    all_ids = lax.dynamic_slice_in_dim(all_ids, replica - group_pos, GROUP, 0)
    all_ids = all_ids[:, : own_ids.size].reshape(GROUP, micro_count, row_count)
    segments = all_ids.swapaxes(0, 1).reshape(micro_count, GROUP * row_count).astype(jnp.int32)

    positions = group_pos * row_count + jnp.arange(row_count)
    local_tables = angles(positions, local_log_base)
    global_tables = angles(positions, global_log_base)

    key_pos = positions[0] - row_count + jnp.arange(3 * row_count)
    around = jnp.pad(segments, ((0, 0), (row_count, row_count)), constant_values=-1)
    key_seg = lax.dynamic_slice_in_dim(around, group_pos * row_count, 3 * row_count, 1)
    visible = (key_seg[:, :, None] == segment_ids[:, None, :]) & (
        jnp.abs(positions[None, :] - key_pos[:, None]) <= HALF_WIN
    )[None]
    bias = jnp.tile(jnp.where(visible, 0.0, masked_score), (1, 1, 2))

    own_seg = lax.dynamic_index_in_dim(segments, group_pos // 8, 0, keepdims=False)
    halves = own_seg.reshape(GROUP, 2, row_count // 2)
    mine = lax.dynamic_index_in_dim(halves, group_pos % 2, 1, keepdims=False).reshape(-1)
    theirs = lax.dynamic_index_in_dim(halves, 1 - group_pos % 2, 1, keepdims=False).reshape(-1)
    shared_seg = jnp.concatenate([mine, theirs])[:, None]
    own_seg = own_seg[:, None]

    rows = micro_count * row_count
    inner = second.shape[1] - width - wide
    hidden = w_out.shape[0]
    pairs = rows * width // (row_count * LANES)
    in_0 = tokens_in.reshape(rows, width)
    normed_0, q_0, kv_0 = on_core(
        local_project_body,
        [((rows, width), BF), ((rows, width), BF), ((rows, 2 * width), BF)],
        (in_0, gain_attn, first, local_tables),
    )
    up_pairs, down_pairs = neighbours(count, 1), neighbours(count, -1)
    around_0 = (
        lax.ppermute(kv_0, "dp", up_pairs),
        kv_0,
        lax.ppermute(kv_0, "dp", down_pairs),
    )
    att_0, total_0 = on_core(
        local_forward_body,
        [((rows, width), BF), ((pairs, 1, LANES), F32)],
        (q_0, *around_0, bias),
    )
    out_0, n2_0, mixed_0, middle_0, gate_up_0 = on_core(
        local_middle_body,
        [
            ((rows, width), BF),
            ((rows, width), BF),
            ((rows, hidden), BF),
            ((rows, width), F32),
            ((rows, inner), F32),
        ],
        (in_0, att_0, gain_mlp, second, w_out),
    )

    in_1 = to_other_section(out_0, 1)
    fold = row_count * 3 // 4
    half = row_count // 2
    normed_1, sent = on_core(
        global_project_body,
        [((rows, width), BF), ((GROUP, 3 * fold, LANES), BF)],
        (in_1, gain_attn, first, global_tables),
    )
    got = exchange(sent, count)
    beside = jnp.concatenate(
        [got[:, row_count : row_count + half], got[:, 3 * fold - half :]], 1
    )
    beside = partner(beside, 1, count)
    keys = GROUP * row_count
    tiles = keys * 3 // 2 // TILE
    head_scratch = [
        pltpu.VMEM((keys * 3 // 2, LANES), BF),
        pltpu.VMEM((2, keys, LANES), BF),
        pltpu.VMEM((2, keys, LANES), BF),
        pltpu.VMEM((2, LANES, keys), BF),
    ]
    folded, total_1 = on_core(
        global_forward_body,
        [((GROUP, fold, LANES), BF), ((tiles, 1, TILE), F32)],
        (got, beside, own_seg, shared_seg),
        head_scratch + [pltpu.VMEM((keys * 3 // 2, LANES), F32)],
    )
    folded = exchange(folded, count)

    up_1 = out_grad.reshape(rows, width)
    out_1, att_1, n2_1, mixed_1, d_gu_1, gain_mlp_1, d_mid_1, d_attn_1, sent = on_core(
        global_middle_body,
        [
            ((rows, width), BF),
            ((rows, width), BF),
            ((rows, width), BF),
            ((rows, hidden), BF),
            ((rows, inner), BF),
            ((1, width), F32),
            ((rows, width), F32),
            ((rows, width), BF),
            ((GROUP, fold, LANES), BF),
        ],
        (folded, in_1, up_1, gain_mlp, second, w_out),
    )
    d_folded = exchange(sent, count)
    sent, to_beside = on_core(
        global_backward_body,
        [((GROUP, 3 * fold, LANES), BF), ((GROUP, 2 * half, LANES), BF)],
        (got, beside, own_seg, shared_seg, total_1, d_folded),
        head_scratch
        + [
            pltpu.VMEM((keys * 3 // 2, LANES), BF),
            pltpu.VMEM((keys * 3 // 2, LANES), F32),
            pltpu.VMEM((2, keys, LANES), F32),
            pltpu.VMEM((2, keys, LANES), F32),
        ],
    )
    back = partner(to_beside, 1, count)
    gap = 3 * fold - half - row_count - half
    back = jnp.concatenate(
        [
            jnp.zeros((GROUP, row_count, LANES), BF),
            back[:, :half],
            jnp.zeros((GROUP, gap, LANES), BF),
            back[:, half:],
        ],
        1,
    )
    sent = (sent.astype(F32) + back.astype(F32)).astype(BF)
    got = exchange(sent, count)
    d_proj_1, grad_1, gain_attn_1 = on_core(
        global_finish_body,
        [((rows, 3 * width), BF), ((rows, width), BF), ((1, width), F32)],
        (got, d_mid_1, in_1, gain_attn, first, global_tables),
    )

    n1, att, n2, mixed = (
        jnp.where(lower, a, b).T.reshape(count, -1, micro_count * row_count)
        for a, b in (
            (normed_0, normed_1),
            (att_0, att_1),
            (n2_0, n2_1),
            (mixed_0, mixed_1),
        )
    )
    left = plane_rows(jnp.concatenate([n1, att, n2, mixed], 1), group_pos, count)

    up_0 = to_other_section(grad_1, -1)
    d_gu_0, gain_mlp_0, d_mid_0, d_attn_0, d_att_0 = on_core(
        local_back_middle_body,
        [
            ((rows, inner), BF),
            ((1, width), F32),
            ((rows, width), F32),
            ((rows, width), BF),
            ((rows, width), BF),
        ],
        (up_0, middle_0, gate_up_0, gain_mlp, second, w_out),
    )
    d_gu, d_mlp, d_attn = (
        jnp.where(lower, a, b)
        for a, b in ((d_gu_0, d_gu_1), (up_0, up_1), (d_attn_0, d_attn_1))
    )
    right = plane_tokens(jnp.concatenate([d_gu, d_mlp, d_attn], 1), count)
    early = jnp.concatenate(
        [
            stacked_columns(
                plane_product(left[:, :, 2 * shard : 3 * shard], right[:, :inner]), width
            ),
            plane_product(left[:, :, 3 * shard :], right[:, inner : inner + width]),
            plane_product(left[:, :, shard : 2 * shard], right[:, inner + width :]),
        ],
        2,
    )
    dq_0, d_own, d_before, d_after = on_core(
        local_backward_body,
        [
            ((rows, width), BF),
            ((rows, 2 * width), F32),
            ((rows, 2 * width), BF),
            ((rows, 2 * width), BF),
        ],
        (q_0, *around_0, bias, total_0, d_att_0, local_tables),
    )
    from_after = lax.ppermute(d_before, "dp", down_pairs)
    from_before = lax.ppermute(d_after, "dp", up_pairs)
    (d_proj_0,) = on_core(
        local_join_body,
        [((rows, 3 * width), BF)],
        (dq_0, d_own, from_after, from_before, local_tables),
    )
    d_proj = jnp.where(lower, d_proj_0, d_proj_1)
    d_proj, early = lax.optimization_barrier((d_proj, early))
    early = sum_planes(early, count)
    late = stacked_columns(
        plane_product(left[:, :, :shard], plane_tokens(d_proj, count)), width
    )
    grad_0, gain_attn_0 = on_core(
        input_backward_body,
        [((rows, width), BF), ((1, width), F32)],
        (d_mid_0, d_proj_0, in_0, gain_attn, first),
    )

    gains = jnp.where(
        lower,
        jnp.concatenate([gain_attn_0, gain_mlp_0]),
        jnp.concatenate([gain_attn_1, gain_mlp_1]),
    )
    gains = gains + partner(gains, 1, count)
    gains = gains + partner(gains, 2, count)
    gains = gains.reshape(2, count // GROUP, 4, 4, shard)
    gains = lax.dynamic_index_in_dim(gains, group_pos % 4, 3, keepdims=False)
    gains = jnp.pad(
        gains.transpose(2, 1, 0, 3), ((0, 0), (0, 0), (0, 14), (0, width - shard))
    )
    late = sum_planes(jnp.concatenate([late, gains], 2), count)

    def columns(rows, parts):
        return jnp.concatenate([rows[p * shard : (p + 1) * shard] for p in range(parts)], 1)[None]

    parts = inner // width
    return (
        jnp.where(lower, out_0, out_1).reshape(1, micro_count, row_count, width),
        jnp.where(lower, grad_0, grad_1).reshape(1, micro_count, row_count, width),
        columns(late, 3),
        early[early.shape[0] - shard :][None],
        columns(early, parts),
        early[parts * shard : early.shape[0] - shard][None],
        late[3 * shard, :shard][None],
        late[3 * shard + 1, :shard][None],
    )


def solution(mesh):
    in_specs = (
        P(None, "dp", None),
        P(None, "dp"),
        P(None, "dp", None),
        P("section", "dp", None),
        P("section", "dp", None),
        P("section", "dp", None),
        P("section", "dp", None),
        P("section", "dp"),
        P("section", "dp"),
    )
    out_specs = (
        P("section", None, "dp", None),
        P("section", None, "dp", None),
        P("section", "dp", None),
        P("section", "dp", None),
        P("section", "dp", None),
        P("section", "dp", None),
        P("section", "dp"),
        P("section", "dp"),
    )
    return jax.shard_map(
        on_device, mesh=mesh, in_specs=in_specs, out_specs=out_specs, check_vma=False
    )
```

```python
import math

import jax
import jax.numpy as jnp
from jax import lax
from jax.experimental import pallas as pl
from jax.experimental.pallas import tpu as pltpu
from jax.sharding import PartitionSpec as P

HEAD_DIM = 64
GROUP = 16
HALF_WIN = 64
LANES = 128
TILE = 256

local_log_base = math.log(10000.0)
global_log_base = math.log(160000.0)
masked_score = -1e30
SCALE = 1.0 / math.sqrt(HEAD_DIM)
BF = jnp.bfloat16
F32 = jnp.float32


def dot(left, right):
    return jnp.dot(left, right, preferred_element_type=F32)


def dot_bt(left, right):
    return lax.dot_general(left, right, (((1,), (1,)), ((), ())), preferred_element_type=F32)


def dot_at(left, right):
    return lax.dot_general(left, right, (((0,), (0,)), ((), ())), preferred_element_type=F32)


def moments(values):
    center = values - jnp.mean(values, -1, keepdims=True)
    scale = lax.rsqrt(jnp.mean(center * center, -1, keepdims=True) + 1e-05)
    return center * scale, scale


def norm_back(grad_out, gain_row, xhat, scale):
    scaled = grad_out * gain_row
    mean_grad = jnp.mean(scaled, -1, keepdims=True)
    mean_dot = jnp.mean(scaled * xhat, -1, keepdims=True)
    return (scaled - mean_grad - xhat * mean_dot) * scale


def angles(positions, log_base):
    half_dim = HEAD_DIM // 2
    fraction = (2 * jnp.arange(half_dim)).astype(F32) / HEAD_DIM
    inverse = jnp.exp(-fraction * log_base)
    table = positions.astype(F32)[:, None] * inverse[None, :]
    cosine, sine = jnp.cos(table), jnp.sin(table)
    none = jnp.zeros_like(sine)
    cosine = jnp.concatenate([cosine, cosine], 1)
    to_first = jnp.concatenate([-sine, none], 1)
    to_second = jnp.concatenate([none, sine], 1)
    return jnp.tile(jnp.stack([cosine, to_first, to_second]), (1, 2, 2))


def on_core(body, outs, args, scratch=(), spaces=None):
    return pl.pallas_call(
        body,
        out_shape=[jax.ShapeDtypeStruct(shape, dtype) for shape, dtype in outs],
        in_specs=[
            pl.BlockSpec(memory_space=space) for space in spaces or [pltpu.VMEM] * len(args)
        ],
        out_specs=[pl.BlockSpec(memory_space=pltpu.VMEM)] * len(outs),
        scratch_shapes=scratch,
        compiler_params=pltpu.CompilerParams(vmem_limit_bytes=24 * 2**20),
    )(*args)


def low_lanes():
    return lax.broadcasted_iota(jnp.int32, (1, LANES), 1) < HEAD_DIM


def swap(chunk):
    return pltpu.roll(chunk, HEAD_DIM, 1)


def chunks_of(rows):
    return [rows[:, c : c + LANES] for c in range(0, rows.shape[1], LANES)]


def rotate(chunk, tables):
    cosine, to_first, to_second = tables
    quarter = HEAD_DIM // 2
    return (
        chunk * cosine
        + pltpu.roll(chunk, LANES - quarter, 1) * to_first
        + pltpu.roll(chunk, quarter, 1) * to_second
    )


def unrotate(chunk, tables):
    cosine, to_first, to_second = tables
    quarter = HEAD_DIM // 2
    return (
        chunk * cosine
        - pltpu.roll(chunk, LANES - quarter, 1) * to_first
        - pltpu.roll(chunk, quarter, 1) * to_second
    )


def low_and_high(chunks):
    swapped = [swap(chunk) for chunk in chunks]
    low = [(swapped if h % 2 else chunks)[h // 2] for h in range(2 * len(chunks))]
    high = [(chunks if h % 2 else swapped)[h // 2] for h in range(2 * len(chunks))]
    return low, high


def targets():
    for d in range(GROUP):
        micro, chip, half = d // 8, d % 8 // 2, d % 2
        yield d, micro, 3 * chip + 2 * half, 3 * chip + 1, half


def pack_folded(chunks, ref, base):
    low, high = low_and_high(chunks)
    first = low_lanes()
    rows = chunks[0].shape[0] // 2
    half, fold = rows // 2, rows * 3 // 4
    for d, micro, own, shared, side in targets():
        start = micro * rows
        part = start + side * half
        upper = jnp.concatenate(
            [high[own][start + fold : start + rows], high[shared][part : part + half]], 0
        )
        ref[d, base : base + fold] = jnp.where(
            first, low[own][start : start + fold], upper
        ).astype(BF)


def pack_pairs(lefts, rights, ref):
    low, high = low_and_high(lefts)[0], low_and_high(rights)[1]
    first = low_lanes()
    rows = lefts[0].shape[0] // 2
    half = rows // 2
    for d, micro, own, shared, side in targets():
        start = micro * rows
        part = start + side * half
        ref[d, 0:rows] = jnp.where(
            first, low[own][start : start + rows], high[own][start : start + rows]
        ).astype(BF)
        ref[d, rows : rows + half] = jnp.where(
            first, low[shared][part : part + half], high[shared][part : part + half]
        ).astype(BF)


def unpack_folded(ref, base, rows):
    first = low_lanes()
    fold = rows * 3 // 4
    low, high = {}, {}
    shared_parts = {}
    for d, micro, own, shared, side in targets():
        block = ref[d, base : base + fold].astype(F32)
        mine = jnp.concatenate([block, swap(block[: rows - fold])], 0)
        if own % 2:
            high[micro, own] = swap(mine)
        else:
            low[micro, own] = mine
        shared_parts[micro, shared, side] = block[rows - fold :]
        if side:
            both = jnp.concatenate([shared_parts[micro, shared, 0], block[rows - fold :]], 0)
            if shared % 2:
                high[micro, shared] = both
            else:
                low[micro, shared] = swap(both)
    heads = GROUP // 4 * 3
    return [
        jnp.concatenate(
            [jnp.where(first, low[m, h], high[m, h + 1]) for m in range(2)], 0
        )
        for h in range(0, heads, 2)
    ]


def unpack_pairs(ref, rows):
    first = low_lanes()
    half = rows // 2
    pairs = {}
    parts = {}
    for d, micro, own, shared, side in targets():
        pairs[micro, own] = ref[d, 0:rows].astype(F32)
        parts[side] = ref[d, rows : rows + half].astype(F32)
        if side:
            pairs[micro, shared] = jnp.concatenate([parts[0], parts[1]], 0)
    heads = GROUP // 4 * 3
    lefts, rights = [], []
    for h in range(0, heads, 2):
        even, odd = [pairs[m, h] for m in range(2)], [pairs[m, h + 1] for m in range(2)]
        lefts.append(
            jnp.concatenate([jnp.where(first, a, swap(b)) for a, b in zip(even, odd)], 0)
        )
        rights.append(
            jnp.concatenate([jnp.where(first, swap(a), b) for a, b in zip(even, odd)], 0)
        )
    return lefts, rights


def mlp_forward(layer_in, attended, gain, wide_ref, out_ref):
    width = layer_in.shape[1]
    inner = wide_ref.shape[1] - width
    middle = layer_in + dot(attended, wide_ref[:, :width])
    xhat, _ = moments(middle)
    normed = (xhat * gain).astype(BF)
    gate_up = dot(normed, wide_ref[:, width : width + inner])
    gate, up = gate_up[:, : inner // 2], gate_up[:, inner // 2 :]
    cdf = 0.5 * (1.0 + lax.erf(gate * math.sqrt(0.5)))
    mixed = (gate * cdf * up).astype(BF)
    result = (middle + dot(mixed, out_ref[...])).astype(BF)
    return middle, normed, gate, up, mixed, result


def mlp_backward(upstream, middle, gate, up, gain, wide_ref, out_ref):
    width = middle.shape[1]
    inner = 2 * gate.shape[1]
    d_mixed = dot_bt(upstream, out_ref[...])
    cdf = 0.5 * (1.0 + lax.erf(gate * math.sqrt(0.5)))
    density = jnp.exp(-0.5 * gate * gate) * (1.0 / math.sqrt(2.0 * math.pi))
    d_gate = d_mixed * up * (cdf + gate * density)
    d_up = d_mixed * gate * cdf
    d_gate_up = jnp.concatenate([d_gate.astype(BF), d_up.astype(BF)], 1)
    d_normed = dot_bt(d_gate_up, wide_ref[:, width : width + inner])
    xhat, scale = moments(middle)
    gain_grad = jnp.sum(d_normed * xhat, 0, keepdims=True)
    d_middle = upstream.astype(F32) + norm_back(d_normed, gain, xhat, scale)
    d_attn = d_middle.astype(BF)
    d_attended = dot_bt(d_attn, wide_ref[:, :width])
    return d_gate_up, gain_grad, d_middle, d_attn, d_attended


def project(xhat, gain, first_ref, table_ref, normed_ref):
    width = xhat.shape[1]
    normed = (xhat * gain).astype(BF)
    normed_ref[...] = normed
    tables = [table_ref[i] for i in range(3)]
    queries = chunks_of(dot(normed, first_ref[:, :width]))
    keys = chunks_of(dot(normed, first_ref[:, width : 2 * width]))
    values = dot(normed, first_ref[:, 2 * width : 3 * width])
    return [rotate(c, tables) for c in queries], [rotate(c, tables) for c in keys], values


def input_backward(d_middle, d_projected, x_ref, gain_ref, first_ref, grad_ref, gain_out_ref):
    d_normed = dot_bt(d_projected, first_ref[:, : d_projected.shape[1]])
    xhat, scale = moments(x_ref[...].astype(F32))
    gain_out_ref[...] = jnp.sum(d_normed * xhat, 0, keepdims=True)
    grad_ref[...] = (d_middle + norm_back(d_normed, gain_ref[...], xhat, scale)).astype(BF)


def local_project_body(place_ref, x_ref, table_ref, *refs):
    pieces, (first_ref, extra_ref, normed_ref, q_ref, kv_ref, sem) = refs[:-6], refs[-6:]
    rows = pieces[0].shape[0]
    copies = []
    for apart, piece in enumerate(pieces):
        start = pl.multiple_of((place_ref[0] ^ apart) * rows, rows) if len(pieces) > 1 else 0
        copies.append(
            pltpu.make_async_copy(piece, first_ref.at[pl.ds(start, rows)], sem.at[apart])
        )
        copies[-1].start()
    xhat, _ = moments(x_ref[...].astype(F32))
    for copy in copies:
        copy.wait()
    extra = first_ref[:, first_ref.shape[1] - LANES :].astype(F32).T
    extra_ref[...] = extra[: extra_ref.shape[0]]
    queries, keys, values = project(xhat, extra[:1], first_ref, table_ref, normed_ref)
    width = values.shape[1]
    for j, (q, k) in enumerate(zip(queries, keys)):
        q_ref[:, LANES * j : LANES * (j + 1)] = q.astype(BF)
        kv_ref[:, LANES * j : LANES * (j + 1)] = k.astype(BF)
    kv_ref[:, width:] = values.astype(BF)


def two_heads(chunk):
    first = low_lanes()
    wide = chunk.astype(F32)
    return jnp.concatenate([jnp.where(first, wide, 0.0), jnp.where(first, 0.0, wide)], 0)


def pick_heads(rows):
    half = rows.shape[0] // 2
    return jnp.where(low_lanes(), rows[:half], rows[half:])


def local_parts(q_ref, before_ref, own_ref, after_ref):
    rows = q_ref.shape[0] // 2
    width = q_ref.shape[1]
    for micro in range(2):
        for j in range(width // LANES):
            here = slice(micro * rows, (micro + 1) * rows)
            lanes = slice(LANES * j, LANES * (j + 1))
            more = slice(width + LANES * j, width + LANES * (j + 1))
            keys, values = (
                jnp.concatenate([ref[here, part] for ref in (before_ref, own_ref, after_ref)], 0)
                for part in (lanes, more)
            )
            queries = (two_heads(q_ref[here, lanes]) * SCALE).astype(BF)
            yield micro * (width // LANES) + j, micro, here, lanes, more, queries, keys, values


def local_forward_body(q_ref, before_ref, own_ref, after_ref, bias_ref, att_ref, total_ref):
    parts = local_parts(q_ref, before_ref, own_ref, after_ref)
    for index, micro, here, lanes, _, queries, keys, values in parts:
        scores = dot_bt(keys, queries) + bias_ref[micro]
        peak = jnp.max(scores, 0, keepdims=True)
        weights = jnp.exp(scores - peak)
        total = jnp.sum(weights, 0, keepdims=True)
        total_ref[index] = peak + jnp.log(total)
        probs = (weights * (1.0 / total)).astype(BF)
        att_ref[here, lanes] = pick_heads(dot_at(probs, values)).astype(BF)


def local_backward_body(
    q_ref, before_ref, own_ref, after_ref, bias_ref, total_ref, d_ref, table_ref,
    dq_ref, d_own_ref, d_before_ref, d_after_ref,
):
    tables = [table_ref[i] for i in range(3)]
    parts = local_parts(q_ref, before_ref, own_ref, after_ref)
    rows = q_ref.shape[0] // 2
    for index, micro, here, lanes, more, queries, keys, values in parts:
        d_out = two_heads(d_ref[here, lanes]).astype(BF)
        probs = jnp.exp(dot_bt(keys, queries) + bias_ref[micro] - total_ref[index])
        d_probs = dot_bt(values, d_out)
        product = probs * d_probs
        delta = jnp.sum(product, 0, keepdims=True)
        d_scores = (product - probs * delta).astype(BF)
        d_queries = pick_heads(dot_at(d_scores, keys)) * SCALE
        local_tables = [table[here] for table in tables]
        dq_ref[here, lanes] = unrotate(d_queries, local_tables).astype(BF)
        for part, grads in ((lanes, dot(d_scores, queries)), (more, dot(probs.astype(BF), d_out))):
            d_before_ref[here, part] = grads[:rows].astype(BF)
            d_own_ref[here, part] = grads[rows : 2 * rows]
            d_after_ref[here, part] = grads[2 * rows :].astype(BF)


def local_join_body(dq_ref, own_ref, low_ref, high_ref, table_ref, out_ref):
    tables = [table_ref[i] for i in range(3)]
    width = dq_ref.shape[1]
    out_ref[:, :width] = dq_ref[...]
    total = own_ref[...] + low_ref[...].astype(F32) + high_ref[...].astype(F32)
    for j, chunk in enumerate(chunks_of(total[:, :width])):
        start = width + LANES * j
        out_ref[:, start : start + LANES] = unrotate(chunk, tables).astype(BF)
    out_ref[:, 2 * width :] = total[:, width:].astype(BF)


def local_middle_body(
    x_ref, att_ref, gain_ref, wide_ref, w_out_ref, out_ref, normed_ref, mixed_ref, middle_ref, gate_up_ref
):
    middle, normed, gate, up, mixed, result = mlp_forward(
        x_ref[...].astype(F32), att_ref[...], gain_ref[...], wide_ref, w_out_ref
    )
    out_ref[...] = result
    normed_ref[...] = normed
    mixed_ref[...] = mixed
    middle_ref[...] = middle
    half = gate.shape[1]
    gate_up_ref[:, :half] = gate
    gate_up_ref[:, half:] = up


def local_back_middle_body(
    up_ref, middle_ref, gate_up_ref, gain_ref, wide_ref, w_out_ref,
    d_gate_up_ref, gain_out_ref, d_middle_ref, d_attn_ref, d_att_ref,
):
    half = gate_up_ref.shape[1] // 2
    d_gate_up, gain_grad, d_middle, d_attn, d_attended = mlp_backward(
        up_ref[...], middle_ref[...], gate_up_ref[:, :half], gate_up_ref[:, half:],
        gain_ref[...], wide_ref, w_out_ref,
    )
    d_gate_up_ref[...] = d_gate_up
    gain_out_ref[...] = gain_grad
    d_middle_ref[...] = d_middle
    d_attn_ref[...] = d_attn
    d_att_ref[...] = d_attended.astype(BF)


def input_backward_body(
    d_middle_ref, d_proj_ref, x_ref, gain_ref, first_ref, grad_ref, gain_out_ref
):
    input_backward(
        d_middle_ref[...], d_proj_ref[...], x_ref, gain_ref, first_ref, grad_ref, gain_out_ref
    )


def global_project_body(x_ref, gain_ref, first_ref, table_ref, normed_ref, sent_ref):
    xhat, _ = moments(x_ref[...].astype(F32))
    queries, keys, values = project(xhat, gain_ref[...], first_ref, table_ref, normed_ref)
    pack_pairs(queries, keys, sent_ref)
    pack_folded(chunks_of(values), sent_ref, sent_ref.shape[1] * 2 // 3)


def flat(blocks):
    return blocks.reshape(-1, LANES)


def own_unfolded(ref, base, rows):
    fold = rows * 3 // 4
    block = ref[:, base : base + fold].astype(F32)
    rest = swap(flat(block[:, : rows - fold])).reshape(GROUP, rows - fold, LANES)
    return flat(jnp.concatenate([block, rest], 1))


def shared_unfolded(ref, start, rows):
    return swap(flat(ref[:, start : start + rows // 2].astype(F32)))


def fill_heads(got_ref, other_ref, own_seg_ref, shared_seg_ref, q_scr, k_scr, v_scr):
    rows = got_ref.shape[1] * 4 // 9
    half = rows // 2
    first = low_lanes()
    lane = lax.broadcasted_iota(jnp.int32, (1, LANES), 1) - HEAD_DIM
    own = flat(got_ref[:, 0:rows].astype(F32))
    shared = flat(got_ref[:, rows : rows + half].astype(F32))
    other = flat(other_ref[:, 0:half].astype(F32))
    count = own.shape[0]
    own_hit = lane == own_seg_ref[...]
    shared_hit = lane == shared_seg_ref[...]
    both = jnp.concatenate([shared, other], 0)
    for start, pairs, hit in (
        (0, own, own_hit),
        (count, shared, shared_hit[: count // 2]),
    ):
        marked = jnp.where(hit, 1.0, 0.0)
        q_scr[start : start + pairs.shape[0]] = jnp.where(first, pairs * SCALE, marked).astype(BF)
    for unit, pairs, hit in ((0, own, own_hit), (1, both, shared_hit)):
        marked = jnp.where(hit, 0.0, masked_score)
        k_scr[unit] = jnp.where(first, swap(pairs), marked).astype(BF)
    base = rows + half
    v_scr[0] = jnp.where(first, own_unfolded(got_ref, base, rows), 0.0).astype(BF)
    start = base + rows - rows * 3 // 4
    shared_v = jnp.concatenate(
        [shared_unfolded(got_ref, start, rows), shared_unfolded(other_ref, half, rows)], 0
    )
    v_scr[1] = jnp.where(first, shared_v, 0.0).astype(BF)


def fold_out(own, shared, rows, ref, base):
    fold = rows * 3 // 4
    blocks = own.reshape(GROUP, rows, LANES)
    swapped = swap(own).reshape(GROUP, rows, LANES)
    upper = jnp.concatenate(
        [swapped[:, fold:], swap(shared).reshape(GROUP, rows // 2, LANES)], 1
    )
    ref[:, base : base + fold] = jnp.where(low_lanes(), blocks[:, :fold], upper).astype(BF)


def global_forward_body(
    got_ref, other_ref, own_seg_ref, shared_seg_ref, out_ref, total_ref,
    q_scr, k_scr, v_scr, vt_scr, o_scr,
):
    fill_heads(got_ref, other_ref, own_seg_ref, shared_seg_ref, q_scr, k_scr, v_scr)
    for unit in range(2):
        vt_scr[unit] = v_scr[unit].astype(F32).T.astype(BF)
    count = k_scr.shape[1]

    def step(tile, carry):
        unit = tile // (count // TILE)
        rows = pl.ds(pl.multiple_of(tile * TILE, TILE), TILE)
        scores = dot_bt(k_scr[unit], q_scr[rows])
        peak = jnp.max(scores, 0, keepdims=True)
        weights = jnp.exp(scores - peak)
        total = jnp.sum(weights, 0, keepdims=True)
        total_ref[tile] = peak + jnp.log(total)
        out = dot(vt_scr[unit], weights.astype(BF)) * (1.0 / total)
        o_scr[rows] = out.T
        return carry

    lax.fori_loop(0, q_scr.shape[0] // TILE, step, 0)
    rows = got_ref.shape[1] * 4 // 9
    fold_out(o_scr[:count], o_scr[count:], rows, out_ref, 0)


def global_backward_body(
    got_ref, other_ref, own_seg_ref, shared_seg_ref, total_ref, d_ref, sent_ref, to_other_ref,
    q_scr, k_scr, v_scr, kt_scr, d_scr, dq_scr, dk_scr, dv_scr,
):
    fill_heads(got_ref, other_ref, own_seg_ref, shared_seg_ref, q_scr, k_scr, v_scr)
    first = low_lanes()
    rows = got_ref.shape[1] * 4 // 9
    half = rows // 2
    for unit in range(2):
        keys = jnp.where(first, k_scr[unit].astype(F32), 0.0)
        kt_scr[unit] = keys.T.astype(BF)
    count = k_scr.shape[1]
    d_scr[:count] = jnp.where(first, own_unfolded(d_ref, 0, rows), 0.0).astype(BF)
    d_scr[count:] = jnp.where(
        first, shared_unfolded(d_ref, rows - rows * 3 // 4, rows), 0.0
    ).astype(BF)
    dk_scr[...] = jnp.zeros_like(dk_scr)
    dv_scr[...] = jnp.zeros_like(dv_scr)

    def step(tile, carry):
        unit = tile // (count // TILE)
        here = pl.ds(pl.multiple_of(tile * TILE, TILE), TILE)
        queries, d_out = q_scr[here], d_scr[here]
        probs = jnp.exp(dot_bt(k_scr[unit], queries) - total_ref[tile])
        d_probs = dot_bt(v_scr[unit], d_out)
        product = probs * d_probs
        delta = jnp.sum(product, 0, keepdims=True)
        d_scores = (product - probs * delta).astype(BF)
        dv_scr[unit] += dot(probs.astype(BF), d_out)
        dk_scr[unit] += dot(d_scores, queries)
        dq_scr[here] = dot(kt_scr[unit], d_scores).T * SCALE
        return carry

    lax.fori_loop(0, q_scr.shape[0] // TILE, step, 0)
    mine = count // 2
    own = jnp.where(first, dq_scr[:count], swap(dk_scr[0]))
    sent_ref[:, 0:rows] = own.reshape(GROUP, rows, LANES).astype(BF)
    shared_k, shared_v = dk_scr[1], dv_scr[1]
    shared = jnp.where(first, dq_scr[count:], swap(shared_k[:mine]))
    sent_ref[:, rows : rows + half] = shared.reshape(GROUP, half, LANES).astype(BF)
    fold_out(dv_scr[0], shared_v[:mine], rows, sent_ref, rows + half)
    for place, grads in enumerate((shared_k, shared_v)):
        other = jnp.where(first, 0.0, swap(grads[mine:])).reshape(GROUP, half, LANES)
        to_other_ref[:, place * half : (place + 1) * half] = other.astype(BF)


def global_middle_body(
    got_ref, x_ref, up_ref, gain_ref, wide_ref, w_out_ref,
    out_ref, att_ref, normed_ref, mixed_ref, d_gate_up_ref, gain_out_ref, d_middle_ref, d_attn_ref, sent_ref,
):
    rows = x_ref.shape[0] // 2
    attended = jnp.concatenate([c.astype(BF) for c in unpack_folded(got_ref, 0, rows)], 1)
    att_ref[...] = attended
    gain = gain_ref[...]
    middle, normed, gate, up, mixed, result = mlp_forward(
        x_ref[...].astype(F32), attended, gain, wide_ref, w_out_ref
    )
    out_ref[...] = result
    normed_ref[...] = normed
    mixed_ref[...] = mixed
    d_gate_up, gain_grad, d_middle, d_attn, d_attended = mlp_backward(
        up_ref[...], middle, gate, up, gain, wide_ref, w_out_ref
    )
    d_gate_up_ref[...] = d_gate_up
    gain_out_ref[...] = gain_grad
    d_middle_ref[...] = d_middle
    d_attn_ref[...] = d_attn
    pack_folded(chunks_of(d_attended), sent_ref, 0)


def global_finish_body(
    got_ref, d_middle_ref, x_ref, gain_ref, first_ref, table_ref, d_proj_ref, grad_ref, gain_out_ref
):
    tables = [table_ref[i] for i in range(3)]
    rows = x_ref.shape[0] // 2
    width = x_ref.shape[1]
    d_queries, d_keys = unpack_pairs(got_ref, rows)
    d_values = unpack_folded(got_ref, rows * 3 // 2, rows)
    parts = [unrotate(c, tables).astype(BF) for c in d_queries + d_keys]
    d_projected = jnp.concatenate(parts + [c.astype(BF) for c in d_values], 1)
    d_proj_ref[...] = d_projected
    input_backward(
        d_middle_ref[...], d_projected, x_ref, gain_ref, first_ref, grad_ref, gain_out_ref
    )


def neighbours(count, step):
    return [
        (i, i + step)
        for i in range(count)
        if 0 <= i + step < count and i // GROUP == (i + step) // GROUP
    ]


def exchange(blocks, count):
    groups = [list(range(s, s + GROUP)) for s in range(0, count, GROUP)]
    return lax.all_to_all(blocks, "dp", 0, 0, axis_index_groups=groups)


def to_other_section(rows, step):
    return lax.ppermute(rows, "section", [(0, 1)] if step > 0 else [(1, 0)])


def partner(rows, apart, count):
    return lax.ppermute(rows, "dp", [(i, i ^ apart) for i in range(count)])


def group_pieces(piece, count, hold=None):
    pieces = {0: piece}
    for apart in (4, 8, 12):
        pieces[apart] = partner(piece, apart, count)
    held = [pieces[apart] for apart in (4, 8, 12)]
    if hold is not None:
        held, hold = lax.optimization_barrier((held, hold))
        for apart, item in zip((4, 8, 12), held):
            pieces[apart] = item
    for apart in (0, 4, 8, 12):
        pieces[apart + 2] = partner(pieces[apart], 2, count)
    for apart in range(0, GROUP, 2):
        pieces[apart + 1] = partner(pieces[apart], 1, count)
    return [pieces[apart] for apart in range(GROUP)], hold


def in_order(pieces, group_pos, count):
    shape = pieces[0].shape
    whole = jnp.zeros((GROUP,) + shape, pieces[0].dtype)
    for apart, item in enumerate(pieces):
        start = (group_pos ^ apart,) + (0,) * len(shape)
        whole = lax.dynamic_update_slice(whole, item[None], start)
    if count > GROUP:
        groups = [list(range(s, count, GROUP)) for s in range(GROUP)]
        whole = lax.all_gather(whole, "dp", axis=0, tiled=True, axis_index_groups=groups)
    return whole.reshape(-1, shape[-1])


def plane_rows(rows, group_pos, count):
    parts = rows.reshape(count // GROUP, 4, 4, *rows.shape[1:])
    place = group_pos % 4
    taken = []
    for apart in range(4):
        block = lax.dynamic_index_in_dim(parts, place ^ apart, 2, keepdims=False)
        taken.append((partner(block, apart, count) if apart else block).swapaxes(0, 1))
    return taken


def product_body(*refs):
    out_ref = refs[-1]
    column = 0
    for start in range(0, len(refs) - 1, 8):
        left = jnp.concatenate([ref[...] for ref in refs[start : start + 4]], 1)
        right = jnp.concatenate([ref[...] for ref in refs[start + 4 : start + 8]], 0)
        end = column + right.shape[1]
        out_ref[:, column:end] = dot(left, right).astype(BF)
        column = end


def plane_product(terms):
    planes, groups, rows, tokens = terms[0][0][0].shape
    args = [
        part
        for lefts, rights in terms
        for part in [item.reshape(-1, tokens) for item in lefts] + list(rights)
    ]
    columns = sum(rights[0].shape[1] for _, rights in terms)
    (product,) = on_core(product_body, [((planes * groups * rows, columns), BF)], args)
    return product.reshape(planes, groups, rows, columns)


def sum_planes(blocks, count):
    groups = [
        [s + 4 * z + k for z in range(4)] for s in range(0, count, GROUP) for k in range(4)
    ]
    got = lax.all_to_all(blocks, "dp", 0, 0, axis_index_groups=groups)
    total = jnp.sum(got.astype(F32), 0)
    if count > GROUP:
        apart = [list(range(s, count, GROUP)) for s in range(GROUP)]
        return lax.psum_scatter(total, "dp", scatter_dimension=0, axis_index_groups=apart)
    return total[0]


def on_device(
    tokens_in,
    segment_ids,
    out_grad,
    qkv_weight,
    attn_out_weight,
    mlp_in_weight,
    mlp_out_weight,
    attn_gain,
    mlp_gain,
):
    lower = lax.axis_index("section") == 0
    count = lax.axis_size("dp")
    replica = lax.axis_index("dp")
    group_pos = replica % GROUP
    micro_count, row_count, width = tokens_in.shape
    shard = qkv_weight.shape[1]
    own_ids = segment_ids.reshape(-1)
    id_columns = -(-own_ids.size // shard)
    ids = jnp.pad(own_ids.astype(BF), (0, id_columns * shard - own_ids.size))
    extra = jnp.concatenate(
        [attn_gain[0][:, None], mlp_gain[0][:, None], ids.reshape(shard, id_columns)], 1
    )
    extra = jnp.pad(extra, ((0, 0), (0, LANES - extra.shape[1])))
    second = lax.all_gather(
        jnp.concatenate([attn_out_weight[0], mlp_in_weight[0]], 1), "dp", axis=0, tiled=True
    )
    pieces, late_weight = group_pieces(
        jnp.concatenate([qkv_weight[0], extra], 1), count, mlp_out_weight[0]
    )
    if count > GROUP:
        pieces = [in_order(pieces, group_pos, count)]
    w_out = in_order(group_pieces(late_weight, count)[0], group_pos, count)

    positions = group_pos * row_count + jnp.arange(row_count)
    local_tables = angles(positions, local_log_base)
    global_tables = angles(positions, global_log_base)

    rows = micro_count * row_count
    inner = second.shape[1] - width
    hidden = w_out.shape[0]
    pairs = rows * width // (row_count * LANES)
    in_0 = tokens_in.reshape(rows, width)
    extra_rows = -(-(2 + id_columns) // 8) * 8
    first, extra, normed_0, q_0, kv_0 = on_core(
        local_project_body,
        [
            ((width, 3 * width + LANES), BF),
            ((extra_rows, width), F32),
            ((rows, width), BF),
            ((rows, width), BF),
            ((rows, 2 * width), BF),
        ],
        (group_pos[None], in_0, local_tables, *pieces),
        [pltpu.SemaphoreType.DMA((len(pieces),))],
        [pltpu.SMEM, pltpu.VMEM, pltpu.VMEM] + [pl.ANY] * len(pieces),
    )
    gain_attn, gain_mlp = extra[:1], extra[1:2]
    all_ids = extra[2 : 2 + id_columns].reshape(id_columns, count, shard)
    all_ids = lax.dynamic_slice_in_dim(all_ids, replica - group_pos, GROUP, 1)
    all_ids = all_ids.transpose(1, 2, 0).reshape(GROUP, -1)
    all_ids = all_ids[:, : own_ids.size].reshape(GROUP, micro_count, row_count)
    segments = all_ids.swapaxes(0, 1).reshape(micro_count, GROUP * row_count).astype(jnp.int32)

    key_pos = positions[0] - row_count + jnp.arange(3 * row_count)
    around = jnp.pad(segments, ((0, 0), (row_count, row_count)), constant_values=-1)
    key_seg = lax.dynamic_slice_in_dim(around, group_pos * row_count, 3 * row_count, 1)
    visible = (key_seg[:, :, None] == segment_ids[:, None, :]) & (
        jnp.abs(positions[None, :] - key_pos[:, None]) <= HALF_WIN
    )[None]
    bias = jnp.tile(jnp.where(visible, 0.0, masked_score), (1, 1, 2))

    own_seg = lax.dynamic_index_in_dim(segments, group_pos // 8, 0, keepdims=False)
    halves = own_seg.reshape(GROUP, 2, row_count // 2)
    mine = lax.dynamic_index_in_dim(halves, group_pos % 2, 1, keepdims=False).reshape(-1)
    theirs = lax.dynamic_index_in_dim(halves, 1 - group_pos % 2, 1, keepdims=False).reshape(-1)
    shared_seg = jnp.concatenate([mine, theirs])[:, None]
    own_seg = own_seg[:, None]

    up_pairs, down_pairs = neighbours(count, 1), neighbours(count, -1)
    around_0 = (
        lax.ppermute(kv_0, "dp", up_pairs),
        kv_0,
        lax.ppermute(kv_0, "dp", down_pairs),
    )
    att_0, total_0 = on_core(
        local_forward_body,
        [((rows, width), BF), ((pairs, 1, LANES), F32)],
        (q_0, *around_0, bias),
    )
    out_0, n2_0, mixed_0, middle_0, gate_up_0 = on_core(
        local_middle_body,
        [
            ((rows, width), BF),
            ((rows, width), BF),
            ((rows, hidden), BF),
            ((rows, width), F32),
            ((rows, inner), F32),
        ],
        (in_0, att_0, gain_mlp, second, w_out),
    )

    in_1 = to_other_section(out_0, 1)
    fold = row_count * 3 // 4
    half = row_count // 2
    normed_1, sent = on_core(
        global_project_body,
        [((rows, width), BF), ((GROUP, 3 * fold, LANES), BF)],
        (in_1, gain_attn, first, global_tables),
    )
    got = exchange(sent, count)
    beside = jnp.concatenate(
        [got[:, row_count : row_count + half], got[:, 3 * fold - half :]], 1
    )
    beside = partner(beside, 1, count)
    keys = GROUP * row_count
    tiles = keys * 3 // 2 // TILE
    head_scratch = [
        pltpu.VMEM((keys * 3 // 2, LANES), BF),
        pltpu.VMEM((2, keys, LANES), BF),
        pltpu.VMEM((2, keys, LANES), BF),
        pltpu.VMEM((2, LANES, keys), BF),
    ]
    folded, total_1 = on_core(
        global_forward_body,
        [((GROUP, fold, LANES), BF), ((tiles, 1, TILE), F32)],
        (got, beside, own_seg, shared_seg),
        head_scratch + [pltpu.VMEM((keys * 3 // 2, LANES), F32)],
    )
    folded = exchange(folded, count)

    up_1 = out_grad.reshape(rows, width)
    out_1, att_1, n2_1, mixed_1, d_gu_1, gain_mlp_1, d_mid_1, d_attn_1, sent = on_core(
        global_middle_body,
        [
            ((rows, width), BF),
            ((rows, width), BF),
            ((rows, width), BF),
            ((rows, hidden), BF),
            ((rows, inner), BF),
            ((1, width), F32),
            ((rows, width), F32),
            ((rows, width), BF),
            ((GROUP, fold, LANES), BF),
        ],
        (folded, in_1, up_1, gain_mlp, second, w_out),
    )
    d_folded = exchange(sent, count)
    sent, to_beside = on_core(
        global_backward_body,
        [((GROUP, 3 * fold, LANES), BF), ((GROUP, 2 * half, LANES), BF)],
        (got, beside, own_seg, shared_seg, total_1, d_folded),
        head_scratch
        + [
            pltpu.VMEM((keys * 3 // 2, LANES), BF),
            pltpu.VMEM((keys * 3 // 2, LANES), F32),
            pltpu.VMEM((2, keys, LANES), F32),
            pltpu.VMEM((2, keys, LANES), F32),
        ],
    )
    back = partner(to_beside, 1, count)
    gap = 3 * fold - half - row_count - half
    back = jnp.concatenate(
        [
            jnp.zeros((GROUP, row_count, LANES), BF),
            back[:, :half],
            jnp.zeros((GROUP, gap, LANES), BF),
            back[:, half:],
        ],
        1,
    )
    sent = (sent.astype(F32) + back.astype(F32)).astype(BF)
    got = exchange(sent, count)

    n1, att, n2, mixed = (
        jnp.where(lower, a, b).T.reshape(count, -1, micro_count * row_count)
        for a, b in (
            (normed_0, normed_1),
            (att_0, att_1),
            (n2_0, n2_1),
            (mixed_0, mixed_1),
        )
    )
    left = jnp.concatenate([n1, att, n2, mixed], 1)
    left, got = lax.optimization_barrier((left, got))
    left = plane_rows(left, group_pos, count)
    n1, att, n2, mixed = (
        [part[:, :, start:end] for part in left]
        for start, end in (
            (0, shard),
            (shard, 2 * shard),
            (2 * shard, 3 * shard),
            (3 * shard, left[0].shape[2]),
        )
    )
    d_proj_1, grad_1, gain_attn_1 = on_core(
        global_finish_body,
        [((rows, 3 * width), BF), ((rows, width), BF), ((1, width), F32)],
        (got, d_mid_1, in_1, gain_attn, first, global_tables),
    )

    up_0 = to_other_section(grad_1, -1)
    d_mlp = jnp.where(lower, up_0, up_1)
    across, beside = partner(d_mlp, 2, count), partner(d_mlp, 1, count)
    d_mlp = [d_mlp, beside, across, partner(across, 1, count)]
    out_blocks = plane_product([(mixed, d_mlp)])
    d_gu_0, gain_mlp_0, d_mid_0, d_attn_0, d_att_0 = on_core(
        local_back_middle_body,
        [
            ((rows, inner), BF),
            ((1, width), F32),
            ((rows, width), F32),
            ((rows, width), BF),
            ((rows, width), BF),
        ],
        (up_0, middle_0, gate_up_0, gain_mlp, second, w_out),
    )
    own = [jnp.where(lower, d_gu_0, d_gu_1), jnp.where(lower, d_attn_0, d_attn_1)]
    beside = [partner(item, 1, count) for item in own]
    across = [partner(item, 2, count) for item in own]
    dq_0, d_own, d_before, d_after = on_core(
        local_backward_body,
        [
            ((rows, width), BF),
            ((rows, 2 * width), F32),
            ((rows, 2 * width), BF),
            ((rows, 2 * width), BF),
        ],
        (q_0, *around_0, bias, total_0, d_att_0, local_tables),
    )
    from_after = lax.ppermute(d_before, "dp", down_pairs)
    from_before = lax.ppermute(d_after, "dp", up_pairs)
    from_after, out_blocks = lax.optimization_barrier((from_after, out_blocks))
    mlp_out_share = sum_planes(out_blocks, count)
    (d_proj_0,) = on_core(
        local_join_body,
        [((rows, 3 * width), BF)],
        (dq_0, d_own, from_after, from_before, local_tables),
    )
    d_proj = jnp.where(lower, d_proj_0, d_proj_1)
    d_proj, across = lax.optimization_barrier((d_proj, across))
    far = [partner(item, 1, count) for item in across]
    d_gu, d_attn = zip(own, beside, across, far)
    in_blocks = plane_product([(n2, d_gu), (att, d_attn)])
    in_share = sum_planes(in_blocks, count)
    across = partner(d_proj, 2, count)
    across, in_blocks = lax.optimization_barrier((across, in_blocks))
    d_proj = [d_proj, partner(d_proj, 1, count), across, partner(across, 1, count)]
    qkv_share = sum_planes(plane_product([(n1, d_proj)]), count)
    grad_0, gain_attn_0 = on_core(
        input_backward_body,
        [((rows, width), BF), ((1, width), F32)],
        (d_mid_0, d_proj_0, in_0, gain_attn, first),
    )

    gains = jnp.where(
        lower,
        jnp.concatenate([gain_attn_0, gain_mlp_0]),
        jnp.concatenate([gain_attn_1, gain_mlp_1]),
    )
    apart = 1
    while apart < count:
        gains = gains + partner(gains, apart, count)
        apart *= 2
    gains = lax.dynamic_slice_in_dim(gains, replica * shard, shard, 1)

    return (
        jnp.where(lower, out_0, out_1).reshape(1, micro_count, row_count, width),
        jnp.where(lower, grad_0, grad_1).reshape(1, micro_count, row_count, width),
        qkv_share[None],
        in_share[None, :, inner:],
        in_share[None, :, :inner],
        mlp_out_share[None],
        gains[:1],
        gains[1:],
    )


def solution(mesh):
    in_specs = (
        P(None, "dp", None),
        P(None, "dp"),
        P(None, "dp", None),
        P("section", "dp", None),
        P("section", "dp", None),
        P("section", "dp", None),
        P("section", "dp", None),
        P("section", "dp"),
        P("section", "dp"),
    )
    out_specs = (
        P("section", None, "dp", None),
        P("section", None, "dp", None),
        P("section", "dp", None),
        P("section", "dp", None),
        P("section", "dp", None),
        P("section", "dp", None),
        P("section", "dp"),
        P("section", "dp"),
    )
    return jax.shard_map(
        on_device, mesh=mesh, in_specs=in_specs, out_specs=out_specs, check_vma=False
    )
```

```python
import math

import jax
import jax.numpy as jnp
from jax import lax
from jax.experimental import pallas as pl
from jax.experimental.pallas import tpu as pltpu
from jax.sharding import PartitionSpec as P

HEAD_DIM = 64
GROUP = 16
HALF_WIN = 64
LANES = 128
TILE = 256

local_log_base = math.log(10000.0)
global_log_base = math.log(160000.0)
masked_score = -1e30
SCALE = 1.0 / math.sqrt(HEAD_DIM)
BF = jnp.bfloat16
F32 = jnp.float32


def dot(left, right):
    return jnp.dot(left, right, preferred_element_type=F32)


def dot_bt(left, right):
    return lax.dot_general(left, right, (((1,), (1,)), ((), ())), preferred_element_type=F32)


def dot_at(left, right):
    return lax.dot_general(left, right, (((0,), (0,)), ((), ())), preferred_element_type=F32)


def moments(values):
    center = values - jnp.mean(values, -1, keepdims=True)
    scale = lax.rsqrt(jnp.mean(center * center, -1, keepdims=True) + 1e-05)
    return center * scale, scale


def norm_back(grad_out, gain_row, xhat, scale):
    scaled = grad_out * gain_row
    mean_grad = jnp.mean(scaled, -1, keepdims=True)
    mean_dot = jnp.mean(scaled * xhat, -1, keepdims=True)
    return (scaled - mean_grad - xhat * mean_dot) * scale


def angles(positions, log_base):
    half_dim = HEAD_DIM // 2
    fraction = (2 * jnp.arange(half_dim)).astype(F32) / HEAD_DIM
    inverse = jnp.exp(-fraction * log_base)
    table = positions.astype(F32)[:, None] * inverse[None, :]
    cosine, sine = jnp.cos(table), jnp.sin(table)
    none = jnp.zeros_like(sine)
    cosine = jnp.concatenate([cosine, cosine], 1)
    to_first = jnp.concatenate([-sine, none], 1)
    to_second = jnp.concatenate([none, sine], 1)
    return jnp.tile(jnp.stack([cosine, to_first, to_second]), (1, 2, 2))


def on_core(body, micros, outs, args, scratch=(), spaces=None):
    return pl.pallas_call(
        body,
        out_shape=[jax.ShapeDtypeStruct(shape, dtype) for shape, dtype in outs],
        in_specs=[
            pl.BlockSpec(memory_space=space) for space in spaces or [pltpu.VMEM] * len(args)
        ],
        out_specs=[pl.BlockSpec(memory_space=pltpu.VMEM)] * len(outs),
        scratch_shapes=scratch,
        cost_estimate=pl.CostEstimate(
            flops=int(micros * 1.15e9), bytes_accessed=2**16, transcendentals=0
        ),
        compiler_params=pltpu.CompilerParams(vmem_limit_bytes=24 * 2**20),
    )(*args)


def low_lanes():
    return lax.broadcasted_iota(jnp.int32, (1, LANES), 1) < HEAD_DIM


def swap(chunk):
    return pltpu.roll(chunk, HEAD_DIM, 1)


def chunks_of(rows):
    return [rows[:, c : c + LANES] for c in range(0, rows.shape[1], LANES)]


def rotate(chunk, tables):
    cosine, to_first, to_second = tables
    quarter = HEAD_DIM // 2
    return (
        chunk * cosine
        + pltpu.roll(chunk, LANES - quarter, 1) * to_first
        + pltpu.roll(chunk, quarter, 1) * to_second
    )


def unrotate(chunk, tables):
    cosine, to_first, to_second = tables
    quarter = HEAD_DIM // 2
    return (
        chunk * cosine
        - pltpu.roll(chunk, LANES - quarter, 1) * to_first
        - pltpu.roll(chunk, quarter, 1) * to_second
    )


def low_and_high(chunks):
    swapped = [swap(chunk) for chunk in chunks]
    low = [(swapped if h % 2 else chunks)[h // 2] for h in range(2 * len(chunks))]
    high = [(chunks if h % 2 else swapped)[h // 2] for h in range(2 * len(chunks))]
    return low, high


def targets():
    for d in range(GROUP):
        micro, chip, half = d // 8, d % 8 // 2, d % 2
        yield d, micro, 3 * chip + 2 * half, 3 * chip + 1, half


def pack_folded(chunks, ref, base):
    low, high = low_and_high(chunks)
    first = low_lanes()
    rows = chunks[0].shape[0] // 2
    half, fold = rows // 2, rows * 3 // 4
    for d, micro, own, shared, side in targets():
        start = micro * rows
        part = start + side * half
        upper = jnp.concatenate(
            [high[own][start + fold : start + rows], high[shared][part : part + half]], 0
        )
        ref[d, base : base + fold] = jnp.where(
            first, low[own][start : start + fold], upper
        ).astype(BF)


def pack_pairs(lefts, rights, ref):
    low, high = low_and_high(lefts)[0], low_and_high(rights)[1]
    first = low_lanes()
    rows = lefts[0].shape[0] // 2
    half = rows // 2
    for d, micro, own, shared, side in targets():
        start = micro * rows
        part = start + side * half
        ref[d, 0:rows] = jnp.where(
            first, low[own][start : start + rows], high[own][start : start + rows]
        ).astype(BF)
        ref[d, rows : rows + half] = jnp.where(
            first, low[shared][part : part + half], high[shared][part : part + half]
        ).astype(BF)


def unpack_folded(ref, base, rows):
    first = low_lanes()
    fold = rows * 3 // 4
    low, high = {}, {}
    shared_parts = {}
    for d, micro, own, shared, side in targets():
        block = ref[d, base : base + fold].astype(F32)
        mine = jnp.concatenate([block, swap(block[: rows - fold])], 0)
        if own % 2:
            high[micro, own] = swap(mine)
        else:
            low[micro, own] = mine
        shared_parts[micro, shared, side] = block[rows - fold :]
        if side:
            both = jnp.concatenate([shared_parts[micro, shared, 0], block[rows - fold :]], 0)
            if shared % 2:
                high[micro, shared] = both
            else:
                low[micro, shared] = swap(both)
    heads = GROUP // 4 * 3
    return [
        jnp.concatenate(
            [jnp.where(first, low[m, h], high[m, h + 1]) for m in range(2)], 0
        )
        for h in range(0, heads, 2)
    ]


def unpack_pairs(ref, rows):
    first = low_lanes()
    half = rows // 2
    pairs = {}
    parts = {}
    for d, micro, own, shared, side in targets():
        pairs[micro, own] = ref[d, 0:rows].astype(F32)
        parts[side] = ref[d, rows : rows + half].astype(F32)
        if side:
            pairs[micro, shared] = jnp.concatenate([parts[0], parts[1]], 0)
    heads = GROUP // 4 * 3
    lefts, rights = [], []
    for h in range(0, heads, 2):
        even, odd = [pairs[m, h] for m in range(2)], [pairs[m, h + 1] for m in range(2)]
        lefts.append(
            jnp.concatenate([jnp.where(first, a, swap(b)) for a, b in zip(even, odd)], 0)
        )
        rights.append(
            jnp.concatenate([jnp.where(first, swap(a), b) for a, b in zip(even, odd)], 0)
        )
    return lefts, rights


def mlp_forward(layer_in, attended, gain, wide_ref, out_ref):
    width = layer_in.shape[1]
    inner = wide_ref.shape[1] - width
    middle = layer_in + dot(attended, wide_ref[:, :width])
    xhat, _ = moments(middle)
    normed = (xhat * gain).astype(BF)
    gate_up = dot(normed, wide_ref[:, width : width + inner])
    gate, up = gate_up[:, : inner // 2], gate_up[:, inner // 2 :]
    cdf = 0.5 * (1.0 + lax.erf(gate * math.sqrt(0.5)))
    mixed = (gate * cdf * up).astype(BF)
    result = (middle + dot(mixed, out_ref[...])).astype(BF)
    return middle, normed, gate, up, mixed, result


def mlp_backward(upstream, middle, gate, up, gain, wide_ref, out_ref):
    width = middle.shape[1]
    inner = 2 * gate.shape[1]
    d_mixed = dot_bt(upstream, out_ref[...])
    cdf = 0.5 * (1.0 + lax.erf(gate * math.sqrt(0.5)))
    density = jnp.exp(-0.5 * gate * gate) * (1.0 / math.sqrt(2.0 * math.pi))
    d_gate = d_mixed * up * (cdf + gate * density)
    d_up = d_mixed * gate * cdf
    d_gate_up = jnp.concatenate([d_gate.astype(BF), d_up.astype(BF)], 1)
    d_normed = dot_bt(d_gate_up, wide_ref[:, width : width + inner])
    xhat, scale = moments(middle)
    gain_grad = jnp.sum(d_normed * xhat, 0, keepdims=True)
    d_middle = upstream.astype(F32) + norm_back(d_normed, gain, xhat, scale)
    d_attn = d_middle.astype(BF)
    d_attended = dot_bt(d_attn, wide_ref[:, :width])
    return d_gate_up, gain_grad, d_middle, d_attn, d_attended


def project(xhat, gain, first_ref, table_ref, normed_ref):
    width = xhat.shape[1]
    normed = (xhat * gain).astype(BF)
    normed_ref[...] = normed
    tables = [table_ref[i] for i in range(3)]
    queries = chunks_of(dot(normed, first_ref[:, :width]))
    keys = chunks_of(dot(normed, first_ref[:, width : 2 * width]))
    values = dot(normed, first_ref[:, 2 * width : 3 * width])
    return [rotate(c, tables) for c in queries], [rotate(c, tables) for c in keys], values


def input_backward(d_middle, d_projected, x_ref, gain_ref, first_ref, grad_ref, gain_out_ref):
    d_normed = dot_bt(d_projected, first_ref[:, : d_projected.shape[1]])
    xhat, scale = moments(x_ref[...].astype(F32))
    gain_out_ref[...] = jnp.sum(d_normed * xhat, 0, keepdims=True)
    grad_ref[...] = (d_middle + norm_back(d_normed, gain_ref[...], xhat, scale)).astype(BF)


def message_body(w_ref, attn_ref, mlp_ref, ids_ref, out_ref, rows_scr, ids_scr):
    shard, columns = w_ref.shape
    micro_count, row_count = ids_ref.shape
    out_ref[:, :columns] = w_ref[...]
    rows_scr[...] = jnp.zeros_like(rows_scr)
    ids_scr[...] = jnp.zeros_like(ids_scr)
    rows_scr[0:1, :shard] = attn_ref[...].astype(F32)
    rows_scr[1:2, :shard] = mlp_ref[...].astype(F32)
    ids_scr[:micro_count, :row_count] = ids_ref[...].astype(F32)
    runs = -(-row_count // shard)
    for run in range(runs):
        turned = ids_scr[...]
        if run:
            turned = pltpu.roll(turned, LANES - run * shard, 1)
        for micro in range(micro_count):
            row = 2 + micro * runs + run
            rows_scr[row : row + 1] = turned[micro : micro + 1]
    out_ref[:, columns:] = rows_scr[...].T[:shard].astype(BF)


def local_project_body(place_ref, x_ref, table_ref, *refs):
    pieces, (first_ref, extra_ref, normed_ref, q_ref, kv_ref, sem) = refs[:-6], refs[-6:]
    rows = pieces[0].shape[0]
    copies = []
    for apart, piece in enumerate(pieces):
        start = pl.multiple_of((place_ref[0] ^ apart) * rows, rows) if len(pieces) > 1 else 0
        copies.append(
            pltpu.make_async_copy(piece, first_ref.at[pl.ds(start, rows)], sem.at[apart])
        )
        copies[-1].start()
    xhat, _ = moments(x_ref[...].astype(F32))
    for copy in copies:
        copy.wait()
    extra = first_ref[:, first_ref.shape[1] - LANES :].astype(F32).T
    extra_ref[...] = extra[: extra_ref.shape[0]]
    queries, keys, values = project(xhat, extra[:1], first_ref, table_ref, normed_ref)
    width = values.shape[1]
    for j, (q, k) in enumerate(zip(queries, keys)):
        q_ref[:, LANES * j : LANES * (j + 1)] = q.astype(BF)
        kv_ref[:, LANES * j : LANES * (j + 1)] = k.astype(BF)
    kv_ref[:, width:] = values.astype(BF)


def two_heads(chunk):
    first = low_lanes()
    wide = chunk.astype(F32)
    return jnp.concatenate([jnp.where(first, wide, 0.0), jnp.where(first, 0.0, wide)], 0)


def pick_heads(rows):
    half = rows.shape[0] // 2
    return jnp.where(low_lanes(), rows[:half], rows[half:])


def local_parts(q_ref, before_ref, own_ref, after_ref):
    rows = q_ref.shape[0] // 2
    width = q_ref.shape[1]
    for micro in range(2):
        for j in range(width // LANES):
            here = slice(micro * rows, (micro + 1) * rows)
            lanes = slice(LANES * j, LANES * (j + 1))
            more = slice(width + LANES * j, width + LANES * (j + 1))
            keys, values = (
                jnp.concatenate([ref[here, part] for ref in (before_ref, own_ref, after_ref)], 0)
                for part in (lanes, more)
            )
            queries = (two_heads(q_ref[here, lanes]) * SCALE).astype(BF)
            yield micro * (width // LANES) + j, micro, here, lanes, more, queries, keys, values


def local_forward_body(q_ref, before_ref, own_ref, after_ref, bias_ref, att_ref, total_ref):
    parts = local_parts(q_ref, before_ref, own_ref, after_ref)
    for index, micro, here, lanes, _, queries, keys, values in parts:
        scores = dot_bt(keys, queries) + bias_ref[micro]
        peak = jnp.max(scores, 0, keepdims=True)
        weights = jnp.exp(scores - peak)
        total = jnp.sum(weights, 0, keepdims=True)
        total_ref[index] = peak + jnp.log(total)
        probs = (weights * (1.0 / total)).astype(BF)
        att_ref[here, lanes] = pick_heads(dot_at(probs, values)).astype(BF)


def local_backward_body(
    q_ref, before_ref, own_ref, after_ref, bias_ref, total_ref, d_ref, table_ref,
    dq_ref, d_own_ref, d_before_ref, d_after_ref,
):
    tables = [table_ref[i] for i in range(3)]
    parts = local_parts(q_ref, before_ref, own_ref, after_ref)
    rows = q_ref.shape[0] // 2
    for index, micro, here, lanes, more, queries, keys, values in parts:
        d_out = two_heads(d_ref[here, lanes]).astype(BF)
        probs = jnp.exp(dot_bt(keys, queries) + bias_ref[micro] - total_ref[index])
        d_probs = dot_bt(values, d_out)
        product = probs * d_probs
        delta = jnp.sum(product, 0, keepdims=True)
        d_scores = (product - probs * delta).astype(BF)
        d_queries = pick_heads(dot_at(d_scores, keys)) * SCALE
        local_tables = [table[here] for table in tables]
        dq_ref[here, lanes] = unrotate(d_queries, local_tables).astype(BF)
        for part, grads in ((lanes, dot(d_scores, queries)), (more, dot(probs.astype(BF), d_out))):
            d_before_ref[here, part] = grads[:rows].astype(BF)
            d_own_ref[here, part] = grads[rows : 2 * rows]
            d_after_ref[here, part] = grads[2 * rows :].astype(BF)


def local_join_body(dq_ref, own_ref, low_ref, high_ref, table_ref, out_ref):
    tables = [table_ref[i] for i in range(3)]
    width = dq_ref.shape[1]
    out_ref[:, :width] = dq_ref[...]
    total = own_ref[...] + low_ref[...].astype(F32) + high_ref[...].astype(F32)
    for j, chunk in enumerate(chunks_of(total[:, :width])):
        start = width + LANES * j
        out_ref[:, start : start + LANES] = unrotate(chunk, tables).astype(BF)
    out_ref[:, 2 * width :] = total[:, width:].astype(BF)


def local_middle_body(
    x_ref, att_ref, gain_ref, wide_ref, w_out_ref, out_ref, normed_ref, mixed_ref, middle_ref, gate_up_ref
):
    middle, normed, gate, up, mixed, result = mlp_forward(
        x_ref[...].astype(F32), att_ref[...], gain_ref[...], wide_ref, w_out_ref
    )
    out_ref[...] = result
    normed_ref[...] = normed
    mixed_ref[...] = mixed
    middle_ref[...] = middle
    half = gate.shape[1]
    gate_up_ref[:, :half] = gate
    gate_up_ref[:, half:] = up


def local_back_middle_body(
    up_ref, middle_ref, gate_up_ref, gain_ref, wide_ref, w_out_ref,
    d_gate_up_ref, gain_out_ref, d_middle_ref, d_attn_ref, d_att_ref,
):
    half = gate_up_ref.shape[1] // 2
    d_gate_up, gain_grad, d_middle, d_attn, d_attended = mlp_backward(
        up_ref[...], middle_ref[...], gate_up_ref[:, :half], gate_up_ref[:, half:],
        gain_ref[...], wide_ref, w_out_ref,
    )
    d_gate_up_ref[...] = d_gate_up
    gain_out_ref[...] = gain_grad
    d_middle_ref[...] = d_middle
    d_attn_ref[...] = d_attn
    d_att_ref[...] = d_attended.astype(BF)


def input_backward_body(
    d_middle_ref, d_proj_ref, x_ref, gain_ref, first_ref, grad_ref, gain_out_ref
):
    input_backward(
        d_middle_ref[...], d_proj_ref[...], x_ref, gain_ref, first_ref, grad_ref, gain_out_ref
    )


def global_project_body(x_ref, gain_ref, first_ref, table_ref, normed_ref, sent_ref):
    xhat, _ = moments(x_ref[...].astype(F32))
    queries, keys, values = project(xhat, gain_ref[...], first_ref, table_ref, normed_ref)
    pack_pairs(queries, keys, sent_ref)
    pack_folded(chunks_of(values), sent_ref, sent_ref.shape[1] * 2 // 3)


def flat(blocks):
    return blocks.reshape(-1, LANES)


def own_unfolded(ref, base, rows):
    fold = rows * 3 // 4
    block = ref[:, base : base + fold].astype(F32)
    rest = swap(flat(block[:, : rows - fold])).reshape(GROUP, rows - fold, LANES)
    return flat(jnp.concatenate([block, rest], 1))


def shared_unfolded(ref, start, rows):
    return swap(flat(ref[:, start : start + rows // 2].astype(F32)))


def fill_heads(got_ref, other_ref, own_seg_ref, shared_seg_ref, q_scr, k_scr, v_scr):
    rows = got_ref.shape[1] * 4 // 9
    half = rows // 2
    first = low_lanes()
    lane = lax.broadcasted_iota(jnp.int32, (1, LANES), 1) - HEAD_DIM
    own = flat(got_ref[:, 0:rows].astype(F32))
    shared = flat(got_ref[:, rows : rows + half].astype(F32))
    other = flat(other_ref[:, 0:half].astype(F32))
    count = own.shape[0]
    own_hit = lane == own_seg_ref[...]
    shared_hit = lane == shared_seg_ref[...]
    both = jnp.concatenate([shared, other], 0)
    for start, pairs, hit in (
        (0, own, own_hit),
        (count, shared, shared_hit[: count // 2]),
    ):
        marked = jnp.where(hit, 1.0, 0.0)
        q_scr[start : start + pairs.shape[0]] = jnp.where(first, pairs * SCALE, marked).astype(BF)
    for unit, pairs, hit in ((0, own, own_hit), (1, both, shared_hit)):
        marked = jnp.where(hit, 0.0, masked_score)
        k_scr[unit] = jnp.where(first, swap(pairs), marked).astype(BF)
    base = rows + half
    v_scr[0] = jnp.where(first, own_unfolded(got_ref, base, rows), 0.0).astype(BF)
    start = base + rows - rows * 3 // 4
    shared_v = jnp.concatenate(
        [shared_unfolded(got_ref, start, rows), shared_unfolded(other_ref, half, rows)], 0
    )
    v_scr[1] = jnp.where(first, shared_v, 0.0).astype(BF)


def fold_out(own, shared, rows, ref, base):
    fold = rows * 3 // 4
    blocks = own.reshape(GROUP, rows, LANES)
    swapped = swap(own).reshape(GROUP, rows, LANES)
    upper = jnp.concatenate(
        [swapped[:, fold:], swap(shared).reshape(GROUP, rows // 2, LANES)], 1
    )
    ref[:, base : base + fold] = jnp.where(low_lanes(), blocks[:, :fold], upper).astype(BF)


def global_forward_body(
    got_ref, other_ref, own_seg_ref, shared_seg_ref, out_ref, total_ref,
    q_scr, k_scr, v_scr, vt_scr, o_scr,
):
    fill_heads(got_ref, other_ref, own_seg_ref, shared_seg_ref, q_scr, k_scr, v_scr)
    for unit in range(2):
        vt_scr[unit] = v_scr[unit].astype(F32).T.astype(BF)
    count = k_scr.shape[1]

    def step(tile, carry):
        unit = tile // (count // TILE)
        rows = pl.ds(pl.multiple_of(tile * TILE, TILE), TILE)
        scores = dot_bt(k_scr[unit], q_scr[rows])
        peak = jnp.max(scores, 0, keepdims=True)
        weights = jnp.exp(scores - peak)
        total = jnp.sum(weights, 0, keepdims=True)
        total_ref[tile] = peak + jnp.log(total)
        out = dot(vt_scr[unit], weights.astype(BF)) * (1.0 / total)
        o_scr[rows] = out.T
        return carry

    lax.fori_loop(0, q_scr.shape[0] // TILE, step, 0)
    rows = got_ref.shape[1] * 4 // 9
    fold_out(o_scr[:count], o_scr[count:], rows, out_ref, 0)


def global_backward_body(
    got_ref, other_ref, own_seg_ref, shared_seg_ref, total_ref, d_ref, sent_ref, to_other_ref,
    q_scr, k_scr, v_scr, kt_scr, d_scr, dq_scr, dk_scr, dv_scr,
):
    fill_heads(got_ref, other_ref, own_seg_ref, shared_seg_ref, q_scr, k_scr, v_scr)
    first = low_lanes()
    rows = got_ref.shape[1] * 4 // 9
    half = rows // 2
    for unit in range(2):
        keys = jnp.where(first, k_scr[unit].astype(F32), 0.0)
        kt_scr[unit] = keys.T.astype(BF)
    count = k_scr.shape[1]
    d_scr[:count] = jnp.where(first, own_unfolded(d_ref, 0, rows), 0.0).astype(BF)
    d_scr[count:] = jnp.where(
        first, shared_unfolded(d_ref, rows - rows * 3 // 4, rows), 0.0
    ).astype(BF)
    dk_scr[...] = jnp.zeros_like(dk_scr)
    dv_scr[...] = jnp.zeros_like(dv_scr)

    def step(tile, carry):
        unit = tile // (count // TILE)
        here = pl.ds(pl.multiple_of(tile * TILE, TILE), TILE)
        queries, d_out = q_scr[here], d_scr[here]
        probs = jnp.exp(dot_bt(k_scr[unit], queries) - total_ref[tile])
        d_probs = dot_bt(v_scr[unit], d_out)
        product = probs * d_probs
        delta = jnp.sum(product, 0, keepdims=True)
        d_scores = (product - probs * delta).astype(BF)
        dv_scr[unit] += dot(probs.astype(BF), d_out)
        dk_scr[unit] += dot(d_scores, queries)
        dq_scr[here] = dot(kt_scr[unit], d_scores).T * SCALE
        return carry

    lax.fori_loop(0, q_scr.shape[0] // TILE, step, 0)
    mine = count // 2
    own = jnp.where(first, dq_scr[:count], swap(dk_scr[0]))
    sent_ref[:, 0:rows] = own.reshape(GROUP, rows, LANES).astype(BF)
    shared_k, shared_v = dk_scr[1], dv_scr[1]
    shared = jnp.where(first, dq_scr[count:], swap(shared_k[:mine]))
    sent_ref[:, rows : rows + half] = shared.reshape(GROUP, half, LANES).astype(BF)
    fold_out(dv_scr[0], shared_v[:mine], rows, sent_ref, rows + half)
    for place, grads in enumerate((shared_k, shared_v)):
        other = jnp.where(first, 0.0, swap(grads[mine:])).reshape(GROUP, half, LANES)
        to_other_ref[:, place * half : (place + 1) * half] = other.astype(BF)


def global_middle_body(
    got_ref, x_ref, up_ref, gain_ref, wide_ref, w_out_ref,
    out_ref, att_ref, normed_ref, mixed_ref, d_gate_up_ref, gain_out_ref, d_middle_ref, d_attn_ref, sent_ref,
):
    rows = x_ref.shape[0] // 2
    attended = jnp.concatenate([c.astype(BF) for c in unpack_folded(got_ref, 0, rows)], 1)
    att_ref[...] = attended
    gain = gain_ref[...]
    middle, normed, gate, up, mixed, result = mlp_forward(
        x_ref[...].astype(F32), attended, gain, wide_ref, w_out_ref
    )
    out_ref[...] = result
    normed_ref[...] = normed
    mixed_ref[...] = mixed
    d_gate_up, gain_grad, d_middle, d_attn, d_attended = mlp_backward(
        up_ref[...], middle, gate, up, gain, wide_ref, w_out_ref
    )
    d_gate_up_ref[...] = d_gate_up
    gain_out_ref[...] = gain_grad
    d_middle_ref[...] = d_middle
    d_attn_ref[...] = d_attn
    pack_folded(chunks_of(d_attended), sent_ref, 0)


def global_finish_body(
    got_ref, d_middle_ref, x_ref, gain_ref, first_ref, table_ref, d_proj_ref, grad_ref, gain_out_ref
):
    tables = [table_ref[i] for i in range(3)]
    rows = x_ref.shape[0] // 2
    width = x_ref.shape[1]
    d_queries, d_keys = unpack_pairs(got_ref, rows)
    d_values = unpack_folded(got_ref, rows * 3 // 2, rows)
    parts = [unrotate(c, tables).astype(BF) for c in d_queries + d_keys]
    d_projected = jnp.concatenate(parts + [c.astype(BF) for c in d_values], 1)
    d_proj_ref[...] = d_projected
    input_backward(
        d_middle_ref[...], d_projected, x_ref, gain_ref, first_ref, grad_ref, gain_out_ref
    )


def neighbours(count, step):
    return [
        (i, i + step)
        for i in range(count)
        if 0 <= i + step < count and i // GROUP == (i + step) // GROUP
    ]


def exchange(blocks, count):
    groups = [list(range(s, s + GROUP)) for s in range(0, count, GROUP)]
    return lax.all_to_all(blocks, "dp", 0, 0, axis_index_groups=groups)


def to_other_section(rows, step):
    return lax.ppermute(rows, "section", [(0, 1)] if step > 0 else [(1, 0)])


def partner(rows, apart, count):
    return lax.ppermute(rows, "dp", [(i, i ^ apart) for i in range(count)])


def group_pieces(piece, count):
    pieces = {0: piece}
    for apart in (4, 8, 12):
        pieces[apart] = partner(piece, apart, count)
    for apart in (0, 4, 8, 12):
        pieces[apart + 2] = partner(pieces[apart], 2, count)
    for apart in range(0, GROUP, 2):
        pieces[apart + 1] = partner(pieces[apart], 1, count)
    return [pieces[apart] for apart in range(GROUP)]


def in_order(pieces, group_pos, count):
    shape = pieces[0].shape
    whole = jnp.zeros((GROUP,) + shape, pieces[0].dtype)
    for apart, item in enumerate(pieces):
        start = (group_pos ^ apart,) + (0,) * len(shape)
        whole = lax.dynamic_update_slice(whole, item[None], start)
    if count > GROUP:
        groups = [list(range(s, count, GROUP)) for s in range(GROUP)]
        whole = lax.all_gather(whole, "dp", axis=0, tiled=True, axis_index_groups=groups)
    return whole.reshape(-1, shape[-1])


def plane_rows(rows, group_pos, count):
    parts = rows.reshape(count // GROUP, 4, 4, *rows.shape[1:])
    place = group_pos % 4
    taken = []
    for apart in range(4):
        block = lax.dynamic_index_in_dim(parts, place ^ apart, 2, keepdims=False)
        taken.append((partner(block, apart, count) if apart else block).swapaxes(0, 1))
    return taken


def product_body(*refs):
    out_ref = refs[-1]
    column = 0
    for start in range(0, len(refs) - 1, 8):
        left = jnp.concatenate([ref[...] for ref in refs[start : start + 4]], 1)
        right = jnp.concatenate([ref[...] for ref in refs[start + 4 : start + 8]], 0)
        end = column + right.shape[1]
        out_ref[:, column:end] = dot(left, right).astype(BF)
        column = end


def plane_product(terms):
    planes, groups, rows, tokens = terms[0][0][0].shape
    args = [
        part
        for lefts, rights in terms
        for part in [item.reshape(-1, tokens) for item in lefts] + list(rights)
    ]
    columns = sum(rights[0].shape[1] for _, rights in terms)
    (product,) = on_core(product_body, 2.0, [((planes * groups * rows, columns), BF)], args)
    return product.reshape(planes, groups, rows, columns)


def sum_planes(blocks, count):
    groups = [
        [s + 4 * z + k for z in range(4)] for s in range(0, count, GROUP) for k in range(4)
    ]
    got = lax.all_to_all(blocks, "dp", 0, 0, axis_index_groups=groups)
    total = jnp.sum(got.astype(F32), 0)
    if count > GROUP:
        apart = [list(range(s, count, GROUP)) for s in range(GROUP)]
        return lax.psum_scatter(total, "dp", scatter_dimension=0, axis_index_groups=apart)
    return total[0]


def on_device(
    tokens_in,
    segment_ids,
    out_grad,
    qkv_weight,
    attn_out_weight,
    mlp_in_weight,
    mlp_out_weight,
    attn_gain,
    mlp_gain,
):
    lower = lax.axis_index("section") == 0
    count = lax.axis_size("dp")
    replica = lax.axis_index("dp")
    group_pos = replica % GROUP
    micro_count, row_count, width = tokens_in.shape
    shard = qkv_weight.shape[1]
    runs = -(-row_count // shard)
    (message,) = on_core(
        message_body,
        1.0,
        [((shard, 3 * width + LANES), BF)],
        (qkv_weight[0], attn_gain, mlp_gain, segment_ids),
        [pltpu.VMEM((LANES, LANES), F32), pltpu.VMEM((8, LANES), F32)],
    )
    second = lax.all_gather(
        jnp.concatenate([attn_out_weight[0], mlp_in_weight[0]], 1), "dp", axis=0, tiled=True
    )
    pieces = group_pieces(message, count)
    late_weight, pieces = lax.optimization_barrier((mlp_out_weight[0], pieces))
    if count > GROUP:
        pieces = [in_order(pieces, group_pos, count)]
    w_out = in_order(group_pieces(late_weight, count), group_pos, count)

    positions = group_pos * row_count + jnp.arange(row_count)
    local_tables = angles(positions, local_log_base)
    global_tables = angles(positions, global_log_base)

    rows = micro_count * row_count
    inner = second.shape[1] - width
    hidden = w_out.shape[0]
    pairs = rows * width // (row_count * LANES)
    in_0 = tokens_in.reshape(rows, width)
    extra_rows = -(-(2 + micro_count * runs) // 8) * 8
    first, extra, normed_0, q_0, kv_0 = on_core(
        local_project_body,
        5,
        [
            ((width, 3 * width + LANES), BF),
            ((extra_rows, width), F32),
            ((rows, width), BF),
            ((rows, width), BF),
            ((rows, 2 * width), BF),
        ],
        (group_pos[None], in_0, local_tables, *pieces),
        [pltpu.SemaphoreType.DMA((len(pieces),))],
        [pltpu.SMEM, pltpu.VMEM, pltpu.VMEM] + [pl.ANY] * len(pieces),
    )
    gain_attn, gain_mlp = extra[:1], extra[1:2]
    all_ids = extra[2 : 2 + micro_count * runs].reshape(micro_count, runs, count, shard)
    all_ids = lax.dynamic_slice_in_dim(all_ids, replica - group_pos, GROUP, 2)
    all_ids = all_ids.swapaxes(1, 2).reshape(micro_count, GROUP, runs * shard)[..., :row_count]
    segments = all_ids.reshape(micro_count, GROUP * row_count).astype(jnp.int32)

    key_pos = positions[0] - row_count + jnp.arange(3 * row_count)
    around = jnp.pad(segments, ((0, 0), (row_count, row_count)), constant_values=-1)
    key_seg = lax.dynamic_slice_in_dim(around, group_pos * row_count, 3 * row_count, 1)
    visible = (key_seg[:, :, None] == segment_ids[:, None, :]) & (
        jnp.abs(positions[None, :] - key_pos[:, None]) <= HALF_WIN
    )[None]
    bias = jnp.tile(jnp.where(visible, 0.0, masked_score), (1, 1, 2))

    own_seg = lax.dynamic_index_in_dim(segments, group_pos // 8, 0, keepdims=False)
    halves = own_seg.reshape(GROUP, 2, row_count // 2)
    mine = lax.dynamic_index_in_dim(halves, group_pos % 2, 1, keepdims=False).reshape(-1)
    theirs = lax.dynamic_index_in_dim(halves, 1 - group_pos % 2, 1, keepdims=False).reshape(-1)
    shared_seg = jnp.concatenate([mine, theirs])[:, None]
    own_seg = own_seg[:, None]

    up_pairs, down_pairs = neighbours(count, 1), neighbours(count, -1)
    around_0 = (
        lax.ppermute(kv_0, "dp", up_pairs),
        kv_0,
        lax.ppermute(kv_0, "dp", down_pairs),
    )
    att_0, total_0 = on_core(
        local_forward_body,
        3.6,
        [((rows, width), BF), ((pairs, 1, LANES), F32)],
        (q_0, *around_0, bias),
    )
    out_0, n2_0, mixed_0, middle_0, gate_up_0 = on_core(
        local_middle_body,
        2.2,
        [
            ((rows, width), BF),
            ((rows, width), BF),
            ((rows, hidden), BF),
            ((rows, width), F32),
            ((rows, inner), F32),
        ],
        (in_0, att_0, gain_mlp, second, w_out),
    )

    in_1 = to_other_section(out_0, 1)
    fold = row_count * 3 // 4
    half = row_count // 2
    normed_1, sent = on_core(
        global_project_body,
        1.2,
        [((rows, width), BF), ((GROUP, 3 * fold, LANES), BF)],
        (in_1, gain_attn, first, global_tables),
    )
    got = exchange(sent, count)
    beside = jnp.concatenate(
        [got[:, row_count : row_count + half], got[:, 3 * fold - half :]], 1
    )
    beside = partner(beside, 1, count)
    keys = GROUP * row_count
    tiles = keys * 3 // 2 // TILE
    head_scratch = [
        pltpu.VMEM((keys * 3 // 2, LANES), BF),
        pltpu.VMEM((2, keys, LANES), BF),
        pltpu.VMEM((2, keys, LANES), BF),
        pltpu.VMEM((2, LANES, keys), BF),
    ]
    folded, total_1 = on_core(
        global_forward_body,
        7,
        [((GROUP, fold, LANES), BF), ((tiles, 1, TILE), F32)],
        (got, beside, own_seg, shared_seg),
        head_scratch + [pltpu.VMEM((keys * 3 // 2, LANES), F32)],
    )
    folded = exchange(folded, count)

    up_1 = out_grad.reshape(rows, width)
    out_1, att_1, n2_1, mixed_1, d_gu_1, gain_mlp_1, d_mid_1, d_attn_1, sent = on_core(
        global_middle_body,
        4.2,
        [
            ((rows, width), BF),
            ((rows, width), BF),
            ((rows, width), BF),
            ((rows, hidden), BF),
            ((rows, inner), BF),
            ((1, width), F32),
            ((rows, width), F32),
            ((rows, width), BF),
            ((GROUP, fold, LANES), BF),
        ],
        (folded, in_1, up_1, gain_mlp, second, w_out),
    )
    d_folded = exchange(sent, count)
    sent, to_beside = on_core(
        global_backward_body,
        9,
        [((GROUP, 3 * fold, LANES), BF), ((GROUP, 2 * half, LANES), BF)],
        (got, beside, own_seg, shared_seg, total_1, d_folded),
        head_scratch
        + [
            pltpu.VMEM((keys * 3 // 2, LANES), BF),
            pltpu.VMEM((keys * 3 // 2, LANES), F32),
            pltpu.VMEM((2, keys, LANES), F32),
            pltpu.VMEM((2, keys, LANES), F32),
        ],
    )
    back = partner(to_beside, 1, count)
    gap = 3 * fold - half - row_count - half
    back = jnp.concatenate(
        [
            jnp.zeros((GROUP, row_count, LANES), BF),
            back[:, :half],
            jnp.zeros((GROUP, gap, LANES), BF),
            back[:, half:],
        ],
        1,
    )
    sent = (sent.astype(F32) + back.astype(F32)).astype(BF)
    got = exchange(sent, count)

    n1, att, n2, mixed = (
        jnp.where(lower, a, b).T.reshape(count, -1, micro_count * row_count)
        for a, b in (
            (normed_0, normed_1),
            (att_0, att_1),
            (n2_0, n2_1),
            (mixed_0, mixed_1),
        )
    )
    left = jnp.concatenate([n1, att, n2, mixed], 1)
    left, got = lax.optimization_barrier((left, got))
    left = plane_rows(left, group_pos, count)
    n1, att, n2, mixed = (
        [part[:, :, start:end] for part in left]
        for start, end in (
            (0, shard),
            (shard, 2 * shard),
            (2 * shard, 3 * shard),
            (3 * shard, left[0].shape[2]),
        )
    )
    d_proj_1, grad_1, gain_attn_1 = on_core(
        global_finish_body,
        1.6,
        [((rows, 3 * width), BF), ((rows, width), BF), ((1, width), F32)],
        (got, d_mid_1, in_1, gain_attn, first, global_tables),
    )

    up_0 = to_other_section(grad_1, -1)
    d_mlp = jnp.where(lower, up_0, up_1)
    across, beside = partner(d_mlp, 2, count), partner(d_mlp, 1, count)
    d_mlp = [d_mlp, beside, across, partner(across, 1, count)]
    out_blocks = plane_product([(mixed, d_mlp)])
    d_gu_0, gain_mlp_0, d_mid_0, d_attn_0, d_att_0 = on_core(
        local_back_middle_body,
        2.9,
        [
            ((rows, inner), BF),
            ((1, width), F32),
            ((rows, width), F32),
            ((rows, width), BF),
            ((rows, width), BF),
        ],
        (up_0, middle_0, gate_up_0, gain_mlp, second, w_out),
    )
    own = [jnp.where(lower, d_gu_0, d_gu_1), jnp.where(lower, d_attn_0, d_attn_1)]
    beside = [partner(item, 1, count) for item in own]
    across = [partner(item, 2, count) for item in own]
    dq_0, d_own, d_before, d_after = on_core(
        local_backward_body,
        4.2,
        [
            ((rows, width), BF),
            ((rows, 2 * width), F32),
            ((rows, 2 * width), BF),
            ((rows, 2 * width), BF),
        ],
        (q_0, *around_0, bias, total_0, d_att_0, local_tables),
    )
    from_after = lax.ppermute(d_before, "dp", down_pairs)
    from_before = lax.ppermute(d_after, "dp", up_pairs)
    from_after, out_blocks = lax.optimization_barrier((from_after, out_blocks))
    mlp_out_share = sum_planes(out_blocks, count)
    (d_proj_0,) = on_core(
        local_join_body,
        0.5,
        [((rows, 3 * width), BF)],
        (dq_0, d_own, from_after, from_before, local_tables),
    )
    d_proj = jnp.where(lower, d_proj_0, d_proj_1)
    far = [partner(item, 1, count) for item in across]
    d_gu, d_attn = zip(own, beside, across, far)
    in_blocks = plane_product([(n2, d_gu), (att, d_attn)])
    in_share = sum_planes(in_blocks, count)
    across = partner(d_proj, 2, count)
    across, in_blocks = lax.optimization_barrier((across, in_blocks))
    d_proj = [d_proj, partner(d_proj, 1, count), across, partner(across, 1, count)]
    qkv_blocks = plane_product([(n1, d_proj)])
    qkv_share = sum_planes(qkv_blocks, count)
    grad_0, gain_attn_0 = on_core(
        input_backward_body,
        1.5,
        [((rows, width), BF), ((1, width), F32)],
        (d_mid_0, d_proj_0, in_0, gain_attn, first),
    )

    gains = jnp.where(
        lower,
        jnp.concatenate([gain_attn_0, gain_mlp_0]),
        jnp.concatenate([gain_attn_1, gain_mlp_1]),
    )
    gains, _ = lax.optimization_barrier((gains, qkv_blocks))
    apart = 1
    while apart < count:
        gains = gains + partner(gains, apart, count)
        apart *= 2
    gains = lax.dynamic_slice_in_dim(gains, replica * shard, shard, 1)

    return (
        jnp.where(lower, out_0, out_1).reshape(1, micro_count, row_count, width),
        jnp.where(lower, grad_0, grad_1).reshape(1, micro_count, row_count, width),
        qkv_share[None],
        in_share[None, :, inner:],
        in_share[None, :, :inner],
        mlp_out_share[None],
        gains[:1],
        gains[1:],
    )


def solution(mesh):
    in_specs = (
        P(None, "dp", None),
        P(None, "dp"),
        P(None, "dp", None),
        P("section", "dp", None),
        P("section", "dp", None),
        P("section", "dp", None),
        P("section", "dp", None),
        P("section", "dp"),
        P("section", "dp"),
    )
    out_specs = (
        P("section", None, "dp", None),
        P("section", None, "dp", None),
        P("section", "dp", None),
        P("section", "dp", None),
        P("section", "dp", None),
        P("section", "dp", None),
        P("section", "dp"),
        P("section", "dp"),
    )
    return jax.shard_map(
        on_device, mesh=mesh, in_specs=in_specs, out_specs=out_specs, check_vma=False
    )
```

```python
import functools
import math

import jax
import jax.numpy as jnp
from jax import lax
from jax.experimental import pallas as pl
from jax.experimental.pallas import tpu as pltpu
from jax.sharding import PartitionSpec as P

HEAD_DIM = 64
GROUP = 16
HALF_WIN = 64
LANES = 128
TILE = 256

local_log_base = math.log(10000.0)
global_log_base = math.log(160000.0)
masked_score = -1e30
SCALE = 1.0 / math.sqrt(HEAD_DIM)
BF = jnp.bfloat16
F32 = jnp.float32


def dot(left, right):
    return jnp.dot(left, right, preferred_element_type=F32)


def dot_bt(left, right):
    return lax.dot_general(left, right, (((1,), (1,)), ((), ())), preferred_element_type=F32)


def dot_at(left, right):
    return lax.dot_general(left, right, (((0,), (0,)), ((), ())), preferred_element_type=F32)


def moments(values):
    center = values - jnp.mean(values, -1, keepdims=True)
    scale = lax.rsqrt(jnp.mean(center * center, -1, keepdims=True) + 1e-05)
    return center * scale, scale


def norm_back(grad_out, gain_row, xhat, scale):
    scaled = grad_out * gain_row
    mean_grad = jnp.mean(scaled, -1, keepdims=True)
    mean_dot = jnp.mean(scaled * xhat, -1, keepdims=True)
    return (scaled - mean_grad - xhat * mean_dot) * scale


def angles(positions, log_base):
    half_dim = HEAD_DIM // 2
    fraction = (2 * jnp.arange(half_dim)).astype(F32) / HEAD_DIM
    inverse = jnp.exp(-fraction * log_base)
    table = positions.astype(F32)[:, None] * inverse[None, :]
    cosine, sine = jnp.cos(table), jnp.sin(table)
    none = jnp.zeros_like(sine)
    cosine = jnp.concatenate([cosine, cosine], 1)
    to_first = jnp.concatenate([-sine, none], 1)
    to_second = jnp.concatenate([none, sine], 1)
    return jnp.tile(jnp.stack([cosine, to_first, to_second]), (1, 2, 2))


def on_core(body, outs, args, scratch=(), spaces=None, out_spaces=None):
    return pl.pallas_call(
        body,
        out_shape=[jax.ShapeDtypeStruct(shape, dtype) for shape, dtype in outs],
        in_specs=[
            pl.BlockSpec(memory_space=space) for space in spaces or [pltpu.VMEM] * len(args)
        ],
        out_specs=[
            pl.BlockSpec(memory_space=space) for space in out_spaces or [pltpu.VMEM] * len(outs)
        ],
        scratch_shapes=scratch,
        cost_estimate=pl.CostEstimate(
            flops=2**10, bytes_accessed=2**10, transcendentals=0
        ),
        compiler_params=pltpu.CompilerParams(vmem_limit_bytes=32 * 2**20),
    )(*args)


def low_lanes():
    return lax.broadcasted_iota(jnp.int32, (1, LANES), 1) < HEAD_DIM


def swap(chunk):
    return pltpu.roll(chunk, HEAD_DIM, 1)


def chunks_of(rows):
    return [rows[:, c : c + LANES] for c in range(0, rows.shape[1], LANES)]


def rotate(chunk, tables):
    cosine, to_first, to_second = tables
    quarter = HEAD_DIM // 2
    return (
        chunk * cosine
        + pltpu.roll(chunk, LANES - quarter, 1) * to_first
        + pltpu.roll(chunk, quarter, 1) * to_second
    )


def unrotate(chunk, tables):
    cosine, to_first, to_second = tables
    quarter = HEAD_DIM // 2
    return (
        chunk * cosine
        - pltpu.roll(chunk, LANES - quarter, 1) * to_first
        - pltpu.roll(chunk, quarter, 1) * to_second
    )


def low_and_high(chunks):
    swapped = [swap(chunk) for chunk in chunks]
    low = [(swapped if h % 2 else chunks)[h // 2] for h in range(2 * len(chunks))]
    high = [(chunks if h % 2 else swapped)[h // 2] for h in range(2 * len(chunks))]
    return low, high


def targets():
    for d in range(GROUP):
        micro, chip, half = d // 8, d % 8 // 2, d % 2
        yield d, micro, 3 * chip + 2 * half, 3 * chip + 1, half


def pack_folded(chunks, ref, base):
    low, high = low_and_high(chunks)
    first = low_lanes()
    rows = chunks[0].shape[0] // 2
    half, fold = rows // 2, rows * 3 // 4
    for d, micro, own, shared, side in targets():
        start = micro * rows
        part = start + side * half
        upper = jnp.concatenate(
            [high[own][start + fold : start + rows], high[shared][part : part + half]], 0
        )
        ref[d, base : base + fold] = jnp.where(
            first, low[own][start : start + fold], upper
        ).astype(BF)


def pack_pairs(lefts, rights, ref):
    low, high = low_and_high(lefts)[0], low_and_high(rights)[1]
    first = low_lanes()
    rows = lefts[0].shape[0] // 2
    half = rows // 2
    for d, micro, own, shared, side in targets():
        start = micro * rows
        part = start + side * half
        ref[d, 0:rows] = jnp.where(
            first, low[own][start : start + rows], high[own][start : start + rows]
        ).astype(BF)
        ref[d, rows : rows + half] = jnp.where(
            first, low[shared][part : part + half], high[shared][part : part + half]
        ).astype(BF)


def unpack_folded(ref, base, rows):
    first = low_lanes()
    fold = rows * 3 // 4
    low, high = {}, {}
    shared_parts = {}
    for d, micro, own, shared, side in targets():
        block = ref[d, base : base + fold].astype(F32)
        mine = jnp.concatenate([block, swap(block[: rows - fold])], 0)
        if own % 2:
            high[micro, own] = swap(mine)
        else:
            low[micro, own] = mine
        shared_parts[micro, shared, side] = block[rows - fold :]
        if side:
            both = jnp.concatenate([shared_parts[micro, shared, 0], block[rows - fold :]], 0)
            if shared % 2:
                high[micro, shared] = both
            else:
                low[micro, shared] = swap(both)
    heads = GROUP // 4 * 3
    return [
        jnp.concatenate(
            [jnp.where(first, low[m, h], high[m, h + 1]) for m in range(2)], 0
        )
        for h in range(0, heads, 2)
    ]


def unpack_pairs(ref, rows):
    first = low_lanes()
    half = rows // 2
    pairs = {}
    parts = {}
    for d, micro, own, shared, side in targets():
        pairs[micro, own] = ref[d, 0:rows].astype(F32)
        parts[side] = ref[d, rows : rows + half].astype(F32)
        if side:
            pairs[micro, shared] = jnp.concatenate([parts[0], parts[1]], 0)
    heads = GROUP // 4 * 3
    lefts, rights = [], []
    for h in range(0, heads, 2):
        even, odd = [pairs[m, h] for m in range(2)], [pairs[m, h + 1] for m in range(2)]
        lefts.append(
            jnp.concatenate([jnp.where(first, a, swap(b)) for a, b in zip(even, odd)], 0)
        )
        rights.append(
            jnp.concatenate([jnp.where(first, swap(a), b) for a, b in zip(even, odd)], 0)
        )
    return lefts, rights


class Weights:
    def __init__(self, sources, scratches, sem):
        attn, mlp_in, mlp_out = self.places = scratches
        width = attn.shape[1]
        copies = [[], [], []]
        if len(sources) == 1:
            (stacked,) = sources
            shard = attn.shape[0] // GROUP
            columns = mlp_in.shape[1] // width
            pair = 2 * mlp_out.shape[0] // GROUP
            upper = first_block(pair)
            block = shard * (1 + columns) + upper
            for d in range(GROUP):
                base = d * block
                here = pl.ds(d * shard, shard)
                copies[0].append((stacked.at[pl.ds(base, shard)], attn.at[here]))
                for p in range(columns):
                    copies[1].append(
                        (
                            stacked.at[pl.ds(base + (1 + p) * shard, shard)],
                            mlp_in.at[here, pl.ds(p * width, width)],
                        )
                    )
                rows = pair - upper if d % 2 else upper
                start = d // 2 * pair + d % 2 * upper
                copies[2].append(
                    (
                        stacked.at[pl.ds(base + (1 + columns) * shard, rows)],
                        mlp_out.at[pl.ds(start, rows)],
                    )
                )
        else:
            for group, source, place in zip(copies, sources, scratches):
                group.append((source, place))
        self.copies, index = [], 0
        for group in copies:
            self.copies.append([])
            for source, place in group:
                self.copies[-1].append(pltpu.make_async_copy(source, place, sem.at[index]))
                index += 1

    def start(self, order):
        for which in order:
            for copy in self.copies[which]:
                copy.start()

    def get(self, which):
        for copy in self.copies[which]:
            copy.wait()
        self.copies[which] = []
        return self.places[which][...]


def first_block(pair):
    return -(-pair // 32) * 16


def weight_scratch(width, inner, hidden):
    return [
        pltpu.VMEM((width, width), BF),
        pltpu.VMEM((width, inner), BF),
        pltpu.VMEM((hidden, width), BF),
        pltpu.SemaphoreType.DMA((GROUP * (2 + inner // width),)),
    ]


def mlp_forward(layer_in, attended, gain, weights):
    middle = layer_in + dot(attended, weights.get(0))
    xhat, _ = moments(middle)
    normed = (xhat * gain).astype(BF)
    gate_up = dot(normed, weights.get(1))
    half = gate_up.shape[1] // 2
    gate, up = gate_up[:, :half], gate_up[:, half:]
    cdf = 0.5 * (1.0 + lax.erf(gate * math.sqrt(0.5)))
    mixed = (gate * cdf * up).astype(BF)
    result = (middle + dot(mixed, weights.get(2))).astype(BF)
    return middle, normed, gate, up, mixed, result


def mlp_backward(upstream, middle, gate, up, gain, weights):
    d_mixed = dot_bt(upstream, weights.get(2))
    cdf = 0.5 * (1.0 + lax.erf(gate * math.sqrt(0.5)))
    density = jnp.exp(-0.5 * gate * gate) * (1.0 / math.sqrt(2.0 * math.pi))
    d_gate = d_mixed * up * (cdf + gate * density)
    d_up = d_mixed * gate * cdf
    d_gate_up = jnp.concatenate([d_gate.astype(BF), d_up.astype(BF)], 1)
    d_normed = dot_bt(d_gate_up, weights.get(1))
    xhat, scale = moments(middle)
    gain_grad = jnp.sum(d_normed * xhat, 0, keepdims=True)
    d_middle = upstream.astype(F32) + norm_back(d_normed, gain, xhat, scale)
    d_attn = d_middle.astype(BF)
    d_attended = dot_bt(d_attn, weights.get(0))
    return d_gate_up, gain_grad, d_middle, d_attn, d_attended


def parts_of(first_ref, place, sem):
    width = place.shape[0]
    return [
        pltpu.make_async_copy(
            first_ref.at[:, pl.ds(c * width, width)], place.at[:, pl.ds(c * width, width)], sem.at[c]
        )
        for c in range(3)
    ]


def qkv_scratch(width):
    return [pltpu.VMEM((width, 3 * width), BF), pltpu.SemaphoreType.DMA((3,))]


def project(xhat, gain, first_ref, table_ref, normed_ref, copies=(None,) * 3):
    width = xhat.shape[1]
    normed = (xhat * gain).astype(BF)
    normed_ref[...] = normed
    tables = [table_ref[i] for i in range(3)]
    results = []
    for part, copy in enumerate(copies):
        if copy is not None:
            copy.wait()
        results.append(dot(normed, first_ref[:, part * width : (part + 1) * width]))
    queries, keys, values = chunks_of(results[0]), chunks_of(results[1]), results[2]
    return [rotate(c, tables) for c in queries], [rotate(c, tables) for c in keys], values


def input_backward(d_middle, d_projected, x_ref, gain_ref, place, copies, grad_ref, gain_out_ref):
    width = x_ref.shape[1]
    xhat, scale = moments(x_ref[...].astype(F32))
    d_normed = jnp.zeros(x_ref.shape, F32)
    for part, copy in enumerate(copies):
        copy.wait()
        lanes = slice(part * width, (part + 1) * width)
        d_normed += dot_bt(d_projected[:, lanes], place[:, lanes])
    gain_out_ref[...] = jnp.sum(d_normed * xhat, 0, keepdims=True)
    grad_ref[...] = (d_middle + norm_back(d_normed, gain_ref[...], xhat, scale)).astype(BF)


def message_body(w_ref, attn_ref, mlp_ref, ids_ref, out_ref, rows_scr, ids_scr):
    shard, columns = w_ref.shape
    micro_count, row_count = ids_ref.shape
    out_ref[:, :columns] = w_ref[...]
    rows_scr[...] = jnp.zeros_like(rows_scr)
    ids_scr[...] = jnp.zeros_like(ids_scr)
    rows_scr[0:1, :shard] = attn_ref[...].astype(F32)
    rows_scr[1:2, :shard] = mlp_ref[...].astype(F32)
    ids_scr[:micro_count, :row_count] = ids_ref[...].astype(F32)
    runs = -(-row_count // shard)
    for run in range(runs):
        turned = ids_scr[...]
        if run:
            turned = pltpu.roll(turned, LANES - run * shard, 1)
        for micro in range(micro_count):
            row = 2 + micro * runs + run
            rows_scr[row : row + 1] = turned[micro : micro + 1]
    out_ref[:, columns:] = rows_scr[...].T[:shard].astype(BF)


def local_project_body(place_ref, x_ref, table_ref, *refs):
    pieces, refs = refs[:-8], refs[-8:]
    stored_ref, extra_ref, normed_ref, q_ref, kv_ref, first_ref, sem, store_sem = refs
    rows = pieces[0].shape[0]
    copies = []
    for apart, piece in enumerate(pieces):
        start = pl.multiple_of((place_ref[0] ^ apart) * rows, rows) if len(pieces) > 1 else 0
        copies.append(
            pltpu.make_async_copy(piece, first_ref.at[pl.ds(start, rows)], sem.at[apart])
        )
        copies[-1].start()
    xhat, _ = moments(x_ref[...].astype(F32))
    for copy in copies:
        copy.wait()
    store = pltpu.make_async_copy(first_ref, stored_ref, store_sem)
    store.start()
    extra = first_ref[:, first_ref.shape[1] - LANES :].astype(F32).T
    extra_ref[...] = extra[: extra_ref.shape[0]]
    queries, keys, values = project(xhat, extra[:1], first_ref, table_ref, normed_ref)
    width = values.shape[1]
    for j, (q, k) in enumerate(zip(queries, keys)):
        q_ref[:, LANES * j : LANES * (j + 1)] = q.astype(BF)
        kv_ref[:, LANES * j : LANES * (j + 1)] = k.astype(BF)
    kv_ref[:, width:] = values.astype(BF)
    store.wait()


def two_heads(chunk):
    first = low_lanes()
    wide = chunk.astype(F32)
    return jnp.concatenate([jnp.where(first, wide, 0.0), jnp.where(first, 0.0, wide)], 0)


def pick_heads(rows):
    half = rows.shape[0] // 2
    return jnp.where(low_lanes(), rows[:half], rows[half:])


def local_parts(q_ref, before_ref, own_ref, after_ref):
    rows = q_ref.shape[0] // 2
    width = q_ref.shape[1]
    for micro in range(2):
        for j in range(width // LANES):
            here = slice(micro * rows, (micro + 1) * rows)
            lanes = slice(LANES * j, LANES * (j + 1))
            more = slice(width + LANES * j, width + LANES * (j + 1))
            keys, values = (
                jnp.concatenate([ref[here, part] for ref in (before_ref, own_ref, after_ref)], 0)
                for part in (lanes, more)
            )
            queries = (two_heads(q_ref[here, lanes]) * SCALE).astype(BF)
            yield micro * (width // LANES) + j, micro, here, lanes, more, queries, keys, values


def local_forward_body(q_ref, before_ref, own_ref, after_ref, bias_ref, att_ref, total_ref):
    parts = local_parts(q_ref, before_ref, own_ref, after_ref)
    for index, micro, here, lanes, _, queries, keys, values in parts:
        scores = dot_bt(keys, queries) + bias_ref[micro]
        peak = jnp.max(scores, 0, keepdims=True)
        weights = jnp.exp(scores - peak)
        total = jnp.sum(weights, 0, keepdims=True)
        total_ref[index] = peak + jnp.log(total)
        probs = (weights * (1.0 / total)).astype(BF)
        att_ref[here, lanes] = pick_heads(dot_at(probs, values)).astype(BF)


def local_backward_body(
    q_ref, before_ref, own_ref, after_ref, bias_ref, total_ref, d_ref, table_ref,
    dq_ref, d_own_ref, d_before_ref, d_after_ref,
):
    tables = [table_ref[i] for i in range(3)]
    parts = local_parts(q_ref, before_ref, own_ref, after_ref)
    rows = q_ref.shape[0] // 2
    for index, micro, here, lanes, more, queries, keys, values in parts:
        d_out = two_heads(d_ref[here, lanes]).astype(BF)
        probs = jnp.exp(dot_bt(keys, queries) + bias_ref[micro] - total_ref[index])
        d_probs = dot_bt(values, d_out)
        product = probs * d_probs
        delta = jnp.sum(product, 0, keepdims=True)
        d_scores = (product - probs * delta).astype(BF)
        d_queries = pick_heads(dot_at(d_scores, keys)) * SCALE
        local_tables = [table[here] for table in tables]
        dq_ref[here, lanes] = unrotate(d_queries, local_tables).astype(BF)
        for part, grads in ((lanes, dot(d_scores, queries)), (more, dot(probs.astype(BF), d_out))):
            d_before_ref[here, part] = grads[:rows].astype(BF)
            d_own_ref[here, part] = grads[rows : 2 * rows]
            d_after_ref[here, part] = grads[2 * rows :].astype(BF)


def local_join_body(
    lower_ref, dq_ref, own_ref, low_ref, high_ref, table_ref, other_ref, out_ref
):
    width = dq_ref.shape[1]

    @pl.when(lower_ref[0] == 1)
    def _():
        tables = [table_ref[i] for i in range(3)]
        out_ref[:, :width] = dq_ref[...]
        total = own_ref[...] + low_ref[...].astype(F32) + high_ref[...].astype(F32)
        for j, chunk in enumerate(chunks_of(total[:, :width])):
            start = width + LANES * j
            out_ref[:, start : start + LANES] = unrotate(chunk, tables).astype(BF)
        out_ref[:, 2 * width :] = total[:, width:].astype(BF)

    @pl.when(lower_ref[0] == 0)
    def _():
        out_ref[...] = other_ref[...]


def local_middle_body(*refs):
    sources, refs = refs[:-12], refs[-12:]
    x_ref, att_ref, gain_ref, out_ref, normed_ref, mixed_ref, middle_ref, gate_up_ref = refs[:8]
    weights = Weights(sources, refs[8:11], refs[11])
    weights.start((0, 1, 2))
    middle, normed, gate, up, mixed, result = mlp_forward(
        x_ref[...].astype(F32), att_ref[...], gain_ref[...], weights
    )
    out_ref[...] = result
    normed_ref[...] = normed
    mixed_ref[...] = mixed
    middle_ref[...] = middle
    half = gate.shape[1]
    gate_up_ref[:, :half] = gate
    gate_up_ref[:, half:] = up


def local_back_middle_body(*refs):
    sources, refs = refs[:-14], refs[-14:]
    lower_ref, up_ref, middle_ref, gate_up_ref, gain_ref, other_ref = refs[:6]
    right_ref, gain_out_ref, d_middle_ref, d_att_ref = refs[6:10]
    weights = Weights(sources, refs[10:13], refs[13])
    weights.start((2, 1, 0))
    half = gate_up_ref.shape[1] // 2
    d_gate_up, gain_grad, d_middle, d_attn, d_attended = mlp_backward(
        up_ref[...], middle_ref[...], gate_up_ref[:, :half], gate_up_ref[:, half:],
        gain_ref[...], weights,
    )
    gain_out_ref[...] = gain_grad
    d_middle_ref[...] = d_middle
    d_att_ref[...] = d_attended.astype(BF)

    @pl.when(lower_ref[0] == 1)
    def _():
        right_ref[:, : 2 * half] = d_gate_up
        right_ref[:, 2 * half :] = d_attn

    @pl.when(lower_ref[0] == 0)
    def _():
        right_ref[...] = other_ref[...]


def input_backward_body(
    first_ref, d_middle_ref, d_proj_ref, x_ref, gain_ref, grad_ref, gain_out_ref, place, sem
):
    copies = parts_of(first_ref, place, sem)
    for copy in copies:
        copy.start()
    input_backward(
        d_middle_ref[...], d_proj_ref[...], x_ref, gain_ref, place, copies, grad_ref, gain_out_ref
    )


def global_project_body(first_ref, x_ref, gain_ref, table_ref, normed_ref, sent_ref, place, sem):
    copies = parts_of(first_ref, place, sem)
    for copy in copies:
        copy.start()
    xhat, _ = moments(x_ref[...].astype(F32))
    queries, keys, values = project(xhat, gain_ref[...], place, table_ref, normed_ref, copies)
    pack_pairs(queries, keys, sent_ref)
    pack_folded(chunks_of(values), sent_ref, sent_ref.shape[1] * 2 // 3)


def flat(blocks):
    return blocks.reshape(-1, LANES)


def own_unfolded(ref, base, rows):
    fold = rows * 3 // 4
    block = ref[:, base : base + fold].astype(F32)
    rest = swap(flat(block[:, : rows - fold])).reshape(GROUP, rows - fold, LANES)
    return flat(jnp.concatenate([block, rest], 1))


def shared_unfolded(ref, start, rows):
    return swap(flat(ref[:, start : start + rows // 2].astype(F32)))


def fill_heads(got_ref, other_ref, own_seg_ref, shared_seg_ref, q_scr, k_scr, v_scr):
    rows = got_ref.shape[1] * 4 // 9
    half = rows // 2
    first = low_lanes()
    lane = lax.broadcasted_iota(jnp.int32, (1, LANES), 1) - HEAD_DIM
    own = flat(got_ref[:, 0:rows].astype(F32))
    shared = flat(got_ref[:, rows : rows + half].astype(F32))
    other = flat(other_ref[:, 0:half].astype(F32))
    count = own.shape[0]
    own_hit = lane == own_seg_ref[...]
    shared_hit = lane == shared_seg_ref[...]
    both = jnp.concatenate([shared, other], 0)
    for start, pairs, hit in (
        (0, own, own_hit),
        (count, shared, shared_hit[: count // 2]),
    ):
        marked = jnp.where(hit, 1.0, 0.0)
        q_scr[start : start + pairs.shape[0]] = jnp.where(first, pairs * SCALE, marked).astype(BF)
    for unit, pairs, hit in ((0, own, own_hit), (1, both, shared_hit)):
        marked = jnp.where(hit, 0.0, masked_score)
        k_scr[unit] = jnp.where(first, swap(pairs), marked).astype(BF)
    base = rows + half
    v_scr[0] = jnp.where(first, own_unfolded(got_ref, base, rows), 0.0).astype(BF)
    start = base + rows - rows * 3 // 4
    shared_v = jnp.concatenate(
        [shared_unfolded(got_ref, start, rows), shared_unfolded(other_ref, half, rows)], 0
    )
    v_scr[1] = jnp.where(first, shared_v, 0.0).astype(BF)


def fold_out(own, shared, rows, ref, base):
    fold = rows * 3 // 4
    blocks = own.reshape(GROUP, rows, LANES)
    swapped = swap(own).reshape(GROUP, rows, LANES)
    upper = jnp.concatenate(
        [swapped[:, fold:], swap(shared).reshape(GROUP, rows // 2, LANES)], 1
    )
    ref[:, base : base + fold] = jnp.where(low_lanes(), blocks[:, :fold], upper).astype(BF)


def global_forward_body(
    got_ref, other_ref, own_seg_ref, shared_seg_ref, out_ref, total_ref,
    q_scr, k_scr, v_scr, vt_scr, o_scr,
):
    fill_heads(got_ref, other_ref, own_seg_ref, shared_seg_ref, q_scr, k_scr, v_scr)
    for unit in range(2):
        vt_scr[unit] = v_scr[unit].astype(F32).T.astype(BF)
    count = k_scr.shape[1]

    def step(tile, carry):
        unit = tile // (count // TILE)
        rows = pl.ds(pl.multiple_of(tile * TILE, TILE), TILE)
        scores = dot_bt(k_scr[unit], q_scr[rows])
        peak = jnp.max(scores, 0, keepdims=True)
        weights = jnp.exp(scores - peak)
        total = jnp.sum(weights, 0, keepdims=True)
        total_ref[tile] = peak + jnp.log(total)
        out = dot(vt_scr[unit], weights.astype(BF)) * (1.0 / total)
        o_scr[rows] = out.T
        return carry

    lax.fori_loop(0, q_scr.shape[0] // TILE, step, 0)
    rows = got_ref.shape[1] * 4 // 9
    fold_out(o_scr[:count], o_scr[count:], rows, out_ref, 0)


def global_backward_body(
    got_ref, other_ref, own_seg_ref, shared_seg_ref, total_ref, d_ref, sent_ref, to_other_ref,
    q_scr, k_scr, v_scr, kt_scr, d_scr, dq_scr, dk_scr, dv_scr,
):
    fill_heads(got_ref, other_ref, own_seg_ref, shared_seg_ref, q_scr, k_scr, v_scr)
    first = low_lanes()
    rows = got_ref.shape[1] * 4 // 9
    half = rows // 2
    for unit in range(2):
        keys = jnp.where(first, k_scr[unit].astype(F32), 0.0)
        kt_scr[unit] = keys.T.astype(BF)
    count = k_scr.shape[1]
    d_scr[:count] = jnp.where(first, own_unfolded(d_ref, 0, rows), 0.0).astype(BF)
    d_scr[count:] = jnp.where(
        first, shared_unfolded(d_ref, rows - rows * 3 // 4, rows), 0.0
    ).astype(BF)
    dk_scr[...] = jnp.zeros_like(dk_scr)
    dv_scr[...] = jnp.zeros_like(dv_scr)

    def step(tile, carry):
        unit = tile // (count // TILE)
        here = pl.ds(pl.multiple_of(tile * TILE, TILE), TILE)
        queries, d_out = q_scr[here], d_scr[here]
        probs = jnp.exp(dot_bt(k_scr[unit], queries) - total_ref[tile])
        d_probs = dot_bt(v_scr[unit], d_out)
        product = probs * d_probs
        delta = jnp.sum(product, 0, keepdims=True)
        d_scores = (product - probs * delta).astype(BF)
        dv_scr[unit] += dot(probs.astype(BF), d_out)
        dk_scr[unit] += dot(d_scores, queries)
        dq_scr[here] = dot(kt_scr[unit], d_scores).T * SCALE
        return carry

    lax.fori_loop(0, q_scr.shape[0] // TILE, step, 0)
    mine = count // 2
    own = jnp.where(first, dq_scr[:count], swap(dk_scr[0]))
    sent_ref[:, 0:rows] = own.reshape(GROUP, rows, LANES).astype(BF)
    shared_k, shared_v = dk_scr[1], dv_scr[1]
    shared = jnp.where(first, dq_scr[count:], swap(shared_k[:mine]))
    sent_ref[:, rows : rows + half] = shared.reshape(GROUP, half, LANES).astype(BF)
    fold_out(dv_scr[0], shared_v[:mine], rows, sent_ref, rows + half)
    for place, grads in enumerate((shared_k, shared_v)):
        other = jnp.where(first, 0.0, swap(grads[mine:])).reshape(GROUP, half, LANES)
        to_other_ref[:, place * half : (place + 1) * half] = other.astype(BF)


def global_middle_body(*refs):
    sources, refs = refs[:-16], refs[-16:]
    got_ref, x_ref, up_ref, gain_ref, out_ref, att_ref, normed_ref, mixed_ref = refs[:8]
    right_ref, gain_out_ref, d_middle_ref, sent_ref = refs[8:12]
    weights = Weights(sources, refs[12:15], refs[15])
    weights.start((0, 1, 2))
    rows = x_ref.shape[0] // 2
    attended = jnp.concatenate([c.astype(BF) for c in unpack_folded(got_ref, 0, rows)], 1)
    att_ref[...] = attended
    gain = gain_ref[...]
    middle, normed, gate, up, mixed, result = mlp_forward(
        x_ref[...].astype(F32), attended, gain, weights
    )
    out_ref[...] = result
    normed_ref[...] = normed
    mixed_ref[...] = mixed
    d_gate_up, gain_grad, d_middle, d_attn, d_attended = mlp_backward(
        up_ref[...], middle, gate, up, gain, weights
    )
    right_ref[:, : d_gate_up.shape[1]] = d_gate_up
    right_ref[:, d_gate_up.shape[1] :] = d_attn
    gain_out_ref[...] = gain_grad
    d_middle_ref[...] = d_middle
    pack_folded(chunks_of(d_attended), sent_ref, 0)


def global_finish_body(
    first_ref, got_ref, d_middle_ref, x_ref, gain_ref, table_ref, d_proj_ref, grad_ref, gain_out_ref, place, sem
):
    copies = parts_of(first_ref, place, sem)
    for copy in copies:
        copy.start()
    tables = [table_ref[i] for i in range(3)]
    rows = x_ref.shape[0] // 2
    d_queries, d_keys = unpack_pairs(got_ref, rows)
    d_values = unpack_folded(got_ref, rows * 3 // 2, rows)
    parts = [unrotate(c, tables).astype(BF) for c in d_queries + d_keys]
    d_projected = jnp.concatenate(parts + [c.astype(BF) for c in d_values], 1)
    d_proj_ref[...] = d_projected
    input_backward(
        d_middle_ref[...], d_projected, x_ref, gain_ref, place, copies, grad_ref, gain_out_ref
    )


def neighbours(count, step):
    return [
        (i, i + step)
        for i in range(count)
        if 0 <= i + step < count and i // GROUP == (i + step) // GROUP
    ]


def exchange(blocks, count):
    groups = [list(range(s, s + GROUP)) for s in range(0, count, GROUP)]
    return lax.all_to_all(blocks, "dp", 0, 0, axis_index_groups=groups)


def to_other_section(rows, step):
    return lax.ppermute(rows, "section", [(0, 1)] if step > 0 else [(1, 0)])


def partner(rows, apart, count):
    return lax.ppermute(rows, "dp", [(i, i ^ apart) for i in range(count)])


def group_pieces(piece, count):
    pieces = {0: piece}
    for apart in (4, 8, 12):
        pieces[apart] = partner(piece, apart, count)
    for apart in (0, 4, 8, 12):
        pieces[apart + 2] = partner(pieces[apart], 2, count)
    for apart in range(0, GROUP, 2):
        pieces[apart + 1] = partner(pieces[apart], 1, count)
    return [pieces[apart] for apart in range(GROUP)]


def in_order(pieces, group_pos, count):
    shape = pieces[0].shape
    whole = jnp.zeros((GROUP,) + shape, pieces[0].dtype)
    for apart, item in enumerate(pieces):
        start = (group_pos ^ apart,) + (0,) * len(shape)
        whole = lax.dynamic_update_slice(whole, item[None], start)
    if count > GROUP:
        groups = [list(range(s, count, GROUP)) for s in range(GROUP)]
        whole = lax.all_gather(whole, "dp", axis=0, tiled=True, axis_index_groups=groups)
    return whole.reshape(-1, shape[-1])


def plane_rows(rows, group_pos, count):
    parts = rows.reshape(count // GROUP, 4, 4, *rows.shape[1:])
    place, plane = group_pos % 4, group_pos // 4
    taken = []
    for apart in range(4):
        block = lax.dynamic_index_in_dim(parts, place ^ apart, 2, keepdims=False)
        block = jnp.stack(
            [lax.dynamic_index_in_dim(block, plane ^ z, 1, keepdims=False) for z in range(4)]
        )
        taken.append(partner(block, apart, count) if apart else block)
    return taken


def product_body(ranges, *refs):
    refs, outs = refs[:-4], refs[-4:]
    rows = outs[0].shape[0]
    for index, (start, end) in enumerate(ranges):
        left = jnp.concatenate([ref[...] for ref in refs[4 + 4 * index : 8 + 4 * index]], 1)
        right = jnp.concatenate([ref[:, start:end] for ref in refs[:4]], 0)
        product = dot(left, right)
        for plane, out_ref in enumerate(outs):
            part = product[plane * rows : (plane + 1) * rows]
            out_ref[:, start:end] = part.astype(out_ref.dtype)


def plane_product(right, terms):
    planes, groups, rows, tokens = terms[0][0][0].shape
    args = list(right) + [item.reshape(-1, tokens) for lefts, _, _ in terms for item in lefts]
    shape = (groups * rows, right[0].shape[1])
    body = functools.partial(product_body, [term[1:] for term in terms])
    return on_core(body, [(shape, F32)] + [(shape, BF)] * (planes - 1), args)


def sum_planes(blocks, count):
    got = [partner(item, 4 * (z + 1), count) for z, item in enumerate(blocks[1:])]
    total = blocks[0]
    for item in got:
        total = total + item.astype(F32)
    if count > GROUP:
        apart = [list(range(s, count, GROUP)) for s in range(GROUP)]
        total = total.reshape(count // GROUP, -1, total.shape[1])
        return lax.psum_scatter(total, "dp", scatter_dimension=0, axis_index_groups=apart)
    return total


def on_device(
    tokens_in,
    segment_ids,
    out_grad,
    qkv_weight,
    attn_out_weight,
    mlp_in_weight,
    mlp_out_weight,
    attn_gain,
    mlp_gain,
):
    lower = lax.axis_index("section") == 0
    lower_flag = lower.astype(jnp.int32)[None]
    count = lax.axis_size("dp")
    replica = lax.axis_index("dp")
    group_pos = replica % GROUP
    micro_count, row_count, width = tokens_in.shape
    shard = qkv_weight.shape[1]
    runs = -(-row_count // shard)
    (message,) = on_core(
        message_body,
        [((shard, 3 * width + LANES), BF)],
        (qkv_weight[0], attn_gain, mlp_gain, segment_ids),
        [pltpu.VMEM((LANES, LANES), F32), pltpu.VMEM((8, LANES), F32)],
    )
    inner = mlp_in_weight.shape[2]
    hidden = mlp_out_weight.shape[1] * count
    if count == GROUP:
        upper = first_block(2 * mlp_out_weight.shape[1])
        moved = upper - mlp_out_weight.shape[1]
        beside = partner(mlp_out_weight[0, :moved], 1, count)
        block = jnp.where(
            replica % 2 == 0,
            jnp.concatenate([mlp_out_weight[0], beside]),
            jnp.concatenate([mlp_out_weight[0, moved:], beside, beside]),
        )
        stacked = [attn_out_weight[0]]
        stacked += [mlp_in_weight[0, :, c : c + width] for c in range(0, inner, width)]
        others = [lax.all_gather(jnp.concatenate(stacked + [block]), "dp", axis=0, tiled=True)]
    else:
        others = [
            lax.all_gather(item[0], "dp", axis=0, tiled=True)
            for item in (attn_out_weight, mlp_in_weight, mlp_out_weight)
        ]
    pieces = group_pieces(message, count)
    if count > GROUP:
        pieces = [in_order(pieces, group_pos, count)]

    positions = group_pos * row_count + jnp.arange(row_count)
    local_tables = angles(positions, local_log_base)
    global_tables = angles(positions, global_log_base)

    rows = micro_count * row_count
    pairs = rows * width // (row_count * LANES)
    in_0 = tokens_in.reshape(rows, width)
    extra_rows = -(-(2 + micro_count * runs) // 8) * 8
    first, extra, normed_0, q_0, kv_0 = on_core(
        local_project_body,
        [
            ((width, 3 * width + LANES), BF),
            ((extra_rows, width), F32),
            ((rows, width), BF),
            ((rows, width), BF),
            ((rows, 2 * width), BF),
        ],
        (group_pos[None], in_0, local_tables, *pieces),
        [
            pltpu.VMEM((width, 3 * width + LANES), BF),
            pltpu.SemaphoreType.DMA((len(pieces),)),
            pltpu.SemaphoreType.DMA,
        ],
        [pltpu.SMEM, pltpu.VMEM, pltpu.VMEM] + [pl.ANY] * len(pieces),
        [pltpu.HBM] + [pltpu.VMEM] * 4,
    )
    gain_attn, gain_mlp = extra[:1], extra[1:2]
    all_ids = extra[2 : 2 + micro_count * runs].reshape(micro_count, runs, count, shard)
    all_ids = lax.dynamic_slice_in_dim(all_ids, replica - group_pos, GROUP, 2)
    all_ids = all_ids.swapaxes(1, 2).reshape(micro_count, GROUP, runs * shard)[..., :row_count]
    segments = all_ids.reshape(micro_count, GROUP * row_count).astype(jnp.int32)

    key_pos = positions[0] - row_count + jnp.arange(3 * row_count)
    around = jnp.pad(segments, ((0, 0), (row_count, row_count)), constant_values=-1)
    key_seg = lax.dynamic_slice_in_dim(around, group_pos * row_count, 3 * row_count, 1)
    visible = (key_seg[:, :, None] == segment_ids[:, None, :]) & (
        jnp.abs(positions[None, :] - key_pos[:, None]) <= HALF_WIN
    )[None]
    bias = jnp.tile(jnp.where(visible, 0.0, masked_score), (1, 1, 2))

    own_seg = lax.dynamic_index_in_dim(segments, group_pos // 8, 0, keepdims=False)
    halves = own_seg.reshape(GROUP, 2, row_count // 2)
    mine = lax.dynamic_index_in_dim(halves, group_pos % 2, 1, keepdims=False).reshape(-1)
    theirs = lax.dynamic_index_in_dim(halves, 1 - group_pos % 2, 1, keepdims=False).reshape(-1)
    shared_seg = jnp.concatenate([mine, theirs])[:, None]
    own_seg = own_seg[:, None]

    up_pairs, down_pairs = neighbours(count, 1), neighbours(count, -1)
    around_0 = (
        lax.ppermute(kv_0, "dp", up_pairs),
        kv_0,
        lax.ppermute(kv_0, "dp", down_pairs),
    )
    att_0, total_0 = on_core(
        local_forward_body,
        [((rows, width), BF), ((pairs, 1, LANES), F32)],
        (q_0, *around_0, bias),
    )
    out_0, n2_0, mixed_0, middle_0, gate_up_0 = on_core(
        local_middle_body,
        [
            ((rows, width), BF),
            ((rows, width), BF),
            ((rows, hidden), BF),
            ((rows, width), F32),
            ((rows, inner), F32),
        ],
        (*others, in_0, att_0, gain_mlp),
        weight_scratch(width, inner, hidden),
        [pltpu.HBM] * len(others) + [pltpu.VMEM] * 3,
    )

    in_1 = to_other_section(out_0, 1)
    fold = row_count * 3 // 4
    half = row_count // 2
    normed_1, sent = on_core(
        global_project_body,
        [((rows, width), BF), ((GROUP, 3 * fold, LANES), BF)],
        (first, in_1, gain_attn, global_tables),
        qkv_scratch(width),
        [pltpu.HBM] + [pltpu.VMEM] * 3,
    )
    got = exchange(sent, count)
    beside = jnp.concatenate(
        [got[:, row_count : row_count + half], got[:, 3 * fold - half :]], 1
    )
    beside = partner(beside, 1, count)
    keys = GROUP * row_count
    tiles = keys * 3 // 2 // TILE
    head_scratch = [
        pltpu.VMEM((keys * 3 // 2, LANES), BF),
        pltpu.VMEM((2, keys, LANES), BF),
        pltpu.VMEM((2, keys, LANES), BF),
        pltpu.VMEM((2, LANES, keys), BF),
    ]
    folded, total_1 = on_core(
        global_forward_body,
        [((GROUP, fold, LANES), BF), ((tiles, 1, TILE), F32)],
        (got, beside, own_seg, shared_seg),
        head_scratch + [pltpu.VMEM((keys * 3 // 2, LANES), F32)],
    )
    folded = exchange(folded, count)

    up_1 = out_grad.reshape(rows, width)
    out_1, att_1, n2_1, mixed_1, right_1, gain_mlp_1, d_mid_1, sent = on_core(
        global_middle_body,
        [
            ((rows, width), BF),
            ((rows, width), BF),
            ((rows, width), BF),
            ((rows, hidden), BF),
            ((rows, inner + width), BF),
            ((1, width), F32),
            ((rows, width), F32),
            ((GROUP, fold, LANES), BF),
        ],
        (*others, folded, in_1, up_1, gain_mlp),
        weight_scratch(width, inner, hidden),
        [pltpu.HBM] * len(others) + [pltpu.VMEM] * 4,
    )
    d_folded = exchange(sent, count)
    sent, to_beside = on_core(
        global_backward_body,
        [((GROUP, 3 * fold, LANES), BF), ((GROUP, 2 * half, LANES), BF)],
        (got, beside, own_seg, shared_seg, total_1, d_folded),
        head_scratch
        + [
            pltpu.VMEM((keys * 3 // 2, LANES), BF),
            pltpu.VMEM((keys * 3 // 2, LANES), F32),
            pltpu.VMEM((2, keys, LANES), F32),
            pltpu.VMEM((2, keys, LANES), F32),
        ],
    )
    back = partner(to_beside, 1, count)
    gap = 3 * fold - half - row_count - half
    back = jnp.concatenate(
        [
            jnp.zeros((GROUP, row_count, LANES), BF),
            back[:, :half],
            jnp.zeros((GROUP, gap, LANES), BF),
            back[:, half:],
        ],
        1,
    )
    sent = (sent.astype(F32) + back.astype(F32)).astype(BF)
    got = exchange(sent, count)

    n1, att, n2, mixed = (
        jnp.where(lower, a, b).T.reshape(count, -1, micro_count * row_count)
        for a, b in (
            (normed_0, normed_1),
            (att_0, att_1),
            (n2_0, n2_1),
            (mixed_0, mixed_1),
        )
    )
    left = jnp.concatenate([n1, att, n2, mixed], 1)
    left, got = lax.optimization_barrier((left, got))
    left = plane_rows(left, group_pos, count)
    n1, att, n2, mixed = (
        [part[:, :, start:end] for part in left]
        for start, end in (
            (0, shard),
            (shard, 2 * shard),
            (2 * shard, 3 * shard),
            (3 * shard, left[0].shape[2]),
        )
    )
    d_proj_1, grad_1, gain_attn_1 = on_core(
        global_finish_body,
        [((rows, 3 * width), BF), ((rows, width), BF), ((1, width), F32)],
        (first, got, d_mid_1, in_1, gain_attn, global_tables),
        qkv_scratch(width),
        [pltpu.HBM] + [pltpu.VMEM] * 5,
    )

    up_0 = to_other_section(grad_1, -1)
    d_mlp = jnp.where(lower, up_0, up_1)
    across, beside = partner(d_mlp, 2, count), partner(d_mlp, 1, count)
    d_mlp = [d_mlp, beside, across, partner(across, 1, count)]
    out_blocks = plane_product(d_mlp, [(mixed, 0, width)])
    right, gain_mlp_0, d_mid_0, d_att_0 = on_core(
        local_back_middle_body,
        [
            ((rows, inner + width), BF),
            ((1, width), F32),
            ((rows, width), F32),
            ((rows, width), BF),
        ],
        (*others, lower_flag, up_0, middle_0, gate_up_0, gain_mlp, right_1),
        weight_scratch(width, inner, hidden),
        [pltpu.HBM] * len(others) + [pltpu.SMEM] + [pltpu.VMEM] * 5,
    )
    beside, across = partner(right, 1, count), partner(right, 2, count)
    dq_0, d_own, d_before, d_after = on_core(
        local_backward_body,
        [
            ((rows, width), BF),
            ((rows, 2 * width), F32),
            ((rows, 2 * width), BF),
            ((rows, 2 * width), BF),
        ],
        (q_0, *around_0, bias, total_0, d_att_0, local_tables),
    )
    from_after = lax.ppermute(d_before, "dp", down_pairs)
    from_before = lax.ppermute(d_after, "dp", up_pairs)
    from_after, out_blocks = lax.optimization_barrier((from_after, out_blocks))
    mlp_out_share = sum_planes(out_blocks, count)
    (d_proj,) = on_core(
        local_join_body,
        [((rows, 3 * width), BF)],
        (lower_flag, dq_0, d_own, from_after, from_before, local_tables, d_proj_1),
        (),
        [pltpu.SMEM] + [pltpu.VMEM] * 6,
    )
    right = [right, beside, across, partner(across, 1, count)]
    in_blocks = plane_product(right, [(n2, 0, inner), (att, inner, inner + width)])
    in_share = sum_planes(in_blocks, count)
    grad_0, gain_attn_0 = on_core(
        input_backward_body,
        [((rows, width), BF), ((1, width), F32)],
        (first, d_mid_0, d_proj, in_0, gain_attn),
        qkv_scratch(width),
        [pltpu.HBM] + [pltpu.VMEM] * 4,
    )
    gains = jnp.where(
        lower,
        jnp.concatenate([gain_attn_0, gain_mlp_0]),
        jnp.concatenate([gain_attn_1, gain_mlp_1]),
    )
    gains = gains + partner(gains, 1, count)
    gains = gains + partner(gains, 2, count)
    across = partner(d_proj, 2, count)
    across, in_blocks, gains = lax.optimization_barrier((across, in_blocks, gains))
    d_proj = [d_proj, partner(d_proj, 1, count), across, partner(across, 1, count)]
    qkv_blocks = plane_product(d_proj, [(n1, 0, 3 * width)])
    qkv_share = sum_planes(qkv_blocks, count)
    gains, _ = lax.optimization_barrier((gains, qkv_blocks))
    apart = 4
    while apart < count:
        gains = gains + partner(gains, apart, count)
        apart *= 2
    gains = lax.dynamic_slice_in_dim(gains, replica * shard, shard, 1)

    return (
        jnp.where(lower, out_0, out_1).reshape(1, micro_count, row_count, width),
        jnp.where(lower, grad_0, grad_1).reshape(1, micro_count, row_count, width),
        qkv_share[None],
        in_share[None, :, inner:],
        in_share[None, :, :inner],
        mlp_out_share[None],
        gains[:1],
        gains[1:],
    )


def solution(mesh):
    in_specs = (
        P(None, "dp", None),
        P(None, "dp"),
        P(None, "dp", None),
        P("section", "dp", None),
        P("section", "dp", None),
        P("section", "dp", None),
        P("section", "dp", None),
        P("section", "dp"),
        P("section", "dp"),
    )
    out_specs = (
        P("section", None, "dp", None),
        P("section", None, "dp", None),
        P("section", "dp", None),
        P("section", "dp", None),
        P("section", "dp", None),
        P("section", "dp", None),
        P("section", "dp"),
        P("section", "dp"),
    )
    return jax.shard_map(
        on_device, mesh=mesh, in_specs=in_specs, out_specs=out_specs, check_vma=False
    )
```

```python
import functools
import math

import jax
import jax.numpy as jnp
from jax import lax
from jax.experimental import pallas as pl
from jax.experimental.pallas import tpu as pltpu
from jax.sharding import PartitionSpec as P

HEAD_DIM = 64
GROUP = 16
HALF_WIN = 64
CHUNKS = 4
LANES = 128
TILE = 256

local_log_base = math.log(10000.0)
global_log_base = math.log(160000.0)
masked_score = -1e30
SCALE = 1.0 / math.sqrt(HEAD_DIM)
BF = jnp.bfloat16
F32 = jnp.float32


def dot(left, right):
    return jnp.dot(left, right, preferred_element_type=F32)


def dot_bt(left, right):
    return lax.dot_general(left, right, (((1,), (1,)), ((), ())), preferred_element_type=F32)


def dot_at(left, right):
    return lax.dot_general(left, right, (((0,), (0,)), ((), ())), preferred_element_type=F32)


def moments(values):
    center = values - jnp.mean(values, -1, keepdims=True)
    scale = lax.rsqrt(jnp.mean(center * center, -1, keepdims=True) + 1e-05)
    return center * scale, scale


def norm_back(grad_out, gain_row, xhat, scale):
    scaled = grad_out * gain_row
    mean_grad = jnp.mean(scaled, -1, keepdims=True)
    mean_dot = jnp.mean(scaled * xhat, -1, keepdims=True)
    return (scaled - mean_grad - xhat * mean_dot) * scale


def angles(positions, log_base):
    half_dim = HEAD_DIM // 2
    fraction = (2 * jnp.arange(half_dim)).astype(F32) / HEAD_DIM
    inverse = jnp.exp(-fraction * log_base)
    table = positions.astype(F32)[:, None] * inverse[None, :]
    cosine, sine = jnp.cos(table), jnp.sin(table)
    none = jnp.zeros_like(sine)
    cosine = jnp.concatenate([cosine, cosine], 1)
    to_first = jnp.concatenate([-sine, none], 1)
    to_second = jnp.concatenate([none, sine], 1)
    return jnp.tile(jnp.stack([cosine, to_first, to_second]), (1, 2, 2))


def on_core(body, outs, args, scratch=(), spaces=None, out_spaces=None):
    return pl.pallas_call(
        body,
        out_shape=[jax.ShapeDtypeStruct(shape, dtype) for shape, dtype in outs],
        in_specs=[
            pl.BlockSpec(memory_space=space) for space in spaces or [pltpu.VMEM] * len(args)
        ],
        out_specs=[
            pl.BlockSpec(memory_space=space) for space in out_spaces or [pltpu.VMEM] * len(outs)
        ],
        scratch_shapes=scratch,
        cost_estimate=pl.CostEstimate(
            flops=2**10, bytes_accessed=2**10, transcendentals=0
        ),
        compiler_params=pltpu.CompilerParams(vmem_limit_bytes=48 * 2**20),
    )(*args)


def low_lanes():
    return lax.broadcasted_iota(jnp.int32, (1, LANES), 1) < HEAD_DIM


def swap(chunk):
    return pltpu.roll(chunk, HEAD_DIM, 1)


def chunks_of(rows):
    return [rows[:, c : c + LANES] for c in range(0, rows.shape[1], LANES)]


def rotate(chunk, tables):
    cosine, to_first, to_second = tables
    quarter = HEAD_DIM // 2
    return (
        chunk * cosine
        + pltpu.roll(chunk, LANES - quarter, 1) * to_first
        + pltpu.roll(chunk, quarter, 1) * to_second
    )


def unrotate(chunk, tables):
    cosine, to_first, to_second = tables
    quarter = HEAD_DIM // 2
    return (
        chunk * cosine
        - pltpu.roll(chunk, LANES - quarter, 1) * to_first
        - pltpu.roll(chunk, quarter, 1) * to_second
    )


def low_and_high(chunks):
    swapped = [swap(chunk) for chunk in chunks]
    low = [(swapped if h % 2 else chunks)[h // 2] for h in range(2 * len(chunks))]
    high = [(chunks if h % 2 else swapped)[h // 2] for h in range(2 * len(chunks))]
    return low, high


def targets():
    for d in range(GROUP):
        micro, chip, half = d // 8, d % 8 // 2, d % 2
        yield d, micro, 3 * chip + 2 * half, 3 * chip + 1, half


def pack_folded(chunks, ref, base):
    low, high = low_and_high(chunks)
    first = low_lanes()
    rows = chunks[0].shape[0] // 2
    half, fold = rows // 2, rows * 3 // 4
    for d, micro, own, shared, side in targets():
        start = micro * rows
        part = start + side * half
        upper = jnp.concatenate(
            [high[own][start + fold : start + rows], high[shared][part : part + half]], 0
        )
        ref[d, base : base + fold] = jnp.where(
            first, low[own][start : start + fold], upper
        ).astype(BF)


def pack_pairs(lefts, rights, ref):
    low, high = low_and_high(lefts)[0], low_and_high(rights)[1]
    first = low_lanes()
    rows = lefts[0].shape[0] // 2
    half = rows // 2
    for d, micro, own, shared, side in targets():
        start = micro * rows
        part = start + side * half
        ref[d, 0:rows] = jnp.where(
            first, low[own][start : start + rows], high[own][start : start + rows]
        ).astype(BF)
        ref[d, rows : rows + half] = jnp.where(
            first, low[shared][part : part + half], high[shared][part : part + half]
        ).astype(BF)


def unpack_folded(ref, base, rows):
    first = low_lanes()
    fold = rows * 3 // 4
    low, high = {}, {}
    shared_parts = {}
    for d, micro, own, shared, side in targets():
        block = ref[d, base : base + fold].astype(F32)
        mine = jnp.concatenate([block, swap(block[: rows - fold])], 0)
        if own % 2:
            high[micro, own] = swap(mine)
        else:
            low[micro, own] = mine
        shared_parts[micro, shared, side] = block[rows - fold :]
        if side:
            both = jnp.concatenate([shared_parts[micro, shared, 0], block[rows - fold :]], 0)
            if shared % 2:
                high[micro, shared] = both
            else:
                low[micro, shared] = swap(both)
    heads = GROUP // 4 * 3
    return [
        jnp.concatenate(
            [jnp.where(first, low[m, h], high[m, h + 1]) for m in range(2)], 0
        )
        for h in range(0, heads, 2)
    ]


def unpack_pairs(ref, rows):
    first = low_lanes()
    half = rows // 2
    pairs = {}
    parts = {}
    for d, micro, own, shared, side in targets():
        pairs[micro, own] = ref[d, 0:rows].astype(F32)
        parts[side] = ref[d, rows : rows + half].astype(F32)
        if side:
            pairs[micro, shared] = jnp.concatenate([parts[0], parts[1]], 0)
    heads = GROUP // 4 * 3
    lefts, rights = [], []
    for h in range(0, heads, 2):
        even, odd = [pairs[m, h] for m in range(2)], [pairs[m, h + 1] for m in range(2)]
        lefts.append(
            jnp.concatenate([jnp.where(first, a, swap(b)) for a, b in zip(even, odd)], 0)
        )
        rights.append(
            jnp.concatenate([jnp.where(first, swap(a), b) for a, b in zip(even, odd)], 0)
        )
    return lefts, rights


class Weights:
    def __init__(self, sources, mlp_out):
        self.sources = sources
        self.mlp_out = sources[-1]
        if len(sources) == 1:
            self.mlp_out = mlp_out
            unpack_rows(sources[0], mlp_out)

    def get(self, which):
        if which == 2:
            return self.mlp_out[...]
        if len(self.sources) > 1:
            return self.sources[which][...]
        (wide,) = self.sources
        width = wide.shape[0]
        inner = 2 * self.mlp_out.shape[0]
        return wide[:, width : width + inner] if which else wide[:, :width]


def first_block(pair):
    return -(-pair // 32) * 16


def packed_pieces(shard, rows, width):
    yield 0, shard, 0, width, 0, 0
    rest = rows - shard
    side = width // 3
    yield 0, rest, width, 2 * side, shard, 0
    yield rest, 16, width, side, shard, 2 * side
    yield rest, 16, width + side, side, shard + 16, 2 * side


def unpack_rows(wide, mlp_out):
    hidden, width = mlp_out.shape
    shard = wide.shape[0] // GROUP
    start = wide.shape[1] - width - 2 * (width // 3)
    pair = 2 * hidden // GROUP
    upper = first_block(pair)
    for d in range(GROUP):
        low = d // 2 * pair + d % 2 * upper
        have = pair - upper if d % 2 else upper
        for row, rows, column, columns, to_row, to_column in packed_pieces(shard, upper, width):
            rows = min(rows, have - to_row)
            if rows > 0:
                mlp_out[low + to_row : low + to_row + rows, to_column : to_column + columns] = wide[
                    d * shard + row : d * shard + row + rows, start + column : start + column + columns
                ]


def stack_body(odd_ref, attn_ref, mlp_in_ref, own_ref, beside_ref, out_ref):
    shard, width = attn_ref.shape
    inner = mlp_in_ref.shape[1]
    out_ref[:, :width] = attn_ref[...]
    out_ref[:, width : width + inner] = mlp_in_ref[...]
    own, beside = own_ref[...].astype(F32), beside_ref[...].astype(F32)
    moved = beside.shape[0]
    even = jnp.concatenate([own, beside], 0)
    odd = jnp.concatenate([own[moved:], beside, beside], 0)
    block = jnp.where(odd_ref[0] == 1, odd, even).astype(BF)
    start = width + inner
    for row, rows, column, columns, from_row, from_column in packed_pieces(
        shard, block.shape[0], width
    ):
        out_ref[row : row + rows, start + column : start + column + columns] = block[
            from_row : from_row + rows, from_column : from_column + columns
        ]


def mlp_forward(layer_in, attended, gain, weights):
    middle = layer_in + dot(attended, weights.get(0))
    xhat, _ = moments(middle)
    normed = (xhat * gain).astype(BF)
    gate_up = dot(normed, weights.get(1))
    half = gate_up.shape[1] // 2
    gate, up = gate_up[:, :half], gate_up[:, half:]
    cdf = 0.5 * (1.0 + lax.erf(gate * math.sqrt(0.5)))
    mixed = (gate * cdf * up).astype(BF)
    result = (middle + dot(mixed, weights.get(2))).astype(BF)
    return middle, normed, gate, up, mixed, result


def mlp_backward(upstream, middle, gate, up, gain, weights):
    d_mixed = dot_bt(upstream, weights.get(2))
    cdf = 0.5 * (1.0 + lax.erf(gate * math.sqrt(0.5)))
    density = jnp.exp(-0.5 * gate * gate) * (1.0 / math.sqrt(2.0 * math.pi))
    d_gate = d_mixed * up * (cdf + gate * density)
    d_up = d_mixed * gate * cdf
    d_gate_up = jnp.concatenate([d_gate.astype(BF), d_up.astype(BF)], 1)
    d_normed = dot_bt(d_gate_up, weights.get(1))
    xhat, scale = moments(middle)
    gain_grad = jnp.sum(d_normed * xhat, 0, keepdims=True)
    d_middle = upstream.astype(F32) + norm_back(d_normed, gain, xhat, scale)
    d_attn = d_middle.astype(BF)
    d_attended = dot_bt(d_attn, weights.get(0))
    return d_gate_up, gain_grad, d_middle, d_attn, d_attended


def project(xhat, gain, first_ref, table_ref, normed_ref):
    width = xhat.shape[1]
    normed = (xhat * gain).astype(BF)
    normed_ref[...] = normed
    tables = [table_ref[i] for i in range(3)]
    results = [dot(normed, first_ref[:, c * width : (c + 1) * width]) for c in range(3)]
    queries, keys, values = chunks_of(results[0]), chunks_of(results[1]), results[2]
    return [rotate(c, tables) for c in queries], [rotate(c, tables) for c in keys], values


def input_backward(d_middle, d_projected, x, gain_ref, first_ref, gain_out_ref):
    d_normed = dot_bt(d_projected, first_ref[:, : d_projected.shape[1]])
    xhat, scale = moments(x)
    gain_out_ref[...] = jnp.sum(d_normed * xhat, 0, keepdims=True)
    return (d_middle + norm_back(d_normed, gain_ref[...], xhat, scale)).astype(BF)


def joined(refs):
    return jnp.concatenate([ref[...] for ref in refs], 0)


def store_chunks(refs, rows):
    size = rows.shape[0] // len(refs)
    for i, ref in enumerate(refs):
        ref[...] = rows[i * size : (i + 1) * size]


def message_body(w_ref, attn_ref, mlp_ref, ids_ref, out_ref, rows_scr, ids_scr):
    shard, columns = w_ref.shape
    micro_count, row_count = ids_ref.shape
    out_ref[:, :columns] = w_ref[...]
    rows_scr[...] = jnp.zeros_like(rows_scr)
    ids_scr[...] = jnp.zeros_like(ids_scr)
    rows_scr[0:1, :shard] = attn_ref[...].astype(F32)
    rows_scr[1:2, :shard] = mlp_ref[...].astype(F32)
    ids_scr[:micro_count, :row_count] = ids_ref[...].astype(F32)
    runs = -(-row_count // shard)
    for run in range(runs):
        turned = ids_scr[...]
        if run:
            turned = pltpu.roll(turned, LANES - run * shard, 1)
        for micro in range(micro_count):
            row = 2 + micro * runs + run
            rows_scr[row : row + 1] = turned[micro : micro + 1]
    out_ref[:, columns:] = rows_scr[...].T[:shard].astype(BF)


def local_project_body(place_ref, x_ref, table_ref, *refs):
    pieces, (first_ref, extra_ref, normed_ref, q_ref, kv_ref, sem) = refs[:-6], refs[-6:]
    rows = pieces[0].shape[0]
    copies = []
    for apart, piece in enumerate(pieces):
        start = pl.multiple_of((place_ref[0] ^ apart) * rows, rows) if len(pieces) > 1 else 0
        copies.append(
            pltpu.make_async_copy(piece, first_ref.at[pl.ds(start, rows)], sem.at[apart])
        )
        copies[-1].start()
    xhat, _ = moments(x_ref[...].astype(F32))
    for copy in copies:
        copy.wait()
    extra = first_ref[:, first_ref.shape[1] - LANES :].astype(F32).T
    extra_ref[...] = extra[: extra_ref.shape[0]]
    queries, keys, values = project(xhat, extra[:1], first_ref, table_ref, normed_ref)
    width = values.shape[1]
    for j, (q, k) in enumerate(zip(queries, keys)):
        q_ref[:, LANES * j : LANES * (j + 1)] = q.astype(BF)
        kv_ref[:, LANES * j : LANES * (j + 1)] = k.astype(BF)
    kv_ref[:, width:] = values.astype(BF)


def two_heads(chunk):
    first = low_lanes()
    wide = chunk.astype(F32)
    return jnp.concatenate([jnp.where(first, wide, 0.0), jnp.where(first, 0.0, wide)], 0)


def pick_heads(rows):
    half = rows.shape[0] // 2
    return jnp.where(low_lanes(), rows[:half], rows[half:])


def local_parts(q_ref, before_ref, own_ref, after_ref):
    rows = q_ref.shape[0] // 2
    width = q_ref.shape[1]
    for micro in range(2):
        for j in range(width // LANES):
            here = slice(micro * rows, (micro + 1) * rows)
            lanes = slice(LANES * j, LANES * (j + 1))
            more = slice(width + LANES * j, width + LANES * (j + 1))
            keys, values = (
                jnp.concatenate([ref[here, part] for ref in (before_ref, own_ref, after_ref)], 0)
                for part in (lanes, more)
            )
            queries = (two_heads(q_ref[here, lanes]) * SCALE).astype(BF)
            yield micro * (width // LANES) + j, micro, here, lanes, more, queries, keys, values


def local_forward_body(q_ref, before_ref, own_ref, after_ref, bias_ref, att_ref, total_ref):
    parts = local_parts(q_ref, before_ref, own_ref, after_ref)
    for index, micro, here, lanes, _, queries, keys, values in parts:
        scores = dot_bt(keys, queries) + bias_ref[micro]
        peak = jnp.max(scores, 0, keepdims=True)
        weights = jnp.exp(scores - peak)
        total = jnp.sum(weights, 0, keepdims=True)
        total_ref[index] = peak + jnp.log(total)
        probs = (weights * (1.0 / total)).astype(BF)
        att_ref[here, lanes] = pick_heads(dot_at(probs, values)).astype(BF)


def local_backward_body(
    q_ref, before_ref, own_ref, after_ref, bias_ref, total_ref, d_ref, table_ref,
    dq_ref, d_own_ref, d_before_ref, d_after_ref,
):
    tables = [table_ref[i] for i in range(3)]
    parts = local_parts(q_ref, before_ref, own_ref, after_ref)
    rows = q_ref.shape[0] // 2
    for index, micro, here, lanes, more, queries, keys, values in parts:
        d_out = two_heads(d_ref[here, lanes]).astype(BF)
        probs = jnp.exp(dot_bt(keys, queries) + bias_ref[micro] - total_ref[index])
        d_probs = dot_bt(values, d_out)
        product = probs * d_probs
        delta = jnp.sum(product, 0, keepdims=True)
        d_scores = (product - probs * delta).astype(BF)
        d_queries = pick_heads(dot_at(d_scores, keys)) * SCALE
        local_tables = [table[here] for table in tables]
        dq_ref[here, lanes] = unrotate(d_queries, local_tables).astype(BF)
        for part, grads in ((lanes, dot(d_scores, queries)), (more, dot(probs.astype(BF), d_out))):
            d_before_ref[here, part] = grads[:rows].astype(BF)
            d_own_ref[here, part] = grads[rows : 2 * rows]
            d_after_ref[here, part] = grads[2 * rows :].astype(BF)


def local_join_body(lower_ref, dq_ref, own_ref, low_ref, high_ref, table_ref, other_ref, *out_refs):
    @pl.when(lower_ref[0] == 1)
    def _():
        tables = [table_ref[i] for i in range(3)]
        width = dq_ref.shape[1]
        total = own_ref[...] + low_ref[...].astype(F32) + high_ref[...].astype(F32)
        keys = [unrotate(chunk, tables).astype(BF) for chunk in chunks_of(total[:, :width])]
        store_chunks(
            out_refs, jnp.concatenate([dq_ref[...]] + keys + [total[:, width:].astype(BF)], 1)
        )

    @pl.when(lower_ref[0] == 0)
    def _():
        store_chunks(out_refs, other_ref[...])


def local_middle_body(*refs):
    sources, refs = refs[:-10], refs[-10:]
    x_ref, att_ref, gain_ref, normed_ref, mixed_ref, middle_ref, gate_up_ref = refs[:7]
    weights = Weights(sources, refs[9])
    middle, normed, gate, up, mixed, result = mlp_forward(
        x_ref[...].astype(F32), att_ref[...], gain_ref[...], weights
    )
    store_chunks(refs[7:9], result)
    normed_ref[...] = normed
    mixed_ref[...] = mixed
    middle_ref[...] = middle
    half = gate.shape[1]
    gate_up_ref[:, :half] = gate
    gate_up_ref[:, half:] = up


def local_back_middle_body(*refs):
    count = 11 + CHUNKS
    sources, refs = refs[:-count], refs[-count:]
    lower_ref, low_ref, high_ref, middle_ref, gate_up_ref, gain_ref, other_ref = refs[:7]
    gain_out_ref, d_middle_ref, d_att_ref = refs[7:10]
    chunk_refs = refs[10 : 10 + CHUNKS]
    weights = Weights(sources, refs[10 + CHUNKS])
    half = gate_up_ref.shape[1] // 2
    d_gate_up, gain_grad, d_middle, d_attn, d_attended = mlp_backward(
        joined([low_ref, high_ref]), middle_ref[...], gate_up_ref[:, :half], gate_up_ref[:, half:],
        gain_ref[...], weights,
    )
    gain_out_ref[...] = gain_grad
    d_middle_ref[...] = d_middle
    d_att_ref[...] = d_attended.astype(BF)

    @pl.when(lower_ref[0] == 1)
    def _():
        store_chunks(chunk_refs, jnp.concatenate([d_gate_up, d_attn], 1))

    @pl.when(lower_ref[0] == 0)
    def _():
        store_chunks(chunk_refs, other_ref[...])


def input_backward_body(first_ref, d_middle_ref, x_ref, gain_ref, *refs):
    d_proj_refs, (grad_ref, gain_out_ref) = refs[:-2], refs[-2:]
    x = x_ref[...].astype(F32)
    grad_ref[...] = input_backward(
        d_middle_ref[...], joined(d_proj_refs), x, gain_ref, first_ref, gain_out_ref
    )


def global_project_body(first_ref, low_ref, high_ref, gain_ref, table_ref, normed_ref, sent_ref):
    xhat, _ = moments(joined([low_ref, high_ref]).astype(F32))
    queries, keys, values = project(xhat, gain_ref[...], first_ref, table_ref, normed_ref)
    pack_pairs(queries, keys, sent_ref)
    pack_folded(chunks_of(values), sent_ref, sent_ref.shape[1] * 2 // 3)


def flat(blocks):
    return blocks.reshape(-1, LANES)


def own_unfolded(ref, base, rows):
    fold = rows * 3 // 4
    block = ref[:, base : base + fold].astype(F32)
    rest = swap(flat(block[:, : rows - fold])).reshape(GROUP, rows - fold, LANES)
    return flat(jnp.concatenate([block, rest], 1))


def shared_unfolded(ref, start, rows):
    return swap(flat(ref[:, start : start + rows // 2].astype(F32)))


def fill_heads(got_ref, other_ref, own_seg_ref, shared_seg_ref, q_scr, k_scr, v_scr):
    rows = got_ref.shape[1] * 4 // 9
    half = rows // 2
    first = low_lanes()
    lane = lax.broadcasted_iota(jnp.int32, (1, LANES), 1) - HEAD_DIM
    own = flat(got_ref[:, 0:rows].astype(F32))
    shared = flat(got_ref[:, rows : rows + half].astype(F32))
    other = flat(other_ref[:, 0:half].astype(F32))
    count = own.shape[0]
    own_hit = lane == own_seg_ref[...]
    shared_hit = lane == shared_seg_ref[...]
    both = jnp.concatenate([shared, other], 0)
    for start, pairs, hit in (
        (0, own, own_hit),
        (count, shared, shared_hit[: count // 2]),
    ):
        marked = jnp.where(hit, 1.0, 0.0)
        q_scr[start : start + pairs.shape[0]] = jnp.where(first, pairs * SCALE, marked).astype(BF)
    for unit, pairs, hit in ((0, own, own_hit), (1, both, shared_hit)):
        marked = jnp.where(hit, 0.0, masked_score)
        k_scr[unit] = jnp.where(first, swap(pairs), marked).astype(BF)
    base = rows + half
    v_scr[0] = jnp.where(first, own_unfolded(got_ref, base, rows), 0.0).astype(BF)
    start = base + rows - rows * 3 // 4
    shared_v = jnp.concatenate(
        [shared_unfolded(got_ref, start, rows), shared_unfolded(other_ref, half, rows)], 0
    )
    v_scr[1] = jnp.where(first, shared_v, 0.0).astype(BF)


def fold_out(own, shared, rows, ref, base):
    fold = rows * 3 // 4
    blocks = own.reshape(GROUP, rows, LANES)
    swapped = swap(own).reshape(GROUP, rows, LANES)
    upper = jnp.concatenate(
        [swapped[:, fold:], swap(shared).reshape(GROUP, rows // 2, LANES)], 1
    )
    ref[:, base : base + fold] = jnp.where(low_lanes(), blocks[:, :fold], upper).astype(BF)


def global_forward_body(
    got_ref, other_ref, own_seg_ref, shared_seg_ref, out_ref, total_ref,
    q_scr, k_scr, v_scr, vt_scr, o_scr,
):
    fill_heads(got_ref, other_ref, own_seg_ref, shared_seg_ref, q_scr, k_scr, v_scr)
    for unit in range(2):
        vt_scr[unit] = v_scr[unit].astype(F32).T.astype(BF)
    count = k_scr.shape[1]

    def step(tile, carry):
        unit = tile // (count // TILE)
        rows = pl.ds(pl.multiple_of(tile * TILE, TILE), TILE)
        scores = dot_bt(k_scr[unit], q_scr[rows])
        peak = jnp.max(scores, 0, keepdims=True)
        weights = jnp.exp(scores - peak)
        total = jnp.sum(weights, 0, keepdims=True)
        total_ref[tile] = peak + jnp.log(total)
        out = dot(vt_scr[unit], weights.astype(BF)) * (1.0 / total)
        o_scr[rows] = out.T
        return carry

    lax.fori_loop(0, q_scr.shape[0] // TILE, step, 0)
    rows = got_ref.shape[1] * 4 // 9
    fold_out(o_scr[:count], o_scr[count:], rows, out_ref, 0)


def global_backward_body(
    got_ref, other_ref, own_seg_ref, shared_seg_ref, total_ref, d_ref, sent_ref, to_other_ref,
    q_scr, k_scr, v_scr, kt_scr, d_scr, dq_scr, dk_scr, dv_scr,
):
    fill_heads(got_ref, other_ref, own_seg_ref, shared_seg_ref, q_scr, k_scr, v_scr)
    first = low_lanes()
    rows = got_ref.shape[1] * 4 // 9
    half = rows // 2
    for unit in range(2):
        keys = jnp.where(first, k_scr[unit].astype(F32), 0.0)
        kt_scr[unit] = keys.T.astype(BF)
    count = k_scr.shape[1]
    d_scr[:count] = jnp.where(first, own_unfolded(d_ref, 0, rows), 0.0).astype(BF)
    d_scr[count:] = jnp.where(
        first, shared_unfolded(d_ref, rows - rows * 3 // 4, rows), 0.0
    ).astype(BF)
    dk_scr[...] = jnp.zeros_like(dk_scr)
    dv_scr[...] = jnp.zeros_like(dv_scr)

    def step(tile, carry):
        unit = tile // (count // TILE)
        here = pl.ds(pl.multiple_of(tile * TILE, TILE), TILE)
        queries, d_out = q_scr[here], d_scr[here]
        probs = jnp.exp(dot_bt(k_scr[unit], queries) - total_ref[tile])
        d_probs = dot_bt(v_scr[unit], d_out)
        product = probs * d_probs
        delta = jnp.sum(product, 0, keepdims=True)
        d_scores = (product - probs * delta).astype(BF)
        dv_scr[unit] += dot(probs.astype(BF), d_out)
        dk_scr[unit] += dot(d_scores, queries)
        dq_scr[here] = dot(kt_scr[unit], d_scores).T * SCALE
        return carry

    lax.fori_loop(0, q_scr.shape[0] // TILE, step, 0)
    mine = count // 2
    own = jnp.where(first, dq_scr[:count], swap(dk_scr[0]))
    sent_ref[:, 0:rows] = own.reshape(GROUP, rows, LANES).astype(BF)
    shared_k, shared_v = dk_scr[1], dv_scr[1]
    shared = jnp.where(first, dq_scr[count:], swap(shared_k[:mine]))
    sent_ref[:, rows : rows + half] = shared.reshape(GROUP, half, LANES).astype(BF)
    fold_out(dv_scr[0], shared_v[:mine], rows, sent_ref, rows + half)
    for place, grads in enumerate((shared_k, shared_v)):
        other = jnp.where(first, 0.0, swap(grads[mine:])).reshape(GROUP, half, LANES)
        to_other_ref[:, place * half : (place + 1) * half] = other.astype(BF)


def global_middle_body(*refs):
    sources, refs = refs[:-14], refs[-14:]
    got_ref, low_ref, high_ref, up_ref, gain_ref, out_ref, att_ref, normed_ref, mixed_ref = refs[:9]
    right_ref, gain_out_ref, d_middle_ref, sent_ref = refs[9:13]
    weights = Weights(sources, refs[13])
    rows = low_ref.shape[0]
    attended = jnp.concatenate([c.astype(BF) for c in unpack_folded(got_ref, 0, rows)], 1)
    att_ref[...] = attended
    gain = gain_ref[...]
    middle, normed, gate, up, mixed, result = mlp_forward(
        joined([low_ref, high_ref]).astype(F32), attended, gain, weights
    )
    out_ref[...] = result
    normed_ref[...] = normed
    mixed_ref[...] = mixed
    d_gate_up, gain_grad, d_middle, d_attn, d_attended = mlp_backward(
        up_ref[...], middle, gate, up, gain, weights
    )
    right_ref[:, : d_gate_up.shape[1]] = d_gate_up
    right_ref[:, d_gate_up.shape[1] :] = d_attn
    gain_out_ref[...] = gain_grad
    d_middle_ref[...] = d_middle
    pack_folded(chunks_of(d_attended), sent_ref, 0)


def global_finish_body(
    first_ref, got_ref, d_middle_ref, low_ref, high_ref, gain_ref, table_ref,
    d_proj_ref, gain_out_ref, *grad_refs,
):
    tables = [table_ref[i] for i in range(3)]
    x = joined([low_ref, high_ref]).astype(F32)
    rows = low_ref.shape[0]
    d_queries, d_keys = unpack_pairs(got_ref, rows)
    d_values = unpack_folded(got_ref, rows * 3 // 2, rows)
    parts = [unrotate(c, tables).astype(BF) for c in d_queries + d_keys]
    d_projected = jnp.concatenate(parts + [c.astype(BF) for c in d_values], 1)
    d_proj_ref[...] = d_projected
    store_chunks(
        grad_refs,
        input_backward(d_middle_ref[...], d_projected, x, gain_ref, first_ref, gain_out_ref),
    )


def neighbours(count, step):
    return [
        (i, i + step)
        for i in range(count)
        if 0 <= i + step < count and i // GROUP == (i + step) // GROUP
    ]


def exchange(blocks, count):
    groups = [list(range(s, s + GROUP)) for s in range(0, count, GROUP)]
    return lax.all_to_all(blocks, "dp", 0, 0, axis_index_groups=groups)


def to_other_section(chunks, step):
    pairs = [(0, 1)] if step > 0 else [(1, 0)]
    return [lax.ppermute(rows, "section", pairs) for rows in chunks]


def partner(rows, apart, count):
    return lax.ppermute(rows, "dp", [(i, i ^ apart) for i in range(count)])


def group_pieces(piece, count):
    pieces = [piece]
    pieces += lax.optimization_barrier([partner(piece, apart, count) for apart in (4, 8, 12)])
    pieces += lax.optimization_barrier([partner(item, 2, count) for item in pieces])
    pieces += [partner(item, 1, count) for item in pieces]
    return [pieces[apart % 2 * 8 + apart // 2 % 2 * 4 + apart // 4] for apart in range(GROUP)]


def in_order(pieces, group_pos, count):
    shape = pieces[0].shape
    whole = jnp.zeros((GROUP,) + shape, pieces[0].dtype)
    for apart, item in enumerate(pieces):
        start = (group_pos ^ apart,) + (0,) * len(shape)
        whole = lax.dynamic_update_slice(whole, item[None], start)
    if count > GROUP:
        groups = [list(range(s, count, GROUP)) for s in range(GROUP)]
        whole = lax.all_gather(whole, "dp", axis=0, tiled=True, axis_index_groups=groups)
    return whole.reshape(-1, shape[-1])


def plane_rows(rows, group_pos, count):
    parts = rows.reshape(count // GROUP, 4, 4, *rows.shape[1:])
    place, plane = group_pos % 4, group_pos // 4
    taken = []
    for apart in range(4):
        block = lax.dynamic_index_in_dim(parts, place ^ apart, 2, keepdims=False)
        block = jnp.stack(
            [lax.dynamic_index_in_dim(block, plane ^ z, 1, keepdims=False) for z in range(4)]
        )
        taken.append(partner(block, apart, count) if apart else block)
    return taken


def product_body(ranges, *refs):
    refs, outs = refs[:-4], refs[-4:]
    rights = refs[: len(refs) - 4 * len(ranges)]
    rows = outs[0].shape[0]
    for index, (start, end) in enumerate(ranges):
        left = jnp.concatenate([ref[...] for ref in refs[len(rights) + 4 * index :][:4]], 1)
        right = jnp.concatenate([ref[:, start:end] for ref in rights], 0)
        product = dot(left, right)
        for plane, out_ref in enumerate(outs):
            part = product[plane * rows : (plane + 1) * rows]
            out_ref[:, start:end] = part.astype(out_ref.dtype)


def plane_product(right, terms):
    planes, groups, rows, tokens = terms[0][0][0].shape
    args = list(right) + [item.reshape(-1, tokens) for lefts, _, _ in terms for item in lefts]
    shape = (groups * rows, right[0].shape[1])
    body = functools.partial(product_body, [term[1:] for term in terms])
    return on_core(body, [(shape, F32)] + [(shape, BF)] * (planes - 1), args)


def sum_planes(blocks, count):
    got = [partner(item, 4 * (z + 1), count) for z, item in enumerate(blocks[1:])]
    total = blocks[0]
    for item in got:
        total = total + item.astype(F32)
    if count > GROUP:
        apart = [list(range(s, count, GROUP)) for s in range(GROUP)]
        total = total.reshape(count // GROUP, -1, total.shape[1])
        return lax.psum_scatter(total, "dp", scatter_dimension=0, axis_index_groups=apart)
    return total


def on_device(
    tokens_in,
    segment_ids,
    out_grad,
    qkv_weight,
    attn_out_weight,
    mlp_in_weight,
    mlp_out_weight,
    attn_gain,
    mlp_gain,
):
    lower = lax.axis_index("section") == 0
    lower_flag = lower.astype(jnp.int32)[None]
    count = lax.axis_size("dp")
    replica = lax.axis_index("dp")
    group_pos = replica % GROUP
    micro_count, row_count, width = tokens_in.shape
    shard = qkv_weight.shape[1]
    runs = -(-row_count // shard)
    (message,) = on_core(
        message_body,
        [((shard, 3 * width + LANES), BF)],
        (qkv_weight[0], attn_gain, mlp_gain, segment_ids),
        [pltpu.VMEM((LANES, LANES), F32), pltpu.VMEM((8, LANES), F32)],
    )
    inner = mlp_in_weight.shape[2]
    hidden = mlp_out_weight.shape[1] * count
    if count == GROUP:
        moved = first_block(2 * mlp_out_weight.shape[1]) - mlp_out_weight.shape[1]
        beside = partner(mlp_out_weight[0, :moved], 1, count)
        (stacked,) = on_core(
            stack_body,
            [((shard, width + inner + width + 2 * (width // 3)), BF)],
            (
                (replica % 2)[None],
                attn_out_weight[0],
                mlp_in_weight[0],
                mlp_out_weight[0],
                beside,
            ),
            (),
            [pltpu.SMEM] + [pltpu.VMEM] * 4,
        )
        others = [lax.all_gather(stacked, "dp", axis=0, tiled=True)]
    else:
        others = [
            lax.all_gather(item[0], "dp", axis=0, tiled=True)
            for item in (attn_out_weight, mlp_in_weight, mlp_out_weight)
        ]
    pieces = group_pieces(message, count)
    if count > GROUP:
        pieces = [in_order(pieces, group_pos, count)]

    positions = group_pos * row_count + jnp.arange(row_count)
    local_tables = angles(positions, local_log_base)
    global_tables = angles(positions, global_log_base)

    rows = micro_count * row_count
    pairs = rows * width // (row_count * LANES)
    in_0 = tokens_in.reshape(rows, width)
    extra_rows = -(-(2 + micro_count * runs) // 8) * 8
    first, extra, normed_0, q_0, kv_0 = on_core(
        local_project_body,
        [
            ((width, 3 * width + LANES), BF),
            ((extra_rows, width), F32),
            ((rows, width), BF),
            ((rows, width), BF),
            ((rows, 2 * width), BF),
        ],
        (group_pos[None], in_0, local_tables, *pieces),
        [pltpu.SemaphoreType.DMA((len(pieces),))],
        [pltpu.SMEM, pltpu.VMEM, pltpu.VMEM] + [pl.ANY] * len(pieces),
    )
    gain_attn, gain_mlp = extra[:1], extra[1:2]
    all_ids = extra[2 : 2 + micro_count * runs].reshape(micro_count, runs, count, shard)
    all_ids = lax.dynamic_slice_in_dim(all_ids, replica - group_pos, GROUP, 2)
    all_ids = all_ids.swapaxes(1, 2).reshape(micro_count, GROUP, runs * shard)[..., :row_count]
    segments = all_ids.reshape(micro_count, GROUP * row_count).astype(jnp.int32)

    key_pos = positions[0] - row_count + jnp.arange(3 * row_count)
    around = jnp.pad(segments, ((0, 0), (row_count, row_count)), constant_values=-1)
    key_seg = lax.dynamic_slice_in_dim(around, group_pos * row_count, 3 * row_count, 1)
    visible = (key_seg[:, :, None] == segment_ids[:, None, :]) & (
        jnp.abs(positions[None, :] - key_pos[:, None]) <= HALF_WIN
    )[None]
    bias = jnp.tile(jnp.where(visible, 0.0, masked_score), (1, 1, 2))

    own_seg = lax.dynamic_index_in_dim(segments, group_pos // 8, 0, keepdims=False)
    halves = own_seg.reshape(GROUP, 2, row_count // 2)
    mine = lax.dynamic_index_in_dim(halves, group_pos % 2, 1, keepdims=False).reshape(-1)
    theirs = lax.dynamic_index_in_dim(halves, 1 - group_pos % 2, 1, keepdims=False).reshape(-1)
    shared_seg = jnp.concatenate([mine, theirs])[:, None]
    own_seg = own_seg[:, None]

    up_pairs, down_pairs = neighbours(count, 1), neighbours(count, -1)
    around_0 = (
        lax.ppermute(kv_0, "dp", up_pairs),
        kv_0,
        lax.ppermute(kv_0, "dp", down_pairs),
    )
    att_0, total_0 = on_core(
        local_forward_body,
        [((rows, width), BF), ((pairs, 1, LANES), F32)],
        (q_0, *around_0, bias),
    )
    n2_0, mixed_0, middle_0, gate_up_0, *out_0 = on_core(
        local_middle_body,
        [
            ((rows, width), BF),
            ((rows, hidden), BF),
            ((rows, width), F32),
            ((rows, inner), F32),
        ]
        + [((row_count, width), BF)] * micro_count,
        (*others, in_0, att_0, gain_mlp),
        [pltpu.VMEM((hidden, width), BF)],
    )

    in_1 = to_other_section(out_0, 1)
    fold = row_count * 3 // 4
    half = row_count // 2
    normed_1, sent = on_core(
        global_project_body,
        [((rows, width), BF), ((GROUP, 3 * fold, LANES), BF)],
        (first, *in_1, gain_attn, global_tables),
    )
    got = exchange(sent, count)
    beside = jnp.concatenate(
        [got[:, row_count : row_count + half], got[:, 3 * fold - half :]], 1
    )
    beside = partner(beside, 1, count)
    keys = GROUP * row_count
    tiles = keys * 3 // 2 // TILE
    head_scratch = [
        pltpu.VMEM((keys * 3 // 2, LANES), BF),
        pltpu.VMEM((2, keys, LANES), BF),
        pltpu.VMEM((2, keys, LANES), BF),
        pltpu.VMEM((2, LANES, keys), BF),
    ]
    folded, total_1 = on_core(
        global_forward_body,
        [((GROUP, fold, LANES), BF), ((tiles, 1, TILE), F32)],
        (got, beside, own_seg, shared_seg),
        head_scratch + [pltpu.VMEM((keys * 3 // 2, LANES), F32)],
    )
    folded = exchange(folded, count)

    up_1 = out_grad.reshape(rows, width)
    out_1, att_1, n2_1, mixed_1, right_1, gain_mlp_1, d_mid_1, sent = on_core(
        global_middle_body,
        [
            ((rows, width), BF),
            ((rows, width), BF),
            ((rows, width), BF),
            ((rows, hidden), BF),
            ((rows, inner + width), BF),
            ((1, width), F32),
            ((rows, width), F32),
            ((GROUP, fold, LANES), BF),
        ],
        (*others, folded, *in_1, up_1, gain_mlp),
        [pltpu.VMEM((hidden, width), BF)],
    )
    d_folded = exchange(sent, count)
    sent, to_beside = on_core(
        global_backward_body,
        [((GROUP, 3 * fold, LANES), BF), ((GROUP, 2 * half, LANES), BF)],
        (got, beside, own_seg, shared_seg, total_1, d_folded),
        head_scratch
        + [
            pltpu.VMEM((keys * 3 // 2, LANES), BF),
            pltpu.VMEM((keys * 3 // 2, LANES), F32),
            pltpu.VMEM((2, keys, LANES), F32),
            pltpu.VMEM((2, keys, LANES), F32),
        ],
    )
    back = partner(to_beside, 1, count)
    gap = 3 * fold - half - row_count - half
    back = jnp.concatenate(
        [
            jnp.zeros((GROUP, row_count, LANES), BF),
            back[:, :half],
            jnp.zeros((GROUP, gap, LANES), BF),
            back[:, half:],
        ],
        1,
    )
    sent = (sent.astype(F32) + back.astype(F32)).astype(BF)
    got = exchange(sent, count)

    n1, att, n2, mixed = (
        jnp.where(lower, a, b).T.reshape(count, -1, micro_count * row_count)
        for a, b in (
            (normed_0, normed_1),
            (att_0, att_1),
            (n2_0, n2_1),
            (mixed_0, mixed_1),
        )
    )
    left = jnp.concatenate([n1, att, n2, mixed], 1)
    left, got = lax.optimization_barrier((left, got))
    left = plane_rows(left, group_pos, count)
    n1, att, n2, mixed = (
        [part[:, :, start:end] for part in left]
        for start, end in (
            (0, shard),
            (shard, 2 * shard),
            (2 * shard, 3 * shard),
            (3 * shard, left[0].shape[2]),
        )
    )
    d_proj_1, gain_attn_1, *grad_1 = on_core(
        global_finish_body,
        [((rows, 3 * width), BF), ((1, width), F32)] + [((row_count, width), BF)] * micro_count,
        (first, got, d_mid_1, *in_1, gain_attn, global_tables),
    )

    up_0 = to_other_section(grad_1, -1)
    d_mlp = [
        jnp.where(lower, a, up_1[i * row_count : (i + 1) * row_count]) for i, a in enumerate(up_0)
    ]
    across_mlp = [partner(item, 2, count) for item in d_mlp]
    beside_mlp = [partner(item, 1, count) for item in d_mlp]
    chunk = rows // CHUNKS
    gain_mlp_0, d_mid_0, d_att_0, *right = on_core(
        local_back_middle_body,
        [((1, width), F32), ((rows, width), F32), ((rows, width), BF)]
        + [((chunk, inner + width), BF)] * CHUNKS,
        (*others, lower_flag, *up_0, middle_0, gate_up_0, gain_mlp, right_1),
        [pltpu.VMEM((hidden, width), BF)],
        [pltpu.VMEM] * len(others) + [pltpu.SMEM] + [pltpu.VMEM] * 6,
    )
    across = [partner(item, 2, count) for item in right]
    beside = [partner(item, 1, count) for item in right]
    dq_0, d_own, d_before, d_after = on_core(
        local_backward_body,
        [
            ((rows, width), BF),
            ((rows, 2 * width), F32),
            ((rows, 2 * width), BF),
            ((rows, 2 * width), BF),
        ],
        (q_0, *around_0, bias, total_0, d_att_0, local_tables),
    )
    from_after = lax.ppermute(d_before, "dp", down_pairs)
    from_before = lax.ppermute(d_after, "dp", up_pairs)
    from_after, across_mlp = lax.optimization_barrier((from_after, across_mlp))
    d_proj = on_core(
        local_join_body,
        [((chunk, 3 * width), BF)] * CHUNKS,
        (lower_flag, dq_0, d_own, from_after, from_before, local_tables, d_proj_1),
        (),
        [pltpu.SMEM] + [pltpu.VMEM] * 6,
    )
    d_mlp += beside_mlp + across_mlp + [partner(item, 1, count) for item in across_mlp]
    mlp_out_share = sum_planes(plane_product(d_mlp, [(mixed, 0, width)]), count)
    d_proj, across = lax.optimization_barrier((list(d_proj), across))
    right = right + beside + across + [partner(item, 1, count) for item in across]
    in_blocks = plane_product(right, [(n2, 0, inner), (att, inner, inner + width)])
    in_share = sum_planes(in_blocks, count)
    grad_0, gain_attn_0 = on_core(
        input_backward_body,
        [((rows, width), BF), ((1, width), F32)],
        (first, d_mid_0, in_0, gain_attn, *d_proj),
    )
    gains = jnp.where(
        lower,
        jnp.concatenate([gain_attn_0, gain_mlp_0]),
        jnp.concatenate([gain_attn_1, gain_mlp_1]),
    )
    gains = gains + partner(gains, 1, count)
    gains = gains + partner(gains, 2, count)
    across = [partner(item, 2, count) for item in d_proj]
    across, in_blocks, gains = lax.optimization_barrier((across, in_blocks, gains))
    beside = [partner(item, 1, count) for item in d_proj]
    d_proj = d_proj + beside + across + [partner(item, 1, count) for item in across]
    qkv_blocks = plane_product(d_proj, [(n1, 0, 3 * width)])
    qkv_share = sum_planes(qkv_blocks, count)
    gains, _ = lax.optimization_barrier((gains, qkv_blocks))
    apart = 4
    while apart < count:
        gains = gains + partner(gains, apart, count)
        apart *= 2
    gains = lax.dynamic_slice_in_dim(gains, replica * shard, shard, 1)

    return (
        jnp.where(lower, jnp.concatenate(out_0), out_1).reshape(1, micro_count, row_count, width),
        jnp.where(lower, grad_0, jnp.concatenate(grad_1)).reshape(1, micro_count, row_count, width),
        qkv_share[None],
        in_share[None, :, inner:],
        in_share[None, :, :inner],
        mlp_out_share[None],
        gains[:1],
        gains[1:],
    )


def solution(mesh):
    in_specs = (
        P(None, "dp", None),
        P(None, "dp"),
        P(None, "dp", None),
        P("section", "dp", None),
        P("section", "dp", None),
        P("section", "dp", None),
        P("section", "dp", None),
        P("section", "dp"),
        P("section", "dp"),
    )
    out_specs = (
        P("section", None, "dp", None),
        P("section", None, "dp", None),
        P("section", "dp", None),
        P("section", "dp", None),
        P("section", "dp", None),
        P("section", "dp", None),
        P("section", "dp"),
        P("section", "dp"),
    )
    return jax.shard_map(
        on_device, mesh=mesh, in_specs=in_specs, out_specs=out_specs, check_vma=False
    )
```

```python
import functools
import math

import jax
import jax.numpy as jnp
from jax import lax
from jax.experimental import pallas as pl
from jax.experimental.pallas import tpu as pltpu
from jax.sharding import PartitionSpec as P

HEAD_DIM = 64
GROUP = 16
HALF_WIN = 64
EXTRA = 16
LANES = 128
TILE = 256

local_log_base = math.log(10000.0)
global_log_base = math.log(160000.0)
masked_score = -1e30
SCALE = 1.0 / math.sqrt(HEAD_DIM)
BF = jnp.bfloat16
F32 = jnp.float32


def dot(left, right):
    return jnp.dot(left, right, preferred_element_type=F32)


def dot_bt(left, right):
    return lax.dot_general(left, right, (((1,), (1,)), ((), ())), preferred_element_type=F32)


def dot_at(left, right):
    return lax.dot_general(left, right, (((0,), (0,)), ((), ())), preferred_element_type=F32)


def moments(values):
    center = values - jnp.mean(values, -1, keepdims=True)
    scale = lax.rsqrt(jnp.mean(center * center, -1, keepdims=True) + 1e-05)
    return center * scale, scale


def norm_back(grad_out, gain_row, xhat, scale):
    scaled = grad_out * gain_row
    mean_grad = jnp.mean(scaled, -1, keepdims=True)
    mean_dot = jnp.mean(scaled * xhat, -1, keepdims=True)
    return (scaled - mean_grad - xhat * mean_dot) * scale


def angles(positions, log_base):
    half_dim = HEAD_DIM // 2
    fraction = (2 * jnp.arange(half_dim)).astype(F32) / HEAD_DIM
    inverse = jnp.exp(-fraction * log_base)
    table = positions.astype(F32)[:, None] * inverse[None, :]
    cosine, sine = jnp.cos(table), jnp.sin(table)
    none = jnp.zeros_like(sine)
    cosine = jnp.concatenate([cosine, cosine], 1)
    to_first = jnp.concatenate([-sine, none], 1)
    to_second = jnp.concatenate([none, sine], 1)
    return jnp.tile(jnp.stack([cosine, to_first, to_second]), (1, 2, 2))


def on_core(body, outs, args, scratch=(), spaces=None, out_spaces=None):
    return pl.pallas_call(
        body,
        out_shape=[jax.ShapeDtypeStruct(shape, dtype) for shape, dtype in outs],
        in_specs=[
            pl.BlockSpec(memory_space=space) for space in spaces or [pltpu.VMEM] * len(args)
        ],
        out_specs=[
            pl.BlockSpec(memory_space=space) for space in out_spaces or [pltpu.VMEM] * len(outs)
        ],
        scratch_shapes=scratch,
        cost_estimate=pl.CostEstimate(
            flops=2**10, bytes_accessed=2**10, transcendentals=0
        ),
        compiler_params=pltpu.CompilerParams(vmem_limit_bytes=48 * 2**20),
    )(*args)


def low_lanes():
    return lax.broadcasted_iota(jnp.int32, (1, LANES), 1) < HEAD_DIM


def swap(chunk):
    return pltpu.roll(chunk, HEAD_DIM, 1)


def chunks_of(rows):
    return [rows[:, c : c + LANES] for c in range(0, rows.shape[1], LANES)]


def rotate(chunk, tables):
    cosine, to_first, to_second = tables
    quarter = HEAD_DIM // 2
    return (
        chunk * cosine
        + pltpu.roll(chunk, LANES - quarter, 1) * to_first
        + pltpu.roll(chunk, quarter, 1) * to_second
    )


def unrotate(chunk, tables):
    cosine, to_first, to_second = tables
    quarter = HEAD_DIM // 2
    return (
        chunk * cosine
        - pltpu.roll(chunk, LANES - quarter, 1) * to_first
        - pltpu.roll(chunk, quarter, 1) * to_second
    )


def low_and_high(chunks):
    swapped = [swap(chunk) for chunk in chunks]
    low = [(swapped if h % 2 else chunks)[h // 2] for h in range(2 * len(chunks))]
    high = [(chunks if h % 2 else swapped)[h // 2] for h in range(2 * len(chunks))]
    return low, high


def targets():
    for d in range(GROUP):
        micro, chip, half = d // 8, d % 8 // 2, d % 2
        yield d, micro, 3 * chip + 2 * half, 3 * chip + 1, half


def pack_folded(chunks, ref, base):
    low, high = low_and_high(chunks)
    first = low_lanes()
    rows = chunks[0].shape[0] // 2
    half, fold = rows // 2, rows * 3 // 4
    for d, micro, own, shared, side in targets():
        start = micro * rows
        part = start + side * half
        upper = jnp.concatenate(
            [high[own][start + fold : start + rows], high[shared][part : part + half]], 0
        )
        ref[d, base : base + fold] = jnp.where(
            first, low[own][start : start + fold], upper
        ).astype(BF)


def pack_pairs(lefts, rights, ref):
    low, high = low_and_high(lefts)[0], low_and_high(rights)[1]
    first = low_lanes()
    rows = lefts[0].shape[0] // 2
    half = rows // 2
    for d, micro, own, shared, side in targets():
        start = micro * rows
        part = start + side * half
        ref[d, 0:rows] = jnp.where(
            first, low[own][start : start + rows], high[own][start : start + rows]
        ).astype(BF)
        ref[d, rows : rows + half] = jnp.where(
            first, low[shared][part : part + half], high[shared][part : part + half]
        ).astype(BF)


def unpack_folded(ref, base, rows):
    first = low_lanes()
    fold = rows * 3 // 4
    low, high = {}, {}
    shared_parts = {}
    for d, micro, own, shared, side in targets():
        block = ref[d, base : base + fold].astype(F32)
        mine = jnp.concatenate([block, swap(block[: rows - fold])], 0)
        if own % 2:
            high[micro, own] = swap(mine)
        else:
            low[micro, own] = mine
        shared_parts[micro, shared, side] = block[rows - fold :]
        if side:
            both = jnp.concatenate([shared_parts[micro, shared, 0], block[rows - fold :]], 0)
            if shared % 2:
                high[micro, shared] = both
            else:
                low[micro, shared] = swap(both)
    heads = GROUP // 4 * 3
    return [
        jnp.concatenate(
            [jnp.where(first, low[m, h], high[m, h + 1]) for m in range(2)], 0
        )
        for h in range(0, heads, 2)
    ]


def unpack_pairs(ref, rows):
    first = low_lanes()
    half = rows // 2
    pairs = {}
    parts = {}
    for d, micro, own, shared, side in targets():
        pairs[micro, own] = ref[d, 0:rows].astype(F32)
        parts[side] = ref[d, rows : rows + half].astype(F32)
        if side:
            pairs[micro, shared] = jnp.concatenate([parts[0], parts[1]], 0)
    heads = GROUP // 4 * 3
    lefts, rights = [], []
    for h in range(0, heads, 2):
        even, odd = [pairs[m, h] for m in range(2)], [pairs[m, h + 1] for m in range(2)]
        lefts.append(
            jnp.concatenate([jnp.where(first, a, swap(b)) for a, b in zip(even, odd)], 0)
        )
        rights.append(
            jnp.concatenate([jnp.where(first, swap(a), b) for a, b in zip(even, odd)], 0)
        )
    return lefts, rights


class Weights:
    def __init__(self, sources, mlp_out):
        self.sources = sources
        self.mlp_out = sources[-1]
        if len(sources) == 1:
            self.mlp_out = mlp_out
            unpack_rows(sources[0], mlp_out)

    def get(self, which):
        if which == 2:
            return self.mlp_out[...]
        if len(self.sources) > 1:
            return self.sources[which][...]
        (wide,) = self.sources
        width = wide.shape[0]
        inner = 2 * self.mlp_out.shape[0]
        return wide[:, width : width + inner] if which else wide[:, :width]


def first_block(pair):
    return -(-pair // 32) * 16


def packed_pieces(shard, rows, width):
    yield 0, shard, 0, width, 0, 0
    rest = rows - shard
    side = width // 3
    yield 0, rest, width, 2 * side, shard, 0
    yield rest, 16, width, side, shard, 2 * side
    yield rest, 16, width + side, side, shard + 16, 2 * side


def unpack_rows(wide, mlp_out):
    hidden, width = mlp_out.shape
    shard = wide.shape[0] // GROUP
    start = wide.shape[1] - width - 2 * (width // 3)
    pair = 2 * hidden // GROUP
    upper = first_block(pair)
    for d in range(GROUP):
        low = d // 2 * pair + d % 2 * upper
        have = pair - upper if d % 2 else upper
        for row, rows, column, columns, to_row, to_column in packed_pieces(shard, upper, width):
            rows = min(rows, have - to_row)
            if rows > 0:
                mlp_out[low + to_row : low + to_row + rows, to_column : to_column + columns] = wide[
                    d * shard + row : d * shard + row + rows, start + column : start + column + columns
                ]


def stack_body(odd_ref, attn_ref, mlp_in_ref, own_ref, beside_ref, out_ref):
    shard, width = attn_ref.shape
    inner = mlp_in_ref.shape[1]
    out_ref[:, :width] = attn_ref[...]
    out_ref[:, width : width + inner] = mlp_in_ref[...]
    own, beside = own_ref[...].astype(F32), beside_ref[...].astype(F32)
    moved = beside.shape[0]
    even = jnp.concatenate([own, beside], 0)
    odd = jnp.concatenate([own[moved:], beside, beside], 0)
    block = jnp.where(odd_ref[0] == 1, odd, even).astype(BF)
    start = width + inner
    for row, rows, column, columns, from_row, from_column in packed_pieces(
        shard, block.shape[0], width
    ):
        out_ref[row : row + rows, start + column : start + column + columns] = block[
            from_row : from_row + rows, from_column : from_column + columns
        ]


def mlp_forward(layer_in, attended, gain, weights):
    middle = layer_in + dot(attended, weights.get(0))
    xhat, _ = moments(middle)
    normed = (xhat * gain).astype(BF)
    gate_up = dot(normed, weights.get(1))
    half = gate_up.shape[1] // 2
    gate, up = gate_up[:, :half], gate_up[:, half:]
    cdf = 0.5 * (1.0 + lax.erf(gate * math.sqrt(0.5)))
    mixed = (gate * cdf * up).astype(BF)
    result = (middle + dot(mixed, weights.get(2))).astype(BF)
    return middle, normed, gate, up, mixed, result


def mlp_backward(upstream, middle, gate, up, gain, weights):
    d_mixed = dot_bt(upstream, weights.get(2))
    cdf = 0.5 * (1.0 + lax.erf(gate * math.sqrt(0.5)))
    density = jnp.exp(-0.5 * gate * gate) * (1.0 / math.sqrt(2.0 * math.pi))
    d_gate = d_mixed * up * (cdf + gate * density)
    d_up = d_mixed * gate * cdf
    d_gate_up = jnp.concatenate([d_gate.astype(BF), d_up.astype(BF)], 1)
    d_normed = dot_bt(d_gate_up, weights.get(1))
    xhat, scale = moments(middle)
    gain_grad = jnp.sum(d_normed * xhat, 0, keepdims=True)
    d_middle = upstream.astype(F32) + norm_back(d_normed, gain, xhat, scale)
    d_attn = d_middle.astype(BF)
    d_attended = dot_bt(d_attn, weights.get(0))
    return d_gate_up, gain_grad, d_middle, d_attn, d_attended


def project(xhat, gain, first_ref, table_ref, normed_ref):
    width = xhat.shape[1]
    normed = (xhat * gain).astype(BF)
    normed_ref[...] = normed
    tables = [table_ref[i] for i in range(3)]
    results = [dot(normed, first_ref[:, c * width : (c + 1) * width]) for c in range(3)]
    queries, keys, values = chunks_of(results[0]), chunks_of(results[1]), results[2]
    return [rotate(c, tables) for c in queries], [rotate(c, tables) for c in keys], values


def input_backward(d_middle, d_projected, x, gain_ref, first_ref, gain_out_ref):
    d_normed = dot_bt(d_projected, first_ref[:, : d_projected.shape[1]])
    xhat, scale = moments(x)
    gain_out_ref[...] = jnp.sum(d_normed * xhat, 0, keepdims=True)
    return (d_middle + norm_back(d_normed, gain_ref[...], xhat, scale)).astype(BF)


def joined(refs):
    return jnp.concatenate([ref[...] for ref in refs], 0)


def store_right(right_ref, d_gate_up, d_attn, d_mlp):
    inner, width = d_gate_up.shape[1], d_attn.shape[1]
    right_ref[:, :inner] = d_gate_up
    right_ref[:, inner : inner + width] = d_attn
    right_ref[:, inner + width :] = d_mlp


def store_chunks(refs, rows):
    size = rows.shape[0] // len(refs)
    for i, ref in enumerate(refs):
        ref[...] = rows[i * size : (i + 1) * size]


def message_body(w_ref, attn_ref, mlp_ref, ids_ref, out_ref, rows_scr, ids_scr):
    shard, columns = w_ref.shape
    micro_count, row_count = ids_ref.shape
    out_ref[:, :columns] = w_ref[...]
    rows_scr[...] = jnp.zeros_like(rows_scr)
    ids_scr[...] = jnp.zeros_like(ids_scr)
    rows_scr[0:1, :shard] = attn_ref[...].astype(F32)
    rows_scr[1:2, :shard] = mlp_ref[...].astype(F32)
    ids_scr[:micro_count, :row_count] = ids_ref[...].astype(F32)
    runs = -(-row_count // shard)
    for run in range(runs):
        turned = ids_scr[...]
        if run:
            turned = pltpu.roll(turned, LANES - run * shard, 1)
        for micro in range(micro_count):
            row = 2 + micro * runs + run
            rows_scr[row : row + 1] = turned[micro : micro + 1]
    out_ref[:, columns:] = rows_scr[...].T[:shard].astype(BF)


def local_project_body(first_ref, x_ref, table_ref, extra_ref, normed_ref, q_ref, kv_ref):
    xhat, _ = moments(x_ref[...].astype(F32))
    extra = first_ref[:, first_ref.shape[1] - LANES :].astype(F32).T
    extra_ref[...] = extra[: extra_ref.shape[0]]
    queries, keys, values = project(xhat, extra[:1], first_ref, table_ref, normed_ref)
    width = values.shape[1]
    for j, (q, k) in enumerate(zip(queries, keys)):
        q_ref[:, LANES * j : LANES * (j + 1)] = q.astype(BF)
        kv_ref[:, LANES * j : LANES * (j + 1)] = k.astype(BF)
    kv_ref[:, width:] = values.astype(BF)


def two_heads(chunk):
    first = low_lanes()
    wide = chunk.astype(F32)
    return jnp.concatenate([jnp.where(first, wide, 0.0), jnp.where(first, 0.0, wide)], 0)


def pick_heads(rows):
    half = rows.shape[0] // 2
    return jnp.where(low_lanes(), rows[:half], rows[half:])


def local_parts(q_ref, before_ref, own_ref, after_ref):
    rows = q_ref.shape[0] // 2
    width = q_ref.shape[1]
    for micro in range(2):
        for j in range(width // LANES):
            here = slice(micro * rows, (micro + 1) * rows)
            lanes = slice(LANES * j, LANES * (j + 1))
            more = slice(width + LANES * j, width + LANES * (j + 1))
            keys, values = (
                jnp.concatenate([ref[here, part] for ref in (before_ref, own_ref, after_ref)], 0)
                for part in (lanes, more)
            )
            queries = (two_heads(q_ref[here, lanes]) * SCALE).astype(BF)
            yield micro * (width // LANES) + j, micro, here, lanes, more, queries, keys, values


def local_forward_body(q_ref, before_ref, own_ref, after_ref, bias_ref, att_ref, total_ref):
    parts = local_parts(q_ref, before_ref, own_ref, after_ref)
    for index, micro, here, lanes, _, queries, keys, values in parts:
        scores = dot_bt(keys, queries) + bias_ref[micro]
        peak = jnp.max(scores, 0, keepdims=True)
        weights = jnp.exp(scores - peak)
        total = jnp.sum(weights, 0, keepdims=True)
        total_ref[index] = peak + jnp.log(total)
        probs = (weights * (1.0 / total)).astype(BF)
        att_ref[here, lanes] = pick_heads(dot_at(probs, values)).astype(BF)


def local_backward_body(
    q_ref, before_ref, own_ref, after_ref, bias_ref, total_ref, d_ref, table_ref,
    dq_ref, d_own_ref, d_before_ref, d_after_ref,
):
    tables = [table_ref[i] for i in range(3)]
    parts = local_parts(q_ref, before_ref, own_ref, after_ref)
    rows = q_ref.shape[0] // 2
    for index, micro, here, lanes, more, queries, keys, values in parts:
        d_out = two_heads(d_ref[here, lanes]).astype(BF)
        probs = jnp.exp(dot_bt(keys, queries) + bias_ref[micro] - total_ref[index])
        d_probs = dot_bt(values, d_out)
        product = probs * d_probs
        delta = jnp.sum(product, 0, keepdims=True)
        d_scores = (product - probs * delta).astype(BF)
        d_queries = pick_heads(dot_at(d_scores, keys)) * SCALE
        local_tables = [table[here] for table in tables]
        dq_ref[here, lanes] = unrotate(d_queries, local_tables).astype(BF)
        for part, grads in ((lanes, dot(d_scores, queries)), (more, dot(probs.astype(BF), d_out))):
            d_before_ref[here, part] = grads[:rows].astype(BF)
            d_own_ref[here, part] = grads[rows : 2 * rows]
            d_after_ref[here, part] = grads[2 * rows :].astype(BF)


def local_finish_body(
    lower_ref, first_ref, dq_ref, own_ref, low_ref, high_ref, table_ref, d_middle_ref, x_ref, gain_ref,
    gain_mlp_ref, other_ref, other_attn_ref, other_mlp_ref, out_ref, grad_ref, gain_attn_ref, gain_scr,
):
    rows, width = dq_ref.shape

    @pl.when(lower_ref[0] == 1)
    def _():
        tables = [table_ref[i] for i in range(3)]
        total = own_ref[...] + low_ref[...].astype(F32) + high_ref[...].astype(F32)
        out_ref[:rows, :width] = dq_ref[...]
        for j, chunk in enumerate(chunks_of(total[:, :width])):
            start = width + LANES * j
            out_ref[:rows, start : start + LANES] = unrotate(chunk, tables).astype(BF)
        out_ref[:rows, 2 * width :] = total[:, width:].astype(BF)
        grad_ref[...] = input_backward(
            d_middle_ref[...], out_ref[:rows], x_ref[...].astype(F32), gain_ref, first_ref, gain_scr
        )

    @pl.when(lower_ref[0] == 0)
    def _():
        out_ref[:rows] = other_ref[...]
        grad_ref[...] = jnp.zeros_like(grad_ref)
        gain_scr[...] = other_attn_ref[...]

    gain_attn_ref[...] = gain_scr[...]
    gain_mlp = jnp.where(lower_ref[0] == 1, gain_mlp_ref[...], other_mlp_ref[...])
    index = lax.broadcasted_iota(jnp.int32, (EXTRA, width), 0)
    tail = jnp.zeros((EXTRA, width), F32)
    for row, gain in ((0, gain_scr[...]), (2, gain_mlp)):
        high = gain.astype(BF).astype(F32)
        tail = jnp.where(index == row, high, tail)
        tail = jnp.where(index == row + 1, gain - high, tail)
    out_ref[rows:] = jnp.zeros((EXTRA, out_ref.shape[1]), BF)
    out_ref[rows:, :width] = tail.astype(BF)


def local_middle_body(*refs):
    sources, refs = refs[:-10], refs[-10:]
    x_ref, att_ref, gain_ref, normed_ref, mixed_ref, middle_ref, gate_up_ref = refs[:7]
    weights = Weights(sources, refs[9])
    middle, normed, gate, up, mixed, result = mlp_forward(
        x_ref[...].astype(F32), att_ref[...], gain_ref[...], weights
    )
    store_chunks(refs[7:9], result)
    normed_ref[...] = normed
    mixed_ref[...] = mixed
    middle_ref[...] = middle
    half = gate.shape[1]
    gate_up_ref[:, :half] = gate
    gate_up_ref[:, half:] = up


def local_back_middle_body(*refs):
    sources, refs = refs[:-12], refs[-12:]
    lower_ref, low_ref, high_ref, middle_ref, gate_up_ref, gain_ref, other_ref = refs[:7]
    gain_out_ref, d_middle_ref, d_att_ref, right_ref = refs[7:11]
    weights = Weights(sources, refs[11])
    half = gate_up_ref.shape[1] // 2
    upstream = joined([low_ref, high_ref])
    d_gate_up, gain_grad, d_middle, d_attn, d_attended = mlp_backward(
        upstream, middle_ref[...], gate_up_ref[:, :half], gate_up_ref[:, half:],
        gain_ref[...], weights,
    )
    gain_out_ref[...] = gain_grad
    d_middle_ref[...] = d_middle
    d_att_ref[...] = d_attended.astype(BF)

    @pl.when(lower_ref[0] == 1)
    def _():
        store_right(right_ref, d_gate_up, d_attn, upstream)

    @pl.when(lower_ref[0] == 0)
    def _():
        right_ref[...] = other_ref[...]


def global_project_body(first_ref, low_ref, high_ref, gain_ref, table_ref, normed_ref, sent_ref):
    xhat, _ = moments(joined([low_ref, high_ref]).astype(F32))
    queries, keys, values = project(xhat, gain_ref[...], first_ref, table_ref, normed_ref)
    pack_pairs(queries, keys, sent_ref)
    pack_folded(chunks_of(values), sent_ref, sent_ref.shape[1] * 2 // 3)


def flat(blocks):
    return blocks.reshape(-1, LANES)


def own_unfolded(ref, base, rows):
    fold = rows * 3 // 4
    block = ref[:, base : base + fold].astype(F32)
    rest = swap(flat(block[:, : rows - fold])).reshape(GROUP, rows - fold, LANES)
    return flat(jnp.concatenate([block, rest], 1))


def shared_unfolded(ref, start, rows):
    return swap(flat(ref[:, start : start + rows // 2].astype(F32)))


def fill_heads(got_ref, other_ref, own_seg_ref, shared_seg_ref, q_scr, k_scr, v_scr):
    rows = got_ref.shape[1] * 4 // 9
    half = rows // 2
    first = low_lanes()
    lane = lax.broadcasted_iota(jnp.int32, (1, LANES), 1) - HEAD_DIM
    own = flat(got_ref[:, 0:rows].astype(F32))
    shared = flat(got_ref[:, rows : rows + half].astype(F32))
    other = flat(other_ref[:, 0:half].astype(F32))
    count = own.shape[0]
    own_hit = lane == own_seg_ref[...]
    shared_hit = lane == shared_seg_ref[...]
    both = jnp.concatenate([shared, other], 0)
    for start, pairs, hit in (
        (0, own, own_hit),
        (count, shared, shared_hit[: count // 2]),
    ):
        marked = jnp.where(hit, 1.0, 0.0)
        q_scr[start : start + pairs.shape[0]] = jnp.where(first, pairs * SCALE, marked).astype(BF)
    for unit, pairs, hit in ((0, own, own_hit), (1, both, shared_hit)):
        marked = jnp.where(hit, 0.0, masked_score)
        k_scr[unit] = jnp.where(first, swap(pairs), marked).astype(BF)
    base = rows + half
    v_scr[0] = jnp.where(first, own_unfolded(got_ref, base, rows), 0.0).astype(BF)
    start = base + rows - rows * 3 // 4
    shared_v = jnp.concatenate(
        [shared_unfolded(got_ref, start, rows), shared_unfolded(other_ref, half, rows)], 0
    )
    v_scr[1] = jnp.where(first, shared_v, 0.0).astype(BF)


def fold_out(own, shared, rows, ref, base):
    fold = rows * 3 // 4
    blocks = own.reshape(GROUP, rows, LANES)
    swapped = swap(own).reshape(GROUP, rows, LANES)
    upper = jnp.concatenate(
        [swapped[:, fold:], swap(shared).reshape(GROUP, rows // 2, LANES)], 1
    )
    ref[:, base : base + fold] = jnp.where(low_lanes(), blocks[:, :fold], upper).astype(BF)


def global_forward_body(
    got_ref, other_ref, own_seg_ref, shared_seg_ref, out_ref, total_ref,
    q_scr, k_scr, v_scr, vt_scr, o_scr,
):
    fill_heads(got_ref, other_ref, own_seg_ref, shared_seg_ref, q_scr, k_scr, v_scr)
    for unit in range(2):
        vt_scr[unit] = v_scr[unit].astype(F32).T.astype(BF)
    count = k_scr.shape[1]

    def step(tile, carry):
        unit = tile // (count // TILE)
        rows = pl.ds(pl.multiple_of(tile * TILE, TILE), TILE)
        scores = dot_bt(k_scr[unit], q_scr[rows])
        peak = jnp.max(scores, 0, keepdims=True)
        weights = jnp.exp(scores - peak)
        total = jnp.sum(weights, 0, keepdims=True)
        total_ref[tile] = peak + jnp.log(total)
        out = dot(vt_scr[unit], weights.astype(BF)) * (1.0 / total)
        o_scr[rows] = out.T
        return carry

    lax.fori_loop(0, q_scr.shape[0] // TILE, step, 0)
    rows = got_ref.shape[1] * 4 // 9
    fold_out(o_scr[:count], o_scr[count:], rows, out_ref, 0)


def global_backward_body(
    got_ref, other_ref, own_seg_ref, shared_seg_ref, total_ref, d_ref, sent_ref, to_other_ref,
    q_scr, k_scr, v_scr, kt_scr, d_scr, dq_scr, dk_scr, dv_scr,
):
    fill_heads(got_ref, other_ref, own_seg_ref, shared_seg_ref, q_scr, k_scr, v_scr)
    first = low_lanes()
    rows = got_ref.shape[1] * 4 // 9
    half = rows // 2
    for unit in range(2):
        keys = jnp.where(first, k_scr[unit].astype(F32), 0.0)
        kt_scr[unit] = keys.T.astype(BF)
    count = k_scr.shape[1]
    d_scr[:count] = jnp.where(first, own_unfolded(d_ref, 0, rows), 0.0).astype(BF)
    d_scr[count:] = jnp.where(
        first, shared_unfolded(d_ref, rows - rows * 3 // 4, rows), 0.0
    ).astype(BF)
    dk_scr[...] = jnp.zeros_like(dk_scr)
    dv_scr[...] = jnp.zeros_like(dv_scr)

    def step(tile, carry):
        unit = tile // (count // TILE)
        here = pl.ds(pl.multiple_of(tile * TILE, TILE), TILE)
        queries, d_out = q_scr[here], d_scr[here]
        probs = jnp.exp(dot_bt(k_scr[unit], queries) - total_ref[tile])
        d_probs = dot_bt(v_scr[unit], d_out)
        product = probs * d_probs
        delta = jnp.sum(product, 0, keepdims=True)
        d_scores = (product - probs * delta).astype(BF)
        dv_scr[unit] += dot(probs.astype(BF), d_out)
        dk_scr[unit] += dot(d_scores, queries)
        dq_scr[here] = dot(kt_scr[unit], d_scores).T * SCALE
        return carry

    lax.fori_loop(0, q_scr.shape[0] // TILE, step, 0)
    mine = count // 2
    own = jnp.where(first, dq_scr[:count], swap(dk_scr[0]))
    sent_ref[:, 0:rows] = own.reshape(GROUP, rows, LANES).astype(BF)
    shared_k, shared_v = dk_scr[1], dv_scr[1]
    shared = jnp.where(first, dq_scr[count:], swap(shared_k[:mine]))
    sent_ref[:, rows : rows + half] = shared.reshape(GROUP, half, LANES).astype(BF)
    fold_out(dv_scr[0], shared_v[:mine], rows, sent_ref, rows + half)
    for place, grads in enumerate((shared_k, shared_v)):
        other = jnp.where(first, 0.0, swap(grads[mine:])).reshape(GROUP, half, LANES)
        to_other_ref[:, place * half : (place + 1) * half] = other.astype(BF)


def global_middle_body(*refs):
    sources, refs = refs[:-14], refs[-14:]
    got_ref, low_ref, high_ref, up_ref, gain_ref, out_ref, att_ref, normed_ref, mixed_ref = refs[:9]
    right_ref, gain_out_ref, d_middle_ref, sent_ref = refs[9:13]
    weights = Weights(sources, refs[13])
    rows = low_ref.shape[0]
    attended = jnp.concatenate([c.astype(BF) for c in unpack_folded(got_ref, 0, rows)], 1)
    att_ref[...] = attended
    gain = gain_ref[...]
    middle, normed, gate, up, mixed, result = mlp_forward(
        joined([low_ref, high_ref]).astype(F32), attended, gain, weights
    )
    out_ref[...] = result
    normed_ref[...] = normed
    mixed_ref[...] = mixed
    d_gate_up, gain_grad, d_middle, d_attn, d_attended = mlp_backward(
        up_ref[...], middle, gate, up, gain, weights
    )
    store_right(right_ref, d_gate_up, d_attn, up_ref[...])
    gain_out_ref[...] = gain_grad
    d_middle_ref[...] = d_middle
    pack_folded(chunks_of(d_attended), sent_ref, 0)


def global_finish_body(
    first_ref, got_ref, d_middle_ref, low_ref, high_ref, gain_ref, table_ref,
    d_proj_ref, gain_out_ref, *grad_refs,
):
    tables = [table_ref[i] for i in range(3)]
    x = joined([low_ref, high_ref]).astype(F32)
    rows = low_ref.shape[0]
    d_queries, d_keys = unpack_pairs(got_ref, rows)
    d_values = unpack_folded(got_ref, rows * 3 // 2, rows)
    parts = [unrotate(c, tables).astype(BF) for c in d_queries + d_keys]
    d_projected = jnp.concatenate(parts + [c.astype(BF) for c in d_values], 1)
    d_proj_ref[...] = d_projected
    store_chunks(
        grad_refs,
        input_backward(d_middle_ref[...], d_projected, x, gain_ref, first_ref, gain_out_ref),
    )


def neighbours(count, step):
    return [
        (i, i + step)
        for i in range(count)
        if 0 <= i + step < count and i // GROUP == (i + step) // GROUP
    ]


def exchange(blocks, count):
    groups = [list(range(s, s + GROUP)) for s in range(0, count, GROUP)]
    return lax.all_to_all(blocks, "dp", 0, 0, axis_index_groups=groups)


def to_other_section(chunks, step):
    pairs = [(0, 1)] if step > 0 else [(1, 0)]
    return [lax.ppermute(rows, "section", pairs) for rows in chunks]


def partner(rows, apart, count):
    return lax.ppermute(rows, "dp", [(i, i ^ apart) for i in range(count)])


def gather_rows(piece, group_pos, count):
    pieces = {0: piece}
    for apart in (4, 8, 12):
        pieces[apart] = partner(piece, apart, count)
    for apart in (0, 4, 8, 12):
        pieces[apart + 2] = partner(pieces[apart], 2, count)
    for apart in range(0, GROUP, 2):
        pieces[apart + 1] = partner(pieces[apart], 1, count)
    whole = jnp.zeros((GROUP,) + piece.shape, piece.dtype)
    for apart, item in pieces.items():
        start = (group_pos ^ apart,) + (0,) * piece.ndim
        whole = lax.dynamic_update_slice(whole, item[None], start)
    if count > GROUP:
        groups = [list(range(s, count, GROUP)) for s in range(GROUP)]
        whole = lax.all_gather(whole, "dp", axis=0, tiled=True, axis_index_groups=groups)
    return whole.reshape(-1, piece.shape[-1]), pieces[2]


def plane_rows(rows, group_pos, count):
    parts = rows.reshape(count // GROUP, 4, 4, *rows.shape[1:])
    place, plane = group_pos % 4, group_pos // 4
    taken = []
    for apart in range(4):
        block = lax.dynamic_index_in_dim(parts, place ^ apart, 2, keepdims=False)
        block = jnp.stack(
            [lax.dynamic_index_in_dim(block, plane ^ z, 1, keepdims=False) for z in range(4)]
        )
        taken.append(partner(block, apart, count) if apart else block)
    return taken


def early_body(shard, *refs):
    refs, outs = refs[:-4], refs[-4:]
    rights, n2, mixed, att = (refs[4 * i : 4 * i + 4] for i in range(4))
    width = outs[0].shape[1]
    inner = rights[0].shape[1] - 2 * width

    def product(lefts, start, end):
        left = jnp.concatenate([ref[...] for ref in lefts], 1)
        return dot(left, jnp.concatenate([ref[:, start:end] for ref in rights], 0))

    base = 0
    for lefts, start, end in (
        (n2, 0, inner),
        (mixed, inner + width, inner + 2 * width),
        (att, inner, inner + width),
    ):
        result = product(lefts, start, end)
        rows = result.shape[0] // 4
        for column in range(0, end - start, width):
            for plane, out_ref in enumerate(outs):
                part = result[plane * rows : (plane + 1) * rows, column : column + width]
                out_ref[base : base + rows] = part.astype(out_ref.dtype)
            base += rows


def late_body(place_ref, *refs):
    refs, (outs, scr) = refs[:-5], (refs[-5:-1], refs[-1])
    rights, lefts = refs[:4], refs[4:]
    tokens = lefts[0].shape[1]
    columns = rights[0].shape[1]
    width = columns // 3
    rows = outs[0].shape[0]
    left = jnp.concatenate([ref[...] for ref in lefts], 1)
    product = dot(left, jnp.concatenate([ref[:tokens] for ref in rights], 0))
    tail = sum(ref[tokens:, :width].astype(F32) for ref in rights)
    both = jnp.concatenate([tail, jnp.zeros((LANES - EXTRA, width), F32)], 0).T
    lane = lax.broadcasted_iota(jnp.int32, (1, LANES), 1)
    lows = pltpu.roll(both, LANES - 1, 1)
    scr[...] = jnp.where(lane % 2 == 0, both + lows, 0.0)
    for plane, out_ref in enumerate(outs):
        part = product[plane * rows : (plane + 1) * rows]
        out_ref[:, :columns] = part.astype(out_ref.dtype)
        d = (place_ref[0] // 4 ^ plane) * 4 + place_ref[0] % 4
        start = pl.multiple_of(d * rows, 16)
        out_ref[:, columns:] = scr[pl.ds(start, rows)].astype(out_ref.dtype)


def flat_rows(parts):
    return [part.reshape(-1, part.shape[-1]) for part in parts]


def four_planes(shape):
    return [(shape, F32)] + [(shape, BF)] * 3


def plane_parts(rows, count, after=None):
    across = partner(rows, 2, count)
    beside = partner(rows, 1, count)
    if after is not None:
        across, _ = lax.optimization_barrier((across, after))
    return [rows, beside, across, partner(across, 1, count)]


def sum_planes(blocks, count):
    got = [partner(item, 4 * (z + 1), count) for z, item in enumerate(blocks[1:])]
    total = blocks[0]
    for item in got:
        total = total + item.astype(F32)
    return total


def over_groups(rows, count):
    if count == GROUP:
        return rows
    apart = [list(range(s, count, GROUP)) for s in range(GROUP)]
    rows = rows.reshape(count // GROUP, -1, rows.shape[1])
    return lax.psum_scatter(rows, "dp", scatter_dimension=0, axis_index_groups=apart)


def on_device(
    tokens_in,
    segment_ids,
    out_grad,
    qkv_weight,
    attn_out_weight,
    mlp_in_weight,
    mlp_out_weight,
    attn_gain,
    mlp_gain,
):
    lower = lax.axis_index("section") == 0
    lower_flag = lower.astype(jnp.int32)[None]
    shard_total = qkv_weight.shape[1] * (lax.axis_size("dp") // GROUP)
    hidden_total = mlp_out_weight.shape[1] * (lax.axis_size("dp") // GROUP)
    count = lax.axis_size("dp")
    replica = lax.axis_index("dp")
    group_pos = replica % GROUP
    micro_count, row_count, width = tokens_in.shape
    shard = qkv_weight.shape[1]
    runs = -(-row_count // shard)
    (message,) = on_core(
        message_body,
        [((shard, 3 * width + LANES), BF)],
        (qkv_weight[0], attn_gain, mlp_gain, segment_ids),
        [pltpu.VMEM((LANES, LANES), F32), pltpu.VMEM((8, LANES), F32)],
    )
    first, early_piece = gather_rows(message, group_pos, count)
    inner = mlp_in_weight.shape[2]
    hidden = mlp_out_weight.shape[1] * count
    if count == GROUP:
        moved = first_block(2 * mlp_out_weight.shape[1]) - mlp_out_weight.shape[1]
        beside = partner(mlp_out_weight[0, :moved], 1, count)
        (stacked,) = on_core(
            stack_body,
            [((shard, width + inner + width + 2 * (width // 3)), BF)],
            (
                (replica % 2)[None],
                attn_out_weight[0],
                mlp_in_weight[0],
                mlp_out_weight[0],
                beside,
            ),
            (),
            [pltpu.SMEM] + [pltpu.VMEM] * 4,
        )
        stacked, _ = lax.optimization_barrier((stacked, early_piece))
        others = [lax.all_gather(stacked, "dp", axis=0, tiled=True)]
    else:
        others = [
            lax.all_gather(item[0], "dp", axis=0, tiled=True)
            for item in (attn_out_weight, mlp_in_weight, mlp_out_weight)
        ]
    positions = group_pos * row_count + jnp.arange(row_count)
    local_tables = angles(positions, local_log_base)
    global_tables = angles(positions, global_log_base)

    rows = micro_count * row_count
    pairs = rows * width // (row_count * LANES)
    in_0 = tokens_in.reshape(rows, width)
    extra_rows = -(-(2 + micro_count * runs) // 8) * 8
    extra, normed_0, q_0, kv_0 = on_core(
        local_project_body,
        [
            ((extra_rows, width), F32),
            ((rows, width), BF),
            ((rows, width), BF),
            ((rows, 2 * width), BF),
        ],
        (first, in_0, local_tables),
    )
    gain_attn, gain_mlp = extra[:1], extra[1:2]
    all_ids = extra[2 : 2 + micro_count * runs].reshape(micro_count, runs, count, shard)
    all_ids = lax.dynamic_slice_in_dim(all_ids, replica - group_pos, GROUP, 2)
    all_ids = all_ids.swapaxes(1, 2).reshape(micro_count, GROUP, runs * shard)[..., :row_count]
    segments = all_ids.reshape(micro_count, GROUP * row_count).astype(jnp.int32)

    key_pos = positions[0] - row_count + jnp.arange(3 * row_count)
    around = jnp.pad(segments, ((0, 0), (row_count, row_count)), constant_values=-1)
    key_seg = lax.dynamic_slice_in_dim(around, group_pos * row_count, 3 * row_count, 1)
    visible = (key_seg[:, :, None] == segment_ids[:, None, :]) & (
        jnp.abs(positions[None, :] - key_pos[:, None]) <= HALF_WIN
    )[None]
    bias = jnp.tile(jnp.where(visible, 0.0, masked_score), (1, 1, 2))

    own_seg = lax.dynamic_index_in_dim(segments, group_pos // 8, 0, keepdims=False)
    halves = own_seg.reshape(GROUP, 2, row_count // 2)
    mine = lax.dynamic_index_in_dim(halves, group_pos % 2, 1, keepdims=False).reshape(-1)
    theirs = lax.dynamic_index_in_dim(halves, 1 - group_pos % 2, 1, keepdims=False).reshape(-1)
    shared_seg = jnp.concatenate([mine, theirs])[:, None]
    own_seg = own_seg[:, None]

    up_pairs, down_pairs = neighbours(count, 1), neighbours(count, -1)
    around_0 = (
        lax.ppermute(kv_0, "dp", up_pairs),
        kv_0,
        lax.ppermute(kv_0, "dp", down_pairs),
    )
    att_0, total_0 = on_core(
        local_forward_body,
        [((rows, width), BF), ((pairs, 1, LANES), F32)],
        (q_0, *around_0, bias),
    )
    n2_0, mixed_0, middle_0, gate_up_0, *out_0 = on_core(
        local_middle_body,
        [
            ((rows, width), BF),
            ((rows, hidden), BF),
            ((rows, width), F32),
            ((rows, inner), F32),
        ]
        + [((row_count, width), BF)] * micro_count,
        (*others, in_0, att_0, gain_mlp),
        [pltpu.VMEM((hidden, width), BF)],
    )

    in_1 = to_other_section(out_0, 1)
    fold = row_count * 3 // 4
    half = row_count // 2
    normed_1, sent = on_core(
        global_project_body,
        [((rows, width), BF), ((GROUP, 3 * fold, LANES), BF)],
        (first, *in_1, gain_attn, global_tables),
    )
    got = exchange(sent, count)
    beside = jnp.concatenate(
        [got[:, row_count : row_count + half], got[:, 3 * fold - half :]], 1
    )
    beside = partner(beside, 1, count)
    keys = GROUP * row_count
    tiles = keys * 3 // 2 // TILE
    head_scratch = [
        pltpu.VMEM((keys * 3 // 2, LANES), BF),
        pltpu.VMEM((2, keys, LANES), BF),
        pltpu.VMEM((2, keys, LANES), BF),
        pltpu.VMEM((2, LANES, keys), BF),
    ]
    folded, total_1 = on_core(
        global_forward_body,
        [((GROUP, fold, LANES), BF), ((tiles, 1, TILE), F32)],
        (got, beside, own_seg, shared_seg),
        head_scratch + [pltpu.VMEM((keys * 3 // 2, LANES), F32)],
    )
    folded = exchange(folded, count)

    up_1 = out_grad.reshape(rows, width)
    out_1, att_1, n2_1, mixed_1, right_1, gain_mlp_1, d_mid_1, sent = on_core(
        global_middle_body,
        [
            ((rows, width), BF),
            ((rows, width), BF),
            ((rows, width), BF),
            ((rows, hidden), BF),
            ((rows, inner + 2 * width), BF),
            ((1, width), F32),
            ((rows, width), F32),
            ((GROUP, fold, LANES), BF),
        ],
        (*others, folded, *in_1, up_1, gain_mlp),
        [pltpu.VMEM((hidden, width), BF)],
    )
    d_folded = exchange(sent, count)
    sent, to_beside = on_core(
        global_backward_body,
        [((GROUP, 3 * fold, LANES), BF), ((GROUP, 2 * half, LANES), BF)],
        (got, beside, own_seg, shared_seg, total_1, d_folded),
        head_scratch
        + [
            pltpu.VMEM((keys * 3 // 2, LANES), BF),
            pltpu.VMEM((keys * 3 // 2, LANES), F32),
            pltpu.VMEM((2, keys, LANES), F32),
            pltpu.VMEM((2, keys, LANES), F32),
        ],
    )
    back = partner(to_beside, 1, count)
    gap = 3 * fold - half - row_count - half
    back = jnp.concatenate(
        [
            jnp.zeros((GROUP, row_count, LANES), BF),
            back[:, :half],
            jnp.zeros((GROUP, gap, LANES), BF),
            back[:, half:],
        ],
        1,
    )
    sent = (sent.astype(F32) + back.astype(F32)).astype(BF)
    got = exchange(sent, count)

    n1, att, n2, mixed = (
        jnp.where(lower, a, b).T.reshape(count, -1, micro_count * row_count)
        for a, b in (
            (normed_0, normed_1),
            (att_0, att_1),
            (n2_0, n2_1),
            (mixed_0, mixed_1),
        )
    )
    left = jnp.concatenate([n1, att, n2, mixed], 1)
    left = plane_rows(left, group_pos, count)
    left, got = lax.optimization_barrier((left, got))
    n1, att, n2, mixed = (
        [part[:, :, start:end] for part in left]
        for start, end in (
            (0, shard),
            (shard, 2 * shard),
            (2 * shard, 3 * shard),
            (3 * shard, left[0].shape[2]),
        )
    )
    d_proj_1, gain_attn_1, *grad_1 = on_core(
        global_finish_body,
        [((rows, 3 * width), BF), ((1, width), F32)] + [((row_count, width), BF)] * micro_count,
        (first, got, d_mid_1, *in_1, gain_attn, global_tables),
    )

    up_0 = to_other_section(grad_1, -1)
    gain_mlp_0, d_mid_0, d_att_0, right = on_core(
        local_back_middle_body,
        [
            ((1, width), F32),
            ((rows, width), F32),
            ((rows, width), BF),
            ((rows, inner + 2 * width), BF),
        ],
        (*others, lower_flag, *up_0, middle_0, gate_up_0, gain_mlp, right_1),
        [pltpu.VMEM((hidden, width), BF)],
        [pltpu.VMEM] * len(others) + [pltpu.SMEM] + [pltpu.VMEM] * 6,
    )
    right = plane_parts(right, count)
    dq_0, d_own, d_before, d_after = on_core(
        local_backward_body,
        [
            ((rows, width), BF),
            ((rows, 2 * width), F32),
            ((rows, 2 * width), BF),
            ((rows, 2 * width), BF),
        ],
        (q_0, *around_0, bias, total_0, d_att_0, local_tables),
    )
    from_after = lax.ppermute(d_before, "dp", down_pairs)
    from_before = lax.ppermute(d_after, "dp", up_pairs)
    d_proj, grad_0, gain_attn_sum = on_core(
        local_finish_body,
        [((rows + EXTRA, 3 * width), BF), ((rows, width), BF), ((1, width), F32)],
        (
            lower_flag, first, dq_0, d_own, from_after, from_before, local_tables, d_mid_0, in_0, gain_attn,
            gain_mlp_0, d_proj_1, gain_attn_1, gain_mlp_1,
        ),
        [pltpu.VMEM((1, width), F32)],
        [pltpu.SMEM] + [pltpu.VMEM] * 13,
    )
    early_rows = shard_total * (inner // width + 1) + hidden_total
    early = on_core(
        functools.partial(early_body, shard),
        four_planes((early_rows, width)),
        (*right, *flat_rows(n2), *flat_rows(mixed), *flat_rows(att)),
    )
    d_proj = plane_parts(d_proj, count, early)
    early = sum_planes(early, count)
    late_in = (group_pos[None], *d_proj, *flat_rows(n1))
    late = on_core(
        late_body,
        four_planes((shard_total, 3 * width + LANES)),
        late_in,
        [pltpu.VMEM((width, LANES), F32)],
        [pltpu.SMEM] + [pltpu.VMEM] * (len(late_in) - 1),
    )
    late = sum_planes(late, count)
    parts = [early[p * shard_total : (p + 1) * shard_total] for p in range(inner // width)]
    start = shard_total * (inner // width)
    in_share = jnp.concatenate(parts, 1)
    mlp_out_share = early[start : start + hidden_total]
    attn_share = early[start + hidden_total :]
    gain_columns = late[:, 3 * width :]
    qkv_share, in_share, mlp_out_share, attn_share, gain_columns = (
        over_groups(item, count)
        for item in (late[:, : 3 * width], in_share, mlp_out_share, attn_share, gain_columns)
    )
    if count == GROUP:
        gains = jnp.stack([gain_columns[:, 0], gain_columns[:, 2]])
    else:
        gain_mlp_sum = jnp.where(lower, gain_mlp_0, gain_mlp_1)
        gains = lax.psum(jnp.concatenate([gain_attn_sum, gain_mlp_sum]), "dp")
        gains = lax.dynamic_slice_in_dim(gains, replica * shard, shard, 1)

    return (
        jnp.where(lower, jnp.concatenate(out_0), out_1).reshape(1, micro_count, row_count, width),
        jnp.where(lower, grad_0, jnp.concatenate(grad_1)).reshape(1, micro_count, row_count, width),
        qkv_share[None],
        attn_share[None],
        in_share[None],
        mlp_out_share[None],
        gains[:1],
        gains[1:],
    )


def solution(mesh):
    in_specs = (
        P(None, "dp", None),
        P(None, "dp"),
        P(None, "dp", None),
        P("section", "dp", None),
        P("section", "dp", None),
        P("section", "dp", None),
        P("section", "dp", None),
        P("section", "dp"),
        P("section", "dp"),
    )
    out_specs = (
        P("section", None, "dp", None),
        P("section", None, "dp", None),
        P("section", "dp", None),
        P("section", "dp", None),
        P("section", "dp", None),
        P("section", "dp", None),
        P("section", "dp"),
        P("section", "dp"),
    )
    return jax.shard_map(
        on_device, mesh=mesh, in_specs=in_specs, out_specs=out_specs, check_vma=False
    )
```

```python
import functools
import math

import jax
import jax.numpy as jnp
from jax import lax
from jax.experimental import pallas as pl
from jax.experimental.pallas import tpu as pltpu
from jax.sharding import PartitionSpec as P

HEAD_DIM = 64
GROUP = 16
HALF_WIN = 64
EXTRA = 16
LANES = 128
TILE = 256

local_log_base = math.log(10000.0)
global_log_base = math.log(160000.0)
masked_score = -1e30
SCALE = 1.0 / math.sqrt(HEAD_DIM)
BF = jnp.bfloat16
F32 = jnp.float32


def dot(left, right):
    return jnp.dot(left, right, preferred_element_type=F32)


def dot_bt(left, right):
    return lax.dot_general(left, right, (((1,), (1,)), ((), ())), preferred_element_type=F32)


def dot_at(left, right):
    return lax.dot_general(left, right, (((0,), (0,)), ((), ())), preferred_element_type=F32)


def moments(values):
    center = values - jnp.mean(values, -1, keepdims=True)
    scale = lax.rsqrt(jnp.mean(center * center, -1, keepdims=True) + 1e-05)
    return center * scale, scale


def norm_back(grad_out, gain_row, xhat, scale):
    scaled = grad_out * gain_row
    mean_grad = jnp.mean(scaled, -1, keepdims=True)
    mean_dot = jnp.mean(scaled * xhat, -1, keepdims=True)
    return (scaled - mean_grad - xhat * mean_dot) * scale


def angles(positions, log_base):
    half_dim = HEAD_DIM // 2
    fraction = (2 * jnp.arange(half_dim)).astype(F32) / HEAD_DIM
    inverse = jnp.exp(-fraction * log_base)
    table = positions.astype(F32)[:, None] * inverse[None, :]
    cosine, sine = jnp.cos(table), jnp.sin(table)
    none = jnp.zeros_like(sine)
    cosine = jnp.concatenate([cosine, cosine], 1)
    to_first = jnp.concatenate([-sine, none], 1)
    to_second = jnp.concatenate([none, sine], 1)
    return jnp.tile(jnp.stack([cosine, to_first, to_second]), (1, 2, 2))


def on_core(body, outs, args, scratch=(), spaces=None, out_spaces=None):
    return pl.pallas_call(
        body,
        out_shape=[jax.ShapeDtypeStruct(shape, dtype) for shape, dtype in outs],
        in_specs=[
            pl.BlockSpec(memory_space=space) for space in spaces or [pltpu.VMEM] * len(args)
        ],
        out_specs=[
            pl.BlockSpec(memory_space=space) for space in out_spaces or [pltpu.VMEM] * len(outs)
        ],
        scratch_shapes=scratch,
        cost_estimate=pl.CostEstimate(
            flops=2**10, bytes_accessed=2**10, transcendentals=0
        ),
        compiler_params=pltpu.CompilerParams(vmem_limit_bytes=60 * 2**20),
    )(*args)


def low_lanes():
    return lax.broadcasted_iota(jnp.int32, (1, LANES), 1) < HEAD_DIM


def swap(chunk):
    return pltpu.roll(chunk, HEAD_DIM, 1)


def chunks_of(rows):
    return [rows[:, c : c + LANES] for c in range(0, rows.shape[1], LANES)]


def rotate(chunk, tables):
    cosine, to_first, to_second = tables
    quarter = HEAD_DIM // 2
    return (
        chunk * cosine
        + pltpu.roll(chunk, LANES - quarter, 1) * to_first
        + pltpu.roll(chunk, quarter, 1) * to_second
    )


def unrotate(chunk, tables):
    cosine, to_first, to_second = tables
    quarter = HEAD_DIM // 2
    return (
        chunk * cosine
        - pltpu.roll(chunk, LANES - quarter, 1) * to_first
        - pltpu.roll(chunk, quarter, 1) * to_second
    )


def low_and_high(chunks):
    swapped = [swap(chunk) for chunk in chunks]
    low = [(swapped if h % 2 else chunks)[h // 2] for h in range(2 * len(chunks))]
    high = [(chunks if h % 2 else swapped)[h // 2] for h in range(2 * len(chunks))]
    return low, high


def targets():
    for d in range(GROUP):
        micro, chip, half = d // 8, d % 8 // 2, d % 2
        yield d, micro, 3 * chip + 2 * half, 3 * chip + 1, half


def pack_folded(chunks, ref, base):
    low, high = low_and_high(chunks)
    first = low_lanes()
    rows = chunks[0].shape[0] // 2
    half, fold = rows // 2, rows * 3 // 4
    for d, micro, own, shared, side in targets():
        start = micro * rows
        part = start + side * half
        upper = jnp.concatenate(
            [high[own][start + fold : start + rows], high[shared][part : part + half]], 0
        )
        ref[d, base : base + fold] = jnp.where(
            first, low[own][start : start + fold], upper
        ).astype(BF)


def pack_pairs(lefts, rights, ref):
    low, high = low_and_high(lefts)[0], low_and_high(rights)[1]
    first = low_lanes()
    rows = lefts[0].shape[0] // 2
    half = rows // 2
    for d, micro, own, shared, side in targets():
        start = micro * rows
        part = start + side * half
        ref[d, 0:rows] = jnp.where(
            first, low[own][start : start + rows], high[own][start : start + rows]
        ).astype(BF)
        ref[d, rows : rows + half] = jnp.where(
            first, low[shared][part : part + half], high[shared][part : part + half]
        ).astype(BF)


def unpack_folded(ref, base, rows):
    first = low_lanes()
    fold = rows * 3 // 4
    low, high = {}, {}
    shared_parts = {}
    for d, micro, own, shared, side in targets():
        block = ref[d, base : base + fold].astype(F32)
        mine = jnp.concatenate([block, swap(block[: rows - fold])], 0)
        if own % 2:
            high[micro, own] = swap(mine)
        else:
            low[micro, own] = mine
        shared_parts[micro, shared, side] = block[rows - fold :]
        if side:
            both = jnp.concatenate([shared_parts[micro, shared, 0], block[rows - fold :]], 0)
            if shared % 2:
                high[micro, shared] = both
            else:
                low[micro, shared] = swap(both)
    heads = GROUP // 4 * 3
    return [
        jnp.concatenate(
            [jnp.where(first, low[m, h], high[m, h + 1]) for m in range(2)], 0
        )
        for h in range(0, heads, 2)
    ]


def unpack_pairs(ref, rows):
    first = low_lanes()
    half = rows // 2
    pairs = {}
    parts = {}
    for d, micro, own, shared, side in targets():
        pairs[micro, own] = ref[d, 0:rows].astype(F32)
        parts[side] = ref[d, rows : rows + half].astype(F32)
        if side:
            pairs[micro, shared] = jnp.concatenate([parts[0], parts[1]], 0)
    heads = GROUP // 4 * 3
    lefts, rights = [], []
    for h in range(0, heads, 2):
        even, odd = [pairs[m, h] for m in range(2)], [pairs[m, h + 1] for m in range(2)]
        lefts.append(
            jnp.concatenate([jnp.where(first, a, swap(b)) for a, b in zip(even, odd)], 0)
        )
        rights.append(
            jnp.concatenate([jnp.where(first, swap(a), b) for a, b in zip(even, odd)], 0)
        )
    return lefts, rights


class Weights:
    def __init__(self, sources, mlp_out):
        self.sources = sources
        self.mlp_out = sources[-1]
        if len(sources) == 1:
            self.mlp_out = mlp_out
            unpack_rows(sources[0], mlp_out)

    def get(self, which):
        if which == 2:
            return self.mlp_out[...]
        if len(self.sources) > 1:
            return self.sources[which][...]
        (wide,) = self.sources
        width = wide.shape[0]
        inner = 2 * self.mlp_out.shape[0]
        return wide[:, width : width + inner] if which else wide[:, :width]


def first_block(pair):
    return -(-pair // 32) * 16


def packed_pieces(shard, rows, width):
    yield 0, shard, 0, width, 0, 0
    rest = rows - shard
    side = width // 3
    yield 0, rest, width, 2 * side, shard, 0
    yield rest, 16, width, side, shard, 2 * side
    yield rest, 16, width + side, side, shard + 16, 2 * side


def unpack_rows(wide, mlp_out):
    hidden, width = mlp_out.shape
    shard = wide.shape[0] // GROUP
    start = wide.shape[1] - width - 2 * (width // 3)
    pair = 2 * hidden // GROUP
    upper = first_block(pair)
    for d in range(GROUP):
        low = d // 2 * pair + d % 2 * upper
        have = pair - upper if d % 2 else upper
        for row, rows, column, columns, to_row, to_column in packed_pieces(shard, upper, width):
            rows = min(rows, have - to_row)
            if rows > 0:
                mlp_out[low + to_row : low + to_row + rows, to_column : to_column + columns] = wide[
                    d * shard + row : d * shard + row + rows, start + column : start + column + columns
                ]


def stack_body(odd_ref, attn_ref, mlp_in_ref, own_ref, beside_ref, out_ref):
    shard, width = attn_ref.shape
    inner = mlp_in_ref.shape[1]
    out_ref[:, :width] = attn_ref[...]
    out_ref[:, width : width + inner] = mlp_in_ref[...]
    own, beside = own_ref[...].astype(F32), beside_ref[...].astype(F32)
    moved = beside.shape[0]
    even = jnp.concatenate([own, beside], 0)
    odd = jnp.concatenate([own[moved:], beside, beside], 0)
    block = jnp.where(odd_ref[0] == 1, odd, even).astype(BF)
    start = width + inner
    for row, rows, column, columns, from_row, from_column in packed_pieces(
        shard, block.shape[0], width
    ):
        out_ref[row : row + rows, start + column : start + column + columns] = block[
            from_row : from_row + rows, from_column : from_column + columns
        ]


def mlp_forward(layer_in, attended, gain, weights):
    middle = layer_in + dot(attended, weights.get(0))
    xhat, _ = moments(middle)
    normed = (xhat * gain).astype(BF)
    gate_up = dot(normed, weights.get(1))
    half = gate_up.shape[1] // 2
    gate, up = gate_up[:, :half], gate_up[:, half:]
    cdf = 0.5 * (1.0 + lax.erf(gate * math.sqrt(0.5)))
    mixed = (gate * cdf * up).astype(BF)
    result = (middle + dot(mixed, weights.get(2))).astype(BF)
    return middle, normed, gate, up, mixed, result


def mlp_backward(upstream, middle, gate, up, gain, weights):
    d_mixed = dot_bt(upstream, weights.get(2))
    cdf = 0.5 * (1.0 + lax.erf(gate * math.sqrt(0.5)))
    density = jnp.exp(-0.5 * gate * gate) * (1.0 / math.sqrt(2.0 * math.pi))
    d_gate = d_mixed * up * (cdf + gate * density)
    d_up = d_mixed * gate * cdf
    d_gate_up = jnp.concatenate([d_gate.astype(BF), d_up.astype(BF)], 1)
    d_normed = dot_bt(d_gate_up, weights.get(1))
    xhat, scale = moments(middle)
    gain_grad = jnp.sum(d_normed * xhat, 0, keepdims=True)
    d_middle = upstream.astype(F32) + norm_back(d_normed, gain, xhat, scale)
    d_attn = d_middle.astype(BF)
    d_attended = dot_bt(d_attn, weights.get(0))
    return d_gate_up, gain_grad, d_middle, d_attn, d_attended


def project(xhat, gain, first_ref, table_ref, normed_ref):
    width = xhat.shape[1]
    normed = (xhat * gain).astype(BF)
    normed_ref[...] = normed
    tables = [table_ref[i] for i in range(3)]
    results = [dot(normed, first_ref[:, c * width : (c + 1) * width]) for c in range(3)]
    queries, keys, values = chunks_of(results[0]), chunks_of(results[1]), results[2]
    return [rotate(c, tables) for c in queries], [rotate(c, tables) for c in keys], values


def input_backward(d_middle, d_projected, x, gain_ref, first_ref, gain_out_ref):
    d_normed = dot_bt(d_projected, first_ref[:, : d_projected.shape[1]])
    xhat, scale = moments(x)
    gain_out_ref[...] = jnp.sum(d_normed * xhat, 0, keepdims=True)
    return (d_middle + norm_back(d_normed, gain_ref[...], xhat, scale)).astype(BF)


def joined(refs):
    return jnp.concatenate([ref[...] for ref in refs], 0)


def store_right(right_ref, d_gate_up, d_attn, d_mlp):
    inner, width = d_gate_up.shape[1], d_attn.shape[1]
    right_ref[:, :inner] = d_gate_up
    right_ref[:, inner : inner + width] = d_attn
    right_ref[:, inner + width :] = d_mlp


def store_chunks(refs, rows):
    size = rows.shape[0] // len(refs)
    for i, ref in enumerate(refs):
        ref[...] = rows[i * size : (i + 1) * size]


def message_body(w_ref, attn_ref, mlp_ref, ids_ref, out_ref, rows_scr, ids_scr):
    shard, columns = w_ref.shape
    micro_count, row_count = ids_ref.shape
    out_ref[:, :columns] = w_ref[...]
    rows_scr[...] = jnp.zeros_like(rows_scr)
    ids_scr[...] = jnp.zeros_like(ids_scr)
    rows_scr[0:1, :shard] = attn_ref[...].astype(F32)
    rows_scr[1:2, :shard] = mlp_ref[...].astype(F32)
    ids_scr[:micro_count, :row_count] = ids_ref[...].astype(F32)
    runs = -(-row_count // shard)
    for run in range(runs):
        turned = ids_scr[...]
        if run:
            turned = pltpu.roll(turned, LANES - run * shard, 1)
        for micro in range(micro_count):
            row = 2 + micro * runs + run
            rows_scr[row : row + 1] = turned[micro : micro + 1]
    out_ref[:, columns:] = rows_scr[...].T[:shard].astype(BF)


def local_project_body(first_ref, x_ref, table_ref, extra_ref, normed_ref, q_ref, kv_ref):
    xhat, _ = moments(x_ref[...].astype(F32))
    extra = first_ref[:, first_ref.shape[1] - LANES :].astype(F32).T
    extra_ref[...] = extra[: extra_ref.shape[0]]
    queries, keys, values = project(xhat, extra[:1], first_ref, table_ref, normed_ref)
    width = values.shape[1]
    for j, (q, k) in enumerate(zip(queries, keys)):
        q_ref[:, LANES * j : LANES * (j + 1)] = q.astype(BF)
        kv_ref[:, LANES * j : LANES * (j + 1)] = k.astype(BF)
    kv_ref[:, width:] = values.astype(BF)


def two_heads(chunk):
    first = low_lanes()
    wide = chunk.astype(F32)
    return jnp.concatenate([jnp.where(first, wide, 0.0), jnp.where(first, 0.0, wide)], 0)


def pick_heads(rows):
    half = rows.shape[0] // 2
    return jnp.where(low_lanes(), rows[:half], rows[half:])


def local_parts(q_ref, before_ref, own_ref, after_ref):
    rows = q_ref.shape[0] // 2
    width = q_ref.shape[1]
    for micro in range(2):
        for j in range(width // LANES):
            here = slice(micro * rows, (micro + 1) * rows)
            lanes = slice(LANES * j, LANES * (j + 1))
            more = slice(width + LANES * j, width + LANES * (j + 1))
            keys, values = (
                jnp.concatenate([ref[here, part] for ref in (before_ref, own_ref, after_ref)], 0)
                for part in (lanes, more)
            )
            queries = (two_heads(q_ref[here, lanes]) * SCALE).astype(BF)
            yield micro * (width // LANES) + j, micro, here, lanes, more, queries, keys, values


def local_forward_body(q_ref, before_ref, own_ref, after_ref, bias_ref, att_ref, total_ref):
    parts = local_parts(q_ref, before_ref, own_ref, after_ref)
    for index, micro, here, lanes, _, queries, keys, values in parts:
        scores = dot_bt(keys, queries) + bias_ref[micro]
        peak = jnp.max(scores, 0, keepdims=True)
        weights = jnp.exp(scores - peak)
        total = jnp.sum(weights, 0, keepdims=True)
        total_ref[index] = peak + jnp.log(total)
        probs = (weights * (1.0 / total)).astype(BF)
        att_ref[here, lanes] = pick_heads(dot_at(probs, values)).astype(BF)


def local_backward_body(
    q_ref, before_ref, own_ref, after_ref, bias_ref, total_ref, d_ref, table_ref,
    dq_ref, d_own_ref, d_before_ref, d_after_ref,
):
    tables = [table_ref[i] for i in range(3)]
    parts = local_parts(q_ref, before_ref, own_ref, after_ref)
    rows = q_ref.shape[0] // 2
    for index, micro, here, lanes, more, queries, keys, values in parts:
        d_out = two_heads(d_ref[here, lanes]).astype(BF)
        probs = jnp.exp(dot_bt(keys, queries) + bias_ref[micro] - total_ref[index])
        d_probs = dot_bt(values, d_out)
        product = probs * d_probs
        delta = jnp.sum(product, 0, keepdims=True)
        d_scores = (product - probs * delta).astype(BF)
        d_queries = pick_heads(dot_at(d_scores, keys)) * SCALE
        local_tables = [table[here] for table in tables]
        dq_ref[here, lanes] = unrotate(d_queries, local_tables).astype(BF)
        for part, grads in ((lanes, dot(d_scores, queries)), (more, dot(probs.astype(BF), d_out))):
            d_before_ref[here, part] = grads[:rows].astype(BF)
            d_own_ref[here, part] = grads[rows : 2 * rows]
            d_after_ref[here, part] = grads[2 * rows :].astype(BF)


def local_finish_body(
    lower_ref, first_ref, dq_ref, own_ref, low_ref, high_ref, table_ref, d_middle_ref, x_ref, gain_ref,
    gain_mlp_ref, other_ref, other_attn_ref, other_mlp_ref, out_ref, grad_ref, gain_attn_ref, gain_scr,
):
    rows, width = dq_ref.shape

    @pl.when(lower_ref[0] == 1)
    def _():
        tables = [table_ref[i] for i in range(3)]
        total = own_ref[...] + low_ref[...].astype(F32) + high_ref[...].astype(F32)
        out_ref[:rows, :width] = dq_ref[...]
        for j, chunk in enumerate(chunks_of(total[:, :width])):
            start = width + LANES * j
            out_ref[:rows, start : start + LANES] = unrotate(chunk, tables).astype(BF)
        out_ref[:rows, 2 * width :] = total[:, width:].astype(BF)
        grad_ref[...] = input_backward(
            d_middle_ref[...], out_ref[:rows], x_ref[...].astype(F32), gain_ref, first_ref, gain_scr
        )

    @pl.when(lower_ref[0] == 0)
    def _():
        out_ref[:rows] = other_ref[...]
        grad_ref[...] = jnp.zeros_like(grad_ref)
        gain_scr[...] = other_attn_ref[...]

    gain_attn_ref[...] = gain_scr[...]
    gain_mlp = jnp.where(lower_ref[0] == 1, gain_mlp_ref[...], other_mlp_ref[...])
    index = lax.broadcasted_iota(jnp.int32, (EXTRA, width), 0)
    tail = jnp.zeros((EXTRA, width), F32)
    for row, gain in ((0, gain_scr[...]), (2, gain_mlp)):
        high = gain.astype(BF).astype(F32)
        tail = jnp.where(index == row, high, tail)
        tail = jnp.where(index == row + 1, gain - high, tail)
    out_ref[rows:] = jnp.zeros((EXTRA, out_ref.shape[1]), BF)
    out_ref[rows:, :width] = tail.astype(BF)


def local_middle_body(*refs):
    sources, refs = refs[:-10], refs[-10:]
    x_ref, att_ref, gain_ref, normed_ref, mixed_ref, middle_ref, gate_up_ref = refs[:7]
    weights = Weights(sources, refs[9])
    middle, normed, gate, up, mixed, result = mlp_forward(
        x_ref[...].astype(F32), att_ref[...], gain_ref[...], weights
    )
    store_chunks(refs[7:9], result)
    normed_ref[...] = normed
    mixed_ref[...] = mixed
    middle_ref[...] = middle
    half = gate.shape[1]
    gate_up_ref[:, :half] = gate
    gate_up_ref[:, half:] = up


def local_back_middle_body(*refs):
    sources, refs = refs[:-12], refs[-12:]
    lower_ref, low_ref, high_ref, middle_ref, gate_up_ref, gain_ref, other_ref = refs[:7]
    gain_out_ref, d_middle_ref, d_att_ref, right_ref = refs[7:11]
    weights = Weights(sources, refs[11])
    half = gate_up_ref.shape[1] // 2
    upstream = joined([low_ref, high_ref])
    d_gate_up, gain_grad, d_middle, d_attn, d_attended = mlp_backward(
        upstream, middle_ref[...], gate_up_ref[:, :half], gate_up_ref[:, half:],
        gain_ref[...], weights,
    )
    gain_out_ref[...] = gain_grad
    d_middle_ref[...] = d_middle
    d_att_ref[...] = d_attended.astype(BF)

    @pl.when(lower_ref[0] == 1)
    def _():
        store_right(right_ref, d_gate_up, d_attn, upstream)

    @pl.when(lower_ref[0] == 0)
    def _():
        right_ref[...] = other_ref[...]


def global_project_body(first_ref, low_ref, high_ref, gain_ref, table_ref, normed_ref, sent_ref):
    xhat, _ = moments(joined([low_ref, high_ref]).astype(F32))
    queries, keys, values = project(xhat, gain_ref[...], first_ref, table_ref, normed_ref)
    pack_pairs(queries, keys, sent_ref)
    pack_folded(chunks_of(values), sent_ref, sent_ref.shape[1] * 2 // 3)


def flat(blocks):
    return blocks.reshape(-1, LANES)


def own_unfolded(ref, base, rows):
    fold = rows * 3 // 4
    block = ref[:, base : base + fold].astype(F32)
    rest = swap(flat(block[:, : rows - fold])).reshape(GROUP, rows - fold, LANES)
    return flat(jnp.concatenate([block, rest], 1))


def shared_unfolded(ref, start, rows):
    return swap(flat(ref[:, start : start + rows // 2].astype(F32)))


def fill_heads(got_ref, other_ref, own_seg_ref, shared_seg_ref, q_scr, k_scr, v_scr):
    rows = got_ref.shape[1] * 4 // 9
    half = rows // 2
    first = low_lanes()
    lane = lax.broadcasted_iota(jnp.int32, (1, LANES), 1) - HEAD_DIM
    own = flat(got_ref[:, 0:rows].astype(F32))
    shared = flat(got_ref[:, rows : rows + half].astype(F32))
    other = flat(other_ref[:, 0:half].astype(F32))
    count = own.shape[0]
    own_hit = lane == own_seg_ref[...]
    shared_hit = lane == shared_seg_ref[...]
    both = jnp.concatenate([shared, other], 0)
    for start, pairs, hit in (
        (0, own, own_hit),
        (count, shared, shared_hit[: count // 2]),
    ):
        marked = jnp.where(hit, 1.0, 0.0)
        q_scr[start : start + pairs.shape[0]] = jnp.where(first, pairs * SCALE, marked).astype(BF)
    for unit, pairs, hit in ((0, own, own_hit), (1, both, shared_hit)):
        marked = jnp.where(hit, 0.0, masked_score)
        k_scr[unit] = jnp.where(first, swap(pairs), marked).astype(BF)
    base = rows + half
    v_scr[0] = jnp.where(first, own_unfolded(got_ref, base, rows), 0.0).astype(BF)
    start = base + rows - rows * 3 // 4
    shared_v = jnp.concatenate(
        [shared_unfolded(got_ref, start, rows), shared_unfolded(other_ref, half, rows)], 0
    )
    v_scr[1] = jnp.where(first, shared_v, 0.0).astype(BF)


def fold_out(own, shared, rows, ref, base):
    fold = rows * 3 // 4
    blocks = own.reshape(GROUP, rows, LANES)
    swapped = swap(own).reshape(GROUP, rows, LANES)
    upper = jnp.concatenate(
        [swapped[:, fold:], swap(shared).reshape(GROUP, rows // 2, LANES)], 1
    )
    ref[:, base : base + fold] = jnp.where(low_lanes(), blocks[:, :fold], upper).astype(BF)


def global_forward_body(
    got_ref, other_ref, own_seg_ref, shared_seg_ref, out_ref, total_ref,
    q_scr, k_scr, v_scr, vt_scr, o_scr,
):
    fill_heads(got_ref, other_ref, own_seg_ref, shared_seg_ref, q_scr, k_scr, v_scr)
    for unit in range(2):
        vt_scr[unit] = v_scr[unit].astype(F32).T.astype(BF)
    count = k_scr.shape[1]

    def step(tile, carry):
        unit = tile // (count // TILE)
        rows = pl.ds(pl.multiple_of(tile * TILE, TILE), TILE)
        scores = dot_bt(k_scr[unit], q_scr[rows])
        peak = jnp.max(scores, 0, keepdims=True)
        weights = jnp.exp(scores - peak)
        total = jnp.sum(weights, 0, keepdims=True)
        total_ref[tile] = peak + jnp.log(total)
        out = dot(vt_scr[unit], weights.astype(BF)) * (1.0 / total)
        o_scr[rows] = out.T
        return carry

    lax.fori_loop(0, q_scr.shape[0] // TILE, step, 0)
    rows = got_ref.shape[1] * 4 // 9
    fold_out(o_scr[:count], o_scr[count:], rows, out_ref, 0)


def global_backward_body(
    got_ref, other_ref, own_seg_ref, shared_seg_ref, total_ref, d_ref, sent_ref, to_other_ref,
    q_scr, k_scr, v_scr, kt_scr, d_scr, dq_scr, dk_scr, dv_scr,
):
    fill_heads(got_ref, other_ref, own_seg_ref, shared_seg_ref, q_scr, k_scr, v_scr)
    first = low_lanes()
    rows = got_ref.shape[1] * 4 // 9
    half = rows // 2
    for unit in range(2):
        keys = jnp.where(first, k_scr[unit].astype(F32), 0.0)
        kt_scr[unit] = keys.T.astype(BF)
    count = k_scr.shape[1]
    d_scr[:count] = jnp.where(first, own_unfolded(d_ref, 0, rows), 0.0).astype(BF)
    d_scr[count:] = jnp.where(
        first, shared_unfolded(d_ref, rows - rows * 3 // 4, rows), 0.0
    ).astype(BF)
    dk_scr[...] = jnp.zeros_like(dk_scr)
    dv_scr[...] = jnp.zeros_like(dv_scr)

    def step(tile, carry):
        unit = tile // (count // TILE)
        here = pl.ds(pl.multiple_of(tile * TILE, TILE), TILE)
        queries, d_out = q_scr[here], d_scr[here]
        probs = jnp.exp(dot_bt(k_scr[unit], queries) - total_ref[tile])
        d_probs = dot_bt(v_scr[unit], d_out)
        product = probs * d_probs
        delta = jnp.sum(product, 0, keepdims=True)
        d_scores = (product - probs * delta).astype(BF)
        dv_scr[unit] += dot(probs.astype(BF), d_out)
        dk_scr[unit] += dot(d_scores, queries)
        dq_scr[here] = dot(kt_scr[unit], d_scores).T * SCALE
        return carry

    lax.fori_loop(0, q_scr.shape[0] // TILE, step, 0)
    mine = count // 2
    own = jnp.where(first, dq_scr[:count], swap(dk_scr[0]))
    sent_ref[:, 0:rows] = own.reshape(GROUP, rows, LANES).astype(BF)
    shared_k, shared_v = dk_scr[1], dv_scr[1]
    shared = jnp.where(first, dq_scr[count:], swap(shared_k[:mine]))
    sent_ref[:, rows : rows + half] = shared.reshape(GROUP, half, LANES).astype(BF)
    fold_out(dv_scr[0], shared_v[:mine], rows, sent_ref, rows + half)
    for place, grads in enumerate((shared_k, shared_v)):
        other = jnp.where(first, 0.0, swap(grads[mine:])).reshape(GROUP, half, LANES)
        to_other_ref[:, place * half : (place + 1) * half] = other.astype(BF)


def global_middle_body(*refs):
    sources, refs = refs[:-14], refs[-14:]
    got_ref, low_ref, high_ref, up_ref, gain_ref, out_ref, att_ref, normed_ref, mixed_ref = refs[:9]
    right_ref, gain_out_ref, d_middle_ref, sent_ref = refs[9:13]
    weights = Weights(sources, refs[13])
    rows = low_ref.shape[0]
    attended = jnp.concatenate([c.astype(BF) for c in unpack_folded(got_ref, 0, rows)], 1)
    att_ref[...] = attended
    gain = gain_ref[...]
    middle, normed, gate, up, mixed, result = mlp_forward(
        joined([low_ref, high_ref]).astype(F32), attended, gain, weights
    )
    out_ref[...] = result
    normed_ref[...] = normed
    mixed_ref[...] = mixed
    d_gate_up, gain_grad, d_middle, d_attn, d_attended = mlp_backward(
        up_ref[...], middle, gate, up, gain, weights
    )
    store_right(right_ref, d_gate_up, d_attn, up_ref[...])
    gain_out_ref[...] = gain_grad
    d_middle_ref[...] = d_middle
    pack_folded(chunks_of(d_attended), sent_ref, 0)


def global_finish_body(
    first_ref, got_ref, d_middle_ref, low_ref, high_ref, gain_ref, table_ref,
    d_proj_ref, gain_out_ref, *grad_refs,
):
    tables = [table_ref[i] for i in range(3)]
    x = joined([low_ref, high_ref]).astype(F32)
    rows = low_ref.shape[0]
    d_queries, d_keys = unpack_pairs(got_ref, rows)
    d_values = unpack_folded(got_ref, rows * 3 // 2, rows)
    parts = [unrotate(c, tables).astype(BF) for c in d_queries + d_keys]
    d_projected = jnp.concatenate(parts + [c.astype(BF) for c in d_values], 1)
    d_proj_ref[...] = d_projected
    store_chunks(
        grad_refs,
        input_backward(d_middle_ref[...], d_projected, x, gain_ref, first_ref, gain_out_ref),
    )


def neighbours(count, step):
    return [
        (i, i + step)
        for i in range(count)
        if 0 <= i + step < count and i // GROUP == (i + step) // GROUP
    ]


def exchange(blocks, count):
    groups = [list(range(s, s + GROUP)) for s in range(0, count, GROUP)]
    return lax.all_to_all(blocks, "dp", 0, 0, axis_index_groups=groups)


def to_other_section(chunks, step):
    pairs = [(0, 1)] if step > 0 else [(1, 0)]
    return [lax.ppermute(rows, "section", pairs) for rows in chunks]


def partner(rows, apart, count):
    return lax.ppermute(rows, "dp", [(i, i ^ apart) for i in range(count)])


def gather_rows(piece, group_pos, count):
    pieces = {0: piece}
    for apart in (4, 8, 12):
        pieces[apart] = partner(piece, apart, count)
    for apart in (0, 4, 8, 12):
        pieces[apart + 2] = partner(pieces[apart], 2, count)
    for apart in range(0, GROUP, 2):
        pieces[apart + 1] = partner(pieces[apart], 1, count)
    whole = jnp.zeros((GROUP,) + piece.shape, piece.dtype)
    for apart, item in pieces.items():
        start = (group_pos ^ apart,) + (0,) * piece.ndim
        whole = lax.dynamic_update_slice(whole, item[None], start)
    if count > GROUP:
        groups = [list(range(s, count, GROUP)) for s in range(GROUP)]
        whole = lax.all_gather(whole, "dp", axis=0, tiled=True, axis_index_groups=groups)
    return whole.reshape(-1, piece.shape[-1]), pieces[2]


def plane_rows(rows, group_pos, count):
    parts = rows.reshape(count // GROUP, 4, 4, *rows.shape[1:])
    place, plane = group_pos % 4, group_pos // 4
    taken = []
    for apart in range(4):
        block = lax.dynamic_index_in_dim(parts, place ^ apart, 2, keepdims=False)
        block = jnp.stack(
            [lax.dynamic_index_in_dim(block, plane ^ z, 1, keepdims=False) for z in range(4)]
        )
        taken.append(partner(block, apart, count) if apart else block)
    return taken


def left_body(lower_ref, place_ref, *refs):
    refs, out_ref = refs[:-1], refs[-1]
    base = 0
    for first_ref, second_ref in zip(refs[0::2], refs[1::2]):
        rows = jnp.where(lower_ref[0] == 1, first_ref[...].astype(F32), second_ref[...].astype(F32))
        turned = rows.T
        size = turned.shape[0] // GROUP
        for d in range(GROUP):
            side = d % 4 ^ place_ref[0] % 4
            plane = d // 4 ^ place_ref[0] // 4
            out_ref[side, plane, base : base + size] = turned[d * size : (d + 1) * size].astype(BF)
        base += size


def early_body(shard, *refs):
    refs, outs = refs[:-4], refs[-4:]
    rights, n2, mixed, att = (refs[4 * i : 4 * i + 4] for i in range(4))
    width = outs[0].shape[1]
    inner = rights[0].shape[1] - 2 * width

    def product(lefts, start, end):
        left = jnp.concatenate([ref[...] for ref in lefts], 1)
        return dot(left, jnp.concatenate([ref[:, start:end] for ref in rights], 0))

    base = 0
    for lefts, start, end in (
        (n2, 0, inner),
        (mixed, inner + width, inner + 2 * width),
        (att, inner, inner + width),
    ):
        result = product(lefts, start, end)
        rows = result.shape[0] // 4
        for column in range(0, end - start, width):
            for plane, out_ref in enumerate(outs):
                part = result[plane * rows : (plane + 1) * rows, column : column + width]
                out_ref[base : base + rows] = part.astype(out_ref.dtype)
            base += rows


def late_body(place_ref, *refs):
    refs, (outs, scr) = refs[:-5], (refs[-5:-1], refs[-1])
    rights, lefts = refs[:4], refs[4:]
    tokens = lefts[0].shape[1]
    columns = rights[0].shape[1]
    width = columns // 3
    rows = outs[0].shape[0]
    left = jnp.concatenate([ref[...] for ref in lefts], 1)
    product = dot(left, jnp.concatenate([ref[:tokens] for ref in rights], 0))
    tail = sum(ref[tokens:, :width].astype(F32) for ref in rights)
    both = jnp.concatenate([tail, jnp.zeros((LANES - EXTRA, width), F32)], 0).T
    lane = lax.broadcasted_iota(jnp.int32, (1, LANES), 1)
    lows = pltpu.roll(both, LANES - 1, 1)
    scr[...] = jnp.where(lane % 2 == 0, both + lows, 0.0)
    for plane, out_ref in enumerate(outs):
        part = product[plane * rows : (plane + 1) * rows]
        out_ref[:, :columns] = part.astype(out_ref.dtype)
        d = (place_ref[0] // 4 ^ plane) * 4 + place_ref[0] % 4
        start = pl.multiple_of(d * rows, 16)
        out_ref[:, columns:] = scr[pl.ds(start, rows)].astype(out_ref.dtype)


def flat_rows(parts):
    return [part.reshape(-1, part.shape[-1]) for part in parts]


def four_planes(shape):
    return [(shape, F32)] + [(shape, BF)] * 3


def plane_parts(rows, count, after=None):
    across = partner(rows, 2, count)
    beside = partner(rows, 1, count)
    if after is not None:
        across, _ = lax.optimization_barrier((across, after))
    return [rows, beside, across, partner(across, 1, count)]


def sent_planes(blocks, count):
    return [blocks[0]] + [partner(item, 4 * (z + 1), count) for z, item in enumerate(blocks[1:])]


def sum_planes(blocks):
    total = blocks[0]
    for item in blocks[1:]:
        total = total + item.astype(F32)
    return total


def over_groups(rows, count):
    if count == GROUP:
        return rows
    apart = [list(range(s, count, GROUP)) for s in range(GROUP)]
    rows = rows.reshape(count // GROUP, -1, rows.shape[1])
    return lax.psum_scatter(rows, "dp", scatter_dimension=0, axis_index_groups=apart)


def on_device(
    tokens_in,
    segment_ids,
    out_grad,
    qkv_weight,
    attn_out_weight,
    mlp_in_weight,
    mlp_out_weight,
    attn_gain,
    mlp_gain,
):
    lower = lax.axis_index("section") == 0
    lower_flag = lower.astype(jnp.int32)[None]
    shard_total = qkv_weight.shape[1] * (lax.axis_size("dp") // GROUP)
    hidden_total = mlp_out_weight.shape[1] * (lax.axis_size("dp") // GROUP)
    count = lax.axis_size("dp")
    replica = lax.axis_index("dp")
    group_pos = replica % GROUP
    micro_count, row_count, width = tokens_in.shape
    shard = qkv_weight.shape[1]
    runs = -(-row_count // shard)
    (message,) = on_core(
        message_body,
        [((shard, 3 * width + LANES), BF)],
        (qkv_weight[0], attn_gain, mlp_gain, segment_ids),
        [pltpu.VMEM((LANES, LANES), F32), pltpu.VMEM((8, LANES), F32)],
    )
    first, early_piece = gather_rows(message, group_pos, count)
    inner = mlp_in_weight.shape[2]
    hidden = mlp_out_weight.shape[1] * count
    if count == GROUP:
        moved = first_block(2 * mlp_out_weight.shape[1]) - mlp_out_weight.shape[1]
        beside = partner(mlp_out_weight[0, :moved], 1, count)
        (stacked,) = on_core(
            stack_body,
            [((shard, width + inner + width + 2 * (width // 3)), BF)],
            (
                (replica % 2)[None],
                attn_out_weight[0],
                mlp_in_weight[0],
                mlp_out_weight[0],
                beside,
            ),
            (),
            [pltpu.SMEM] + [pltpu.VMEM] * 4,
        )
        stacked, _ = lax.optimization_barrier((stacked, early_piece))
        others = [lax.all_gather(stacked, "dp", axis=0, tiled=True)]
    else:
        others = [
            lax.all_gather(item[0], "dp", axis=0, tiled=True)
            for item in (attn_out_weight, mlp_in_weight, mlp_out_weight)
        ]
    positions = group_pos * row_count + jnp.arange(row_count)
    local_tables = angles(positions, local_log_base)
    global_tables = angles(positions, global_log_base)

    rows = micro_count * row_count
    pairs = rows * width // (row_count * LANES)
    in_0 = tokens_in.reshape(rows, width)
    extra_rows = -(-(2 + micro_count * runs) // 8) * 8
    extra, normed_0, q_0, kv_0 = on_core(
        local_project_body,
        [
            ((extra_rows, width), F32),
            ((rows, width), BF),
            ((rows, width), BF),
            ((rows, 2 * width), BF),
        ],
        (first, in_0, local_tables),
    )
    gain_attn, gain_mlp = extra[:1], extra[1:2]
    all_ids = extra[2 : 2 + micro_count * runs].reshape(micro_count, runs, count, shard)
    all_ids = lax.dynamic_slice_in_dim(all_ids, replica - group_pos, GROUP, 2)
    all_ids = all_ids.swapaxes(1, 2).reshape(micro_count, GROUP, runs * shard)[..., :row_count]
    segments = all_ids.reshape(micro_count, GROUP * row_count).astype(jnp.int32)

    key_pos = positions[0] - row_count + jnp.arange(3 * row_count)
    around = jnp.pad(segments, ((0, 0), (row_count, row_count)), constant_values=-1)
    key_seg = lax.dynamic_slice_in_dim(around, group_pos * row_count, 3 * row_count, 1)
    visible = (key_seg[:, :, None] == segment_ids[:, None, :]) & (
        jnp.abs(positions[None, :] - key_pos[:, None]) <= HALF_WIN
    )[None]
    bias = jnp.tile(jnp.where(visible, 0.0, masked_score), (1, 1, 2))

    own_seg = lax.dynamic_index_in_dim(segments, group_pos // 8, 0, keepdims=False)
    halves = own_seg.reshape(GROUP, 2, row_count // 2)
    mine = lax.dynamic_index_in_dim(halves, group_pos % 2, 1, keepdims=False).reshape(-1)
    theirs = lax.dynamic_index_in_dim(halves, 1 - group_pos % 2, 1, keepdims=False).reshape(-1)
    shared_seg = jnp.concatenate([mine, theirs])[:, None]
    own_seg = own_seg[:, None]

    up_pairs, down_pairs = neighbours(count, 1), neighbours(count, -1)
    around_0 = (
        lax.ppermute(kv_0, "dp", up_pairs),
        kv_0,
        lax.ppermute(kv_0, "dp", down_pairs),
    )
    att_0, total_0 = on_core(
        local_forward_body,
        [((rows, width), BF), ((pairs, 1, LANES), F32)],
        (q_0, *around_0, bias),
    )
    n2_0, mixed_0, middle_0, gate_up_0, *out_0 = on_core(
        local_middle_body,
        [
            ((rows, width), BF),
            ((rows, hidden), BF),
            ((rows, width), F32),
            ((rows, inner), F32),
        ]
        + [((row_count, width), BF)] * micro_count,
        (*others, in_0, att_0, gain_mlp),
        [pltpu.VMEM((hidden, width), BF)],
    )

    in_1 = to_other_section(out_0, 1)
    fold = row_count * 3 // 4
    half = row_count // 2
    normed_1, sent = on_core(
        global_project_body,
        [((rows, width), BF), ((GROUP, 3 * fold, LANES), BF)],
        (first, *in_1, gain_attn, global_tables),
    )
    got = exchange(sent, count)
    beside = jnp.concatenate(
        [got[:, row_count : row_count + half], got[:, 3 * fold - half :]], 1
    )
    beside = partner(beside, 1, count)
    keys = GROUP * row_count
    tiles = keys * 3 // 2 // TILE
    head_scratch = [
        pltpu.VMEM((keys * 3 // 2, LANES), BF),
        pltpu.VMEM((2, keys, LANES), BF),
        pltpu.VMEM((2, keys, LANES), BF),
        pltpu.VMEM((2, LANES, keys), BF),
    ]
    folded, total_1 = on_core(
        global_forward_body,
        [((GROUP, fold, LANES), BF), ((tiles, 1, TILE), F32)],
        (got, beside, own_seg, shared_seg),
        head_scratch + [pltpu.VMEM((keys * 3 // 2, LANES), F32)],
    )
    folded = exchange(folded, count)

    up_1 = out_grad.reshape(rows, width)
    out_1, att_1, n2_1, mixed_1, right_1, gain_mlp_1, d_mid_1, sent = on_core(
        global_middle_body,
        [
            ((rows, width), BF),
            ((rows, width), BF),
            ((rows, width), BF),
            ((rows, hidden), BF),
            ((rows, inner + 2 * width), BF),
            ((1, width), F32),
            ((rows, width), F32),
            ((GROUP, fold, LANES), BF),
        ],
        (*others, folded, *in_1, up_1, gain_mlp),
        [pltpu.VMEM((hidden, width), BF)],
    )
    d_folded = exchange(sent, count)
    sent, to_beside = on_core(
        global_backward_body,
        [((GROUP, 3 * fold, LANES), BF), ((GROUP, 2 * half, LANES), BF)],
        (got, beside, own_seg, shared_seg, total_1, d_folded),
        head_scratch
        + [
            pltpu.VMEM((keys * 3 // 2, LANES), BF),
            pltpu.VMEM((keys * 3 // 2, LANES), F32),
            pltpu.VMEM((2, keys, LANES), F32),
            pltpu.VMEM((2, keys, LANES), F32),
        ],
    )
    pairs = ((normed_0, normed_1), (att_0, att_1), (n2_0, n2_1), (mixed_0, mixed_1))
    left_rows = 3 * shard + mlp_out_weight.shape[1]
    if count == GROUP:
        (left,) = on_core(
            left_body,
            [((4, 4, left_rows, rows), BF)],
            (lower_flag, group_pos[None], *(item for pair in pairs for item in pair)),
            (),
            [pltpu.SMEM] * 2 + [pltpu.VMEM] * 8,
        )
        left, sent = lax.optimization_barrier((left, sent))
        left = [left[0]] + [partner(left[apart], apart, count) for apart in range(1, 4)]
        left = [item[:, None] for item in left]
    else:
        left = [jnp.where(lower, a, b).T.reshape(count, -1, rows) for a, b in pairs]
        left = plane_rows(jnp.concatenate(left, 1), group_pos, count)
    back = partner(to_beside, 1, count)
    gap = 3 * fold - half - row_count - half
    back = jnp.concatenate(
        [
            jnp.zeros((GROUP, row_count, LANES), BF),
            back[:, :half],
            jnp.zeros((GROUP, gap, LANES), BF),
            back[:, half:],
        ],
        1,
    )
    sent = (sent.astype(F32) + back.astype(F32)).astype(BF)
    got = exchange(sent, count)

    left, got = lax.optimization_barrier((left, got))
    n1, att, n2, mixed = (
        [part[:, :, start:end] for part in left]
        for start, end in (
            (0, shard),
            (shard, 2 * shard),
            (2 * shard, 3 * shard),
            (3 * shard, left_rows),
        )
    )
    d_proj_1, gain_attn_1, *grad_1 = on_core(
        global_finish_body,
        [((rows, 3 * width), BF), ((1, width), F32)] + [((row_count, width), BF)] * micro_count,
        (first, got, d_mid_1, *in_1, gain_attn, global_tables),
    )

    up_0 = to_other_section(grad_1, -1)
    gain_mlp_0, d_mid_0, d_att_0, right = on_core(
        local_back_middle_body,
        [
            ((1, width), F32),
            ((rows, width), F32),
            ((rows, width), BF),
            ((rows, inner + 2 * width), BF),
        ],
        (*others, lower_flag, *up_0, middle_0, gate_up_0, gain_mlp, right_1),
        [pltpu.VMEM((hidden, width), BF)],
        [pltpu.VMEM] * len(others) + [pltpu.SMEM] + [pltpu.VMEM] * 6,
    )
    across, beside = partner(right, 2, count), partner(right, 1, count)
    dq_0, d_own, d_before, d_after = on_core(
        local_backward_body,
        [
            ((rows, width), BF),
            ((rows, 2 * width), F32),
            ((rows, 2 * width), BF),
            ((rows, 2 * width), BF),
        ],
        (q_0, *around_0, bias, total_0, d_att_0, local_tables),
    )
    from_after = lax.ppermute(d_before, "dp", down_pairs)
    from_before = lax.ppermute(d_after, "dp", up_pairs)
    d_proj, grad_0, gain_attn_sum = on_core(
        local_finish_body,
        [((rows + EXTRA, 3 * width), BF), ((rows, width), BF), ((1, width), F32)],
        (
            lower_flag, first, dq_0, d_own, from_after, from_before, local_tables, d_mid_0, in_0, gain_attn,
            gain_mlp_0, d_proj_1, gain_attn_1, gain_mlp_1,
        ),
        [pltpu.VMEM((1, width), F32)],
        [pltpu.SMEM] + [pltpu.VMEM] * 13,
    )
    across, d_proj = lax.optimization_barrier((across, d_proj))
    right = [right, beside, across, partner(across, 1, count)]
    early_rows = shard_total * (inner // width + 1) + hidden_total
    early = on_core(
        functools.partial(early_body, shard),
        four_planes((early_rows, width)),
        (*right, *flat_rows(n2), *flat_rows(mixed), *flat_rows(att)),
    )
    d_proj = plane_parts(d_proj, count, early)
    early = sent_planes(early, count)
    late_in = (group_pos[None], *d_proj, *flat_rows(n1))
    late = on_core(
        late_body,
        four_planes((shard_total, 3 * width + LANES)),
        late_in,
        [pltpu.VMEM((width, LANES), F32)],
        [pltpu.SMEM] + [pltpu.VMEM] * (len(late_in) - 1),
    )
    early, late = lax.optimization_barrier((early, list(late)))
    early, late = sum_planes(early), sum_planes(sent_planes(late, count))
    parts = [early[p * shard_total : (p + 1) * shard_total] for p in range(inner // width)]
    start = shard_total * (inner // width)
    in_share = jnp.concatenate(parts, 1)
    mlp_out_share = early[start : start + hidden_total]
    attn_share = early[start + hidden_total :]
    gain_columns = late[:, 3 * width :]
    qkv_share, in_share, mlp_out_share, attn_share, gain_columns = (
        over_groups(item, count)
        for item in (late[:, : 3 * width], in_share, mlp_out_share, attn_share, gain_columns)
    )
    if count == GROUP:
        gains = jnp.stack([gain_columns[:, 0], gain_columns[:, 2]])
    else:
        gain_mlp_sum = jnp.where(lower, gain_mlp_0, gain_mlp_1)
        gains = lax.psum(jnp.concatenate([gain_attn_sum, gain_mlp_sum]), "dp")
        gains = lax.dynamic_slice_in_dim(gains, replica * shard, shard, 1)

    return (
        jnp.where(lower, jnp.concatenate(out_0), out_1).reshape(1, micro_count, row_count, width),
        jnp.where(lower, grad_0, jnp.concatenate(grad_1)).reshape(1, micro_count, row_count, width),
        qkv_share[None],
        attn_share[None],
        in_share[None],
        mlp_out_share[None],
        gains[:1],
        gains[1:],
    )


def solution(mesh):
    in_specs = (
        P(None, "dp", None),
        P(None, "dp"),
        P(None, "dp", None),
        P("section", "dp", None),
        P("section", "dp", None),
        P("section", "dp", None),
        P("section", "dp", None),
        P("section", "dp"),
        P("section", "dp"),
    )
    out_specs = (
        P("section", None, "dp", None),
        P("section", None, "dp", None),
        P("section", "dp", None),
        P("section", "dp", None),
        P("section", "dp", None),
        P("section", "dp", None),
        P("section", "dp"),
        P("section", "dp"),
    )
    return jax.shard_map(
        on_device, mesh=mesh, in_specs=in_specs, out_specs=out_specs, check_vma=False
    )
```

```python
import functools
import math

import jax
import jax.numpy as jnp
from jax import lax
from jax.experimental import pallas as pl
from jax.experimental.pallas import tpu as pltpu
from jax.sharding import PartitionSpec as P

HEAD_DIM = 64
GROUP = 16
HALF_WIN = 64
EXTRA = 16
LANES = 128
TILE = 256

local_log_base = math.log(10000.0)
global_log_base = math.log(160000.0)
masked_score = -1e30
SCALE = 1.0 / math.sqrt(HEAD_DIM)
BF = jnp.bfloat16
F32 = jnp.float32


def dot(left, right):
    return jnp.dot(left, right, preferred_element_type=F32)


def dot_bt(left, right):
    return lax.dot_general(left, right, (((1,), (1,)), ((), ())), preferred_element_type=F32)


def dot_at(left, right):
    return lax.dot_general(left, right, (((0,), (0,)), ((), ())), preferred_element_type=F32)


def moments(values):
    center = values - jnp.mean(values, -1, keepdims=True)
    scale = lax.rsqrt(jnp.mean(center * center, -1, keepdims=True) + 1e-05)
    return center * scale, scale


def norm_back(grad_out, gain_row, xhat, scale):
    scaled = grad_out * gain_row
    mean_grad = jnp.mean(scaled, -1, keepdims=True)
    mean_dot = jnp.mean(scaled * xhat, -1, keepdims=True)
    return (scaled - mean_grad - xhat * mean_dot) * scale


def angles(positions, log_base):
    half_dim = HEAD_DIM // 2
    fraction = (2 * jnp.arange(half_dim)).astype(F32) / HEAD_DIM
    inverse = jnp.exp(-fraction * log_base)
    table = positions.astype(F32)[:, None] * inverse[None, :]
    cosine, sine = jnp.cos(table), jnp.sin(table)
    none = jnp.zeros_like(sine)
    cosine = jnp.concatenate([cosine, cosine], 1)
    to_first = jnp.concatenate([-sine, none], 1)
    to_second = jnp.concatenate([none, sine], 1)
    return jnp.tile(jnp.stack([cosine, to_first, to_second]), (1, 2, 2))


def on_core(body, outs, args, scratch=(), spaces=None, out_spaces=None):
    return pl.pallas_call(
        body,
        out_shape=[jax.ShapeDtypeStruct(shape, dtype) for shape, dtype in outs],
        in_specs=[
            pl.BlockSpec(memory_space=space) for space in spaces or [pltpu.VMEM] * len(args)
        ],
        out_specs=[
            pl.BlockSpec(memory_space=space) for space in out_spaces or [pltpu.VMEM] * len(outs)
        ],
        scratch_shapes=scratch,
        cost_estimate=pl.CostEstimate(
            flops=2**10, bytes_accessed=2**10, transcendentals=0
        ),
        compiler_params=pltpu.CompilerParams(vmem_limit_bytes=48 * 2**20),
    )(*args)


def low_lanes():
    return lax.broadcasted_iota(jnp.int32, (1, LANES), 1) < HEAD_DIM


def swap(chunk):
    return pltpu.roll(chunk, HEAD_DIM, 1)


def chunks_of(rows):
    return [rows[:, c : c + LANES] for c in range(0, rows.shape[1], LANES)]


def rotate(chunk, tables):
    cosine, to_first, to_second = tables
    quarter = HEAD_DIM // 2
    return (
        chunk * cosine
        + pltpu.roll(chunk, LANES - quarter, 1) * to_first
        + pltpu.roll(chunk, quarter, 1) * to_second
    )


def unrotate(chunk, tables):
    cosine, to_first, to_second = tables
    quarter = HEAD_DIM // 2
    return (
        chunk * cosine
        - pltpu.roll(chunk, LANES - quarter, 1) * to_first
        - pltpu.roll(chunk, quarter, 1) * to_second
    )


def low_and_high(chunks):
    swapped = [swap(chunk) for chunk in chunks]
    low = [(swapped if h % 2 else chunks)[h // 2] for h in range(2 * len(chunks))]
    high = [(chunks if h % 2 else swapped)[h // 2] for h in range(2 * len(chunks))]
    return low, high


def targets():
    for d in range(GROUP):
        micro, chip, half = d // 8, d % 8 // 2, d % 2
        yield d, micro, 3 * chip + 2 * half, 3 * chip + 1, half


def pack_folded(chunks, ref, base):
    low, high = low_and_high(chunks)
    first = low_lanes()
    rows = chunks[0].shape[0] // 2
    half, fold = rows // 2, rows * 3 // 4
    for d, micro, own, shared, side in targets():
        start = micro * rows
        part = start + side * half
        upper = jnp.concatenate(
            [high[own][start + fold : start + rows], high[shared][part : part + half]], 0
        )
        ref[d, base : base + fold] = jnp.where(
            first, low[own][start : start + fold], upper
        ).astype(BF)


def pack_pairs(lefts, rights, ref):
    low, high = low_and_high(lefts)[0], low_and_high(rights)[1]
    first = low_lanes()
    rows = lefts[0].shape[0] // 2
    half = rows // 2
    for d, micro, own, shared, side in targets():
        start = micro * rows
        part = start + side * half
        ref[d, 0:rows] = jnp.where(
            first, low[own][start : start + rows], high[own][start : start + rows]
        ).astype(BF)
        ref[d, rows : rows + half] = jnp.where(
            first, low[shared][part : part + half], high[shared][part : part + half]
        ).astype(BF)


def unpack_folded(ref, base, rows):
    first = low_lanes()
    fold = rows * 3 // 4
    low, high = {}, {}
    shared_parts = {}
    for d, micro, own, shared, side in targets():
        block = ref[d, base : base + fold].astype(F32)
        mine = jnp.concatenate([block, swap(block[: rows - fold])], 0)
        if own % 2:
            high[micro, own] = swap(mine)
        else:
            low[micro, own] = mine
        shared_parts[micro, shared, side] = block[rows - fold :]
        if side:
            both = jnp.concatenate([shared_parts[micro, shared, 0], block[rows - fold :]], 0)
            if shared % 2:
                high[micro, shared] = both
            else:
                low[micro, shared] = swap(both)
    heads = GROUP // 4 * 3
    return [
        jnp.concatenate(
            [jnp.where(first, low[m, h], high[m, h + 1]) for m in range(2)], 0
        )
        for h in range(0, heads, 2)
    ]


def unpack_pairs(ref, rows):
    first = low_lanes()
    half = rows // 2
    pairs = {}
    parts = {}
    for d, micro, own, shared, side in targets():
        pairs[micro, own] = ref[d, 0:rows].astype(F32)
        parts[side] = ref[d, rows : rows + half].astype(F32)
        if side:
            pairs[micro, shared] = jnp.concatenate([parts[0], parts[1]], 0)
    heads = GROUP // 4 * 3
    lefts, rights = [], []
    for h in range(0, heads, 2):
        even, odd = [pairs[m, h] for m in range(2)], [pairs[m, h + 1] for m in range(2)]
        lefts.append(
            jnp.concatenate([jnp.where(first, a, swap(b)) for a, b in zip(even, odd)], 0)
        )
        rights.append(
            jnp.concatenate([jnp.where(first, swap(a), b) for a, b in zip(even, odd)], 0)
        )
    return lefts, rights


class Weights:
    def __init__(self, sources, mlp_out):
        self.sources = sources
        self.mlp_out = sources[-1]
        if len(sources) == 1:
            self.mlp_out = mlp_out
            unpack_rows(sources[0], mlp_out)

    def get(self, which):
        if which == 2:
            return self.mlp_out[...]
        if len(self.sources) > 1:
            return self.sources[which][...]
        (wide,) = self.sources
        width = wide.shape[0]
        inner = 2 * self.mlp_out.shape[0]
        return wide[:, width : width + inner] if which else wide[:, :width]


def first_block(pair):
    return -(-pair // 32) * 16


def packed_pieces(shard, rows, width):
    yield 0, shard, 0, width, 0, 0
    rest = rows - shard
    side = width // 3
    yield 0, rest, width, 2 * side, shard, 0
    yield rest, 16, width, side, shard, 2 * side
    yield rest, 16, width + side, side, shard + 16, 2 * side


def unpack_rows(wide, mlp_out):
    hidden, width = mlp_out.shape
    shard = wide.shape[0] // GROUP
    start = wide.shape[1] - width - 2 * (width // 3)
    pair = 2 * hidden // GROUP
    upper = first_block(pair)
    for d in range(GROUP):
        low = d // 2 * pair + d % 2 * upper
        have = pair - upper if d % 2 else upper
        for row, rows, column, columns, to_row, to_column in packed_pieces(shard, upper, width):
            rows = min(rows, have - to_row)
            if rows > 0:
                mlp_out[low + to_row : low + to_row + rows, to_column : to_column + columns] = wide[
                    d * shard + row : d * shard + row + rows, start + column : start + column + columns
                ]


def stack_body(odd_ref, attn_ref, mlp_in_ref, own_ref, beside_ref, out_ref):
    shard, width = attn_ref.shape
    inner = mlp_in_ref.shape[1]
    out_ref[:, :width] = attn_ref[...]
    out_ref[:, width : width + inner] = mlp_in_ref[...]
    own, beside = own_ref[...].astype(F32), beside_ref[...].astype(F32)
    moved = beside.shape[0]
    even = jnp.concatenate([own, beside], 0)
    odd = jnp.concatenate([own[moved:], beside, beside], 0)
    block = jnp.where(odd_ref[0] == 1, odd, even).astype(BF)
    start = width + inner
    for row, rows, column, columns, from_row, from_column in packed_pieces(
        shard, block.shape[0], width
    ):
        out_ref[row : row + rows, start + column : start + column + columns] = block[
            from_row : from_row + rows, from_column : from_column + columns
        ]


def mlp_forward(layer_in, attended, gain, weights):
    middle = layer_in + dot(attended, weights.get(0))
    xhat, _ = moments(middle)
    normed = (xhat * gain).astype(BF)
    gate_up = dot(normed, weights.get(1))
    half = gate_up.shape[1] // 2
    gate, up = gate_up[:, :half], gate_up[:, half:]
    cdf = 0.5 * (1.0 + lax.erf(gate * math.sqrt(0.5)))
    mixed = (gate * cdf * up).astype(BF)
    result = (middle + dot(mixed, weights.get(2))).astype(BF)
    return middle, normed, gate, up, mixed, result


def mlp_backward(upstream, middle, gate, up, gain, weights):
    d_mixed = dot_bt(upstream, weights.get(2))
    cdf = 0.5 * (1.0 + lax.erf(gate * math.sqrt(0.5)))
    density = jnp.exp(-0.5 * gate * gate) * (1.0 / math.sqrt(2.0 * math.pi))
    d_gate = d_mixed * up * (cdf + gate * density)
    d_up = d_mixed * gate * cdf
    d_gate_up = jnp.concatenate([d_gate.astype(BF), d_up.astype(BF)], 1)
    d_normed = dot_bt(d_gate_up, weights.get(1))
    xhat, scale = moments(middle)
    gain_grad = jnp.sum(d_normed * xhat, 0, keepdims=True)
    d_middle = upstream.astype(F32) + norm_back(d_normed, gain, xhat, scale)
    d_attn = d_middle.astype(BF)
    d_attended = dot_bt(d_attn, weights.get(0))
    return d_gate_up, gain_grad, d_middle, d_attn, d_attended


def project(xhat, gain, first_ref, table_ref, normed_ref):
    width = xhat.shape[1]
    normed = (xhat * gain).astype(BF)
    normed_ref[...] = normed
    tables = [table_ref[i] for i in range(3)]
    results = [dot(normed, first_ref[:, c * width : (c + 1) * width]) for c in range(3)]
    queries, keys, values = chunks_of(results[0]), chunks_of(results[1]), results[2]
    return [rotate(c, tables) for c in queries], [rotate(c, tables) for c in keys], values


def input_backward(d_middle, d_projected, x, gain_ref, first_ref, gain_out_ref):
    d_normed = dot_bt(d_projected, first_ref[:, : d_projected.shape[1]])
    xhat, scale = moments(x)
    gain_out_ref[...] = jnp.sum(d_normed * xhat, 0, keepdims=True)
    return (d_middle + norm_back(d_normed, gain_ref[...], xhat, scale)).astype(BF)


def joined(refs):
    return jnp.concatenate([ref[...] for ref in refs], 0)


def store_chunks(refs, rows):
    size = rows.shape[0] // len(refs)
    for i, ref in enumerate(refs):
        ref[...] = rows[i * size : (i + 1) * size]


def message_body(w_ref, attn_ref, mlp_ref, ids_ref, out_ref, rows_scr, ids_scr):
    shard, columns = w_ref.shape
    micro_count, row_count = ids_ref.shape
    out_ref[:, :columns] = w_ref[...]
    rows_scr[...] = jnp.zeros_like(rows_scr)
    ids_scr[...] = jnp.zeros_like(ids_scr)
    rows_scr[0:1, :shard] = attn_ref[...].astype(F32)
    rows_scr[1:2, :shard] = mlp_ref[...].astype(F32)
    ids_scr[:micro_count, :row_count] = ids_ref[...].astype(F32)
    runs = -(-row_count // shard)
    for run in range(runs):
        turned = ids_scr[...]
        if run:
            turned = pltpu.roll(turned, LANES - run * shard, 1)
        for micro in range(micro_count):
            row = 2 + micro * runs + run
            rows_scr[row : row + 1] = turned[micro : micro + 1]
    out_ref[:, columns:] = rows_scr[...].T[:shard].astype(BF)


def local_project_body(first_ref, x_ref, table_ref, extra_ref, normed_ref, q_ref, kv_ref):
    xhat, _ = moments(x_ref[...].astype(F32))
    extra = first_ref[:, first_ref.shape[1] - LANES :].astype(F32).T
    extra_ref[...] = extra[: extra_ref.shape[0]]
    queries, keys, values = project(xhat, extra[:1], first_ref, table_ref, normed_ref)
    width = values.shape[1]
    for j, (q, k) in enumerate(zip(queries, keys)):
        q_ref[:, LANES * j : LANES * (j + 1)] = q.astype(BF)
        kv_ref[:, LANES * j : LANES * (j + 1)] = k.astype(BF)
    kv_ref[:, width:] = values.astype(BF)


def two_heads(chunk):
    first = low_lanes()
    wide = chunk.astype(F32)
    return jnp.concatenate([jnp.where(first, wide, 0.0), jnp.where(first, 0.0, wide)], 0)


def pick_heads(rows):
    half = rows.shape[0] // 2
    return jnp.where(low_lanes(), rows[:half], rows[half:])


def local_parts(q_ref, before_ref, own_ref, after_ref):
    rows = q_ref.shape[0] // 2
    width = q_ref.shape[1]
    for micro in range(2):
        for j in range(width // LANES):
            here = slice(micro * rows, (micro + 1) * rows)
            lanes = slice(LANES * j, LANES * (j + 1))
            more = slice(width + LANES * j, width + LANES * (j + 1))
            keys, values = (
                jnp.concatenate([ref[here, part] for ref in (before_ref, own_ref, after_ref)], 0)
                for part in (lanes, more)
            )
            queries = (two_heads(q_ref[here, lanes]) * SCALE).astype(BF)
            yield micro * (width // LANES) + j, micro, here, lanes, more, queries, keys, values


def local_forward_body(q_ref, before_ref, own_ref, after_ref, bias_ref, att_ref, total_ref):
    parts = local_parts(q_ref, before_ref, own_ref, after_ref)
    for index, micro, here, lanes, _, queries, keys, values in parts:
        scores = dot_bt(keys, queries) + bias_ref[micro]
        peak = jnp.max(scores, 0, keepdims=True)
        weights = jnp.exp(scores - peak)
        total = jnp.sum(weights, 0, keepdims=True)
        total_ref[index] = peak + jnp.log(total)
        probs = (weights * (1.0 / total)).astype(BF)
        att_ref[here, lanes] = pick_heads(dot_at(probs, values)).astype(BF)


def local_backward_body(
    q_ref, before_ref, own_ref, after_ref, bias_ref, total_ref, d_ref, table_ref,
    dq_ref, d_own_ref, d_before_ref, d_after_ref,
):
    tables = [table_ref[i] for i in range(3)]
    parts = local_parts(q_ref, before_ref, own_ref, after_ref)
    rows = q_ref.shape[0] // 2
    for index, micro, here, lanes, more, queries, keys, values in parts:
        d_out = two_heads(d_ref[here, lanes]).astype(BF)
        probs = jnp.exp(dot_bt(keys, queries) + bias_ref[micro] - total_ref[index])
        d_probs = dot_bt(values, d_out)
        product = probs * d_probs
        delta = jnp.sum(product, 0, keepdims=True)
        d_scores = (product - probs * delta).astype(BF)
        d_queries = pick_heads(dot_at(d_scores, keys)) * SCALE
        local_tables = [table[here] for table in tables]
        dq_ref[here, lanes] = unrotate(d_queries, local_tables).astype(BF)
        for part, grads in ((lanes, dot(d_scores, queries)), (more, dot(probs.astype(BF), d_out))):
            d_before_ref[here, part] = grads[:rows].astype(BF)
            d_own_ref[here, part] = grads[rows : 2 * rows]
            d_after_ref[here, part] = grads[2 * rows :].astype(BF)


def local_finish_body(
    lower_ref, first_ref, dq_ref, own_ref, low_ref, high_ref, table_ref, d_middle_ref, x_ref, gain_ref,
    gain_mlp_ref, other_ref, other_attn_ref, other_mlp_ref, out_ref, grad_ref, gain_attn_ref, gain_scr,
):
    rows, width = dq_ref.shape

    @pl.when(lower_ref[0] == 1)
    def _():
        tables = [table_ref[i] for i in range(3)]
        total = own_ref[...] + low_ref[...].astype(F32) + high_ref[...].astype(F32)
        out_ref[:rows, :width] = dq_ref[...]
        for j, chunk in enumerate(chunks_of(total[:, :width])):
            start = width + LANES * j
            out_ref[:rows, start : start + LANES] = unrotate(chunk, tables).astype(BF)
        out_ref[:rows, 2 * width :] = total[:, width:].astype(BF)
        grad_ref[...] = input_backward(
            d_middle_ref[...], out_ref[:rows], x_ref[...].astype(F32), gain_ref, first_ref, gain_scr
        )

    @pl.when(lower_ref[0] == 0)
    def _():
        out_ref[:rows] = other_ref[...]
        grad_ref[...] = jnp.zeros_like(grad_ref)
        gain_scr[...] = other_attn_ref[...]

    gain_attn_ref[...] = gain_scr[...]
    gain_mlp = jnp.where(lower_ref[0] == 1, gain_mlp_ref[...], other_mlp_ref[...])
    index = lax.broadcasted_iota(jnp.int32, (EXTRA, width), 0)
    tail = jnp.zeros((EXTRA, width), F32)
    for row, gain in ((0, gain_scr[...]), (2, gain_mlp)):
        high = gain.astype(BF).astype(F32)
        tail = jnp.where(index == row, high, tail)
        tail = jnp.where(index == row + 1, gain - high, tail)
    out_ref[rows:] = jnp.zeros((EXTRA, out_ref.shape[1]), BF)
    out_ref[rows:, :width] = tail.astype(BF)


def local_middle_body(*refs):
    sources, refs = refs[:-10], refs[-10:]
    x_ref, att_ref, gain_ref, normed_ref, mixed_ref, middle_ref, gate_up_ref = refs[:7]
    weights = Weights(sources, refs[9])
    middle, normed, gate, up, mixed, result = mlp_forward(
        x_ref[...].astype(F32), att_ref[...], gain_ref[...], weights
    )
    store_chunks(refs[7:9], result)
    normed_ref[...] = normed
    mixed_ref[...] = mixed
    middle_ref[...] = middle
    half = gate.shape[1]
    gate_up_ref[:, :half] = gate
    gate_up_ref[:, half:] = up


def local_back_middle_body(*refs):
    sources, refs = refs[:-12], refs[-12:]
    lower_ref, low_ref, high_ref, middle_ref, gate_up_ref, gain_ref, other_ref = refs[:7]
    gain_out_ref, d_middle_ref, d_att_ref, right_ref = refs[7:11]
    weights = Weights(sources, refs[11])
    half = gate_up_ref.shape[1] // 2
    upstream = joined([low_ref, high_ref])
    d_gate_up, gain_grad, d_middle, d_attn, d_attended = mlp_backward(
        upstream, middle_ref[...], gate_up_ref[:, :half], gate_up_ref[:, half:],
        gain_ref[...], weights,
    )
    gain_out_ref[...] = gain_grad
    d_middle_ref[...] = d_middle
    d_att_ref[...] = d_attended.astype(BF)

    @pl.when(lower_ref[0] == 1)
    def _():
        right_ref[:, : 2 * half] = d_gate_up
        right_ref[:, 2 * half :] = d_attn

    @pl.when(lower_ref[0] == 0)
    def _():
        right_ref[...] = other_ref[...]


def global_project_body(first_ref, low_ref, high_ref, gain_ref, table_ref, normed_ref, sent_ref):
    xhat, _ = moments(joined([low_ref, high_ref]).astype(F32))
    queries, keys, values = project(xhat, gain_ref[...], first_ref, table_ref, normed_ref)
    pack_pairs(queries, keys, sent_ref)
    pack_folded(chunks_of(values), sent_ref, sent_ref.shape[1] * 2 // 3)


def flat(blocks):
    return blocks.reshape(-1, LANES)


def own_unfolded(ref, base, rows):
    fold = rows * 3 // 4
    block = ref[:, base : base + fold].astype(F32)
    rest = swap(flat(block[:, : rows - fold])).reshape(GROUP, rows - fold, LANES)
    return flat(jnp.concatenate([block, rest], 1))


def shared_unfolded(ref, start, rows):
    return swap(flat(ref[:, start : start + rows // 2].astype(F32)))


def fill_heads(got_ref, other_ref, own_seg_ref, shared_seg_ref, q_scr, k_scr, v_scr):
    rows = got_ref.shape[1] * 4 // 9
    half = rows // 2
    first = low_lanes()
    lane = lax.broadcasted_iota(jnp.int32, (1, LANES), 1) - HEAD_DIM
    own = flat(got_ref[:, 0:rows].astype(F32))
    shared = flat(got_ref[:, rows : rows + half].astype(F32))
    other = flat(other_ref[:, 0:half].astype(F32))
    count = own.shape[0]
    own_hit = lane == own_seg_ref[...]
    shared_hit = lane == shared_seg_ref[...]
    both = jnp.concatenate([shared, other], 0)
    for start, pairs, hit in (
        (0, own, own_hit),
        (count, shared, shared_hit[: count // 2]),
    ):
        marked = jnp.where(hit, 1.0, 0.0)
        q_scr[start : start + pairs.shape[0]] = jnp.where(first, pairs * SCALE, marked).astype(BF)
    for unit, pairs, hit in ((0, own, own_hit), (1, both, shared_hit)):
        marked = jnp.where(hit, 0.0, masked_score)
        k_scr[unit] = jnp.where(first, swap(pairs), marked).astype(BF)
    base = rows + half
    v_scr[0] = jnp.where(first, own_unfolded(got_ref, base, rows), 0.0).astype(BF)
    start = base + rows - rows * 3 // 4
    shared_v = jnp.concatenate(
        [shared_unfolded(got_ref, start, rows), shared_unfolded(other_ref, half, rows)], 0
    )
    v_scr[1] = jnp.where(first, shared_v, 0.0).astype(BF)


def fold_out(own, shared, rows, ref, base):
    fold = rows * 3 // 4
    blocks = own.reshape(GROUP, rows, LANES)
    swapped = swap(own).reshape(GROUP, rows, LANES)
    upper = jnp.concatenate(
        [swapped[:, fold:], swap(shared).reshape(GROUP, rows // 2, LANES)], 1
    )
    ref[:, base : base + fold] = jnp.where(low_lanes(), blocks[:, :fold], upper).astype(BF)


def global_forward_body(
    got_ref, other_ref, own_seg_ref, shared_seg_ref, out_ref, total_ref,
    q_scr, k_scr, v_scr, vt_scr, o_scr,
):
    fill_heads(got_ref, other_ref, own_seg_ref, shared_seg_ref, q_scr, k_scr, v_scr)
    for unit in range(2):
        vt_scr[unit] = v_scr[unit].astype(F32).T.astype(BF)
    count = k_scr.shape[1]

    def step(tile, carry):
        unit = tile // (count // TILE)
        rows = pl.ds(pl.multiple_of(tile * TILE, TILE), TILE)
        scores = dot_bt(k_scr[unit], q_scr[rows])
        peak = jnp.max(scores, 0, keepdims=True)
        weights = jnp.exp(scores - peak)
        total = jnp.sum(weights, 0, keepdims=True)
        total_ref[tile] = peak + jnp.log(total)
        out = dot(vt_scr[unit], weights.astype(BF)) * (1.0 / total)
        o_scr[rows] = out.T
        return carry

    lax.fori_loop(0, q_scr.shape[0] // TILE, step, 0)
    rows = got_ref.shape[1] * 4 // 9
    fold_out(o_scr[:count], o_scr[count:], rows, out_ref, 0)


def global_backward_body(
    got_ref, other_ref, own_seg_ref, shared_seg_ref, total_ref, d_ref, sent_ref, to_other_ref,
    q_scr, k_scr, v_scr, kt_scr, d_scr, dq_scr, dk_scr, dv_scr,
):
    fill_heads(got_ref, other_ref, own_seg_ref, shared_seg_ref, q_scr, k_scr, v_scr)
    first = low_lanes()
    rows = got_ref.shape[1] * 4 // 9
    half = rows // 2
    for unit in range(2):
        keys = jnp.where(first, k_scr[unit].astype(F32), 0.0)
        kt_scr[unit] = keys.T.astype(BF)
    count = k_scr.shape[1]
    d_scr[:count] = jnp.where(first, own_unfolded(d_ref, 0, rows), 0.0).astype(BF)
    d_scr[count:] = jnp.where(
        first, shared_unfolded(d_ref, rows - rows * 3 // 4, rows), 0.0
    ).astype(BF)
    dk_scr[...] = jnp.zeros_like(dk_scr)
    dv_scr[...] = jnp.zeros_like(dv_scr)

    def step(tile, carry):
        unit = tile // (count // TILE)
        here = pl.ds(pl.multiple_of(tile * TILE, TILE), TILE)
        queries, d_out = q_scr[here], d_scr[here]
        probs = jnp.exp(dot_bt(k_scr[unit], queries) - total_ref[tile])
        d_probs = dot_bt(v_scr[unit], d_out)
        product = probs * d_probs
        delta = jnp.sum(product, 0, keepdims=True)
        d_scores = (product - probs * delta).astype(BF)
        dv_scr[unit] += dot(probs.astype(BF), d_out)
        dk_scr[unit] += dot(d_scores, queries)
        dq_scr[here] = dot(kt_scr[unit], d_scores).T * SCALE
        return carry

    lax.fori_loop(0, q_scr.shape[0] // TILE, step, 0)
    mine = count // 2
    own = jnp.where(first, dq_scr[:count], swap(dk_scr[0]))
    sent_ref[:, 0:rows] = own.reshape(GROUP, rows, LANES).astype(BF)
    shared_k, shared_v = dk_scr[1], dv_scr[1]
    shared = jnp.where(first, dq_scr[count:], swap(shared_k[:mine]))
    sent_ref[:, rows : rows + half] = shared.reshape(GROUP, half, LANES).astype(BF)
    fold_out(dv_scr[0], shared_v[:mine], rows, sent_ref, rows + half)
    for place, grads in enumerate((shared_k, shared_v)):
        other = jnp.where(first, 0.0, swap(grads[mine:])).reshape(GROUP, half, LANES)
        to_other_ref[:, place * half : (place + 1) * half] = other.astype(BF)


def global_middle_body(*refs):
    sources, refs = refs[:-14], refs[-14:]
    got_ref, low_ref, high_ref, up_ref, gain_ref, out_ref, att_ref, normed_ref, mixed_ref = refs[:9]
    right_ref, gain_out_ref, d_middle_ref, sent_ref = refs[9:13]
    weights = Weights(sources, refs[13])
    rows = low_ref.shape[0]
    attended = jnp.concatenate([c.astype(BF) for c in unpack_folded(got_ref, 0, rows)], 1)
    att_ref[...] = attended
    gain = gain_ref[...]
    middle, normed, gate, up, mixed, result = mlp_forward(
        joined([low_ref, high_ref]).astype(F32), attended, gain, weights
    )
    out_ref[...] = result
    normed_ref[...] = normed
    mixed_ref[...] = mixed
    d_gate_up, gain_grad, d_middle, d_attn, d_attended = mlp_backward(
        up_ref[...], middle, gate, up, gain, weights
    )
    right_ref[:, : d_gate_up.shape[1]] = d_gate_up
    right_ref[:, d_gate_up.shape[1] :] = d_attn
    gain_out_ref[...] = gain_grad
    d_middle_ref[...] = d_middle
    pack_folded(chunks_of(d_attended), sent_ref, 0)


def global_finish_body(
    first_ref, got_ref, d_middle_ref, low_ref, high_ref, gain_ref, table_ref,
    d_proj_ref, gain_out_ref, *grad_refs,
):
    tables = [table_ref[i] for i in range(3)]
    x = joined([low_ref, high_ref]).astype(F32)
    rows = low_ref.shape[0]
    d_queries, d_keys = unpack_pairs(got_ref, rows)
    d_values = unpack_folded(got_ref, rows * 3 // 2, rows)
    parts = [unrotate(c, tables).astype(BF) for c in d_queries + d_keys]
    d_projected = jnp.concatenate(parts + [c.astype(BF) for c in d_values], 1)
    d_proj_ref[...] = d_projected
    store_chunks(
        grad_refs,
        input_backward(d_middle_ref[...], d_projected, x, gain_ref, first_ref, gain_out_ref),
    )


def neighbours(count, step):
    return [
        (i, i + step)
        for i in range(count)
        if 0 <= i + step < count and i // GROUP == (i + step) // GROUP
    ]


def exchange(blocks, count):
    groups = [list(range(s, s + GROUP)) for s in range(0, count, GROUP)]
    return lax.all_to_all(blocks, "dp", 0, 0, axis_index_groups=groups)


def to_other_section(chunks, step):
    pairs = [(0, 1)] if step > 0 else [(1, 0)]
    return [lax.ppermute(rows, "section", pairs) for rows in chunks]


def partner(rows, apart, count):
    return lax.ppermute(rows, "dp", [(i, i ^ apart) for i in range(count)])


def gather_rows(piece, group_pos, count):
    pieces = {0: piece}
    for apart in (4, 8, 12):
        pieces[apart] = partner(piece, apart, count)
    for apart in (0, 4, 8, 12):
        pieces[apart + 2] = partner(pieces[apart], 2, count)
    for apart in range(0, GROUP, 2):
        pieces[apart + 1] = partner(pieces[apart], 1, count)
    whole = jnp.zeros((GROUP,) + piece.shape, piece.dtype)
    for apart, item in pieces.items():
        start = (group_pos ^ apart,) + (0,) * piece.ndim
        whole = lax.dynamic_update_slice(whole, item[None], start)
    if count > GROUP:
        groups = [list(range(s, count, GROUP)) for s in range(GROUP)]
        whole = lax.all_gather(whole, "dp", axis=0, tiled=True, axis_index_groups=groups)
    return whole.reshape(-1, piece.shape[-1]), pieces[2]


def plane_rows(rows, group_pos, count):
    parts = rows.reshape(count // GROUP, 4, 4, *rows.shape[1:])
    place, plane = group_pos % 4, group_pos // 4
    taken = []
    for apart in range(4):
        block = lax.dynamic_index_in_dim(parts, place ^ apart, 2, keepdims=False)
        block = jnp.stack(
            [lax.dynamic_index_in_dim(block, plane ^ z, 1, keepdims=False) for z in range(4)]
        )
        taken.append(partner(block, apart, count) if apart else block)
    return taken


def left_body(lower_ref, place_ref, *refs):
    refs, out_ref = refs[:-1], refs[-1]
    base = 0
    for first_ref, second_ref in zip(refs[0::2], refs[1::2]):
        rows = jnp.where(lower_ref[0] == 1, first_ref[...].astype(F32), second_ref[...].astype(F32))
        turned = rows.T
        size = turned.shape[0] // GROUP
        for d in range(GROUP):
            side = d % 4 ^ place_ref[0] % 4
            plane = d // 4 ^ place_ref[0] // 4
            out_ref[side, plane, base : base + size] = turned[d * size : (d + 1) * size].astype(BF)
        base += size


def left_rows_of(refs, rows):
    start, end = rows
    parts = [
        jnp.concatenate([ref[p, start:end].astype(F32) for p in range(4)], 0).astype(BF) for ref in refs
    ]
    return jnp.concatenate(parts, 1)


def by_plane(result, base, outs, columns=slice(None)):
    keep, keep_far, send = outs
    rows = result.shape[0] // 4
    half = send.shape[0] // 2
    here = slice(base, base + rows)
    keep[here, columns] = result[:rows]
    keep_far[here, columns] = result[2 * rows : 3 * rows]
    send[here, columns] = result[rows : 2 * rows].astype(BF)
    send[half + base : half + base + rows, columns] = result[3 * rows :].astype(BF)


def early_body(terms, *refs):
    refs, outs = refs[:-3], refs[-3:]
    rights, lefts = refs[:4], refs[4:]
    width = outs[0].shape[1]
    base = 0
    for rows, (start, end) in terms:
        right = jnp.concatenate([ref[:, start:end] for ref in rights], 0)
        result = dot(left_rows_of(lefts, rows), right)
        for column in range(0, end - start, width):
            by_plane(result[:, column : column + width], base, outs)
            base += result.shape[0] // 4


def late_body(rows, place_ref, *refs):
    refs, outs, scr = refs[:-4], refs[-4:-1], refs[-1]
    rights, lefts = refs[:4], refs[4:]
    tokens = lefts[0].shape[2]
    columns = rights[0].shape[1]
    width = columns // 3
    size = outs[0].shape[0]
    right = jnp.concatenate([ref[:tokens] for ref in rights], 0)
    by_plane(dot(left_rows_of(lefts, rows), right), 0, outs, slice(0, columns))
    tail = sum(ref[tokens:, :width].astype(F32) for ref in rights)
    both = jnp.concatenate([tail, jnp.zeros((LANES - EXTRA, width), F32)], 0).T
    lane = lax.broadcasted_iota(jnp.int32, (1, LANES), 1)
    lows = pltpu.roll(both, LANES - 1, 1)
    scr[...] = jnp.where(lane % 2 == 0, both + lows, 0.0)
    gains = []
    for plane in range(4):
        d = (place_ref[0] // 4 ^ plane) * 4 + place_ref[0] % 4
        gains.append(scr[pl.ds(pl.multiple_of(d * size, 16), size)])
    by_plane(jnp.concatenate(gains, 0), 0, outs, slice(columns, columns + LANES))


def three_parts(shape):
    return [(shape, F32), (shape, F32), ((2 * shape[0], shape[1]), BF)]


def first_hop(blocks, count):
    keep, keep_far, send = blocks
    got = partner(send, 4, count)
    half = keep.shape[0]
    return keep + got[:half].astype(F32), (keep_far + got[half:].astype(F32)).astype(BF)


def second_hop(near, far, count):
    return near + partner(far, 8, count).astype(F32)


def over_groups(rows, count):
    if count == GROUP:
        return rows
    apart = [list(range(s, count, GROUP)) for s in range(GROUP)]
    rows = rows.reshape(count // GROUP, -1, rows.shape[1])
    return lax.psum_scatter(rows, "dp", scatter_dimension=0, axis_index_groups=apart)


def on_device(
    tokens_in,
    segment_ids,
    out_grad,
    qkv_weight,
    attn_out_weight,
    mlp_in_weight,
    mlp_out_weight,
    attn_gain,
    mlp_gain,
):
    lower = lax.axis_index("section") == 0
    lower_flag = lower.astype(jnp.int32)[None]
    shard_total = qkv_weight.shape[1] * (lax.axis_size("dp") // GROUP)
    hidden_total = mlp_out_weight.shape[1] * (lax.axis_size("dp") // GROUP)
    count = lax.axis_size("dp")
    replica = lax.axis_index("dp")
    group_pos = replica % GROUP
    micro_count, row_count, width = tokens_in.shape
    shard = qkv_weight.shape[1]
    runs = -(-row_count // shard)
    (message,) = on_core(
        message_body,
        [((shard, 3 * width + LANES), BF)],
        (qkv_weight[0], attn_gain, mlp_gain, segment_ids),
        [pltpu.VMEM((LANES, LANES), F32), pltpu.VMEM((8, LANES), F32)],
    )
    first, early_piece = gather_rows(message, group_pos, count)
    inner = mlp_in_weight.shape[2]
    hidden = mlp_out_weight.shape[1] * count
    if count == GROUP:
        moved = first_block(2 * mlp_out_weight.shape[1]) - mlp_out_weight.shape[1]
        beside = partner(mlp_out_weight[0, :moved], 1, count)
        (stacked,) = on_core(
            stack_body,
            [((shard, width + inner + width + 2 * (width // 3)), BF)],
            (
                (replica % 2)[None],
                attn_out_weight[0],
                mlp_in_weight[0],
                mlp_out_weight[0],
                beside,
            ),
            (),
            [pltpu.SMEM] + [pltpu.VMEM] * 4,
        )
        stacked, _ = lax.optimization_barrier((stacked, early_piece))
        others = [lax.all_gather(stacked, "dp", axis=0, tiled=True)]
    else:
        others = [
            lax.all_gather(item[0], "dp", axis=0, tiled=True)
            for item in (attn_out_weight, mlp_in_weight, mlp_out_weight)
        ]
    positions = group_pos * row_count + jnp.arange(row_count)
    local_tables = angles(positions, local_log_base)
    global_tables = angles(positions, global_log_base)

    rows = micro_count * row_count
    pairs = rows * width // (row_count * LANES)
    in_0 = tokens_in.reshape(rows, width)
    extra_rows = -(-(2 + micro_count * runs) // 8) * 8
    extra, normed_0, q_0, kv_0 = on_core(
        local_project_body,
        [
            ((extra_rows, width), F32),
            ((rows, width), BF),
            ((rows, width), BF),
            ((rows, 2 * width), BF),
        ],
        (first, in_0, local_tables),
    )
    gain_attn, gain_mlp = extra[:1], extra[1:2]
    all_ids = extra[2 : 2 + micro_count * runs].reshape(micro_count, runs, count, shard)
    all_ids = lax.dynamic_slice_in_dim(all_ids, replica - group_pos, GROUP, 2)
    all_ids = all_ids.swapaxes(1, 2).reshape(micro_count, GROUP, runs * shard)[..., :row_count]
    segments = all_ids.reshape(micro_count, GROUP * row_count).astype(jnp.int32)

    key_pos = positions[0] - row_count + jnp.arange(3 * row_count)
    around = jnp.pad(segments, ((0, 0), (row_count, row_count)), constant_values=-1)
    key_seg = lax.dynamic_slice_in_dim(around, group_pos * row_count, 3 * row_count, 1)
    visible = (key_seg[:, :, None] == segment_ids[:, None, :]) & (
        jnp.abs(positions[None, :] - key_pos[:, None]) <= HALF_WIN
    )[None]
    bias = jnp.tile(jnp.where(visible, 0.0, masked_score), (1, 1, 2))

    own_seg = lax.dynamic_index_in_dim(segments, group_pos // 8, 0, keepdims=False)
    halves = own_seg.reshape(GROUP, 2, row_count // 2)
    mine = lax.dynamic_index_in_dim(halves, group_pos % 2, 1, keepdims=False).reshape(-1)
    theirs = lax.dynamic_index_in_dim(halves, 1 - group_pos % 2, 1, keepdims=False).reshape(-1)
    shared_seg = jnp.concatenate([mine, theirs])[:, None]
    own_seg = own_seg[:, None]

    up_pairs, down_pairs = neighbours(count, 1), neighbours(count, -1)
    around_0 = (
        lax.ppermute(kv_0, "dp", up_pairs),
        kv_0,
        lax.ppermute(kv_0, "dp", down_pairs),
    )
    att_0, total_0 = on_core(
        local_forward_body,
        [((rows, width), BF), ((pairs, 1, LANES), F32)],
        (q_0, *around_0, bias),
    )
    n2_0, mixed_0, middle_0, gate_up_0, *out_0 = on_core(
        local_middle_body,
        [
            ((rows, width), BF),
            ((rows, hidden), BF),
            ((rows, width), F32),
            ((rows, inner), F32),
        ]
        + [((row_count, width), BF)] * micro_count,
        (*others, in_0, att_0, gain_mlp),
        [pltpu.VMEM((hidden, width), BF)],
    )

    in_1 = to_other_section(out_0, 1)
    fold = row_count * 3 // 4
    half = row_count // 2
    normed_1, sent = on_core(
        global_project_body,
        [((rows, width), BF), ((GROUP, 3 * fold, LANES), BF)],
        (first, *in_1, gain_attn, global_tables),
    )
    got = exchange(sent, count)
    beside = jnp.concatenate(
        [got[:, row_count : row_count + half], got[:, 3 * fold - half :]], 1
    )
    beside = partner(beside, 1, count)
    keys = GROUP * row_count
    tiles = keys * 3 // 2 // TILE
    head_scratch = [
        pltpu.VMEM((keys * 3 // 2, LANES), BF),
        pltpu.VMEM((2, keys, LANES), BF),
        pltpu.VMEM((2, keys, LANES), BF),
        pltpu.VMEM((2, LANES, keys), BF),
    ]
    folded, total_1 = on_core(
        global_forward_body,
        [((GROUP, fold, LANES), BF), ((tiles, 1, TILE), F32)],
        (got, beside, own_seg, shared_seg),
        head_scratch + [pltpu.VMEM((keys * 3 // 2, LANES), F32)],
    )
    folded = exchange(folded, count)

    up_1 = out_grad.reshape(rows, width)
    out_1, att_1, n2_1, mixed_1, right_1, gain_mlp_1, d_mid_1, sent = on_core(
        global_middle_body,
        [
            ((rows, width), BF),
            ((rows, width), BF),
            ((rows, width), BF),
            ((rows, hidden), BF),
            ((rows, inner + width), BF),
            ((1, width), F32),
            ((rows, width), F32),
            ((GROUP, fold, LANES), BF),
        ],
        (*others, folded, *in_1, up_1, gain_mlp),
        [pltpu.VMEM((hidden, width), BF)],
    )
    d_folded = exchange(sent, count)
    pairs = ((normed_0, normed_1), (att_0, att_1), (n2_0, n2_1), (mixed_0, mixed_1))
    left_total = 3 * shard_total + hidden_total
    if count == GROUP:
        (left,) = on_core(
            left_body,
            [((4, 4, left_total, rows), BF)],
            (lower_flag, group_pos[None], *(item for pair in pairs for item in pair)),
            (),
            [pltpu.SMEM] * 2 + [pltpu.VMEM] * 8,
        )
        left, d_folded = lax.optimization_barrier((left, d_folded))
        left = [left[0]] + [partner(left[apart], apart, count) for apart in range(1, 4)]
    else:
        left = [
            plane_rows(jnp.where(lower, a, b).T.reshape(count, -1, rows), group_pos, count)
            for a, b in pairs
        ]
        left = [jnp.concatenate([i.reshape(4, -1, rows) for i in items], 1) for items in zip(*left)]
    sent, to_beside = on_core(
        global_backward_body,
        [((GROUP, 3 * fold, LANES), BF), ((GROUP, 2 * half, LANES), BF)],
        (got, beside, own_seg, shared_seg, total_1, d_folded),
        head_scratch
        + [
            pltpu.VMEM((keys * 3 // 2, LANES), BF),
            pltpu.VMEM((keys * 3 // 2, LANES), F32),
            pltpu.VMEM((2, keys, LANES), F32),
            pltpu.VMEM((2, keys, LANES), F32),
        ],
    )
    back = partner(to_beside, 1, count)
    gap = 3 * fold - half - row_count - half
    back = jnp.concatenate(
        [
            jnp.zeros((GROUP, row_count, LANES), BF),
            back[:, :half],
            jnp.zeros((GROUP, gap, LANES), BF),
            back[:, half:],
        ],
        1,
    )
    sent = (sent.astype(F32) + back.astype(F32)).astype(BF)
    left, sent = lax.optimization_barrier((left, sent))
    got = exchange(sent, count)

    d_proj_1, gain_attn_1, *grad_1 = on_core(
        global_finish_body,
        [((rows, 3 * width), BF), ((1, width), F32)] + [((row_count, width), BF)] * micro_count,
        (first, got, d_mid_1, *in_1, gain_attn, global_tables),
    )

    up_0 = to_other_section(grad_1, -1)
    d_mlp = jnp.concatenate(
        [jnp.where(lower, a, up_1[i * row_count :][:row_count]) for i, a in enumerate(up_0)]
    )
    across_mlp, beside_mlp = partner(d_mlp, 2, count), partner(d_mlp, 1, count)
    gain_mlp_0, d_mid_0, d_att_0, right = on_core(
        local_back_middle_body,
        [
            ((1, width), F32),
            ((rows, width), F32),
            ((rows, width), BF),
            ((rows, inner + width), BF),
        ],
        (*others, lower_flag, *up_0, middle_0, gate_up_0, gain_mlp, right_1),
        [pltpu.VMEM((hidden, width), BF)],
        [pltpu.VMEM] * len(others) + [pltpu.SMEM] + [pltpu.VMEM] * 6,
    )
    d_att_0, right, across_mlp = lax.optimization_barrier((d_att_0, right, across_mlp))
    across, beside = partner(right, 2, count), partner(right, 1, count)
    d_mlp = [d_mlp, beside_mlp, across_mlp, partner(across_mlp, 1, count)]
    out_near, out_far = first_hop(
        on_core(
            functools.partial(early_body, [((3 * shard_total, left_total), (0, width))]),
            three_parts((hidden_total, width)),
            (*d_mlp, *left),
        ),
        count,
    )
    dq_0, d_own, d_before, d_after = on_core(
        local_backward_body,
        [
            ((rows, width), BF),
            ((rows, 2 * width), F32),
            ((rows, 2 * width), BF),
            ((rows, 2 * width), BF),
        ],
        (q_0, *around_0, bias, total_0, d_att_0, local_tables),
    )
    from_after = lax.ppermute(d_before, "dp", down_pairs)
    from_before = lax.ppermute(d_after, "dp", up_pairs)
    d_proj, grad_0, gain_attn_sum = on_core(
        local_finish_body,
        [((rows + EXTRA, 3 * width), BF), ((rows, width), BF), ((1, width), F32)],
        (
            lower_flag, first, dq_0, d_own, from_after, from_before, local_tables, d_mid_0, in_0, gain_attn,
            gain_mlp_0, d_proj_1, gain_attn_1, gain_mlp_1,
        ),
        [pltpu.VMEM((1, width), F32)],
        [pltpu.SMEM] + [pltpu.VMEM] * 13,
    )
    across, d_proj, out_far = lax.optimization_barrier((across, d_proj, out_far))
    mlp_out_share = second_hop(out_near, out_far, count)
    right = [right, beside, across, partner(across, 1, count)]
    early_rows = shard_total * (inner // width + 1)
    near, far = first_hop(
        on_core(
            functools.partial(
                early_body,
                [
                    ((2 * shard_total, 3 * shard_total), (0, inner)),
                    ((shard_total, 2 * shard_total), (inner, inner + width)),
                ],
            ),
            three_parts((early_rows, width)),
            (*right, *left),
        ),
        count,
    )
    across, beside = partner(d_proj, 2, count), partner(d_proj, 1, count)
    across, far = lax.optimization_barrier((across, far))
    early = second_hop(near, far, count)
    late_in = (group_pos[None], d_proj, beside, across, partner(across, 1, count), *left)
    late = on_core(
        functools.partial(late_body, (0, shard_total)),
        three_parts((shard_total, 3 * width + LANES)),
        late_in,
        [pltpu.VMEM((width, LANES), F32)],
        [pltpu.SMEM] + [pltpu.VMEM] * (len(late_in) - 1),
    )
    late = second_hop(*first_hop(late, count), count)
    parts = [early[p * shard_total : (p + 1) * shard_total] for p in range(inner // width)]
    in_share = jnp.concatenate(parts, 1)
    attn_share = early[early_rows - shard_total :]
    gain_columns = late[:, 3 * width :]
    qkv_share, in_share, mlp_out_share, attn_share, gain_columns = (
        over_groups(item, count)
        for item in (late[:, : 3 * width], in_share, mlp_out_share, attn_share, gain_columns)
    )
    if count == GROUP:
        gains = jnp.stack([gain_columns[:, 0], gain_columns[:, 2]])
    else:
        gain_mlp_sum = jnp.where(lower, gain_mlp_0, gain_mlp_1)
        gains = lax.psum(jnp.concatenate([gain_attn_sum, gain_mlp_sum]), "dp")
        gains = lax.dynamic_slice_in_dim(gains, replica * shard, shard, 1)

    return (
        jnp.where(lower, jnp.concatenate(out_0), out_1).reshape(1, micro_count, row_count, width),
        jnp.where(lower, grad_0, jnp.concatenate(grad_1)).reshape(1, micro_count, row_count, width),
        qkv_share[None],
        attn_share[None],
        in_share[None],
        mlp_out_share[None],
        gains[:1],
        gains[1:],
    )


def solution(mesh):
    in_specs = (
        P(None, "dp", None),
        P(None, "dp"),
        P(None, "dp", None),
        P("section", "dp", None),
        P("section", "dp", None),
        P("section", "dp", None),
        P("section", "dp", None),
        P("section", "dp"),
        P("section", "dp"),
    )
    out_specs = (
        P("section", None, "dp", None),
        P("section", None, "dp", None),
        P("section", "dp", None),
        P("section", "dp", None),
        P("section", "dp", None),
        P("section", "dp", None),
        P("section", "dp"),
        P("section", "dp"),
    )
    return jax.shard_map(
        on_device, mesh=mesh, in_specs=in_specs, out_specs=out_specs, check_vma=False
    )
```

```python
import functools
import math

import jax
import jax.numpy as jnp
from jax import lax
from jax.experimental import pallas as pl
from jax.experimental.pallas import tpu as pltpu
from jax.sharding import PartitionSpec as P

HEAD_DIM = 64
GROUP = 16
HALF_WIN = 64
EXTRA = 16
LANES = 128
TILE = 256

local_log_base = math.log(10000.0)
global_log_base = math.log(160000.0)
masked_score = -1e30
SCALE = 1.0 / math.sqrt(HEAD_DIM)
BF = jnp.bfloat16
F32 = jnp.float32


def dot(left, right):
    return jnp.dot(left, right, preferred_element_type=F32)


def dot_bt(left, right):
    return lax.dot_general(left, right, (((1,), (1,)), ((), ())), preferred_element_type=F32)


def dot_at(left, right):
    return lax.dot_general(left, right, (((0,), (0,)), ((), ())), preferred_element_type=F32)


def moments(values):
    center = values - jnp.mean(values, -1, keepdims=True)
    scale = lax.rsqrt(jnp.mean(center * center, -1, keepdims=True) + 1e-05)
    return center * scale, scale


def norm_back(grad_out, gain_row, xhat, scale):
    scaled = grad_out * gain_row
    mean_grad = jnp.mean(scaled, -1, keepdims=True)
    mean_dot = jnp.mean(scaled * xhat, -1, keepdims=True)
    return (scaled - mean_grad - xhat * mean_dot) * scale


def angles(positions, log_base):
    half_dim = HEAD_DIM // 2
    fraction = (2 * jnp.arange(half_dim)).astype(F32) / HEAD_DIM
    inverse = jnp.exp(-fraction * log_base)
    table = positions.astype(F32)[:, None] * inverse[None, :]
    cosine, sine = jnp.cos(table), jnp.sin(table)
    none = jnp.zeros_like(sine)
    cosine = jnp.concatenate([cosine, cosine], 1)
    to_first = jnp.concatenate([-sine, none], 1)
    to_second = jnp.concatenate([none, sine], 1)
    return jnp.tile(jnp.stack([cosine, to_first, to_second]), (1, 2, 2))


def on_core(body, outs, args, scratch=(), spaces=None, out_spaces=None):
    return pl.pallas_call(
        body,
        out_shape=[jax.ShapeDtypeStruct(shape, dtype) for shape, dtype in outs],
        in_specs=[
            pl.BlockSpec(memory_space=space) for space in spaces or [pltpu.VMEM] * len(args)
        ],
        out_specs=[
            pl.BlockSpec(memory_space=space) for space in out_spaces or [pltpu.VMEM] * len(outs)
        ],
        scratch_shapes=scratch,
        cost_estimate=pl.CostEstimate(
            flops=2**10, bytes_accessed=2**10, transcendentals=0
        ),
        compiler_params=pltpu.CompilerParams(vmem_limit_bytes=48 * 2**20),
    )(*args)


def low_lanes():
    return lax.broadcasted_iota(jnp.int32, (1, LANES), 1) < HEAD_DIM


def swap(chunk):
    return pltpu.roll(chunk, HEAD_DIM, 1)


def chunks_of(rows):
    return [rows[:, c : c + LANES] for c in range(0, rows.shape[1], LANES)]


def rotate(chunk, tables):
    cosine, to_first, to_second = tables
    quarter = HEAD_DIM // 2
    return (
        chunk * cosine
        + pltpu.roll(chunk, LANES - quarter, 1) * to_first
        + pltpu.roll(chunk, quarter, 1) * to_second
    )


def unrotate(chunk, tables):
    cosine, to_first, to_second = tables
    quarter = HEAD_DIM // 2
    return (
        chunk * cosine
        - pltpu.roll(chunk, LANES - quarter, 1) * to_first
        - pltpu.roll(chunk, quarter, 1) * to_second
    )


def low_and_high(chunks):
    swapped = [swap(chunk) for chunk in chunks]
    low = [(swapped if h % 2 else chunks)[h // 2] for h in range(2 * len(chunks))]
    high = [(chunks if h % 2 else swapped)[h // 2] for h in range(2 * len(chunks))]
    return low, high


def targets():
    for d in range(GROUP):
        micro, chip, half = d // 8, d % 8 // 2, d % 2
        yield d, micro, 3 * chip + 2 * half, 3 * chip + 1, half


def pack_folded(chunks, ref, base):
    low, high = low_and_high(chunks)
    first = low_lanes()
    rows = chunks[0].shape[0] // 2
    half, fold = rows // 2, rows * 3 // 4
    for d, micro, own, shared, side in targets():
        start = micro * rows
        part = start + side * half
        upper = jnp.concatenate(
            [high[own][start + fold : start + rows], high[shared][part : part + half]], 0
        )
        ref[d, base : base + fold] = jnp.where(
            first, low[own][start : start + fold], upper
        ).astype(BF)


def pack_pairs(lefts, rights, ref):
    low, high = low_and_high(lefts)[0], low_and_high(rights)[1]
    first = low_lanes()
    rows = lefts[0].shape[0] // 2
    half = rows // 2
    for d, micro, own, shared, side in targets():
        start = micro * rows
        part = start + side * half
        ref[d, 0:rows] = jnp.where(
            first, low[own][start : start + rows], high[own][start : start + rows]
        ).astype(BF)
        ref[d, rows : rows + half] = jnp.where(
            first, low[shared][part : part + half], high[shared][part : part + half]
        ).astype(BF)


def unpack_folded(ref, base, rows):
    first = low_lanes()
    fold = rows * 3 // 4
    low, high = {}, {}
    shared_parts = {}
    for d, micro, own, shared, side in targets():
        block = ref[d, base : base + fold].astype(F32)
        mine = jnp.concatenate([block, swap(block[: rows - fold])], 0)
        if own % 2:
            high[micro, own] = swap(mine)
        else:
            low[micro, own] = mine
        shared_parts[micro, shared, side] = block[rows - fold :]
        if side:
            both = jnp.concatenate([shared_parts[micro, shared, 0], block[rows - fold :]], 0)
            if shared % 2:
                high[micro, shared] = both
            else:
                low[micro, shared] = swap(both)
    heads = GROUP // 4 * 3
    return [
        jnp.concatenate(
            [jnp.where(first, low[m, h], high[m, h + 1]) for m in range(2)], 0
        )
        for h in range(0, heads, 2)
    ]


def unpack_pairs(ref, rows):
    first = low_lanes()
    half = rows // 2
    pairs = {}
    parts = {}
    for d, micro, own, shared, side in targets():
        pairs[micro, own] = ref[d, 0:rows].astype(F32)
        parts[side] = ref[d, rows : rows + half].astype(F32)
        if side:
            pairs[micro, shared] = jnp.concatenate([parts[0], parts[1]], 0)
    heads = GROUP // 4 * 3
    lefts, rights = [], []
    for h in range(0, heads, 2):
        even, odd = [pairs[m, h] for m in range(2)], [pairs[m, h + 1] for m in range(2)]
        lefts.append(
            jnp.concatenate([jnp.where(first, a, swap(b)) for a, b in zip(even, odd)], 0)
        )
        rights.append(
            jnp.concatenate([jnp.where(first, swap(a), b) for a, b in zip(even, odd)], 0)
        )
    return lefts, rights


class Weights:
    def __init__(self, sources, mlp_out):
        self.sources = sources
        self.mlp_out = sources[-1]
        if len(sources) == 1:
            self.mlp_out = mlp_out
            unpack_rows(sources[0], mlp_out)

    def get(self, which):
        if which == 2:
            return self.mlp_out[...]
        if len(self.sources) > 1:
            return self.sources[which][...]
        (wide,) = self.sources
        width = wide.shape[0]
        inner = 2 * self.mlp_out.shape[0]
        return wide[:, width : width + inner] if which else wide[:, :width]


def first_block(pair):
    return -(-pair // 32) * 16


def packed_pieces(shard, rows, width):
    yield 0, shard, 0, width, 0, 0
    rest = rows - shard
    side = width // 3
    yield 0, rest, width, 2 * side, shard, 0
    yield rest, 16, width, side, shard, 2 * side
    yield rest, 16, width + side, side, shard + 16, 2 * side


def unpack_rows(wide, mlp_out):
    hidden, width = mlp_out.shape
    shard = wide.shape[0] // GROUP
    start = wide.shape[1] - width - 2 * (width // 3)
    pair = 2 * hidden // GROUP
    upper = first_block(pair)
    for d in range(GROUP):
        low = d // 2 * pair + d % 2 * upper
        have = pair - upper if d % 2 else upper
        for row, rows, column, columns, to_row, to_column in packed_pieces(shard, upper, width):
            rows = min(rows, have - to_row)
            if rows > 0:
                mlp_out[low + to_row : low + to_row + rows, to_column : to_column + columns] = wide[
                    d * shard + row : d * shard + row + rows, start + column : start + column + columns
                ]


def stack_body(odd_ref, attn_ref, mlp_in_ref, own_ref, beside_ref, out_ref):
    shard, width = attn_ref.shape
    inner = mlp_in_ref.shape[1]
    out_ref[:, :width] = attn_ref[...]
    out_ref[:, width : width + inner] = mlp_in_ref[...]
    own, beside = own_ref[...].astype(F32), beside_ref[...].astype(F32)
    moved = beside.shape[0]
    even = jnp.concatenate([own, beside], 0)
    odd = jnp.concatenate([own[moved:], beside, beside], 0)
    block = jnp.where(odd_ref[0] == 1, odd, even).astype(BF)
    start = width + inner
    for row, rows, column, columns, from_row, from_column in packed_pieces(
        shard, block.shape[0], width
    ):
        out_ref[row : row + rows, start + column : start + column + columns] = block[
            from_row : from_row + rows, from_column : from_column + columns
        ]


def mlp_forward(layer_in, attended, gain, weights):
    middle = layer_in + dot(attended, weights.get(0))
    xhat, _ = moments(middle)
    normed = (xhat * gain).astype(BF)
    gate_up = dot(normed, weights.get(1))
    half = gate_up.shape[1] // 2
    gate, up = gate_up[:, :half], gate_up[:, half:]
    cdf = 0.5 * (1.0 + lax.erf(gate * math.sqrt(0.5)))
    mixed = (gate * cdf * up).astype(BF)
    result = (middle + dot(mixed, weights.get(2))).astype(BF)
    return middle, normed, gate, up, mixed, result


def mlp_backward(upstream, middle, gate, up, gain, weights):
    d_mixed = dot_bt(upstream, weights.get(2))
    cdf = 0.5 * (1.0 + lax.erf(gate * math.sqrt(0.5)))
    density = jnp.exp(-0.5 * gate * gate) * (1.0 / math.sqrt(2.0 * math.pi))
    d_gate = d_mixed * up * (cdf + gate * density)
    d_up = d_mixed * gate * cdf
    d_gate_up = jnp.concatenate([d_gate.astype(BF), d_up.astype(BF)], 1)
    d_normed = dot_bt(d_gate_up, weights.get(1))
    xhat, scale = moments(middle)
    gain_grad = jnp.sum(d_normed * xhat, 0, keepdims=True)
    d_middle = upstream.astype(F32) + norm_back(d_normed, gain, xhat, scale)
    d_attn = d_middle.astype(BF)
    d_attended = dot_bt(d_attn, weights.get(0))
    return d_gate_up, gain_grad, d_middle, d_attn, d_attended


def project(xhat, gain, first_ref, table_ref, normed_ref):
    width = xhat.shape[1]
    normed = (xhat * gain).astype(BF)
    normed_ref[...] = normed
    tables = [table_ref[i] for i in range(3)]
    results = [dot(normed, first_ref[:, c * width : (c + 1) * width]) for c in range(3)]
    queries, keys, values = chunks_of(results[0]), chunks_of(results[1]), results[2]
    return [rotate(c, tables) for c in queries], [rotate(c, tables) for c in keys], values


def input_backward(d_middle, d_projected, x, gain_ref, first_ref, gain_out_ref):
    d_normed = dot_bt(d_projected, first_ref[:, : d_projected.shape[1]])
    xhat, scale = moments(x)
    gain_out_ref[...] = jnp.sum(d_normed * xhat, 0, keepdims=True)
    return (d_middle + norm_back(d_normed, gain_ref[...], xhat, scale)).astype(BF)


def joined(refs):
    return jnp.concatenate([ref[...] for ref in refs], 0)


def store_chunks(refs, rows):
    size = rows.shape[0] // len(refs)
    for i, ref in enumerate(refs):
        ref[...] = rows[i * size : (i + 1) * size]


def message_body(w_ref, attn_ref, mlp_ref, ids_ref, out_ref, rows_scr, ids_scr):
    shard, columns = w_ref.shape
    micro_count, row_count = ids_ref.shape
    out_ref[:, :columns] = w_ref[...]
    rows_scr[...] = jnp.zeros_like(rows_scr)
    ids_scr[...] = jnp.zeros_like(ids_scr)
    rows_scr[0:1, :shard] = attn_ref[...].astype(F32)
    rows_scr[1:2, :shard] = mlp_ref[...].astype(F32)
    ids_scr[:micro_count, :row_count] = ids_ref[...].astype(F32)
    runs = -(-row_count // shard)
    for run in range(runs):
        turned = ids_scr[...]
        if run:
            turned = pltpu.roll(turned, LANES - run * shard, 1)
        for micro in range(micro_count):
            row = 2 + micro * runs + run
            rows_scr[row : row + 1] = turned[micro : micro + 1]
    out_ref[:, columns:] = rows_scr[...].T[:shard].astype(BF)


def local_project_body(first_ref, x_ref, table_ref, extra_ref, normed_ref, q_ref, kv_ref):
    xhat, _ = moments(x_ref[...].astype(F32))
    extra = first_ref[:, first_ref.shape[1] - LANES :].astype(F32).T
    extra_ref[...] = extra[: extra_ref.shape[0]]
    queries, keys, values = project(xhat, extra[:1], first_ref, table_ref, normed_ref)
    width = values.shape[1]
    for j, (q, k) in enumerate(zip(queries, keys)):
        q_ref[:, LANES * j : LANES * (j + 1)] = q.astype(BF)
        kv_ref[:, LANES * j : LANES * (j + 1)] = k.astype(BF)
    kv_ref[:, width:] = values.astype(BF)


def two_heads(chunk):
    first = low_lanes()
    wide = chunk.astype(F32)
    return jnp.concatenate([jnp.where(first, wide, 0.0), jnp.where(first, 0.0, wide)], 0)


def pick_heads(rows):
    half = rows.shape[0] // 2
    return jnp.where(low_lanes(), rows[:half], rows[half:])


def local_parts(q_ref, before_ref, own_ref, after_ref):
    rows = q_ref.shape[0] // 2
    width = q_ref.shape[1]
    for micro in range(2):
        for j in range(width // LANES):
            here = slice(micro * rows, (micro + 1) * rows)
            lanes = slice(LANES * j, LANES * (j + 1))
            more = slice(width + LANES * j, width + LANES * (j + 1))
            keys, values = (
                jnp.concatenate([ref[here, part] for ref in (before_ref, own_ref, after_ref)], 0)
                for part in (lanes, more)
            )
            queries = (two_heads(q_ref[here, lanes]) * SCALE).astype(BF)
            yield micro * (width // LANES) + j, micro, here, lanes, more, queries, keys, values


def local_forward_body(q_ref, before_ref, own_ref, after_ref, bias_ref, att_ref, total_ref):
    parts = local_parts(q_ref, before_ref, own_ref, after_ref)
    for index, micro, here, lanes, _, queries, keys, values in parts:
        scores = dot_bt(keys, queries) + bias_ref[micro]
        peak = jnp.max(scores, 0, keepdims=True)
        weights = jnp.exp(scores - peak)
        total = jnp.sum(weights, 0, keepdims=True)
        total_ref[index] = peak + jnp.log(total)
        probs = (weights * (1.0 / total)).astype(BF)
        att_ref[here, lanes] = pick_heads(dot_at(probs, values)).astype(BF)


def local_backward_body(
    q_ref, before_ref, own_ref, after_ref, bias_ref, total_ref, d_ref, table_ref,
    dq_ref, d_own_ref, d_before_ref, d_after_ref,
):
    tables = [table_ref[i] for i in range(3)]
    parts = local_parts(q_ref, before_ref, own_ref, after_ref)
    rows = q_ref.shape[0] // 2
    for index, micro, here, lanes, more, queries, keys, values in parts:
        d_out = two_heads(d_ref[here, lanes]).astype(BF)
        probs = jnp.exp(dot_bt(keys, queries) + bias_ref[micro] - total_ref[index])
        d_probs = dot_bt(values, d_out)
        product = probs * d_probs
        delta = jnp.sum(product, 0, keepdims=True)
        d_scores = (product - probs * delta).astype(BF)
        d_queries = pick_heads(dot_at(d_scores, keys)) * SCALE
        local_tables = [table[here] for table in tables]
        dq_ref[here, lanes] = unrotate(d_queries, local_tables).astype(BF)
        for part, grads in ((lanes, dot(d_scores, queries)), (more, dot(probs.astype(BF), d_out))):
            d_before_ref[here, part] = grads[:rows].astype(BF)
            d_own_ref[here, part] = grads[rows : 2 * rows]
            d_after_ref[here, part] = grads[2 * rows :].astype(BF)


def local_finish_body(
    lower_ref, first_ref, dq_ref, own_ref, low_ref, high_ref, table_ref, d_middle_ref, x_ref, gain_ref,
    gain_mlp_ref, other_ref, other_attn_ref, other_mlp_ref, low_out_ref, high_out_ref, grad_ref, gain_attn_ref,
    gain_scr, out_ref,
):
    rows, width = dq_ref.shape

    @pl.when(lower_ref[0] == 1)
    def _():
        tables = [table_ref[i] for i in range(3)]
        total = own_ref[...] + low_ref[...].astype(F32) + high_ref[...].astype(F32)
        out_ref[:, :width] = dq_ref[...]
        for j, chunk in enumerate(chunks_of(total[:, :width])):
            start = width + LANES * j
            out_ref[:, start : start + LANES] = unrotate(chunk, tables).astype(BF)
        out_ref[:, 2 * width :] = total[:, width:].astype(BF)
        grad_ref[...] = input_backward(
            d_middle_ref[...], out_ref[...], x_ref[...].astype(F32), gain_ref, first_ref, gain_scr
        )

    @pl.when(lower_ref[0] == 0)
    def _():
        out_ref[...] = other_ref[...]
        grad_ref[...] = jnp.zeros_like(grad_ref)
        gain_scr[...] = other_attn_ref[...]

    gain_attn_ref[...] = gain_scr[...]
    gain_mlp = jnp.where(lower_ref[0] == 1, gain_mlp_ref[...], other_mlp_ref[...])
    index = lax.broadcasted_iota(jnp.int32, (EXTRA, width), 0)
    tail = jnp.zeros((EXTRA, width), F32)
    for row, gain in ((0, gain_scr[...]), (2, gain_mlp)):
        high = gain.astype(BF).astype(F32)
        tail = jnp.where(index == row, high, tail)
        tail = jnp.where(index == row + 1, gain - high, tail)
    half = rows // 2
    low_out_ref[...] = out_ref[:half]
    high_out_ref[:half] = out_ref[half:]
    high_out_ref[half:] = jnp.zeros((EXTRA, out_ref.shape[1]), BF)
    high_out_ref[half:, :width] = tail.astype(BF)


def local_middle_body(*refs):
    sources, refs = refs[:-10], refs[-10:]
    x_ref, att_ref, gain_ref, normed_ref, mixed_ref, middle_ref, gate_up_ref = refs[:7]
    weights = Weights(sources, refs[9])
    middle, normed, gate, up, mixed, result = mlp_forward(
        x_ref[...].astype(F32), att_ref[...], gain_ref[...], weights
    )
    store_chunks(refs[7:9], result)
    normed_ref[...] = normed
    mixed_ref[...] = mixed
    middle_ref[...] = middle
    half = gate.shape[1]
    gate_up_ref[:, :half] = gate
    gate_up_ref[:, half:] = up


def local_back_middle_body(*refs):
    sources, refs = refs[:-13], refs[-13:]
    lower_ref, low_ref, high_ref, middle_ref, gate_up_ref, gain_ref, other_ref = refs[:7]
    gain_out_ref, d_middle_ref, d_att_ref, right_low_ref, right_high_ref = refs[7:12]
    weights = Weights(sources, refs[12])
    half = gate_up_ref.shape[1] // 2
    upstream = joined([low_ref, high_ref])
    d_gate_up, gain_grad, d_middle, d_attn, d_attended = mlp_backward(
        upstream, middle_ref[...], gate_up_ref[:, :half], gate_up_ref[:, half:],
        gain_ref[...], weights,
    )
    gain_out_ref[...] = gain_grad
    d_middle_ref[...] = d_middle
    d_att_ref[...] = d_attended.astype(BF)

    @pl.when(lower_ref[0] == 1)
    def _():
        store_chunks(
            (right_low_ref, right_high_ref), jnp.concatenate([d_gate_up, d_attn], 1)
        )

    @pl.when(lower_ref[0] == 0)
    def _():
        store_chunks((right_low_ref, right_high_ref), other_ref[...])


def global_project_body(first_ref, low_ref, high_ref, gain_ref, table_ref, normed_ref, sent_ref):
    xhat, _ = moments(joined([low_ref, high_ref]).astype(F32))
    queries, keys, values = project(xhat, gain_ref[...], first_ref, table_ref, normed_ref)
    pack_pairs(queries, keys, sent_ref)
    pack_folded(chunks_of(values), sent_ref, sent_ref.shape[1] * 2 // 3)


def flat(blocks):
    return blocks.reshape(-1, LANES)


def own_unfolded(ref, base, rows):
    fold = rows * 3 // 4
    block = ref[:, base : base + fold].astype(F32)
    rest = swap(flat(block[:, : rows - fold])).reshape(GROUP, rows - fold, LANES)
    return flat(jnp.concatenate([block, rest], 1))


def shared_unfolded(ref, start, rows):
    return swap(flat(ref[:, start : start + rows // 2].astype(F32)))


def fill_heads(got_ref, other_ref, own_seg_ref, shared_seg_ref, q_scr, k_scr, v_scr):
    rows = got_ref.shape[1] * 4 // 9
    half = rows // 2
    first = low_lanes()
    lane = lax.broadcasted_iota(jnp.int32, (1, LANES), 1) - HEAD_DIM
    own = flat(got_ref[:, 0:rows].astype(F32))
    shared = flat(got_ref[:, rows : rows + half].astype(F32))
    other = flat(other_ref[:, 0:half].astype(F32))
    count = own.shape[0]
    own_hit = lane == own_seg_ref[...]
    shared_hit = lane == shared_seg_ref[...]
    both = jnp.concatenate([shared, other], 0)
    for start, pairs, hit in (
        (0, own, own_hit),
        (count, shared, shared_hit[: count // 2]),
    ):
        marked = jnp.where(hit, 1.0, 0.0)
        q_scr[start : start + pairs.shape[0]] = jnp.where(first, pairs * SCALE, marked).astype(BF)
    for unit, pairs, hit in ((0, own, own_hit), (1, both, shared_hit)):
        marked = jnp.where(hit, 0.0, masked_score)
        k_scr[unit] = jnp.where(first, swap(pairs), marked).astype(BF)
    base = rows + half
    v_scr[0] = jnp.where(first, own_unfolded(got_ref, base, rows), 0.0).astype(BF)
    start = base + rows - rows * 3 // 4
    shared_v = jnp.concatenate(
        [shared_unfolded(got_ref, start, rows), shared_unfolded(other_ref, half, rows)], 0
    )
    v_scr[1] = jnp.where(first, shared_v, 0.0).astype(BF)


def fold_out(own, shared, rows, ref, base):
    fold = rows * 3 // 4
    blocks = own.reshape(GROUP, rows, LANES)
    swapped = swap(own).reshape(GROUP, rows, LANES)
    upper = jnp.concatenate(
        [swapped[:, fold:], swap(shared).reshape(GROUP, rows // 2, LANES)], 1
    )
    ref[:, base : base + fold] = jnp.where(low_lanes(), blocks[:, :fold], upper).astype(BF)


def global_forward_body(
    got_ref, other_ref, own_seg_ref, shared_seg_ref, out_ref, total_ref,
    q_scr, k_scr, v_scr, vt_scr, o_scr,
):
    fill_heads(got_ref, other_ref, own_seg_ref, shared_seg_ref, q_scr, k_scr, v_scr)
    for unit in range(2):
        vt_scr[unit] = v_scr[unit].astype(F32).T.astype(BF)
    count = k_scr.shape[1]

    def step(tile, carry):
        unit = tile // (count // TILE)
        rows = pl.ds(pl.multiple_of(tile * TILE, TILE), TILE)
        scores = dot_bt(k_scr[unit], q_scr[rows])
        peak = jnp.max(scores, 0, keepdims=True)
        weights = jnp.exp(scores - peak)
        total = jnp.sum(weights, 0, keepdims=True)
        total_ref[tile] = peak + jnp.log(total)
        out = dot(vt_scr[unit], weights.astype(BF)) * (1.0 / total)
        o_scr[rows] = out.T
        return carry

    lax.fori_loop(0, q_scr.shape[0] // TILE, step, 0)
    rows = got_ref.shape[1] * 4 // 9
    fold_out(o_scr[:count], o_scr[count:], rows, out_ref, 0)


def global_backward_body(
    got_ref, other_ref, own_seg_ref, shared_seg_ref, total_ref, d_ref, sent_ref, to_other_ref,
    q_scr, k_scr, v_scr, kt_scr, d_scr, dq_scr, dk_scr, dv_scr,
):
    fill_heads(got_ref, other_ref, own_seg_ref, shared_seg_ref, q_scr, k_scr, v_scr)
    first = low_lanes()
    rows = got_ref.shape[1] * 4 // 9
    half = rows // 2
    for unit in range(2):
        keys = jnp.where(first, k_scr[unit].astype(F32), 0.0)
        kt_scr[unit] = keys.T.astype(BF)
    count = k_scr.shape[1]
    d_scr[:count] = jnp.where(first, own_unfolded(d_ref, 0, rows), 0.0).astype(BF)
    d_scr[count:] = jnp.where(
        first, shared_unfolded(d_ref, rows - rows * 3 // 4, rows), 0.0
    ).astype(BF)
    dk_scr[...] = jnp.zeros_like(dk_scr)
    dv_scr[...] = jnp.zeros_like(dv_scr)

    def step(tile, carry):
        unit = tile // (count // TILE)
        here = pl.ds(pl.multiple_of(tile * TILE, TILE), TILE)
        queries, d_out = q_scr[here], d_scr[here]
        probs = jnp.exp(dot_bt(k_scr[unit], queries) - total_ref[tile])
        d_probs = dot_bt(v_scr[unit], d_out)
        product = probs * d_probs
        delta = jnp.sum(product, 0, keepdims=True)
        d_scores = (product - probs * delta).astype(BF)
        dv_scr[unit] += dot(probs.astype(BF), d_out)
        dk_scr[unit] += dot(d_scores, queries)
        dq_scr[here] = dot(kt_scr[unit], d_scores).T * SCALE
        return carry

    lax.fori_loop(0, q_scr.shape[0] // TILE, step, 0)
    mine = count // 2
    own = jnp.where(first, dq_scr[:count], swap(dk_scr[0]))
    sent_ref[:, 0:rows] = own.reshape(GROUP, rows, LANES).astype(BF)
    shared_k, shared_v = dk_scr[1], dv_scr[1]
    shared = jnp.where(first, dq_scr[count:], swap(shared_k[:mine]))
    sent_ref[:, rows : rows + half] = shared.reshape(GROUP, half, LANES).astype(BF)
    fold_out(dv_scr[0], shared_v[:mine], rows, sent_ref, rows + half)
    for place, grads in enumerate((shared_k, shared_v)):
        other = jnp.where(first, 0.0, swap(grads[mine:])).reshape(GROUP, half, LANES)
        to_other_ref[:, place * half : (place + 1) * half] = other.astype(BF)


def global_middle_body(*refs):
    sources, refs = refs[:-14], refs[-14:]
    got_ref, low_ref, high_ref, up_ref, gain_ref, out_ref, att_ref, normed_ref, mixed_ref = refs[:9]
    right_ref, gain_out_ref, d_middle_ref, sent_ref = refs[9:13]
    weights = Weights(sources, refs[13])
    rows = low_ref.shape[0]
    attended = jnp.concatenate([c.astype(BF) for c in unpack_folded(got_ref, 0, rows)], 1)
    att_ref[...] = attended
    gain = gain_ref[...]
    middle, normed, gate, up, mixed, result = mlp_forward(
        joined([low_ref, high_ref]).astype(F32), attended, gain, weights
    )
    out_ref[...] = result
    normed_ref[...] = normed
    mixed_ref[...] = mixed
    d_gate_up, gain_grad, d_middle, d_attn, d_attended = mlp_backward(
        up_ref[...], middle, gate, up, gain, weights
    )
    right_ref[:, : d_gate_up.shape[1]] = d_gate_up
    right_ref[:, d_gate_up.shape[1] :] = d_attn
    gain_out_ref[...] = gain_grad
    d_middle_ref[...] = d_middle
    pack_folded(chunks_of(d_attended), sent_ref, 0)


def global_finish_body(
    first_ref, got_ref, d_middle_ref, low_ref, high_ref, gain_ref, table_ref,
    d_proj_ref, gain_out_ref, *grad_refs,
):
    tables = [table_ref[i] for i in range(3)]
    x = joined([low_ref, high_ref]).astype(F32)
    rows = low_ref.shape[0]
    d_queries, d_keys = unpack_pairs(got_ref, rows)
    d_values = unpack_folded(got_ref, rows * 3 // 2, rows)
    parts = [unrotate(c, tables).astype(BF) for c in d_queries + d_keys]
    d_projected = jnp.concatenate(parts + [c.astype(BF) for c in d_values], 1)
    d_proj_ref[...] = d_projected
    store_chunks(
        grad_refs,
        input_backward(d_middle_ref[...], d_projected, x, gain_ref, first_ref, gain_out_ref),
    )


def neighbours(count, step):
    return [
        (i, i + step)
        for i in range(count)
        if 0 <= i + step < count and i // GROUP == (i + step) // GROUP
    ]


def exchange(blocks, count):
    groups = [list(range(s, s + GROUP)) for s in range(0, count, GROUP)]
    return lax.all_to_all(blocks, "dp", 0, 0, axis_index_groups=groups)


def to_other_section(chunks, step):
    pairs = [(0, 1)] if step > 0 else [(1, 0)]
    return [lax.ppermute(rows, "section", pairs) for rows in chunks]


def partner(rows, apart, count):
    return lax.ppermute(rows, "dp", [(i, i ^ apart) for i in range(count)])


def gather_rows(piece, group_pos, count):
    pieces = {0: piece}
    for apart in (4, 8, 12):
        pieces[apart] = partner(piece, apart, count)
    for apart in (0, 4, 8, 12):
        pieces[apart + 2] = partner(pieces[apart], 2, count)
    for apart in range(0, GROUP, 2):
        pieces[apart + 1] = partner(pieces[apart], 1, count)
    whole = jnp.zeros((GROUP,) + piece.shape, piece.dtype)
    for apart, item in pieces.items():
        start = (group_pos ^ apart,) + (0,) * piece.ndim
        whole = lax.dynamic_update_slice(whole, item[None], start)
    if count > GROUP:
        groups = [list(range(s, count, GROUP)) for s in range(GROUP)]
        whole = lax.all_gather(whole, "dp", axis=0, tiled=True, axis_index_groups=groups)
    return whole.reshape(-1, piece.shape[-1]), pieces[2]


def plane_rows(rows, group_pos, count):
    parts = rows.reshape(count // GROUP, 4, 4, *rows.shape[1:])
    place, plane = group_pos % 4, group_pos // 4
    taken = []
    for apart in range(4):
        block = lax.dynamic_index_in_dim(parts, place ^ apart, 2, keepdims=False)
        block = jnp.stack(
            [lax.dynamic_index_in_dim(block, plane ^ z, 1, keepdims=False) for z in range(4)]
        )
        taken.append(partner(block, apart, count) if apart else block)
    return taken


def left_body(lower_ref, place_ref, *refs):
    refs, out_ref = refs[:-1], refs[-1]
    base = 0
    for first_ref, second_ref in zip(refs[0::2], refs[1::2]):
        rows = jnp.where(lower_ref[0] == 1, first_ref[...].astype(F32), second_ref[...].astype(F32))
        turned = rows.T
        size = turned.shape[0] // GROUP
        for d in range(GROUP):
            side = d % 4 ^ place_ref[0] % 4
            plane = d // 4 ^ place_ref[0] // 4
            out_ref[side, plane, base : base + size] = turned[d * size : (d + 1) * size].astype(BF)
        base += size


def left_rows_of(refs, rows):
    start, end = rows
    parts = [
        jnp.concatenate([ref[p, start:end].astype(F32) for p in range(4)], 0).astype(BF) for ref in refs
    ]
    return jnp.concatenate(parts, 1)


def by_plane(result, base, outs, columns=slice(None)):
    keep, keep_far, send = outs
    rows = result.shape[0] // 4
    half = send.shape[0] // 2
    here = slice(base, base + rows)
    keep[here, columns] = result[:rows]
    keep_far[here, columns] = result[2 * rows : 3 * rows]
    send[here, columns] = result[rows : 2 * rows].astype(BF)
    send[half + base : half + base + rows, columns] = result[3 * rows :].astype(BF)


def early_body(terms, *refs):
    refs, outs = refs[:-3], refs[-3:]
    rights, lefts = refs[:-4], refs[-4:]
    width = outs[0].shape[1]
    base = 0
    for rows, (start, end) in terms:
        right = jnp.concatenate([ref[:, start:end] for ref in rights], 0)
        result = dot(left_rows_of(lefts, rows), right)
        for column in range(0, end - start, width):
            by_plane(result[:, column : column + width], base, outs)
            base += result.shape[0] // 4


def late_body(rows, place_ref, *refs):
    refs, outs, scr = refs[:-4], refs[-4:-1], refs[-1]
    rights, lefts = refs[:-4], refs[-4:]
    columns = rights[0].shape[1]
    width = columns // 3
    size = outs[0].shape[0]
    low, high = rights[0::2], rights[1::2]
    half = low[0].shape[0]
    right = jnp.concatenate([part for a, b in zip(low, high) for part in (a[...], b[:half])], 0)
    by_plane(dot(left_rows_of(lefts, rows), right), 0, outs, slice(0, columns))
    tail = sum(ref[half:, :width].astype(F32) for ref in high)
    both = jnp.concatenate([tail, jnp.zeros((LANES - EXTRA, width), F32)], 0).T
    lane = lax.broadcasted_iota(jnp.int32, (1, LANES), 1)
    lows = pltpu.roll(both, LANES - 1, 1)
    scr[...] = jnp.where(lane % 2 == 0, both + lows, 0.0)
    gains = []
    for plane in range(4):
        d = (place_ref[0] // 4 ^ plane) * 4 + place_ref[0] % 4
        gains.append(scr[pl.ds(pl.multiple_of(d * size, 16), size)])
    by_plane(jnp.concatenate(gains, 0), 0, outs, slice(columns, columns + LANES))


def three_parts(shape):
    return [(shape, F32), (shape, F32), ((2 * shape[0], shape[1]), BF)]


def first_hop(blocks, count):
    keep, keep_far, send = blocks
    got = partner(send, 4, count)
    half = keep.shape[0]
    return keep + got[:half].astype(F32), (keep_far + got[half:].astype(F32)).astype(BF)


def second_hop(near, far, count):
    return near + partner(far, 8, count).astype(F32)


def over_groups(rows, count):
    if count == GROUP:
        return rows
    apart = [list(range(s, count, GROUP)) for s in range(GROUP)]
    rows = rows.reshape(count // GROUP, -1, rows.shape[1])
    return lax.psum_scatter(rows, "dp", scatter_dimension=0, axis_index_groups=apart)


def on_device(
    tokens_in,
    segment_ids,
    out_grad,
    qkv_weight,
    attn_out_weight,
    mlp_in_weight,
    mlp_out_weight,
    attn_gain,
    mlp_gain,
):
    lower = lax.axis_index("section") == 0
    lower_flag = lower.astype(jnp.int32)[None]
    shard_total = qkv_weight.shape[1] * (lax.axis_size("dp") // GROUP)
    hidden_total = mlp_out_weight.shape[1] * (lax.axis_size("dp") // GROUP)
    count = lax.axis_size("dp")
    replica = lax.axis_index("dp")
    group_pos = replica % GROUP
    micro_count, row_count, width = tokens_in.shape
    shard = qkv_weight.shape[1]
    runs = -(-row_count // shard)
    (message,) = on_core(
        message_body,
        [((shard, 3 * width + LANES), BF)],
        (qkv_weight[0], attn_gain, mlp_gain, segment_ids),
        [pltpu.VMEM((LANES, LANES), F32), pltpu.VMEM((8, LANES), F32)],
    )
    first, early_piece = gather_rows(message, group_pos, count)
    inner = mlp_in_weight.shape[2]
    hidden = mlp_out_weight.shape[1] * count
    if count == GROUP:
        moved = first_block(2 * mlp_out_weight.shape[1]) - mlp_out_weight.shape[1]
        beside = partner(mlp_out_weight[0, :moved], 1, count)
        (stacked,) = on_core(
            stack_body,
            [((shard, width + inner + width + 2 * (width // 3)), BF)],
            (
                (replica % 2)[None],
                attn_out_weight[0],
                mlp_in_weight[0],
                mlp_out_weight[0],
                beside,
            ),
            (),
            [pltpu.SMEM] + [pltpu.VMEM] * 4,
        )
        stacked, _ = lax.optimization_barrier((stacked, early_piece))
        others = [lax.all_gather(stacked, "dp", axis=0, tiled=True)]
    else:
        others = [
            lax.all_gather(item[0], "dp", axis=0, tiled=True)
            for item in (attn_out_weight, mlp_in_weight, mlp_out_weight)
        ]
    positions = group_pos * row_count + jnp.arange(row_count)
    local_tables = angles(positions, local_log_base)
    global_tables = angles(positions, global_log_base)

    rows = micro_count * row_count
    pairs = rows * width // (row_count * LANES)
    in_0 = tokens_in.reshape(rows, width)
    extra_rows = -(-(2 + micro_count * runs) // 8) * 8
    extra, normed_0, q_0, kv_0 = on_core(
        local_project_body,
        [
            ((extra_rows, width), F32),
            ((rows, width), BF),
            ((rows, width), BF),
            ((rows, 2 * width), BF),
        ],
        (first, in_0, local_tables),
    )
    gain_attn, gain_mlp = extra[:1], extra[1:2]
    all_ids = extra[2 : 2 + micro_count * runs].reshape(micro_count, runs, count, shard)
    all_ids = lax.dynamic_slice_in_dim(all_ids, replica - group_pos, GROUP, 2)
    all_ids = all_ids.swapaxes(1, 2).reshape(micro_count, GROUP, runs * shard)[..., :row_count]
    segments = all_ids.reshape(micro_count, GROUP * row_count).astype(jnp.int32)

    key_pos = positions[0] - row_count + jnp.arange(3 * row_count)
    around = jnp.pad(segments, ((0, 0), (row_count, row_count)), constant_values=-1)
    key_seg = lax.dynamic_slice_in_dim(around, group_pos * row_count, 3 * row_count, 1)
    visible = (key_seg[:, :, None] == segment_ids[:, None, :]) & (
        jnp.abs(positions[None, :] - key_pos[:, None]) <= HALF_WIN
    )[None]
    bias = jnp.tile(jnp.where(visible, 0.0, masked_score), (1, 1, 2))

    own_seg = lax.dynamic_index_in_dim(segments, group_pos // 8, 0, keepdims=False)
    halves = own_seg.reshape(GROUP, 2, row_count // 2)
    mine = lax.dynamic_index_in_dim(halves, group_pos % 2, 1, keepdims=False).reshape(-1)
    theirs = lax.dynamic_index_in_dim(halves, 1 - group_pos % 2, 1, keepdims=False).reshape(-1)
    shared_seg = jnp.concatenate([mine, theirs])[:, None]
    own_seg = own_seg[:, None]

    up_pairs, down_pairs = neighbours(count, 1), neighbours(count, -1)
    around_0 = (
        lax.ppermute(kv_0, "dp", up_pairs),
        kv_0,
        lax.ppermute(kv_0, "dp", down_pairs),
    )
    att_0, total_0 = on_core(
        local_forward_body,
        [((rows, width), BF), ((pairs, 1, LANES), F32)],
        (q_0, *around_0, bias),
    )
    n2_0, mixed_0, middle_0, gate_up_0, *out_0 = on_core(
        local_middle_body,
        [
            ((rows, width), BF),
            ((rows, hidden), BF),
            ((rows, width), F32),
            ((rows, inner), F32),
        ]
        + [((row_count, width), BF)] * micro_count,
        (*others, in_0, att_0, gain_mlp),
        [pltpu.VMEM((hidden, width), BF)],
    )

    in_1 = to_other_section(out_0, 1)
    fold = row_count * 3 // 4
    half = row_count // 2
    normed_1, sent = on_core(
        global_project_body,
        [((rows, width), BF), ((GROUP, 3 * fold, LANES), BF)],
        (first, *in_1, gain_attn, global_tables),
    )
    got = exchange(sent, count)
    beside = jnp.concatenate(
        [got[:, row_count : row_count + half], got[:, 3 * fold - half :]], 1
    )
    beside = partner(beside, 1, count)
    keys = GROUP * row_count
    tiles = keys * 3 // 2 // TILE
    head_scratch = [
        pltpu.VMEM((keys * 3 // 2, LANES), BF),
        pltpu.VMEM((2, keys, LANES), BF),
        pltpu.VMEM((2, keys, LANES), BF),
        pltpu.VMEM((2, LANES, keys), BF),
    ]
    folded, total_1 = on_core(
        global_forward_body,
        [((GROUP, fold, LANES), BF), ((tiles, 1, TILE), F32)],
        (got, beside, own_seg, shared_seg),
        head_scratch + [pltpu.VMEM((keys * 3 // 2, LANES), F32)],
    )
    folded = exchange(folded, count)

    up_1 = out_grad.reshape(rows, width)
    out_1, att_1, n2_1, mixed_1, right_1, gain_mlp_1, d_mid_1, sent = on_core(
        global_middle_body,
        [
            ((rows, width), BF),
            ((rows, width), BF),
            ((rows, width), BF),
            ((rows, hidden), BF),
            ((rows, inner + width), BF),
            ((1, width), F32),
            ((rows, width), F32),
            ((GROUP, fold, LANES), BF),
        ],
        (*others, folded, *in_1, up_1, gain_mlp),
        [pltpu.VMEM((hidden, width), BF)],
    )
    d_folded = exchange(sent, count)
    pairs = ((normed_0, normed_1), (att_0, att_1), (n2_0, n2_1), (mixed_0, mixed_1))
    left_total = 3 * shard_total + hidden_total
    if count == GROUP:
        (left,) = on_core(
            left_body,
            [((4, 4, left_total, rows), BF)],
            (lower_flag, group_pos[None], *(item for pair in pairs for item in pair)),
            (),
            [pltpu.SMEM] * 2 + [pltpu.VMEM] * 8,
        )
        left, d_folded = lax.optimization_barrier((left, d_folded))
    else:
        left = [
            plane_rows(jnp.where(lower, a, b).T.reshape(count, -1, rows), group_pos, count)
            for a, b in pairs
        ]
        left = [jnp.concatenate([i.reshape(4, -1, rows) for i in items], 1) for items in zip(*left)]
    sent, to_beside = on_core(
        global_backward_body,
        [((GROUP, 3 * fold, LANES), BF), ((GROUP, 2 * half, LANES), BF)],
        (got, beside, own_seg, shared_seg, total_1, d_folded),
        head_scratch
        + [
            pltpu.VMEM((keys * 3 // 2, LANES), BF),
            pltpu.VMEM((keys * 3 // 2, LANES), F32),
            pltpu.VMEM((2, keys, LANES), F32),
            pltpu.VMEM((2, keys, LANES), F32),
        ],
    )
    back = partner(to_beside, 1, count)
    gap = 3 * fold - half - row_count - half
    back = jnp.concatenate(
        [
            jnp.zeros((GROUP, row_count, LANES), BF),
            back[:, :half],
            jnp.zeros((GROUP, gap, LANES), BF),
            back[:, half:],
        ],
        1,
    )
    sent = (sent.astype(F32) + back.astype(F32)).astype(BF)
    got = exchange(sent, count)

    d_proj_1, gain_attn_1, *grad_1 = on_core(
        global_finish_body,
        [((rows, 3 * width), BF), ((1, width), F32)] + [((row_count, width), BF)] * micro_count,
        (first, got, d_mid_1, *in_1, gain_attn, global_tables),
    )

    if count == GROUP:
        left, grad_1 = lax.optimization_barrier((left, grad_1))
        left = [left[0]] + [partner(left[apart], apart, count) for apart in range(1, 4)]
    up_0 = to_other_section(grad_1, -1)
    d_mlp = jnp.concatenate(
        [jnp.where(lower, a, up_1[i * row_count :][:row_count]) for i, a in enumerate(up_0)]
    )
    across_mlp, beside_mlp = partner(d_mlp, 2, count), partner(d_mlp, 1, count)
    gain_mlp_0, d_mid_0, d_att_0, *right = on_core(
        local_back_middle_body,
        [
            ((1, width), F32),
            ((rows, width), F32),
            ((rows, width), BF),
        ]
        + [((row_count, inner + width), BF)] * micro_count,
        (*others, lower_flag, *up_0, middle_0, gate_up_0, gain_mlp, right_1),
        [pltpu.VMEM((hidden, width), BF)],
        [pltpu.VMEM] * len(others) + [pltpu.SMEM] + [pltpu.VMEM] * 6,
    )
    d_att_0, right, across_mlp = lax.optimization_barrier((d_att_0, right, across_mlp))
    across = [partner(item, 2, count) for item in right]
    beside = [partner(item, 1, count) for item in right]
    d_mlp = [d_mlp, beside_mlp, across_mlp, partner(across_mlp, 1, count)]
    out_near, out_far = first_hop(
        on_core(
            functools.partial(early_body, [((3 * shard_total, left_total), (0, width))]),
            three_parts((hidden_total, width)),
            (*d_mlp, *left),
        ),
        count,
    )
    dq_0, d_own, d_before, d_after = on_core(
        local_backward_body,
        [
            ((rows, width), BF),
            ((rows, 2 * width), F32),
            ((rows, 2 * width), BF),
            ((rows, 2 * width), BF),
        ],
        (q_0, *around_0, bias, total_0, d_att_0, local_tables),
    )
    from_after = lax.ppermute(d_before, "dp", down_pairs)
    from_before = lax.ppermute(d_after, "dp", up_pairs)
    *d_proj, grad_0, gain_attn_sum = on_core(
        local_finish_body,
        [
            ((row_count, 3 * width), BF),
            ((row_count + EXTRA, 3 * width), BF),
            ((rows, width), BF),
            ((1, width), F32),
        ],
        (
            lower_flag, first, dq_0, d_own, from_after, from_before, local_tables, d_mid_0, in_0, gain_attn,
            gain_mlp_0, d_proj_1, gain_attn_1, gain_mlp_1,
        ),
        [pltpu.VMEM((1, width), F32), pltpu.VMEM((rows, 3 * width), BF)],
        [pltpu.SMEM] + [pltpu.VMEM] * 13,
    )
    across, out_far, _ = lax.optimization_barrier((across, out_far, d_proj[0]))
    right = right + beside + across + [partner(item, 1, count) for item in across]
    early_rows = shard_total * (inner // width + 1)
    near, far = first_hop(
        on_core(
            functools.partial(
                early_body,
                [
                    ((2 * shard_total, 3 * shard_total), (0, inner)),
                    ((shard_total, 2 * shard_total), (inner, inner + width)),
                ],
            ),
            three_parts((early_rows, width)),
            (*right, *left),
        ),
        count,
    )
    across = [partner(item, 2, count) for item in d_proj]
    beside = [partner(item, 1, count) for item in d_proj]
    far = jnp.concatenate([far, out_far])
    across, far = lax.optimization_barrier((across, far))
    far = partner(far, 8, count)
    right = []
    for low, high in zip(d_proj[:1] + beside[:1] + across[:1], d_proj[1:] + beside[1:] + across[1:]):
        right += [low, high]
    right += [partner(item, 1, count) for item in across]
    late_in = (group_pos[None], *right, *left)
    late = on_core(
        functools.partial(late_body, (0, shard_total)),
        three_parts((shard_total, 3 * width + LANES)),
        late_in,
        [pltpu.VMEM((width, LANES), F32)],
        [pltpu.SMEM] + [pltpu.VMEM] * (len(late_in) - 1),
    )
    far, late = lax.optimization_barrier((far, list(late)))
    early = near + far[:early_rows].astype(F32)
    mlp_out_share = out_near + far[early_rows:].astype(F32)
    late = second_hop(*first_hop(late, count), count)
    parts = [early[p * shard_total : (p + 1) * shard_total] for p in range(inner // width)]
    in_share = jnp.concatenate(parts, 1)
    attn_share = early[early_rows - shard_total :]
    gain_columns = late[:, 3 * width :]
    qkv_share, in_share, mlp_out_share, attn_share, gain_columns = (
        over_groups(item, count)
        for item in (late[:, : 3 * width], in_share, mlp_out_share, attn_share, gain_columns)
    )
    if count == GROUP:
        gains = jnp.stack([gain_columns[:, 0], gain_columns[:, 2]])
    else:
        gain_mlp_sum = jnp.where(lower, gain_mlp_0, gain_mlp_1)
        gains = lax.psum(jnp.concatenate([gain_attn_sum, gain_mlp_sum]), "dp")
        gains = lax.dynamic_slice_in_dim(gains, replica * shard, shard, 1)

    return (
        jnp.where(lower, jnp.concatenate(out_0), out_1).reshape(1, micro_count, row_count, width),
        jnp.where(lower, grad_0, jnp.concatenate(grad_1)).reshape(1, micro_count, row_count, width),
        qkv_share[None],
        attn_share[None],
        in_share[None],
        mlp_out_share[None],
        gains[:1],
        gains[1:],
    )


def solution(mesh):
    in_specs = (
        P(None, "dp", None),
        P(None, "dp"),
        P(None, "dp", None),
        P("section", "dp", None),
        P("section", "dp", None),
        P("section", "dp", None),
        P("section", "dp", None),
        P("section", "dp"),
        P("section", "dp"),
    )
    out_specs = (
        P("section", None, "dp", None),
        P("section", None, "dp", None),
        P("section", "dp", None),
        P("section", "dp", None),
        P("section", "dp", None),
        P("section", "dp", None),
        P("section", "dp"),
        P("section", "dp"),
    )
    return jax.shard_map(
        on_device, mesh=mesh, in_specs=in_specs, out_specs=out_specs, check_vma=False
    )
```

```python
import functools
import math

import jax
import jax.numpy as jnp
from jax import lax
from jax.experimental import pallas as pl
from jax.experimental.pallas import tpu as pltpu
from jax.sharding import PartitionSpec as P

HEAD_DIM = 64
GROUP = 16
HALF_WIN = 64
EXTRA = 16
LANES = 128
TILE = 256

local_log_base = math.log(10000.0)
global_log_base = math.log(160000.0)
masked_score = -1e30
SCALE = 1.0 / math.sqrt(HEAD_DIM)
BF = jnp.bfloat16
F32 = jnp.float32


def dot(left, right):
    return jnp.dot(left, right, preferred_element_type=F32)


def dot_bt(left, right):
    return lax.dot_general(left, right, (((1,), (1,)), ((), ())), preferred_element_type=F32)


def dot_at(left, right):
    return lax.dot_general(left, right, (((0,), (0,)), ((), ())), preferred_element_type=F32)


def moments(values):
    center = values - jnp.mean(values, -1, keepdims=True)
    scale = lax.rsqrt(jnp.mean(center * center, -1, keepdims=True) + 1e-05)
    return center * scale, scale


def norm_back(grad_out, gain_row, xhat, scale):
    scaled = grad_out * gain_row
    mean_grad = jnp.mean(scaled, -1, keepdims=True)
    mean_dot = jnp.mean(scaled * xhat, -1, keepdims=True)
    return (scaled - mean_grad - xhat * mean_dot) * scale


def angles(positions, log_base):
    half_dim = HEAD_DIM // 2
    fraction = (2 * jnp.arange(half_dim)).astype(F32) / HEAD_DIM
    inverse = jnp.exp(-fraction * log_base)
    table = positions.astype(F32)[:, None] * inverse[None, :]
    cosine, sine = jnp.cos(table), jnp.sin(table)
    none = jnp.zeros_like(sine)
    cosine = jnp.concatenate([cosine, cosine], 1)
    to_first = jnp.concatenate([-sine, none], 1)
    to_second = jnp.concatenate([none, sine], 1)
    return jnp.tile(jnp.stack([cosine, to_first, to_second]), (1, 2, 2))


def on_core(body, outs, args, scratch=(), spaces=None, out_spaces=None):
    return pl.pallas_call(
        body,
        out_shape=[jax.ShapeDtypeStruct(shape, dtype) for shape, dtype in outs],
        in_specs=[
            pl.BlockSpec(memory_space=space) for space in spaces or [pltpu.VMEM] * len(args)
        ],
        out_specs=[
            pl.BlockSpec(memory_space=space) for space in out_spaces or [pltpu.VMEM] * len(outs)
        ],
        scratch_shapes=scratch,
        cost_estimate=pl.CostEstimate(
            flops=2**10, bytes_accessed=2**10, transcendentals=0
        ),
        compiler_params=pltpu.CompilerParams(vmem_limit_bytes=48 * 2**20),
    )(*args)


def low_lanes():
    return lax.broadcasted_iota(jnp.int32, (1, LANES), 1) < HEAD_DIM


def swap(chunk):
    return pltpu.roll(chunk, HEAD_DIM, 1)


def chunks_of(rows):
    return [rows[:, c : c + LANES] for c in range(0, rows.shape[1], LANES)]


def rotate(chunk, tables):
    cosine, to_first, to_second = tables
    quarter = HEAD_DIM // 2
    return (
        chunk * cosine
        + pltpu.roll(chunk, LANES - quarter, 1) * to_first
        + pltpu.roll(chunk, quarter, 1) * to_second
    )


def unrotate(chunk, tables):
    cosine, to_first, to_second = tables
    quarter = HEAD_DIM // 2
    return (
        chunk * cosine
        - pltpu.roll(chunk, LANES - quarter, 1) * to_first
        - pltpu.roll(chunk, quarter, 1) * to_second
    )


def low_and_high(chunks):
    swapped = [swap(chunk) for chunk in chunks]
    low = [(swapped if h % 2 else chunks)[h // 2] for h in range(2 * len(chunks))]
    high = [(chunks if h % 2 else swapped)[h // 2] for h in range(2 * len(chunks))]
    return low, high


def targets():
    for d in range(GROUP):
        micro, chip, half = d // 8, d % 8 // 2, d % 2
        yield d, micro, 3 * chip + 2 * half, 3 * chip + 1, half


def pack_folded(chunks, ref, base):
    low, high = low_and_high(chunks)
    first = low_lanes()
    rows = chunks[0].shape[0] // 2
    half, fold = rows // 2, rows * 3 // 4
    for d, micro, own, shared, side in targets():
        start = micro * rows
        part = start + side * half
        upper = jnp.concatenate(
            [high[own][start + fold : start + rows], high[shared][part : part + half]], 0
        )
        ref[d, base : base + fold] = jnp.where(
            first, low[own][start : start + fold], upper
        ).astype(BF)


def pack_pairs(lefts, rights, ref):
    low, high = low_and_high(lefts)[0], low_and_high(rights)[1]
    first = low_lanes()
    rows = lefts[0].shape[0] // 2
    half = rows // 2
    for d, micro, own, shared, side in targets():
        start = micro * rows
        part = start + side * half
        ref[d, 0:rows] = jnp.where(
            first, low[own][start : start + rows], high[own][start : start + rows]
        ).astype(BF)
        ref[d, rows : rows + half] = jnp.where(
            first, low[shared][part : part + half], high[shared][part : part + half]
        ).astype(BF)


def unpack_folded(ref, base, rows):
    first = low_lanes()
    fold = rows * 3 // 4
    low, high = {}, {}
    shared_parts = {}
    for d, micro, own, shared, side in targets():
        block = ref[d, base : base + fold].astype(F32)
        mine = jnp.concatenate([block, swap(block[: rows - fold])], 0)
        if own % 2:
            high[micro, own] = swap(mine)
        else:
            low[micro, own] = mine
        shared_parts[micro, shared, side] = block[rows - fold :]
        if side:
            both = jnp.concatenate([shared_parts[micro, shared, 0], block[rows - fold :]], 0)
            if shared % 2:
                high[micro, shared] = both
            else:
                low[micro, shared] = swap(both)
    heads = GROUP // 4 * 3
    return [
        jnp.concatenate(
            [jnp.where(first, low[m, h], high[m, h + 1]) for m in range(2)], 0
        )
        for h in range(0, heads, 2)
    ]


def unpack_pairs(ref, rows):
    first = low_lanes()
    half = rows // 2
    pairs = {}
    parts = {}
    for d, micro, own, shared, side in targets():
        pairs[micro, own] = ref[d, 0:rows].astype(F32)
        parts[side] = ref[d, rows : rows + half].astype(F32)
        if side:
            pairs[micro, shared] = jnp.concatenate([parts[0], parts[1]], 0)
    heads = GROUP // 4 * 3
    lefts, rights = [], []
    for h in range(0, heads, 2):
        even, odd = [pairs[m, h] for m in range(2)], [pairs[m, h + 1] for m in range(2)]
        lefts.append(
            jnp.concatenate([jnp.where(first, a, swap(b)) for a, b in zip(even, odd)], 0)
        )
        rights.append(
            jnp.concatenate([jnp.where(first, swap(a), b) for a, b in zip(even, odd)], 0)
        )
    return lefts, rights


class Weights:
    def __init__(self, sources, mlp_out):
        self.sources = sources
        self.mlp_out = sources[-1]
        if len(sources) == 1:
            self.mlp_out = mlp_out
            unpack_rows(sources[0], mlp_out)

    def get(self, which):
        if which == 2:
            return self.mlp_out[...]
        if len(self.sources) > 1:
            return self.sources[which][...]
        (wide,) = self.sources
        width = wide.shape[0]
        inner = 2 * self.mlp_out.shape[0]
        return wide[:, width : width + inner] if which else wide[:, :width]


def first_block(pair):
    return -(-pair // 32) * 16


def packed_pieces(shard, rows, width):
    yield 0, shard, 0, width, 0, 0
    rest = rows - shard
    side = width // 3
    yield 0, rest, width, 2 * side, shard, 0
    yield rest, 16, width, side, shard, 2 * side
    yield rest, 16, width + side, side, shard + 16, 2 * side


def unpack_rows(wide, mlp_out):
    hidden, width = mlp_out.shape
    shard = wide.shape[0] // GROUP
    start = wide.shape[1] - width - 2 * (width // 3)
    pair = 2 * hidden // GROUP
    upper = first_block(pair)
    for d in range(GROUP):
        low = d // 2 * pair + d % 2 * upper
        have = pair - upper if d % 2 else upper
        for row, rows, column, columns, to_row, to_column in packed_pieces(shard, upper, width):
            rows = min(rows, have - to_row)
            if rows > 0:
                mlp_out[low + to_row : low + to_row + rows, to_column : to_column + columns] = wide[
                    d * shard + row : d * shard + row + rows, start + column : start + column + columns
                ]


def stack_body(odd_ref, attn_ref, mlp_in_ref, own_ref, beside_ref, out_ref):
    shard, width = attn_ref.shape
    inner = mlp_in_ref.shape[1]
    out_ref[:, :width] = attn_ref[...]
    out_ref[:, width : width + inner] = mlp_in_ref[...]
    own, beside = own_ref[...].astype(F32), beside_ref[...].astype(F32)
    moved = beside.shape[0]
    even = jnp.concatenate([own, beside], 0)
    odd = jnp.concatenate([own[moved:], beside, beside], 0)
    block = jnp.where(odd_ref[0] == 1, odd, even).astype(BF)
    start = width + inner
    for row, rows, column, columns, from_row, from_column in packed_pieces(
        shard, block.shape[0], width
    ):
        out_ref[row : row + rows, start + column : start + column + columns] = block[
            from_row : from_row + rows, from_column : from_column + columns
        ]


def mlp_forward(layer_in, attended, gain, weights):
    middle = layer_in + dot(attended, weights.get(0))
    xhat, _ = moments(middle)
    normed = (xhat * gain).astype(BF)
    gate_up = dot(normed, weights.get(1))
    half = gate_up.shape[1] // 2
    gate, up = gate_up[:, :half], gate_up[:, half:]
    cdf = 0.5 * (1.0 + lax.erf(gate * math.sqrt(0.5)))
    mixed = (gate * cdf * up).astype(BF)
    result = (middle + dot(mixed, weights.get(2))).astype(BF)
    return middle, normed, gate, up, mixed, result


def mlp_backward(upstream, middle, gate, up, gain, weights):
    d_mixed = dot_bt(upstream, weights.get(2))
    cdf = 0.5 * (1.0 + lax.erf(gate * math.sqrt(0.5)))
    density = jnp.exp(-0.5 * gate * gate) * (1.0 / math.sqrt(2.0 * math.pi))
    d_gate = d_mixed * up * (cdf + gate * density)
    d_up = d_mixed * gate * cdf
    d_gate_up = jnp.concatenate([d_gate.astype(BF), d_up.astype(BF)], 1)
    d_normed = dot_bt(d_gate_up, weights.get(1))
    xhat, scale = moments(middle)
    gain_grad = jnp.sum(d_normed * xhat, 0, keepdims=True)
    d_middle = upstream.astype(F32) + norm_back(d_normed, gain, xhat, scale)
    d_attn = d_middle.astype(BF)
    d_attended = dot_bt(d_attn, weights.get(0))
    return d_gate_up, gain_grad, d_middle, d_attn, d_attended


def project(xhat, gain, first_ref, table_ref, normed_ref):
    width = xhat.shape[1]
    normed = (xhat * gain).astype(BF)
    normed_ref[...] = normed
    tables = [table_ref[i] for i in range(3)]
    results = [dot(normed, first_ref[:, c * width : (c + 1) * width]) for c in range(3)]
    queries, keys, values = chunks_of(results[0]), chunks_of(results[1]), results[2]
    return [rotate(c, tables) for c in queries], [rotate(c, tables) for c in keys], values


def input_backward(d_middle, d_projected, x, gain_ref, first_ref, gain_out_ref):
    d_normed = dot_bt(d_projected, first_ref[:, : d_projected.shape[1]])
    xhat, scale = moments(x)
    gain_out_ref[...] = jnp.sum(d_normed * xhat, 0, keepdims=True)
    return (d_middle + norm_back(d_normed, gain_ref[...], xhat, scale)).astype(BF)


def joined(refs):
    return jnp.concatenate([ref[...] for ref in refs], 0)


def store_chunks(refs, rows):
    size = rows.shape[0] // len(refs)
    for i, ref in enumerate(refs):
        ref[...] = rows[i * size : (i + 1) * size]


def message_body(w_ref, attn_ref, mlp_ref, ids_ref, out_ref, rows_scr, ids_scr):
    shard, columns = w_ref.shape
    micro_count, row_count = ids_ref.shape
    out_ref[:, :columns] = w_ref[...]
    rows_scr[...] = jnp.zeros_like(rows_scr)
    ids_scr[...] = jnp.zeros_like(ids_scr)
    rows_scr[0:1, :shard] = attn_ref[...].astype(F32)
    rows_scr[1:2, :shard] = mlp_ref[...].astype(F32)
    ids_scr[:micro_count, :row_count] = ids_ref[...].astype(F32)
    runs = -(-row_count // shard)
    for run in range(runs):
        turned = ids_scr[...]
        if run:
            turned = pltpu.roll(turned, LANES - run * shard, 1)
        for micro in range(micro_count):
            row = 2 + micro * runs + run
            rows_scr[row : row + 1] = turned[micro : micro + 1]
    out_ref[:, columns:] = rows_scr[...].T[:shard].astype(BF)


def local_project_body(first_ref, x_ref, table_ref, extra_ref, normed_ref, q_ref, kv_ref):
    xhat, _ = moments(x_ref[...].astype(F32))
    extra = first_ref[:, first_ref.shape[1] - LANES :].astype(F32).T
    extra_ref[...] = extra[: extra_ref.shape[0]]
    queries, keys, values = project(xhat, extra[:1], first_ref, table_ref, normed_ref)
    width = values.shape[1]
    for j, (q, k) in enumerate(zip(queries, keys)):
        q_ref[:, LANES * j : LANES * (j + 1)] = q.astype(BF)
        kv_ref[:, LANES * j : LANES * (j + 1)] = k.astype(BF)
    kv_ref[:, width:] = values.astype(BF)


def two_heads(chunk):
    first = low_lanes()
    wide = chunk.astype(F32)
    return jnp.concatenate([jnp.where(first, wide, 0.0), jnp.where(first, 0.0, wide)], 0)


def pick_heads(rows):
    half = rows.shape[0] // 2
    return jnp.where(low_lanes(), rows[:half], rows[half:])


def local_parts(q_ref, before_ref, own_ref, after_ref):
    rows = q_ref.shape[0] // 2
    width = q_ref.shape[1]
    for micro in range(2):
        for j in range(width // LANES):
            here = slice(micro * rows, (micro + 1) * rows)
            lanes = slice(LANES * j, LANES * (j + 1))
            more = slice(width + LANES * j, width + LANES * (j + 1))
            keys, values = (
                jnp.concatenate([ref[here, part] for ref in (before_ref, own_ref, after_ref)], 0)
                for part in (lanes, more)
            )
            queries = (two_heads(q_ref[here, lanes]) * SCALE).astype(BF)
            yield micro * (width // LANES) + j, micro, here, lanes, more, queries, keys, values


def local_forward_body(q_ref, before_ref, own_ref, after_ref, bias_ref, att_ref, total_ref):
    parts = local_parts(q_ref, before_ref, own_ref, after_ref)
    for index, micro, here, lanes, _, queries, keys, values in parts:
        scores = dot_bt(keys, queries) + bias_ref[micro]
        peak = jnp.max(scores, 0, keepdims=True)
        weights = jnp.exp(scores - peak)
        total = jnp.sum(weights, 0, keepdims=True)
        total_ref[index] = peak + jnp.log(total)
        probs = (weights * (1.0 / total)).astype(BF)
        att_ref[here, lanes] = pick_heads(dot_at(probs, values)).astype(BF)


def local_backward_body(
    q_ref, before_ref, own_ref, after_ref, bias_ref, total_ref, d_ref, table_ref,
    dq_ref, d_own_ref, d_before_ref, d_after_ref,
):
    tables = [table_ref[i] for i in range(3)]
    parts = local_parts(q_ref, before_ref, own_ref, after_ref)
    rows = q_ref.shape[0] // 2
    for index, micro, here, lanes, more, queries, keys, values in parts:
        d_out = two_heads(d_ref[here, lanes]).astype(BF)
        probs = jnp.exp(dot_bt(keys, queries) + bias_ref[micro] - total_ref[index])
        d_probs = dot_bt(values, d_out)
        product = probs * d_probs
        delta = jnp.sum(product, 0, keepdims=True)
        d_scores = (product - probs * delta).astype(BF)
        d_queries = pick_heads(dot_at(d_scores, keys)) * SCALE
        local_tables = [table[here] for table in tables]
        dq_ref[here, lanes] = unrotate(d_queries, local_tables).astype(BF)
        for part, grads in ((lanes, dot(d_scores, queries)), (more, dot(probs.astype(BF), d_out))):
            d_before_ref[here, part] = grads[:rows].astype(BF)
            d_own_ref[here, part] = grads[rows : 2 * rows]
            d_after_ref[here, part] = grads[2 * rows :].astype(BF)


def local_finish_body(
    lower_ref, first_ref, dq_ref, own_ref, low_ref, high_ref, table_ref, d_middle_ref, x_ref, gain_ref,
    gain_mlp_ref, other_ref, other_attn_ref, other_mlp_ref, low_out_ref, high_out_ref, grad_ref, gain_attn_ref,
    gain_scr, out_ref,
):
    rows, width = dq_ref.shape

    @pl.when(lower_ref[0] == 1)
    def _():
        tables = [table_ref[i] for i in range(3)]
        total = own_ref[...] + low_ref[...].astype(F32) + high_ref[...].astype(F32)
        out_ref[:, :width] = dq_ref[...]
        for j, chunk in enumerate(chunks_of(total[:, :width])):
            start = width + LANES * j
            out_ref[:, start : start + LANES] = unrotate(chunk, tables).astype(BF)
        out_ref[:, 2 * width :] = total[:, width:].astype(BF)
        grad_ref[...] = input_backward(
            d_middle_ref[...], out_ref[...], x_ref[...].astype(F32), gain_ref, first_ref, gain_scr
        )

    @pl.when(lower_ref[0] == 0)
    def _():
        out_ref[...] = other_ref[...]
        grad_ref[...] = jnp.zeros_like(grad_ref)
        gain_scr[...] = other_attn_ref[...]

    gain_attn_ref[...] = gain_scr[...]
    gain_mlp = jnp.where(lower_ref[0] == 1, gain_mlp_ref[...], other_mlp_ref[...])
    index = lax.broadcasted_iota(jnp.int32, (EXTRA, width), 0)
    tail = jnp.zeros((EXTRA, width), F32)
    for row, gain in ((0, gain_scr[...]), (2, gain_mlp)):
        high = gain.astype(BF).astype(F32)
        tail = jnp.where(index == row, high, tail)
        tail = jnp.where(index == row + 1, gain - high, tail)
    half = rows // 2
    low_out_ref[...] = out_ref[:half]
    high_out_ref[:half] = out_ref[half:]
    high_out_ref[half:] = jnp.zeros((EXTRA, out_ref.shape[1]), BF)
    high_out_ref[half:, :width] = tail.astype(BF)


def local_middle_body(*refs):
    sources, refs = refs[:-10], refs[-10:]
    x_ref, att_ref, gain_ref, normed_ref, mixed_ref, middle_ref, gate_up_ref = refs[:7]
    weights = Weights(sources, refs[9])
    middle, normed, gate, up, mixed, result = mlp_forward(
        x_ref[...].astype(F32), att_ref[...], gain_ref[...], weights
    )
    store_chunks(refs[7:9], result)
    normed_ref[...] = normed
    mixed_ref[...] = mixed
    middle_ref[...] = middle
    half = gate.shape[1]
    gate_up_ref[:, :half] = gate
    gate_up_ref[:, half:] = up


def local_back_middle_body(*refs):
    sources, refs = refs[:-13], refs[-13:]
    lower_ref, low_ref, high_ref, middle_ref, gate_up_ref, gain_ref, other_ref = refs[:7]
    gain_out_ref, d_middle_ref, d_att_ref, right_low_ref, right_high_ref = refs[7:12]
    weights = Weights(sources, refs[12])
    half = gate_up_ref.shape[1] // 2
    upstream = joined([low_ref, high_ref])
    d_gate_up, gain_grad, d_middle, d_attn, d_attended = mlp_backward(
        upstream, middle_ref[...], gate_up_ref[:, :half], gate_up_ref[:, half:],
        gain_ref[...], weights,
    )
    gain_out_ref[...] = gain_grad
    d_middle_ref[...] = d_middle
    d_att_ref[...] = d_attended.astype(BF)

    @pl.when(lower_ref[0] == 1)
    def _():
        store_chunks(
            (right_low_ref, right_high_ref), jnp.concatenate([d_gate_up, d_attn], 1)
        )

    @pl.when(lower_ref[0] == 0)
    def _():
        store_chunks((right_low_ref, right_high_ref), other_ref[...])


def global_project_body(first_ref, low_ref, high_ref, gain_ref, table_ref, normed_ref, sent_ref):
    xhat, _ = moments(joined([low_ref, high_ref]).astype(F32))
    queries, keys, values = project(xhat, gain_ref[...], first_ref, table_ref, normed_ref)
    pack_pairs(queries, keys, sent_ref)
    pack_folded(chunks_of(values), sent_ref, sent_ref.shape[1] * 2 // 3)


def flat(blocks):
    return blocks.reshape(-1, LANES)


def own_unfolded(ref, base, rows):
    fold = rows * 3 // 4
    block = ref[:, base : base + fold].astype(F32)
    rest = swap(flat(block[:, : rows - fold])).reshape(GROUP, rows - fold, LANES)
    return flat(jnp.concatenate([block, rest], 1))


def shared_unfolded(ref, start, rows):
    return swap(flat(ref[:, start : start + rows // 2].astype(F32)))


def fill_heads(got_ref, other_ref, own_seg_ref, shared_seg_ref, q_scr, k_scr, v_scr):
    rows = got_ref.shape[1] * 4 // 9
    half = rows // 2
    first = low_lanes()
    lane = lax.broadcasted_iota(jnp.int32, (1, LANES), 1) - HEAD_DIM
    own = flat(got_ref[:, 0:rows].astype(F32))
    shared = flat(got_ref[:, rows : rows + half].astype(F32))
    other = flat(other_ref[:, 0:half].astype(F32))
    count = own.shape[0]
    own_hit = lane == own_seg_ref[...]
    shared_hit = lane == shared_seg_ref[...]
    both = jnp.concatenate([shared, other], 0)
    for start, pairs, hit in (
        (0, own, own_hit),
        (count, shared, shared_hit[: count // 2]),
    ):
        marked = jnp.where(hit, 1.0, 0.0)
        q_scr[start : start + pairs.shape[0]] = jnp.where(first, pairs * SCALE, marked).astype(BF)
    for unit, pairs, hit in ((0, own, own_hit), (1, both, shared_hit)):
        marked = jnp.where(hit, 0.0, masked_score)
        k_scr[unit] = jnp.where(first, swap(pairs), marked).astype(BF)
    base = rows + half
    v_scr[0] = jnp.where(first, own_unfolded(got_ref, base, rows), 0.0).astype(BF)
    start = base + rows - rows * 3 // 4
    shared_v = jnp.concatenate(
        [shared_unfolded(got_ref, start, rows), shared_unfolded(other_ref, half, rows)], 0
    )
    v_scr[1] = jnp.where(first, shared_v, 0.0).astype(BF)


def fold_out(own, shared, rows, ref, base):
    fold = rows * 3 // 4
    blocks = own.reshape(GROUP, rows, LANES)
    swapped = swap(own).reshape(GROUP, rows, LANES)
    upper = jnp.concatenate(
        [swapped[:, fold:], swap(shared).reshape(GROUP, rows // 2, LANES)], 1
    )
    ref[:, base : base + fold] = jnp.where(low_lanes(), blocks[:, :fold], upper).astype(BF)


def global_forward_body(
    got_ref, other_ref, own_seg_ref, shared_seg_ref, out_ref, total_ref,
    q_scr, k_scr, v_scr, vt_scr, o_scr,
):
    fill_heads(got_ref, other_ref, own_seg_ref, shared_seg_ref, q_scr, k_scr, v_scr)
    for unit in range(2):
        vt_scr[unit] = v_scr[unit].astype(F32).T.astype(BF)
    count = k_scr.shape[1]

    def step(tile, carry):
        unit = tile // (count // TILE)
        rows = pl.ds(pl.multiple_of(tile * TILE, TILE), TILE)
        scores = dot_bt(k_scr[unit], q_scr[rows])
        peak = jnp.max(scores, 0, keepdims=True)
        weights = jnp.exp(scores - peak)
        total = jnp.sum(weights, 0, keepdims=True)
        total_ref[tile] = peak + jnp.log(total)
        out = dot(vt_scr[unit], weights.astype(BF)) * (1.0 / total)
        o_scr[rows] = out.T
        return carry

    lax.fori_loop(0, q_scr.shape[0] // TILE, step, 0)
    rows = got_ref.shape[1] * 4 // 9
    fold_out(o_scr[:count], o_scr[count:], rows, out_ref, 0)


def global_backward_body(
    got_ref, other_ref, own_seg_ref, shared_seg_ref, total_ref, d_ref, sent_ref, to_other_ref,
    q_scr, k_scr, v_scr, kt_scr, d_scr, dq_scr, dk_scr, dv_scr,
):
    fill_heads(got_ref, other_ref, own_seg_ref, shared_seg_ref, q_scr, k_scr, v_scr)
    first = low_lanes()
    rows = got_ref.shape[1] * 4 // 9
    half = rows // 2
    for unit in range(2):
        keys = jnp.where(first, k_scr[unit].astype(F32), 0.0)
        kt_scr[unit] = keys.T.astype(BF)
    count = k_scr.shape[1]
    d_scr[:count] = jnp.where(first, own_unfolded(d_ref, 0, rows), 0.0).astype(BF)
    d_scr[count:] = jnp.where(
        first, shared_unfolded(d_ref, rows - rows * 3 // 4, rows), 0.0
    ).astype(BF)
    dk_scr[...] = jnp.zeros_like(dk_scr)
    dv_scr[...] = jnp.zeros_like(dv_scr)

    def step(tile, carry):
        unit = tile // (count // TILE)
        here = pl.ds(pl.multiple_of(tile * TILE, TILE), TILE)
        queries, d_out = q_scr[here], d_scr[here]
        probs = jnp.exp(dot_bt(k_scr[unit], queries) - total_ref[tile])
        d_probs = dot_bt(v_scr[unit], d_out)
        product = probs * d_probs
        delta = jnp.sum(product, 0, keepdims=True)
        d_scores = (product - probs * delta).astype(BF)
        dv_scr[unit] += dot(probs.astype(BF), d_out)
        dk_scr[unit] += dot(d_scores, queries)
        dq_scr[here] = dot(kt_scr[unit], d_scores).T * SCALE
        return carry

    lax.fori_loop(0, q_scr.shape[0] // TILE, step, 0)
    mine = count // 2
    own = jnp.where(first, dq_scr[:count], swap(dk_scr[0]))
    sent_ref[:, 0:rows] = own.reshape(GROUP, rows, LANES).astype(BF)
    shared_k, shared_v = dk_scr[1], dv_scr[1]
    shared = jnp.where(first, dq_scr[count:], swap(shared_k[:mine]))
    sent_ref[:, rows : rows + half] = shared.reshape(GROUP, half, LANES).astype(BF)
    fold_out(dv_scr[0], shared_v[:mine], rows, sent_ref, rows + half)
    for place, grads in enumerate((shared_k, shared_v)):
        other = jnp.where(first, 0.0, swap(grads[mine:])).reshape(GROUP, half, LANES)
        to_other_ref[:, place * half : (place + 1) * half] = other.astype(BF)


def global_middle_body(*refs):
    sources, refs = refs[:-14], refs[-14:]
    got_ref, low_ref, high_ref, up_ref, gain_ref, out_ref, att_ref, normed_ref, mixed_ref = refs[:9]
    right_ref, gain_out_ref, d_middle_ref, sent_ref = refs[9:13]
    weights = Weights(sources, refs[13])
    rows = low_ref.shape[0]
    attended = jnp.concatenate([c.astype(BF) for c in unpack_folded(got_ref, 0, rows)], 1)
    att_ref[...] = attended
    gain = gain_ref[...]
    middle, normed, gate, up, mixed, result = mlp_forward(
        joined([low_ref, high_ref]).astype(F32), attended, gain, weights
    )
    out_ref[...] = result
    normed_ref[...] = normed
    mixed_ref[...] = mixed
    d_gate_up, gain_grad, d_middle, d_attn, d_attended = mlp_backward(
        up_ref[...], middle, gate, up, gain, weights
    )
    right_ref[:, : d_gate_up.shape[1]] = d_gate_up
    right_ref[:, d_gate_up.shape[1] :] = d_attn
    gain_out_ref[...] = gain_grad
    d_middle_ref[...] = d_middle
    pack_folded(chunks_of(d_attended), sent_ref, 0)


def global_finish_body(
    first_ref, got_ref, d_middle_ref, low_ref, high_ref, gain_ref, table_ref,
    d_proj_ref, gain_out_ref, *grad_refs,
):
    tables = [table_ref[i] for i in range(3)]
    x = joined([low_ref, high_ref]).astype(F32)
    rows = low_ref.shape[0]
    d_queries, d_keys = unpack_pairs(got_ref, rows)
    d_values = unpack_folded(got_ref, rows * 3 // 2, rows)
    parts = [unrotate(c, tables).astype(BF) for c in d_queries + d_keys]
    d_projected = jnp.concatenate(parts + [c.astype(BF) for c in d_values], 1)
    d_proj_ref[...] = d_projected
    store_chunks(
        grad_refs,
        input_backward(d_middle_ref[...], d_projected, x, gain_ref, first_ref, gain_out_ref),
    )


def neighbours(count, step):
    return [
        (i, i + step)
        for i in range(count)
        if 0 <= i + step < count and i // GROUP == (i + step) // GROUP
    ]


def exchange(blocks, count):
    groups = [list(range(s, s + GROUP)) for s in range(0, count, GROUP)]
    return lax.all_to_all(blocks, "dp", 0, 0, axis_index_groups=groups)


def to_other_section(chunks, step):
    pairs = [(0, 1)] if step > 0 else [(1, 0)]
    return [lax.ppermute(rows, "section", pairs) for rows in chunks]


def partner(rows, apart, count):
    return lax.ppermute(rows, "dp", [(i, i ^ apart) for i in range(count)])


def gather_rows(piece, group_pos, count):
    pieces = {0: piece}
    for apart in (4, 8, 12):
        pieces[apart] = partner(piece, apart, count)
    for apart in (0, 4, 8, 12):
        pieces[apart + 2] = partner(pieces[apart], 2, count)
    for apart in range(0, GROUP, 2):
        pieces[apart + 1] = partner(pieces[apart], 1, count)
    whole = jnp.zeros((GROUP,) + piece.shape, piece.dtype)
    for apart, item in pieces.items():
        start = (group_pos ^ apart,) + (0,) * piece.ndim
        whole = lax.dynamic_update_slice(whole, item[None], start)
    if count > GROUP:
        groups = [list(range(s, count, GROUP)) for s in range(GROUP)]
        whole = lax.all_gather(whole, "dp", axis=0, tiled=True, axis_index_groups=groups)
    return whole.reshape(-1, piece.shape[-1]), pieces[2]


def plane_rows(rows, group_pos, count):
    parts = rows.reshape(count // GROUP, 4, 4, *rows.shape[1:])
    place, plane = group_pos % 4, group_pos // 4
    taken = []
    for apart in range(4):
        block = lax.dynamic_index_in_dim(parts, place ^ apart, 2, keepdims=False)
        block = jnp.stack(
            [lax.dynamic_index_in_dim(block, plane ^ z, 1, keepdims=False) for z in range(4)]
        )
        taken.append(partner(block, apart, count) if apart else block)
    return taken


def left_body(lower_ref, place_ref, *refs):
    refs, out_ref = refs[:-1], refs[-1]
    base = 0
    for first_ref, second_ref in zip(refs[0::2], refs[1::2]):
        rows = jnp.where(lower_ref[0] == 1, first_ref[...].astype(F32), second_ref[...].astype(F32))
        turned = rows.T
        size = turned.shape[0] // GROUP
        for d in range(GROUP):
            side = d % 4 ^ place_ref[0] % 4
            plane = d // 4 ^ place_ref[0] // 4
            out_ref[side, plane, base : base + size] = turned[d * size : (d + 1) * size].astype(BF)
        base += size


def left_rows_of(refs, rows):
    start, end = rows
    parts = [
        jnp.concatenate([ref[p, start:end].astype(F32) for p in range(4)], 0).astype(BF) for ref in refs
    ]
    return jnp.concatenate(parts, 1)


def by_plane(result, base, outs, columns=slice(None)):
    keep, keep_far, send = outs
    rows = result.shape[0] // 4
    half = send.shape[0] // 2
    here = slice(base, base + rows)
    keep[here, columns] = result[:rows]
    keep_far[here, columns] = result[2 * rows : 3 * rows]
    send[here, columns] = result[rows : 2 * rows].astype(BF)
    send[half + base : half + base + rows, columns] = result[3 * rows :].astype(BF)


def early_body(terms, *refs):
    refs, outs = refs[:-3], refs[-3:]
    rights, lefts = refs[:-4], refs[-4:]
    width = outs[0].shape[1]
    base = 0
    for rows, (start, end) in terms:
        right = jnp.concatenate([ref[:, start:end] for ref in rights], 0)
        result = dot(left_rows_of(lefts, rows), right)
        for column in range(0, end - start, width):
            by_plane(result[:, column : column + width], base, outs)
            base += result.shape[0] // 4


def late_body(rows, place_ref, *refs):
    refs, outs, scr = refs[:-4], refs[-4:-1], refs[-1]
    rights, lefts = refs[:-4], refs[-4:]
    columns = rights[0].shape[1]
    width = columns // 3
    size = outs[0].shape[0]
    low, high = rights[0::2], rights[1::2]
    half = low[0].shape[0]
    right = jnp.concatenate([part for a, b in zip(low, high) for part in (a[...], b[:half])], 0)
    by_plane(dot(left_rows_of(lefts, rows), right), 0, outs, slice(0, columns))
    tail = sum(ref[half:, :width].astype(F32) for ref in high)
    both = jnp.concatenate([tail, jnp.zeros((LANES - EXTRA, width), F32)], 0).T
    lane = lax.broadcasted_iota(jnp.int32, (1, LANES), 1)
    lows = pltpu.roll(both, LANES - 1, 1)
    scr[...] = jnp.where(lane % 2 == 0, both + lows, 0.0)
    gains = []
    for plane in range(4):
        d = (place_ref[0] // 4 ^ plane) * 4 + place_ref[0] % 4
        gains.append(scr[pl.ds(pl.multiple_of(d * size, 16), size)])
    by_plane(jnp.concatenate(gains, 0), 0, outs, slice(columns, columns + LANES))


def three_parts(shape):
    return [(shape, F32), (shape, F32), ((2 * shape[0], shape[1]), BF)]


def first_hop(blocks, count):
    keep, keep_far, send = blocks
    got = partner(send, 4, count)
    half = keep.shape[0]
    return keep + got[:half].astype(F32), (keep_far + got[half:].astype(F32)).astype(BF)


def second_hop(near, far, count):
    return near + partner(far, 8, count).astype(F32)


def over_groups(rows, count):
    if count == GROUP:
        return rows
    apart = [list(range(s, count, GROUP)) for s in range(GROUP)]
    rows = rows.reshape(count // GROUP, -1, rows.shape[1])
    return lax.psum_scatter(rows, "dp", scatter_dimension=0, axis_index_groups=apart)


def on_device(
    tokens_in,
    segment_ids,
    out_grad,
    qkv_weight,
    attn_out_weight,
    mlp_in_weight,
    mlp_out_weight,
    attn_gain,
    mlp_gain,
):
    lower = lax.axis_index("section") == 0
    lower_flag = lower.astype(jnp.int32)[None]
    shard_total = qkv_weight.shape[1] * (lax.axis_size("dp") // GROUP)
    hidden_total = mlp_out_weight.shape[1] * (lax.axis_size("dp") // GROUP)
    count = lax.axis_size("dp")
    replica = lax.axis_index("dp")
    group_pos = replica % GROUP
    micro_count, row_count, width = tokens_in.shape
    shard = qkv_weight.shape[1]
    runs = -(-row_count // shard)
    (message,) = on_core(
        message_body,
        [((shard, 3 * width + LANES), BF)],
        (qkv_weight[0], attn_gain, mlp_gain, segment_ids),
        [pltpu.VMEM((LANES, LANES), F32), pltpu.VMEM((8, LANES), F32)],
    )
    first, early_piece = gather_rows(message, group_pos, count)
    inner = mlp_in_weight.shape[2]
    hidden = mlp_out_weight.shape[1] * count
    if count == GROUP:
        moved = first_block(2 * mlp_out_weight.shape[1]) - mlp_out_weight.shape[1]
        beside = partner(mlp_out_weight[0, :moved], 1, count)
        (stacked,) = on_core(
            stack_body,
            [((shard, width + inner + width + 2 * (width // 3)), BF)],
            (
                (replica % 2)[None],
                attn_out_weight[0],
                mlp_in_weight[0],
                mlp_out_weight[0],
                beside,
            ),
            (),
            [pltpu.SMEM] + [pltpu.VMEM] * 4,
        )
        stacked, _ = lax.optimization_barrier((stacked, early_piece))
        others = [lax.all_gather(stacked, "dp", axis=0, tiled=True)]
    else:
        others = [
            lax.all_gather(item[0], "dp", axis=0, tiled=True)
            for item in (attn_out_weight, mlp_in_weight, mlp_out_weight)
        ]
    positions = group_pos * row_count + jnp.arange(row_count)
    local_tables = angles(positions, local_log_base)
    global_tables = angles(positions, global_log_base)

    rows = micro_count * row_count
    pairs = rows * width // (row_count * LANES)
    in_0 = tokens_in.reshape(rows, width)
    extra_rows = -(-(2 + micro_count * runs) // 8) * 8
    extra, normed_0, q_0, kv_0 = on_core(
        local_project_body,
        [
            ((extra_rows, width), F32),
            ((rows, width), BF),
            ((rows, width), BF),
            ((rows, 2 * width), BF),
        ],
        (first, in_0, local_tables),
    )
    gain_attn, gain_mlp = extra[:1], extra[1:2]
    all_ids = extra[2 : 2 + micro_count * runs].reshape(micro_count, runs, count, shard)
    all_ids = lax.dynamic_slice_in_dim(all_ids, replica - group_pos, GROUP, 2)
    all_ids = all_ids.swapaxes(1, 2).reshape(micro_count, GROUP, runs * shard)[..., :row_count]
    segments = all_ids.reshape(micro_count, GROUP * row_count).astype(jnp.int32)

    key_pos = positions[0] - row_count + jnp.arange(3 * row_count)
    around = jnp.pad(segments, ((0, 0), (row_count, row_count)), constant_values=-1)
    key_seg = lax.dynamic_slice_in_dim(around, group_pos * row_count, 3 * row_count, 1)
    visible = (key_seg[:, :, None] == segment_ids[:, None, :]) & (
        jnp.abs(positions[None, :] - key_pos[:, None]) <= HALF_WIN
    )[None]
    bias = jnp.tile(jnp.where(visible, 0.0, masked_score), (1, 1, 2))

    own_seg = lax.dynamic_index_in_dim(segments, group_pos // 8, 0, keepdims=False)
    halves = own_seg.reshape(GROUP, 2, row_count // 2)
    mine = lax.dynamic_index_in_dim(halves, group_pos % 2, 1, keepdims=False).reshape(-1)
    theirs = lax.dynamic_index_in_dim(halves, 1 - group_pos % 2, 1, keepdims=False).reshape(-1)
    shared_seg = jnp.concatenate([mine, theirs])[:, None]
    own_seg = own_seg[:, None]

    up_pairs, down_pairs = neighbours(count, 1), neighbours(count, -1)
    around_0 = (
        lax.ppermute(kv_0, "dp", up_pairs),
        kv_0,
        lax.ppermute(kv_0, "dp", down_pairs),
    )
    att_0, total_0 = on_core(
        local_forward_body,
        [((rows, width), BF), ((pairs, 1, LANES), F32)],
        (q_0, *around_0, bias),
    )
    n2_0, mixed_0, middle_0, gate_up_0, *out_0 = on_core(
        local_middle_body,
        [
            ((rows, width), BF),
            ((rows, hidden), BF),
            ((rows, width), F32),
            ((rows, inner), F32),
        ]
        + [((row_count, width), BF)] * micro_count,
        (*others, in_0, att_0, gain_mlp),
        [pltpu.VMEM((hidden, width), BF)],
    )

    in_1 = to_other_section(out_0, 1)
    fold = row_count * 3 // 4
    half = row_count // 2
    normed_1, sent = on_core(
        global_project_body,
        [((rows, width), BF), ((GROUP, 3 * fold, LANES), BF)],
        (first, *in_1, gain_attn, global_tables),
    )
    got = exchange(sent, count)
    beside = jnp.concatenate(
        [got[:, row_count : row_count + half], got[:, 3 * fold - half :]], 1
    )
    beside = partner(beside, 1, count)
    keys = GROUP * row_count
    tiles = keys * 3 // 2 // TILE
    head_scratch = [
        pltpu.VMEM((keys * 3 // 2, LANES), BF),
        pltpu.VMEM((2, keys, LANES), BF),
        pltpu.VMEM((2, keys, LANES), BF),
        pltpu.VMEM((2, LANES, keys), BF),
    ]
    folded, total_1 = on_core(
        global_forward_body,
        [((GROUP, fold, LANES), BF), ((tiles, 1, TILE), F32)],
        (got, beside, own_seg, shared_seg),
        head_scratch + [pltpu.VMEM((keys * 3 // 2, LANES), F32)],
    )
    folded = exchange(folded, count)

    up_1 = out_grad.reshape(rows, width)
    out_1, att_1, n2_1, mixed_1, right_1, gain_mlp_1, d_mid_1, sent = on_core(
        global_middle_body,
        [
            ((rows, width), BF),
            ((rows, width), BF),
            ((rows, width), BF),
            ((rows, hidden), BF),
            ((rows, inner + width), BF),
            ((1, width), F32),
            ((rows, width), F32),
            ((GROUP, fold, LANES), BF),
        ],
        (*others, folded, *in_1, up_1, gain_mlp),
        [pltpu.VMEM((hidden, width), BF)],
    )
    d_folded = exchange(sent, count)
    pairs = ((normed_0, normed_1), (att_0, att_1), (n2_0, n2_1), (mixed_0, mixed_1))
    left_total = 3 * shard_total + hidden_total
    if count == GROUP:
        (left,) = on_core(
            left_body,
            [((4, 4, left_total, rows), BF)],
            (lower_flag, group_pos[None], *(item for pair in pairs for item in pair)),
            (),
            [pltpu.SMEM] * 2 + [pltpu.VMEM] * 8,
        )
        left, d_folded = lax.optimization_barrier((left, d_folded))
    else:
        left = [
            plane_rows(jnp.where(lower, a, b).T.reshape(count, -1, rows), group_pos, count)
            for a, b in pairs
        ]
        left = [jnp.concatenate([i.reshape(4, -1, rows) for i in items], 1) for items in zip(*left)]
    sent, to_beside = on_core(
        global_backward_body,
        [((GROUP, 3 * fold, LANES), BF), ((GROUP, 2 * half, LANES), BF)],
        (got, beside, own_seg, shared_seg, total_1, d_folded),
        head_scratch
        + [
            pltpu.VMEM((keys * 3 // 2, LANES), BF),
            pltpu.VMEM((keys * 3 // 2, LANES), F32),
            pltpu.VMEM((2, keys, LANES), F32),
            pltpu.VMEM((2, keys, LANES), F32),
        ],
    )
    back = partner(to_beside, 1, count)
    gap = 3 * fold - half - row_count - half
    back = jnp.concatenate(
        [
            jnp.zeros((GROUP, row_count, LANES), BF),
            back[:, :half],
            jnp.zeros((GROUP, gap, LANES), BF),
            back[:, half:],
        ],
        1,
    )
    sent = (sent.astype(F32) + back.astype(F32)).astype(BF)
    if count == GROUP:
        left, sent = lax.optimization_barrier((left, sent))
        left = [left[0]] + [partner(left[apart], apart, count) for apart in range(1, 4)]
    got = exchange(sent, count)
    left, got = lax.optimization_barrier((left, got))

    d_proj_1, gain_attn_1, *grad_1 = on_core(
        global_finish_body,
        [((rows, 3 * width), BF), ((1, width), F32)] + [((row_count, width), BF)] * micro_count,
        (first, got, d_mid_1, *in_1, gain_attn, global_tables),
    )

    up_0 = to_other_section(grad_1, -1)
    d_mlp = jnp.concatenate(
        [jnp.where(lower, a, up_1[i * row_count :][:row_count]) for i, a in enumerate(up_0)]
    )
    across_mlp, beside_mlp = partner(d_mlp, 2, count), partner(d_mlp, 1, count)
    gain_mlp_0, d_mid_0, d_att_0, *right = on_core(
        local_back_middle_body,
        [
            ((1, width), F32),
            ((rows, width), F32),
            ((rows, width), BF),
        ]
        + [((row_count, inner + width), BF)] * micro_count,
        (*others, lower_flag, *up_0, middle_0, gate_up_0, gain_mlp, right_1),
        [pltpu.VMEM((hidden, width), BF)],
        [pltpu.VMEM] * len(others) + [pltpu.SMEM] + [pltpu.VMEM] * 6,
    )
    d_att_0, right, across_mlp = lax.optimization_barrier((d_att_0, right, across_mlp))
    across = [partner(item, 2, count) for item in right]
    beside = [partner(item, 1, count) for item in right]
    d_mlp = [d_mlp, beside_mlp, across_mlp, partner(across_mlp, 1, count)]
    out_near, out_far = first_hop(
        on_core(
            functools.partial(early_body, [((3 * shard_total, left_total), (0, width))]),
            three_parts((hidden_total, width)),
            (*d_mlp, *left),
        ),
        count,
    )
    dq_0, d_own, d_before, d_after = on_core(
        local_backward_body,
        [
            ((rows, width), BF),
            ((rows, 2 * width), F32),
            ((rows, 2 * width), BF),
            ((rows, 2 * width), BF),
        ],
        (q_0, *around_0, bias, total_0, d_att_0, local_tables),
    )
    from_after = lax.ppermute(d_before, "dp", down_pairs)
    from_before = lax.ppermute(d_after, "dp", up_pairs)
    *d_proj, grad_0, gain_attn_sum = on_core(
        local_finish_body,
        [
            ((row_count, 3 * width), BF),
            ((row_count + EXTRA, 3 * width), BF),
            ((rows, width), BF),
            ((1, width), F32),
        ],
        (
            lower_flag, first, dq_0, d_own, from_after, from_before, local_tables, d_mid_0, in_0, gain_attn,
            gain_mlp_0, d_proj_1, gain_attn_1, gain_mlp_1,
        ),
        [pltpu.VMEM((1, width), F32), pltpu.VMEM((rows, 3 * width), BF)],
        [pltpu.SMEM] + [pltpu.VMEM] * 13,
    )
    across, out_far, _ = lax.optimization_barrier((across, out_far, d_proj[0]))
    right = right + beside + across + [partner(item, 1, count) for item in across]
    early_rows = shard_total * (inner // width + 1)
    near, far = first_hop(
        on_core(
            functools.partial(
                early_body,
                [
                    ((2 * shard_total, 3 * shard_total), (0, inner)),
                    ((shard_total, 2 * shard_total), (inner, inner + width)),
                ],
            ),
            three_parts((early_rows, width)),
            (*right, *left),
        ),
        count,
    )
    across = [partner(item, 2, count) for item in d_proj]
    beside = [partner(item, 1, count) for item in d_proj]
    far = jnp.concatenate([far, out_far])
    across, _ = lax.optimization_barrier((across, far))
    far = partner(far, 8, count)
    right = []
    for low, high in zip(d_proj[:1] + beside[:1] + across[:1], d_proj[1:] + beside[1:] + across[1:]):
        right += [low, high]
    right += [partner(item, 1, count) for item in across]
    late_in = (group_pos[None], *right, *left)
    late = on_core(
        functools.partial(late_body, (0, shard_total)),
        three_parts((shard_total, 3 * width + LANES)),
        late_in,
        [pltpu.VMEM((width, LANES), F32)],
        [pltpu.SMEM] + [pltpu.VMEM] * (len(late_in) - 1),
    )
    far, _ = lax.optimization_barrier((far, late[0]))
    early = near + far[:early_rows].astype(F32)
    mlp_out_share = out_near + far[early_rows:].astype(F32)
    late = second_hop(*first_hop(late, count), count)
    parts = [early[p * shard_total : (p + 1) * shard_total] for p in range(inner // width)]
    in_share = jnp.concatenate(parts, 1)
    attn_share = early[early_rows - shard_total :]
    gain_columns = late[:, 3 * width :]
    qkv_share, in_share, mlp_out_share, attn_share, gain_columns = (
        over_groups(item, count)
        for item in (late[:, : 3 * width], in_share, mlp_out_share, attn_share, gain_columns)
    )
    if count == GROUP:
        gains = jnp.stack([gain_columns[:, 0], gain_columns[:, 2]])
    else:
        gain_mlp_sum = jnp.where(lower, gain_mlp_0, gain_mlp_1)
        gains = lax.psum(jnp.concatenate([gain_attn_sum, gain_mlp_sum]), "dp")
        gains = lax.dynamic_slice_in_dim(gains, replica * shard, shard, 1)

    return (
        jnp.where(lower, jnp.concatenate(out_0), out_1).reshape(1, micro_count, row_count, width),
        jnp.where(lower, grad_0, jnp.concatenate(grad_1)).reshape(1, micro_count, row_count, width),
        qkv_share[None],
        attn_share[None],
        in_share[None],
        mlp_out_share[None],
        gains[:1],
        gains[1:],
    )


def solution(mesh):
    in_specs = (
        P(None, "dp", None),
        P(None, "dp"),
        P(None, "dp", None),
        P("section", "dp", None),
        P("section", "dp", None),
        P("section", "dp", None),
        P("section", "dp", None),
        P("section", "dp"),
        P("section", "dp"),
    )
    out_specs = (
        P("section", None, "dp", None),
        P("section", None, "dp", None),
        P("section", "dp", None),
        P("section", "dp", None),
        P("section", "dp", None),
        P("section", "dp", None),
        P("section", "dp"),
        P("section", "dp"),
    )
    return jax.shard_map(
        on_device, mesh=mesh, in_specs=in_specs, out_specs=out_specs, check_vma=False
    )
```

```python
import functools
import math

import jax
import jax.numpy as jnp
from jax import lax
from jax.experimental import pallas as pl
from jax.experimental.pallas import tpu as pltpu
from jax.sharding import PartitionSpec as P

HEAD_DIM = 64
GROUP = 16
HALF_WIN = 64
EXTRA = 16
LANES = 128
TILE = 256

local_log_base = math.log(10000.0)
global_log_base = math.log(160000.0)
masked_score = -1e30
SCALE = 1.0 / math.sqrt(HEAD_DIM)
BF = jnp.bfloat16
F32 = jnp.float32


def dot(left, right):
    return jnp.dot(left, right, preferred_element_type=F32)


def dot_bt(left, right):
    return lax.dot_general(left, right, (((1,), (1,)), ((), ())), preferred_element_type=F32)


def dot_at(left, right):
    return lax.dot_general(left, right, (((0,), (0,)), ((), ())), preferred_element_type=F32)


def moments(values):
    center = values - jnp.mean(values, -1, keepdims=True)
    scale = lax.rsqrt(jnp.mean(center * center, -1, keepdims=True) + 1e-05)
    return center * scale, scale


def norm_back(grad_out, gain_row, xhat, scale):
    scaled = grad_out * gain_row
    mean_grad = jnp.mean(scaled, -1, keepdims=True)
    mean_dot = jnp.mean(scaled * xhat, -1, keepdims=True)
    return (scaled - mean_grad - xhat * mean_dot) * scale


def angles(positions, log_base):
    half_dim = HEAD_DIM // 2
    fraction = (2 * jnp.arange(half_dim)).astype(F32) / HEAD_DIM
    inverse = jnp.exp(-fraction * log_base)
    table = positions.astype(F32)[:, None] * inverse[None, :]
    cosine, sine = jnp.cos(table), jnp.sin(table)
    none = jnp.zeros_like(sine)
    cosine = jnp.concatenate([cosine, cosine], 1)
    to_first = jnp.concatenate([-sine, none], 1)
    to_second = jnp.concatenate([none, sine], 1)
    return jnp.tile(jnp.stack([cosine, to_first, to_second]), (1, 2, 2))


def on_core(body, outs, args, scratch=(), spaces=None, out_spaces=None):
    return pl.pallas_call(
        body,
        out_shape=[jax.ShapeDtypeStruct(shape, dtype) for shape, dtype in outs],
        in_specs=[
            pl.BlockSpec(memory_space=space) for space in spaces or [pltpu.VMEM] * len(args)
        ],
        out_specs=[
            pl.BlockSpec(memory_space=space) for space in out_spaces or [pltpu.VMEM] * len(outs)
        ],
        scratch_shapes=scratch,
        cost_estimate=pl.CostEstimate(
            flops=2**10, bytes_accessed=2**10, transcendentals=0
        ),
        compiler_params=pltpu.CompilerParams(vmem_limit_bytes=48 * 2**20),
    )(*args)


def low_lanes():
    return lax.broadcasted_iota(jnp.int32, (1, LANES), 1) < HEAD_DIM


def swap(chunk):
    return pltpu.roll(chunk, HEAD_DIM, 1)


def chunks_of(rows):
    return [rows[:, c : c + LANES] for c in range(0, rows.shape[1], LANES)]


def rotate(chunk, tables):
    cosine, to_first, to_second = tables
    quarter = HEAD_DIM // 2
    return (
        chunk * cosine
        + pltpu.roll(chunk, LANES - quarter, 1) * to_first
        + pltpu.roll(chunk, quarter, 1) * to_second
    )


def unrotate(chunk, tables):
    cosine, to_first, to_second = tables
    quarter = HEAD_DIM // 2
    return (
        chunk * cosine
        - pltpu.roll(chunk, LANES - quarter, 1) * to_first
        - pltpu.roll(chunk, quarter, 1) * to_second
    )


def low_and_high(chunks):
    swapped = [swap(chunk) for chunk in chunks]
    low = [(swapped if h % 2 else chunks)[h // 2] for h in range(2 * len(chunks))]
    high = [(chunks if h % 2 else swapped)[h // 2] for h in range(2 * len(chunks))]
    return low, high


def targets():
    for d in range(GROUP):
        micro, chip, half = d // 8, d % 8 // 2, d % 2
        yield d, micro, 3 * chip + 2 * half, 3 * chip + 1, half


def pack_folded(chunks, ref, base):
    low, high = low_and_high(chunks)
    first = low_lanes()
    rows = chunks[0].shape[0] // 2
    half, fold = rows // 2, rows * 3 // 4
    for d, micro, own, shared, side in targets():
        start = micro * rows
        part = start + side * half
        upper = jnp.concatenate(
            [high[own][start + fold : start + rows], high[shared][part : part + half]], 0
        )
        ref[d, base : base + fold] = jnp.where(
            first, low[own][start : start + fold], upper
        ).astype(BF)


def pack_pairs(lefts, rights, ref):
    low, high = low_and_high(lefts)[0], low_and_high(rights)[1]
    first = low_lanes()
    rows = lefts[0].shape[0] // 2
    half = rows // 2
    for d, micro, own, shared, side in targets():
        start = micro * rows
        part = start + side * half
        ref[d, 0:rows] = jnp.where(
            first, low[own][start : start + rows], high[own][start : start + rows]
        ).astype(BF)
        ref[d, rows : rows + half] = jnp.where(
            first, low[shared][part : part + half], high[shared][part : part + half]
        ).astype(BF)


def unpack_folded(ref, base, rows):
    first = low_lanes()
    fold = rows * 3 // 4
    low, high = {}, {}
    shared_parts = {}
    for d, micro, own, shared, side in targets():
        block = ref[d, base : base + fold].astype(F32)
        mine = jnp.concatenate([block, swap(block[: rows - fold])], 0)
        if own % 2:
            high[micro, own] = swap(mine)
        else:
            low[micro, own] = mine
        shared_parts[micro, shared, side] = block[rows - fold :]
        if side:
            both = jnp.concatenate([shared_parts[micro, shared, 0], block[rows - fold :]], 0)
            if shared % 2:
                high[micro, shared] = both
            else:
                low[micro, shared] = swap(both)
    heads = GROUP // 4 * 3
    return [
        jnp.concatenate(
            [jnp.where(first, low[m, h], high[m, h + 1]) for m in range(2)], 0
        )
        for h in range(0, heads, 2)
    ]


def unpack_pairs(ref, rows):
    first = low_lanes()
    half = rows // 2
    pairs = {}
    parts = {}
    for d, micro, own, shared, side in targets():
        pairs[micro, own] = ref[d, 0:rows].astype(F32)
        parts[side] = ref[d, rows : rows + half].astype(F32)
        if side:
            pairs[micro, shared] = jnp.concatenate([parts[0], parts[1]], 0)
    heads = GROUP // 4 * 3
    lefts, rights = [], []
    for h in range(0, heads, 2):
        even, odd = [pairs[m, h] for m in range(2)], [pairs[m, h + 1] for m in range(2)]
        lefts.append(
            jnp.concatenate([jnp.where(first, a, swap(b)) for a, b in zip(even, odd)], 0)
        )
        rights.append(
            jnp.concatenate([jnp.where(first, swap(a), b) for a, b in zip(even, odd)], 0)
        )
    return lefts, rights


class Weights:
    def __init__(self, sources, mlp_out):
        self.sources = sources
        self.mlp_out = sources[-1]
        if len(sources) == 1:
            self.mlp_out = mlp_out
            unpack_rows(sources[0], mlp_out)

    def get(self, which):
        if which == 2:
            return self.mlp_out[...]
        if len(self.sources) > 1:
            return self.sources[which][...]
        (wide,) = self.sources
        width = wide.shape[0]
        inner = 2 * self.mlp_out.shape[0]
        return wide[:, width : width + inner] if which else wide[:, :width]


def first_block(pair):
    return -(-pair // 32) * 16


def packed_pieces(shard, rows, width):
    yield 0, shard, 0, width, 0, 0
    rest = rows - shard
    side = width // 3
    yield 0, rest, width, 2 * side, shard, 0
    yield rest, 16, width, side, shard, 2 * side
    yield rest, 16, width + side, side, shard + 16, 2 * side


def unpack_rows(wide, mlp_out):
    hidden, width = mlp_out.shape
    shard = wide.shape[0] // GROUP
    start = wide.shape[1] - width - 2 * (width // 3)
    pair = 2 * hidden // GROUP
    upper = first_block(pair)
    for d in range(GROUP):
        low = d // 2 * pair + d % 2 * upper
        have = pair - upper if d % 2 else upper
        for row, rows, column, columns, to_row, to_column in packed_pieces(shard, upper, width):
            rows = min(rows, have - to_row)
            if rows > 0:
                mlp_out[low + to_row : low + to_row + rows, to_column : to_column + columns] = wide[
                    d * shard + row : d * shard + row + rows, start + column : start + column + columns
                ]


def stack_body(odd_ref, attn_ref, mlp_in_ref, own_ref, beside_ref, out_ref):
    shard, width = attn_ref.shape
    inner = mlp_in_ref.shape[1]
    out_ref[:, :width] = attn_ref[...]
    out_ref[:, width : width + inner] = mlp_in_ref[...]
    own, beside = own_ref[...].astype(F32), beside_ref[...].astype(F32)
    moved = beside.shape[0]
    even = jnp.concatenate([own, beside], 0)
    odd = jnp.concatenate([own[moved:], beside, beside], 0)
    block = jnp.where(odd_ref[0] == 1, odd, even).astype(BF)
    start = width + inner
    for row, rows, column, columns, from_row, from_column in packed_pieces(
        shard, block.shape[0], width
    ):
        out_ref[row : row + rows, start + column : start + column + columns] = block[
            from_row : from_row + rows, from_column : from_column + columns
        ]


def mlp_forward(layer_in, attended, gain, weights):
    middle = layer_in + dot(attended, weights.get(0))
    xhat, _ = moments(middle)
    normed = (xhat * gain).astype(BF)
    gate_up = dot(normed, weights.get(1))
    half = gate_up.shape[1] // 2
    gate, up = gate_up[:, :half], gate_up[:, half:]
    cdf = 0.5 * (1.0 + lax.erf(gate * math.sqrt(0.5)))
    mixed = (gate * cdf * up).astype(BF)
    result = (middle + dot(mixed, weights.get(2))).astype(BF)
    return middle, normed, gate, up, mixed, result


def mlp_backward(upstream, middle, gate, up, gain, weights):
    d_mixed = dot_bt(upstream, weights.get(2))
    cdf = 0.5 * (1.0 + lax.erf(gate * math.sqrt(0.5)))
    density = jnp.exp(-0.5 * gate * gate) * (1.0 / math.sqrt(2.0 * math.pi))
    d_gate = d_mixed * up * (cdf + gate * density)
    d_up = d_mixed * gate * cdf
    d_gate_up = jnp.concatenate([d_gate.astype(BF), d_up.astype(BF)], 1)
    d_normed = dot_bt(d_gate_up, weights.get(1))
    xhat, scale = moments(middle)
    gain_grad = jnp.sum(d_normed * xhat, 0, keepdims=True)
    d_middle = upstream.astype(F32) + norm_back(d_normed, gain, xhat, scale)
    d_attn = d_middle.astype(BF)
    d_attended = dot_bt(d_attn, weights.get(0))
    return d_gate_up, gain_grad, d_middle, d_attn, d_attended


def project(xhat, gain, first_ref, table_ref, normed_ref):
    width = xhat.shape[1]
    normed = (xhat * gain).astype(BF)
    normed_ref[...] = normed
    tables = [table_ref[i] for i in range(3)]
    results = [dot(normed, first_ref[:, c * width : (c + 1) * width]) for c in range(3)]
    queries, keys, values = chunks_of(results[0]), chunks_of(results[1]), results[2]
    return [rotate(c, tables) for c in queries], [rotate(c, tables) for c in keys], values


def input_backward(d_middle, d_projected, x, gain_ref, first_ref, gain_out_ref):
    d_normed = dot_bt(d_projected, first_ref[:, : d_projected.shape[1]])
    xhat, scale = moments(x)
    gain_out_ref[...] = jnp.sum(d_normed * xhat, 0, keepdims=True)
    return (d_middle + norm_back(d_normed, gain_ref[...], xhat, scale)).astype(BF)


def joined(refs):
    return jnp.concatenate([ref[...] for ref in refs], 0)


def store_chunks(refs, rows):
    size = rows.shape[0] // len(refs)
    for i, ref in enumerate(refs):
        ref[...] = rows[i * size : (i + 1) * size]


def message_body(w_ref, attn_ref, mlp_ref, ids_ref, out_ref, rows_scr, ids_scr):
    shard, columns = w_ref.shape
    micro_count, row_count = ids_ref.shape
    out_ref[:, :columns] = w_ref[...]
    rows_scr[...] = jnp.zeros_like(rows_scr)
    ids_scr[...] = jnp.zeros_like(ids_scr)
    rows_scr[0:1, :shard] = attn_ref[...].astype(F32)
    rows_scr[1:2, :shard] = mlp_ref[...].astype(F32)
    ids_scr[:micro_count, :row_count] = ids_ref[...].astype(F32)
    runs = -(-row_count // shard)
    for run in range(runs):
        turned = ids_scr[...]
        if run:
            turned = pltpu.roll(turned, LANES - run * shard, 1)
        for micro in range(micro_count):
            row = 2 + micro * runs + run
            rows_scr[row : row + 1] = turned[micro : micro + 1]
    out_ref[:, columns:] = rows_scr[...].T[:shard].astype(BF)


def local_project_body(first_ref, x_ref, table_ref, extra_ref, normed_ref, q_ref, kv_ref):
    xhat, _ = moments(x_ref[...].astype(F32))
    extra = first_ref[:, first_ref.shape[1] - LANES :].astype(F32).T
    extra_ref[...] = extra[: extra_ref.shape[0]]
    queries, keys, values = project(xhat, extra[:1], first_ref, table_ref, normed_ref)
    width = values.shape[1]
    for j, (q, k) in enumerate(zip(queries, keys)):
        q_ref[:, LANES * j : LANES * (j + 1)] = q.astype(BF)
        kv_ref[:, LANES * j : LANES * (j + 1)] = k.astype(BF)
    kv_ref[:, width:] = values.astype(BF)


def two_heads(chunk):
    first = low_lanes()
    wide = chunk.astype(F32)
    return jnp.concatenate([jnp.where(first, wide, 0.0), jnp.where(first, 0.0, wide)], 0)


def pick_heads(rows):
    half = rows.shape[0] // 2
    return jnp.where(low_lanes(), rows[:half], rows[half:])


def local_parts(q_ref, before_ref, own_ref, after_ref):
    rows = q_ref.shape[0] // 2
    width = q_ref.shape[1]
    for micro in range(2):
        for j in range(width // LANES):
            here = slice(micro * rows, (micro + 1) * rows)
            lanes = slice(LANES * j, LANES * (j + 1))
            more = slice(width + LANES * j, width + LANES * (j + 1))
            keys, values = (
                jnp.concatenate([ref[here, part] for ref in (before_ref, own_ref, after_ref)], 0)
                for part in (lanes, more)
            )
            queries = (two_heads(q_ref[here, lanes]) * SCALE).astype(BF)
            yield micro * (width // LANES) + j, micro, here, lanes, more, queries, keys, values


def local_forward_body(q_ref, before_ref, own_ref, after_ref, bias_ref, att_ref, total_ref):
    parts = local_parts(q_ref, before_ref, own_ref, after_ref)
    for index, micro, here, lanes, _, queries, keys, values in parts:
        scores = dot_bt(keys, queries) + bias_ref[micro]
        peak = jnp.max(scores, 0, keepdims=True)
        weights = jnp.exp(scores - peak)
        total = jnp.sum(weights, 0, keepdims=True)
        total_ref[index] = peak + jnp.log(total)
        probs = (weights * (1.0 / total)).astype(BF)
        att_ref[here, lanes] = pick_heads(dot_at(probs, values)).astype(BF)


def local_backward_body(
    q_ref, before_ref, own_ref, after_ref, bias_ref, total_ref, d_ref, table_ref,
    dq_ref, d_own_ref, d_before_ref, d_after_ref,
):
    tables = [table_ref[i] for i in range(3)]
    parts = local_parts(q_ref, before_ref, own_ref, after_ref)
    rows = q_ref.shape[0] // 2
    for index, micro, here, lanes, more, queries, keys, values in parts:
        d_out = two_heads(d_ref[here, lanes]).astype(BF)
        probs = jnp.exp(dot_bt(keys, queries) + bias_ref[micro] - total_ref[index])
        d_probs = dot_bt(values, d_out)
        product = probs * d_probs
        delta = jnp.sum(product, 0, keepdims=True)
        d_scores = (product - probs * delta).astype(BF)
        d_queries = pick_heads(dot_at(d_scores, keys)) * SCALE
        local_tables = [table[here] for table in tables]
        dq_ref[here, lanes] = unrotate(d_queries, local_tables).astype(BF)
        for part, grads in ((lanes, dot(d_scores, queries)), (more, dot(probs.astype(BF), d_out))):
            d_before_ref[here, part] = grads[:rows].astype(BF)
            d_own_ref[here, part] = grads[rows : 2 * rows]
            d_after_ref[here, part] = grads[2 * rows :].astype(BF)


def local_finish_body(
    lower_ref, first_ref, dq_ref, own_ref, low_ref, high_ref, table_ref, d_middle_ref, x_ref, gain_ref,
    gain_mlp_ref, other_ref, other_attn_ref, other_mlp_ref, out_ref, grad_ref, gain_attn_ref,
    gain_scr,
):
    rows, width = dq_ref.shape

    @pl.when(lower_ref[0] == 1)
    def _():
        tables = [table_ref[i] for i in range(3)]
        total = own_ref[...] + low_ref[...].astype(F32) + high_ref[...].astype(F32)
        out_ref[:rows, :width] = dq_ref[...]
        for j, chunk in enumerate(chunks_of(total[:, :width])):
            start = width + LANES * j
            out_ref[:rows, start : start + LANES] = unrotate(chunk, tables).astype(BF)
        out_ref[:rows, 2 * width :] = total[:, width:].astype(BF)
        grad_ref[...] = input_backward(
            d_middle_ref[...], out_ref[:rows], x_ref[...].astype(F32), gain_ref, first_ref, gain_scr
        )

    @pl.when(lower_ref[0] == 0)
    def _():
        out_ref[:rows] = other_ref[...]
        grad_ref[...] = jnp.zeros_like(grad_ref)
        gain_scr[...] = other_attn_ref[...]

    gain_attn_ref[...] = gain_scr[...]
    gain_mlp = jnp.where(lower_ref[0] == 1, gain_mlp_ref[...], other_mlp_ref[...])
    index = lax.broadcasted_iota(jnp.int32, (EXTRA, width), 0)
    tail = jnp.zeros((EXTRA, width), F32)
    for row, gain in ((0, gain_scr[...]), (2, gain_mlp)):
        high = gain.astype(BF).astype(F32)
        tail = jnp.where(index == row, high, tail)
        tail = jnp.where(index == row + 1, gain - high, tail)
    out_ref[rows:] = jnp.zeros((EXTRA, out_ref.shape[1]), BF)
    out_ref[rows:, :width] = tail.astype(BF)


def local_middle_body(*refs):
    sources, refs = refs[:-10], refs[-10:]
    x_ref, att_ref, gain_ref, normed_ref, mixed_ref, middle_ref, gate_up_ref = refs[:7]
    weights = Weights(sources, refs[9])
    middle, normed, gate, up, mixed, result = mlp_forward(
        x_ref[...].astype(F32), att_ref[...], gain_ref[...], weights
    )
    store_chunks(refs[7:9], result)
    normed_ref[...] = normed
    mixed_ref[...] = mixed
    middle_ref[...] = middle
    half = gate.shape[1]
    gate_up_ref[:, :half] = gate
    gate_up_ref[:, half:] = up


def local_back_middle_body(*refs):
    sources, refs = refs[:-12], refs[-12:]
    lower_ref, low_ref, high_ref, middle_ref, gate_up_ref, gain_ref, other_ref = refs[:7]
    gain_out_ref, d_middle_ref, d_att_ref, right_ref = refs[7:11]
    weights = Weights(sources, refs[11])
    half = gate_up_ref.shape[1] // 2
    upstream = joined([low_ref, high_ref])
    d_gate_up, gain_grad, d_middle, d_attn, d_attended = mlp_backward(
        upstream, middle_ref[...], gate_up_ref[:, :half], gate_up_ref[:, half:],
        gain_ref[...], weights,
    )
    gain_out_ref[...] = gain_grad
    d_middle_ref[...] = d_middle
    d_att_ref[...] = d_attended.astype(BF)

    @pl.when(lower_ref[0] == 1)
    def _():
        right_ref[:, : 2 * half] = d_gate_up
        right_ref[:, 2 * half :] = d_attn

    @pl.when(lower_ref[0] == 0)
    def _():
        right_ref[...] = other_ref[...]


def global_project_body(first_ref, low_ref, high_ref, gain_ref, table_ref, normed_ref, sent_ref):
    xhat, _ = moments(joined([low_ref, high_ref]).astype(F32))
    queries, keys, values = project(xhat, gain_ref[...], first_ref, table_ref, normed_ref)
    pack_pairs(queries, keys, sent_ref)
    pack_folded(chunks_of(values), sent_ref, sent_ref.shape[1] * 2 // 3)


def flat(blocks):
    return blocks.reshape(-1, LANES)


def own_unfolded(ref, base, rows):
    fold = rows * 3 // 4
    block = ref[:, base : base + fold].astype(F32)
    rest = swap(flat(block[:, : rows - fold])).reshape(GROUP, rows - fold, LANES)
    return flat(jnp.concatenate([block, rest], 1))


def shared_unfolded(ref, start, rows):
    return swap(flat(ref[:, start : start + rows // 2].astype(F32)))


def fill_heads(got_ref, other_ref, own_seg_ref, shared_seg_ref, q_scr, k_scr, v_scr):
    rows = got_ref.shape[1] * 4 // 9
    half = rows // 2
    first = low_lanes()
    lane = lax.broadcasted_iota(jnp.int32, (1, LANES), 1) - HEAD_DIM
    own = flat(got_ref[:, 0:rows].astype(F32))
    shared = flat(got_ref[:, rows : rows + half].astype(F32))
    other = flat(other_ref[:, 0:half].astype(F32))
    count = own.shape[0]
    own_hit = lane == own_seg_ref[...]
    shared_hit = lane == shared_seg_ref[...]
    both = jnp.concatenate([shared, other], 0)
    for start, pairs, hit in (
        (0, own, own_hit),
        (count, shared, shared_hit[: count // 2]),
    ):
        marked = jnp.where(hit, 1.0, 0.0)
        q_scr[start : start + pairs.shape[0]] = jnp.where(first, pairs * SCALE, marked).astype(BF)
    for unit, pairs, hit in ((0, own, own_hit), (1, both, shared_hit)):
        marked = jnp.where(hit, 0.0, masked_score)
        k_scr[unit] = jnp.where(first, swap(pairs), marked).astype(BF)
    base = rows + half
    v_scr[0] = jnp.where(first, own_unfolded(got_ref, base, rows), 0.0).astype(BF)
    start = base + rows - rows * 3 // 4
    shared_v = jnp.concatenate(
        [shared_unfolded(got_ref, start, rows), shared_unfolded(other_ref, half, rows)], 0
    )
    v_scr[1] = jnp.where(first, shared_v, 0.0).astype(BF)


def fold_out(own, shared, rows, ref, base):
    fold = rows * 3 // 4
    blocks = own.reshape(GROUP, rows, LANES)
    swapped = swap(own).reshape(GROUP, rows, LANES)
    upper = jnp.concatenate(
        [swapped[:, fold:], swap(shared).reshape(GROUP, rows // 2, LANES)], 1
    )
    ref[:, base : base + fold] = jnp.where(low_lanes(), blocks[:, :fold], upper).astype(BF)


def global_forward_body(
    got_ref, other_ref, own_seg_ref, shared_seg_ref, out_ref, total_ref,
    q_scr, k_scr, v_scr, vt_scr, o_scr,
):
    fill_heads(got_ref, other_ref, own_seg_ref, shared_seg_ref, q_scr, k_scr, v_scr)
    for unit in range(2):
        vt_scr[unit] = v_scr[unit].astype(F32).T.astype(BF)
    count = k_scr.shape[1]

    def step(tile, carry):
        unit = tile // (count // TILE)
        rows = pl.ds(pl.multiple_of(tile * TILE, TILE), TILE)
        scores = dot_bt(k_scr[unit], q_scr[rows])
        peak = jnp.max(scores, 0, keepdims=True)
        weights = jnp.exp(scores - peak)
        total = jnp.sum(weights, 0, keepdims=True)
        total_ref[tile] = peak + jnp.log(total)
        out = dot(vt_scr[unit], weights.astype(BF)) * (1.0 / total)
        o_scr[rows] = out.T
        return carry

    lax.fori_loop(0, q_scr.shape[0] // TILE, step, 0)
    rows = got_ref.shape[1] * 4 // 9
    fold_out(o_scr[:count], o_scr[count:], rows, out_ref, 0)


def global_backward_body(
    got_ref, other_ref, own_seg_ref, shared_seg_ref, total_ref, d_ref, sent_ref, to_other_ref,
    q_scr, k_scr, v_scr, kt_scr, d_scr, dq_scr, dk_scr, dv_scr,
):
    fill_heads(got_ref, other_ref, own_seg_ref, shared_seg_ref, q_scr, k_scr, v_scr)
    first = low_lanes()
    rows = got_ref.shape[1] * 4 // 9
    half = rows // 2
    for unit in range(2):
        keys = jnp.where(first, k_scr[unit].astype(F32), 0.0)
        kt_scr[unit] = keys.T.astype(BF)
    count = k_scr.shape[1]
    d_scr[:count] = jnp.where(first, own_unfolded(d_ref, 0, rows), 0.0).astype(BF)
    d_scr[count:] = jnp.where(
        first, shared_unfolded(d_ref, rows - rows * 3 // 4, rows), 0.0
    ).astype(BF)
    dk_scr[...] = jnp.zeros_like(dk_scr)
    dv_scr[...] = jnp.zeros_like(dv_scr)

    def step(tile, carry):
        unit = tile // (count // TILE)
        here = pl.ds(pl.multiple_of(tile * TILE, TILE), TILE)
        queries, d_out = q_scr[here], d_scr[here]
        probs = jnp.exp(dot_bt(k_scr[unit], queries) - total_ref[tile])
        d_probs = dot_bt(v_scr[unit], d_out)
        product = probs * d_probs
        delta = jnp.sum(product, 0, keepdims=True)
        d_scores = (product - probs * delta).astype(BF)
        dv_scr[unit] += dot(probs.astype(BF), d_out)
        dk_scr[unit] += dot(d_scores, queries)
        dq_scr[here] = dot(kt_scr[unit], d_scores).T * SCALE
        return carry

    lax.fori_loop(0, q_scr.shape[0] // TILE, step, 0)
    mine = count // 2
    own = jnp.where(first, dq_scr[:count], swap(dk_scr[0]))
    sent_ref[:, 0:rows] = own.reshape(GROUP, rows, LANES).astype(BF)
    shared_k, shared_v = dk_scr[1], dv_scr[1]
    shared = jnp.where(first, dq_scr[count:], swap(shared_k[:mine]))
    sent_ref[:, rows : rows + half] = shared.reshape(GROUP, half, LANES).astype(BF)
    fold_out(dv_scr[0], shared_v[:mine], rows, sent_ref, rows + half)
    for place, grads in enumerate((shared_k, shared_v)):
        other = jnp.where(first, 0.0, swap(grads[mine:])).reshape(GROUP, half, LANES)
        to_other_ref[:, place * half : (place + 1) * half] = other.astype(BF)


def global_middle_body(*refs):
    sources, refs = refs[:-14], refs[-14:]
    got_ref, low_ref, high_ref, up_ref, gain_ref, out_ref, att_ref, normed_ref, mixed_ref = refs[:9]
    right_ref, gain_out_ref, d_middle_ref, sent_ref = refs[9:13]
    weights = Weights(sources, refs[13])
    rows = low_ref.shape[0]
    attended = jnp.concatenate([c.astype(BF) for c in unpack_folded(got_ref, 0, rows)], 1)
    att_ref[...] = attended
    gain = gain_ref[...]
    middle, normed, gate, up, mixed, result = mlp_forward(
        joined([low_ref, high_ref]).astype(F32), attended, gain, weights
    )
    out_ref[...] = result
    normed_ref[...] = normed
    mixed_ref[...] = mixed
    d_gate_up, gain_grad, d_middle, d_attn, d_attended = mlp_backward(
        up_ref[...], middle, gate, up, gain, weights
    )
    right_ref[:, : d_gate_up.shape[1]] = d_gate_up
    right_ref[:, d_gate_up.shape[1] :] = d_attn
    gain_out_ref[...] = gain_grad
    d_middle_ref[...] = d_middle
    pack_folded(chunks_of(d_attended), sent_ref, 0)


def global_finish_body(
    first_ref, got_ref, d_middle_ref, low_ref, high_ref, gain_ref, table_ref,
    d_proj_ref, gain_out_ref, *grad_refs,
):
    tables = [table_ref[i] for i in range(3)]
    x = joined([low_ref, high_ref]).astype(F32)
    rows = low_ref.shape[0]
    d_queries, d_keys = unpack_pairs(got_ref, rows)
    d_values = unpack_folded(got_ref, rows * 3 // 2, rows)
    parts = [unrotate(c, tables).astype(BF) for c in d_queries + d_keys]
    d_projected = jnp.concatenate(parts + [c.astype(BF) for c in d_values], 1)
    d_proj_ref[...] = d_projected
    store_chunks(
        grad_refs,
        input_backward(d_middle_ref[...], d_projected, x, gain_ref, first_ref, gain_out_ref),
    )


def neighbours(count, step):
    return [
        (i, i + step)
        for i in range(count)
        if 0 <= i + step < count and i // GROUP == (i + step) // GROUP
    ]


def exchange(blocks, count):
    groups = [list(range(s, s + GROUP)) for s in range(0, count, GROUP)]
    return lax.all_to_all(blocks, "dp", 0, 0, axis_index_groups=groups)


def to_other_section(chunks, step):
    pairs = [(0, 1)] if step > 0 else [(1, 0)]
    return [lax.ppermute(rows, "section", pairs) for rows in chunks]


def partner(rows, apart, count):
    return lax.ppermute(rows, "dp", [(i, i ^ apart) for i in range(count)])


def gather_rows(piece, group_pos, count):
    pieces = {0: piece}
    for apart in (4, 8, 12):
        pieces[apart] = partner(piece, apart, count)
    for apart in (0, 4, 8, 12):
        pieces[apart + 2] = partner(pieces[apart], 2, count)
    for apart in range(0, GROUP, 2):
        pieces[apart + 1] = partner(pieces[apart], 1, count)
    whole = jnp.zeros((GROUP,) + piece.shape, piece.dtype)
    for apart, item in pieces.items():
        start = (group_pos ^ apart,) + (0,) * piece.ndim
        whole = lax.dynamic_update_slice(whole, item[None], start)
    if count > GROUP:
        groups = [list(range(s, count, GROUP)) for s in range(GROUP)]
        whole = lax.all_gather(whole, "dp", axis=0, tiled=True, axis_index_groups=groups)
    return whole.reshape(-1, piece.shape[-1]), pieces[2]


def plane_rows(rows, group_pos, count):
    parts = rows.reshape(count // GROUP, 4, 4, *rows.shape[1:])
    place, plane = group_pos % 4, group_pos // 4
    taken = []
    for apart in range(4):
        block = lax.dynamic_index_in_dim(parts, place ^ apart, 2, keepdims=False)
        block = jnp.stack(
            [lax.dynamic_index_in_dim(block, plane ^ z, 1, keepdims=False) for z in range(4)]
        )
        taken.append(partner(block, apart, count) if apart else block)
    return taken


def left_body(lower_ref, place_ref, *refs):
    refs, out_ref = refs[:-1], refs[-1]
    base = 0
    for first_ref, second_ref in zip(refs[0::2], refs[1::2]):
        rows = jnp.where(lower_ref[0] == 1, first_ref[...].astype(F32), second_ref[...].astype(F32))
        turned = rows.T
        size = turned.shape[0] // GROUP
        for d in range(GROUP):
            side = d % 4 ^ place_ref[0] % 4
            plane = d // 4 ^ place_ref[0] // 4
            out_ref[side, plane, base : base + size] = turned[d * size : (d + 1) * size].astype(BF)
        base += size


def left_rows_of(refs, rows):
    start, end = rows
    parts = [
        jnp.concatenate([ref[p, start:end].astype(F32) for p in range(4)], 0).astype(BF) for ref in refs
    ]
    return jnp.concatenate(parts, 1)


def by_plane(result, base, outs, columns=slice(None)):
    keep, keep_far, send = outs
    rows = result.shape[0] // 4
    half = send.shape[0] // 2
    here = slice(base, base + rows)
    keep[here, columns] = result[:rows]
    keep_far[here, columns] = result[2 * rows : 3 * rows]
    send[here, columns] = result[rows : 2 * rows].astype(BF)
    send[half + base : half + base + rows, columns] = result[3 * rows :].astype(BF)


def early_body(terms, split, *refs):
    refs, outs = refs[:-3], refs[-3:]
    operands, lefts = (refs[:split], refs[split:-4]), refs[-4:]
    width = outs[0].shape[1]
    base = 0
    for which, rows, (start, end) in terms:
        right = jnp.concatenate([ref[:, start:end] for ref in operands[which]], 0)
        result = dot(left_rows_of(lefts, rows), right)
        for column in range(0, end - start, width):
            by_plane(result[:, column : column + width], base, outs)
            base += result.shape[0] // 4


def late_body(rows, place_ref, *refs):
    refs, outs, scr = refs[:-4], refs[-4:-1], refs[-1]
    rights, lefts = refs[:-4], refs[-4:]
    columns = rights[0].shape[1]
    width = columns // 3
    size = outs[0].shape[0]
    tokens = lefts[0].shape[2]
    right = jnp.concatenate([ref[:tokens] for ref in rights], 0)
    by_plane(dot(left_rows_of(lefts, rows), right), 0, outs, slice(0, columns))
    tail = sum(ref[tokens:, :width].astype(F32) for ref in rights)
    both = jnp.concatenate([tail, jnp.zeros((LANES - EXTRA, width), F32)], 0).T
    lane = lax.broadcasted_iota(jnp.int32, (1, LANES), 1)
    lows = pltpu.roll(both, LANES - 1, 1)
    scr[...] = jnp.where(lane % 2 == 0, both + lows, 0.0)
    gains = []
    for plane in range(4):
        d = (place_ref[0] // 4 ^ plane) * 4 + place_ref[0] % 4
        gains.append(scr[pl.ds(pl.multiple_of(d * size, 16), size)])
    by_plane(jnp.concatenate(gains, 0), 0, outs, slice(columns, columns + LANES))


def three_parts(shape):
    return [(shape, F32), (shape, F32), ((2 * shape[0], shape[1]), BF)]


def first_hop(blocks, count):
    keep, keep_far, send = blocks
    got = partner(send, 4, count)
    half = keep.shape[0]
    return keep + got[:half].astype(F32), (keep_far + got[half:].astype(F32)).astype(BF)


def second_hop(near, far, count):
    return near + partner(far, 8, count).astype(F32)


def over_groups(rows, count):
    if count == GROUP:
        return rows
    apart = [list(range(s, count, GROUP)) for s in range(GROUP)]
    rows = rows.reshape(count // GROUP, -1, rows.shape[1])
    return lax.psum_scatter(rows, "dp", scatter_dimension=0, axis_index_groups=apart)


def on_device(
    tokens_in,
    segment_ids,
    out_grad,
    qkv_weight,
    attn_out_weight,
    mlp_in_weight,
    mlp_out_weight,
    attn_gain,
    mlp_gain,
):
    lower = lax.axis_index("section") == 0
    lower_flag = lower.astype(jnp.int32)[None]
    shard_total = qkv_weight.shape[1] * (lax.axis_size("dp") // GROUP)
    hidden_total = mlp_out_weight.shape[1] * (lax.axis_size("dp") // GROUP)
    count = lax.axis_size("dp")
    replica = lax.axis_index("dp")
    group_pos = replica % GROUP
    micro_count, row_count, width = tokens_in.shape
    shard = qkv_weight.shape[1]
    runs = -(-row_count // shard)
    (message,) = on_core(
        message_body,
        [((shard, 3 * width + LANES), BF)],
        (qkv_weight[0], attn_gain, mlp_gain, segment_ids),
        [pltpu.VMEM((LANES, LANES), F32), pltpu.VMEM((8, LANES), F32)],
    )
    first, early_piece = gather_rows(message, group_pos, count)
    inner = mlp_in_weight.shape[2]
    hidden = mlp_out_weight.shape[1] * count
    if count == GROUP:
        moved = first_block(2 * mlp_out_weight.shape[1]) - mlp_out_weight.shape[1]
        beside = partner(mlp_out_weight[0, :moved], 1, count)
        (stacked,) = on_core(
            stack_body,
            [((shard, width + inner + width + 2 * (width // 3)), BF)],
            (
                (replica % 2)[None],
                attn_out_weight[0],
                mlp_in_weight[0],
                mlp_out_weight[0],
                beside,
            ),
            (),
            [pltpu.SMEM] + [pltpu.VMEM] * 4,
        )
        stacked, _ = lax.optimization_barrier((stacked, early_piece))
        others = [lax.all_gather(stacked, "dp", axis=0, tiled=True)]
    else:
        others = [
            lax.all_gather(item[0], "dp", axis=0, tiled=True)
            for item in (attn_out_weight, mlp_in_weight, mlp_out_weight)
        ]
    positions = group_pos * row_count + jnp.arange(row_count)
    local_tables = angles(positions, local_log_base)
    global_tables = angles(positions, global_log_base)

    rows = micro_count * row_count
    pairs = rows * width // (row_count * LANES)
    in_0 = tokens_in.reshape(rows, width)
    extra_rows = -(-(2 + micro_count * runs) // 8) * 8
    extra, normed_0, q_0, kv_0 = on_core(
        local_project_body,
        [
            ((extra_rows, width), F32),
            ((rows, width), BF),
            ((rows, width), BF),
            ((rows, 2 * width), BF),
        ],
        (first, in_0, local_tables),
    )
    gain_attn, gain_mlp = extra[:1], extra[1:2]
    all_ids = extra[2 : 2 + micro_count * runs].reshape(micro_count, runs, count, shard)
    all_ids = lax.dynamic_slice_in_dim(all_ids, replica - group_pos, GROUP, 2)
    all_ids = all_ids.swapaxes(1, 2).reshape(micro_count, GROUP, runs * shard)[..., :row_count]
    segments = all_ids.reshape(micro_count, GROUP * row_count).astype(jnp.int32)

    key_pos = positions[0] - row_count + jnp.arange(3 * row_count)
    around = jnp.pad(segments, ((0, 0), (row_count, row_count)), constant_values=-1)
    key_seg = lax.dynamic_slice_in_dim(around, group_pos * row_count, 3 * row_count, 1)
    visible = (key_seg[:, :, None] == segment_ids[:, None, :]) & (
        jnp.abs(positions[None, :] - key_pos[:, None]) <= HALF_WIN
    )[None]
    bias = jnp.tile(jnp.where(visible, 0.0, masked_score), (1, 1, 2))

    own_seg = lax.dynamic_index_in_dim(segments, group_pos // 8, 0, keepdims=False)
    halves = own_seg.reshape(GROUP, 2, row_count // 2)
    mine = lax.dynamic_index_in_dim(halves, group_pos % 2, 1, keepdims=False).reshape(-1)
    theirs = lax.dynamic_index_in_dim(halves, 1 - group_pos % 2, 1, keepdims=False).reshape(-1)
    shared_seg = jnp.concatenate([mine, theirs])[:, None]
    own_seg = own_seg[:, None]

    up_pairs, down_pairs = neighbours(count, 1), neighbours(count, -1)
    around_0 = (
        lax.ppermute(kv_0, "dp", up_pairs),
        kv_0,
        lax.ppermute(kv_0, "dp", down_pairs),
    )
    att_0, total_0 = on_core(
        local_forward_body,
        [((rows, width), BF), ((pairs, 1, LANES), F32)],
        (q_0, *around_0, bias),
    )
    n2_0, mixed_0, middle_0, gate_up_0, *out_0 = on_core(
        local_middle_body,
        [
            ((rows, width), BF),
            ((rows, hidden), BF),
            ((rows, width), F32),
            ((rows, inner), F32),
        ]
        + [((row_count, width), BF)] * micro_count,
        (*others, in_0, att_0, gain_mlp),
        [pltpu.VMEM((hidden, width), BF)],
    )

    in_1 = to_other_section(out_0, 1)
    fold = row_count * 3 // 4
    half = row_count // 2
    normed_1, sent = on_core(
        global_project_body,
        [((rows, width), BF), ((GROUP, 3 * fold, LANES), BF)],
        (first, *in_1, gain_attn, global_tables),
    )
    got = exchange(sent, count)
    beside = jnp.concatenate(
        [got[:, row_count : row_count + half], got[:, 3 * fold - half :]], 1
    )
    beside = partner(beside, 1, count)
    keys = GROUP * row_count
    tiles = keys * 3 // 2 // TILE
    head_scratch = [
        pltpu.VMEM((keys * 3 // 2, LANES), BF),
        pltpu.VMEM((2, keys, LANES), BF),
        pltpu.VMEM((2, keys, LANES), BF),
        pltpu.VMEM((2, LANES, keys), BF),
    ]
    folded, total_1 = on_core(
        global_forward_body,
        [((GROUP, fold, LANES), BF), ((tiles, 1, TILE), F32)],
        (got, beside, own_seg, shared_seg),
        head_scratch + [pltpu.VMEM((keys * 3 // 2, LANES), F32)],
    )
    folded = exchange(folded, count)

    up_1 = out_grad.reshape(rows, width)
    out_1, att_1, n2_1, mixed_1, right_1, gain_mlp_1, d_mid_1, sent = on_core(
        global_middle_body,
        [
            ((rows, width), BF),
            ((rows, width), BF),
            ((rows, width), BF),
            ((rows, hidden), BF),
            ((rows, inner + width), BF),
            ((1, width), F32),
            ((rows, width), F32),
            ((GROUP, fold, LANES), BF),
        ],
        (*others, folded, *in_1, up_1, gain_mlp),
        [pltpu.VMEM((hidden, width), BF)],
    )
    d_folded = exchange(sent, count)
    pairs = ((normed_0, normed_1), (att_0, att_1), (n2_0, n2_1), (mixed_0, mixed_1))
    left_total = 3 * shard_total + hidden_total
    if count == GROUP:
        (left,) = on_core(
            left_body,
            [((4, 4, left_total, rows), BF)],
            (lower_flag, group_pos[None], *(item for pair in pairs for item in pair)),
            (),
            [pltpu.SMEM] * 2 + [pltpu.VMEM] * 8,
        )
        left, d_folded = lax.optimization_barrier((left, d_folded))
    else:
        left = [
            plane_rows(jnp.where(lower, a, b).T.reshape(count, -1, rows), group_pos, count)
            for a, b in pairs
        ]
        left = [jnp.concatenate([i.reshape(4, -1, rows) for i in items], 1) for items in zip(*left)]
    sent, to_beside = on_core(
        global_backward_body,
        [((GROUP, 3 * fold, LANES), BF), ((GROUP, 2 * half, LANES), BF)],
        (got, beside, own_seg, shared_seg, total_1, d_folded),
        head_scratch
        + [
            pltpu.VMEM((keys * 3 // 2, LANES), BF),
            pltpu.VMEM((keys * 3 // 2, LANES), F32),
            pltpu.VMEM((2, keys, LANES), F32),
            pltpu.VMEM((2, keys, LANES), F32),
        ],
    )
    back = partner(to_beside, 1, count)
    gap = 3 * fold - half - row_count - half
    back = jnp.concatenate(
        [
            jnp.zeros((GROUP, row_count, LANES), BF),
            back[:, :half],
            jnp.zeros((GROUP, gap, LANES), BF),
            back[:, half:],
        ],
        1,
    )
    sent = (sent.astype(F32) + back.astype(F32)).astype(BF)
    if count == GROUP:
        left, sent = lax.optimization_barrier((left, sent))
        left = [left[0]] + [partner(left[apart], apart, count) for apart in range(1, 4)]
    got = exchange(sent, count)
    left, got = lax.optimization_barrier((left, got))

    d_proj_1, gain_attn_1, *grad_1 = on_core(
        global_finish_body,
        [((rows, 3 * width), BF), ((1, width), F32)] + [((row_count, width), BF)] * micro_count,
        (first, got, d_mid_1, *in_1, gain_attn, global_tables),
    )

    up_0 = to_other_section(grad_1, -1)
    d_mlp = jnp.concatenate(
        [jnp.where(lower, a, up_1[i * row_count :][:row_count]) for i, a in enumerate(up_0)]
    )
    across_mlp = partner(d_mlp, 2, count)
    gain_mlp_0, d_mid_0, d_att_0, right = on_core(
        local_back_middle_body,
        [
            ((1, width), F32),
            ((rows, width), F32),
            ((rows, width), BF),
            ((rows, inner + width), BF),
        ],
        (*others, lower_flag, *up_0, middle_0, gate_up_0, gain_mlp, right_1),
        [pltpu.VMEM((hidden, width), BF)],
        [pltpu.VMEM] * len(others) + [pltpu.SMEM] + [pltpu.VMEM] * 6,
    )
    d_att_0, right, across_mlp = lax.optimization_barrier((d_att_0, right, across_mlp))
    across = [partner(right, 2, count)]
    d_mlp = [d_mlp, partner(d_mlp, 1, count), across_mlp, partner(across_mlp, 1, count)]
    out_near, out_far = first_hop(
        on_core(
            functools.partial(early_body, [(0, (3 * shard_total, left_total), (0, width))], 4),
            three_parts((hidden_total, width)),
            (*d_mlp, *left),
        ),
        count,
    )
    dq_0, d_own, d_before, d_after = on_core(
        local_backward_body,
        [
            ((rows, width), BF),
            ((rows, 2 * width), F32),
            ((rows, 2 * width), BF),
            ((rows, 2 * width), BF),
        ],
        (q_0, *around_0, bias, total_0, d_att_0, local_tables),
    )
    from_after = lax.ppermute(d_before, "dp", down_pairs)
    from_before = lax.ppermute(d_after, "dp", up_pairs)
    from_after, out_far = lax.optimization_barrier((from_after, out_far))
    d_proj, grad_0, gain_attn_sum = on_core(
        local_finish_body,
        [
            ((rows + EXTRA, 3 * width), BF),
            ((rows, width), BF),
            ((1, width), F32),
        ],
        (
            lower_flag, first, dq_0, d_own, from_after, from_before, local_tables, d_mid_0, in_0, gain_attn,
            gain_mlp_0, d_proj_1, gain_attn_1, gain_mlp_1,
        ),
        [pltpu.VMEM((1, width), F32)],
        [pltpu.SMEM] + [pltpu.VMEM] * 13,
    )
    across_chunks = [partner(d_proj, 2, count)]
    across, right, _ = lax.optimization_barrier((across, right, d_proj))
    right = [right, partner(right, 1, count)] + across
    right += [partner(item, 1, count) for item in across]
    in_rows, attn_rows = shard_total * (inner // width), shard_total
    early_rows = in_rows + attn_rows
    terms = [
        (0, (2 * shard_total, 3 * shard_total), (0, inner)),
        (0, (shard_total, 2 * shard_total), (inner, inner + width)),
    ]
    near, far = first_hop(
        on_core(
            functools.partial(early_body, terms, len(right)),
            three_parts((early_rows, width)),
            (*right, *left),
        ),
        count,
    )
    far = jnp.concatenate([far, out_far])
    across_chunks, d_proj, _ = lax.optimization_barrier((across_chunks, d_proj, far))
    far = partner(far, 8, count)
    right = [d_proj, partner(d_proj, 1, count)] + across_chunks
    right += [partner(item, 1, count) for item in across_chunks]
    late_in = (group_pos[None], *right, *left)
    late = on_core(
        functools.partial(late_body, (0, shard_total)),
        three_parts((shard_total, 3 * width + LANES)),
        late_in,
        [pltpu.VMEM((width, LANES), F32)],
        [pltpu.SMEM] + [pltpu.VMEM] * (len(late_in) - 1),
    )
    far, _ = lax.optimization_barrier((far, late[0]))
    early = near + far[:early_rows].astype(F32)
    mlp_out_share = out_near + far[early_rows:].astype(F32)
    late = second_hop(*first_hop(late, count), count)
    parts = [early[p * shard_total : (p + 1) * shard_total] for p in range(inner // width)]
    in_share = jnp.concatenate(parts, 1)
    attn_share = early[in_rows : in_rows + attn_rows]
    gain_columns = late[:, 3 * width :]
    qkv_share, in_share, mlp_out_share, attn_share, gain_columns = (
        over_groups(item, count)
        for item in (late[:, : 3 * width], in_share, mlp_out_share, attn_share, gain_columns)
    )
    if count == GROUP:
        gains = jnp.stack([gain_columns[:, 0], gain_columns[:, 2]])
    else:
        gain_mlp_sum = jnp.where(lower, gain_mlp_0, gain_mlp_1)
        gains = lax.psum(jnp.concatenate([gain_attn_sum, gain_mlp_sum]), "dp")
        gains = lax.dynamic_slice_in_dim(gains, replica * shard, shard, 1)

    return (
        jnp.where(lower, jnp.concatenate(out_0), out_1).reshape(1, micro_count, row_count, width),
        jnp.where(lower, grad_0, jnp.concatenate(grad_1)).reshape(1, micro_count, row_count, width),
        qkv_share[None],
        attn_share[None],
        in_share[None],
        mlp_out_share[None],
        gains[:1],
        gains[1:],
    )


def solution(mesh):
    in_specs = (
        P(None, "dp", None),
        P(None, "dp"),
        P(None, "dp", None),
        P("section", "dp", None),
        P("section", "dp", None),
        P("section", "dp", None),
        P("section", "dp", None),
        P("section", "dp"),
        P("section", "dp"),
    )
    out_specs = (
        P("section", None, "dp", None),
        P("section", None, "dp", None),
        P("section", "dp", None),
        P("section", "dp", None),
        P("section", "dp", None),
        P("section", "dp", None),
        P("section", "dp"),
        P("section", "dp"),
    )
    return jax.shard_map(
        on_device, mesh=mesh, in_specs=in_specs, out_specs=out_specs, check_vma=False
    )
```

```python
import functools
import math

import jax
import jax.numpy as jnp
from jax import lax
from jax.experimental import pallas as pl
from jax.experimental.pallas import tpu as pltpu
from jax.sharding import PartitionSpec as P

HEAD_DIM = 64
GROUP = 16
HALF_WIN = 64
EXTRA = 16
LANES = 128
TILE = 256

local_log_base = math.log(10000.0)
global_log_base = math.log(160000.0)
masked_score = -1e30
SCALE = 1.0 / math.sqrt(HEAD_DIM)
BF = jnp.bfloat16
F32 = jnp.float32


def dot(left, right):
    return jnp.dot(left, right, preferred_element_type=F32)


def dot_bt(left, right):
    return lax.dot_general(left, right, (((1,), (1,)), ((), ())), preferred_element_type=F32)


def dot_at(left, right):
    return lax.dot_general(left, right, (((0,), (0,)), ((), ())), preferred_element_type=F32)


def moments(values):
    center = values - jnp.mean(values, -1, keepdims=True)
    scale = lax.rsqrt(jnp.mean(center * center, -1, keepdims=True) + 1e-05)
    return center * scale, scale


def norm_back(grad_out, gain_row, xhat, scale):
    scaled = grad_out * gain_row
    mean_grad = jnp.mean(scaled, -1, keepdims=True)
    mean_dot = jnp.mean(scaled * xhat, -1, keepdims=True)
    return (scaled - mean_grad - xhat * mean_dot) * scale


def angles(positions, log_base):
    half_dim = HEAD_DIM // 2
    fraction = (2 * jnp.arange(half_dim)).astype(F32) / HEAD_DIM
    inverse = jnp.exp(-fraction * log_base)
    table = positions.astype(F32)[:, None] * inverse[None, :]
    cosine, sine = jnp.cos(table), jnp.sin(table)
    none = jnp.zeros_like(sine)
    cosine = jnp.concatenate([cosine, cosine], 1)
    to_first = jnp.concatenate([-sine, none], 1)
    to_second = jnp.concatenate([none, sine], 1)
    return jnp.tile(jnp.stack([cosine, to_first, to_second]), (1, 2, 2))


def on_core(body, outs, args, scratch=(), spaces=None, out_spaces=None):
    return pl.pallas_call(
        body,
        out_shape=[jax.ShapeDtypeStruct(shape, dtype) for shape, dtype in outs],
        in_specs=[
            pl.BlockSpec(memory_space=space) for space in spaces or [pltpu.VMEM] * len(args)
        ],
        out_specs=[
            pl.BlockSpec(memory_space=space) for space in out_spaces or [pltpu.VMEM] * len(outs)
        ],
        scratch_shapes=scratch,
        cost_estimate=pl.CostEstimate(
            flops=2**10, bytes_accessed=2**10, transcendentals=0
        ),
        compiler_params=pltpu.CompilerParams(vmem_limit_bytes=48 * 2**20),
    )(*args)


def low_lanes():
    return lax.broadcasted_iota(jnp.int32, (1, LANES), 1) < HEAD_DIM


def swap(chunk):
    return pltpu.roll(chunk, HEAD_DIM, 1)


def chunks_of(rows):
    return [rows[:, c : c + LANES] for c in range(0, rows.shape[1], LANES)]


def rotate(chunk, tables):
    cosine, to_first, to_second = tables
    quarter = HEAD_DIM // 2
    return (
        chunk * cosine
        + pltpu.roll(chunk, LANES - quarter, 1) * to_first
        + pltpu.roll(chunk, quarter, 1) * to_second
    )


def unrotate(chunk, tables):
    cosine, to_first, to_second = tables
    quarter = HEAD_DIM // 2
    return (
        chunk * cosine
        - pltpu.roll(chunk, LANES - quarter, 1) * to_first
        - pltpu.roll(chunk, quarter, 1) * to_second
    )


def low_and_high(chunks):
    swapped = [swap(chunk) for chunk in chunks]
    low = [(swapped if h % 2 else chunks)[h // 2] for h in range(2 * len(chunks))]
    high = [(chunks if h % 2 else swapped)[h // 2] for h in range(2 * len(chunks))]
    return low, high


def targets():
    for d in range(GROUP):
        micro, chip, half = d // 8, d % 8 // 2, d % 2
        yield d, micro, 3 * chip + 2 * half, 3 * chip + 1, half


def pack_folded(chunks, ref, base):
    low, high = low_and_high(chunks)
    first = low_lanes()
    rows = chunks[0].shape[0] // 2
    half, fold = rows // 2, rows * 3 // 4
    for d, micro, own, shared, side in targets():
        start = micro * rows
        part = start + side * half
        upper = jnp.concatenate(
            [high[own][start + fold : start + rows], high[shared][part : part + half]], 0
        )
        ref[d, base : base + fold] = jnp.where(
            first, low[own][start : start + fold], upper
        ).astype(BF)


def pack_pairs(lefts, rights, ref):
    low, high = low_and_high(lefts)[0], low_and_high(rights)[1]
    first = low_lanes()
    rows = lefts[0].shape[0] // 2
    half = rows // 2
    for d, micro, own, shared, side in targets():
        start = micro * rows
        part = start + side * half
        ref[d, 0:rows] = jnp.where(
            first, low[own][start : start + rows], high[own][start : start + rows]
        ).astype(BF)
        ref[d, rows : rows + half] = jnp.where(
            first, low[shared][part : part + half], high[shared][part : part + half]
        ).astype(BF)


def unpack_folded(ref, base, rows):
    first = low_lanes()
    fold = rows * 3 // 4
    low, high = {}, {}
    shared_parts = {}
    for d, micro, own, shared, side in targets():
        block = ref[d, base : base + fold].astype(F32)
        mine = jnp.concatenate([block, swap(block[: rows - fold])], 0)
        if own % 2:
            high[micro, own] = swap(mine)
        else:
            low[micro, own] = mine
        shared_parts[micro, shared, side] = block[rows - fold :]
        if side:
            both = jnp.concatenate([shared_parts[micro, shared, 0], block[rows - fold :]], 0)
            if shared % 2:
                high[micro, shared] = both
            else:
                low[micro, shared] = swap(both)
    heads = GROUP // 4 * 3
    return [
        jnp.concatenate(
            [jnp.where(first, low[m, h], high[m, h + 1]) for m in range(2)], 0
        )
        for h in range(0, heads, 2)
    ]


def unpack_pairs(ref, rows):
    first = low_lanes()
    half = rows // 2
    pairs = {}
    parts = {}
    for d, micro, own, shared, side in targets():
        pairs[micro, own] = ref[d, 0:rows].astype(F32)
        parts[side] = ref[d, rows : rows + half].astype(F32)
        if side:
            pairs[micro, shared] = jnp.concatenate([parts[0], parts[1]], 0)
    heads = GROUP // 4 * 3
    lefts, rights = [], []
    for h in range(0, heads, 2):
        even, odd = [pairs[m, h] for m in range(2)], [pairs[m, h + 1] for m in range(2)]
        lefts.append(
            jnp.concatenate([jnp.where(first, a, swap(b)) for a, b in zip(even, odd)], 0)
        )
        rights.append(
            jnp.concatenate([jnp.where(first, swap(a), b) for a, b in zip(even, odd)], 0)
        )
    return lefts, rights


class Weights:
    def __init__(self, sources, mlp_out):
        self.sources = sources
        self.mlp_out = sources[-1]
        if len(sources) == 1:
            self.mlp_out = mlp_out
            unpack_rows(sources[0], mlp_out)

    def get(self, which):
        if which == 2:
            return self.mlp_out[...]
        if len(self.sources) > 1:
            return self.sources[which][...]
        (wide,) = self.sources
        width = wide.shape[0]
        inner = 2 * self.mlp_out.shape[0]
        return wide[:, width : width + inner] if which else wide[:, :width]


def first_block(pair):
    return -(-pair // 32) * 16


def packed_pieces(shard, rows, width):
    yield 0, shard, 0, width, 0, 0
    rest = rows - shard
    side = width // 3
    yield 0, rest, width, 2 * side, shard, 0
    yield rest, 16, width, side, shard, 2 * side
    yield rest, 16, width + side, side, shard + 16, 2 * side


def unpack_rows(wide, mlp_out):
    hidden, width = mlp_out.shape
    shard = wide.shape[0] // GROUP
    start = wide.shape[1] - width - 2 * (width // 3)
    pair = 2 * hidden // GROUP
    upper = first_block(pair)
    for d in range(GROUP):
        low = d // 2 * pair + d % 2 * upper
        have = pair - upper if d % 2 else upper
        for row, rows, column, columns, to_row, to_column in packed_pieces(shard, upper, width):
            rows = min(rows, have - to_row)
            if rows > 0:
                mlp_out[low + to_row : low + to_row + rows, to_column : to_column + columns] = wide[
                    d * shard + row : d * shard + row + rows, start + column : start + column + columns
                ]


def stack_body(odd_ref, attn_ref, mlp_in_ref, own_ref, beside_ref, out_ref):
    shard, width = attn_ref.shape
    inner = mlp_in_ref.shape[1]
    out_ref[:, :width] = attn_ref[...]
    out_ref[:, width : width + inner] = mlp_in_ref[...]
    own, beside = own_ref[...].astype(F32), beside_ref[...].astype(F32)
    moved = beside.shape[0]
    even = jnp.concatenate([own, beside], 0)
    odd = jnp.concatenate([own[moved:], beside, beside], 0)
    block = jnp.where(odd_ref[0] == 1, odd, even).astype(BF)
    start = width + inner
    for row, rows, column, columns, from_row, from_column in packed_pieces(
        shard, block.shape[0], width
    ):
        out_ref[row : row + rows, start + column : start + column + columns] = block[
            from_row : from_row + rows, from_column : from_column + columns
        ]


def mlp_forward(layer_in, attended, gain, weights):
    middle = layer_in + dot(attended, weights.get(0))
    xhat, _ = moments(middle)
    normed = (xhat * gain).astype(BF)
    gate_up = dot(normed, weights.get(1))
    half = gate_up.shape[1] // 2
    gate, up = gate_up[:, :half], gate_up[:, half:]
    cdf = 0.5 * (1.0 + lax.erf(gate * math.sqrt(0.5)))
    mixed = (gate * cdf * up).astype(BF)
    result = (middle + dot(mixed, weights.get(2))).astype(BF)
    return middle, normed, gate, up, mixed, result


def mlp_backward(upstream, middle, gate, up, gain, weights):
    d_mixed = dot_bt(upstream, weights.get(2))
    cdf = 0.5 * (1.0 + lax.erf(gate * math.sqrt(0.5)))
    density = jnp.exp(-0.5 * gate * gate) * (1.0 / math.sqrt(2.0 * math.pi))
    d_gate = d_mixed * up * (cdf + gate * density)
    d_up = d_mixed * gate * cdf
    d_gate_up = jnp.concatenate([d_gate.astype(BF), d_up.astype(BF)], 1)
    d_normed = dot_bt(d_gate_up, weights.get(1))
    xhat, scale = moments(middle)
    gain_grad = jnp.sum(d_normed * xhat, 0, keepdims=True)
    d_middle = upstream.astype(F32) + norm_back(d_normed, gain, xhat, scale)
    d_attn = d_middle.astype(BF)
    d_attended = dot_bt(d_attn, weights.get(0))
    return d_gate_up, gain_grad, d_middle, d_attn, d_attended


def project(xhat, gain, first_ref, table_ref, normed_ref):
    width = xhat.shape[1]
    normed = (xhat * gain).astype(BF)
    normed_ref[...] = normed
    tables = [table_ref[i] for i in range(3)]
    results = [dot(normed, first_ref[:, c * width : (c + 1) * width]) for c in range(3)]
    queries, keys, values = chunks_of(results[0]), chunks_of(results[1]), results[2]
    return [rotate(c, tables) for c in queries], [rotate(c, tables) for c in keys], values


def input_backward(d_middle, d_projected, x, gain_ref, first_ref, gain_out_ref):
    d_normed = dot_bt(d_projected, first_ref[:, : d_projected.shape[1]])
    xhat, scale = moments(x)
    gain_out_ref[...] = jnp.sum(d_normed * xhat, 0, keepdims=True)
    return (d_middle + norm_back(d_normed, gain_ref[...], xhat, scale)).astype(BF)


def joined(refs):
    return jnp.concatenate([ref[...] for ref in refs], 0)


def store_chunks(refs, rows):
    size = rows.shape[0] // len(refs)
    for i, ref in enumerate(refs):
        ref[...] = rows[i * size : (i + 1) * size]


def message_body(w_ref, attn_ref, mlp_ref, ids_ref, out_ref, rows_scr, ids_scr):
    shard, columns = w_ref.shape
    micro_count, row_count = ids_ref.shape
    out_ref[:, :columns] = w_ref[...]
    rows_scr[...] = jnp.zeros_like(rows_scr)
    ids_scr[...] = jnp.zeros_like(ids_scr)
    rows_scr[0:1, :shard] = attn_ref[...].astype(F32)
    rows_scr[1:2, :shard] = mlp_ref[...].astype(F32)
    ids_scr[:micro_count, :row_count] = ids_ref[...].astype(F32)
    runs = -(-row_count // shard)
    for run in range(runs):
        turned = ids_scr[...]
        if run:
            turned = pltpu.roll(turned, LANES - run * shard, 1)
        for micro in range(micro_count):
            row = 2 + micro * runs + run
            rows_scr[row : row + 1] = turned[micro : micro + 1]
    out_ref[:, columns:] = rows_scr[...].T[:shard].astype(BF)


def local_project_body(first_ref, x_ref, table_ref, extra_ref, normed_ref, q_ref, kv_ref):
    xhat, _ = moments(x_ref[...].astype(F32))
    extra = first_ref[:, first_ref.shape[1] - LANES :].astype(F32).T
    extra_ref[...] = extra[: extra_ref.shape[0]]
    queries, keys, values = project(xhat, extra[:1], first_ref, table_ref, normed_ref)
    width = values.shape[1]
    for j, (q, k) in enumerate(zip(queries, keys)):
        q_ref[:, LANES * j : LANES * (j + 1)] = q.astype(BF)
        kv_ref[:, LANES * j : LANES * (j + 1)] = k.astype(BF)
    kv_ref[:, width:] = values.astype(BF)


def two_heads(chunk):
    first = low_lanes()
    wide = chunk.astype(F32)
    return jnp.concatenate([jnp.where(first, wide, 0.0), jnp.where(first, 0.0, wide)], 0)


def pick_heads(rows):
    half = rows.shape[0] // 2
    return jnp.where(low_lanes(), rows[:half], rows[half:])


def local_parts(q_ref, before_ref, own_ref, after_ref):
    rows = q_ref.shape[0] // 2
    width = q_ref.shape[1]
    for micro in range(2):
        for j in range(width // LANES):
            here = slice(micro * rows, (micro + 1) * rows)
            lanes = slice(LANES * j, LANES * (j + 1))
            more = slice(width + LANES * j, width + LANES * (j + 1))
            keys, values = (
                jnp.concatenate([ref[here, part] for ref in (before_ref, own_ref, after_ref)], 0)
                for part in (lanes, more)
            )
            queries = (two_heads(q_ref[here, lanes]) * SCALE).astype(BF)
            yield micro * (width // LANES) + j, micro, here, lanes, more, queries, keys, values


def local_forward_body(q_ref, before_ref, own_ref, after_ref, bias_ref, att_ref, total_ref):
    parts = local_parts(q_ref, before_ref, own_ref, after_ref)
    for index, micro, here, lanes, _, queries, keys, values in parts:
        scores = dot_bt(keys, queries) + bias_ref[micro]
        peak = jnp.max(scores, 0, keepdims=True)
        weights = jnp.exp(scores - peak)
        total = jnp.sum(weights, 0, keepdims=True)
        total_ref[index] = peak + jnp.log(total)
        probs = (weights * (1.0 / total)).astype(BF)
        att_ref[here, lanes] = pick_heads(dot_at(probs, values)).astype(BF)


def local_backward_body(
    q_ref, before_ref, own_ref, after_ref, bias_ref, total_ref, d_ref, table_ref,
    dq_ref, d_own_ref, d_before_ref, d_after_ref,
):
    tables = [table_ref[i] for i in range(3)]
    parts = local_parts(q_ref, before_ref, own_ref, after_ref)
    rows = q_ref.shape[0] // 2
    for index, micro, here, lanes, more, queries, keys, values in parts:
        d_out = two_heads(d_ref[here, lanes]).astype(BF)
        probs = jnp.exp(dot_bt(keys, queries) + bias_ref[micro] - total_ref[index])
        d_probs = dot_bt(values, d_out)
        product = probs * d_probs
        delta = jnp.sum(product, 0, keepdims=True)
        d_scores = (product - probs * delta).astype(BF)
        d_queries = pick_heads(dot_at(d_scores, keys)) * SCALE
        local_tables = [table[here] for table in tables]
        dq_ref[here, lanes] = unrotate(d_queries, local_tables).astype(BF)
        for part, grads in ((lanes, dot(d_scores, queries)), (more, dot(probs.astype(BF), d_out))):
            d_before_ref[here, part] = grads[:rows].astype(BF)
            d_own_ref[here, part] = grads[rows : 2 * rows]
            d_after_ref[here, part] = grads[2 * rows :].astype(BF)


def local_finish_body(
    lower_ref, first_ref, dq_ref, own_ref, low_ref, high_ref, table_ref, d_middle_ref, x_ref, gain_ref,
    gain_mlp_ref, other_ref, other_attn_ref, other_mlp_ref, out_ref, grad_ref, gain_attn_ref,
    gain_scr,
):
    rows, width = dq_ref.shape

    @pl.when(lower_ref[0] == 1)
    def _():
        tables = [table_ref[i] for i in range(3)]
        total = own_ref[...] + low_ref[...].astype(F32) + high_ref[...].astype(F32)
        out_ref[:rows, :width] = dq_ref[...]
        for j, chunk in enumerate(chunks_of(total[:, :width])):
            start = width + LANES * j
            out_ref[:rows, start : start + LANES] = unrotate(chunk, tables).astype(BF)
        out_ref[:rows, 2 * width :] = total[:, width:].astype(BF)
        grad_ref[...] = input_backward(
            d_middle_ref[...], out_ref[:rows], x_ref[...].astype(F32), gain_ref, first_ref, gain_scr
        )

    @pl.when(lower_ref[0] == 0)
    def _():
        out_ref[:rows] = other_ref[...]
        grad_ref[...] = jnp.zeros_like(grad_ref)
        gain_scr[...] = other_attn_ref[...]

    gain_attn_ref[...] = gain_scr[...]
    gain_mlp = jnp.where(lower_ref[0] == 1, gain_mlp_ref[...], other_mlp_ref[...])
    index = lax.broadcasted_iota(jnp.int32, (EXTRA, width), 0)
    tail = jnp.zeros((EXTRA, width), F32)
    for row, gain in ((0, gain_scr[...]), (2, gain_mlp)):
        high = gain.astype(BF).astype(F32)
        tail = jnp.where(index == row, high, tail)
        tail = jnp.where(index == row + 1, gain - high, tail)
    out_ref[rows:] = jnp.zeros((EXTRA, out_ref.shape[1]), BF)
    out_ref[rows:, :width] = tail.astype(BF)


def local_middle_body(*refs):
    sources, refs = refs[:-10], refs[-10:]
    x_ref, att_ref, gain_ref, normed_ref, mixed_ref, middle_ref, gate_up_ref = refs[:7]
    weights = Weights(sources, refs[9])
    middle, normed, gate, up, mixed, result = mlp_forward(
        x_ref[...].astype(F32), att_ref[...], gain_ref[...], weights
    )
    store_chunks(refs[7:9], result)
    normed_ref[...] = normed
    mixed_ref[...] = mixed
    middle_ref[...] = middle
    half = gate.shape[1]
    gate_up_ref[:, :half] = gate
    gate_up_ref[:, half:] = up


def local_back_middle_body(*refs):
    sources, refs = refs[:-14], refs[-14:]
    lower_ref, low_ref, high_ref, middle_ref, gate_up_ref, gain_ref, other_ref = refs[:7]
    gain_out_ref, d_middle_ref, d_att_ref, right_ref, right_low_ref, right_high_ref = refs[7:13]
    weights = Weights(sources, refs[13])
    half = gate_up_ref.shape[1] // 2
    upstream = joined([low_ref, high_ref])
    d_gate_up, gain_grad, d_middle, d_attn, d_attended = mlp_backward(
        upstream, middle_ref[...], gate_up_ref[:, :half], gate_up_ref[:, half:],
        gain_ref[...], weights,
    )
    gain_out_ref[...] = gain_grad
    d_middle_ref[...] = d_middle
    d_att_ref[...] = d_attended.astype(BF)

    @pl.when(lower_ref[0] == 1)
    def _():
        right_ref[:, : 2 * half] = d_gate_up
        right_ref[:, 2 * half :] = d_attn

    @pl.when(lower_ref[0] == 0)
    def _():
        right_ref[...] = other_ref[...]

    store_chunks((right_low_ref, right_high_ref), right_ref[...])


def global_project_body(first_ref, low_ref, high_ref, gain_ref, table_ref, normed_ref, sent_ref):
    xhat, _ = moments(joined([low_ref, high_ref]).astype(F32))
    queries, keys, values = project(xhat, gain_ref[...], first_ref, table_ref, normed_ref)
    pack_pairs(queries, keys, sent_ref)
    pack_folded(chunks_of(values), sent_ref, sent_ref.shape[1] * 2 // 3)


def flat(blocks):
    return blocks.reshape(-1, LANES)


def own_unfolded(ref, base, rows):
    fold = rows * 3 // 4
    block = ref[:, base : base + fold].astype(F32)
    rest = swap(flat(block[:, : rows - fold])).reshape(GROUP, rows - fold, LANES)
    return flat(jnp.concatenate([block, rest], 1))


def shared_unfolded(ref, start, rows):
    return swap(flat(ref[:, start : start + rows // 2].astype(F32)))


def fill_heads(got_ref, other_ref, own_seg_ref, shared_seg_ref, q_scr, k_scr, v_scr):
    rows = got_ref.shape[1] * 4 // 9
    half = rows // 2
    first = low_lanes()
    lane = lax.broadcasted_iota(jnp.int32, (1, LANES), 1) - HEAD_DIM
    own = flat(got_ref[:, 0:rows].astype(F32))
    shared = flat(got_ref[:, rows : rows + half].astype(F32))
    other = flat(other_ref[:, 0:half].astype(F32))
    count = own.shape[0]
    own_hit = lane == own_seg_ref[...]
    shared_hit = lane == shared_seg_ref[...]
    both = jnp.concatenate([shared, other], 0)
    for start, pairs, hit in (
        (0, own, own_hit),
        (count, shared, shared_hit[: count // 2]),
    ):
        marked = jnp.where(hit, 1.0, 0.0)
        q_scr[start : start + pairs.shape[0]] = jnp.where(first, pairs * SCALE, marked).astype(BF)
    for unit, pairs, hit in ((0, own, own_hit), (1, both, shared_hit)):
        marked = jnp.where(hit, 0.0, masked_score)
        k_scr[unit] = jnp.where(first, swap(pairs), marked).astype(BF)
    base = rows + half
    v_scr[0] = jnp.where(first, own_unfolded(got_ref, base, rows), 0.0).astype(BF)
    start = base + rows - rows * 3 // 4
    shared_v = jnp.concatenate(
        [shared_unfolded(got_ref, start, rows), shared_unfolded(other_ref, half, rows)], 0
    )
    v_scr[1] = jnp.where(first, shared_v, 0.0).astype(BF)


def fold_out(own, shared, rows, ref, base):
    fold = rows * 3 // 4
    blocks = own.reshape(GROUP, rows, LANES)
    swapped = swap(own).reshape(GROUP, rows, LANES)
    upper = jnp.concatenate(
        [swapped[:, fold:], swap(shared).reshape(GROUP, rows // 2, LANES)], 1
    )
    ref[:, base : base + fold] = jnp.where(low_lanes(), blocks[:, :fold], upper).astype(BF)


def global_forward_body(
    got_ref, other_ref, own_seg_ref, shared_seg_ref, out_ref, total_ref,
    q_scr, k_scr, v_scr, vt_scr, o_scr,
):
    fill_heads(got_ref, other_ref, own_seg_ref, shared_seg_ref, q_scr, k_scr, v_scr)
    for unit in range(2):
        vt_scr[unit] = v_scr[unit].astype(F32).T.astype(BF)
    count = k_scr.shape[1]

    def step(tile, carry):
        unit = tile // (count // TILE)
        rows = pl.ds(pl.multiple_of(tile * TILE, TILE), TILE)
        scores = dot_bt(k_scr[unit], q_scr[rows])
        peak = jnp.max(scores, 0, keepdims=True)
        weights = jnp.exp(scores - peak)
        total = jnp.sum(weights, 0, keepdims=True)
        total_ref[tile] = peak + jnp.log(total)
        out = dot(vt_scr[unit], weights.astype(BF)) * (1.0 / total)
        o_scr[rows] = out.T
        return carry

    lax.fori_loop(0, q_scr.shape[0] // TILE, step, 0)
    rows = got_ref.shape[1] * 4 // 9
    fold_out(o_scr[:count], o_scr[count:], rows, out_ref, 0)


def global_backward_body(
    got_ref, other_ref, own_seg_ref, shared_seg_ref, total_ref, d_ref, sent_ref, to_other_ref,
    q_scr, k_scr, v_scr, kt_scr, d_scr, dq_scr, dk_scr, dv_scr,
):
    fill_heads(got_ref, other_ref, own_seg_ref, shared_seg_ref, q_scr, k_scr, v_scr)
    first = low_lanes()
    rows = got_ref.shape[1] * 4 // 9
    half = rows // 2
    for unit in range(2):
        keys = jnp.where(first, k_scr[unit].astype(F32), 0.0)
        kt_scr[unit] = keys.T.astype(BF)
    count = k_scr.shape[1]
    d_scr[:count] = jnp.where(first, own_unfolded(d_ref, 0, rows), 0.0).astype(BF)
    d_scr[count:] = jnp.where(
        first, shared_unfolded(d_ref, rows - rows * 3 // 4, rows), 0.0
    ).astype(BF)
    dk_scr[...] = jnp.zeros_like(dk_scr)
    dv_scr[...] = jnp.zeros_like(dv_scr)

    def step(tile, carry):
        unit = tile // (count // TILE)
        here = pl.ds(pl.multiple_of(tile * TILE, TILE), TILE)
        queries, d_out = q_scr[here], d_scr[here]
        probs = jnp.exp(dot_bt(k_scr[unit], queries) - total_ref[tile])
        d_probs = dot_bt(v_scr[unit], d_out)
        product = probs * d_probs
        delta = jnp.sum(product, 0, keepdims=True)
        d_scores = (product - probs * delta).astype(BF)
        dv_scr[unit] += dot(probs.astype(BF), d_out)
        dk_scr[unit] += dot(d_scores, queries)
        dq_scr[here] = dot(kt_scr[unit], d_scores).T * SCALE
        return carry

    lax.fori_loop(0, q_scr.shape[0] // TILE, step, 0)
    mine = count // 2
    own = jnp.where(first, dq_scr[:count], swap(dk_scr[0]))
    sent_ref[:, 0:rows] = own.reshape(GROUP, rows, LANES).astype(BF)
    shared_k, shared_v = dk_scr[1], dv_scr[1]
    shared = jnp.where(first, dq_scr[count:], swap(shared_k[:mine]))
    sent_ref[:, rows : rows + half] = shared.reshape(GROUP, half, LANES).astype(BF)
    fold_out(dv_scr[0], shared_v[:mine], rows, sent_ref, rows + half)
    for place, grads in enumerate((shared_k, shared_v)):
        other = jnp.where(first, 0.0, swap(grads[mine:])).reshape(GROUP, half, LANES)
        to_other_ref[:, place * half : (place + 1) * half] = other.astype(BF)


def global_middle_body(*refs):
    sources, refs = refs[:-14], refs[-14:]
    got_ref, low_ref, high_ref, up_ref, gain_ref, out_ref, att_ref, normed_ref, mixed_ref = refs[:9]
    right_ref, gain_out_ref, d_middle_ref, sent_ref = refs[9:13]
    weights = Weights(sources, refs[13])
    rows = low_ref.shape[0]
    attended = jnp.concatenate([c.astype(BF) for c in unpack_folded(got_ref, 0, rows)], 1)
    att_ref[...] = attended
    gain = gain_ref[...]
    middle, normed, gate, up, mixed, result = mlp_forward(
        joined([low_ref, high_ref]).astype(F32), attended, gain, weights
    )
    out_ref[...] = result
    normed_ref[...] = normed
    mixed_ref[...] = mixed
    d_gate_up, gain_grad, d_middle, d_attn, d_attended = mlp_backward(
        up_ref[...], middle, gate, up, gain, weights
    )
    right_ref[:, : d_gate_up.shape[1]] = d_gate_up
    right_ref[:, d_gate_up.shape[1] :] = d_attn
    gain_out_ref[...] = gain_grad
    d_middle_ref[...] = d_middle
    pack_folded(chunks_of(d_attended), sent_ref, 0)


def global_finish_body(
    first_ref, got_ref, d_middle_ref, low_ref, high_ref, gain_ref, table_ref,
    d_proj_ref, gain_out_ref, *grad_refs,
):
    tables = [table_ref[i] for i in range(3)]
    x = joined([low_ref, high_ref]).astype(F32)
    rows = low_ref.shape[0]
    d_queries, d_keys = unpack_pairs(got_ref, rows)
    d_values = unpack_folded(got_ref, rows * 3 // 2, rows)
    parts = [unrotate(c, tables).astype(BF) for c in d_queries + d_keys]
    d_projected = jnp.concatenate(parts + [c.astype(BF) for c in d_values], 1)
    d_proj_ref[...] = d_projected
    store_chunks(
        grad_refs,
        input_backward(d_middle_ref[...], d_projected, x, gain_ref, first_ref, gain_out_ref),
    )


def neighbours(count, step):
    return [
        (i, i + step)
        for i in range(count)
        if 0 <= i + step < count and i // GROUP == (i + step) // GROUP
    ]


def exchange(blocks, count):
    groups = [list(range(s, s + GROUP)) for s in range(0, count, GROUP)]
    return lax.all_to_all(blocks, "dp", 0, 0, axis_index_groups=groups)


def to_other_section(chunks, step):
    pairs = [(0, 1)] if step > 0 else [(1, 0)]
    return [lax.ppermute(rows, "section", pairs) for rows in chunks]


def partner(rows, apart, count):
    return lax.ppermute(rows, "dp", [(i, i ^ apart) for i in range(count)])


def gather_rows(piece, group_pos, count):
    pieces = {0: piece}
    for apart in (4, 8, 12):
        pieces[apart] = partner(piece, apart, count)
    for apart in (0, 4, 8, 12):
        pieces[apart + 2] = partner(pieces[apart], 2, count)
    for apart in range(0, GROUP, 2):
        pieces[apart + 1] = partner(pieces[apart], 1, count)
    whole = jnp.zeros((GROUP,) + piece.shape, piece.dtype)
    for apart, item in pieces.items():
        start = (group_pos ^ apart,) + (0,) * piece.ndim
        whole = lax.dynamic_update_slice(whole, item[None], start)
    if count > GROUP:
        groups = [list(range(s, count, GROUP)) for s in range(GROUP)]
        whole = lax.all_gather(whole, "dp", axis=0, tiled=True, axis_index_groups=groups)
    return whole.reshape(-1, piece.shape[-1]), pieces[2]


def plane_rows(rows, group_pos, count):
    parts = rows.reshape(count // GROUP, 4, 4, *rows.shape[1:])
    place, plane = group_pos % 4, group_pos // 4
    taken = []
    for apart in range(4):
        block = lax.dynamic_index_in_dim(parts, place ^ apart, 2, keepdims=False)
        block = jnp.stack(
            [lax.dynamic_index_in_dim(block, plane ^ z, 1, keepdims=False) for z in range(4)]
        )
        taken.append(partner(block, apart, count) if apart else block)
    return taken


def left_body(lower_ref, place_ref, *refs):
    refs, out_ref = refs[:-1], refs[-1]
    base = 0
    for first_ref, second_ref in zip(refs[0::2], refs[1::2]):
        rows = jnp.where(lower_ref[0] == 1, first_ref[...].astype(F32), second_ref[...].astype(F32))
        turned = rows.T
        size = turned.shape[0] // GROUP
        for d in range(GROUP):
            side = d % 4 ^ place_ref[0] % 4
            plane = d // 4 ^ place_ref[0] // 4
            out_ref[side, plane, base : base + size] = turned[d * size : (d + 1) * size].astype(BF)
        base += size


def left_rows_of(refs, rows):
    start, end = rows
    parts = [
        jnp.concatenate([ref[p, start:end].astype(F32) for p in range(4)], 0).astype(BF) for ref in refs
    ]
    return jnp.concatenate(parts, 1)


def by_plane(result, base, outs, columns=slice(None)):
    keep, keep_far, send = outs
    rows = result.shape[0] // 4
    half = send.shape[0] // 2
    here = slice(base, base + rows)
    keep[here, columns] = result[:rows]
    keep_far[here, columns] = result[2 * rows : 3 * rows]
    send[here, columns] = result[rows : 2 * rows].astype(BF)
    send[half + base : half + base + rows, columns] = result[3 * rows :].astype(BF)


def four_parts(refs, columns, tokens):
    own, other, across = refs[0], refs[1], refs[2:]
    size = own.shape[0]
    got = [across[0][:tokens, columns]] if len(across) == 1 else [ref[:, columns] for ref in across]
    parts = [own[:tokens, columns], other[:tokens, columns], *got]
    return jnp.concatenate(parts + [other[size : size + tokens, columns]], 0)


def early_body(terms, split, *refs):
    refs, outs = refs[:-3], refs[-3:]
    operands, lefts = (refs[:split], refs[split:-4]), refs[-4:]
    width = outs[0].shape[1]
    base = 0
    for which, rows, (start, end) in terms:
        right = four_parts(operands[which], slice(start, end), lefts[0].shape[2])
        result = dot(left_rows_of(lefts, rows), right)
        for column in range(0, end - start, width):
            by_plane(result[:, column : column + width], base, outs)
            base += result.shape[0] // 4


def late_body(rows, place_ref, *refs):
    refs, outs, scr = refs[:-4], refs[-4:-1], refs[-1]
    rights, lefts = refs[:-4], refs[-4:]
    columns = rights[0].shape[1]
    width = columns // 3
    size = outs[0].shape[0]
    tokens = lefts[0].shape[2]
    right = four_parts(rights, slice(None), tokens)
    by_plane(dot(left_rows_of(lefts, rows), right), 0, outs, slice(0, columns))
    own, other, across = rights
    ends = [ref[tokens : tokens + EXTRA, :width] for ref in rights]
    ends.append(other[own.shape[0] + tokens :, :width])
    tail = sum(part.astype(F32) for part in ends)
    both = jnp.concatenate([tail, jnp.zeros((LANES - EXTRA, width), F32)], 0).T
    lane = lax.broadcasted_iota(jnp.int32, (1, LANES), 1)
    lows = pltpu.roll(both, LANES - 1, 1)
    scr[...] = jnp.where(lane % 2 == 0, both + lows, 0.0)
    gains = []
    for plane in range(4):
        d = (place_ref[0] // 4 ^ plane) * 4 + place_ref[0] % 4
        gains.append(scr[pl.ds(pl.multiple_of(d * size, 16), size)])
    by_plane(jnp.concatenate(gains, 0), 0, outs, slice(columns, columns + LANES))


def three_parts(shape):
    return [(shape, F32), (shape, F32), ((2 * shape[0], shape[1]), BF)]


def with_core(rows, across, count):
    return [rows, partner(jnp.concatenate([rows, *across]), 1, count), *across]


def first_hop(blocks, count):
    keep, keep_far, send = blocks
    got = partner(send, 4, count)
    half = keep.shape[0]
    return keep + got[:half].astype(F32), (keep_far + got[half:].astype(F32)).astype(BF)


def second_hop(near, far, count):
    return near + partner(far, 8, count).astype(F32)


def over_groups(rows, count):
    if count == GROUP:
        return rows
    apart = [list(range(s, count, GROUP)) for s in range(GROUP)]
    rows = rows.reshape(count // GROUP, -1, rows.shape[1])
    return lax.psum_scatter(rows, "dp", scatter_dimension=0, axis_index_groups=apart)


def on_device(
    tokens_in,
    segment_ids,
    out_grad,
    qkv_weight,
    attn_out_weight,
    mlp_in_weight,
    mlp_out_weight,
    attn_gain,
    mlp_gain,
):
    lower = lax.axis_index("section") == 0
    lower_flag = lower.astype(jnp.int32)[None]
    shard_total = qkv_weight.shape[1] * (lax.axis_size("dp") // GROUP)
    hidden_total = mlp_out_weight.shape[1] * (lax.axis_size("dp") // GROUP)
    count = lax.axis_size("dp")
    replica = lax.axis_index("dp")
    group_pos = replica % GROUP
    micro_count, row_count, width = tokens_in.shape
    shard = qkv_weight.shape[1]
    runs = -(-row_count // shard)
    (message,) = on_core(
        message_body,
        [((shard, 3 * width + LANES), BF)],
        (qkv_weight[0], attn_gain, mlp_gain, segment_ids),
        [pltpu.VMEM((LANES, LANES), F32), pltpu.VMEM((8, LANES), F32)],
    )
    first, early_piece = gather_rows(message, group_pos, count)
    inner = mlp_in_weight.shape[2]
    hidden = mlp_out_weight.shape[1] * count
    if count == GROUP:
        moved = first_block(2 * mlp_out_weight.shape[1]) - mlp_out_weight.shape[1]
        beside = partner(mlp_out_weight[0, :moved], 1, count)
        (stacked,) = on_core(
            stack_body,
            [((shard, width + inner + width + 2 * (width // 3)), BF)],
            (
                (replica % 2)[None],
                attn_out_weight[0],
                mlp_in_weight[0],
                mlp_out_weight[0],
                beside,
            ),
            (),
            [pltpu.SMEM] + [pltpu.VMEM] * 4,
        )
        stacked, _ = lax.optimization_barrier((stacked, early_piece))
        others = [lax.all_gather(stacked, "dp", axis=0, tiled=True)]
    else:
        others = [
            lax.all_gather(item[0], "dp", axis=0, tiled=True)
            for item in (attn_out_weight, mlp_in_weight, mlp_out_weight)
        ]
    positions = group_pos * row_count + jnp.arange(row_count)
    local_tables = angles(positions, local_log_base)
    global_tables = angles(positions, global_log_base)

    rows = micro_count * row_count
    pairs = rows * width // (row_count * LANES)
    in_0 = tokens_in.reshape(rows, width)
    extra_rows = -(-(2 + micro_count * runs) // 8) * 8
    extra, normed_0, q_0, kv_0 = on_core(
        local_project_body,
        [
            ((extra_rows, width), F32),
            ((rows, width), BF),
            ((rows, width), BF),
            ((rows, 2 * width), BF),
        ],
        (first, in_0, local_tables),
    )
    gain_attn, gain_mlp = extra[:1], extra[1:2]
    all_ids = extra[2 : 2 + micro_count * runs].reshape(micro_count, runs, count, shard)
    all_ids = lax.dynamic_slice_in_dim(all_ids, replica - group_pos, GROUP, 2)
    all_ids = all_ids.swapaxes(1, 2).reshape(micro_count, GROUP, runs * shard)[..., :row_count]
    segments = all_ids.reshape(micro_count, GROUP * row_count).astype(jnp.int32)

    key_pos = positions[0] - row_count + jnp.arange(3 * row_count)
    around = jnp.pad(segments, ((0, 0), (row_count, row_count)), constant_values=-1)
    key_seg = lax.dynamic_slice_in_dim(around, group_pos * row_count, 3 * row_count, 1)
    visible = (key_seg[:, :, None] == segment_ids[:, None, :]) & (
        jnp.abs(positions[None, :] - key_pos[:, None]) <= HALF_WIN
    )[None]
    bias = jnp.tile(jnp.where(visible, 0.0, masked_score), (1, 1, 2))

    own_seg = lax.dynamic_index_in_dim(segments, group_pos // 8, 0, keepdims=False)
    halves = own_seg.reshape(GROUP, 2, row_count // 2)
    mine = lax.dynamic_index_in_dim(halves, group_pos % 2, 1, keepdims=False).reshape(-1)
    theirs = lax.dynamic_index_in_dim(halves, 1 - group_pos % 2, 1, keepdims=False).reshape(-1)
    shared_seg = jnp.concatenate([mine, theirs])[:, None]
    own_seg = own_seg[:, None]

    up_pairs, down_pairs = neighbours(count, 1), neighbours(count, -1)
    around_0 = (
        lax.ppermute(kv_0, "dp", up_pairs),
        kv_0,
        lax.ppermute(kv_0, "dp", down_pairs),
    )
    att_0, total_0 = on_core(
        local_forward_body,
        [((rows, width), BF), ((pairs, 1, LANES), F32)],
        (q_0, *around_0, bias),
    )
    n2_0, mixed_0, middle_0, gate_up_0, *out_0 = on_core(
        local_middle_body,
        [
            ((rows, width), BF),
            ((rows, hidden), BF),
            ((rows, width), F32),
            ((rows, inner), F32),
        ]
        + [((row_count, width), BF)] * micro_count,
        (*others, in_0, att_0, gain_mlp),
        [pltpu.VMEM((hidden, width), BF)],
    )

    in_1 = to_other_section(out_0, 1)
    fold = row_count * 3 // 4
    half = row_count // 2
    normed_1, sent = on_core(
        global_project_body,
        [((rows, width), BF), ((GROUP, 3 * fold, LANES), BF)],
        (first, *in_1, gain_attn, global_tables),
    )
    got = exchange(sent, count)
    beside = jnp.concatenate(
        [got[:, row_count : row_count + half], got[:, 3 * fold - half :]], 1
    )
    beside = partner(beside, 1, count)
    keys = GROUP * row_count
    tiles = keys * 3 // 2 // TILE
    head_scratch = [
        pltpu.VMEM((keys * 3 // 2, LANES), BF),
        pltpu.VMEM((2, keys, LANES), BF),
        pltpu.VMEM((2, keys, LANES), BF),
        pltpu.VMEM((2, LANES, keys), BF),
    ]
    folded, total_1 = on_core(
        global_forward_body,
        [((GROUP, fold, LANES), BF), ((tiles, 1, TILE), F32)],
        (got, beside, own_seg, shared_seg),
        head_scratch + [pltpu.VMEM((keys * 3 // 2, LANES), F32)],
    )
    folded = exchange(folded, count)

    up_1 = out_grad.reshape(rows, width)
    out_1, att_1, n2_1, mixed_1, right_1, gain_mlp_1, d_mid_1, sent = on_core(
        global_middle_body,
        [
            ((rows, width), BF),
            ((rows, width), BF),
            ((rows, width), BF),
            ((rows, hidden), BF),
            ((rows, inner + width), BF),
            ((1, width), F32),
            ((rows, width), F32),
            ((GROUP, fold, LANES), BF),
        ],
        (*others, folded, *in_1, up_1, gain_mlp),
        [pltpu.VMEM((hidden, width), BF)],
    )
    d_folded = exchange(sent, count)
    pairs = ((normed_0, normed_1), (att_0, att_1), (n2_0, n2_1), (mixed_0, mixed_1))
    left_total = 3 * shard_total + hidden_total
    if count == GROUP:
        (left,) = on_core(
            left_body,
            [((4, 4, left_total, rows), BF)],
            (lower_flag, group_pos[None], *(item for pair in pairs for item in pair)),
            (),
            [pltpu.SMEM] * 2 + [pltpu.VMEM] * 8,
        )
        left, d_folded = lax.optimization_barrier((left, d_folded))
    else:
        left = [
            plane_rows(jnp.where(lower, a, b).T.reshape(count, -1, rows), group_pos, count)
            for a, b in pairs
        ]
        left = [jnp.concatenate([i.reshape(4, -1, rows) for i in items], 1) for items in zip(*left)]
    sent, to_beside = on_core(
        global_backward_body,
        [((GROUP, 3 * fold, LANES), BF), ((GROUP, 2 * half, LANES), BF)],
        (got, beside, own_seg, shared_seg, total_1, d_folded),
        head_scratch
        + [
            pltpu.VMEM((keys * 3 // 2, LANES), BF),
            pltpu.VMEM((keys * 3 // 2, LANES), F32),
            pltpu.VMEM((2, keys, LANES), F32),
            pltpu.VMEM((2, keys, LANES), F32),
        ],
    )
    back = partner(to_beside, 1, count)
    gap = 3 * fold - half - row_count - half
    back = jnp.concatenate(
        [
            jnp.zeros((GROUP, row_count, LANES), BF),
            back[:, :half],
            jnp.zeros((GROUP, gap, LANES), BF),
            back[:, half:],
        ],
        1,
    )
    sent = (sent.astype(F32) + back.astype(F32)).astype(BF)
    if count == GROUP:
        left, sent = lax.optimization_barrier((left, sent))
        left = [left[0]] + [partner(left[apart], apart, count) for apart in range(1, 4)]
    got = exchange(sent, count)
    left, got = lax.optimization_barrier((left, got))

    d_proj_1, gain_attn_1, *grad_1 = on_core(
        global_finish_body,
        [((rows, 3 * width), BF), ((1, width), F32)] + [((row_count, width), BF)] * micro_count,
        (first, got, d_mid_1, *in_1, gain_attn, global_tables),
    )

    up_0 = to_other_section(grad_1, -1)
    d_mlp = jnp.concatenate(
        [jnp.where(lower, a, up_1[i * row_count :][:row_count]) for i, a in enumerate(up_0)]
    )
    across_mlp = partner(d_mlp, 2, count)
    gain_mlp_0, d_mid_0, d_att_0, right, *right_chunks = on_core(
        local_back_middle_body,
        [
            ((1, width), F32),
            ((rows, width), F32),
            ((rows, width), BF),
            ((rows, inner + width), BF),
        ]
        + [((row_count, inner + width), BF)] * micro_count,
        (*others, lower_flag, *up_0, middle_0, gate_up_0, gain_mlp, right_1),
        [pltpu.VMEM((hidden, width), BF)],
        [pltpu.VMEM] * len(others) + [pltpu.SMEM] + [pltpu.VMEM] * 6,
    )
    d_att_0, right_chunks, across_mlp = lax.optimization_barrier(
        (d_att_0, right_chunks, across_mlp)
    )
    across = [partner(item, 2, count) for item in right_chunks]
    d_mlp = with_core(d_mlp, [across_mlp], count)
    out_near, out_far = first_hop(
        on_core(
            functools.partial(early_body, [(0, (3 * shard_total, left_total), (0, width))], 3),
            three_parts((hidden_total, width)),
            (*d_mlp, *left),
        ),
        count,
    )
    dq_0, d_own, d_before, d_after = on_core(
        local_backward_body,
        [
            ((rows, width), BF),
            ((rows, 2 * width), F32),
            ((rows, 2 * width), BF),
            ((rows, 2 * width), BF),
        ],
        (q_0, *around_0, bias, total_0, d_att_0, local_tables),
    )
    from_after = lax.ppermute(d_before, "dp", down_pairs)
    from_before = lax.ppermute(d_after, "dp", up_pairs)
    across, right, _ = lax.optimization_barrier((across, right, d_own))
    right = with_core(right, across, count)
    in_rows, attn_rows = shard_total * (inner // width), shard_total
    early_rows = in_rows + attn_rows
    terms = [
        (0, (2 * shard_total, 3 * shard_total), (0, inner)),
        (0, (shard_total, 2 * shard_total), (inner, inner + width)),
    ]
    early = on_core(
        functools.partial(early_body, terms, len(right)),
        three_parts((early_rows, width)),
        (*right, *left),
    )
    from_after, _ = lax.optimization_barrier((from_after, early[0]))
    near, far = first_hop(early, count)
    d_proj, grad_0, gain_attn_sum = on_core(
        local_finish_body,
        [
            ((rows + EXTRA, 3 * width), BF),
            ((rows, width), BF),
            ((1, width), F32),
        ],
        (
            lower_flag, first, dq_0, d_own, from_after, from_before, local_tables, d_mid_0, in_0, gain_attn,
            gain_mlp_0, d_proj_1, gain_attn_1, gain_mlp_1,
        ),
        [pltpu.VMEM((1, width), F32)],
        [pltpu.SMEM] + [pltpu.VMEM] * 13,
    )
    across_chunks = [partner(d_proj, 2, count)]
    far = jnp.concatenate([far, out_far])
    across_chunks, d_proj, _ = lax.optimization_barrier((across_chunks, d_proj, far))
    far = partner(far, 8, count)
    right = with_core(d_proj, across_chunks, count)
    late_in = (group_pos[None], *right, *left)
    late = on_core(
        functools.partial(late_body, (0, shard_total)),
        three_parts((shard_total, 3 * width + LANES)),
        late_in,
        [pltpu.VMEM((width, LANES), F32)],
        [pltpu.SMEM] + [pltpu.VMEM] * (len(late_in) - 1),
    )
    far, _ = lax.optimization_barrier((far, late[0]))
    early = near + far[:early_rows].astype(F32)
    mlp_out_share = out_near + far[early_rows:].astype(F32)
    late = second_hop(*first_hop(late, count), count)
    parts = [early[p * shard_total : (p + 1) * shard_total] for p in range(inner // width)]
    in_share = jnp.concatenate(parts, 1)
    attn_share = early[in_rows : in_rows + attn_rows]
    gain_columns = late[:, 3 * width :]
    qkv_share, in_share, mlp_out_share, attn_share, gain_columns = (
        over_groups(item, count)
        for item in (late[:, : 3 * width], in_share, mlp_out_share, attn_share, gain_columns)
    )
    if count == GROUP:
        gains = jnp.stack([gain_columns[:, 0], gain_columns[:, 2]])
    else:
        gain_mlp_sum = jnp.where(lower, gain_mlp_0, gain_mlp_1)
        gains = lax.psum(jnp.concatenate([gain_attn_sum, gain_mlp_sum]), "dp")
        gains = lax.dynamic_slice_in_dim(gains, replica * shard, shard, 1)

    return (
        jnp.where(lower, jnp.concatenate(out_0), out_1).reshape(1, micro_count, row_count, width),
        jnp.where(lower, grad_0, jnp.concatenate(grad_1)).reshape(1, micro_count, row_count, width),
        qkv_share[None],
        attn_share[None],
        in_share[None],
        mlp_out_share[None],
        gains[:1],
        gains[1:],
    )


def solution(mesh):
    in_specs = (
        P(None, "dp", None),
        P(None, "dp"),
        P(None, "dp", None),
        P("section", "dp", None),
        P("section", "dp", None),
        P("section", "dp", None),
        P("section", "dp", None),
        P("section", "dp"),
        P("section", "dp"),
    )
    out_specs = (
        P("section", None, "dp", None),
        P("section", None, "dp", None),
        P("section", "dp", None),
        P("section", "dp", None),
        P("section", "dp", None),
        P("section", "dp", None),
        P("section", "dp"),
        P("section", "dp"),
    )
    return jax.shard_map(
        on_device, mesh=mesh, in_specs=in_specs, out_specs=out_specs, check_vma=False
    )
```

```python
import functools
import math

import jax
import jax.numpy as jnp
from jax import lax
from jax.experimental import pallas as pl
from jax.experimental.pallas import tpu as pltpu
from jax.sharding import PartitionSpec as P

HEAD_DIM = 64
GROUP = 16
HALF_WIN = 64
EXTRA = 16
LANES = 128
TILE = 256

local_log_base = math.log(10000.0)
global_log_base = math.log(160000.0)
masked_score = -1e30
SCALE = 1.0 / math.sqrt(HEAD_DIM)
BF = jnp.bfloat16
F32 = jnp.float32


def dot(left, right):
    return jnp.dot(left, right, preferred_element_type=F32)


def dot_bt(left, right):
    return lax.dot_general(left, right, (((1,), (1,)), ((), ())), preferred_element_type=F32)


def dot_at(left, right):
    return lax.dot_general(left, right, (((0,), (0,)), ((), ())), preferred_element_type=F32)


def moments(values):
    center = values - jnp.mean(values, -1, keepdims=True)
    scale = lax.rsqrt(jnp.mean(center * center, -1, keepdims=True) + 1e-05)
    return center * scale, scale


def norm_back(grad_out, gain_row, xhat, scale):
    scaled = grad_out * gain_row
    mean_grad = jnp.mean(scaled, -1, keepdims=True)
    mean_dot = jnp.mean(scaled * xhat, -1, keepdims=True)
    return (scaled - mean_grad - xhat * mean_dot) * scale


def angles(positions, log_base):
    half_dim = HEAD_DIM // 2
    fraction = (2 * jnp.arange(half_dim)).astype(F32) / HEAD_DIM
    inverse = jnp.exp(-fraction * log_base)
    table = positions.astype(F32)[:, None] * inverse[None, :]
    cosine, sine = jnp.cos(table), jnp.sin(table)
    none = jnp.zeros_like(sine)
    cosine = jnp.concatenate([cosine, cosine], 1)
    to_first = jnp.concatenate([-sine, none], 1)
    to_second = jnp.concatenate([none, sine], 1)
    return jnp.tile(jnp.stack([cosine, to_first, to_second]), (1, 2, 2))


def on_core(body, outs, args, scratch=(), spaces=None, out_spaces=None):
    return pl.pallas_call(
        body,
        out_shape=[jax.ShapeDtypeStruct(shape, dtype) for shape, dtype in outs],
        in_specs=[
            pl.BlockSpec(memory_space=space) for space in spaces or [pltpu.VMEM] * len(args)
        ],
        out_specs=[
            pl.BlockSpec(memory_space=space) for space in out_spaces or [pltpu.VMEM] * len(outs)
        ],
        scratch_shapes=scratch,
        cost_estimate=pl.CostEstimate(
            flops=2**10, bytes_accessed=2**10, transcendentals=0
        ),
        compiler_params=pltpu.CompilerParams(vmem_limit_bytes=48 * 2**20),
    )(*args)


def low_lanes():
    return lax.broadcasted_iota(jnp.int32, (1, LANES), 1) < HEAD_DIM


def swap(chunk):
    return pltpu.roll(chunk, HEAD_DIM, 1)


def chunks_of(rows):
    return [rows[:, c : c + LANES] for c in range(0, rows.shape[1], LANES)]


def rotate(chunk, tables):
    cosine, to_first, to_second = tables
    quarter = HEAD_DIM // 2
    return (
        chunk * cosine
        + pltpu.roll(chunk, LANES - quarter, 1) * to_first
        + pltpu.roll(chunk, quarter, 1) * to_second
    )


def unrotate(chunk, tables):
    cosine, to_first, to_second = tables
    quarter = HEAD_DIM // 2
    return (
        chunk * cosine
        - pltpu.roll(chunk, LANES - quarter, 1) * to_first
        - pltpu.roll(chunk, quarter, 1) * to_second
    )


def low_and_high(chunks):
    swapped = [swap(chunk) for chunk in chunks]
    low = [(swapped if h % 2 else chunks)[h // 2] for h in range(2 * len(chunks))]
    high = [(chunks if h % 2 else swapped)[h // 2] for h in range(2 * len(chunks))]
    return low, high


def targets():
    for d in range(GROUP):
        micro, chip, half = d // 8, d % 8 // 2, d % 2
        yield d, micro, 3 * chip + 2 * half, 3 * chip + 1, half


def pack_folded(chunks, ref, base):
    low, high = low_and_high(chunks)
    first = low_lanes()
    rows = chunks[0].shape[0] // 2
    half, fold = rows // 2, rows * 3 // 4
    for d, micro, own, shared, side in targets():
        start = micro * rows
        part = start + side * half
        upper = jnp.concatenate(
            [high[own][start + fold : start + rows], high[shared][part : part + half]], 0
        )
        ref[d, base : base + fold] = jnp.where(
            first, low[own][start : start + fold], upper
        ).astype(BF)


def pack_pairs(lefts, rights, ref):
    low, high = low_and_high(lefts)[0], low_and_high(rights)[1]
    first = low_lanes()
    rows = lefts[0].shape[0] // 2
    half = rows // 2
    for d, micro, own, shared, side in targets():
        start = micro * rows
        part = start + side * half
        ref[d, 0:rows] = jnp.where(
            first, low[own][start : start + rows], high[own][start : start + rows]
        ).astype(BF)
        ref[d, rows : rows + half] = jnp.where(
            first, low[shared][part : part + half], high[shared][part : part + half]
        ).astype(BF)


def unpack_folded(ref, base, rows):
    first = low_lanes()
    fold = rows * 3 // 4
    low, high = {}, {}
    shared_parts = {}
    for d, micro, own, shared, side in targets():
        block = ref[d, base : base + fold].astype(F32)
        mine = jnp.concatenate([block, swap(block[: rows - fold])], 0)
        if own % 2:
            high[micro, own] = swap(mine)
        else:
            low[micro, own] = mine
        shared_parts[micro, shared, side] = block[rows - fold :]
        if side:
            both = jnp.concatenate([shared_parts[micro, shared, 0], block[rows - fold :]], 0)
            if shared % 2:
                high[micro, shared] = both
            else:
                low[micro, shared] = swap(both)
    heads = GROUP // 4 * 3
    return [
        jnp.concatenate(
            [jnp.where(first, low[m, h], high[m, h + 1]) for m in range(2)], 0
        )
        for h in range(0, heads, 2)
    ]


def unpack_pairs(ref, rows):
    first = low_lanes()
    half = rows // 2
    pairs = {}
    parts = {}
    for d, micro, own, shared, side in targets():
        pairs[micro, own] = ref[d, 0:rows].astype(F32)
        parts[side] = ref[d, rows : rows + half].astype(F32)
        if side:
            pairs[micro, shared] = jnp.concatenate([parts[0], parts[1]], 0)
    heads = GROUP // 4 * 3
    lefts, rights = [], []
    for h in range(0, heads, 2):
        even, odd = [pairs[m, h] for m in range(2)], [pairs[m, h + 1] for m in range(2)]
        lefts.append(
            jnp.concatenate([jnp.where(first, a, swap(b)) for a, b in zip(even, odd)], 0)
        )
        rights.append(
            jnp.concatenate([jnp.where(first, swap(a), b) for a, b in zip(even, odd)], 0)
        )
    return lefts, rights


class Weights:
    def __init__(self, sources, mlp_out):
        self.sources = sources
        self.mlp_out = sources[-1]
        if len(sources) == 1:
            self.mlp_out = mlp_out
            unpack_rows(sources[0], mlp_out)

    def get(self, which):
        if which == 2:
            return self.mlp_out[...]
        if len(self.sources) > 1:
            return self.sources[which][...]
        (wide,) = self.sources
        width = wide.shape[0]
        inner = 2 * self.mlp_out.shape[0]
        return wide[:, width : width + inner] if which else wide[:, :width]


def first_block(pair):
    return -(-pair // 32) * 16


def packed_pieces(shard, rows, width):
    yield 0, shard, 0, width, 0, 0
    rest = rows - shard
    side = width // 3
    yield 0, rest, width, 2 * side, shard, 0
    yield rest, 16, width, side, shard, 2 * side
    yield rest, 16, width + side, side, shard + 16, 2 * side


def unpack_rows(wide, mlp_out):
    hidden, width = mlp_out.shape
    shard = wide.shape[0] // GROUP
    start = wide.shape[1] - width - 2 * (width // 3)
    pair = 2 * hidden // GROUP
    upper = first_block(pair)
    for d in range(GROUP):
        low = d // 2 * pair + d % 2 * upper
        have = pair - upper if d % 2 else upper
        for row, rows, column, columns, to_row, to_column in packed_pieces(shard, upper, width):
            rows = min(rows, have - to_row)
            if rows > 0:
                mlp_out[low + to_row : low + to_row + rows, to_column : to_column + columns] = wide[
                    d * shard + row : d * shard + row + rows, start + column : start + column + columns
                ]


def stack_body(odd_ref, attn_ref, mlp_in_ref, own_ref, beside_ref, out_ref):
    shard, width = attn_ref.shape
    inner = mlp_in_ref.shape[1]
    out_ref[:, :width] = attn_ref[...]
    out_ref[:, width : width + inner] = mlp_in_ref[...]
    own, beside = own_ref[...].astype(F32), beside_ref[...].astype(F32)
    moved = beside.shape[0]
    even = jnp.concatenate([own, beside], 0)
    odd = jnp.concatenate([own[moved:], beside, beside], 0)
    block = jnp.where(odd_ref[0] == 1, odd, even).astype(BF)
    start = width + inner
    for row, rows, column, columns, from_row, from_column in packed_pieces(
        shard, block.shape[0], width
    ):
        out_ref[row : row + rows, start + column : start + column + columns] = block[
            from_row : from_row + rows, from_column : from_column + columns
        ]


def mlp_forward(layer_in, attended, gain, weights):
    middle = layer_in + dot(attended, weights.get(0))
    xhat, _ = moments(middle)
    normed = (xhat * gain).astype(BF)
    gate_up = dot(normed, weights.get(1))
    half = gate_up.shape[1] // 2
    gate, up = gate_up[:, :half], gate_up[:, half:]
    cdf = 0.5 * (1.0 + lax.erf(gate * math.sqrt(0.5)))
    mixed = (gate * cdf * up).astype(BF)
    result = (middle + dot(mixed, weights.get(2))).astype(BF)
    return middle, normed, gate, up, mixed, result


def mlp_backward(upstream, middle, gate, up, gain, weights):
    d_mixed = dot_bt(upstream, weights.get(2))
    cdf = 0.5 * (1.0 + lax.erf(gate * math.sqrt(0.5)))
    density = jnp.exp(-0.5 * gate * gate) * (1.0 / math.sqrt(2.0 * math.pi))
    d_gate = d_mixed * up * (cdf + gate * density)
    d_up = d_mixed * gate * cdf
    d_gate_up = jnp.concatenate([d_gate.astype(BF), d_up.astype(BF)], 1)
    d_normed = dot_bt(d_gate_up, weights.get(1))
    xhat, scale = moments(middle)
    gain_grad = jnp.sum(d_normed * xhat, 0, keepdims=True)
    d_middle = upstream.astype(F32) + norm_back(d_normed, gain, xhat, scale)
    d_attn = d_middle.astype(BF)
    d_attended = dot_bt(d_attn, weights.get(0))
    return d_gate_up, gain_grad, d_middle, d_attn, d_attended


def project(xhat, gain, first_ref, table_ref, normed_ref):
    width = xhat.shape[1]
    normed = (xhat * gain).astype(BF)
    normed_ref[...] = normed
    tables = [table_ref[i] for i in range(3)]
    results = [dot(normed, first_ref[:, c * width : (c + 1) * width]) for c in range(3)]
    queries, keys, values = chunks_of(results[0]), chunks_of(results[1]), results[2]
    return [rotate(c, tables) for c in queries], [rotate(c, tables) for c in keys], values


def input_backward(d_middle, d_projected, x, gain_ref, first_ref, gain_out_ref):
    d_normed = dot_bt(d_projected, first_ref[:, : d_projected.shape[1]])
    xhat, scale = moments(x)
    gain_out_ref[...] = jnp.sum(d_normed * xhat, 0, keepdims=True)
    return (d_middle + norm_back(d_normed, gain_ref[...], xhat, scale)).astype(BF)


def joined(refs):
    return jnp.concatenate([ref[...] for ref in refs], 0)


def store_chunks(refs, rows):
    size = rows.shape[0] // len(refs)
    for i, ref in enumerate(refs):
        ref[...] = rows[i * size : (i + 1) * size]


def message_body(w_ref, attn_ref, mlp_ref, ids_ref, out_ref, rows_scr, ids_scr):
    shard, columns = w_ref.shape
    micro_count, row_count = ids_ref.shape
    out_ref[:, :columns] = w_ref[...]
    rows_scr[...] = jnp.zeros_like(rows_scr)
    ids_scr[...] = jnp.zeros_like(ids_scr)
    rows_scr[0:1, :shard] = attn_ref[...].astype(F32)
    rows_scr[1:2, :shard] = mlp_ref[...].astype(F32)
    ids_scr[:micro_count, :row_count] = ids_ref[...].astype(F32)
    runs = -(-row_count // shard)
    for run in range(runs):
        turned = ids_scr[...]
        if run:
            turned = pltpu.roll(turned, LANES - run * shard, 1)
        for micro in range(micro_count):
            row = 2 + micro * runs + run
            rows_scr[row : row + 1] = turned[micro : micro + 1]
    out_ref[:, columns:] = rows_scr[...].T[:shard].astype(BF)


def local_project_body(first_ref, x_ref, table_ref, extra_ref, normed_ref, q_ref, kv_ref):
    xhat, _ = moments(x_ref[...].astype(F32))
    extra = first_ref[:, first_ref.shape[1] - LANES :].astype(F32).T
    extra_ref[...] = extra[: extra_ref.shape[0]]
    queries, keys, values = project(xhat, extra[:1], first_ref, table_ref, normed_ref)
    width = values.shape[1]
    for j, (q, k) in enumerate(zip(queries, keys)):
        q_ref[:, LANES * j : LANES * (j + 1)] = q.astype(BF)
        kv_ref[:, LANES * j : LANES * (j + 1)] = k.astype(BF)
    kv_ref[:, width:] = values.astype(BF)


def two_heads(chunk):
    first = low_lanes()
    wide = chunk.astype(F32)
    return jnp.concatenate([jnp.where(first, wide, 0.0), jnp.where(first, 0.0, wide)], 0)


def pick_heads(rows):
    half = rows.shape[0] // 2
    return jnp.where(low_lanes(), rows[:half], rows[half:])


def local_parts(q_ref, before_ref, own_ref, after_ref):
    rows = q_ref.shape[0] // 2
    width = q_ref.shape[1]
    for micro in range(2):
        for j in range(width // LANES):
            here = slice(micro * rows, (micro + 1) * rows)
            lanes = slice(LANES * j, LANES * (j + 1))
            more = slice(width + LANES * j, width + LANES * (j + 1))
            keys, values = (
                jnp.concatenate([ref[here, part] for ref in (before_ref, own_ref, after_ref)], 0)
                for part in (lanes, more)
            )
            queries = (two_heads(q_ref[here, lanes]) * SCALE).astype(BF)
            yield micro * (width // LANES) + j, micro, here, lanes, more, queries, keys, values


def local_forward_body(q_ref, before_ref, own_ref, after_ref, bias_ref, att_ref, total_ref):
    parts = local_parts(q_ref, before_ref, own_ref, after_ref)
    for index, micro, here, lanes, _, queries, keys, values in parts:
        scores = dot_bt(keys, queries) + bias_ref[micro]
        peak = jnp.max(scores, 0, keepdims=True)
        weights = jnp.exp(scores - peak)
        total = jnp.sum(weights, 0, keepdims=True)
        total_ref[index] = peak + jnp.log(total)
        probs = (weights * (1.0 / total)).astype(BF)
        att_ref[here, lanes] = pick_heads(dot_at(probs, values)).astype(BF)


def local_backward_body(
    q_ref, before_ref, own_ref, after_ref, bias_ref, total_ref, d_ref, table_ref,
    dq_ref, d_own_ref, d_before_ref, d_after_ref,
):
    tables = [table_ref[i] for i in range(3)]
    parts = local_parts(q_ref, before_ref, own_ref, after_ref)
    rows = q_ref.shape[0] // 2
    for index, micro, here, lanes, more, queries, keys, values in parts:
        d_out = two_heads(d_ref[here, lanes]).astype(BF)
        probs = jnp.exp(dot_bt(keys, queries) + bias_ref[micro] - total_ref[index])
        d_probs = dot_bt(values, d_out)
        product = probs * d_probs
        delta = jnp.sum(product, 0, keepdims=True)
        d_scores = (product - probs * delta).astype(BF)
        d_queries = pick_heads(dot_at(d_scores, keys)) * SCALE
        local_tables = [table[here] for table in tables]
        dq_ref[here, lanes] = unrotate(d_queries, local_tables).astype(BF)
        for part, grads in ((lanes, dot(d_scores, queries)), (more, dot(probs.astype(BF), d_out))):
            d_before_ref[here, part] = grads[:rows].astype(BF)
            d_own_ref[here, part] = grads[rows : 2 * rows]
            d_after_ref[here, part] = grads[2 * rows :].astype(BF)


def local_finish_body(
    lower_ref, first_ref, dq_ref, own_ref, low_ref, high_ref, table_ref, d_middle_ref, x_ref, gain_ref,
    gain_mlp_ref, other_ref, other_attn_ref, other_mlp_ref, out_ref, grad_ref, gain_attn_ref,
    gain_scr,
):
    rows, width = dq_ref.shape

    @pl.when(lower_ref[0] == 1)
    def _():
        tables = [table_ref[i] for i in range(3)]
        total = own_ref[...] + low_ref[...].astype(F32) + high_ref[...].astype(F32)
        out_ref[:rows, :width] = dq_ref[...]
        for j, chunk in enumerate(chunks_of(total[:, :width])):
            start = width + LANES * j
            out_ref[:rows, start : start + LANES] = unrotate(chunk, tables).astype(BF)
        out_ref[:rows, 2 * width :] = total[:, width:].astype(BF)
        grad_ref[...] = input_backward(
            d_middle_ref[...], out_ref[:rows], x_ref[...].astype(F32), gain_ref, first_ref, gain_scr
        )

    @pl.when(lower_ref[0] == 0)
    def _():
        out_ref[:rows] = other_ref[...]
        grad_ref[...] = jnp.zeros_like(grad_ref)
        gain_scr[...] = other_attn_ref[...]

    gain_attn_ref[...] = gain_scr[...]
    gain_mlp = jnp.where(lower_ref[0] == 1, gain_mlp_ref[...], other_mlp_ref[...])
    index = lax.broadcasted_iota(jnp.int32, (EXTRA, width), 0)
    tail = jnp.zeros((EXTRA, width), F32)
    for row, gain in ((0, gain_scr[...]), (2, gain_mlp)):
        high = gain.astype(BF).astype(F32)
        tail = jnp.where(index == row, high, tail)
        tail = jnp.where(index == row + 1, gain - high, tail)
    out_ref[rows:] = jnp.zeros((EXTRA, out_ref.shape[1]), BF)
    out_ref[rows:, :width] = tail.astype(BF)


def local_middle_body(*refs):
    sources, refs = refs[:-10], refs[-10:]
    x_ref, att_ref, gain_ref, normed_ref, mixed_ref, middle_ref, gate_up_ref = refs[:7]
    weights = Weights(sources, refs[9])
    middle, normed, gate, up, mixed, result = mlp_forward(
        x_ref[...].astype(F32), att_ref[...], gain_ref[...], weights
    )
    store_chunks(refs[7:9], result)
    normed_ref[...] = normed
    mixed_ref[...] = mixed
    middle_ref[...] = middle
    half = gate.shape[1]
    gate_up_ref[:, :half] = gate
    gate_up_ref[:, half:] = up


def local_back_middle_body(*refs):
    sources, refs = refs[:-14], refs[-14:]
    lower_ref, low_ref, high_ref, middle_ref, gate_up_ref, gain_ref, other_ref = refs[:7]
    gain_out_ref, d_middle_ref, d_att_ref, right_ref, right_low_ref, right_high_ref = refs[7:13]
    weights = Weights(sources, refs[13])
    half = gate_up_ref.shape[1] // 2
    upstream = joined([low_ref, high_ref])
    d_gate_up, gain_grad, d_middle, d_attn, d_attended = mlp_backward(
        upstream, middle_ref[...], gate_up_ref[:, :half], gate_up_ref[:, half:],
        gain_ref[...], weights,
    )
    gain_out_ref[...] = gain_grad
    d_middle_ref[...] = d_middle
    d_att_ref[...] = d_attended.astype(BF)

    @pl.when(lower_ref[0] == 1)
    def _():
        right_ref[:, : 2 * half] = d_gate_up
        right_ref[:, 2 * half :] = d_attn

    @pl.when(lower_ref[0] == 0)
    def _():
        right_ref[...] = other_ref[...]

    store_chunks((right_low_ref, right_high_ref), right_ref[...])


def global_project_body(first_ref, low_ref, high_ref, gain_ref, table_ref, normed_ref, sent_ref):
    xhat, _ = moments(joined([low_ref, high_ref]).astype(F32))
    queries, keys, values = project(xhat, gain_ref[...], first_ref, table_ref, normed_ref)
    pack_pairs(queries, keys, sent_ref)
    pack_folded(chunks_of(values), sent_ref, sent_ref.shape[1] * 2 // 3)


def flat(blocks):
    return blocks.reshape(-1, LANES)


def own_unfolded(ref, base, rows):
    fold = rows * 3 // 4
    block = ref[:, base : base + fold].astype(F32)
    rest = swap(flat(block[:, : rows - fold])).reshape(GROUP, rows - fold, LANES)
    return flat(jnp.concatenate([block, rest], 1))


def shared_unfolded(ref, start, rows):
    return swap(flat(ref[:, start : start + rows // 2].astype(F32)))


def fill_heads(got_ref, other_ref, own_seg_ref, shared_seg_ref, q_scr, k_scr, v_scr):
    rows = got_ref.shape[1] * 4 // 9
    half = rows // 2
    first = low_lanes()
    lane = lax.broadcasted_iota(jnp.int32, (1, LANES), 1) - HEAD_DIM
    own = flat(got_ref[:, 0:rows].astype(F32))
    shared = flat(got_ref[:, rows : rows + half].astype(F32))
    other = flat(other_ref[:, 0:half].astype(F32))
    count = own.shape[0]
    own_hit = lane == own_seg_ref[...]
    shared_hit = lane == shared_seg_ref[...]
    both = jnp.concatenate([shared, other], 0)
    for start, pairs, hit in (
        (0, own, own_hit),
        (count, shared, shared_hit[: count // 2]),
    ):
        marked = jnp.where(hit, 1.0, 0.0)
        q_scr[start : start + pairs.shape[0]] = jnp.where(first, pairs * SCALE, marked).astype(BF)
    for unit, pairs, hit in ((0, own, own_hit), (1, both, shared_hit)):
        marked = jnp.where(hit, 0.0, masked_score)
        k_scr[unit] = jnp.where(first, swap(pairs), marked).astype(BF)
    base = rows + half
    v_scr[0] = jnp.where(first, own_unfolded(got_ref, base, rows), 0.0).astype(BF)
    start = base + rows - rows * 3 // 4
    shared_v = jnp.concatenate(
        [shared_unfolded(got_ref, start, rows), shared_unfolded(other_ref, half, rows)], 0
    )
    v_scr[1] = jnp.where(first, shared_v, 0.0).astype(BF)


def fold_out(own, shared, rows, ref, base):
    fold = rows * 3 // 4
    blocks = own.reshape(GROUP, rows, LANES)
    swapped = swap(own).reshape(GROUP, rows, LANES)
    upper = jnp.concatenate(
        [swapped[:, fold:], swap(shared).reshape(GROUP, rows // 2, LANES)], 1
    )
    ref[:, base : base + fold] = jnp.where(low_lanes(), blocks[:, :fold], upper).astype(BF)


def global_forward_body(
    got_ref, other_ref, own_seg_ref, shared_seg_ref, out_ref, total_ref,
    q_scr, k_scr, v_scr, vt_scr, o_scr,
):
    fill_heads(got_ref, other_ref, own_seg_ref, shared_seg_ref, q_scr, k_scr, v_scr)
    for unit in range(2):
        vt_scr[unit] = v_scr[unit].astype(F32).T.astype(BF)
    count = k_scr.shape[1]

    def step(tile, carry):
        unit = tile // (count // TILE)
        rows = pl.ds(pl.multiple_of(tile * TILE, TILE), TILE)
        scores = dot_bt(k_scr[unit], q_scr[rows])
        peak = jnp.max(scores, 0, keepdims=True)
        weights = jnp.exp(scores - peak)
        total = jnp.sum(weights, 0, keepdims=True)
        total_ref[tile] = peak + jnp.log(total)
        out = dot(vt_scr[unit], weights.astype(BF)) * (1.0 / total)
        o_scr[rows] = out.T
        return carry

    lax.fori_loop(0, q_scr.shape[0] // TILE, step, 0)
    rows = got_ref.shape[1] * 4 // 9
    fold_out(o_scr[:count], o_scr[count:], rows, out_ref, 0)


def global_backward_body(
    got_ref, other_ref, own_seg_ref, shared_seg_ref, total_ref, d_ref, sent_ref, to_other_ref,
    q_scr, k_scr, v_scr, kt_scr, d_scr, dq_scr, dk_scr, dv_scr,
):
    fill_heads(got_ref, other_ref, own_seg_ref, shared_seg_ref, q_scr, k_scr, v_scr)
    first = low_lanes()
    rows = got_ref.shape[1] * 4 // 9
    half = rows // 2
    for unit in range(2):
        keys = jnp.where(first, k_scr[unit].astype(F32), 0.0)
        kt_scr[unit] = keys.T.astype(BF)
    count = k_scr.shape[1]
    d_scr[:count] = jnp.where(first, own_unfolded(d_ref, 0, rows), 0.0).astype(BF)
    d_scr[count:] = jnp.where(
        first, shared_unfolded(d_ref, rows - rows * 3 // 4, rows), 0.0
    ).astype(BF)
    dk_scr[...] = jnp.zeros_like(dk_scr)
    dv_scr[...] = jnp.zeros_like(dv_scr)

    def step(tile, carry):
        unit = tile // (count // TILE)
        here = pl.ds(pl.multiple_of(tile * TILE, TILE), TILE)
        queries, d_out = q_scr[here], d_scr[here]
        probs = jnp.exp(dot_bt(k_scr[unit], queries) - total_ref[tile])
        d_probs = dot_bt(v_scr[unit], d_out)
        product = probs * d_probs
        delta = jnp.sum(product, 0, keepdims=True)
        d_scores = (product - probs * delta).astype(BF)
        dv_scr[unit] += dot(probs.astype(BF), d_out)
        dk_scr[unit] += dot(d_scores, queries)
        dq_scr[here] = dot(kt_scr[unit], d_scores).T * SCALE
        return carry

    lax.fori_loop(0, q_scr.shape[0] // TILE, step, 0)
    mine = count // 2
    own = jnp.where(first, dq_scr[:count], swap(dk_scr[0]))
    sent_ref[:, 0:rows] = own.reshape(GROUP, rows, LANES).astype(BF)
    shared_k, shared_v = dk_scr[1], dv_scr[1]
    shared = jnp.where(first, dq_scr[count:], swap(shared_k[:mine]))
    sent_ref[:, rows : rows + half] = shared.reshape(GROUP, half, LANES).astype(BF)
    fold_out(dv_scr[0], shared_v[:mine], rows, sent_ref, rows + half)
    for place, grads in enumerate((shared_k, shared_v)):
        other = jnp.where(first, 0.0, swap(grads[mine:])).reshape(GROUP, half, LANES)
        to_other_ref[:, place * half : (place + 1) * half] = other.astype(BF)


def global_middle_body(*refs):
    sources, refs = refs[:-14], refs[-14:]
    got_ref, low_ref, high_ref, up_ref, gain_ref, out_ref, att_ref, normed_ref, mixed_ref = refs[:9]
    right_ref, gain_out_ref, d_middle_ref, sent_ref = refs[9:13]
    weights = Weights(sources, refs[13])
    rows = low_ref.shape[0]
    attended = jnp.concatenate([c.astype(BF) for c in unpack_folded(got_ref, 0, rows)], 1)
    att_ref[...] = attended
    gain = gain_ref[...]
    middle, normed, gate, up, mixed, result = mlp_forward(
        joined([low_ref, high_ref]).astype(F32), attended, gain, weights
    )
    out_ref[...] = result
    normed_ref[...] = normed
    mixed_ref[...] = mixed
    d_gate_up, gain_grad, d_middle, d_attn, d_attended = mlp_backward(
        up_ref[...], middle, gate, up, gain, weights
    )
    right_ref[:, : d_gate_up.shape[1]] = d_gate_up
    right_ref[:, d_gate_up.shape[1] :] = d_attn
    gain_out_ref[...] = gain_grad
    d_middle_ref[...] = d_middle
    pack_folded(chunks_of(d_attended), sent_ref, 0)


def global_finish_body(
    first_ref, got_ref, d_middle_ref, low_ref, high_ref, gain_ref, table_ref,
    d_proj_ref, gain_out_ref, *grad_refs,
):
    tables = [table_ref[i] for i in range(3)]
    x = joined([low_ref, high_ref]).astype(F32)
    rows = low_ref.shape[0]
    d_queries, d_keys = unpack_pairs(got_ref, rows)
    d_values = unpack_folded(got_ref, rows * 3 // 2, rows)
    parts = [unrotate(c, tables).astype(BF) for c in d_queries + d_keys]
    d_projected = jnp.concatenate(parts + [c.astype(BF) for c in d_values], 1)
    d_proj_ref[...] = d_projected
    store_chunks(
        grad_refs,
        input_backward(d_middle_ref[...], d_projected, x, gain_ref, first_ref, gain_out_ref),
    )


def neighbours(count, step):
    return [
        (i, i + step)
        for i in range(count)
        if 0 <= i + step < count and i // GROUP == (i + step) // GROUP
    ]


def exchange(blocks, count):
    groups = [list(range(s, s + GROUP)) for s in range(0, count, GROUP)]
    return lax.all_to_all(blocks, "dp", 0, 0, axis_index_groups=groups)


def to_other_section(chunks, step):
    pairs = [(0, 1)] if step > 0 else [(1, 0)]
    return [lax.ppermute(rows, "section", pairs) for rows in chunks]


def partner(rows, apart, count):
    return lax.ppermute(rows, "dp", [(i, i ^ apart) for i in range(count)])


def gather_rows(piece, group_pos, count):
    pieces = {0: piece}
    for apart in (4, 8, 12):
        pieces[apart] = partner(piece, apart, count)
    for apart in (0, 4, 8, 12):
        pieces[apart + 2] = partner(pieces[apart], 2, count)
    for apart in range(0, GROUP, 2):
        pieces[apart + 1] = partner(pieces[apart], 1, count)
    whole = jnp.zeros((GROUP,) + piece.shape, piece.dtype)
    for apart, item in pieces.items():
        start = (group_pos ^ apart,) + (0,) * piece.ndim
        whole = lax.dynamic_update_slice(whole, item[None], start)
    if count > GROUP:
        groups = [list(range(s, count, GROUP)) for s in range(GROUP)]
        whole = lax.all_gather(whole, "dp", axis=0, tiled=True, axis_index_groups=groups)
    return whole.reshape(-1, piece.shape[-1]), pieces[2]


def plane_rows(rows, group_pos, count):
    parts = rows.reshape(count // GROUP, 4, 4, *rows.shape[1:])
    place, plane = group_pos % 4, group_pos // 4
    taken = []
    for apart in range(4):
        block = lax.dynamic_index_in_dim(parts, place ^ apart, 2, keepdims=False)
        block = jnp.stack(
            [lax.dynamic_index_in_dim(block, plane ^ z, 1, keepdims=False) for z in range(4)]
        )
        taken.append(partner(block, apart, count) if apart else block)
    return taken


def left_body(lower_ref, place_ref, *refs):
    refs, out_ref = refs[:-1], refs[-1]
    base = 0
    for first_ref, second_ref in zip(refs[0::2], refs[1::2]):
        rows = jnp.where(lower_ref[0] == 1, first_ref[...].astype(F32), second_ref[...].astype(F32))
        turned = rows.T
        size = turned.shape[0] // GROUP
        for d in range(GROUP):
            side = d % 4 ^ place_ref[0] % 4
            plane = d // 4 ^ place_ref[0] // 4
            out_ref[side, plane, base : base + size] = turned[d * size : (d + 1) * size].astype(BF)
        base += size


def left_rows_of(refs, rows):
    start, end = rows
    parts = [
        jnp.concatenate([ref[p, start:end].astype(F32) for p in range(4)], 0).astype(BF) for ref in refs
    ]
    return jnp.concatenate(parts, 1)


def by_plane(result, base, outs, columns=slice(None)):
    rows = result.shape[0] // 4
    for plane, out_ref in enumerate(outs):
        part = result[plane * rows : (plane + 1) * rows]
        out_ref[base : base + rows, columns] = part.astype(out_ref.dtype)


def four_parts(refs, columns, tokens):
    own, other, across = refs[0], refs[1], refs[2:]
    size = own.shape[0]
    got = [across[0][:tokens, columns]] if len(across) == 1 else [ref[:, columns] for ref in across]
    parts = [own[:tokens, columns], other[:tokens, columns], *got]
    return jnp.concatenate(parts + [other[size : size + tokens, columns]], 0)


def early_body(terms, split, *refs):
    refs, outs = refs[:-4], refs[-4:]
    operands, lefts = (refs[:split], refs[split:-4]), refs[-4:]
    width = outs[0].shape[1]
    base = 0
    for which, rows, (start, end) in terms:
        right = four_parts(operands[which], slice(start, end), lefts[0].shape[2])
        result = dot(left_rows_of(lefts, rows), right)
        for column in range(0, end - start, width):
            by_plane(result[:, column : column + width], base, outs)
            base += result.shape[0] // 4


def late_body(rows, place_ref, *refs):
    refs, outs, scr = refs[:-5], refs[-5:-1], refs[-1]
    rights, lefts = refs[:-4], refs[-4:]
    columns = rights[0].shape[1]
    width = columns // 3
    size = outs[0].shape[0]
    tokens = lefts[0].shape[2]
    right = four_parts(rights, slice(None), tokens)
    by_plane(dot(left_rows_of(lefts, rows), right), 0, outs, slice(0, columns))
    own, other, across = rights
    ends = [ref[tokens : tokens + EXTRA, :width] for ref in rights]
    ends.append(other[own.shape[0] + tokens :, :width])
    tail = sum(part.astype(F32) for part in ends)
    both = jnp.concatenate([tail, jnp.zeros((LANES - EXTRA, width), F32)], 0).T
    lane = lax.broadcasted_iota(jnp.int32, (1, LANES), 1)
    lows = pltpu.roll(both, LANES - 1, 1)
    scr[...] = jnp.where(lane % 2 == 0, both + lows, 0.0)
    gains = []
    for plane in range(4):
        d = (place_ref[0] // 4 ^ plane) * 4 + place_ref[0] % 4
        gains.append(scr[pl.ds(pl.multiple_of(d * size, 16), size)])
    by_plane(jnp.concatenate(gains, 0), 0, outs, slice(columns, columns + LANES))


def four_planes(shape):
    return [(shape, F32)] + [(shape, BF)] * 3


def with_core(rows, across, count):
    return [rows, partner(jnp.concatenate([rows, *across]), 1, count), *across]


def from_planes(blocks, count):
    return [partner(item, 4 * (z + 1), count) for z, item in enumerate(blocks[1:])]


def sum_planes(own, got):
    for item in got:
        own = own + item.astype(F32)
    return own


def over_groups(rows, count):
    if count == GROUP:
        return rows
    apart = [list(range(s, count, GROUP)) for s in range(GROUP)]
    rows = rows.reshape(count // GROUP, -1, rows.shape[1])
    return lax.psum_scatter(rows, "dp", scatter_dimension=0, axis_index_groups=apart)


def on_device(
    tokens_in,
    segment_ids,
    out_grad,
    qkv_weight,
    attn_out_weight,
    mlp_in_weight,
    mlp_out_weight,
    attn_gain,
    mlp_gain,
):
    lower = lax.axis_index("section") == 0
    lower_flag = lower.astype(jnp.int32)[None]
    shard_total = qkv_weight.shape[1] * (lax.axis_size("dp") // GROUP)
    hidden_total = mlp_out_weight.shape[1] * (lax.axis_size("dp") // GROUP)
    count = lax.axis_size("dp")
    replica = lax.axis_index("dp")
    group_pos = replica % GROUP
    micro_count, row_count, width = tokens_in.shape
    shard = qkv_weight.shape[1]
    runs = -(-row_count // shard)
    (message,) = on_core(
        message_body,
        [((shard, 3 * width + LANES), BF)],
        (qkv_weight[0], attn_gain, mlp_gain, segment_ids),
        [pltpu.VMEM((LANES, LANES), F32), pltpu.VMEM((8, LANES), F32)],
    )
    first, early_piece = gather_rows(message, group_pos, count)
    inner = mlp_in_weight.shape[2]
    hidden = mlp_out_weight.shape[1] * count
    if count == GROUP:
        moved = first_block(2 * mlp_out_weight.shape[1]) - mlp_out_weight.shape[1]
        beside = partner(mlp_out_weight[0, :moved], 1, count)
        (stacked,) = on_core(
            stack_body,
            [((shard, width + inner + width + 2 * (width // 3)), BF)],
            (
                (replica % 2)[None],
                attn_out_weight[0],
                mlp_in_weight[0],
                mlp_out_weight[0],
                beside,
            ),
            (),
            [pltpu.SMEM] + [pltpu.VMEM] * 4,
        )
        stacked, _ = lax.optimization_barrier((stacked, early_piece))
        others = [lax.all_gather(stacked, "dp", axis=0, tiled=True)]
    else:
        others = [
            lax.all_gather(item[0], "dp", axis=0, tiled=True)
            for item in (attn_out_weight, mlp_in_weight, mlp_out_weight)
        ]
    positions = group_pos * row_count + jnp.arange(row_count)
    local_tables = angles(positions, local_log_base)
    global_tables = angles(positions, global_log_base)

    rows = micro_count * row_count
    pairs = rows * width // (row_count * LANES)
    in_0 = tokens_in.reshape(rows, width)
    extra_rows = -(-(2 + micro_count * runs) // 8) * 8
    extra, normed_0, q_0, kv_0 = on_core(
        local_project_body,
        [
            ((extra_rows, width), F32),
            ((rows, width), BF),
            ((rows, width), BF),
            ((rows, 2 * width), BF),
        ],
        (first, in_0, local_tables),
    )
    gain_attn, gain_mlp = extra[:1], extra[1:2]
    all_ids = extra[2 : 2 + micro_count * runs].reshape(micro_count, runs, count, shard)
    all_ids = lax.dynamic_slice_in_dim(all_ids, replica - group_pos, GROUP, 2)
    all_ids = all_ids.swapaxes(1, 2).reshape(micro_count, GROUP, runs * shard)[..., :row_count]
    segments = all_ids.reshape(micro_count, GROUP * row_count).astype(jnp.int32)

    key_pos = positions[0] - row_count + jnp.arange(3 * row_count)
    around = jnp.pad(segments, ((0, 0), (row_count, row_count)), constant_values=-1)
    key_seg = lax.dynamic_slice_in_dim(around, group_pos * row_count, 3 * row_count, 1)
    visible = (key_seg[:, :, None] == segment_ids[:, None, :]) & (
        jnp.abs(positions[None, :] - key_pos[:, None]) <= HALF_WIN
    )[None]
    bias = jnp.tile(jnp.where(visible, 0.0, masked_score), (1, 1, 2))

    own_seg = lax.dynamic_index_in_dim(segments, group_pos // 8, 0, keepdims=False)
    halves = own_seg.reshape(GROUP, 2, row_count // 2)
    mine = lax.dynamic_index_in_dim(halves, group_pos % 2, 1, keepdims=False).reshape(-1)
    theirs = lax.dynamic_index_in_dim(halves, 1 - group_pos % 2, 1, keepdims=False).reshape(-1)
    shared_seg = jnp.concatenate([mine, theirs])[:, None]
    own_seg = own_seg[:, None]

    up_pairs, down_pairs = neighbours(count, 1), neighbours(count, -1)
    around_0 = (
        lax.ppermute(kv_0, "dp", up_pairs),
        kv_0,
        lax.ppermute(kv_0, "dp", down_pairs),
    )
    att_0, total_0 = on_core(
        local_forward_body,
        [((rows, width), BF), ((pairs, 1, LANES), F32)],
        (q_0, *around_0, bias),
    )
    n2_0, mixed_0, middle_0, gate_up_0, *out_0 = on_core(
        local_middle_body,
        [
            ((rows, width), BF),
            ((rows, hidden), BF),
            ((rows, width), F32),
            ((rows, inner), F32),
        ]
        + [((row_count, width), BF)] * micro_count,
        (*others, in_0, att_0, gain_mlp),
        [pltpu.VMEM((hidden, width), BF)],
    )

    in_1 = to_other_section(out_0, 1)
    fold = row_count * 3 // 4
    half = row_count // 2
    normed_1, sent = on_core(
        global_project_body,
        [((rows, width), BF), ((GROUP, 3 * fold, LANES), BF)],
        (first, *in_1, gain_attn, global_tables),
    )
    got = exchange(sent, count)
    beside = jnp.concatenate(
        [got[:, row_count : row_count + half], got[:, 3 * fold - half :]], 1
    )
    beside = partner(beside, 1, count)
    keys = GROUP * row_count
    tiles = keys * 3 // 2 // TILE
    head_scratch = [
        pltpu.VMEM((keys * 3 // 2, LANES), BF),
        pltpu.VMEM((2, keys, LANES), BF),
        pltpu.VMEM((2, keys, LANES), BF),
        pltpu.VMEM((2, LANES, keys), BF),
    ]
    folded, total_1 = on_core(
        global_forward_body,
        [((GROUP, fold, LANES), BF), ((tiles, 1, TILE), F32)],
        (got, beside, own_seg, shared_seg),
        head_scratch + [pltpu.VMEM((keys * 3 // 2, LANES), F32)],
    )
    folded = exchange(folded, count)

    up_1 = out_grad.reshape(rows, width)
    out_1, att_1, n2_1, mixed_1, right_1, gain_mlp_1, d_mid_1, sent = on_core(
        global_middle_body,
        [
            ((rows, width), BF),
            ((rows, width), BF),
            ((rows, width), BF),
            ((rows, hidden), BF),
            ((rows, inner + width), BF),
            ((1, width), F32),
            ((rows, width), F32),
            ((GROUP, fold, LANES), BF),
        ],
        (*others, folded, *in_1, up_1, gain_mlp),
        [pltpu.VMEM((hidden, width), BF)],
    )
    d_folded = exchange(sent, count)
    pairs = ((normed_0, normed_1), (att_0, att_1), (n2_0, n2_1), (mixed_0, mixed_1))
    left_total = 3 * shard_total + hidden_total
    if count == GROUP:
        (left,) = on_core(
            left_body,
            [((4, 4, left_total, rows), BF)],
            (lower_flag, group_pos[None], *(item for pair in pairs for item in pair)),
            (),
            [pltpu.SMEM] * 2 + [pltpu.VMEM] * 8,
        )
        left, d_folded = lax.optimization_barrier((left, d_folded))
    else:
        left = [
            plane_rows(jnp.where(lower, a, b).T.reshape(count, -1, rows), group_pos, count)
            for a, b in pairs
        ]
        left = [jnp.concatenate([i.reshape(4, -1, rows) for i in items], 1) for items in zip(*left)]
    sent, to_beside = on_core(
        global_backward_body,
        [((GROUP, 3 * fold, LANES), BF), ((GROUP, 2 * half, LANES), BF)],
        (got, beside, own_seg, shared_seg, total_1, d_folded),
        head_scratch
        + [
            pltpu.VMEM((keys * 3 // 2, LANES), BF),
            pltpu.VMEM((keys * 3 // 2, LANES), F32),
            pltpu.VMEM((2, keys, LANES), F32),
            pltpu.VMEM((2, keys, LANES), F32),
        ],
    )
    back = partner(to_beside, 1, count)
    gap = 3 * fold - half - row_count - half
    back = jnp.concatenate(
        [
            jnp.zeros((GROUP, row_count, LANES), BF),
            back[:, :half],
            jnp.zeros((GROUP, gap, LANES), BF),
            back[:, half:],
        ],
        1,
    )
    sent = (sent.astype(F32) + back.astype(F32)).astype(BF)
    if count == GROUP:
        left, sent = lax.optimization_barrier((left, sent))
        left = [left[0]] + [partner(left[apart], apart, count) for apart in range(1, 4)]
    got = exchange(sent, count)
    left, got = lax.optimization_barrier((left, got))

    d_proj_1, gain_attn_1, *grad_1 = on_core(
        global_finish_body,
        [((rows, 3 * width), BF), ((1, width), F32)] + [((row_count, width), BF)] * micro_count,
        (first, got, d_mid_1, *in_1, gain_attn, global_tables),
    )

    up_0 = to_other_section(grad_1, -1)
    d_mlp = jnp.concatenate(
        [jnp.where(lower, a, up_1[i * row_count :][:row_count]) for i, a in enumerate(up_0)]
    )
    across_mlp = partner(d_mlp, 2, count)
    gain_mlp_0, d_mid_0, d_att_0, right, *right_chunks = on_core(
        local_back_middle_body,
        [
            ((1, width), F32),
            ((rows, width), F32),
            ((rows, width), BF),
            ((rows, inner + width), BF),
        ]
        + [((row_count, inner + width), BF)] * micro_count,
        (*others, lower_flag, *up_0, middle_0, gate_up_0, gain_mlp, right_1),
        [pltpu.VMEM((hidden, width), BF)],
        [pltpu.VMEM] * len(others) + [pltpu.SMEM] + [pltpu.VMEM] * 6,
    )
    d_att_0, right_chunks, across_mlp = lax.optimization_barrier(
        (d_att_0, right_chunks, across_mlp)
    )
    across = [partner(item, 2, count) for item in right_chunks]
    d_mlp = with_core(d_mlp, [across_mlp], count)
    dq_0, d_own, d_before, d_after = on_core(
        local_backward_body,
        [
            ((rows, width), BF),
            ((rows, 2 * width), F32),
            ((rows, 2 * width), BF),
            ((rows, 2 * width), BF),
        ],
        (q_0, *around_0, bias, total_0, d_att_0, local_tables),
    )
    from_after = lax.ppermute(d_before, "dp", down_pairs)
    from_before = lax.ppermute(d_after, "dp", up_pairs)
    across, right, _ = lax.optimization_barrier((across, right, d_own))
    right = with_core(right, across, count)
    in_rows, attn_rows = shard_total * (inner // width), shard_total
    early_rows = in_rows + attn_rows + hidden_total
    terms = [
        (0, (2 * shard_total, 3 * shard_total), (0, inner)),
        (0, (shard_total, 2 * shard_total), (inner, inner + width)),
        (1, (3 * shard_total, left_total), (0, width)),
    ]
    early = on_core(
        functools.partial(early_body, terms, len(right)),
        four_planes((early_rows, width)),
        (*right, *d_mlp, *left),
    )
    from_after, _ = lax.optimization_barrier((from_after, early[0]))
    early_got = from_planes(early, count)
    d_proj, grad_0, gain_attn_sum = on_core(
        local_finish_body,
        [
            ((rows + EXTRA, 3 * width), BF),
            ((rows, width), BF),
            ((1, width), F32),
        ],
        (
            lower_flag, first, dq_0, d_own, from_after, from_before, local_tables, d_mid_0, in_0, gain_attn,
            gain_mlp_0, d_proj_1, gain_attn_1, gain_mlp_1,
        ),
        [pltpu.VMEM((1, width), F32)],
        [pltpu.SMEM] + [pltpu.VMEM] * 13,
    )
    across_chunks = [partner(d_proj, 2, count)]
    early = sum_planes(early[0], early_got)
    parts = [early[p * shard_total : (p + 1) * shard_total] for p in range(inner // width)]
    in_share = jnp.concatenate(parts, 1)
    across_chunks, d_proj, _ = lax.optimization_barrier((across_chunks, d_proj, in_share))
    right = with_core(d_proj, across_chunks, count)
    late_in = (group_pos[None], *right, *left)
    late = on_core(
        functools.partial(late_body, (0, shard_total)),
        four_planes((shard_total, 3 * width + LANES)),
        late_in,
        [pltpu.VMEM((width, LANES), F32)],
        [pltpu.SMEM] + [pltpu.VMEM] * (len(late_in) - 1),
    )
    late = sum_planes(late[0], from_planes(late, count))
    mlp_out_share = early[in_rows + attn_rows :]
    attn_share = early[in_rows : in_rows + attn_rows]
    gain_columns = late[:, 3 * width :]
    qkv_share, in_share, mlp_out_share, attn_share, gain_columns = (
        over_groups(item, count)
        for item in (late[:, : 3 * width], in_share, mlp_out_share, attn_share, gain_columns)
    )
    if count == GROUP:
        gains = jnp.stack([gain_columns[:, 0], gain_columns[:, 2]])
    else:
        gain_mlp_sum = jnp.where(lower, gain_mlp_0, gain_mlp_1)
        gains = lax.psum(jnp.concatenate([gain_attn_sum, gain_mlp_sum]), "dp")
        gains = lax.dynamic_slice_in_dim(gains, replica * shard, shard, 1)

    return (
        jnp.where(lower, jnp.concatenate(out_0), out_1).reshape(1, micro_count, row_count, width),
        jnp.where(lower, grad_0, jnp.concatenate(grad_1)).reshape(1, micro_count, row_count, width),
        qkv_share[None],
        attn_share[None],
        in_share[None],
        mlp_out_share[None],
        gains[:1],
        gains[1:],
    )


def solution(mesh):
    in_specs = (
        P(None, "dp", None),
        P(None, "dp"),
        P(None, "dp", None),
        P("section", "dp", None),
        P("section", "dp", None),
        P("section", "dp", None),
        P("section", "dp", None),
        P("section", "dp"),
        P("section", "dp"),
    )
    out_specs = (
        P("section", None, "dp", None),
        P("section", None, "dp", None),
        P("section", "dp", None),
        P("section", "dp", None),
        P("section", "dp", None),
        P("section", "dp", None),
        P("section", "dp"),
        P("section", "dp"),
    )
    return jax.shard_map(
        on_device, mesh=mesh, in_specs=in_specs, out_specs=out_specs, check_vma=False
    )
```

```python
import functools
import math

import jax
import jax.numpy as jnp
from jax import lax
from jax.experimental import pallas as pl
from jax.experimental.pallas import tpu as pltpu
from jax.sharding import PartitionSpec as P

HEAD_DIM = 64
GROUP = 16
HALF_WIN = 64
EXTRA = 16
LANES = 128
TILE = 256

local_log_base = math.log(10000.0)
global_log_base = math.log(160000.0)
masked_score = -1e30
SCALE = 1.0 / math.sqrt(HEAD_DIM)
BF = jnp.bfloat16
F32 = jnp.float32


def dot(left, right):
    return jnp.dot(left, right, preferred_element_type=F32)


def dot_bt(left, right):
    return lax.dot_general(left, right, (((1,), (1,)), ((), ())), preferred_element_type=F32)


def dot_at(left, right):
    return lax.dot_general(left, right, (((0,), (0,)), ((), ())), preferred_element_type=F32)


def moments(values):
    center = values - jnp.mean(values, -1, keepdims=True)
    scale = lax.rsqrt(jnp.mean(center * center, -1, keepdims=True) + 1e-05)
    return center * scale, scale


def norm_back(grad_out, gain_row, xhat, scale):
    scaled = grad_out * gain_row
    mean_grad = jnp.mean(scaled, -1, keepdims=True)
    mean_dot = jnp.mean(scaled * xhat, -1, keepdims=True)
    return (scaled - mean_grad - xhat * mean_dot) * scale


def angles(positions, log_base):
    half_dim = HEAD_DIM // 2
    fraction = (2 * jnp.arange(half_dim)).astype(F32) / HEAD_DIM
    inverse = jnp.exp(-fraction * log_base)
    table = positions.astype(F32)[:, None] * inverse[None, :]
    cosine, sine = jnp.cos(table), jnp.sin(table)
    none = jnp.zeros_like(sine)
    cosine = jnp.concatenate([cosine, cosine], 1)
    to_first = jnp.concatenate([-sine, none], 1)
    to_second = jnp.concatenate([none, sine], 1)
    return jnp.tile(jnp.stack([cosine, to_first, to_second]), (1, 2, 2))


def on_core(body, outs, args, scratch=(), spaces=None, out_spaces=None):
    return pl.pallas_call(
        body,
        out_shape=[jax.ShapeDtypeStruct(shape, dtype) for shape, dtype in outs],
        in_specs=[
            pl.BlockSpec(memory_space=space) for space in spaces or [pltpu.VMEM] * len(args)
        ],
        out_specs=[
            pl.BlockSpec(memory_space=space) for space in out_spaces or [pltpu.VMEM] * len(outs)
        ],
        scratch_shapes=scratch,
        cost_estimate=pl.CostEstimate(
            flops=2**10, bytes_accessed=2**10, transcendentals=0
        ),
        compiler_params=pltpu.CompilerParams(vmem_limit_bytes=48 * 2**20),
    )(*args)


def low_lanes():
    return lax.broadcasted_iota(jnp.int32, (1, LANES), 1) < HEAD_DIM


def swap(chunk):
    return pltpu.roll(chunk, HEAD_DIM, 1)


def chunks_of(rows):
    return [rows[:, c : c + LANES] for c in range(0, rows.shape[1], LANES)]


def rotate(chunk, tables):
    cosine, to_first, to_second = tables
    quarter = HEAD_DIM // 2
    return (
        chunk * cosine
        + pltpu.roll(chunk, LANES - quarter, 1) * to_first
        + pltpu.roll(chunk, quarter, 1) * to_second
    )


def unrotate(chunk, tables):
    cosine, to_first, to_second = tables
    quarter = HEAD_DIM // 2
    return (
        chunk * cosine
        - pltpu.roll(chunk, LANES - quarter, 1) * to_first
        - pltpu.roll(chunk, quarter, 1) * to_second
    )


def low_and_high(chunks):
    swapped = [swap(chunk) for chunk in chunks]
    low = [(swapped if h % 2 else chunks)[h // 2] for h in range(2 * len(chunks))]
    high = [(chunks if h % 2 else swapped)[h // 2] for h in range(2 * len(chunks))]
    return low, high


def targets():
    for d in range(GROUP):
        micro, chip, half = d // 8, d % 8 // 2, d % 2
        yield d, micro, 3 * chip + 2 * half, 3 * chip + 1, half


def pack_folded(chunks, ref, base):
    low, high = low_and_high(chunks)
    first = low_lanes()
    rows = chunks[0].shape[0] // 2
    half, fold = rows // 2, rows * 3 // 4
    for d, micro, own, shared, side in targets():
        start = micro * rows
        part = start + side * half
        upper = jnp.concatenate(
            [high[own][start + fold : start + rows], high[shared][part : part + half]], 0
        )
        ref[d, base : base + fold] = jnp.where(
            first, low[own][start : start + fold], upper
        ).astype(BF)


def pack_pairs(lefts, rights, ref):
    low, high = low_and_high(lefts)[0], low_and_high(rights)[1]
    first = low_lanes()
    rows = lefts[0].shape[0] // 2
    half = rows // 2
    for d, micro, own, shared, side in targets():
        start = micro * rows
        part = start + side * half
        ref[d, 0:rows] = jnp.where(
            first, low[own][start : start + rows], high[own][start : start + rows]
        ).astype(BF)
        ref[d, rows : rows + half] = jnp.where(
            first, low[shared][part : part + half], high[shared][part : part + half]
        ).astype(BF)


def unpack_folded(ref, base, rows):
    first = low_lanes()
    fold = rows * 3 // 4
    low, high = {}, {}
    shared_parts = {}
    for d, micro, own, shared, side in targets():
        block = ref[d, base : base + fold].astype(F32)
        mine = jnp.concatenate([block, swap(block[: rows - fold])], 0)
        if own % 2:
            high[micro, own] = swap(mine)
        else:
            low[micro, own] = mine
        shared_parts[micro, shared, side] = block[rows - fold :]
        if side:
            both = jnp.concatenate([shared_parts[micro, shared, 0], block[rows - fold :]], 0)
            if shared % 2:
                high[micro, shared] = both
            else:
                low[micro, shared] = swap(both)
    heads = GROUP // 4 * 3
    return [
        jnp.concatenate(
            [jnp.where(first, low[m, h], high[m, h + 1]) for m in range(2)], 0
        )
        for h in range(0, heads, 2)
    ]


def unpack_pairs(ref, rows):
    first = low_lanes()
    half = rows // 2
    pairs = {}
    parts = {}
    for d, micro, own, shared, side in targets():
        pairs[micro, own] = ref[d, 0:rows].astype(F32)
        parts[side] = ref[d, rows : rows + half].astype(F32)
        if side:
            pairs[micro, shared] = jnp.concatenate([parts[0], parts[1]], 0)
    heads = GROUP // 4 * 3
    lefts, rights = [], []
    for h in range(0, heads, 2):
        even, odd = [pairs[m, h] for m in range(2)], [pairs[m, h + 1] for m in range(2)]
        lefts.append(
            jnp.concatenate([jnp.where(first, a, swap(b)) for a, b in zip(even, odd)], 0)
        )
        rights.append(
            jnp.concatenate([jnp.where(first, swap(a), b) for a, b in zip(even, odd)], 0)
        )
    return lefts, rights


class Weights:
    def __init__(self, sources, mlp_out):
        self.sources = sources
        self.mlp_out = sources[-1]
        if len(sources) == 1:
            self.mlp_out = mlp_out
            unpack_rows(sources[0], mlp_out)

    def get(self, which):
        if which == 2:
            return self.mlp_out[...]
        if len(self.sources) > 1:
            return self.sources[which][...]
        (wide,) = self.sources
        width = wide.shape[0]
        inner = 2 * self.mlp_out.shape[0]
        return wide[:, width : width + inner] if which else wide[:, :width]


def first_block(pair):
    return -(-pair // 32) * 16


def packed_pieces(shard, rows, width):
    yield 0, shard, 0, width, 0, 0
    rest = rows - shard
    side = width // 3
    yield 0, rest, width, 2 * side, shard, 0
    yield rest, 16, width, side, shard, 2 * side
    yield rest, 16, width + side, side, shard + 16, 2 * side


def unpack_rows(wide, mlp_out):
    hidden, width = mlp_out.shape
    shard = wide.shape[0] // GROUP
    start = wide.shape[1] - width - 2 * (width // 3)
    pair = 2 * hidden // GROUP
    upper = first_block(pair)
    for d in range(GROUP):
        low = d // 2 * pair + d % 2 * upper
        have = pair - upper if d % 2 else upper
        for row, rows, column, columns, to_row, to_column in packed_pieces(shard, upper, width):
            rows = min(rows, have - to_row)
            if rows > 0:
                mlp_out[low + to_row : low + to_row + rows, to_column : to_column + columns] = wide[
                    d * shard + row : d * shard + row + rows, start + column : start + column + columns
                ]


def stack_body(odd_ref, attn_ref, mlp_in_ref, own_ref, beside_ref, out_ref):
    shard, width = attn_ref.shape
    inner = mlp_in_ref.shape[1]
    out_ref[:, :width] = attn_ref[...]
    out_ref[:, width : width + inner] = mlp_in_ref[...]
    own, beside = own_ref[...].astype(F32), beside_ref[...].astype(F32)
    moved = beside.shape[0]
    even = jnp.concatenate([own, beside], 0)
    odd = jnp.concatenate([own[moved:], beside, beside], 0)
    block = jnp.where(odd_ref[0] == 1, odd, even).astype(BF)
    start = width + inner
    for row, rows, column, columns, from_row, from_column in packed_pieces(
        shard, block.shape[0], width
    ):
        out_ref[row : row + rows, start + column : start + column + columns] = block[
            from_row : from_row + rows, from_column : from_column + columns
        ]


def mlp_forward(layer_in, attended, gain, weights):
    middle = layer_in + dot(attended, weights.get(0))
    xhat, _ = moments(middle)
    normed = (xhat * gain).astype(BF)
    gate_up = dot(normed, weights.get(1))
    half = gate_up.shape[1] // 2
    gate, up = gate_up[:, :half], gate_up[:, half:]
    cdf = 0.5 * (1.0 + lax.erf(gate * math.sqrt(0.5)))
    mixed = (gate * cdf * up).astype(BF)
    result = (middle + dot(mixed, weights.get(2))).astype(BF)
    return middle, normed, gate, up, mixed, result


def mlp_backward(upstream, middle, gate, up, gain, weights):
    d_mixed = dot_bt(upstream, weights.get(2))
    cdf = 0.5 * (1.0 + lax.erf(gate * math.sqrt(0.5)))
    density = jnp.exp(-0.5 * gate * gate) * (1.0 / math.sqrt(2.0 * math.pi))
    d_gate = d_mixed * up * (cdf + gate * density)
    d_up = d_mixed * gate * cdf
    d_gate_up = jnp.concatenate([d_gate.astype(BF), d_up.astype(BF)], 1)
    d_normed = dot_bt(d_gate_up, weights.get(1))
    xhat, scale = moments(middle)
    gain_grad = jnp.sum(d_normed * xhat, 0, keepdims=True)
    d_middle = upstream.astype(F32) + norm_back(d_normed, gain, xhat, scale)
    d_attn = d_middle.astype(BF)
    d_attended = dot_bt(d_attn, weights.get(0))
    return d_gate_up, gain_grad, d_middle, d_attn, d_attended


def project(xhat, gain, first_ref, table_ref, normed_ref):
    width = xhat.shape[1]
    normed = (xhat * gain).astype(BF)
    normed_ref[...] = normed
    tables = [table_ref[i] for i in range(3)]
    results = [dot(normed, first_ref[:, c * width : (c + 1) * width]) for c in range(3)]
    queries, keys, values = chunks_of(results[0]), chunks_of(results[1]), results[2]
    return [rotate(c, tables) for c in queries], [rotate(c, tables) for c in keys], values


def input_backward(d_middle, d_projected, x, gain_ref, first_ref, gain_out_ref):
    d_normed = dot_bt(d_projected, first_ref[:, : d_projected.shape[1]])
    xhat, scale = moments(x)
    gain_out_ref[...] = jnp.sum(d_normed * xhat, 0, keepdims=True)
    return (d_middle + norm_back(d_normed, gain_ref[...], xhat, scale)).astype(BF)


def joined(refs):
    return jnp.concatenate([ref[...] for ref in refs], 0)


def store_chunks(refs, rows):
    size = rows.shape[0] // len(refs)
    for i, ref in enumerate(refs):
        ref[...] = rows[i * size : (i + 1) * size]


def message_body(w_ref, attn_ref, mlp_ref, ids_ref, out_ref, rows_scr, ids_scr):
    shard, columns = w_ref.shape
    micro_count, row_count = ids_ref.shape
    out_ref[:, :columns] = w_ref[...]
    rows_scr[...] = jnp.zeros_like(rows_scr)
    ids_scr[...] = jnp.zeros_like(ids_scr)
    rows_scr[0:1, :shard] = attn_ref[...].astype(F32)
    rows_scr[1:2, :shard] = mlp_ref[...].astype(F32)
    ids_scr[:micro_count, :row_count] = ids_ref[...].astype(F32)
    runs = -(-row_count // shard)
    for run in range(runs):
        turned = ids_scr[...]
        if run:
            turned = pltpu.roll(turned, LANES - run * shard, 1)
        for micro in range(micro_count):
            row = 2 + micro * runs + run
            rows_scr[row : row + 1] = turned[micro : micro + 1]
    out_ref[:, columns:] = rows_scr[...].T[:shard].astype(BF)


def local_project_body(first_ref, x_ref, table_ref, extra_ref, normed_ref, q_ref, kv_ref):
    xhat, _ = moments(x_ref[...].astype(F32))
    extra = first_ref[:, first_ref.shape[1] - LANES :].astype(F32).T
    extra_ref[...] = extra[: extra_ref.shape[0]]
    queries, keys, values = project(xhat, extra[:1], first_ref, table_ref, normed_ref)
    width = values.shape[1]
    for j, (q, k) in enumerate(zip(queries, keys)):
        q_ref[:, LANES * j : LANES * (j + 1)] = q.astype(BF)
        kv_ref[:, LANES * j : LANES * (j + 1)] = k.astype(BF)
    kv_ref[:, width:] = values.astype(BF)


def two_heads(chunk):
    first = low_lanes()
    wide = chunk.astype(F32)
    return jnp.concatenate([jnp.where(first, wide, 0.0), jnp.where(first, 0.0, wide)], 0)


def pick_heads(rows):
    half = rows.shape[0] // 2
    return jnp.where(low_lanes(), rows[:half], rows[half:])


def local_parts(q_ref, before_ref, own_ref, after_ref):
    rows = q_ref.shape[0] // 2
    width = q_ref.shape[1]
    for micro in range(2):
        for j in range(width // LANES):
            here = slice(micro * rows, (micro + 1) * rows)
            lanes = slice(LANES * j, LANES * (j + 1))
            more = slice(width + LANES * j, width + LANES * (j + 1))
            keys, values = (
                jnp.concatenate([ref[here, part] for ref in (before_ref, own_ref, after_ref)], 0)
                for part in (lanes, more)
            )
            queries = (two_heads(q_ref[here, lanes]) * SCALE).astype(BF)
            yield micro * (width // LANES) + j, micro, here, lanes, more, queries, keys, values


def local_forward_body(q_ref, before_ref, own_ref, after_ref, bias_ref, att_ref, total_ref):
    parts = local_parts(q_ref, before_ref, own_ref, after_ref)
    for index, micro, here, lanes, _, queries, keys, values in parts:
        scores = dot_bt(keys, queries) + bias_ref[micro]
        peak = jnp.max(scores, 0, keepdims=True)
        weights = jnp.exp(scores - peak)
        total = jnp.sum(weights, 0, keepdims=True)
        total_ref[index] = peak + jnp.log(total)
        probs = (weights * (1.0 / total)).astype(BF)
        att_ref[here, lanes] = pick_heads(dot_at(probs, values)).astype(BF)


def local_backward_body(
    q_ref, before_ref, own_ref, after_ref, bias_ref, total_ref, d_ref, table_ref,
    dq_ref, d_own_ref, d_before_ref, d_after_ref,
):
    tables = [table_ref[i] for i in range(3)]
    parts = local_parts(q_ref, before_ref, own_ref, after_ref)
    rows = q_ref.shape[0] // 2
    for index, micro, here, lanes, more, queries, keys, values in parts:
        d_out = two_heads(d_ref[here, lanes]).astype(BF)
        probs = jnp.exp(dot_bt(keys, queries) + bias_ref[micro] - total_ref[index])
        d_probs = dot_bt(values, d_out)
        product = probs * d_probs
        delta = jnp.sum(product, 0, keepdims=True)
        d_scores = (product - probs * delta).astype(BF)
        d_queries = pick_heads(dot_at(d_scores, keys)) * SCALE
        local_tables = [table[here] for table in tables]
        dq_ref[here, lanes] = unrotate(d_queries, local_tables).astype(BF)
        for part, grads in ((lanes, dot(d_scores, queries)), (more, dot(probs.astype(BF), d_out))):
            d_before_ref[here, part] = grads[:rows].astype(BF)
            d_own_ref[here, part] = grads[rows : 2 * rows]
            d_after_ref[here, part] = grads[2 * rows :].astype(BF)


def local_finish_body(
    lower_ref, first_ref, dq_ref, own_ref, low_ref, high_ref, table_ref, d_middle_ref, x_ref, gain_ref,
    gain_mlp_ref, other_ref, other_attn_ref, other_mlp_ref, out_ref, grad_ref, gain_attn_ref,
    gain_scr,
):
    rows, width = dq_ref.shape

    @pl.when(lower_ref[0] == 1)
    def _():
        tables = [table_ref[i] for i in range(3)]
        total = own_ref[...] + low_ref[...].astype(F32) + high_ref[...].astype(F32)
        out_ref[:rows, :width] = dq_ref[...]
        for j, chunk in enumerate(chunks_of(total[:, :width])):
            start = width + LANES * j
            out_ref[:rows, start : start + LANES] = unrotate(chunk, tables).astype(BF)
        out_ref[:rows, 2 * width :] = total[:, width:].astype(BF)
        grad_ref[...] = input_backward(
            d_middle_ref[...], out_ref[:rows], x_ref[...].astype(F32), gain_ref, first_ref, gain_scr
        )

    @pl.when(lower_ref[0] == 0)
    def _():
        out_ref[:rows] = other_ref[...]
        grad_ref[...] = jnp.zeros_like(grad_ref)
        gain_scr[...] = other_attn_ref[...]

    gain_attn_ref[...] = gain_scr[...]
    gain_mlp = jnp.where(lower_ref[0] == 1, gain_mlp_ref[...], other_mlp_ref[...])
    index = lax.broadcasted_iota(jnp.int32, (EXTRA, width), 0)
    tail = jnp.zeros((EXTRA, width), F32)
    for row, gain in ((0, gain_scr[...]), (2, gain_mlp)):
        high = gain.astype(BF).astype(F32)
        tail = jnp.where(index == row, high, tail)
        tail = jnp.where(index == row + 1, gain - high, tail)
    out_ref[rows:] = jnp.zeros((EXTRA, out_ref.shape[1]), BF)
    out_ref[rows:, :width] = tail.astype(BF)


def local_middle_body(*refs):
    sources, refs = refs[:-8], refs[-8:]
    x_ref, att_ref, gain_ref, kept_ref, state_ref = refs[:5]
    weights = Weights(sources, refs[7])
    middle, normed, gate, up, mixed, result = mlp_forward(
        x_ref[...].astype(F32), att_ref[...], gain_ref[...], weights
    )
    store_chunks(refs[5:7], result)
    width, half = middle.shape[1], gate.shape[1]
    kept_ref[:, :width] = normed
    kept_ref[:, width:] = mixed
    state_ref[:, :width] = middle
    state_ref[:, width : width + half] = gate
    state_ref[:, width + half :] = up


def local_back_middle_body(*refs):
    sources, refs = refs[:-11], refs[-11:]
    lower_ref, low_ref, high_ref, state_ref, gain_ref, other_ref = refs[:6]
    gain_out_ref, d_middle_ref, d_att_ref, right_ref = refs[6:10]
    weights = Weights(sources, refs[10])
    width = low_ref.shape[1]
    half = (state_ref.shape[1] - width) // 2
    upstream = joined([low_ref, high_ref])
    d_gate_up, gain_grad, d_middle, d_attn, d_attended = mlp_backward(
        upstream, state_ref[:, :width], state_ref[:, width : width + half], state_ref[:, width + half :],
        gain_ref[...], weights,
    )
    gain_out_ref[...] = gain_grad
    d_middle_ref[...] = d_middle
    d_att_ref[...] = d_attended.astype(BF)

    @pl.when(lower_ref[0] == 1)
    def _():
        right_ref[:, : 2 * half] = d_gate_up
        right_ref[:, 2 * half :] = d_attn

    @pl.when(lower_ref[0] == 0)
    def _():
        right_ref[...] = other_ref[:, other_ref.shape[1] - right_ref.shape[1] :]


def global_project_body(first_ref, low_ref, high_ref, gain_ref, table_ref, normed_ref, sent_ref):
    xhat, _ = moments(joined([low_ref, high_ref]).astype(F32))
    queries, keys, values = project(xhat, gain_ref[...], first_ref, table_ref, normed_ref)
    pack_pairs(queries, keys, sent_ref)
    pack_folded(chunks_of(values), sent_ref, sent_ref.shape[1] * 2 // 3)


def flat(blocks):
    return blocks.reshape(-1, LANES)


def own_unfolded(ref, base, rows):
    fold = rows * 3 // 4
    block = ref[:, base : base + fold].astype(F32)
    rest = swap(flat(block[:, : rows - fold])).reshape(GROUP, rows - fold, LANES)
    return flat(jnp.concatenate([block, rest], 1))


def shared_unfolded(ref, start, rows):
    return swap(flat(ref[:, start : start + rows // 2].astype(F32)))


def fill_heads(got_ref, other_ref, own_seg_ref, shared_seg_ref, q_scr, k_scr, v_scr):
    rows = got_ref.shape[1] * 4 // 9
    half = rows // 2
    first = low_lanes()
    lane = lax.broadcasted_iota(jnp.int32, (1, LANES), 1) - HEAD_DIM
    own = flat(got_ref[:, 0:rows].astype(F32))
    shared = flat(got_ref[:, rows : rows + half].astype(F32))
    other = flat(other_ref[:, 0:half].astype(F32))
    count = own.shape[0]
    own_hit = lane == own_seg_ref[...]
    shared_hit = lane == shared_seg_ref[...]
    both = jnp.concatenate([shared, other], 0)
    for start, pairs, hit in (
        (0, own, own_hit),
        (count, shared, shared_hit[: count // 2]),
    ):
        marked = jnp.where(hit, 1.0, 0.0)
        q_scr[start : start + pairs.shape[0]] = jnp.where(first, pairs * SCALE, marked).astype(BF)
    for unit, pairs, hit in ((0, own, own_hit), (1, both, shared_hit)):
        marked = jnp.where(hit, 0.0, masked_score)
        k_scr[unit] = jnp.where(first, swap(pairs), marked).astype(BF)
    base = rows + half
    v_scr[0] = jnp.where(first, own_unfolded(got_ref, base, rows), 0.0).astype(BF)
    start = base + rows - rows * 3 // 4
    shared_v = jnp.concatenate(
        [shared_unfolded(got_ref, start, rows), shared_unfolded(other_ref, half, rows)], 0
    )
    v_scr[1] = jnp.where(first, shared_v, 0.0).astype(BF)


def fold_out(own, shared, rows, ref, base):
    fold = rows * 3 // 4
    blocks = own.reshape(GROUP, rows, LANES)
    swapped = swap(own).reshape(GROUP, rows, LANES)
    upper = jnp.concatenate(
        [swapped[:, fold:], swap(shared).reshape(GROUP, rows // 2, LANES)], 1
    )
    ref[:, base : base + fold] = jnp.where(low_lanes(), blocks[:, :fold], upper).astype(BF)


def global_forward_body(
    got_ref, other_ref, own_seg_ref, shared_seg_ref, out_ref, total_ref,
    q_scr, k_scr, v_scr, vt_scr, o_scr,
):
    fill_heads(got_ref, other_ref, own_seg_ref, shared_seg_ref, q_scr, k_scr, v_scr)
    for unit in range(2):
        vt_scr[unit] = v_scr[unit].astype(F32).T.astype(BF)
    count = k_scr.shape[1]

    def step(tile, carry):
        unit = tile // (count // TILE)
        rows = pl.ds(pl.multiple_of(tile * TILE, TILE), TILE)
        scores = dot_bt(k_scr[unit], q_scr[rows])
        peak = jnp.max(scores, 0, keepdims=True)
        weights = jnp.exp(scores - peak)
        total = jnp.sum(weights, 0, keepdims=True)
        total_ref[tile] = peak + jnp.log(total)
        out = dot(vt_scr[unit], weights.astype(BF)) * (1.0 / total)
        o_scr[rows] = out.T
        return carry

    lax.fori_loop(0, q_scr.shape[0] // TILE, step, 0)
    rows = got_ref.shape[1] * 4 // 9
    fold_out(o_scr[:count], o_scr[count:], rows, out_ref, 0)


def global_backward_body(
    got_ref, other_ref, own_seg_ref, shared_seg_ref, total_ref, d_ref, sent_ref, to_other_ref,
    q_scr, k_scr, v_scr, kt_scr, d_scr, dq_scr, dk_scr, dv_scr,
):
    fill_heads(got_ref, other_ref, own_seg_ref, shared_seg_ref, q_scr, k_scr, v_scr)
    first = low_lanes()
    rows = got_ref.shape[1] * 4 // 9
    half = rows // 2
    for unit in range(2):
        keys = jnp.where(first, k_scr[unit].astype(F32), 0.0)
        kt_scr[unit] = keys.T.astype(BF)
    count = k_scr.shape[1]
    d_scr[:count] = jnp.where(first, own_unfolded(d_ref, 0, rows), 0.0).astype(BF)
    d_scr[count:] = jnp.where(
        first, shared_unfolded(d_ref, rows - rows * 3 // 4, rows), 0.0
    ).astype(BF)
    dk_scr[...] = jnp.zeros_like(dk_scr)
    dv_scr[...] = jnp.zeros_like(dv_scr)

    def step(tile, carry):
        unit = tile // (count // TILE)
        here = pl.ds(pl.multiple_of(tile * TILE, TILE), TILE)
        queries, d_out = q_scr[here], d_scr[here]
        probs = jnp.exp(dot_bt(k_scr[unit], queries) - total_ref[tile])
        d_probs = dot_bt(v_scr[unit], d_out)
        product = probs * d_probs
        delta = jnp.sum(product, 0, keepdims=True)
        d_scores = (product - probs * delta).astype(BF)
        dv_scr[unit] += dot(probs.astype(BF), d_out)
        dk_scr[unit] += dot(d_scores, queries)
        dq_scr[here] = dot(kt_scr[unit], d_scores).T * SCALE
        return carry

    lax.fori_loop(0, q_scr.shape[0] // TILE, step, 0)
    mine = count // 2
    own = jnp.where(first, dq_scr[:count], swap(dk_scr[0]))
    sent_ref[:, 0:rows] = own.reshape(GROUP, rows, LANES).astype(BF)
    shared_k, shared_v = dk_scr[1], dv_scr[1]
    shared = jnp.where(first, dq_scr[count:], swap(shared_k[:mine]))
    sent_ref[:, rows : rows + half] = shared.reshape(GROUP, half, LANES).astype(BF)
    fold_out(dv_scr[0], shared_v[:mine], rows, sent_ref, rows + half)
    for place, grads in enumerate((shared_k, shared_v)):
        other = jnp.where(first, 0.0, swap(grads[mine:])).reshape(GROUP, half, LANES)
        to_other_ref[:, place * half : (place + 1) * half] = other.astype(BF)


def global_middle_body(*refs):
    sources, refs = refs[:-10], refs[-10:]
    got_ref, low_ref, high_ref, up_ref, gain_ref, kept_ref, gain_out_ref, d_middle_ref, sent_ref = refs[:9]
    weights = Weights(sources, refs[9])
    rows, width = low_ref.shape
    attended = jnp.concatenate([c.astype(BF) for c in unpack_folded(got_ref, 0, rows)], 1)
    gain = gain_ref[...]
    middle, normed, gate, up, mixed, result = mlp_forward(
        joined([low_ref, high_ref]).astype(F32), attended, gain, weights
    )
    d_gate_up, gain_grad, d_middle, d_attn, d_attended = mlp_backward(
        up_ref[...], middle, gate, up, gain, weights
    )
    start = 0
    for part in (result, attended, normed, mixed, d_gate_up, d_attn):
        kept_ref[:, start : start + part.shape[1]] = part
        start += part.shape[1]
    gain_out_ref[...] = gain_grad
    d_middle_ref[...] = d_middle
    pack_folded(chunks_of(d_attended), sent_ref, 0)


def global_finish_body(
    first_ref, got_ref, d_middle_ref, low_ref, high_ref, gain_ref, table_ref,
    d_proj_ref, gain_out_ref, *grad_refs,
):
    tables = [table_ref[i] for i in range(3)]
    x = joined([low_ref, high_ref]).astype(F32)
    rows = low_ref.shape[0]
    d_queries, d_keys = unpack_pairs(got_ref, rows)
    d_values = unpack_folded(got_ref, rows * 3 // 2, rows)
    parts = [unrotate(c, tables).astype(BF) for c in d_queries + d_keys]
    d_projected = jnp.concatenate(parts + [c.astype(BF) for c in d_values], 1)
    d_proj_ref[...] = d_projected
    store_chunks(
        grad_refs,
        input_backward(d_middle_ref[...], d_projected, x, gain_ref, first_ref, gain_out_ref),
    )


def neighbours(count, step):
    return [
        (i, i + step)
        for i in range(count)
        if 0 <= i + step < count and i // GROUP == (i + step) // GROUP
    ]


def exchange(blocks, count):
    groups = [list(range(s, s + GROUP)) for s in range(0, count, GROUP)]
    return lax.all_to_all(blocks, "dp", 0, 0, axis_index_groups=groups)


def to_other_section(chunks, step):
    pairs = [(0, 1)] if step > 0 else [(1, 0)]
    return [lax.ppermute(rows, "section", pairs) for rows in chunks]


def partner(rows, apart, count):
    return lax.ppermute(rows, "dp", [(i, i ^ apart) for i in range(count)])


def gather_rows(piece, group_pos, count):
    pieces = {0: piece}
    for apart in (4, 8, 12):
        pieces[apart] = partner(piece, apart, count)
    for apart in (0, 4, 8, 12):
        pieces[apart + 2] = partner(pieces[apart], 2, count)
    for apart in range(0, GROUP, 2):
        pieces[apart + 1] = partner(pieces[apart], 1, count)
    whole = jnp.zeros((GROUP,) + piece.shape, piece.dtype)
    for apart, item in pieces.items():
        start = (group_pos ^ apart,) + (0,) * piece.ndim
        whole = lax.dynamic_update_slice(whole, item[None], start)
    if count > GROUP:
        groups = [list(range(s, count, GROUP)) for s in range(GROUP)]
        whole = lax.all_gather(whole, "dp", axis=0, tiled=True, axis_index_groups=groups)
    return whole.reshape(-1, piece.shape[-1]), pieces[2]


def plane_rows(rows, group_pos, count):
    parts = rows.reshape(count // GROUP, 4, 4, *rows.shape[1:])
    place, plane = group_pos % 4, group_pos // 4
    taken = []
    for apart in range(4):
        block = lax.dynamic_index_in_dim(parts, place ^ apart, 2, keepdims=False)
        block = jnp.stack(
            [lax.dynamic_index_in_dim(block, plane ^ z, 1, keepdims=False) for z in range(4)]
        )
        taken.append(partner(block, apart, count) if apart else block)
    return taken


def left_body(spans, lower_ref, place_ref, *refs):
    refs, out_ref = refs[:-1], refs[-1]
    base = 0
    for span in spans:
        first, second = (refs[i][:, start:end].astype(F32) for i, start, end in span)
        turned = jnp.where(lower_ref[0] == 1, first, second).T
        size = turned.shape[0] // GROUP
        for d in range(GROUP):
            side = d % 4 ^ place_ref[0] % 4
            plane = d // 4 ^ place_ref[0] // 4
            out_ref[side, plane, base : base + size] = turned[d * size : (d + 1) * size].astype(BF)
        base += size


def left_rows_of(refs, rows):
    start, end = rows
    parts = [
        jnp.concatenate([ref[p, start:end].astype(F32) for p in range(4)], 0).astype(BF) for ref in refs
    ]
    return jnp.concatenate(parts, 1)


def by_plane(result, base, outs, columns=slice(None)):
    keep, keep_far, send = outs
    rows = result.shape[0] // 4
    half = send.shape[0] // 2
    here = slice(base, base + rows)
    keep[here, columns] = result[:rows]
    keep_far[here, columns] = result[2 * rows : 3 * rows]
    send[here, columns] = result[rows : 2 * rows].astype(BF)
    send[half + base : half + base + rows, columns] = result[3 * rows :].astype(BF)


def early_body(terms, split, *refs):
    refs, outs = refs[:-3], refs[-3:]
    operands, lefts = (refs[:split], refs[split:-4]), refs[-4:]
    width = outs[0].shape[1]
    base = 0
    for which, rows, (start, end) in terms:
        right = jnp.concatenate([ref[:, start:end] for ref in operands[which]], 0)
        result = dot(left_rows_of(lefts, rows), right)
        for column in range(0, end - start, width):
            by_plane(result[:, column : column + width], base, outs)
            base += result.shape[0] // 4


def late_body(rows, place_ref, *refs):
    refs, outs, scr = refs[:-4], refs[-4:-1], refs[-1]
    rights, lefts = refs[:-4], refs[-4:]
    columns = rights[0].shape[1]
    width = columns // 3
    size = outs[0].shape[0]
    tokens = lefts[0].shape[2]
    right = jnp.concatenate([ref[:tokens] for ref in rights], 0)
    by_plane(dot(left_rows_of(lefts, rows), right), 0, outs, slice(0, columns))
    tail = sum(ref[tokens:, :width].astype(F32) for ref in rights)
    both = jnp.concatenate([tail, jnp.zeros((LANES - EXTRA, width), F32)], 0).T
    lane = lax.broadcasted_iota(jnp.int32, (1, LANES), 1)
    lows = pltpu.roll(both, LANES - 1, 1)
    scr[...] = jnp.where(lane % 2 == 0, both + lows, 0.0)
    gains = []
    for plane in range(4):
        d = (place_ref[0] // 4 ^ plane) * 4 + place_ref[0] % 4
        gains.append(scr[pl.ds(pl.multiple_of(d * size, 16), size)])
    by_plane(jnp.concatenate(gains, 0), 0, outs, slice(columns, columns + LANES))


def three_parts(shape):
    return [(shape, F32), (shape, F32), ((2 * shape[0], shape[1]), BF)]


def first_hop(blocks, count):
    keep, keep_far, send = blocks
    got = partner(send, 4, count)
    half = keep.shape[0]
    return keep + got[:half].astype(F32), (keep_far + got[half:].astype(F32)).astype(BF)


def second_hop(near, far, count):
    return near + partner(far, 8, count).astype(F32)


def over_groups(rows, count):
    if count == GROUP:
        return rows
    apart = [list(range(s, count, GROUP)) for s in range(GROUP)]
    rows = rows.reshape(count // GROUP, -1, rows.shape[1])
    return lax.psum_scatter(rows, "dp", scatter_dimension=0, axis_index_groups=apart)


def on_device(
    tokens_in,
    segment_ids,
    out_grad,
    qkv_weight,
    attn_out_weight,
    mlp_in_weight,
    mlp_out_weight,
    attn_gain,
    mlp_gain,
):
    lower = lax.axis_index("section") == 0
    lower_flag = lower.astype(jnp.int32)[None]
    shard_total = qkv_weight.shape[1] * (lax.axis_size("dp") // GROUP)
    hidden_total = mlp_out_weight.shape[1] * (lax.axis_size("dp") // GROUP)
    count = lax.axis_size("dp")
    replica = lax.axis_index("dp")
    group_pos = replica % GROUP
    micro_count, row_count, width = tokens_in.shape
    shard = qkv_weight.shape[1]
    runs = -(-row_count // shard)
    (message,) = on_core(
        message_body,
        [((shard, 3 * width + LANES), BF)],
        (qkv_weight[0], attn_gain, mlp_gain, segment_ids),
        [pltpu.VMEM((LANES, LANES), F32), pltpu.VMEM((8, LANES), F32)],
    )
    first, early_piece = gather_rows(message, group_pos, count)
    inner = mlp_in_weight.shape[2]
    hidden = mlp_out_weight.shape[1] * count
    if count == GROUP:
        moved = first_block(2 * mlp_out_weight.shape[1]) - mlp_out_weight.shape[1]
        beside = partner(mlp_out_weight[0, :moved], 1, count)
        (stacked,) = on_core(
            stack_body,
            [((shard, width + inner + width + 2 * (width // 3)), BF)],
            (
                (replica % 2)[None],
                attn_out_weight[0],
                mlp_in_weight[0],
                mlp_out_weight[0],
                beside,
            ),
            (),
            [pltpu.SMEM] + [pltpu.VMEM] * 4,
        )
        stacked, _ = lax.optimization_barrier((stacked, early_piece))
        others = [lax.all_gather(stacked, "dp", axis=0, tiled=True)]
    else:
        others = [
            lax.all_gather(item[0], "dp", axis=0, tiled=True)
            for item in (attn_out_weight, mlp_in_weight, mlp_out_weight)
        ]
    positions = group_pos * row_count + jnp.arange(row_count)
    local_tables = angles(positions, local_log_base)
    global_tables = angles(positions, global_log_base)

    rows = micro_count * row_count
    pairs = rows * width // (row_count * LANES)
    in_0 = tokens_in.reshape(rows, width)
    extra_rows = -(-(2 + micro_count * runs) // 8) * 8
    extra, normed_0, q_0, kv_0 = on_core(
        local_project_body,
        [
            ((extra_rows, width), F32),
            ((rows, width), BF),
            ((rows, width), BF),
            ((rows, 2 * width), BF),
        ],
        (first, in_0, local_tables),
    )
    gain_attn, gain_mlp = extra[:1], extra[1:2]
    all_ids = extra[2 : 2 + micro_count * runs].reshape(micro_count, runs, count, shard)
    all_ids = lax.dynamic_slice_in_dim(all_ids, replica - group_pos, GROUP, 2)
    all_ids = all_ids.swapaxes(1, 2).reshape(micro_count, GROUP, runs * shard)[..., :row_count]
    segments = all_ids.reshape(micro_count, GROUP * row_count).astype(jnp.int32)

    key_pos = positions[0] - row_count + jnp.arange(3 * row_count)
    around = jnp.pad(segments, ((0, 0), (row_count, row_count)), constant_values=-1)
    key_seg = lax.dynamic_slice_in_dim(around, group_pos * row_count, 3 * row_count, 1)
    visible = (key_seg[:, :, None] == segment_ids[:, None, :]) & (
        jnp.abs(positions[None, :] - key_pos[:, None]) <= HALF_WIN
    )[None]
    bias = jnp.tile(jnp.where(visible, 0.0, masked_score), (1, 1, 2))

    own_seg = lax.dynamic_index_in_dim(segments, group_pos // 8, 0, keepdims=False)
    halves = own_seg.reshape(GROUP, 2, row_count // 2)
    mine = lax.dynamic_index_in_dim(halves, group_pos % 2, 1, keepdims=False).reshape(-1)
    theirs = lax.dynamic_index_in_dim(halves, 1 - group_pos % 2, 1, keepdims=False).reshape(-1)
    shared_seg = jnp.concatenate([mine, theirs])[:, None]
    own_seg = own_seg[:, None]

    up_pairs, down_pairs = neighbours(count, 1), neighbours(count, -1)
    around_0 = (
        lax.ppermute(kv_0, "dp", up_pairs),
        kv_0,
        lax.ppermute(kv_0, "dp", down_pairs),
    )
    att_0, total_0 = on_core(
        local_forward_body,
        [((rows, width), BF), ((pairs, 1, LANES), F32)],
        (q_0, *around_0, bias),
    )
    kept_0, state_0, *out_0 = on_core(
        local_middle_body,
        [((rows, width + hidden), BF), ((rows, width + inner), F32)]
        + [((row_count, width), BF)] * micro_count,
        (*others, in_0, att_0, gain_mlp),
        [pltpu.VMEM((hidden, width), BF)],
    )

    in_1 = to_other_section(out_0, 1)
    fold = row_count * 3 // 4
    half = row_count // 2
    normed_1, sent = on_core(
        global_project_body,
        [((rows, width), BF), ((GROUP, 3 * fold, LANES), BF)],
        (first, *in_1, gain_attn, global_tables),
    )
    got = exchange(sent, count)
    beside = jnp.concatenate(
        [got[:, row_count : row_count + half], got[:, 3 * fold - half :]], 1
    )
    beside = partner(beside, 1, count)
    keys = GROUP * row_count
    tiles = keys * 3 // 2 // TILE
    head_scratch = [
        pltpu.VMEM((keys * 3 // 2, LANES), BF),
        pltpu.VMEM((2, keys, LANES), BF),
        pltpu.VMEM((2, keys, LANES), BF),
        pltpu.VMEM((2, LANES, keys), BF),
    ]
    folded, total_1 = on_core(
        global_forward_body,
        [((GROUP, fold, LANES), BF), ((tiles, 1, TILE), F32)],
        (got, beside, own_seg, shared_seg),
        head_scratch + [pltpu.VMEM((keys * 3 // 2, LANES), F32)],
    )
    folded = exchange(folded, count)

    up_1 = out_grad.reshape(rows, width)
    kept_1, gain_mlp_1, d_mid_1, sent = on_core(
        global_middle_body,
        [
            ((rows, 4 * width + hidden + inner), BF),
            ((1, width), F32),
            ((rows, width), F32),
            ((GROUP, fold, LANES), BF),
        ],
        (*others, folded, *in_1, up_1, gain_mlp),
        [pltpu.VMEM((hidden, width), BF)],
    )
    d_folded = exchange(sent, count)
    sources = (normed_0, normed_1, att_0, kept_0, kept_1)
    cut = 2 * width
    spans = (
        ((0, 0, width), (1, 0, width)),
        ((2, 0, width), (4, width, cut)),
        ((3, 0, width), (4, cut, cut + width)),
        ((3, width, width + hidden), (4, cut + width, cut + width + hidden)),
    )
    left_total = 3 * shard_total + hidden_total
    if count == GROUP:
        (left,) = on_core(
            functools.partial(left_body, spans),
            [((4, 4, left_total, rows), BF)],
            (lower_flag, group_pos[None], *sources),
            (),
            [pltpu.SMEM] * 2 + [pltpu.VMEM] * len(sources),
        )
        left, d_folded = lax.optimization_barrier((left, d_folded))
    else:
        left = [
            plane_rows(
                jnp.where(lower, *(sources[i][:, start:end] for i, start, end in span))
                .T.reshape(count, -1, rows),
                group_pos,
                count,
            )
            for span in spans
        ]
        left = [jnp.concatenate([i.reshape(4, -1, rows) for i in items], 1) for items in zip(*left)]
    sent, to_beside = on_core(
        global_backward_body,
        [((GROUP, 3 * fold, LANES), BF), ((GROUP, 2 * half, LANES), BF)],
        (got, beside, own_seg, shared_seg, total_1, d_folded),
        head_scratch
        + [
            pltpu.VMEM((keys * 3 // 2, LANES), BF),
            pltpu.VMEM((keys * 3 // 2, LANES), F32),
            pltpu.VMEM((2, keys, LANES), F32),
            pltpu.VMEM((2, keys, LANES), F32),
        ],
    )
    back = partner(to_beside, 1, count)
    gap = 3 * fold - half - row_count - half
    back = jnp.concatenate(
        [
            jnp.zeros((GROUP, row_count, LANES), BF),
            back[:, :half],
            jnp.zeros((GROUP, gap, LANES), BF),
            back[:, half:],
        ],
        1,
    )
    sent = (sent.astype(F32) + back.astype(F32)).astype(BF)
    if count == GROUP:
        left, sent = lax.optimization_barrier((left, sent))
        left = [left[0]] + [partner(left[apart], apart, count) for apart in range(1, 4)]
    got = exchange(sent, count)
    left, got = lax.optimization_barrier((left, got))

    d_proj_1, gain_attn_1, *grad_1 = on_core(
        global_finish_body,
        [((rows, 3 * width), BF), ((1, width), F32)] + [((row_count, width), BF)] * micro_count,
        (first, got, d_mid_1, *in_1, gain_attn, global_tables),
    )

    up_0 = to_other_section(grad_1, -1)
    d_mlp = jnp.concatenate(
        [jnp.where(lower, a, up_1[i * row_count :][:row_count]) for i, a in enumerate(up_0)]
    )
    across_mlp = partner(d_mlp, 2, count)
    gain_mlp_0, d_mid_0, d_att_0, right = on_core(
        local_back_middle_body,
        [
            ((1, width), F32),
            ((rows, width), F32),
            ((rows, width), BF),
            ((rows, inner + width), BF),
        ],
        (*others, lower_flag, *up_0, state_0, gain_mlp, kept_1),
        [pltpu.VMEM((hidden, width), BF)],
        [pltpu.VMEM] * len(others) + [pltpu.SMEM] + [pltpu.VMEM] * 5,
    )
    d_att_0, right, across_mlp = lax.optimization_barrier((d_att_0, right, across_mlp))
    across = [partner(right, 2, count)]
    d_mlp = [d_mlp, partner(d_mlp, 1, count), across_mlp, partner(across_mlp, 1, count)]
    out_near, out_far = first_hop(
        on_core(
            functools.partial(early_body, [(0, (3 * shard_total, left_total), (0, width))], 4),
            three_parts((hidden_total, width)),
            (*d_mlp, *left),
        ),
        count,
    )
    dq_0, d_own, d_before, d_after = on_core(
        local_backward_body,
        [
            ((rows, width), BF),
            ((rows, 2 * width), F32),
            ((rows, 2 * width), BF),
            ((rows, 2 * width), BF),
        ],
        (q_0, *around_0, bias, total_0, d_att_0, local_tables),
    )
    from_after = lax.ppermute(d_before, "dp", down_pairs)
    from_before = lax.ppermute(d_after, "dp", up_pairs)
    from_after, out_far = lax.optimization_barrier((from_after, out_far))
    d_proj, grad_0, gain_attn_sum = on_core(
        local_finish_body,
        [
            ((rows + EXTRA, 3 * width), BF),
            ((rows, width), BF),
            ((1, width), F32),
        ],
        (
            lower_flag, first, dq_0, d_own, from_after, from_before, local_tables, d_mid_0, in_0, gain_attn,
            gain_mlp_0, d_proj_1, gain_attn_1, gain_mlp_1,
        ),
        [pltpu.VMEM((1, width), F32)],
        [pltpu.SMEM] + [pltpu.VMEM] * 13,
    )
    across_chunks = [partner(d_proj, 2, count)]
    across, right, _ = lax.optimization_barrier((across, right, d_proj))
    right = [right, partner(right, 1, count)] + across
    right += [partner(item, 1, count) for item in across]
    in_rows, attn_rows = shard_total * (inner // width), shard_total
    early_rows = in_rows + attn_rows
    terms = [
        (0, (2 * shard_total, 3 * shard_total), (0, inner)),
        (0, (shard_total, 2 * shard_total), (inner, inner + width)),
    ]
    near, far = first_hop(
        on_core(
            functools.partial(early_body, terms, len(right)),
            three_parts((early_rows, width)),
            (*right, *left),
        ),
        count,
    )
    far = jnp.concatenate([far, out_far])
    across_chunks, d_proj, _ = lax.optimization_barrier((across_chunks, d_proj, far))
    far = partner(far, 8, count)
    right = [d_proj, partner(d_proj, 1, count)] + across_chunks
    right += [partner(item, 1, count) for item in across_chunks]
    late_in = (group_pos[None], *right, *left)
    late = on_core(
        functools.partial(late_body, (0, shard_total)),
        three_parts((shard_total, 3 * width + LANES)),
        late_in,
        [pltpu.VMEM((width, LANES), F32)],
        [pltpu.SMEM] + [pltpu.VMEM] * (len(late_in) - 1),
    )
    far, _ = lax.optimization_barrier((far, late[0]))
    early = near + far[:early_rows].astype(F32)
    mlp_out_share = out_near + far[early_rows:].astype(F32)
    late = second_hop(*first_hop(late, count), count)
    parts = [early[p * shard_total : (p + 1) * shard_total] for p in range(inner // width)]
    in_share = jnp.concatenate(parts, 1)
    attn_share = early[in_rows : in_rows + attn_rows]
    gain_columns = late[:, 3 * width :]
    qkv_share, in_share, mlp_out_share, attn_share, gain_columns = (
        over_groups(item, count)
        for item in (late[:, : 3 * width], in_share, mlp_out_share, attn_share, gain_columns)
    )
    if count == GROUP:
        gains = jnp.stack([gain_columns[:, 0], gain_columns[:, 2]])
    else:
        gain_mlp_sum = jnp.where(lower, gain_mlp_0, gain_mlp_1)
        gains = lax.psum(jnp.concatenate([gain_attn_sum, gain_mlp_sum]), "dp")
        gains = lax.dynamic_slice_in_dim(gains, replica * shard, shard, 1)

    return (
        jnp.where(lower, jnp.concatenate(out_0), kept_1[:, :width]).reshape(1, micro_count, row_count, width),
        jnp.where(lower, grad_0, jnp.concatenate(grad_1)).reshape(1, micro_count, row_count, width),
        qkv_share[None],
        attn_share[None],
        in_share[None],
        mlp_out_share[None],
        gains[:1],
        gains[1:],
    )


def solution(mesh):
    in_specs = (
        P(None, "dp", None),
        P(None, "dp"),
        P(None, "dp", None),
        P("section", "dp", None),
        P("section", "dp", None),
        P("section", "dp", None),
        P("section", "dp", None),
        P("section", "dp"),
        P("section", "dp"),
    )
    out_specs = (
        P("section", None, "dp", None),
        P("section", None, "dp", None),
        P("section", "dp", None),
        P("section", "dp", None),
        P("section", "dp", None),
        P("section", "dp", None),
        P("section", "dp"),
        P("section", "dp"),
    )
    return jax.shard_map(
        on_device, mesh=mesh, in_specs=in_specs, out_specs=out_specs, check_vma=False
    )
```

```python
import functools
import math

import jax
import jax.numpy as jnp
from jax import lax
from jax.experimental import pallas as pl
from jax.experimental.pallas import tpu as pltpu
from jax.sharding import PartitionSpec as P

HEAD_DIM = 64
GROUP = 16
HALF_WIN = 64
EXTRA = 16
LANES = 128
TILE = 256

local_log_base = math.log(10000.0)
global_log_base = math.log(160000.0)
masked_score = -1e30
SCALE = 1.0 / math.sqrt(HEAD_DIM)
BF = jnp.bfloat16
F32 = jnp.float32


def dot(left, right):
    return jnp.dot(left, right, preferred_element_type=F32)


def dot_bt(left, right):
    return lax.dot_general(left, right, (((1,), (1,)), ((), ())), preferred_element_type=F32)


def dot_at(left, right):
    return lax.dot_general(left, right, (((0,), (0,)), ((), ())), preferred_element_type=F32)


def moments(values):
    center = values - jnp.mean(values, -1, keepdims=True)
    scale = lax.rsqrt(jnp.mean(center * center, -1, keepdims=True) + 1e-05)
    return center * scale, scale


def norm_back(grad_out, gain_row, xhat, scale):
    scaled = grad_out * gain_row
    mean_grad = jnp.mean(scaled, -1, keepdims=True)
    mean_dot = jnp.mean(scaled * xhat, -1, keepdims=True)
    return (scaled - mean_grad - xhat * mean_dot) * scale


def angles(positions, log_base):
    half_dim = HEAD_DIM // 2
    fraction = (2 * jnp.arange(half_dim)).astype(F32) / HEAD_DIM
    inverse = jnp.exp(-fraction * log_base)
    table = positions.astype(F32)[:, None] * inverse[None, :]
    cosine, sine = jnp.cos(table), jnp.sin(table)
    none = jnp.zeros_like(sine)
    cosine = jnp.concatenate([cosine, cosine], 1)
    to_first = jnp.concatenate([-sine, none], 1)
    to_second = jnp.concatenate([none, sine], 1)
    return jnp.tile(jnp.stack([cosine, to_first, to_second]), (1, 2, 2))


def on_core(body, outs, args, scratch=(), spaces=None, out_spaces=None):
    return pl.pallas_call(
        body,
        out_shape=[jax.ShapeDtypeStruct(shape, dtype) for shape, dtype in outs],
        in_specs=[
            pl.BlockSpec(memory_space=space) for space in spaces or [pltpu.VMEM] * len(args)
        ],
        out_specs=[
            pl.BlockSpec(memory_space=space) for space in out_spaces or [pltpu.VMEM] * len(outs)
        ],
        scratch_shapes=scratch,
        cost_estimate=pl.CostEstimate(
            flops=2**10, bytes_accessed=2**10, transcendentals=0
        ),
        compiler_params=pltpu.CompilerParams(
            vmem_limit_bytes=(60 if body in LARGE else 48) * 2**20
        ),
    )(*args)


def low_lanes():
    return lax.broadcasted_iota(jnp.int32, (1, LANES), 1) < HEAD_DIM


def swap(chunk):
    return pltpu.roll(chunk, HEAD_DIM, 1)


def chunks_of(rows):
    return [rows[:, c : c + LANES] for c in range(0, rows.shape[1], LANES)]


def rotate(chunk, tables):
    cosine, to_first, to_second = tables
    quarter = HEAD_DIM // 2
    return (
        chunk * cosine
        + pltpu.roll(chunk, LANES - quarter, 1) * to_first
        + pltpu.roll(chunk, quarter, 1) * to_second
    )


def unrotate(chunk, tables):
    cosine, to_first, to_second = tables
    quarter = HEAD_DIM // 2
    return (
        chunk * cosine
        - pltpu.roll(chunk, LANES - quarter, 1) * to_first
        - pltpu.roll(chunk, quarter, 1) * to_second
    )


def low_and_high(chunks):
    swapped = [swap(chunk) for chunk in chunks]
    low = [(swapped if h % 2 else chunks)[h // 2] for h in range(2 * len(chunks))]
    high = [(chunks if h % 2 else swapped)[h // 2] for h in range(2 * len(chunks))]
    return low, high


def targets():
    for d in range(GROUP):
        micro, chip, half = d // 8, d % 8 // 2, d % 2
        yield d, micro, 3 * chip + 2 * half, 3 * chip + 1, half


def pack_folded(chunks, ref, base):
    low, high = low_and_high(chunks)
    first = low_lanes()
    rows = chunks[0].shape[0] // 2
    half, fold = rows // 2, rows * 3 // 4
    for d, micro, own, shared, side in targets():
        start = micro * rows
        part = start + side * half
        upper = jnp.concatenate(
            [high[own][start + fold : start + rows], high[shared][part : part + half]], 0
        )
        ref[d, base : base + fold] = jnp.where(
            first, low[own][start : start + fold], upper
        ).astype(BF)


def pack_pairs(lefts, rights, ref):
    low, high = low_and_high(lefts)[0], low_and_high(rights)[1]
    first = low_lanes()
    rows = lefts[0].shape[0] // 2
    half = rows // 2
    for d, micro, own, shared, side in targets():
        start = micro * rows
        part = start + side * half
        ref[d, 0:rows] = jnp.where(
            first, low[own][start : start + rows], high[own][start : start + rows]
        ).astype(BF)
        ref[d, rows : rows + half] = jnp.where(
            first, low[shared][part : part + half], high[shared][part : part + half]
        ).astype(BF)


def unpack_folded(ref, base, rows):
    first = low_lanes()
    fold = rows * 3 // 4
    low, high = {}, {}
    shared_parts = {}
    for d, micro, own, shared, side in targets():
        block = ref[d, base : base + fold].astype(F32)
        mine = jnp.concatenate([block, swap(block[: rows - fold])], 0)
        if own % 2:
            high[micro, own] = swap(mine)
        else:
            low[micro, own] = mine
        shared_parts[micro, shared, side] = block[rows - fold :]
        if side:
            both = jnp.concatenate([shared_parts[micro, shared, 0], block[rows - fold :]], 0)
            if shared % 2:
                high[micro, shared] = both
            else:
                low[micro, shared] = swap(both)
    heads = GROUP // 4 * 3
    return [
        jnp.concatenate(
            [jnp.where(first, low[m, h], high[m, h + 1]) for m in range(2)], 0
        )
        for h in range(0, heads, 2)
    ]


def unpack_pairs(ref, rows):
    first = low_lanes()
    half = rows // 2
    pairs = {}
    parts = {}
    for d, micro, own, shared, side in targets():
        pairs[micro, own] = ref[d, 0:rows].astype(F32)
        parts[side] = ref[d, rows : rows + half].astype(F32)
        if side:
            pairs[micro, shared] = jnp.concatenate([parts[0], parts[1]], 0)
    heads = GROUP // 4 * 3
    lefts, rights = [], []
    for h in range(0, heads, 2):
        even, odd = [pairs[m, h] for m in range(2)], [pairs[m, h + 1] for m in range(2)]
        lefts.append(
            jnp.concatenate([jnp.where(first, a, swap(b)) for a, b in zip(even, odd)], 0)
        )
        rights.append(
            jnp.concatenate([jnp.where(first, swap(a), b) for a, b in zip(even, odd)], 0)
        )
    return lefts, rights


class Weights:
    def __init__(self, sources, mlp_out):
        self.sources = sources
        self.mlp_out = sources[-1]
        if len(sources) == 1:
            self.mlp_out = mlp_out
            unpack_rows(sources[0], mlp_out)

    def get(self, which):
        if which == 2:
            return self.mlp_out[...]
        if len(self.sources) > 1:
            return self.sources[which][...]
        (wide,) = self.sources
        width = wide.shape[0]
        inner = 2 * self.mlp_out.shape[0]
        return wide[:, width : width + inner] if which else wide[:, :width]


def first_block(pair):
    return -(-pair // 32) * 16


def packed_pieces(shard, rows, width):
    yield 0, shard, 0, width, 0, 0
    rest = rows - shard
    side = width // 3
    yield 0, rest, width, 2 * side, shard, 0
    yield rest, 16, width, side, shard, 2 * side
    yield rest, 16, width + side, side, shard + 16, 2 * side


def unpack_rows(wide, mlp_out):
    hidden, width = mlp_out.shape
    shard = wide.shape[0] // GROUP
    start = wide.shape[1] - width - 2 * (width // 3)
    pair = 2 * hidden // GROUP
    upper = first_block(pair)
    for d in range(GROUP):
        low = d // 2 * pair + d % 2 * upper
        have = pair - upper if d % 2 else upper
        for row, rows, column, columns, to_row, to_column in packed_pieces(shard, upper, width):
            rows = min(rows, have - to_row)
            if rows > 0:
                mlp_out[low + to_row : low + to_row + rows, to_column : to_column + columns] = wide[
                    d * shard + row : d * shard + row + rows, start + column : start + column + columns
                ]


def stack_body(odd_ref, attn_ref, mlp_in_ref, own_ref, beside_ref, out_ref):
    shard, width = attn_ref.shape
    inner = mlp_in_ref.shape[1]
    out_ref[:, :width] = attn_ref[...]
    out_ref[:, width : width + inner] = mlp_in_ref[...]
    own, beside = own_ref[...].astype(F32), beside_ref[...].astype(F32)
    moved = beside.shape[0]
    even = jnp.concatenate([own, beside], 0)
    odd = jnp.concatenate([own[moved:], beside, beside], 0)
    block = jnp.where(odd_ref[0] == 1, odd, even).astype(BF)
    start = width + inner
    for row, rows, column, columns, from_row, from_column in packed_pieces(
        shard, block.shape[0], width
    ):
        out_ref[row : row + rows, start + column : start + column + columns] = block[
            from_row : from_row + rows, from_column : from_column + columns
        ]


def mlp_forward(layer_in, attended, gain, weights):
    middle = layer_in + dot(attended, weights.get(0))
    xhat, _ = moments(middle)
    normed = (xhat * gain).astype(BF)
    gate_up = dot(normed, weights.get(1))
    half = gate_up.shape[1] // 2
    gate, up = gate_up[:, :half], gate_up[:, half:]
    cdf = 0.5 * (1.0 + lax.erf(gate * math.sqrt(0.5)))
    mixed = (gate * cdf * up).astype(BF)
    result = (middle + dot(mixed, weights.get(2))).astype(BF)
    return middle, normed, gate, up, mixed, result


def mlp_backward(upstream, middle, gate, up, gain, weights):
    d_mixed = dot_bt(upstream, weights.get(2))
    cdf = 0.5 * (1.0 + lax.erf(gate * math.sqrt(0.5)))
    density = jnp.exp(-0.5 * gate * gate) * (1.0 / math.sqrt(2.0 * math.pi))
    d_gate = d_mixed * up * (cdf + gate * density)
    d_up = d_mixed * gate * cdf
    d_gate_up = jnp.concatenate([d_gate.astype(BF), d_up.astype(BF)], 1)
    d_normed = dot_bt(d_gate_up, weights.get(1))
    xhat, scale = moments(middle)
    gain_grad = jnp.sum(d_normed * xhat, 0, keepdims=True)
    d_middle = upstream.astype(F32) + norm_back(d_normed, gain, xhat, scale)
    d_attn = d_middle.astype(BF)
    d_attended = dot_bt(d_attn, weights.get(0))
    return d_gate_up, gain_grad, d_middle, d_attn, d_attended


def project(xhat, gain, first_ref, table_ref, normed_ref):
    width = xhat.shape[1]
    normed = (xhat * gain).astype(BF)
    normed_ref[...] = normed
    tables = [table_ref[i] for i in range(3)]
    results = [dot(normed, first_ref[:, c * width : (c + 1) * width]) for c in range(3)]
    queries, keys, values = chunks_of(results[0]), chunks_of(results[1]), results[2]
    return [rotate(c, tables) for c in queries], [rotate(c, tables) for c in keys], values


def input_backward(d_middle, d_projected, x, gain_ref, first_ref, gain_out_ref):
    d_normed = dot_bt(d_projected, first_ref[:, : d_projected.shape[1]])
    xhat, scale = moments(x)
    gain_out_ref[...] = jnp.sum(d_normed * xhat, 0, keepdims=True)
    return (d_middle + norm_back(d_normed, gain_ref[...], xhat, scale)).astype(BF)


def joined(refs):
    return jnp.concatenate([ref[...] for ref in refs], 0)


def store_chunks(refs, rows):
    size = rows.shape[0] // len(refs)
    for i, ref in enumerate(refs):
        ref[...] = rows[i * size : (i + 1) * size]


def message_body(w_ref, attn_ref, mlp_ref, ids_ref, out_ref, rows_scr, ids_scr):
    shard, columns = w_ref.shape
    micro_count, row_count = ids_ref.shape
    out_ref[:, :columns] = w_ref[...]
    rows_scr[...] = jnp.zeros_like(rows_scr)
    ids_scr[...] = jnp.zeros_like(ids_scr)
    rows_scr[0:1, :shard] = attn_ref[...].astype(F32)
    rows_scr[1:2, :shard] = mlp_ref[...].astype(F32)
    ids_scr[:micro_count, :row_count] = ids_ref[...].astype(F32)
    runs = -(-row_count // shard)
    for run in range(runs):
        turned = ids_scr[...]
        if run:
            turned = pltpu.roll(turned, LANES - run * shard, 1)
        for micro in range(micro_count):
            row = 2 + micro * runs + run
            rows_scr[row : row + 1] = turned[micro : micro + 1]
    out_ref[:, columns:] = rows_scr[...].T[:shard].astype(BF)


def local_project_body(first_ref, x_ref, table_ref, extra_ref, normed_ref, q_ref, kv_ref):
    xhat, _ = moments(x_ref[...].astype(F32))
    extra = first_ref[:, first_ref.shape[1] - LANES :].astype(F32).T
    extra_ref[...] = extra[: extra_ref.shape[0]]
    queries, keys, values = project(xhat, extra[:1], first_ref, table_ref, normed_ref)
    width = values.shape[1]
    for j, (q, k) in enumerate(zip(queries, keys)):
        q_ref[:, LANES * j : LANES * (j + 1)] = q.astype(BF)
        kv_ref[:, LANES * j : LANES * (j + 1)] = k.astype(BF)
    kv_ref[:, width:] = values.astype(BF)


def two_heads(chunk):
    first = low_lanes()
    wide = chunk.astype(F32)
    return jnp.concatenate([jnp.where(first, wide, 0.0), jnp.where(first, 0.0, wide)], 0)


def pick_heads(rows):
    half = rows.shape[0] // 2
    return jnp.where(low_lanes(), rows[:half], rows[half:])


def local_parts(q_ref, before_ref, own_ref, after_ref):
    rows = q_ref.shape[0] // 2
    width = q_ref.shape[1]
    for micro in range(2):
        for j in range(width // LANES):
            here = slice(micro * rows, (micro + 1) * rows)
            lanes = slice(LANES * j, LANES * (j + 1))
            more = slice(width + LANES * j, width + LANES * (j + 1))
            keys, values = (
                jnp.concatenate([ref[here, part] for ref in (before_ref, own_ref, after_ref)], 0)
                for part in (lanes, more)
            )
            queries = (two_heads(q_ref[here, lanes]) * SCALE).astype(BF)
            yield micro * (width // LANES) + j, micro, here, lanes, more, queries, keys, values


def local_forward_body(q_ref, before_ref, own_ref, after_ref, bias_ref, att_ref, total_ref):
    parts = local_parts(q_ref, before_ref, own_ref, after_ref)
    for index, micro, here, lanes, _, queries, keys, values in parts:
        scores = dot_bt(keys, queries) + bias_ref[micro]
        peak = jnp.max(scores, 0, keepdims=True)
        weights = jnp.exp(scores - peak)
        total = jnp.sum(weights, 0, keepdims=True)
        total_ref[index] = peak + jnp.log(total)
        probs = (weights * (1.0 / total)).astype(BF)
        att_ref[here, lanes] = pick_heads(dot_at(probs, values)).astype(BF)


def local_backward_body(
    q_ref, before_ref, own_ref, after_ref, bias_ref, total_ref, d_ref, table_ref,
    dq_ref, d_own_ref, d_before_ref, d_after_ref,
):
    tables = [table_ref[i] for i in range(3)]
    parts = local_parts(q_ref, before_ref, own_ref, after_ref)
    rows = q_ref.shape[0] // 2
    for index, micro, here, lanes, more, queries, keys, values in parts:
        d_out = two_heads(d_ref[here, lanes]).astype(BF)
        probs = jnp.exp(dot_bt(keys, queries) + bias_ref[micro] - total_ref[index])
        d_probs = dot_bt(values, d_out)
        product = probs * d_probs
        delta = jnp.sum(product, 0, keepdims=True)
        d_scores = (product - probs * delta).astype(BF)
        d_queries = pick_heads(dot_at(d_scores, keys)) * SCALE
        local_tables = [table[here] for table in tables]
        dq_ref[here, lanes] = unrotate(d_queries, local_tables).astype(BF)
        for part, grads in ((lanes, dot(d_scores, queries)), (more, dot(probs.astype(BF), d_out))):
            d_before_ref[here, part] = grads[:rows].astype(BF)
            d_own_ref[here, part] = grads[rows : 2 * rows]
            d_after_ref[here, part] = grads[2 * rows :].astype(BF)


def local_finish_body(
    lower_ref, first_ref, dq_ref, own_ref, low_ref, high_ref, table_ref, d_middle_ref, x_ref, gain_ref,
    gain_mlp_ref, other_ref, other_attn_ref, other_mlp_ref, out_ref, grad_ref, gain_attn_ref,
    gain_scr,
):
    rows, width = dq_ref.shape

    @pl.when(lower_ref[0] == 1)
    def _():
        tables = [table_ref[i] for i in range(3)]
        total = own_ref[...] + low_ref[...].astype(F32) + high_ref[...].astype(F32)
        out_ref[:rows, :width] = dq_ref[...]
        for j, chunk in enumerate(chunks_of(total[:, :width])):
            start = width + LANES * j
            out_ref[:rows, start : start + LANES] = unrotate(chunk, tables).astype(BF)
        out_ref[:rows, 2 * width :] = total[:, width:].astype(BF)
        grad_ref[...] = input_backward(
            d_middle_ref[...], out_ref[:rows], x_ref[...].astype(F32), gain_ref, first_ref, gain_scr
        )

    @pl.when(lower_ref[0] == 0)
    def _():
        out_ref[:rows] = other_ref[...]
        grad_ref[...] = jnp.zeros_like(grad_ref)
        gain_scr[...] = other_attn_ref[...]

    gain_attn_ref[...] = gain_scr[...]
    gain_mlp = jnp.where(lower_ref[0] == 1, gain_mlp_ref[...], other_mlp_ref[...])
    index = lax.broadcasted_iota(jnp.int32, (EXTRA, width), 0)
    tail = jnp.zeros((EXTRA, width), F32)
    for row, gain in ((0, gain_scr[...]), (2, gain_mlp)):
        high = gain.astype(BF).astype(F32)
        tail = jnp.where(index == row, high, tail)
        tail = jnp.where(index == row + 1, gain - high, tail)
    out_ref[rows:] = jnp.zeros((EXTRA, out_ref.shape[1]), BF)
    out_ref[rows:, :width] = tail.astype(BF)


def local_middle_body(*refs):
    sources, refs = refs[:-8], refs[-8:]
    x_ref, att_ref, gain_ref, kept_ref, state_ref = refs[:5]
    weights = Weights(sources, refs[7])
    middle, normed, gate, up, mixed, result = mlp_forward(
        x_ref[...].astype(F32), att_ref[...], gain_ref[...], weights
    )
    store_chunks(refs[5:7], result)
    width, half = middle.shape[1], gate.shape[1]
    kept_ref[:, :width] = normed
    kept_ref[:, width:] = mixed
    state_ref[:, :width] = middle
    state_ref[:, width : width + half] = gate
    state_ref[:, width + half :] = up


def local_back_middle_body(*refs):
    sources, refs = refs[:-11], refs[-11:]
    lower_ref, low_ref, high_ref, state_ref, gain_ref, other_ref = refs[:6]
    gain_out_ref, d_middle_ref, d_att_ref, right_ref = refs[6:10]
    weights = Weights(sources, refs[10])
    width = low_ref.shape[1]
    half = (state_ref.shape[1] - width) // 2
    upstream = joined([low_ref, high_ref])
    d_gate_up, gain_grad, d_middle, d_attn, d_attended = mlp_backward(
        upstream, state_ref[:, :width], state_ref[:, width : width + half], state_ref[:, width + half :],
        gain_ref[...], weights,
    )
    gain_out_ref[...] = gain_grad
    d_middle_ref[...] = d_middle
    d_att_ref[...] = d_attended.astype(BF)

    @pl.when(lower_ref[0] == 1)
    def _():
        right_ref[:, : 2 * half] = d_gate_up
        right_ref[:, 2 * half :] = d_attn

    @pl.when(lower_ref[0] == 0)
    def _():
        right_ref[...] = other_ref[:, other_ref.shape[1] - right_ref.shape[1] :]


def global_project_body(first_ref, low_ref, high_ref, gain_ref, table_ref, normed_ref, sent_ref):
    xhat, _ = moments(joined([low_ref, high_ref]).astype(F32))
    queries, keys, values = project(xhat, gain_ref[...], first_ref, table_ref, normed_ref)
    pack_pairs(queries, keys, sent_ref)
    pack_folded(chunks_of(values), sent_ref, sent_ref.shape[1] * 2 // 3)


def flat(blocks):
    return blocks.reshape(-1, LANES)


def own_unfolded(ref, base, rows):
    fold = rows * 3 // 4
    block = ref[:, base : base + fold].astype(F32)
    rest = swap(flat(block[:, : rows - fold])).reshape(GROUP, rows - fold, LANES)
    return flat(jnp.concatenate([block, rest], 1))


def shared_unfolded(ref, start, rows):
    return swap(flat(ref[:, start : start + rows // 2].astype(F32)))


def fill_heads(got_ref, other_ref, own_seg_ref, shared_seg_ref, q_scr, k_scr, v_scr):
    rows = got_ref.shape[1] * 4 // 9
    half = rows // 2
    first = low_lanes()
    lane = lax.broadcasted_iota(jnp.int32, (1, LANES), 1) - HEAD_DIM
    own = flat(got_ref[:, 0:rows].astype(F32))
    shared = flat(got_ref[:, rows : rows + half].astype(F32))
    other = flat(other_ref[:, 0:half].astype(F32))
    count = own.shape[0]
    own_hit = lane == own_seg_ref[...]
    shared_hit = lane == shared_seg_ref[...]
    both = jnp.concatenate([shared, other], 0)
    for start, pairs, hit in (
        (0, own, own_hit),
        (count, shared, shared_hit[: count // 2]),
    ):
        marked = jnp.where(hit, 1.0, 0.0)
        q_scr[start : start + pairs.shape[0]] = jnp.where(first, pairs * SCALE, marked).astype(BF)
    for unit, pairs, hit in ((0, own, own_hit), (1, both, shared_hit)):
        marked = jnp.where(hit, 0.0, masked_score)
        k_scr[unit] = jnp.where(first, swap(pairs), marked).astype(BF)
    base = rows + half
    v_scr[0] = jnp.where(first, own_unfolded(got_ref, base, rows), 0.0).astype(BF)
    start = base + rows - rows * 3 // 4
    shared_v = jnp.concatenate(
        [shared_unfolded(got_ref, start, rows), shared_unfolded(other_ref, half, rows)], 0
    )
    v_scr[1] = jnp.where(first, shared_v, 0.0).astype(BF)


def fold_out(own, shared, rows, ref, base):
    fold = rows * 3 // 4
    blocks = own.reshape(GROUP, rows, LANES)
    swapped = swap(own).reshape(GROUP, rows, LANES)
    upper = jnp.concatenate(
        [swapped[:, fold:], swap(shared).reshape(GROUP, rows // 2, LANES)], 1
    )
    ref[:, base : base + fold] = jnp.where(low_lanes(), blocks[:, :fold], upper).astype(BF)


def global_forward_body(
    got_ref, other_ref, own_seg_ref, shared_seg_ref, out_ref, total_ref,
    q_scr, k_scr, v_scr, vt_scr, o_scr,
):
    fill_heads(got_ref, other_ref, own_seg_ref, shared_seg_ref, q_scr, k_scr, v_scr)
    for unit in range(2):
        vt_scr[unit] = v_scr[unit].astype(F32).T.astype(BF)
    count = k_scr.shape[1]

    def step(tile, carry):
        unit = tile // (count // TILE)
        rows = pl.ds(pl.multiple_of(tile * TILE, TILE), TILE)
        scores = dot_bt(k_scr[unit], q_scr[rows])
        peak = jnp.max(scores, 0, keepdims=True)
        weights = jnp.exp(scores - peak)
        total = jnp.sum(weights, 0, keepdims=True)
        total_ref[tile] = peak + jnp.log(total)
        out = dot(vt_scr[unit], weights.astype(BF)) * (1.0 / total)
        o_scr[rows] = out.T
        return carry

    lax.fori_loop(0, q_scr.shape[0] // TILE, step, 0)
    rows = got_ref.shape[1] * 4 // 9
    fold_out(o_scr[:count], o_scr[count:], rows, out_ref, 0)


def global_backward_body(
    got_ref, other_ref, own_seg_ref, shared_seg_ref, total_ref, d_ref, sent_ref, to_other_ref,
    q_scr, k_scr, v_scr, kt_scr, d_scr, dq_scr, dk_scr, dv_scr,
):
    fill_heads(got_ref, other_ref, own_seg_ref, shared_seg_ref, q_scr, k_scr, v_scr)
    first = low_lanes()
    rows = got_ref.shape[1] * 4 // 9
    half = rows // 2
    for unit in range(2):
        keys = jnp.where(first, k_scr[unit].astype(F32), 0.0)
        kt_scr[unit] = keys.T.astype(BF)
    count = k_scr.shape[1]
    d_scr[:count] = jnp.where(first, own_unfolded(d_ref, 0, rows), 0.0).astype(BF)
    d_scr[count:] = jnp.where(
        first, shared_unfolded(d_ref, rows - rows * 3 // 4, rows), 0.0
    ).astype(BF)
    dk_scr[...] = jnp.zeros_like(dk_scr)
    dv_scr[...] = jnp.zeros_like(dv_scr)

    def step(tile, carry):
        unit = tile // (count // TILE)
        here = pl.ds(pl.multiple_of(tile * TILE, TILE), TILE)
        queries, d_out = q_scr[here], d_scr[here]
        probs = jnp.exp(dot_bt(k_scr[unit], queries) - total_ref[tile])
        d_probs = dot_bt(v_scr[unit], d_out)
        product = probs * d_probs
        delta = jnp.sum(product, 0, keepdims=True)
        d_scores = (product - probs * delta).astype(BF)
        dv_scr[unit] += dot(probs.astype(BF), d_out)
        dk_scr[unit] += dot(d_scores, queries)
        dq_scr[here] = dot(kt_scr[unit], d_scores).T * SCALE
        return carry

    lax.fori_loop(0, q_scr.shape[0] // TILE, step, 0)
    mine = count // 2
    own = jnp.where(first, dq_scr[:count], swap(dk_scr[0]))
    sent_ref[:, 0:rows] = own.reshape(GROUP, rows, LANES).astype(BF)
    shared_k, shared_v = dk_scr[1], dv_scr[1]
    shared = jnp.where(first, dq_scr[count:], swap(shared_k[:mine]))
    sent_ref[:, rows : rows + half] = shared.reshape(GROUP, half, LANES).astype(BF)
    fold_out(dv_scr[0], shared_v[:mine], rows, sent_ref, rows + half)
    for place, grads in enumerate((shared_k, shared_v)):
        other = jnp.where(first, 0.0, swap(grads[mine:])).reshape(GROUP, half, LANES)
        to_other_ref[:, place * half : (place + 1) * half] = other.astype(BF)


def global_middle_body(*refs):
    sources, refs = refs[:-10], refs[-10:]
    got_ref, low_ref, high_ref, up_ref, gain_ref, kept_ref, gain_out_ref, d_middle_ref, sent_ref = refs[:9]
    weights = Weights(sources, refs[9])
    rows, width = low_ref.shape
    attended = jnp.concatenate([c.astype(BF) for c in unpack_folded(got_ref, 0, rows)], 1)
    gain = gain_ref[...]
    middle, normed, gate, up, mixed, result = mlp_forward(
        joined([low_ref, high_ref]).astype(F32), attended, gain, weights
    )
    d_gate_up, gain_grad, d_middle, d_attn, d_attended = mlp_backward(
        up_ref[...], middle, gate, up, gain, weights
    )
    start = 0
    for part in (result, attended, normed, mixed, d_gate_up, d_attn):
        kept_ref[:, start : start + part.shape[1]] = part
        start += part.shape[1]
    gain_out_ref[...] = gain_grad
    d_middle_ref[...] = d_middle
    pack_folded(chunks_of(d_attended), sent_ref, 0)


def global_finish_body(
    first_ref, got_ref, d_middle_ref, low_ref, high_ref, gain_ref, table_ref,
    d_proj_ref, gain_out_ref, *grad_refs,
):
    tables = [table_ref[i] for i in range(3)]
    x = joined([low_ref, high_ref]).astype(F32)
    rows = low_ref.shape[0]
    d_queries, d_keys = unpack_pairs(got_ref, rows)
    d_values = unpack_folded(got_ref, rows * 3 // 2, rows)
    parts = [unrotate(c, tables).astype(BF) for c in d_queries + d_keys]
    d_projected = jnp.concatenate(parts + [c.astype(BF) for c in d_values], 1)
    d_proj_ref[...] = d_projected
    store_chunks(
        grad_refs,
        input_backward(d_middle_ref[...], d_projected, x, gain_ref, first_ref, gain_out_ref),
    )


LARGE = (
    message_body,
    stack_body,
    local_middle_body,
    global_middle_body,
    global_finish_body,
)


def neighbours(count, step):
    return [
        (i, i + step)
        for i in range(count)
        if 0 <= i + step < count and i // GROUP == (i + step) // GROUP
    ]


def exchange(blocks, count):
    groups = [list(range(s, s + GROUP)) for s in range(0, count, GROUP)]
    return lax.all_to_all(blocks, "dp", 0, 0, axis_index_groups=groups)


def to_other_section(chunks, step):
    pairs = [(0, 1)] if step > 0 else [(1, 0)]
    return [lax.ppermute(rows, "section", pairs) for rows in chunks]


def partner(rows, apart, count):
    return lax.ppermute(rows, "dp", [(i, i ^ apart) for i in range(count)])


def gather_rows(piece, group_pos, count):
    pieces = {0: piece}
    for apart in (4, 8, 12):
        pieces[apart] = partner(piece, apart, count)
    for apart in (0, 4, 8, 12):
        pieces[apart + 2] = partner(pieces[apart], 2, count)
    for apart in range(0, GROUP, 2):
        pieces[apart + 1] = partner(pieces[apart], 1, count)
    whole = jnp.zeros((GROUP,) + piece.shape, piece.dtype)
    for apart, item in pieces.items():
        start = (group_pos ^ apart,) + (0,) * piece.ndim
        whole = lax.dynamic_update_slice(whole, item[None], start)
    if count > GROUP:
        groups = [list(range(s, count, GROUP)) for s in range(GROUP)]
        whole = lax.all_gather(whole, "dp", axis=0, tiled=True, axis_index_groups=groups)
    return whole.reshape(-1, piece.shape[-1]), pieces[2]


def plane_rows(rows, group_pos, count):
    parts = rows.reshape(count // GROUP, 4, 4, *rows.shape[1:])
    place, plane = group_pos % 4, group_pos // 4
    taken = []
    for apart in range(4):
        block = lax.dynamic_index_in_dim(parts, place ^ apart, 2, keepdims=False)
        block = jnp.stack(
            [lax.dynamic_index_in_dim(block, plane ^ z, 1, keepdims=False) for z in range(4)]
        )
        taken.append(partner(block, apart, count) if apart else block)
    return taken


def left_body(spans, lower_ref, place_ref, *refs):
    refs, out_ref = refs[:-1], refs[-1]
    base = 0
    for span in spans:
        first, second = (refs[i][:, start:end].astype(F32) for i, start, end in span)
        turned = jnp.where(lower_ref[0] == 1, first, second).T
        size = turned.shape[0] // GROUP
        for d in range(GROUP):
            side = d % 4 ^ place_ref[0] % 4
            plane = d // 4 ^ place_ref[0] // 4
            out_ref[side, plane, base : base + size] = turned[d * size : (d + 1) * size].astype(BF)
        base += size


def left_rows_of(refs, rows):
    start, end = rows
    parts = [
        jnp.concatenate([ref[p, start:end].astype(F32) for p in range(4)], 0).astype(BF) for ref in refs
    ]
    return jnp.concatenate(parts, 1)


def by_plane(result, base, outs, columns=slice(None)):
    keep, keep_far, send = outs
    rows = result.shape[0] // 4
    half = send.shape[0] // 2
    here = slice(base, base + rows)
    keep[here, columns] = result[:rows]
    keep_far[here, columns] = result[2 * rows : 3 * rows]
    send[here, columns] = result[rows : 2 * rows].astype(BF)
    send[half + base : half + base + rows, columns] = result[3 * rows :].astype(BF)


def early_body(terms, split, *refs):
    refs, outs = refs[:-3], refs[-3:]
    operands, lefts = (refs[:split], refs[split:-4]), refs[-4:]
    width = outs[0].shape[1]
    base = 0
    for which, rows, (start, end) in terms:
        right = jnp.concatenate([ref[:, start:end] for ref in operands[which]], 0)
        result = dot(left_rows_of(lefts, rows), right)
        for column in range(0, end - start, width):
            by_plane(result[:, column : column + width], base, outs)
            base += result.shape[0] // 4


def late_body(rows, place_ref, *refs):
    refs, outs, scr = refs[:-4], refs[-4:-1], refs[-1]
    rights, lefts = refs[:-4], refs[-4:]
    columns = rights[0].shape[1]
    width = columns // 3
    size = outs[0].shape[0]
    tokens = lefts[0].shape[2]
    right = jnp.concatenate([ref[:tokens] for ref in rights], 0)
    by_plane(dot(left_rows_of(lefts, rows), right), 0, outs, slice(0, columns))
    tail = sum(ref[tokens:, :width].astype(F32) for ref in rights)
    both = jnp.concatenate([tail, jnp.zeros((LANES - EXTRA, width), F32)], 0).T
    lane = lax.broadcasted_iota(jnp.int32, (1, LANES), 1)
    lows = pltpu.roll(both, LANES - 1, 1)
    scr[...] = jnp.where(lane % 2 == 0, both + lows, 0.0)
    gains = []
    for plane in range(4):
        d = (place_ref[0] // 4 ^ plane) * 4 + place_ref[0] % 4
        gains.append(scr[pl.ds(pl.multiple_of(d * size, 16), size)])
    by_plane(jnp.concatenate(gains, 0), 0, outs, slice(columns, columns + LANES))


def three_parts(shape):
    return [(shape, F32), (shape, F32), ((2 * shape[0], shape[1]), BF)]


def first_hop(blocks, count):
    keep, keep_far, send = blocks
    got = partner(send, 4, count)
    half = keep.shape[0]
    return keep + got[:half].astype(F32), (keep_far + got[half:].astype(F32)).astype(BF)


def second_hop(near, far, count):
    return near + partner(far, 8, count).astype(F32)


def over_groups(rows, count):
    if count == GROUP:
        return rows
    apart = [list(range(s, count, GROUP)) for s in range(GROUP)]
    rows = rows.reshape(count // GROUP, -1, rows.shape[1])
    return lax.psum_scatter(rows, "dp", scatter_dimension=0, axis_index_groups=apart)


def on_device(
    tokens_in,
    segment_ids,
    out_grad,
    qkv_weight,
    attn_out_weight,
    mlp_in_weight,
    mlp_out_weight,
    attn_gain,
    mlp_gain,
):
    lower = lax.axis_index("section") == 0
    lower_flag = lower.astype(jnp.int32)[None]
    shard_total = qkv_weight.shape[1] * (lax.axis_size("dp") // GROUP)
    hidden_total = mlp_out_weight.shape[1] * (lax.axis_size("dp") // GROUP)
    count = lax.axis_size("dp")
    replica = lax.axis_index("dp")
    group_pos = replica % GROUP
    micro_count, row_count, width = tokens_in.shape
    shard = qkv_weight.shape[1]
    runs = -(-row_count // shard)
    (message,) = on_core(
        message_body,
        [((shard, 3 * width + LANES), BF)],
        (qkv_weight[0], attn_gain, mlp_gain, segment_ids),
        [pltpu.VMEM((LANES, LANES), F32), pltpu.VMEM((8, LANES), F32)],
    )
    first, early_piece = gather_rows(message, group_pos, count)
    inner = mlp_in_weight.shape[2]
    hidden = mlp_out_weight.shape[1] * count
    if count == GROUP:
        moved = first_block(2 * mlp_out_weight.shape[1]) - mlp_out_weight.shape[1]
        beside = partner(mlp_out_weight[0, :moved], 1, count)
        (stacked,) = on_core(
            stack_body,
            [((shard, width + inner + width + 2 * (width // 3)), BF)],
            (
                (replica % 2)[None],
                attn_out_weight[0],
                mlp_in_weight[0],
                mlp_out_weight[0],
                beside,
            ),
            (),
            [pltpu.SMEM] + [pltpu.VMEM] * 4,
        )
        stacked, _ = lax.optimization_barrier((stacked, early_piece))
        others = [lax.all_gather(stacked, "dp", axis=0, tiled=True)]
    else:
        others = [
            lax.all_gather(item[0], "dp", axis=0, tiled=True)
            for item in (attn_out_weight, mlp_in_weight, mlp_out_weight)
        ]
    positions = group_pos * row_count + jnp.arange(row_count)
    local_tables = angles(positions, local_log_base)
    global_tables = angles(positions, global_log_base)

    rows = micro_count * row_count
    pairs = rows * width // (row_count * LANES)
    in_0 = tokens_in.reshape(rows, width)
    extra_rows = -(-(2 + micro_count * runs) // 8) * 8
    extra, normed_0, q_0, kv_0 = on_core(
        local_project_body,
        [
            ((extra_rows, width), F32),
            ((rows, width), BF),
            ((rows, width), BF),
            ((rows, 2 * width), BF),
        ],
        (first, in_0, local_tables),
    )
    gain_attn, gain_mlp = extra[:1], extra[1:2]
    all_ids = extra[2 : 2 + micro_count * runs].reshape(micro_count, runs, count, shard)
    all_ids = lax.dynamic_slice_in_dim(all_ids, replica - group_pos, GROUP, 2)
    all_ids = all_ids.swapaxes(1, 2).reshape(micro_count, GROUP, runs * shard)[..., :row_count]
    segments = all_ids.reshape(micro_count, GROUP * row_count).astype(jnp.int32)

    key_pos = positions[0] - row_count + jnp.arange(3 * row_count)
    around = jnp.pad(segments, ((0, 0), (row_count, row_count)), constant_values=-1)
    key_seg = lax.dynamic_slice_in_dim(around, group_pos * row_count, 3 * row_count, 1)
    visible = (key_seg[:, :, None] == segment_ids[:, None, :]) & (
        jnp.abs(positions[None, :] - key_pos[:, None]) <= HALF_WIN
    )[None]
    bias = jnp.tile(jnp.where(visible, 0.0, masked_score), (1, 1, 2))

    own_seg = lax.dynamic_index_in_dim(segments, group_pos // 8, 0, keepdims=False)
    halves = own_seg.reshape(GROUP, 2, row_count // 2)
    mine = lax.dynamic_index_in_dim(halves, group_pos % 2, 1, keepdims=False).reshape(-1)
    theirs = lax.dynamic_index_in_dim(halves, 1 - group_pos % 2, 1, keepdims=False).reshape(-1)
    shared_seg = jnp.concatenate([mine, theirs])[:, None]
    own_seg = own_seg[:, None]

    up_pairs, down_pairs = neighbours(count, 1), neighbours(count, -1)
    around_0 = (
        lax.ppermute(kv_0, "dp", up_pairs),
        kv_0,
        lax.ppermute(kv_0, "dp", down_pairs),
    )
    att_0, total_0 = on_core(
        local_forward_body,
        [((rows, width), BF), ((pairs, 1, LANES), F32)],
        (q_0, *around_0, bias),
    )
    kept_0, state_0, *out_0 = on_core(
        local_middle_body,
        [((rows, width + hidden), BF), ((rows, width + inner), F32)]
        + [((row_count, width), BF)] * micro_count,
        (*others, in_0, att_0, gain_mlp),
        [pltpu.VMEM((hidden, width), BF)],
    )

    in_1 = to_other_section(out_0, 1)
    fold = row_count * 3 // 4
    half = row_count // 2
    normed_1, sent = on_core(
        global_project_body,
        [((rows, width), BF), ((GROUP, 3 * fold, LANES), BF)],
        (first, *in_1, gain_attn, global_tables),
    )
    got = exchange(sent, count)
    beside = jnp.concatenate(
        [got[:, row_count : row_count + half], got[:, 3 * fold - half :]], 1
    )
    beside = partner(beside, 1, count)
    keys = GROUP * row_count
    tiles = keys * 3 // 2 // TILE
    head_scratch = [
        pltpu.VMEM((keys * 3 // 2, LANES), BF),
        pltpu.VMEM((2, keys, LANES), BF),
        pltpu.VMEM((2, keys, LANES), BF),
        pltpu.VMEM((2, LANES, keys), BF),
    ]
    folded, total_1 = on_core(
        global_forward_body,
        [((GROUP, fold, LANES), BF), ((tiles, 1, TILE), F32)],
        (got, beside, own_seg, shared_seg),
        head_scratch + [pltpu.VMEM((keys * 3 // 2, LANES), F32)],
    )
    folded = exchange(folded, count)

    up_1 = out_grad.reshape(rows, width)
    kept_1, gain_mlp_1, d_mid_1, sent = on_core(
        global_middle_body,
        [
            ((rows, 4 * width + hidden + inner), BF),
            ((1, width), F32),
            ((rows, width), F32),
            ((GROUP, fold, LANES), BF),
        ],
        (*others, folded, *in_1, up_1, gain_mlp),
        [pltpu.VMEM((hidden, width), BF)],
    )
    d_folded = exchange(sent, count)
    sources = (normed_0, normed_1, att_0, kept_0, kept_1)
    cut = 2 * width
    spans = (
        ((0, 0, width), (1, 0, width)),
        ((2, 0, width), (4, width, cut)),
        ((3, 0, width), (4, cut, cut + width)),
        ((3, width, width + hidden), (4, cut + width, cut + width + hidden)),
    )
    left_total = 3 * shard_total + hidden_total
    if count == GROUP:
        (left,) = on_core(
            functools.partial(left_body, spans),
            [((4, 4, left_total, rows), BF)],
            (lower_flag, group_pos[None], *sources),
            (),
            [pltpu.SMEM] * 2 + [pltpu.VMEM] * len(sources),
        )
        left, d_folded = lax.optimization_barrier((left, d_folded))
    else:
        left = [
            plane_rows(
                jnp.where(lower, *(sources[i][:, start:end] for i, start, end in span))
                .T.reshape(count, -1, rows),
                group_pos,
                count,
            )
            for span in spans
        ]
        left = [jnp.concatenate([i.reshape(4, -1, rows) for i in items], 1) for items in zip(*left)]
    sent, to_beside = on_core(
        global_backward_body,
        [((GROUP, 3 * fold, LANES), BF), ((GROUP, 2 * half, LANES), BF)],
        (got, beside, own_seg, shared_seg, total_1, d_folded),
        head_scratch
        + [
            pltpu.VMEM((keys * 3 // 2, LANES), BF),
            pltpu.VMEM((keys * 3 // 2, LANES), F32),
            pltpu.VMEM((2, keys, LANES), F32),
            pltpu.VMEM((2, keys, LANES), F32),
        ],
    )
    back = partner(to_beside, 1, count)
    gap = 3 * fold - half - row_count - half
    back = jnp.concatenate(
        [
            jnp.zeros((GROUP, row_count, LANES), BF),
            back[:, :half],
            jnp.zeros((GROUP, gap, LANES), BF),
            back[:, half:],
        ],
        1,
    )
    sent = (sent.astype(F32) + back.astype(F32)).astype(BF)
    if count == GROUP:
        left, sent = lax.optimization_barrier((left, sent))
        left = [left[0]] + [partner(left[apart], apart, count) for apart in range(1, 4)]
    got = exchange(sent, count)
    left, got = lax.optimization_barrier((left, got))

    d_proj_1, gain_attn_1, *grad_1 = on_core(
        global_finish_body,
        [((rows, 3 * width), BF), ((1, width), F32)] + [((row_count, width), BF)] * micro_count,
        (first, got, d_mid_1, *in_1, gain_attn, global_tables),
    )

    up_0 = to_other_section(grad_1, -1)
    d_mlp = jnp.concatenate(
        [jnp.where(lower, a, up_1[i * row_count :][:row_count]) for i, a in enumerate(up_0)]
    )
    across_mlp = partner(d_mlp, 2, count)
    gain_mlp_0, d_mid_0, d_att_0, right = on_core(
        local_back_middle_body,
        [
            ((1, width), F32),
            ((rows, width), F32),
            ((rows, width), BF),
            ((rows, inner + width), BF),
        ],
        (*others, lower_flag, *up_0, state_0, gain_mlp, kept_1),
        [pltpu.VMEM((hidden, width), BF)],
        [pltpu.VMEM] * len(others) + [pltpu.SMEM] + [pltpu.VMEM] * 5,
    )
    d_att_0, right, across_mlp = lax.optimization_barrier((d_att_0, right, across_mlp))
    across = [partner(right, 2, count)]
    d_mlp = [d_mlp, partner(d_mlp, 1, count), across_mlp, partner(across_mlp, 1, count)]
    out_near, out_far = first_hop(
        on_core(
            functools.partial(early_body, [(0, (3 * shard_total, left_total), (0, width))], 4),
            three_parts((hidden_total, width)),
            (*d_mlp, *left),
        ),
        count,
    )
    dq_0, d_own, d_before, d_after = on_core(
        local_backward_body,
        [
            ((rows, width), BF),
            ((rows, 2 * width), F32),
            ((rows, 2 * width), BF),
            ((rows, 2 * width), BF),
        ],
        (q_0, *around_0, bias, total_0, d_att_0, local_tables),
    )
    from_after = lax.ppermute(d_before, "dp", down_pairs)
    from_before = lax.ppermute(d_after, "dp", up_pairs)
    from_after, out_far = lax.optimization_barrier((from_after, out_far))
    d_proj, grad_0, gain_attn_sum = on_core(
        local_finish_body,
        [
            ((rows + EXTRA, 3 * width), BF),
            ((rows, width), BF),
            ((1, width), F32),
        ],
        (
            lower_flag, first, dq_0, d_own, from_after, from_before, local_tables, d_mid_0, in_0, gain_attn,
            gain_mlp_0, d_proj_1, gain_attn_1, gain_mlp_1,
        ),
        [pltpu.VMEM((1, width), F32)],
        [pltpu.SMEM] + [pltpu.VMEM] * 13,
    )
    across_chunks = [partner(d_proj, 2, count)]
    across, right, _ = lax.optimization_barrier((across, right, d_proj))
    right = [right, partner(right, 1, count)] + across
    right += [partner(item, 1, count) for item in across]
    in_rows, attn_rows = shard_total * (inner // width), shard_total
    early_rows = in_rows + attn_rows
    terms = [
        (0, (2 * shard_total, 3 * shard_total), (0, inner)),
        (0, (shard_total, 2 * shard_total), (inner, inner + width)),
    ]
    near, far = first_hop(
        on_core(
            functools.partial(early_body, terms, len(right)),
            three_parts((early_rows, width)),
            (*right, *left),
        ),
        count,
    )
    far = jnp.concatenate([far, out_far])
    across_chunks, d_proj, _ = lax.optimization_barrier((across_chunks, d_proj, far))
    far = partner(far, 8, count)
    right = [d_proj, partner(d_proj, 1, count)] + across_chunks
    right += [partner(item, 1, count) for item in across_chunks]
    late_in = (group_pos[None], *right, *left)
    late = on_core(
        functools.partial(late_body, (0, shard_total)),
        three_parts((shard_total, 3 * width + LANES)),
        late_in,
        [pltpu.VMEM((width, LANES), F32)],
        [pltpu.SMEM] + [pltpu.VMEM] * (len(late_in) - 1),
    )
    far, _ = lax.optimization_barrier((far, late[0]))
    early = near + far[:early_rows].astype(F32)
    mlp_out_share = out_near + far[early_rows:].astype(F32)
    late = second_hop(*first_hop(late, count), count)
    parts = [early[p * shard_total : (p + 1) * shard_total] for p in range(inner // width)]
    in_share = jnp.concatenate(parts, 1)
    attn_share = early[in_rows : in_rows + attn_rows]
    gain_columns = late[:, 3 * width :]
    qkv_share, in_share, mlp_out_share, attn_share, gain_columns = (
        over_groups(item, count)
        for item in (late[:, : 3 * width], in_share, mlp_out_share, attn_share, gain_columns)
    )
    if count == GROUP:
        gains = jnp.stack([gain_columns[:, 0], gain_columns[:, 2]])
    else:
        gain_mlp_sum = jnp.where(lower, gain_mlp_0, gain_mlp_1)
        gains = lax.psum(jnp.concatenate([gain_attn_sum, gain_mlp_sum]), "dp")
        gains = lax.dynamic_slice_in_dim(gains, replica * shard, shard, 1)

    return (
        jnp.where(lower, jnp.concatenate(out_0), kept_1[:, :width]).reshape(1, micro_count, row_count, width),
        jnp.where(lower, grad_0, jnp.concatenate(grad_1)).reshape(1, micro_count, row_count, width),
        qkv_share[None],
        attn_share[None],
        in_share[None],
        mlp_out_share[None],
        gains[:1],
        gains[1:],
    )


def solution(mesh):
    in_specs = (
        P(None, "dp", None),
        P(None, "dp"),
        P(None, "dp", None),
        P("section", "dp", None),
        P("section", "dp", None),
        P("section", "dp", None),
        P("section", "dp", None),
        P("section", "dp"),
        P("section", "dp"),
    )
    out_specs = (
        P("section", None, "dp", None),
        P("section", None, "dp", None),
        P("section", "dp", None),
        P("section", "dp", None),
        P("section", "dp", None),
        P("section", "dp", None),
        P("section", "dp"),
        P("section", "dp"),
    )
    return jax.shard_map(
        on_device, mesh=mesh, in_specs=in_specs, out_specs=out_specs, check_vma=False
    )
```

```python
import functools
import math

import jax
import jax.numpy as jnp
from jax import lax
from jax.experimental import pallas as pl
from jax.experimental.pallas import tpu as pltpu
from jax.sharding import PartitionSpec as P

HEAD_DIM = 64
GROUP = 16
HALF_WIN = 64
EXTRA = 16
LANES = 128
TILE = 256

local_log_base = math.log(10000.0)
global_log_base = math.log(160000.0)
masked_score = -1e30
SCALE = 1.0 / math.sqrt(HEAD_DIM)
BF = jnp.bfloat16
F32 = jnp.float32


def dot(left, right):
    return jnp.dot(left, right, preferred_element_type=F32)


def dot_bt(left, right):
    return lax.dot_general(left, right, (((1,), (1,)), ((), ())), preferred_element_type=F32)


def dot_at(left, right):
    return lax.dot_general(left, right, (((0,), (0,)), ((), ())), preferred_element_type=F32)


def moments(values):
    center = values - jnp.mean(values, -1, keepdims=True)
    scale = lax.rsqrt(jnp.mean(center * center, -1, keepdims=True) + 1e-05)
    return center * scale, scale


def norm_back(grad_out, gain_row, xhat, scale):
    scaled = grad_out * gain_row
    mean_grad = jnp.mean(scaled, -1, keepdims=True)
    mean_dot = jnp.mean(scaled * xhat, -1, keepdims=True)
    return (scaled - mean_grad - xhat * mean_dot) * scale


def angles(positions, log_base):
    half_dim = HEAD_DIM // 2
    fraction = (2 * jnp.arange(half_dim)).astype(F32) / HEAD_DIM
    inverse = jnp.exp(-fraction * log_base)
    table = positions.astype(F32)[:, None] * inverse[None, :]
    cosine, sine = jnp.cos(table), jnp.sin(table)
    none = jnp.zeros_like(sine)
    cosine = jnp.concatenate([cosine, cosine], 1)
    to_first = jnp.concatenate([-sine, none], 1)
    to_second = jnp.concatenate([none, sine], 1)
    return jnp.tile(jnp.stack([cosine, to_first, to_second]), (1, 2, 2))


def on_core(body, outs, args, scratch=(), spaces=None, out_spaces=None):
    return pl.pallas_call(
        body,
        out_shape=[jax.ShapeDtypeStruct(shape, dtype) for shape, dtype in outs],
        in_specs=[
            pl.BlockSpec(memory_space=space) for space in spaces or [pltpu.VMEM] * len(args)
        ],
        out_specs=[
            pl.BlockSpec(memory_space=space) for space in out_spaces or [pltpu.VMEM] * len(outs)
        ],
        scratch_shapes=scratch,
        cost_estimate=pl.CostEstimate(
            flops=2**10, bytes_accessed=2**10, transcendentals=0
        ),
        compiler_params=pltpu.CompilerParams(
            vmem_limit_bytes=(60 if body in LARGE else 48) * 2**20
        ),
    )(*args)


def low_lanes():
    return lax.broadcasted_iota(jnp.int32, (1, LANES), 1) < HEAD_DIM


def swap(chunk):
    return pltpu.roll(chunk, HEAD_DIM, 1)


def chunks_of(rows):
    return [rows[:, c : c + LANES] for c in range(0, rows.shape[1], LANES)]


def rotate(chunk, tables):
    cosine, to_first, to_second = tables
    quarter = HEAD_DIM // 2
    return (
        chunk * cosine
        + pltpu.roll(chunk, LANES - quarter, 1) * to_first
        + pltpu.roll(chunk, quarter, 1) * to_second
    )


def unrotate(chunk, tables):
    cosine, to_first, to_second = tables
    quarter = HEAD_DIM // 2
    return (
        chunk * cosine
        - pltpu.roll(chunk, LANES - quarter, 1) * to_first
        - pltpu.roll(chunk, quarter, 1) * to_second
    )


def low_and_high(chunks):
    swapped = [swap(chunk) for chunk in chunks]
    low = [(swapped if h % 2 else chunks)[h // 2] for h in range(2 * len(chunks))]
    high = [(chunks if h % 2 else swapped)[h // 2] for h in range(2 * len(chunks))]
    return low, high


def targets():
    for d in range(GROUP):
        micro, chip, half = d // 8, d % 8 // 2, d % 2
        yield d, micro, 3 * chip + 2 * half, 3 * chip + 1, half


def pack_folded(chunks, ref, base):
    low, high = low_and_high(chunks)
    first = low_lanes()
    rows = chunks[0].shape[0] // 2
    half, fold = rows // 2, rows * 3 // 4
    for d, micro, own, shared, side in targets():
        start = micro * rows
        part = start + side * half
        upper = jnp.concatenate(
            [high[own][start + fold : start + rows], high[shared][part : part + half]], 0
        )
        ref[d, base : base + fold] = jnp.where(
            first, low[own][start : start + fold], upper
        ).astype(BF)


def pack_pairs(lefts, rights, ref):
    low, high = low_and_high(lefts)[0], low_and_high(rights)[1]
    first = low_lanes()
    rows = lefts[0].shape[0] // 2
    half = rows // 2
    for d, micro, own, shared, side in targets():
        start = micro * rows
        part = start + side * half
        ref[d, 0:rows] = jnp.where(
            first, low[own][start : start + rows], high[own][start : start + rows]
        ).astype(BF)
        ref[d, rows : rows + half] = jnp.where(
            first, low[shared][part : part + half], high[shared][part : part + half]
        ).astype(BF)


def unpack_folded(ref, base, rows):
    first = low_lanes()
    fold = rows * 3 // 4
    low, high = {}, {}
    shared_parts = {}
    for d, micro, own, shared, side in targets():
        block = ref[d, base : base + fold].astype(F32)
        mine = jnp.concatenate([block, swap(block[: rows - fold])], 0)
        if own % 2:
            high[micro, own] = swap(mine)
        else:
            low[micro, own] = mine
        shared_parts[micro, shared, side] = block[rows - fold :]
        if side:
            both = jnp.concatenate([shared_parts[micro, shared, 0], block[rows - fold :]], 0)
            if shared % 2:
                high[micro, shared] = both
            else:
                low[micro, shared] = swap(both)
    heads = GROUP // 4 * 3
    return [
        jnp.concatenate(
            [jnp.where(first, low[m, h], high[m, h + 1]) for m in range(2)], 0
        )
        for h in range(0, heads, 2)
    ]


def unpack_pairs(ref, rows):
    first = low_lanes()
    half = rows // 2
    pairs = {}
    parts = {}
    for d, micro, own, shared, side in targets():
        pairs[micro, own] = ref[d, 0:rows].astype(F32)
        parts[side] = ref[d, rows : rows + half].astype(F32)
        if side:
            pairs[micro, shared] = jnp.concatenate([parts[0], parts[1]], 0)
    heads = GROUP // 4 * 3
    lefts, rights = [], []
    for h in range(0, heads, 2):
        even, odd = [pairs[m, h] for m in range(2)], [pairs[m, h + 1] for m in range(2)]
        lefts.append(
            jnp.concatenate([jnp.where(first, a, swap(b)) for a, b in zip(even, odd)], 0)
        )
        rights.append(
            jnp.concatenate([jnp.where(first, swap(a), b) for a, b in zip(even, odd)], 0)
        )
    return lefts, rights


class Weights:
    def __init__(self, sources, mlp_out):
        self.sources = sources
        self.mlp_out = sources[-1]
        if len(sources) == 1:
            self.mlp_out = mlp_out
            unpack_rows(sources[0], mlp_out)

    def get(self, which):
        if which == 2:
            return self.mlp_out[...]
        if len(self.sources) > 1:
            return self.sources[which][...]
        (wide,) = self.sources
        width = wide.shape[0]
        inner = 2 * self.mlp_out.shape[0]
        return wide[:, width : width + inner] if which else wide[:, :width]


def first_block(pair):
    return -(-pair // 32) * 16


def packed_pieces(shard, rows, width):
    yield 0, shard, 0, width, 0, 0
    rest = rows - shard
    side = width // 3
    yield 0, rest, width, 2 * side, shard, 0
    yield rest, 16, width, side, shard, 2 * side
    yield rest, 16, width + side, side, shard + 16, 2 * side


def unpack_rows(wide, mlp_out):
    hidden, width = mlp_out.shape
    shard = wide.shape[0] // GROUP
    start = wide.shape[1] - width - 2 * (width // 3)
    pair = 2 * hidden // GROUP
    upper = first_block(pair)
    for d in range(GROUP):
        low = d // 2 * pair + d % 2 * upper
        have = pair - upper if d % 2 else upper
        for row, rows, column, columns, to_row, to_column in packed_pieces(shard, upper, width):
            rows = min(rows, have - to_row)
            if rows > 0:
                mlp_out[low + to_row : low + to_row + rows, to_column : to_column + columns] = wide[
                    d * shard + row : d * shard + row + rows, start + column : start + column + columns
                ]


def stack_body(odd_ref, attn_ref, mlp_in_ref, own_ref, beside_ref, out_ref):
    shard, width = attn_ref.shape
    inner = mlp_in_ref.shape[1]
    out_ref[:, :width] = attn_ref[...]
    out_ref[:, width : width + inner] = mlp_in_ref[...]
    own, beside = own_ref[...].astype(F32), beside_ref[...].astype(F32)
    moved = beside.shape[0]
    even = jnp.concatenate([own, beside], 0)
    odd = jnp.concatenate([own[moved:], beside, beside], 0)
    block = jnp.where(odd_ref[0] == 1, odd, even).astype(BF)
    start = width + inner
    for row, rows, column, columns, from_row, from_column in packed_pieces(
        shard, block.shape[0], width
    ):
        out_ref[row : row + rows, start + column : start + column + columns] = block[
            from_row : from_row + rows, from_column : from_column + columns
        ]


def mlp_forward(layer_in, attended, gain, weights):
    middle = layer_in + dot(attended, weights.get(0))
    xhat, _ = moments(middle)
    normed = (xhat * gain).astype(BF)
    gate_up = dot(normed, weights.get(1))
    half = gate_up.shape[1] // 2
    gate, up = gate_up[:, :half], gate_up[:, half:]
    cdf = 0.5 * (1.0 + lax.erf(gate * math.sqrt(0.5)))
    mixed = (gate * cdf * up).astype(BF)
    result = (middle + dot(mixed, weights.get(2))).astype(BF)
    return middle, normed, gate, up, mixed, result


def mlp_backward(upstream, middle, gate, up, gain, weights):
    d_mixed = dot_bt(upstream, weights.get(2))
    cdf = 0.5 * (1.0 + lax.erf(gate * math.sqrt(0.5)))
    density = jnp.exp(-0.5 * gate * gate) * (1.0 / math.sqrt(2.0 * math.pi))
    d_gate = d_mixed * up * (cdf + gate * density)
    d_up = d_mixed * gate * cdf
    d_gate_up = jnp.concatenate([d_gate.astype(BF), d_up.astype(BF)], 1)
    d_normed = dot_bt(d_gate_up, weights.get(1))
    xhat, scale = moments(middle)
    gain_grad = jnp.sum(d_normed * xhat, 0, keepdims=True)
    d_middle = upstream.astype(F32) + norm_back(d_normed, gain, xhat, scale)
    d_attn = d_middle.astype(BF)
    d_attended = dot_bt(d_attn, weights.get(0))
    return d_gate_up, gain_grad, d_middle, d_attn, d_attended


def project(xhat, gain, first_ref, table_ref, normed_ref):
    width = xhat.shape[1]
    normed = (xhat * gain).astype(BF)
    normed_ref[...] = normed
    tables = [table_ref[i] for i in range(3)]
    results = [dot(normed, first_ref[:, c * width : (c + 1) * width]) for c in range(3)]
    queries, keys, values = chunks_of(results[0]), chunks_of(results[1]), results[2]
    return [rotate(c, tables) for c in queries], [rotate(c, tables) for c in keys], values


def input_backward(d_middle, d_projected, x, gain_ref, first_ref, gain_out_ref):
    d_normed = dot_bt(d_projected, first_ref[:, : d_projected.shape[1]])
    xhat, scale = moments(x)
    gain_out_ref[...] = jnp.sum(d_normed * xhat, 0, keepdims=True)
    return (d_middle + norm_back(d_normed, gain_ref[...], xhat, scale)).astype(BF)


def joined(refs):
    return jnp.concatenate([ref[...] for ref in refs], 0)


def store_chunks(refs, rows):
    size = rows.shape[0] // len(refs)
    for i, ref in enumerate(refs):
        ref[...] = rows[i * size : (i + 1) * size]


def message_body(w_ref, attn_ref, mlp_ref, ids_ref, out_ref, rows_scr, ids_scr):
    shard, columns = w_ref.shape
    micro_count, row_count = ids_ref.shape
    out_ref[:, :columns] = w_ref[...]
    rows_scr[...] = jnp.zeros_like(rows_scr)
    ids_scr[...] = jnp.zeros_like(ids_scr)
    rows_scr[0:1, :shard] = attn_ref[...].astype(F32)
    rows_scr[1:2, :shard] = mlp_ref[...].astype(F32)
    ids_scr[:micro_count, :row_count] = ids_ref[...].astype(F32)
    runs = -(-row_count // shard)
    for run in range(runs):
        turned = ids_scr[...]
        if run:
            turned = pltpu.roll(turned, LANES - run * shard, 1)
        for micro in range(micro_count):
            row = 2 + micro * runs + run
            rows_scr[row : row + 1] = turned[micro : micro + 1]
    out_ref[:, columns:] = rows_scr[...].T[:shard].astype(BF)


def local_project_body(first_ref, x_ref, table_ref, extra_ref, normed_ref, q_ref, kv_ref):
    xhat, _ = moments(x_ref[...].astype(F32))
    extra = first_ref[:, first_ref.shape[1] - LANES :].astype(F32).T
    extra_ref[...] = extra[: extra_ref.shape[0]]
    queries, keys, values = project(xhat, extra[:1], first_ref, table_ref, normed_ref)
    width = values.shape[1]
    for j, (q, k) in enumerate(zip(queries, keys)):
        q_ref[:, LANES * j : LANES * (j + 1)] = q.astype(BF)
        kv_ref[:, LANES * j : LANES * (j + 1)] = k.astype(BF)
    kv_ref[:, width:] = values.astype(BF)


def two_heads(chunk):
    first = low_lanes()
    wide = chunk.astype(F32)
    return jnp.concatenate([jnp.where(first, wide, 0.0), jnp.where(first, 0.0, wide)], 0)


def pick_heads(rows):
    half = rows.shape[0] // 2
    return jnp.where(low_lanes(), rows[:half], rows[half:])


def local_parts(q_ref, before_ref, own_ref, after_ref):
    rows = q_ref.shape[0] // 2
    width = q_ref.shape[1]
    for micro in range(2):
        for j in range(width // LANES):
            here = slice(micro * rows, (micro + 1) * rows)
            lanes = slice(LANES * j, LANES * (j + 1))
            more = slice(width + LANES * j, width + LANES * (j + 1))
            keys, values = (
                jnp.concatenate([ref[here, part] for ref in (before_ref, own_ref, after_ref)], 0)
                for part in (lanes, more)
            )
            queries = (two_heads(q_ref[here, lanes]) * SCALE).astype(BF)
            yield micro * (width // LANES) + j, micro, here, lanes, more, queries, keys, values


def local_forward_body(q_ref, before_ref, own_ref, after_ref, bias_ref, att_ref, total_ref):
    parts = local_parts(q_ref, before_ref, own_ref, after_ref)
    for index, micro, here, lanes, _, queries, keys, values in parts:
        scores = dot_bt(keys, queries) + bias_ref[micro]
        peak = jnp.max(scores, 0, keepdims=True)
        weights = jnp.exp(scores - peak)
        total = jnp.sum(weights, 0, keepdims=True)
        total_ref[index] = peak + jnp.log(total)
        probs = (weights * (1.0 / total)).astype(BF)
        att_ref[here, lanes] = pick_heads(dot_at(probs, values)).astype(BF)


def local_backward_body(
    q_ref, before_ref, own_ref, after_ref, bias_ref, total_ref, d_ref, table_ref,
    dq_ref, d_own_ref, d_before_ref, d_after_ref,
):
    tables = [table_ref[i] for i in range(3)]
    parts = local_parts(q_ref, before_ref, own_ref, after_ref)
    rows = q_ref.shape[0] // 2
    for index, micro, here, lanes, more, queries, keys, values in parts:
        d_out = two_heads(d_ref[here, lanes]).astype(BF)
        probs = jnp.exp(dot_bt(keys, queries) + bias_ref[micro] - total_ref[index])
        d_probs = dot_bt(values, d_out)
        product = probs * d_probs
        delta = jnp.sum(product, 0, keepdims=True)
        d_scores = (product - probs * delta).astype(BF)
        d_queries = pick_heads(dot_at(d_scores, keys)) * SCALE
        local_tables = [table[here] for table in tables]
        dq_ref[here, lanes] = unrotate(d_queries, local_tables).astype(BF)
        for part, grads in ((lanes, dot(d_scores, queries)), (more, dot(probs.astype(BF), d_out))):
            d_before_ref[here, part] = grads[:rows].astype(BF)
            d_own_ref[here, part] = grads[rows : 2 * rows]
            d_after_ref[here, part] = grads[2 * rows :].astype(BF)


def local_finish_body(
    lower_ref, first_ref, dq_ref, own_ref, low_ref, high_ref, table_ref, d_middle_ref, x_ref, gain_ref,
    gain_mlp_ref, other_ref, other_attn_ref, other_mlp_ref, out_ref, grad_ref, gain_attn_ref,
    gain_scr,
):
    rows, width = dq_ref.shape

    @pl.when(lower_ref[0] == 1)
    def _():
        tables = [table_ref[i] for i in range(3)]
        total = own_ref[...] + low_ref[...].astype(F32) + high_ref[...].astype(F32)
        out_ref[:rows, :width] = dq_ref[...]
        for j, chunk in enumerate(chunks_of(total[:, :width])):
            start = width + LANES * j
            out_ref[:rows, start : start + LANES] = unrotate(chunk, tables).astype(BF)
        out_ref[:rows, 2 * width :] = total[:, width:].astype(BF)
        grad_ref[...] = input_backward(
            d_middle_ref[...], out_ref[:rows], x_ref[...].astype(F32), gain_ref, first_ref, gain_scr
        )

    @pl.when(lower_ref[0] == 0)
    def _():
        out_ref[:rows] = other_ref[...]
        grad_ref[...] = jnp.zeros_like(grad_ref)
        gain_scr[...] = other_attn_ref[...]

    gain_attn_ref[...] = gain_scr[...]
    gain_mlp = jnp.where(lower_ref[0] == 1, gain_mlp_ref[...], other_mlp_ref[...])
    index = lax.broadcasted_iota(jnp.int32, (EXTRA, width), 0)
    tail = jnp.zeros((EXTRA, width), F32)
    for row, gain in ((0, gain_scr[...]), (2, gain_mlp)):
        high = gain.astype(BF).astype(F32)
        tail = jnp.where(index == row, high, tail)
        tail = jnp.where(index == row + 1, gain - high, tail)
    out_ref[rows:] = jnp.zeros((EXTRA, out_ref.shape[1]), BF)
    out_ref[rows:, :width] = tail.astype(BF)


def local_middle_body(*refs):
    sources, refs = refs[:-8], refs[-8:]
    x_ref, att_ref, gain_ref, kept_ref, state_ref = refs[:5]
    weights = Weights(sources, refs[7])
    middle, normed, gate, up, mixed, result = mlp_forward(
        x_ref[...].astype(F32), att_ref[...], gain_ref[...], weights
    )
    store_chunks(refs[5:7], result)
    width, half = middle.shape[1], gate.shape[1]
    kept_ref[:, :width] = normed
    kept_ref[:, width:] = mixed
    state_ref[:, :width] = middle
    state_ref[:, width : width + half] = gate
    state_ref[:, width + half :] = up


def local_back_middle_body(*refs):
    sources, refs = refs[:-11], refs[-11:]
    lower_ref, low_ref, high_ref, state_ref, gain_ref, other_ref = refs[:6]
    gain_out_ref, d_middle_ref, d_att_ref, right_ref = refs[6:10]
    weights = Weights(sources, refs[10])
    width = low_ref.shape[1]
    half = (state_ref.shape[1] - width) // 2
    upstream = joined([low_ref, high_ref])
    d_gate_up, gain_grad, d_middle, d_attn, d_attended = mlp_backward(
        upstream, state_ref[:, :width], state_ref[:, width : width + half], state_ref[:, width + half :],
        gain_ref[...], weights,
    )
    gain_out_ref[...] = gain_grad
    d_middle_ref[...] = d_middle
    d_att_ref[...] = d_attended.astype(BF)

    @pl.when(lower_ref[0] == 1)
    def _():
        right_ref[:, : 2 * half] = d_gate_up
        right_ref[:, 2 * half :] = d_attn

    @pl.when(lower_ref[0] == 0)
    def _():
        right_ref[...] = other_ref[:, other_ref.shape[1] - right_ref.shape[1] :]


def global_project_body(first_ref, low_ref, high_ref, gain_ref, table_ref, normed_ref, sent_ref):
    xhat, _ = moments(joined([low_ref, high_ref]).astype(F32))
    queries, keys, values = project(xhat, gain_ref[...], first_ref, table_ref, normed_ref)
    pack_pairs(queries, keys, sent_ref)
    pack_folded(chunks_of(values), sent_ref, sent_ref.shape[1] * 2 // 3)


def flat(blocks):
    return blocks.reshape(-1, LANES)


def own_unfolded(ref, base, rows):
    fold = rows * 3 // 4
    block = ref[:, base : base + fold].astype(F32)
    rest = swap(flat(block[:, : rows - fold])).reshape(GROUP, rows - fold, LANES)
    return flat(jnp.concatenate([block, rest], 1))


def shared_unfolded(ref, start, rows):
    return swap(flat(ref[:, start : start + rows // 2].astype(F32)))


def fill_heads(got_ref, other_ref, own_seg_ref, shared_seg_ref, q_scr, k_scr, v_scr):
    rows = got_ref.shape[1] * 4 // 9
    half = rows // 2
    first = low_lanes()
    lane = lax.broadcasted_iota(jnp.int32, (1, LANES), 1) - HEAD_DIM
    own = flat(got_ref[:, 0:rows].astype(F32))
    shared = flat(got_ref[:, rows : rows + half].astype(F32))
    other = flat(other_ref[:, 0:half].astype(F32))
    count = own.shape[0]
    own_hit = lane == own_seg_ref[...]
    shared_hit = lane == shared_seg_ref[...]
    both = jnp.concatenate([shared, other], 0)
    for start, pairs, hit in (
        (0, own, own_hit),
        (count, shared, shared_hit[: count // 2]),
    ):
        marked = jnp.where(hit, 1.0, 0.0)
        q_scr[start : start + pairs.shape[0]] = jnp.where(first, pairs * SCALE, marked).astype(BF)
    for unit, pairs, hit in ((0, own, own_hit), (1, both, shared_hit)):
        marked = jnp.where(hit, 0.0, masked_score)
        k_scr[unit] = jnp.where(first, swap(pairs), marked).astype(BF)
    base = rows + half
    v_scr[0] = jnp.where(first, own_unfolded(got_ref, base, rows), 0.0).astype(BF)
    start = base + rows - rows * 3 // 4
    shared_v = jnp.concatenate(
        [shared_unfolded(got_ref, start, rows), shared_unfolded(other_ref, half, rows)], 0
    )
    v_scr[1] = jnp.where(first, shared_v, 0.0).astype(BF)


def fold_out(own, shared, rows, ref, base):
    fold = rows * 3 // 4
    blocks = own.reshape(GROUP, rows, LANES)
    swapped = swap(own).reshape(GROUP, rows, LANES)
    upper = jnp.concatenate(
        [swapped[:, fold:], swap(shared).reshape(GROUP, rows // 2, LANES)], 1
    )
    ref[:, base : base + fold] = jnp.where(low_lanes(), blocks[:, :fold], upper).astype(BF)


def global_forward_body(
    got_ref, other_ref, own_seg_ref, shared_seg_ref, out_ref, total_ref,
    q_scr, k_scr, v_scr, vt_scr, o_scr,
):
    fill_heads(got_ref, other_ref, own_seg_ref, shared_seg_ref, q_scr, k_scr, v_scr)
    for unit in range(2):
        vt_scr[unit] = v_scr[unit].astype(F32).T.astype(BF)
    count = k_scr.shape[1]

    def step(tile, carry):
        unit = tile // (count // TILE)
        rows = pl.ds(pl.multiple_of(tile * TILE, TILE), TILE)
        scores = dot_bt(k_scr[unit], q_scr[rows])
        peak = jnp.max(scores, 0, keepdims=True)
        weights = jnp.exp(scores - peak)
        total = jnp.sum(weights, 0, keepdims=True)
        total_ref[tile] = peak + jnp.log(total)
        out = dot(vt_scr[unit], weights.astype(BF)) * (1.0 / total)
        o_scr[rows] = out.T
        return carry

    lax.fori_loop(0, q_scr.shape[0] // TILE, step, 0)
    rows = got_ref.shape[1] * 4 // 9
    fold_out(o_scr[:count], o_scr[count:], rows, out_ref, 0)


def global_backward_body(
    got_ref, other_ref, own_seg_ref, shared_seg_ref, total_ref, d_ref, sent_ref, to_other_ref,
    q_scr, k_scr, v_scr, kt_scr, d_scr, dq_scr, dk_scr, dv_scr,
):
    fill_heads(got_ref, other_ref, own_seg_ref, shared_seg_ref, q_scr, k_scr, v_scr)
    first = low_lanes()
    rows = got_ref.shape[1] * 4 // 9
    half = rows // 2
    for unit in range(2):
        keys = jnp.where(first, k_scr[unit].astype(F32), 0.0)
        kt_scr[unit] = keys.T.astype(BF)
    count = k_scr.shape[1]
    d_scr[:count] = jnp.where(first, own_unfolded(d_ref, 0, rows), 0.0).astype(BF)
    d_scr[count:] = jnp.where(
        first, shared_unfolded(d_ref, rows - rows * 3 // 4, rows), 0.0
    ).astype(BF)
    dk_scr[...] = jnp.zeros_like(dk_scr)
    dv_scr[...] = jnp.zeros_like(dv_scr)

    def step(tile, carry):
        unit = tile // (count // TILE)
        here = pl.ds(pl.multiple_of(tile * TILE, TILE), TILE)
        queries, d_out = q_scr[here], d_scr[here]
        probs = jnp.exp(dot_bt(k_scr[unit], queries) - total_ref[tile])
        d_probs = dot_bt(v_scr[unit], d_out)
        product = probs * d_probs
        delta = jnp.sum(product, 0, keepdims=True)
        d_scores = (product - probs * delta).astype(BF)
        dv_scr[unit] += dot(probs.astype(BF), d_out)
        dk_scr[unit] += dot(d_scores, queries)
        dq_scr[here] = dot(kt_scr[unit], d_scores).T * SCALE
        return carry

    lax.fori_loop(0, q_scr.shape[0] // TILE, step, 0)
    mine = count // 2
    own = jnp.where(first, dq_scr[:count], swap(dk_scr[0]))
    sent_ref[:, 0:rows] = own.reshape(GROUP, rows, LANES).astype(BF)
    shared_k, shared_v = dk_scr[1], dv_scr[1]
    shared = jnp.where(first, dq_scr[count:], swap(shared_k[:mine]))
    sent_ref[:, rows : rows + half] = shared.reshape(GROUP, half, LANES).astype(BF)
    fold_out(dv_scr[0], shared_v[:mine], rows, sent_ref, rows + half)
    for place, grads in enumerate((shared_k, shared_v)):
        other = jnp.where(first, 0.0, swap(grads[mine:])).reshape(GROUP, half, LANES)
        to_other_ref[:, place * half : (place + 1) * half] = other.astype(BF)


def global_middle_body(*refs):
    sources, refs = refs[:-10], refs[-10:]
    got_ref, low_ref, high_ref, up_ref, gain_ref, kept_ref, gain_out_ref, d_middle_ref, sent_ref = refs[:9]
    weights = Weights(sources, refs[9])
    rows, width = low_ref.shape
    attended = jnp.concatenate([c.astype(BF) for c in unpack_folded(got_ref, 0, rows)], 1)
    gain = gain_ref[...]
    middle, normed, gate, up, mixed, result = mlp_forward(
        joined([low_ref, high_ref]).astype(F32), attended, gain, weights
    )
    d_gate_up, gain_grad, d_middle, d_attn, d_attended = mlp_backward(
        up_ref[...], middle, gate, up, gain, weights
    )
    start = 0
    for part in (result, attended, normed, mixed, d_gate_up, d_attn):
        kept_ref[:, start : start + part.shape[1]] = part
        start += part.shape[1]
    gain_out_ref[...] = gain_grad
    d_middle_ref[...] = d_middle
    pack_folded(chunks_of(d_attended), sent_ref, 0)


def global_finish_body(
    first_ref, got_ref, d_middle_ref, low_ref, high_ref, gain_ref, table_ref,
    d_proj_ref, gain_out_ref, *grad_refs,
):
    tables = [table_ref[i] for i in range(3)]
    x = joined([low_ref, high_ref]).astype(F32)
    rows = low_ref.shape[0]
    d_queries, d_keys = unpack_pairs(got_ref, rows)
    d_values = unpack_folded(got_ref, rows * 3 // 2, rows)
    parts = [unrotate(c, tables).astype(BF) for c in d_queries + d_keys]
    d_projected = jnp.concatenate(parts + [c.astype(BF) for c in d_values], 1)
    d_proj_ref[...] = d_projected
    store_chunks(
        grad_refs,
        input_backward(d_middle_ref[...], d_projected, x, gain_ref, first_ref, gain_out_ref),
    )


LARGE = (
    message_body,
    stack_body,
    local_middle_body,
    global_middle_body,
    global_finish_body,
)


def neighbours(count, step):
    return [
        (i, i + step)
        for i in range(count)
        if 0 <= i + step < count and i // GROUP == (i + step) // GROUP
    ]


def exchange(blocks, count):
    groups = [list(range(s, s + GROUP)) for s in range(0, count, GROUP)]
    return lax.all_to_all(blocks, "dp", 0, 0, axis_index_groups=groups)


def to_other_section(chunks, step):
    pairs = [(0, 1)] if step > 0 else [(1, 0)]
    return [lax.ppermute(rows, "section", pairs) for rows in chunks]


def partner(rows, apart, count):
    return lax.ppermute(rows, "dp", [(i, i ^ apart) for i in range(count)])


def gather_rows(piece, group_pos, count):
    pieces = {0: piece}
    for apart in (4, 8, 12):
        pieces[apart] = partner(piece, apart, count)
    for apart in (0, 4, 8, 12):
        pieces[apart + 2] = partner(pieces[apart], 2, count)
    for apart in range(0, GROUP, 2):
        pieces[apart + 1] = partner(pieces[apart], 1, count)
    whole = jnp.zeros((GROUP,) + piece.shape, piece.dtype)
    for apart, item in pieces.items():
        start = (group_pos ^ apart,) + (0,) * piece.ndim
        whole = lax.dynamic_update_slice(whole, item[None], start)
    if count > GROUP:
        groups = [list(range(s, count, GROUP)) for s in range(GROUP)]
        whole = lax.all_gather(whole, "dp", axis=0, tiled=True, axis_index_groups=groups)
    return whole.reshape(-1, piece.shape[-1]), pieces[2]


def plane_rows(rows, group_pos, count):
    parts = rows.reshape(count // GROUP, 4, 4, *rows.shape[1:])
    place, plane = group_pos % 4, group_pos // 4
    taken = []
    for apart in range(4):
        block = lax.dynamic_index_in_dim(parts, place ^ apart, 2, keepdims=False)
        block = jnp.stack(
            [lax.dynamic_index_in_dim(block, plane ^ z, 1, keepdims=False) for z in range(4)]
        )
        taken.append(partner(block, apart, count) if apart else block)
    return taken


def left_body(spans, lower_ref, place_ref, *refs):
    refs, out_ref = refs[:-1], refs[-1]
    base = 0
    for span in spans:
        first, second = (refs[i][:, start:end].astype(F32) for i, start, end in span)
        turned = jnp.where(lower_ref[0] == 1, first, second).T
        size = turned.shape[0] // GROUP
        for d in range(GROUP):
            side = d % 4 ^ place_ref[0] % 4
            plane = d // 4 ^ place_ref[0] // 4
            out_ref[side, plane, base : base + size] = turned[d * size : (d + 1) * size].astype(BF)
        base += size


def left_rows_of(refs, rows):
    start, end = rows
    parts = [
        jnp.concatenate([ref[p, start:end].astype(F32) for p in range(4)], 0).astype(BF) for ref in refs
    ]
    return jnp.concatenate(parts, 1)


def by_plane(result, base, outs, columns=slice(None)):
    keep, keep_far, send = outs
    rows = result.shape[0] // 4
    half = send.shape[0] // 2
    here = slice(base, base + rows)
    keep[here, columns] = result[:rows]
    keep_far[here, columns] = result[2 * rows : 3 * rows]
    send[here, columns] = result[rows : 2 * rows].astype(BF)
    send[half + base : half + base + rows, columns] = result[3 * rows :].astype(BF)


def four_parts(refs, columns, tokens):
    own, other, across = refs
    size = own.shape[0]
    parts = [ref[:tokens, columns] for ref in (own, other, across)]
    return jnp.concatenate(parts + [other[size : size + tokens, columns]], 0)


def early_body(terms, split, *refs):
    refs, outs = refs[:-3], refs[-3:]
    operands, lefts = (refs[:split], refs[split:-4]), refs[-4:]
    width = outs[0].shape[1]
    base = 0
    for which, rows, (start, end) in terms:
        right = four_parts(operands[which], slice(start, end), lefts[0].shape[2])
        result = dot(left_rows_of(lefts, rows), right)
        for column in range(0, end - start, width):
            by_plane(result[:, column : column + width], base, outs)
            base += result.shape[0] // 4


def late_body(rows, place_ref, *refs):
    refs, outs, scr = refs[:-4], refs[-4:-1], refs[-1]
    rights, lefts = refs[:-4], refs[-4:]
    columns = rights[0].shape[1]
    width = columns // 3
    size = outs[0].shape[0]
    tokens = lefts[0].shape[2]
    right = four_parts(rights, slice(None), tokens)
    by_plane(dot(left_rows_of(lefts, rows), right), 0, outs, slice(0, columns))
    ends = [ref[tokens : tokens + EXTRA, :width] for ref in rights]
    ends.append(rights[1][rights[0].shape[0] + tokens :, :width])
    tail = sum(part.astype(F32) for part in ends)
    both = jnp.concatenate([tail, jnp.zeros((LANES - EXTRA, width), F32)], 0).T
    lane = lax.broadcasted_iota(jnp.int32, (1, LANES), 1)
    lows = pltpu.roll(both, LANES - 1, 1)
    scr[...] = jnp.where(lane % 2 == 0, both + lows, 0.0)
    gains = []
    for plane in range(4):
        d = (place_ref[0] // 4 ^ plane) * 4 + place_ref[0] % 4
        gains.append(scr[pl.ds(pl.multiple_of(d * size, 16), size)])
    by_plane(jnp.concatenate(gains, 0), 0, outs, slice(columns, columns + LANES))


def three_parts(shape):
    return [(shape, F32), (shape, F32), ((2 * shape[0], shape[1]), BF)]


def with_core(rows, across, count):
    return [rows, partner(jnp.concatenate([rows, *across]), 1, count), *across]


def first_hop(blocks, count):
    keep, keep_far, send = blocks
    got = partner(send, 4, count)
    half = keep.shape[0]
    return keep + got[:half].astype(F32), (keep_far + got[half:].astype(F32)).astype(BF)


def second_hop(near, far, count):
    return near + partner(far, 8, count).astype(F32)


def over_groups(rows, count):
    if count == GROUP:
        return rows
    apart = [list(range(s, count, GROUP)) for s in range(GROUP)]
    rows = rows.reshape(count // GROUP, -1, rows.shape[1])
    return lax.psum_scatter(rows, "dp", scatter_dimension=0, axis_index_groups=apart)


def on_device(
    tokens_in,
    segment_ids,
    out_grad,
    qkv_weight,
    attn_out_weight,
    mlp_in_weight,
    mlp_out_weight,
    attn_gain,
    mlp_gain,
):
    lower = lax.axis_index("section") == 0
    lower_flag = lower.astype(jnp.int32)[None]
    shard_total = qkv_weight.shape[1] * (lax.axis_size("dp") // GROUP)
    hidden_total = mlp_out_weight.shape[1] * (lax.axis_size("dp") // GROUP)
    count = lax.axis_size("dp")
    replica = lax.axis_index("dp")
    group_pos = replica % GROUP
    micro_count, row_count, width = tokens_in.shape
    shard = qkv_weight.shape[1]
    runs = -(-row_count // shard)
    (message,) = on_core(
        message_body,
        [((shard, 3 * width + LANES), BF)],
        (qkv_weight[0], attn_gain, mlp_gain, segment_ids),
        [pltpu.VMEM((LANES, LANES), F32), pltpu.VMEM((8, LANES), F32)],
    )
    first, early_piece = gather_rows(message, group_pos, count)
    inner = mlp_in_weight.shape[2]
    hidden = mlp_out_weight.shape[1] * count
    if count == GROUP:
        moved = first_block(2 * mlp_out_weight.shape[1]) - mlp_out_weight.shape[1]
        beside = partner(mlp_out_weight[0, :moved], 1, count)
        (stacked,) = on_core(
            stack_body,
            [((shard, width + inner + width + 2 * (width // 3)), BF)],
            (
                (replica % 2)[None],
                attn_out_weight[0],
                mlp_in_weight[0],
                mlp_out_weight[0],
                beside,
            ),
            (),
            [pltpu.SMEM] + [pltpu.VMEM] * 4,
        )
        stacked, _ = lax.optimization_barrier((stacked, early_piece))
        others = [lax.all_gather(stacked, "dp", axis=0, tiled=True)]
    else:
        others = [
            lax.all_gather(item[0], "dp", axis=0, tiled=True)
            for item in (attn_out_weight, mlp_in_weight, mlp_out_weight)
        ]
    positions = group_pos * row_count + jnp.arange(row_count)
    local_tables = angles(positions, local_log_base)
    global_tables = angles(positions, global_log_base)

    rows = micro_count * row_count
    pairs = rows * width // (row_count * LANES)
    in_0 = tokens_in.reshape(rows, width)
    extra_rows = -(-(2 + micro_count * runs) // 8) * 8
    extra, normed_0, q_0, kv_0 = on_core(
        local_project_body,
        [
            ((extra_rows, width), F32),
            ((rows, width), BF),
            ((rows, width), BF),
            ((rows, 2 * width), BF),
        ],
        (first, in_0, local_tables),
    )
    gain_attn, gain_mlp = extra[:1], extra[1:2]
    all_ids = extra[2 : 2 + micro_count * runs].reshape(micro_count, runs, count, shard)
    all_ids = lax.dynamic_slice_in_dim(all_ids, replica - group_pos, GROUP, 2)
    all_ids = all_ids.swapaxes(1, 2).reshape(micro_count, GROUP, runs * shard)[..., :row_count]
    segments = all_ids.reshape(micro_count, GROUP * row_count).astype(jnp.int32)

    key_pos = positions[0] - row_count + jnp.arange(3 * row_count)
    around = jnp.pad(segments, ((0, 0), (row_count, row_count)), constant_values=-1)
    key_seg = lax.dynamic_slice_in_dim(around, group_pos * row_count, 3 * row_count, 1)
    visible = (key_seg[:, :, None] == segment_ids[:, None, :]) & (
        jnp.abs(positions[None, :] - key_pos[:, None]) <= HALF_WIN
    )[None]
    bias = jnp.tile(jnp.where(visible, 0.0, masked_score), (1, 1, 2))

    own_seg = lax.dynamic_index_in_dim(segments, group_pos // 8, 0, keepdims=False)
    halves = own_seg.reshape(GROUP, 2, row_count // 2)
    mine = lax.dynamic_index_in_dim(halves, group_pos % 2, 1, keepdims=False).reshape(-1)
    theirs = lax.dynamic_index_in_dim(halves, 1 - group_pos % 2, 1, keepdims=False).reshape(-1)
    shared_seg = jnp.concatenate([mine, theirs])[:, None]
    own_seg = own_seg[:, None]

    up_pairs, down_pairs = neighbours(count, 1), neighbours(count, -1)
    around_0 = (
        lax.ppermute(kv_0, "dp", up_pairs),
        kv_0,
        lax.ppermute(kv_0, "dp", down_pairs),
    )
    att_0, total_0 = on_core(
        local_forward_body,
        [((rows, width), BF), ((pairs, 1, LANES), F32)],
        (q_0, *around_0, bias),
    )
    kept_0, state_0, *out_0 = on_core(
        local_middle_body,
        [((rows, width + hidden), BF), ((rows, width + inner), F32)]
        + [((row_count, width), BF)] * micro_count,
        (*others, in_0, att_0, gain_mlp),
        [pltpu.VMEM((hidden, width), BF)],
    )

    in_1 = to_other_section(out_0, 1)
    fold = row_count * 3 // 4
    half = row_count // 2
    normed_1, sent = on_core(
        global_project_body,
        [((rows, width), BF), ((GROUP, 3 * fold, LANES), BF)],
        (first, *in_1, gain_attn, global_tables),
    )
    got = exchange(sent, count)
    beside = jnp.concatenate(
        [got[:, row_count : row_count + half], got[:, 3 * fold - half :]], 1
    )
    beside = partner(beside, 1, count)
    keys = GROUP * row_count
    tiles = keys * 3 // 2 // TILE
    head_scratch = [
        pltpu.VMEM((keys * 3 // 2, LANES), BF),
        pltpu.VMEM((2, keys, LANES), BF),
        pltpu.VMEM((2, keys, LANES), BF),
        pltpu.VMEM((2, LANES, keys), BF),
    ]
    folded, total_1 = on_core(
        global_forward_body,
        [((GROUP, fold, LANES), BF), ((tiles, 1, TILE), F32)],
        (got, beside, own_seg, shared_seg),
        head_scratch + [pltpu.VMEM((keys * 3 // 2, LANES), F32)],
    )
    folded = exchange(folded, count)

    up_1 = out_grad.reshape(rows, width)
    kept_1, gain_mlp_1, d_mid_1, sent = on_core(
        global_middle_body,
        [
            ((rows, 4 * width + hidden + inner), BF),
            ((1, width), F32),
            ((rows, width), F32),
            ((GROUP, fold, LANES), BF),
        ],
        (*others, folded, *in_1, up_1, gain_mlp),
        [pltpu.VMEM((hidden, width), BF)],
    )
    d_folded = exchange(sent, count)
    sources = (normed_0, normed_1, att_0, kept_0, kept_1)
    cut = 2 * width
    spans = (
        ((0, 0, width), (1, 0, width)),
        ((2, 0, width), (4, width, cut)),
        ((3, 0, width), (4, cut, cut + width)),
        ((3, width, width + hidden), (4, cut + width, cut + width + hidden)),
    )
    left_total = 3 * shard_total + hidden_total
    if count == GROUP:
        (left,) = on_core(
            functools.partial(left_body, spans),
            [((4, 4, left_total, rows), BF)],
            (lower_flag, group_pos[None], *sources),
            (),
            [pltpu.SMEM] * 2 + [pltpu.VMEM] * len(sources),
        )
        left, d_folded = lax.optimization_barrier((left, d_folded))
    else:
        left = [
            plane_rows(
                jnp.where(lower, *(sources[i][:, start:end] for i, start, end in span))
                .T.reshape(count, -1, rows),
                group_pos,
                count,
            )
            for span in spans
        ]
        left = [jnp.concatenate([i.reshape(4, -1, rows) for i in items], 1) for items in zip(*left)]
    sent, to_beside = on_core(
        global_backward_body,
        [((GROUP, 3 * fold, LANES), BF), ((GROUP, 2 * half, LANES), BF)],
        (got, beside, own_seg, shared_seg, total_1, d_folded),
        head_scratch
        + [
            pltpu.VMEM((keys * 3 // 2, LANES), BF),
            pltpu.VMEM((keys * 3 // 2, LANES), F32),
            pltpu.VMEM((2, keys, LANES), F32),
            pltpu.VMEM((2, keys, LANES), F32),
        ],
    )
    back = partner(to_beside, 1, count)
    gap = 3 * fold - half - row_count - half
    back = jnp.concatenate(
        [
            jnp.zeros((GROUP, row_count, LANES), BF),
            back[:, :half],
            jnp.zeros((GROUP, gap, LANES), BF),
            back[:, half:],
        ],
        1,
    )
    sent = (sent.astype(F32) + back.astype(F32)).astype(BF)
    if count == GROUP:
        left, sent = lax.optimization_barrier((left, sent))
        left = [left[0]] + [partner(left[apart], apart, count) for apart in range(1, 4)]
    got = exchange(sent, count)
    left, got = lax.optimization_barrier((left, got))

    d_proj_1, gain_attn_1, *grad_1 = on_core(
        global_finish_body,
        [((rows, 3 * width), BF), ((1, width), F32)] + [((row_count, width), BF)] * micro_count,
        (first, got, d_mid_1, *in_1, gain_attn, global_tables),
    )

    up_0 = to_other_section(grad_1, -1)
    d_mlp = jnp.concatenate(
        [jnp.where(lower, a, up_1[i * row_count :][:row_count]) for i, a in enumerate(up_0)]
    )
    across_mlp = partner(d_mlp, 2, count)
    gain_mlp_0, d_mid_0, d_att_0, right = on_core(
        local_back_middle_body,
        [
            ((1, width), F32),
            ((rows, width), F32),
            ((rows, width), BF),
            ((rows, inner + width), BF),
        ],
        (*others, lower_flag, *up_0, state_0, gain_mlp, kept_1),
        [pltpu.VMEM((hidden, width), BF)],
        [pltpu.VMEM] * len(others) + [pltpu.SMEM] + [pltpu.VMEM] * 5,
    )
    d_att_0, right, across_mlp = lax.optimization_barrier((d_att_0, right, across_mlp))
    across = [partner(right, 2, count)]
    d_mlp = with_core(d_mlp, [across_mlp], count)
    out_near, out_far = first_hop(
        on_core(
            functools.partial(early_body, [(0, (3 * shard_total, left_total), (0, width))], 3),
            three_parts((hidden_total, width)),
            (*d_mlp, *left),
        ),
        count,
    )
    dq_0, d_own, d_before, d_after = on_core(
        local_backward_body,
        [
            ((rows, width), BF),
            ((rows, 2 * width), F32),
            ((rows, 2 * width), BF),
            ((rows, 2 * width), BF),
        ],
        (q_0, *around_0, bias, total_0, d_att_0, local_tables),
    )
    from_after = lax.ppermute(d_before, "dp", down_pairs)
    from_before = lax.ppermute(d_after, "dp", up_pairs)
    from_after, out_far = lax.optimization_barrier((from_after, out_far))
    d_proj, grad_0, gain_attn_sum = on_core(
        local_finish_body,
        [
            ((rows + EXTRA, 3 * width), BF),
            ((rows, width), BF),
            ((1, width), F32),
        ],
        (
            lower_flag, first, dq_0, d_own, from_after, from_before, local_tables, d_mid_0, in_0, gain_attn,
            gain_mlp_0, d_proj_1, gain_attn_1, gain_mlp_1,
        ),
        [pltpu.VMEM((1, width), F32)],
        [pltpu.SMEM] + [pltpu.VMEM] * 13,
    )
    across_chunks = [partner(d_proj, 2, count)]
    across, right, _ = lax.optimization_barrier((across, right, d_proj))
    right = with_core(right, across, count)
    in_rows, attn_rows = shard_total * (inner // width), shard_total
    early_rows = in_rows + attn_rows
    terms = [
        (0, (2 * shard_total, 3 * shard_total), (0, inner)),
        (0, (shard_total, 2 * shard_total), (inner, inner + width)),
    ]
    near, far = first_hop(
        on_core(
            functools.partial(early_body, terms, len(right)),
            three_parts((early_rows, width)),
            (*right, *left),
        ),
        count,
    )
    far = jnp.concatenate([far, out_far])
    across_chunks, d_proj, _ = lax.optimization_barrier((across_chunks, d_proj, far))
    far = partner(far, 8, count)
    right = with_core(d_proj, across_chunks, count)
    late_in = (group_pos[None], *right, *left)
    late = on_core(
        functools.partial(late_body, (0, shard_total)),
        three_parts((shard_total, 3 * width + LANES)),
        late_in,
        [pltpu.VMEM((width, LANES), F32)],
        [pltpu.SMEM] + [pltpu.VMEM] * (len(late_in) - 1),
    )
    far, _ = lax.optimization_barrier((far, late[0]))
    early = near + far[:early_rows].astype(F32)
    mlp_out_share = out_near + far[early_rows:].astype(F32)
    late = second_hop(*first_hop(late, count), count)
    parts = [early[p * shard_total : (p + 1) * shard_total] for p in range(inner // width)]
    in_share = jnp.concatenate(parts, 1)
    attn_share = early[in_rows : in_rows + attn_rows]
    gain_columns = late[:, 3 * width :]
    qkv_share, in_share, mlp_out_share, attn_share, gain_columns = (
        over_groups(item, count)
        for item in (late[:, : 3 * width], in_share, mlp_out_share, attn_share, gain_columns)
    )
    if count == GROUP:
        gains = jnp.stack([gain_columns[:, 0], gain_columns[:, 2]])
    else:
        gain_mlp_sum = jnp.where(lower, gain_mlp_0, gain_mlp_1)
        gains = lax.psum(jnp.concatenate([gain_attn_sum, gain_mlp_sum]), "dp")
        gains = lax.dynamic_slice_in_dim(gains, replica * shard, shard, 1)

    return (
        jnp.where(lower, jnp.concatenate(out_0), kept_1[:, :width]).reshape(1, micro_count, row_count, width),
        jnp.where(lower, grad_0, jnp.concatenate(grad_1)).reshape(1, micro_count, row_count, width),
        qkv_share[None],
        attn_share[None],
        in_share[None],
        mlp_out_share[None],
        gains[:1],
        gains[1:],
    )


def solution(mesh):
    in_specs = (
        P(None, "dp", None),
        P(None, "dp"),
        P(None, "dp", None),
        P("section", "dp", None),
        P("section", "dp", None),
        P("section", "dp", None),
        P("section", "dp", None),
        P("section", "dp"),
        P("section", "dp"),
    )
    out_specs = (
        P("section", None, "dp", None),
        P("section", None, "dp", None),
        P("section", "dp", None),
        P("section", "dp", None),
        P("section", "dp", None),
        P("section", "dp", None),
        P("section", "dp"),
        P("section", "dp"),
    )
    return jax.shard_map(
        on_device, mesh=mesh, in_specs=in_specs, out_specs=out_specs, check_vma=False
    )
```

```python
import functools
import math

import jax
import jax.numpy as jnp
from jax import lax
from jax.experimental import pallas as pl
from jax.experimental.pallas import tpu as pltpu
from jax.sharding import PartitionSpec as P

HEAD_DIM = 64
GROUP = 16
HALF_WIN = 64
EXTRA = 16
LANES = 128
TILE = 512

local_log_base = math.log(10000.0)
global_log_base = math.log(160000.0)
masked_score = -1e30
SCALE = 1.0 / math.sqrt(HEAD_DIM)
BF = jnp.bfloat16
F32 = jnp.float32


def dot(left, right):
    return jnp.dot(left, right, preferred_element_type=F32)


def dot_bt(left, right):
    return lax.dot_general(left, right, (((1,), (1,)), ((), ())), preferred_element_type=F32)


def dot_at(left, right):
    return lax.dot_general(left, right, (((0,), (0,)), ((), ())), preferred_element_type=F32)


def moments(values):
    center = values - jnp.mean(values, -1, keepdims=True)
    scale = lax.rsqrt(jnp.mean(center * center, -1, keepdims=True) + 1e-05)
    return center * scale, scale


def norm_back(grad_out, gain_row, xhat, scale):
    scaled = grad_out * gain_row
    mean_grad = jnp.mean(scaled, -1, keepdims=True)
    mean_dot = jnp.mean(scaled * xhat, -1, keepdims=True)
    return (scaled - mean_grad - xhat * mean_dot) * scale


def angles(positions, log_base):
    half_dim = HEAD_DIM // 2
    fraction = (2 * jnp.arange(half_dim)).astype(F32) / HEAD_DIM
    inverse = jnp.exp(-fraction * log_base)
    table = positions.astype(F32)[:, None] * inverse[None, :]
    cosine, sine = jnp.cos(table), jnp.sin(table)
    none = jnp.zeros_like(sine)
    cosine = jnp.concatenate([cosine, cosine], 1)
    to_first = jnp.concatenate([-sine, none], 1)
    to_second = jnp.concatenate([none, sine], 1)
    return jnp.tile(jnp.stack([cosine, to_first, to_second]), (1, 2, 2))


def on_core(body, outs, args, scratch=(), spaces=None, out_spaces=None):
    return pl.pallas_call(
        body,
        out_shape=[jax.ShapeDtypeStruct(shape, dtype) for shape, dtype in outs],
        in_specs=[
            pl.BlockSpec(memory_space=space) for space in spaces or [pltpu.VMEM] * len(args)
        ],
        out_specs=[
            pl.BlockSpec(memory_space=space) for space in out_spaces or [pltpu.VMEM] * len(outs)
        ],
        scratch_shapes=scratch,
        cost_estimate=pl.CostEstimate(
            flops=2**10, bytes_accessed=2**10, transcendentals=0
        ),
        compiler_params=pltpu.CompilerParams(
            vmem_limit_bytes=(60 if body in LARGE else 48) * 2**20
        ),
    )(*args)


def low_lanes():
    return lax.broadcasted_iota(jnp.int32, (1, LANES), 1) < HEAD_DIM


def swap(chunk):
    return pltpu.roll(chunk, HEAD_DIM, 1)


def chunks_of(rows):
    return [rows[:, c : c + LANES] for c in range(0, rows.shape[1], LANES)]


def rotate(chunk, tables):
    cosine, to_first, to_second = tables
    quarter = HEAD_DIM // 2
    return (
        chunk * cosine
        + pltpu.roll(chunk, LANES - quarter, 1) * to_first
        + pltpu.roll(chunk, quarter, 1) * to_second
    )


def unrotate(chunk, tables):
    cosine, to_first, to_second = tables
    quarter = HEAD_DIM // 2
    return (
        chunk * cosine
        - pltpu.roll(chunk, LANES - quarter, 1) * to_first
        - pltpu.roll(chunk, quarter, 1) * to_second
    )


def low_and_high(chunks):
    swapped = [swap(chunk) for chunk in chunks]
    low = [(swapped if h % 2 else chunks)[h // 2] for h in range(2 * len(chunks))]
    high = [(chunks if h % 2 else swapped)[h // 2] for h in range(2 * len(chunks))]
    return low, high


def targets():
    for d in range(GROUP):
        micro, chip, half = d // 8, d % 8 // 2, d % 2
        yield d, micro, 3 * chip + 2 * half, 3 * chip + 1, half


def pack_folded(chunks, ref, base):
    low, high = low_and_high(chunks)
    first = low_lanes()
    rows = chunks[0].shape[0] // 2
    half, fold = rows // 2, rows * 3 // 4
    for d, micro, own, shared, side in targets():
        start = micro * rows
        part = start + side * half
        upper = jnp.concatenate(
            [high[own][start + fold : start + rows], high[shared][part : part + half]], 0
        )
        ref[d, base : base + fold] = jnp.where(
            first, low[own][start : start + fold], upper
        ).astype(BF)


def pack_pairs(lefts, rights, ref):
    low, high = low_and_high(lefts)[0], low_and_high(rights)[1]
    first = low_lanes()
    rows = lefts[0].shape[0] // 2
    half = rows // 2
    for d, micro, own, shared, side in targets():
        start = micro * rows
        part = start + side * half
        ref[d, 0:rows] = jnp.where(
            first, low[own][start : start + rows], high[own][start : start + rows]
        ).astype(BF)
        ref[d, rows : rows + half] = jnp.where(
            first, low[shared][part : part + half], high[shared][part : part + half]
        ).astype(BF)


def unpack_folded(ref, base, rows):
    first = low_lanes()
    fold = rows * 3 // 4
    low, high = {}, {}
    shared_parts = {}
    for d, micro, own, shared, side in targets():
        block = ref[d, base : base + fold].astype(F32)
        mine = jnp.concatenate([block, swap(block[: rows - fold])], 0)
        if own % 2:
            high[micro, own] = swap(mine)
        else:
            low[micro, own] = mine
        shared_parts[micro, shared, side] = block[rows - fold :]
        if side:
            both = jnp.concatenate([shared_parts[micro, shared, 0], block[rows - fold :]], 0)
            if shared % 2:
                high[micro, shared] = both
            else:
                low[micro, shared] = swap(both)
    heads = GROUP // 4 * 3
    return [
        jnp.concatenate(
            [jnp.where(first, low[m, h], high[m, h + 1]) for m in range(2)], 0
        )
        for h in range(0, heads, 2)
    ]


def unpack_pairs(ref, rows):
    first = low_lanes()
    half = rows // 2
    pairs = {}
    parts = {}
    for d, micro, own, shared, side in targets():
        pairs[micro, own] = ref[d, 0:rows].astype(F32)
        parts[side] = ref[d, rows : rows + half].astype(F32)
        if side:
            pairs[micro, shared] = jnp.concatenate([parts[0], parts[1]], 0)
    heads = GROUP // 4 * 3
    lefts, rights = [], []
    for h in range(0, heads, 2):
        even, odd = [pairs[m, h] for m in range(2)], [pairs[m, h + 1] for m in range(2)]
        lefts.append(
            jnp.concatenate([jnp.where(first, a, swap(b)) for a, b in zip(even, odd)], 0)
        )
        rights.append(
            jnp.concatenate([jnp.where(first, swap(a), b) for a, b in zip(even, odd)], 0)
        )
    return lefts, rights


class Weights:
    def __init__(self, sources, mlp_out):
        self.sources = sources
        self.mlp_out = sources[-1]
        if len(sources) == 1:
            self.mlp_out = mlp_out
            unpack_rows(sources[0], mlp_out)

    def get(self, which):
        if which == 2:
            return self.mlp_out[...]
        if len(self.sources) > 1:
            return self.sources[which][...]
        (wide,) = self.sources
        width = wide.shape[0]
        inner = 2 * self.mlp_out.shape[0]
        return wide[:, width : width + inner] if which else wide[:, :width]


def first_block(pair):
    return -(-pair // 32) * 16


def packed_pieces(shard, rows, width):
    yield 0, shard, 0, width, 0, 0
    rest = rows - shard
    side = width // 3
    yield 0, rest, width, 2 * side, shard, 0
    yield rest, 16, width, side, shard, 2 * side
    yield rest, 16, width + side, side, shard + 16, 2 * side


def unpack_rows(wide, mlp_out):
    hidden, width = mlp_out.shape
    shard = wide.shape[0] // GROUP
    start = wide.shape[1] - width - 2 * (width // 3)
    pair = 2 * hidden // GROUP
    upper = first_block(pair)
    for d in range(GROUP):
        low = d // 2 * pair + d % 2 * upper
        have = pair - upper if d % 2 else upper
        for row, rows, column, columns, to_row, to_column in packed_pieces(shard, upper, width):
            rows = min(rows, have - to_row)
            if rows > 0:
                mlp_out[low + to_row : low + to_row + rows, to_column : to_column + columns] = wide[
                    d * shard + row : d * shard + row + rows, start + column : start + column + columns
                ]


def stack_body(odd_ref, attn_ref, mlp_in_ref, own_ref, beside_ref, out_ref):
    shard, width = attn_ref.shape
    inner = mlp_in_ref.shape[1]
    out_ref[:, :width] = attn_ref[...]
    out_ref[:, width : width + inner] = mlp_in_ref[...]
    own, beside = own_ref[...].astype(F32), beside_ref[...].astype(F32)
    moved = beside.shape[0]
    even = jnp.concatenate([own, beside], 0)
    odd = jnp.concatenate([own[moved:], beside, beside], 0)
    block = jnp.where(odd_ref[0] == 1, odd, even).astype(BF)
    start = width + inner
    for row, rows, column, columns, from_row, from_column in packed_pieces(
        shard, block.shape[0], width
    ):
        out_ref[row : row + rows, start + column : start + column + columns] = block[
            from_row : from_row + rows, from_column : from_column + columns
        ]


def mlp_forward(layer_in, attended, gain, weights):
    middle = layer_in + dot(attended, weights.get(0))
    xhat, _ = moments(middle)
    normed = (xhat * gain).astype(BF)
    gate_up = dot(normed, weights.get(1))
    half = gate_up.shape[1] // 2
    gate, up = gate_up[:, :half], gate_up[:, half:]
    cdf = 0.5 * (1.0 + lax.erf(gate * math.sqrt(0.5)))
    mixed = (gate * cdf * up).astype(BF)
    result = (middle + dot(mixed, weights.get(2))).astype(BF)
    return middle, normed, gate, up, mixed, result


def mlp_backward(upstream, middle, gate, up, gain, weights):
    d_mixed = dot_bt(upstream, weights.get(2))
    cdf = 0.5 * (1.0 + lax.erf(gate * math.sqrt(0.5)))
    density = jnp.exp(-0.5 * gate * gate) * (1.0 / math.sqrt(2.0 * math.pi))
    d_gate = d_mixed * up * (cdf + gate * density)
    d_up = d_mixed * gate * cdf
    d_gate_up = jnp.concatenate([d_gate.astype(BF), d_up.astype(BF)], 1)
    d_normed = dot_bt(d_gate_up, weights.get(1))
    xhat, scale = moments(middle)
    gain_grad = jnp.sum(d_normed * xhat, 0, keepdims=True)
    d_middle = upstream.astype(F32) + norm_back(d_normed, gain, xhat, scale)
    d_attn = d_middle.astype(BF)
    d_attended = dot_bt(d_attn, weights.get(0))
    return d_gate_up, gain_grad, d_middle, d_attn, d_attended


def project(xhat, gain, first_ref, table_ref, normed_ref):
    width = xhat.shape[1]
    normed = (xhat * gain).astype(BF)
    normed_ref[...] = normed
    tables = [table_ref[i] for i in range(3)]
    results = [dot(normed, first_ref[:, c * width : (c + 1) * width]) for c in range(3)]
    queries, keys, values = chunks_of(results[0]), chunks_of(results[1]), results[2]
    return [rotate(c, tables) for c in queries], [rotate(c, tables) for c in keys], values


def input_backward(d_middle, d_projected, x, gain_ref, first_ref, gain_out_ref):
    d_normed = dot_bt(d_projected, first_ref[:, : d_projected.shape[1]])
    xhat, scale = moments(x)
    gain_out_ref[...] = jnp.sum(d_normed * xhat, 0, keepdims=True)
    return (d_middle + norm_back(d_normed, gain_ref[...], xhat, scale)).astype(BF)


def joined(refs):
    return jnp.concatenate([ref[...] for ref in refs], 0)


def store_chunks(refs, rows):
    size = rows.shape[0] // len(refs)
    for i, ref in enumerate(refs):
        ref[...] = rows[i * size : (i + 1) * size]


def message_body(w_ref, attn_ref, mlp_ref, ids_ref, out_ref, rows_scr, ids_scr):
    shard, columns = w_ref.shape
    micro_count, row_count = ids_ref.shape
    out_ref[:, :columns] = w_ref[...]
    rows_scr[...] = jnp.zeros_like(rows_scr)
    ids_scr[...] = jnp.zeros_like(ids_scr)
    rows_scr[0:1, :shard] = attn_ref[...].astype(F32)
    rows_scr[1:2, :shard] = mlp_ref[...].astype(F32)
    ids_scr[:micro_count, :row_count] = ids_ref[...].astype(F32)
    runs = -(-row_count // shard)
    for run in range(runs):
        turned = ids_scr[...]
        if run:
            turned = pltpu.roll(turned, LANES - run * shard, 1)
        for micro in range(micro_count):
            row = 2 + micro * runs + run
            rows_scr[row : row + 1] = turned[micro : micro + 1]
    out_ref[:, columns:] = rows_scr[...].T[:shard].astype(BF)


def local_project_body(first_ref, x_ref, table_ref, extra_ref, normed_ref, q_ref, kv_ref):
    xhat, _ = moments(x_ref[...].astype(F32))
    extra = first_ref[:, first_ref.shape[1] - LANES :].astype(F32).T
    extra_ref[...] = extra[: extra_ref.shape[0]]
    queries, keys, values = project(xhat, extra[:1], first_ref, table_ref, normed_ref)
    width = values.shape[1]
    for j, (q, k) in enumerate(zip(queries, keys)):
        q_ref[:, LANES * j : LANES * (j + 1)] = q.astype(BF)
        kv_ref[:, LANES * j : LANES * (j + 1)] = k.astype(BF)
    kv_ref[:, width:] = values.astype(BF)


def two_heads(chunk):
    first = low_lanes()
    wide = chunk.astype(F32)
    return jnp.concatenate([jnp.where(first, wide, 0.0), jnp.where(first, 0.0, wide)], 0)


def pick_heads(rows):
    half = rows.shape[0] // 2
    return jnp.where(low_lanes(), rows[:half], rows[half:])


def local_parts(q_ref, before_ref, own_ref, after_ref):
    rows = q_ref.shape[0] // 2
    width = q_ref.shape[1]
    for micro in range(2):
        for j in range(width // LANES):
            here = slice(micro * rows, (micro + 1) * rows)
            lanes = slice(LANES * j, LANES * (j + 1))
            more = slice(width + LANES * j, width + LANES * (j + 1))
            keys, values = (
                jnp.concatenate([ref[here, part] for ref in (before_ref, own_ref, after_ref)], 0)
                for part in (lanes, more)
            )
            queries = (two_heads(q_ref[here, lanes]) * SCALE).astype(BF)
            yield micro * (width // LANES) + j, micro, here, lanes, more, queries, keys, values


def local_forward_body(q_ref, before_ref, own_ref, after_ref, bias_ref, att_ref, total_ref):
    parts = local_parts(q_ref, before_ref, own_ref, after_ref)
    for index, micro, here, lanes, _, queries, keys, values in parts:
        scores = dot_bt(keys, queries) + bias_ref[micro]
        peak = jnp.max(scores, 0, keepdims=True)
        weights = jnp.exp(scores - peak)
        total = jnp.sum(weights, 0, keepdims=True)
        total_ref[index] = peak + jnp.log(total)
        probs = (weights * (1.0 / total)).astype(BF)
        att_ref[here, lanes] = pick_heads(dot_at(probs, values)).astype(BF)


def local_backward_body(
    q_ref, before_ref, own_ref, after_ref, bias_ref, total_ref, d_ref, table_ref,
    dq_ref, d_own_ref, d_before_ref, d_after_ref,
):
    tables = [table_ref[i] for i in range(3)]
    parts = local_parts(q_ref, before_ref, own_ref, after_ref)
    rows = q_ref.shape[0] // 2
    for index, micro, here, lanes, more, queries, keys, values in parts:
        d_out = two_heads(d_ref[here, lanes]).astype(BF)
        probs = jnp.exp(dot_bt(keys, queries) + bias_ref[micro] - total_ref[index])
        d_probs = dot_bt(values, d_out)
        product = probs * d_probs
        delta = jnp.sum(product, 0, keepdims=True)
        d_scores = (product - probs * delta).astype(BF)
        d_queries = pick_heads(dot_at(d_scores, keys)) * SCALE
        local_tables = [table[here] for table in tables]
        dq_ref[here, lanes] = unrotate(d_queries, local_tables).astype(BF)
        for part, grads in ((lanes, dot(d_scores, queries)), (more, dot(probs.astype(BF), d_out))):
            d_before_ref[here, part] = grads[:rows].astype(BF)
            d_own_ref[here, part] = grads[rows : 2 * rows]
            d_after_ref[here, part] = grads[2 * rows :].astype(BF)


def local_finish_body(
    lower_ref, first_ref, dq_ref, own_ref, low_ref, high_ref, table_ref, d_middle_ref, x_ref, gain_ref,
    gain_mlp_ref, other_ref, other_attn_ref, other_mlp_ref, out_ref, grad_ref, gain_attn_ref,
    gain_scr,
):
    rows, width = dq_ref.shape

    @pl.when(lower_ref[0] == 1)
    def _():
        tables = [table_ref[i] for i in range(3)]
        total = own_ref[...] + low_ref[...].astype(F32) + high_ref[...].astype(F32)
        out_ref[:rows, :width] = dq_ref[...]
        for j, chunk in enumerate(chunks_of(total[:, :width])):
            start = width + LANES * j
            out_ref[:rows, start : start + LANES] = unrotate(chunk, tables).astype(BF)
        out_ref[:rows, 2 * width :] = total[:, width:].astype(BF)
        grad_ref[...] = input_backward(
            d_middle_ref[...], out_ref[:rows], x_ref[...].astype(F32), gain_ref, first_ref, gain_scr
        )

    @pl.when(lower_ref[0] == 0)
    def _():
        out_ref[:rows] = other_ref[...]
        grad_ref[...] = jnp.zeros_like(grad_ref)
        gain_scr[...] = other_attn_ref[...]

    gain_attn_ref[...] = gain_scr[...]
    gain_mlp = jnp.where(lower_ref[0] == 1, gain_mlp_ref[...], other_mlp_ref[...])
    index = lax.broadcasted_iota(jnp.int32, (EXTRA, width), 0)
    tail = jnp.zeros((EXTRA, width), F32)
    for row, gain in ((0, gain_scr[...]), (2, gain_mlp)):
        high = gain.astype(BF).astype(F32)
        tail = jnp.where(index == row, high, tail)
        tail = jnp.where(index == row + 1, gain - high, tail)
    out_ref[rows:] = jnp.zeros((EXTRA, out_ref.shape[1]), BF)
    out_ref[rows:, :width] = tail.astype(BF)


def local_middle_body(*refs):
    sources, refs = refs[:-8], refs[-8:]
    x_ref, att_ref, gain_ref, kept_ref, state_ref = refs[:5]
    weights = Weights(sources, refs[7])
    middle, normed, gate, up, mixed, result = mlp_forward(
        x_ref[...].astype(F32), att_ref[...], gain_ref[...], weights
    )
    store_chunks(refs[5:7], result)
    width, half = middle.shape[1], gate.shape[1]
    kept_ref[:, :width] = normed
    kept_ref[:, width:] = mixed
    state_ref[:, :width] = middle
    state_ref[:, width : width + half] = gate
    state_ref[:, width + half :] = up


def local_back_middle_body(*refs):
    sources, refs = refs[:-11], refs[-11:]
    lower_ref, low_ref, high_ref, state_ref, gain_ref, other_ref = refs[:6]
    gain_out_ref, d_middle_ref, d_att_ref, right_ref = refs[6:10]
    weights = Weights(sources, refs[10])
    width = low_ref.shape[1]
    half = (state_ref.shape[1] - width) // 2
    upstream = joined([low_ref, high_ref])
    d_gate_up, gain_grad, d_middle, d_attn, d_attended = mlp_backward(
        upstream, state_ref[:, :width], state_ref[:, width : width + half], state_ref[:, width + half :],
        gain_ref[...], weights,
    )
    gain_out_ref[...] = gain_grad
    d_middle_ref[...] = d_middle
    d_att_ref[...] = d_attended.astype(BF)

    @pl.when(lower_ref[0] == 1)
    def _():
        right_ref[:, : 2 * half] = d_gate_up
        right_ref[:, 2 * half :] = d_attn

    @pl.when(lower_ref[0] == 0)
    def _():
        right_ref[...] = other_ref[:, other_ref.shape[1] - right_ref.shape[1] :]


def global_project_body(first_ref, low_ref, high_ref, gain_ref, table_ref, normed_ref, sent_ref):
    xhat, _ = moments(joined([low_ref, high_ref]).astype(F32))
    queries, keys, values = project(xhat, gain_ref[...], first_ref, table_ref, normed_ref)
    pack_pairs(queries, keys, sent_ref)
    pack_folded(chunks_of(values), sent_ref, sent_ref.shape[1] * 2 // 3)


def flat(blocks):
    return blocks.reshape(-1, LANES)


def own_unfolded(ref, base, rows):
    fold = rows * 3 // 4
    block = ref[:, base : base + fold].astype(F32)
    rest = swap(flat(block[:, : rows - fold])).reshape(GROUP, rows - fold, LANES)
    return flat(jnp.concatenate([block, rest], 1))


def shared_unfolded(ref, start, rows):
    return swap(flat(ref[:, start : start + rows // 2].astype(F32)))


def fill_heads(got_ref, other_ref, own_seg_ref, shared_seg_ref, q_scr, k_scr, v_scr):
    rows = got_ref.shape[1] * 4 // 9
    half = rows // 2
    first = low_lanes()
    lane = lax.broadcasted_iota(jnp.int32, (1, LANES), 1) - HEAD_DIM
    own = flat(got_ref[:, 0:rows].astype(F32))
    shared = flat(got_ref[:, rows : rows + half].astype(F32))
    other = flat(other_ref[:, 0:half].astype(F32))
    count = own.shape[0]
    own_hit = lane == own_seg_ref[...]
    shared_hit = lane == shared_seg_ref[...]
    both = jnp.concatenate([shared, other], 0)
    for start, pairs, hit in (
        (0, own, own_hit),
        (count, shared, shared_hit[: count // 2]),
    ):
        marked = jnp.where(hit, 1.0, 0.0)
        q_scr[start : start + pairs.shape[0]] = jnp.where(first, pairs * SCALE, marked).astype(BF)
    for unit, pairs, hit in ((0, own, own_hit), (1, both, shared_hit)):
        marked = jnp.where(hit, 0.0, masked_score)
        k_scr[unit] = jnp.where(first, swap(pairs), marked).astype(BF)
    base = rows + half
    v_scr[0] = jnp.where(first, own_unfolded(got_ref, base, rows), 0.0).astype(BF)
    start = base + rows - rows * 3 // 4
    shared_v = jnp.concatenate(
        [shared_unfolded(got_ref, start, rows), shared_unfolded(other_ref, half, rows)], 0
    )
    v_scr[1] = jnp.where(first, shared_v, 0.0).astype(BF)


def fold_out(own, shared, rows, ref, base):
    fold = rows * 3 // 4
    blocks = own.reshape(GROUP, rows, LANES)
    swapped = swap(own).reshape(GROUP, rows, LANES)
    upper = jnp.concatenate(
        [swapped[:, fold:], swap(shared).reshape(GROUP, rows // 2, LANES)], 1
    )
    ref[:, base : base + fold] = jnp.where(low_lanes(), blocks[:, :fold], upper).astype(BF)


def global_forward_body(
    got_ref, other_ref, own_seg_ref, shared_seg_ref, out_ref, total_ref,
    q_scr, k_scr, v_scr, vt_scr, o_scr,
):
    fill_heads(got_ref, other_ref, own_seg_ref, shared_seg_ref, q_scr, k_scr, v_scr)
    for unit in range(2):
        vt_scr[unit] = v_scr[unit].astype(F32).T.astype(BF)
    count = k_scr.shape[1]

    def step(tile, carry):
        unit = tile // (count // TILE)
        rows = pl.ds(pl.multiple_of(tile * TILE, TILE), TILE)
        scores = dot_bt(k_scr[unit], q_scr[rows])
        peak = jnp.max(scores, 0, keepdims=True)
        weights = jnp.exp(scores - peak)
        total = jnp.sum(weights, 0, keepdims=True)
        total_ref[tile] = peak + jnp.log(total)
        out = dot(vt_scr[unit], weights.astype(BF)) * (1.0 / total)
        o_scr[rows] = out.T
        return carry

    lax.fori_loop(0, q_scr.shape[0] // TILE, step, 0)
    rows = got_ref.shape[1] * 4 // 9
    fold_out(o_scr[:count], o_scr[count:], rows, out_ref, 0)


def global_backward_body(
    got_ref, other_ref, own_seg_ref, shared_seg_ref, total_ref, d_ref, sent_ref, to_other_ref,
    q_scr, k_scr, v_scr, kt_scr, d_scr, dq_scr, dk_scr, dv_scr,
):
    fill_heads(got_ref, other_ref, own_seg_ref, shared_seg_ref, q_scr, k_scr, v_scr)
    first = low_lanes()
    rows = got_ref.shape[1] * 4 // 9
    half = rows // 2
    for unit in range(2):
        keys = jnp.where(first, k_scr[unit].astype(F32), 0.0)
        kt_scr[unit] = keys.T.astype(BF)
    count = k_scr.shape[1]
    d_scr[:count] = jnp.where(first, own_unfolded(d_ref, 0, rows), 0.0).astype(BF)
    d_scr[count:] = jnp.where(
        first, shared_unfolded(d_ref, rows - rows * 3 // 4, rows), 0.0
    ).astype(BF)
    dk_scr[...] = jnp.zeros_like(dk_scr)
    dv_scr[...] = jnp.zeros_like(dv_scr)

    def step(tile, carry):
        unit = tile // (count // TILE)
        here = pl.ds(pl.multiple_of(tile * TILE, TILE), TILE)
        queries, d_out = q_scr[here], d_scr[here]
        probs = jnp.exp(dot_bt(k_scr[unit], queries) - total_ref[tile])
        d_probs = dot_bt(v_scr[unit], d_out)
        product = probs * d_probs
        delta = jnp.sum(product, 0, keepdims=True)
        d_scores = (product - probs * delta).astype(BF)
        dv_scr[unit] += dot(probs.astype(BF), d_out)
        dk_scr[unit] += dot(d_scores, queries)
        dq_scr[here] = dot(kt_scr[unit], d_scores).T * SCALE
        return carry

    lax.fori_loop(0, q_scr.shape[0] // TILE, step, 0)
    mine = count // 2
    own = jnp.where(first, dq_scr[:count], swap(dk_scr[0]))
    sent_ref[:, 0:rows] = own.reshape(GROUP, rows, LANES).astype(BF)
    shared_k, shared_v = dk_scr[1], dv_scr[1]
    shared = jnp.where(first, dq_scr[count:], swap(shared_k[:mine]))
    sent_ref[:, rows : rows + half] = shared.reshape(GROUP, half, LANES).astype(BF)
    fold_out(dv_scr[0], shared_v[:mine], rows, sent_ref, rows + half)
    for place, grads in enumerate((shared_k, shared_v)):
        other = jnp.where(first, 0.0, swap(grads[mine:])).reshape(GROUP, half, LANES)
        to_other_ref[:, place * half : (place + 1) * half] = other.astype(BF)


def global_middle_body(*refs):
    sources, refs = refs[:-10], refs[-10:]
    got_ref, low_ref, high_ref, up_ref, gain_ref, kept_ref, gain_out_ref, d_middle_ref, sent_ref = refs[:9]
    weights = Weights(sources, refs[9])
    rows, width = low_ref.shape
    attended = jnp.concatenate([c.astype(BF) for c in unpack_folded(got_ref, 0, rows)], 1)
    gain = gain_ref[...]
    middle, normed, gate, up, mixed, result = mlp_forward(
        joined([low_ref, high_ref]).astype(F32), attended, gain, weights
    )
    d_gate_up, gain_grad, d_middle, d_attn, d_attended = mlp_backward(
        up_ref[...], middle, gate, up, gain, weights
    )
    start = 0
    for part in (result, attended, normed, mixed, d_gate_up, d_attn):
        kept_ref[:, start : start + part.shape[1]] = part
        start += part.shape[1]
    gain_out_ref[...] = gain_grad
    d_middle_ref[...] = d_middle
    pack_folded(chunks_of(d_attended), sent_ref, 0)


def global_finish_body(
    first_ref, got_ref, d_middle_ref, low_ref, high_ref, gain_ref, table_ref,
    d_proj_ref, gain_out_ref, *grad_refs,
):
    tables = [table_ref[i] for i in range(3)]
    x = joined([low_ref, high_ref]).astype(F32)
    rows = low_ref.shape[0]
    d_queries, d_keys = unpack_pairs(got_ref, rows)
    d_values = unpack_folded(got_ref, rows * 3 // 2, rows)
    parts = [unrotate(c, tables).astype(BF) for c in d_queries + d_keys]
    d_projected = jnp.concatenate(parts + [c.astype(BF) for c in d_values], 1)
    d_proj_ref[...] = d_projected
    store_chunks(
        grad_refs,
        input_backward(d_middle_ref[...], d_projected, x, gain_ref, first_ref, gain_out_ref),
    )


LARGE = (
    message_body,
    stack_body,
    local_middle_body,
    global_middle_body,
    global_finish_body,
)


def neighbours(count, step):
    return [
        (i, i + step)
        for i in range(count)
        if 0 <= i + step < count and i // GROUP == (i + step) // GROUP
    ]


def exchange(blocks, count):
    groups = [list(range(s, s + GROUP)) for s in range(0, count, GROUP)]
    return lax.all_to_all(blocks, "dp", 0, 0, axis_index_groups=groups)


def to_other_section(chunks, step):
    pairs = [(0, 1)] if step > 0 else [(1, 0)]
    return [lax.ppermute(rows, "section", pairs) for rows in chunks]


def partner(rows, apart, count):
    return lax.ppermute(rows, "dp", [(i, i ^ apart) for i in range(count)])


def gather_rows(piece, group_pos, count):
    pieces = {0: piece}
    for apart in (4, 8, 12):
        pieces[apart] = partner(piece, apart, count)
    for apart in (0, 4, 8, 12):
        pieces[apart + 2] = partner(pieces[apart], 2, count)
    for apart in range(0, GROUP, 2):
        pieces[apart + 1] = partner(pieces[apart], 1, count)
    whole = jnp.zeros((GROUP,) + piece.shape, piece.dtype)
    for apart, item in pieces.items():
        start = (group_pos ^ apart,) + (0,) * piece.ndim
        whole = lax.dynamic_update_slice(whole, item[None], start)
    if count > GROUP:
        groups = [list(range(s, count, GROUP)) for s in range(GROUP)]
        whole = lax.all_gather(whole, "dp", axis=0, tiled=True, axis_index_groups=groups)
    return whole.reshape(-1, piece.shape[-1]), pieces[2]


def plane_rows(rows, group_pos, count):
    parts = rows.reshape(count // GROUP, 4, 4, *rows.shape[1:])
    place, plane = group_pos % 4, group_pos // 4
    taken = []
    for apart in range(4):
        block = lax.dynamic_index_in_dim(parts, place ^ apart, 2, keepdims=False)
        block = jnp.stack(
            [lax.dynamic_index_in_dim(block, plane ^ z, 1, keepdims=False) for z in range(4)]
        )
        taken.append(partner(block, apart, count) if apart else block)
    return taken


def left_body(spans, lower_ref, place_ref, *refs):
    refs, out_ref = refs[:-1], refs[-1]
    base = 0
    for span in spans:
        first, second = (refs[i][:, start:end].astype(F32) for i, start, end in span)
        turned = jnp.where(lower_ref[0] == 1, first, second).T
        size = turned.shape[0] // GROUP
        for d in range(GROUP):
            side = d % 4 ^ place_ref[0] % 4
            plane = d // 4 ^ place_ref[0] // 4
            out_ref[side, plane, base : base + size] = turned[d * size : (d + 1) * size].astype(BF)
        base += size


def left_rows_of(refs, rows):
    start, end = rows
    parts = [
        jnp.concatenate([ref[p, start:end].astype(F32) for p in range(4)], 0).astype(BF) for ref in refs
    ]
    return jnp.concatenate(parts, 1)


def by_plane(result, base, outs, columns=slice(None)):
    keep, keep_far, send = outs
    rows = result.shape[0] // 4
    half = send.shape[0] // 2
    here = slice(base, base + rows)
    keep[here, columns] = result[:rows]
    keep_far[here, columns] = result[2 * rows : 3 * rows]
    send[here, columns] = result[rows : 2 * rows].astype(BF)
    send[half + base : half + base + rows, columns] = result[3 * rows :].astype(BF)


def early_body(terms, split, *refs):
    refs, outs = refs[:-3], refs[-3:]
    operands, lefts = (refs[:split], refs[split:-4]), refs[-4:]
    width = outs[0].shape[1]
    base = 0
    for which, rows, (start, end) in terms:
        right = jnp.concatenate([ref[:, start:end] for ref in operands[which]], 0)
        result = dot(left_rows_of(lefts, rows), right)
        for column in range(0, end - start, width):
            by_plane(result[:, column : column + width], base, outs)
            base += result.shape[0] // 4


def late_body(rows, place_ref, *refs):
    refs, outs, scr = refs[:-4], refs[-4:-1], refs[-1]
    rights, lefts = refs[:-4], refs[-4:]
    columns = rights[0].shape[1]
    width = columns // 3
    size = outs[0].shape[0]
    tokens = lefts[0].shape[2]
    right = jnp.concatenate([ref[:tokens] for ref in rights], 0)
    by_plane(dot(left_rows_of(lefts, rows), right), 0, outs, slice(0, columns))
    tail = sum(ref[tokens:, :width].astype(F32) for ref in rights)
    both = jnp.concatenate([tail, jnp.zeros((LANES - EXTRA, width), F32)], 0).T
    lane = lax.broadcasted_iota(jnp.int32, (1, LANES), 1)
    lows = pltpu.roll(both, LANES - 1, 1)
    scr[...] = jnp.where(lane % 2 == 0, both + lows, 0.0)
    gains = []
    for plane in range(4):
        d = (place_ref[0] // 4 ^ plane) * 4 + place_ref[0] % 4
        gains.append(scr[pl.ds(pl.multiple_of(d * size, 16), size)])
    by_plane(jnp.concatenate(gains, 0), 0, outs, slice(columns, columns + LANES))


def three_parts(shape):
    return [(shape, F32), (shape, F32), ((2 * shape[0], shape[1]), BF)]


def first_hop(blocks, count):
    keep, keep_far, send = blocks
    got = partner(send, 4, count)
    half = keep.shape[0]
    return keep + got[:half].astype(F32), (keep_far + got[half:].astype(F32)).astype(BF)


def second_hop(near, far, count):
    return near + partner(far, 8, count).astype(F32)


def over_groups(rows, count):
    if count == GROUP:
        return rows
    apart = [list(range(s, count, GROUP)) for s in range(GROUP)]
    rows = rows.reshape(count // GROUP, -1, rows.shape[1])
    return lax.psum_scatter(rows, "dp", scatter_dimension=0, axis_index_groups=apart)


def on_device(
    tokens_in,
    segment_ids,
    out_grad,
    qkv_weight,
    attn_out_weight,
    mlp_in_weight,
    mlp_out_weight,
    attn_gain,
    mlp_gain,
):
    lower = lax.axis_index("section") == 0
    lower_flag = lower.astype(jnp.int32)[None]
    shard_total = qkv_weight.shape[1] * (lax.axis_size("dp") // GROUP)
    hidden_total = mlp_out_weight.shape[1] * (lax.axis_size("dp") // GROUP)
    count = lax.axis_size("dp")
    replica = lax.axis_index("dp")
    group_pos = replica % GROUP
    micro_count, row_count, width = tokens_in.shape
    shard = qkv_weight.shape[1]
    runs = -(-row_count // shard)
    (message,) = on_core(
        message_body,
        [((shard, 3 * width + LANES), BF)],
        (qkv_weight[0], attn_gain, mlp_gain, segment_ids),
        [pltpu.VMEM((LANES, LANES), F32), pltpu.VMEM((8, LANES), F32)],
    )
    first, early_piece = gather_rows(message, group_pos, count)
    inner = mlp_in_weight.shape[2]
    hidden = mlp_out_weight.shape[1] * count
    if count == GROUP:
        moved = first_block(2 * mlp_out_weight.shape[1]) - mlp_out_weight.shape[1]
        beside = partner(mlp_out_weight[0, :moved], 1, count)
        (stacked,) = on_core(
            stack_body,
            [((shard, width + inner + width + 2 * (width // 3)), BF)],
            (
                (replica % 2)[None],
                attn_out_weight[0],
                mlp_in_weight[0],
                mlp_out_weight[0],
                beside,
            ),
            (),
            [pltpu.SMEM] + [pltpu.VMEM] * 4,
        )
        stacked, _ = lax.optimization_barrier((stacked, early_piece))
        others = [lax.all_gather(stacked, "dp", axis=0, tiled=True)]
    else:
        others = [
            lax.all_gather(item[0], "dp", axis=0, tiled=True)
            for item in (attn_out_weight, mlp_in_weight, mlp_out_weight)
        ]
    positions = group_pos * row_count + jnp.arange(row_count)
    local_tables = angles(positions, local_log_base)
    global_tables = angles(positions, global_log_base)

    rows = micro_count * row_count
    pairs = rows * width // (row_count * LANES)
    in_0 = tokens_in.reshape(rows, width)
    extra_rows = -(-(2 + micro_count * runs) // 8) * 8
    extra, normed_0, q_0, kv_0 = on_core(
        local_project_body,
        [
            ((extra_rows, width), F32),
            ((rows, width), BF),
            ((rows, width), BF),
            ((rows, 2 * width), BF),
        ],
        (first, in_0, local_tables),
    )
    gain_attn, gain_mlp = extra[:1], extra[1:2]
    all_ids = extra[2 : 2 + micro_count * runs].reshape(micro_count, runs, count, shard)
    all_ids = lax.dynamic_slice_in_dim(all_ids, replica - group_pos, GROUP, 2)
    all_ids = all_ids.swapaxes(1, 2).reshape(micro_count, GROUP, runs * shard)[..., :row_count]
    segments = all_ids.reshape(micro_count, GROUP * row_count).astype(jnp.int32)

    key_pos = positions[0] - row_count + jnp.arange(3 * row_count)
    around = jnp.pad(segments, ((0, 0), (row_count, row_count)), constant_values=-1)
    key_seg = lax.dynamic_slice_in_dim(around, group_pos * row_count, 3 * row_count, 1)
    visible = (key_seg[:, :, None] == segment_ids[:, None, :]) & (
        jnp.abs(positions[None, :] - key_pos[:, None]) <= HALF_WIN
    )[None]
    bias = jnp.tile(jnp.where(visible, 0.0, masked_score), (1, 1, 2))

    own_seg = lax.dynamic_index_in_dim(segments, group_pos // 8, 0, keepdims=False)
    halves = own_seg.reshape(GROUP, 2, row_count // 2)
    mine = lax.dynamic_index_in_dim(halves, group_pos % 2, 1, keepdims=False).reshape(-1)
    theirs = lax.dynamic_index_in_dim(halves, 1 - group_pos % 2, 1, keepdims=False).reshape(-1)
    shared_seg = jnp.concatenate([mine, theirs])[:, None]
    own_seg = own_seg[:, None]

    up_pairs, down_pairs = neighbours(count, 1), neighbours(count, -1)
    around_0 = (
        lax.ppermute(kv_0, "dp", up_pairs),
        kv_0,
        lax.ppermute(kv_0, "dp", down_pairs),
    )
    att_0, total_0 = on_core(
        local_forward_body,
        [((rows, width), BF), ((pairs, 1, LANES), F32)],
        (q_0, *around_0, bias),
    )
    kept_0, state_0, *out_0 = on_core(
        local_middle_body,
        [((rows, width + hidden), BF), ((rows, width + inner), F32)]
        + [((row_count, width), BF)] * micro_count,
        (*others, in_0, att_0, gain_mlp),
        [pltpu.VMEM((hidden, width), BF)],
    )

    in_1 = to_other_section(out_0, 1)
    fold = row_count * 3 // 4
    half = row_count // 2
    normed_1, sent = on_core(
        global_project_body,
        [((rows, width), BF), ((GROUP, 3 * fold, LANES), BF)],
        (first, *in_1, gain_attn, global_tables),
    )
    got = exchange(sent, count)
    beside = jnp.concatenate(
        [got[:, row_count : row_count + half], got[:, 3 * fold - half :]], 1
    )
    beside = partner(beside, 1, count)
    keys = GROUP * row_count
    tiles = keys * 3 // 2 // TILE
    head_scratch = [
        pltpu.VMEM((keys * 3 // 2, LANES), BF),
        pltpu.VMEM((2, keys, LANES), BF),
        pltpu.VMEM((2, keys, LANES), BF),
        pltpu.VMEM((2, LANES, keys), BF),
    ]
    folded, total_1 = on_core(
        global_forward_body,
        [((GROUP, fold, LANES), BF), ((tiles, 1, TILE), F32)],
        (got, beside, own_seg, shared_seg),
        head_scratch + [pltpu.VMEM((keys * 3 // 2, LANES), F32)],
    )
    folded = exchange(folded, count)

    up_1 = out_grad.reshape(rows, width)
    kept_1, gain_mlp_1, d_mid_1, sent = on_core(
        global_middle_body,
        [
            ((rows, 4 * width + hidden + inner), BF),
            ((1, width), F32),
            ((rows, width), F32),
            ((GROUP, fold, LANES), BF),
        ],
        (*others, folded, *in_1, up_1, gain_mlp),
        [pltpu.VMEM((hidden, width), BF)],
    )
    d_folded = exchange(sent, count)
    sources = (normed_0, normed_1, att_0, kept_0, kept_1)
    cut = 2 * width
    spans = (
        ((0, 0, width), (1, 0, width)),
        ((2, 0, width), (4, width, cut)),
        ((3, 0, width), (4, cut, cut + width)),
        ((3, width, width + hidden), (4, cut + width, cut + width + hidden)),
    )
    left_total = 3 * shard_total + hidden_total
    if count == GROUP:
        (left,) = on_core(
            functools.partial(left_body, spans),
            [((4, 4, left_total, rows), BF)],
            (lower_flag, group_pos[None], *sources),
            (),
            [pltpu.SMEM] * 2 + [pltpu.VMEM] * len(sources),
        )
        left, d_folded = lax.optimization_barrier((left, d_folded))
    else:
        left = [
            plane_rows(
                jnp.where(lower, *(sources[i][:, start:end] for i, start, end in span))
                .T.reshape(count, -1, rows),
                group_pos,
                count,
            )
            for span in spans
        ]
        left = [jnp.concatenate([i.reshape(4, -1, rows) for i in items], 1) for items in zip(*left)]
    sent, to_beside = on_core(
        global_backward_body,
        [((GROUP, 3 * fold, LANES), BF), ((GROUP, 2 * half, LANES), BF)],
        (got, beside, own_seg, shared_seg, total_1, d_folded),
        head_scratch
        + [
            pltpu.VMEM((keys * 3 // 2, LANES), BF),
            pltpu.VMEM((keys * 3 // 2, LANES), F32),
            pltpu.VMEM((2, keys, LANES), F32),
            pltpu.VMEM((2, keys, LANES), F32),
        ],
    )
    back = partner(to_beside, 1, count)
    gap = 3 * fold - half - row_count - half
    back = jnp.concatenate(
        [
            jnp.zeros((GROUP, row_count, LANES), BF),
            back[:, :half],
            jnp.zeros((GROUP, gap, LANES), BF),
            back[:, half:],
        ],
        1,
    )
    sent = (sent.astype(F32) + back.astype(F32)).astype(BF)
    if count == GROUP:
        left, sent = lax.optimization_barrier((left, sent))
        left = [left[0]] + [partner(left[apart], apart, count) for apart in range(1, 4)]
    got = exchange(sent, count)
    left, got = lax.optimization_barrier((left, got))

    d_proj_1, gain_attn_1, *grad_1 = on_core(
        global_finish_body,
        [((rows, 3 * width), BF), ((1, width), F32)] + [((row_count, width), BF)] * micro_count,
        (first, got, d_mid_1, *in_1, gain_attn, global_tables),
    )

    up_0 = to_other_section(grad_1, -1)
    d_mlp = jnp.concatenate(
        [jnp.where(lower, a, up_1[i * row_count :][:row_count]) for i, a in enumerate(up_0)]
    )
    across_mlp = partner(d_mlp, 2, count)
    gain_mlp_0, d_mid_0, d_att_0, right = on_core(
        local_back_middle_body,
        [
            ((1, width), F32),
            ((rows, width), F32),
            ((rows, width), BF),
            ((rows, inner + width), BF),
        ],
        (*others, lower_flag, *up_0, state_0, gain_mlp, kept_1),
        [pltpu.VMEM((hidden, width), BF)],
        [pltpu.VMEM] * len(others) + [pltpu.SMEM] + [pltpu.VMEM] * 5,
    )
    d_att_0, right, across_mlp = lax.optimization_barrier((d_att_0, right, across_mlp))
    across = [partner(right, 2, count)]
    d_mlp = [d_mlp, partner(d_mlp, 1, count), across_mlp, partner(across_mlp, 1, count)]
    out_near, out_far = first_hop(
        on_core(
            functools.partial(early_body, [(0, (3 * shard_total, left_total), (0, width))], 4),
            three_parts((hidden_total, width)),
            (*d_mlp, *left),
        ),
        count,
    )
    dq_0, d_own, d_before, d_after = on_core(
        local_backward_body,
        [
            ((rows, width), BF),
            ((rows, 2 * width), F32),
            ((rows, 2 * width), BF),
            ((rows, 2 * width), BF),
        ],
        (q_0, *around_0, bias, total_0, d_att_0, local_tables),
    )
    from_after = lax.ppermute(d_before, "dp", down_pairs)
    from_before = lax.ppermute(d_after, "dp", up_pairs)
    from_after, out_far = lax.optimization_barrier((from_after, out_far))
    d_proj, grad_0, gain_attn_sum = on_core(
        local_finish_body,
        [
            ((rows + EXTRA, 3 * width), BF),
            ((rows, width), BF),
            ((1, width), F32),
        ],
        (
            lower_flag, first, dq_0, d_own, from_after, from_before, local_tables, d_mid_0, in_0, gain_attn,
            gain_mlp_0, d_proj_1, gain_attn_1, gain_mlp_1,
        ),
        [pltpu.VMEM((1, width), F32)],
        [pltpu.SMEM] + [pltpu.VMEM] * 13,
    )
    across_chunks = [partner(d_proj, 2, count)]
    across, right, _ = lax.optimization_barrier((across, right, d_proj))
    right = [right, partner(right, 1, count)] + across
    right += [partner(item, 1, count) for item in across]
    in_rows, attn_rows = shard_total * (inner // width), shard_total
    early_rows = in_rows + attn_rows
    terms = [
        (0, (2 * shard_total, 3 * shard_total), (0, inner)),
        (0, (shard_total, 2 * shard_total), (inner, inner + width)),
    ]
    near, far = first_hop(
        on_core(
            functools.partial(early_body, terms, len(right)),
            three_parts((early_rows, width)),
            (*right, *left),
        ),
        count,
    )
    far = jnp.concatenate([far, out_far])
    across_chunks, d_proj, _ = lax.optimization_barrier((across_chunks, d_proj, far))
    far = partner(far, 8, count)
    right = [d_proj, partner(d_proj, 1, count)] + across_chunks
    right += [partner(item, 1, count) for item in across_chunks]
    late_in = (group_pos[None], *right, *left)
    late = on_core(
        functools.partial(late_body, (0, shard_total)),
        three_parts((shard_total, 3 * width + LANES)),
        late_in,
        [pltpu.VMEM((width, LANES), F32)],
        [pltpu.SMEM] + [pltpu.VMEM] * (len(late_in) - 1),
    )
    far, _ = lax.optimization_barrier((far, late[0]))
    early = near + far[:early_rows].astype(F32)
    mlp_out_share = out_near + far[early_rows:].astype(F32)
    late = second_hop(*first_hop(late, count), count)
    parts = [early[p * shard_total : (p + 1) * shard_total] for p in range(inner // width)]
    in_share = jnp.concatenate(parts, 1)
    attn_share = early[in_rows : in_rows + attn_rows]
    gain_columns = late[:, 3 * width :]
    qkv_share, in_share, mlp_out_share, attn_share, gain_columns = (
        over_groups(item, count)
        for item in (late[:, : 3 * width], in_share, mlp_out_share, attn_share, gain_columns)
    )
    if count == GROUP:
        gains = jnp.stack([gain_columns[:, 0], gain_columns[:, 2]])
    else:
        gain_mlp_sum = jnp.where(lower, gain_mlp_0, gain_mlp_1)
        gains = lax.psum(jnp.concatenate([gain_attn_sum, gain_mlp_sum]), "dp")
        gains = lax.dynamic_slice_in_dim(gains, replica * shard, shard, 1)

    return (
        jnp.where(lower, jnp.concatenate(out_0), kept_1[:, :width]).reshape(1, micro_count, row_count, width),
        jnp.where(lower, grad_0, jnp.concatenate(grad_1)).reshape(1, micro_count, row_count, width),
        qkv_share[None],
        attn_share[None],
        in_share[None],
        mlp_out_share[None],
        gains[:1],
        gains[1:],
    )


def solution(mesh):
    in_specs = (
        P(None, "dp", None),
        P(None, "dp"),
        P(None, "dp", None),
        P("section", "dp", None),
        P("section", "dp", None),
        P("section", "dp", None),
        P("section", "dp", None),
        P("section", "dp"),
        P("section", "dp"),
    )
    out_specs = (
        P("section", None, "dp", None),
        P("section", None, "dp", None),
        P("section", "dp", None),
        P("section", "dp", None),
        P("section", "dp", None),
        P("section", "dp", None),
        P("section", "dp"),
        P("section", "dp"),
    )
    return jax.shard_map(
        on_device, mesh=mesh, in_specs=in_specs, out_specs=out_specs, check_vma=False
    )
```
